32 devices in a mesh: section: 2 (over core), gx: 4 (over y, x), gy: 4 (over z).
Axes of the slice: x: 2, y: 2, z: 4, core: 2. Of those that a mesh axis runs over, the one named last changes fastest.
Arguments:
- block_input: bfloat16 [4, 512, 768], P(None, 'gx', 'gy'), may hold values from -6 to 6
- output_grad: bfloat16 [4, 512, 768], P(None, 'gx', 'gy'), may hold values from -6 to 6
- attention_gain: float32 [2, 768], P('section', 'gy'), may hold values from 0.1 to 1.9
- attention_in: bfloat16 [2, 768, 3, 768], P('section', 'gy', None, 'gx'), may hold values from -0.21875 to 0.21875
- attention_out: bfloat16 [2, 768, 768], P('section', 'gx', 'gy'), may hold values from -0.4375 to 0.4375
- feed_gain: float32 [2, 768], P('section', 'gy'), may hold values from 0.1 to 1.9
- router_weight: bfloat16 [2, 768, 16], P('section', 'gy'), may hold values from -0.21875 to 0.21875
- expert_in: bfloat16 [2, 16, 768, 2, 2048], P('section', None, 'gy', None, 'gx'), may hold values from -0.21875 to 0.21875
- expert_down: bfloat16 [2, 16, 2048, 768], P('section', None, 'gx', 'gy'), may hold values from -0.125 to 0.125
- shared_in: bfloat16 [2, 768, 2, 2048], P('section', 'gy', None, 'gx'), may hold values from -0.21875 to 0.21875
- shared_down: bfloat16 [2, 2048, 768], P('section', 'gx', 'gy'), may hold values from -0.125 to 0.125
- routes: int32 [2, 4, 512, 2], P('section'), may hold values from 0 to 15, all different within a row; in each aligned block of 512 rows (0 to 511, 512 to 1023, ..., all dimensions but the last counted through in order) at most 80 rows name the same one
Outputs:
- layer_outputs: bfloat16 [2, 4, 512, 768], P('section', None, 'gx', 'gy')
- input_grads: bfloat16 [2, 4, 512, 768], P('section', None, 'gx', 'gy')
- attention_gain_grad: float32 [2, 768], P('section', 'gy')
- attention_in_grad: float32 [2, 768, 3, 768], P('section', 'gy', None, 'gx')
- attention_out_grad: float32 [2, 768, 768], P('section', 'gx', 'gy')
- feed_gain_grad: float32 [2, 768], P('section', 'gy')
- router_weight_grad: float32 [2, 768, 16], P('section', 'gy')
- expert_in_grad: float32 [2, 16, 768, 2, 2048], P('section', None, 'gy', None, 'gx')
- expert_down_grad: float32 [2, 16, 2048, 768], P('section', None, 'gx', 'gy')
- shared_in_grad: float32 [2, 768, 2, 2048], P('section', 'gy', None, 'gx')
- shared_down_grad: float32 [2, 2048, 768], P('section', 'gx', 'gy')
The draws below stay inside these ranges and needn't reach their ends.
Inputs may be any that keep to these rules, and one draw needn't show every extreme that they name: `routes`: each token names two different experts; in each layer and micro-batch at most 80 tokens name one expert, a bound that some block reaches of them.
All inputs are finite; a program needn't handle non-finite values.
Results may differ from the reference program's by a relative error of at most 0.024.
Values may be sent and summed in bfloat16 or wider, within the bound.
A program may use at most 384 MiB of HBM per device.

```python
import math
import jax
import jax.numpy as jnp
import numpy as np
from jax import lax

D = 768
H = 12
DH = 64
E = 16
FE = 2048
FS = 2048
SEQ_LEN = 128
MB = 4
TOK_MB = 512
CAP = 80


def block_scale(key, dims, cuts, least, high):
    level = 1.0
    for axis_at, parts in cuts:
        steps = jax.random.uniform(jax.random.fold_in(jax.random.fold_in(key, 6), axis_at), (parts,), jnp.float32, least / len(cuts), high / len(cuts))
        level = level * jnp.repeat(jnp.exp(steps), dims[axis_at] // parts).reshape((-1,) + (1,) * (len(dims) - 1 - axis_at))
    return level


def shared_out(stream_key, own, number, rows, amount, top, limit, skew):
    sequence = jax.random.permutation(stream_key, amount)
    heavy_load, ordinary = shares(amount, rows * top, limit, skew, True), shares(amount, rows * top, limit, skew, False)
    places = jnp.arange(amount)

    def named(lengths, rotation):
        used = int((lengths > 0).sum())
        fixed = max(1, used // 4)
        moved = fixed + (places - fixed + rotation * (used - fixed)) % max(1, amount - fixed)
        return jnp.zeros((amount,), jnp.int32).at[sequence[jnp.where(places < fixed, places, moved)]].set(jnp.asarray(lengths, jnp.int32))

    lengths = jnp.where(number % 4 == 0, named(heavy_load, number // 4), named(ordinary, number - number // 4 - 1))
    mixed = jax.random.permutation(jax.random.fold_in(own, 3), amount)
    giver, sink = mixed[0:amount // 2 * 2:2], mixed[1:amount // 2 * 2:2]
    room = jnp.minimum(lengths[giver] - 1, limit - lengths[sink]) // 2
    room = jnp.where((giver == sequence[0]) | (sink == sequence[0]) | (lengths[sink] == 0), 0, jnp.maximum(room, 0))
    moved = jax.random.randint(jax.random.fold_in(own, 4), (amount // 2,), 0, 1 << 20) % (room + 1)
    lengths = lengths.at[giver].add(-moved).at[sink].add(moved)
    labels = jnp.searchsorted(jnp.cumsum(lengths), jnp.arange(rows * top), side="right").astype(jnp.int32)
    listing = labels.reshape(top, rows).T
    listing = listing[jax.random.permutation(jax.random.fold_in(own, 1), rows)]
    rotation = jax.random.randint(jax.random.fold_in(own, 2), (rows, 1), 0, top)
    return jnp.take_along_axis(listing, (jnp.arange(top)[None, :] + rotation) % top, axis=1)


def shares(count, total, reach, lean, full):
    weights = [(1 << 20) // math.isqrt(rank ** lean) + 1 for rank in range(1, count + 1)]
    largest = reach if full else min(reach, max(-(-total // count), total * weights[0] // sum(weights)))
    least = 1 if total - largest >= count - 1 else 0
    holding, surplus = [largest] + [least] * (count - 1), total - largest - least * (count - 1)
    while surplus > 0:
        free = [i for i in range(1, count) if holding[i] < largest] or [i for i in range(1, count) if holding[i] < reach]
        whole, budget = sum([weights[i] for i in free]), surplus
        for i in free:
            more = min(reach - holding[i], max(1, budget * weights[i] // whole), surplus)
            holding[i] = holding[i] + more
            surplus = surplus - more
    return np.array(holding)


def normal_values(own_key, extent, scale, limit, split=(), kind=jnp.bfloat16):
    array = scale * jax.random.normal(own_key, extent, jnp.float32)
    if split:
        array = array * block_scale(own_key, extent, split, -0.22, 0.18)
    return jnp.clip(array, -limit, limit).astype(kind)


def setup_inputs(seed: int = 0) -> dict:
    arg_keys = jax.random.split(jax.random.key(seed), 13)
    block_input = normal_values(arg_keys[0], (MB, TOK_MB, D), 1.0, 6.0, ((1, 4), (2, 4)))
    output_grad = normal_values(arg_keys[1], (MB, TOK_MB, D), 1.0, 6.0, ((1, 4), (2, 4)))
    attention_gain = jnp.clip(1.0 + 0.18 * jax.random.normal(arg_keys[2], (2, D), jnp.float32), 0.1, 1.9)
    attention_in = normal_values(arg_keys[3], (2, D, 3, H * DH), D ** -0.5, 0.21875, ((0, 2), (1, 4), (3, 4)))
    attention_out = normal_values(arg_keys[4], (2, H * DH, D), (H * DH * 32 // SEQ_LEN) ** -0.5, 0.4375, ((0, 2), (1, 4), (2, 4)))
    feed_gain = jnp.clip(1.0 + 0.18 * jax.random.normal(arg_keys[5], (2, D), jnp.float32), 0.1, 1.9)
    router_weight = normal_values(arg_keys[6], (2, D, E), D ** -0.5, 0.21875, ((0, 2), (1, 4)))
    expert_in = normal_values(arg_keys[7], (2, E, D, 2, FE), D ** -0.5, 0.21875, ((0, 2), (2, 4), (4, 4)))
    expert_down = normal_values(arg_keys[8], (2, E, FE, D), FE ** -0.5, 0.125, ((0, 2), (2, 4), (3, 4)))
    shared_in = normal_values(arg_keys[9], (2, D, 2, FS), D ** -0.5, 0.21875, ((0, 2), (1, 4), (3, 4)))
    shared_down = normal_values(arg_keys[10], (2, FS, D), FS ** -0.5, 0.125, ((0, 2), (1, 4), (2, 4)))
    routes_keys = jax.random.split(jax.random.fold_in(arg_keys[11], 1), 2 * MB * TOK_MB // TOK_MB)
    routes_turns = jax.random.permutation(jax.random.fold_in(arg_keys[11], 3), 2 * MB * TOK_MB // TOK_MB)
    routes = jax.vmap(lambda own, number: shared_out(jax.random.fold_in(arg_keys[11], 2), own, number, TOK_MB, E, 2, CAP, 0))(routes_keys, routes_turns).reshape((2, MB, TOK_MB, 2))
    return {"block_input": block_input, "output_grad": output_grad, "attention_gain": attention_gain, "attention_in": attention_in, "attention_out": attention_out, "feed_gain": feed_gain, "router_weight": router_weight, "expert_in": expert_in, "expert_down": expert_down, "shared_in": shared_in, "shared_down": shared_down, "routes": routes}


epsilon = 1e-06
highest = lax.Precision.HIGHEST

@jax.custom_vjp
def low(v):
    return lax.optimization_barrier(v.astype(jnp.bfloat16)).astype(jnp.float32)

@jax.custom_vjp
def low_back(v):
    return v

def low_keep(v):
    return (low(v), None)

def low_pass(kept, grad):
    return (grad,)

def back_keep(v):
    return (v, None)

def back_low(kept, grad):
    return (low(grad),)
low.defvjp(low_keep, low_pass)
low_back.defvjp(back_keep, back_low)

def rope_turn(values, positions):
    half_size = values.shape[-1] // 2
    frequency = 10000.0 ** (-jnp.arange(half_size, dtype=jnp.float32) / half_size)
    angles = positions[:, None] * frequency[None, :]
    cosine = jnp.cos(angles)[:, None, :]
    sine_part = jnp.sin(angles)[:, None, :]
    first_half = values[..., :half_size]
    second_half = values[..., half_size:]
    return jnp.concatenate([first_half * cosine - second_half * sine_part, first_half * sine_part + second_half * cosine], axis=-1)

def rms_norm(stream, gain):
    inverse_rms = lax.rsqrt(lax.optimization_barrier(jnp.mean(stream * stream, axis=-1, keepdims=True)) + epsilon)
    return low(stream * inverse_rms * gain)

def attend_one(members):
    queries, keys_part, values_part = members
    score_scale = queries.shape[-1] ** (-0.5)
    scores = low_back(jnp.einsum('qhd,khd->hqk', queries, keys_part, precision=highest) * score_scale)
    length = queries.shape[0]
    causal = jnp.arange(length)[:, None] >= jnp.arange(length)[None, :]
    scores = jnp.where(causal[None], scores, -1e+30)
    weights = low(jax.nn.softmax(scores, axis=-1))
    return jnp.einsum('hqk,khd->qhd', weights, values_part, precision=highest)

def slot_table(route_ids, experts, capacity):
    flat_ids = route_ids.reshape(-1).astype(jnp.int32)
    assigned = (flat_ids[:, None] == jnp.arange(experts, dtype=jnp.int32)[None, :]).astype(jnp.int32)
    earlier = (jnp.cumsum(assigned, axis=0) - assigned).astype(jnp.int32)
    places = (flat_ids * capacity + lax.optimization_barrier(jnp.sum(earlier * assigned, axis=1))).astype(jnp.int32)
    owners = (jnp.arange(flat_ids.shape[0], dtype=jnp.int32) // 2).astype(jnp.int32)
    slot_token = jnp.zeros((experts * capacity,), jnp.int32).at[places].set(owners)
    slot_valid = jnp.zeros((experts * capacity,), jnp.int32).at[places].set(jnp.ones_like(owners))
    return (places.reshape(-1, 2), slot_token, slot_valid)

def layer(stream, weights, route_ids):
    attention_gain, attention_in, attention_out, feed_gain, router_weight, expert_in, expert_down, shared_in, shared_down = weights
    tokens = stream.shape[0]
    normed = rms_norm(stream, attention_gain)
    projected = low_back(jnp.dot(normed, attention_in.reshape(D, 3 * H * DH), precision=highest))
    projected = projected.reshape(tokens // SEQ_LEN, SEQ_LEN, 3, H, DH)
    positions = jnp.arange(SEQ_LEN, dtype=jnp.float32)
    queries = low(rope_turn(projected[:, :, 0], positions))
    keys_all = low(rope_turn(projected[:, :, 1], positions))
    values_all = low(projected[:, :, 2])
    attended = lax.map(jax.checkpoint(attend_one), (queries, keys_all, values_all))
    attended = low(low_back(attended.reshape(tokens, H * DH)))
    middle = stream + low_back(jnp.dot(attended, attention_out, precision=highest))
    normed_feed = rms_norm(middle, feed_gain)
    route_slot, slot_token, slot_valid = slot_table(route_ids, E, CAP)
    grouped = (normed_feed[slot_token] * slot_valid[:, None].astype(jnp.float32)).reshape(E, CAP, D)
    gate_up = low_back(jnp.einsum('ecd,edf->ecf', grouped, expert_in.reshape(E, D, 2 * FE), precision=highest))
    router = jnp.einsum('ecd,de->ec', grouped, router_weight, precision=highest)
    hidden = low(jax.nn.silu(gate_up[..., :FE]) * gate_up[..., FE:] * jax.nn.sigmoid(router)[..., None])
    expert_result = jnp.einsum('ecf,efd->ecd', hidden, expert_down, precision=highest).reshape(E * CAP, D)
    shared = low_back(jnp.dot(normed_feed, shared_in.reshape(D, 2 * FS), precision=highest))
    shared_hidden = low(jax.nn.silu(shared[:, :FS]) * shared[:, FS:])
    branch = expert_result[route_slot[:, 0]] + expert_result[route_slot[:, 1]] + jnp.dot(shared_hidden, shared_down, precision=highest)
    return middle + low_back(branch)

def reference(block_input, output_grad, attention_gain, attention_in, attention_out, feed_gain, router_weight, expert_in, expert_down, shared_in, shared_down, routes):
    params = tuple((member.astype(jnp.float32) for member in (attention_gain, attention_in, attention_out, feed_gain, router_weight, expert_in, expert_down, shared_in, shared_down)))

    def micro_step(totals, members):
        stream_in, grad_out, route_pair = members
        probe = jnp.zeros((TOK_MB, D), jnp.float32)

        def forward(first_input, probe_input, weights):
            first = tuple((member[0] for member in weights))
            second = tuple((member[1] for member in weights))
            middle_out = low(low_back(layer(first_input, first, route_pair[0])))
            return (middle_out, layer(middle_out + probe_input, second, route_pair[1]))
        (middle_out, final_out), backward = jax.vjp(forward, stream_in.astype(jnp.float32), probe, params)
        grad_first, grad_second, grad_params = backward((jnp.zeros_like(middle_out), grad_out.astype(jnp.float32)))
        totals = tuple((total + member for total, member in zip(totals, grad_params)))
        return (totals, (middle_out, final_out, grad_first, grad_second))
    initial = tuple((jnp.zeros_like(member) for member in params))
    totals, (middle_all, final_all, grad_first_all, grad_second_all) = lax.scan(micro_step, initial, (block_input, output_grad, jnp.moveaxis(routes, 1, 0)))
    outputs = jnp.stack([middle_all, final_all]).astype(jnp.bfloat16)
    gradients = jnp.stack([grad_first_all, grad_second_all]).astype(jnp.bfloat16)
    return (outputs, gradients, totals[0], totals[1], totals[2], totals[3], totals[4], totals[5], totals[6], totals[7], totals[8])
```

```python
import functools

import jax
import jax.numpy as jnp
from jax import lax
from jax.experimental import pallas as pl
from jax.experimental.pallas import tpu as pltpu
from jax.sharding import PartitionSpec as P

DH = 64


epsilon = 1e-06
highest = lax.Precision.HIGHEST


def from_partner(array, axis, apart):
    return lax.ppermute(array, axis, [(i, i ^ 1 << apart) for i in range(lax.axis_size(axis))])


def token_rows(values):
    return lax.all_gather(values, "gx", axis=0, tiled=True)


def output_rows(values):
    return lax.psum_scatter(values, "gx", scatter_dimension=0, tiled=True)


def width_sum(values):
    return lax.psum(values, "gy")


def pass_section(values):
    return from_partner(values, "section", 0)


def sequence_sums(values):
    return lax.psum_scatter(values, "gy", scatter_dimension=0, tiled=True)


def sequence_rows(values):
    return lax.all_gather(values, "gy", axis=0, tiled=True)


def gather_hidden(hidden, shared_hidden):
    return (
        lax.all_gather(hidden, "gy", axis=0, tiled=True),
        lax.all_gather(shared_hidden, "gy", axis=0, tiled=True),
    )


def rope_turn(values, positions, turn_sign):
    half_size = values.shape[-1] // 2
    frequency = 10000.0 ** (-jnp.arange(half_size, dtype=jnp.float32) / half_size)
    angles = positions[:, None] * frequency[None, :]
    cosine = jnp.cos(angles)[:, None, :]
    sine_part = turn_sign * jnp.sin(angles)[:, None, :]
    first_half = values[..., :half_size]
    second_half = values[..., half_size:]
    return jnp.concatenate(
        [
            first_half * cosine - second_half * sine_part,
            first_half * sine_part + second_half * cosine,
        ],
        axis=-1,
    )


def norm_forward(stream, gain):
    full_width = stream.shape[1] * lax.axis_size("gy")
    square_sum = width_sum(jnp.sum(stream * stream, axis=1))
    inverse_rms = lax.rsqrt(square_sum / full_width + epsilon)
    return ((stream * inverse_rms[:, None] * gain[None, :]).astype(jnp.bfloat16), inverse_rms)


def norm_backward(stream, inverse_rms, gain, grad_normed):
    full_width = stream.shape[1] * lax.axis_size("gy")
    scaled = grad_normed * gain[None, :]
    inner_sum = width_sum(jnp.sum(scaled * stream, axis=1))
    cubed = inverse_rms * inverse_rms * inverse_rms
    grad_stream = inverse_rms[:, None] * scaled - stream * (cubed * inner_sum / full_width)[:, None]
    grad_gain = jnp.sum(grad_normed * stream * inverse_rms[:, None], axis=0)
    return (grad_stream, grad_gain)


def slot_table(route_ids, experts, capacity):
    flat_ids = route_ids.reshape(-1)
    assigned = (flat_ids[:, None] == jnp.arange(experts, dtype=jnp.int32)[None, :]).astype(
        jnp.int32
    )
    earlier = jnp.cumsum(assigned, axis=0) - assigned
    places = flat_ids * capacity + jnp.sum(earlier * assigned, axis=1)
    owners = jnp.arange(flat_ids.shape[0], dtype=jnp.int32) // 2
    slot_token = jnp.zeros((experts * capacity,), jnp.int32).at[places].set(owners)
    slot_valid = jnp.zeros((experts * capacity,), jnp.int32).at[places].set(jnp.ones_like(owners))
    return (places.reshape(-1, 2), slot_token, slot_valid)


def expert_act(gate_up, logits):
    half_size = gate_up.shape[1] // 2
    return (
        jax.nn.silu(gate_up[:, :half_size])
        * gate_up[:, half_size:]
        * jax.nn.sigmoid(logits)[:, None]
    )


def shared_act(gate_up):
    half_size = gate_up.shape[1] // 2
    return jax.nn.silu(gate_up[:, :half_size]) * gate_up[:, half_size:]


def causal_scores(queries, keys_part):
    score_scale = queries.shape[-1] ** (-0.5)
    scores = (
        jnp.einsum("qhd,khd->hqk", queries, keys_part, preferred_element_type=jnp.float32)
        * score_scale
    )
    length = queries.shape[0]
    causal = jnp.arange(length)[:, None] >= jnp.arange(length)[None, :]
    return jnp.where(causal[None], scores, -1e30)


def attend_forward(queries, keys_part, values_part):
    scores = causal_scores(queries, keys_part)
    row_max = jnp.max(scores, axis=-1, keepdims=True)
    exponent = jnp.exp(scores - row_max)
    row_total = jnp.sum(exponent, axis=-1, keepdims=True)
    probabilities = (exponent / row_total).astype(jnp.bfloat16)
    attended = jnp.einsum(
        "hqk,khd->qhd", probabilities, values_part, preferred_element_type=jnp.float32
    )
    return (attended, row_max + jnp.log(row_total))


def attend_backward(queries, keys_part, values_part, log_total, grad_attended):
    score_scale = queries.shape[-1] ** (-0.5)
    probabilities = jnp.exp(causal_scores(queries, keys_part) - log_total)
    grad_values = jnp.einsum(
        "hqk,qhd->khd",
        probabilities.astype(jnp.bfloat16),
        grad_attended,
        preferred_element_type=jnp.float32,
    )
    grad_probs = jnp.einsum(
        "qhd,khd->hqk", grad_attended, values_part, preferred_element_type=jnp.float32
    )
    grad_scores = (
        probabilities * (grad_probs - jnp.sum(grad_probs * probabilities, axis=-1, keepdims=True))
    ).astype(jnp.bfloat16)
    grad_queries = (
        jnp.einsum("hqk,khd->qhd", grad_scores, keys_part, preferred_element_type=jnp.float32)
        * score_scale
    )
    grad_keys = (
        jnp.einsum("hqk,qhd->khd", grad_scores, queries, preferred_element_type=jnp.float32)
        * score_scale
    )
    return (grad_queries, grad_keys, grad_values)


def layer_forward(stream, weights, route_ids):
    (
        attention_gain,
        attention_in,
        attention_out,
        feed_gain,
        router_weight,
        expert_in,
        expert_down,
        shared_in,
        shared_down,
    ) = weights
    local_width = stream.shape[1]
    experts = expert_in.shape[0]
    normed, inverse_first = norm_forward(stream, attention_gain)
    rows_first = token_rows(normed)
    tokens = rows_first.shape[0]
    capacity = 5 * tokens // (2 * experts)
    slot_count = experts * capacity
    projected = sequence_sums(
        jnp.dot(
            rows_first, attention_in.reshape(local_width, -1), preferred_element_type=jnp.float32
        )
    )
    length = projected.shape[0]
    projected = projected.reshape(length, 3, -1, DH)
    positions = jnp.arange(length, dtype=jnp.float32)
    queries = rope_turn(projected[:, 0], positions, 1.0).astype(jnp.bfloat16)
    keys_part = rope_turn(projected[:, 1], positions, 1.0).astype(jnp.bfloat16)
    values_part = projected[:, 2].astype(jnp.bfloat16)
    attended, log_total = attend_forward(queries, keys_part, values_part)
    attended_rows = sequence_rows(attended.astype(jnp.bfloat16).reshape(length, -1))
    middle = stream + output_rows(
        jnp.dot(attended_rows, attention_out, preferred_element_type=jnp.float32)
    )
    normed_feed, inverse_second = norm_forward(middle, feed_gain)
    rows_second = token_rows(normed_feed)
    route_slot, slot_token, slot_valid = slot_table(route_ids, experts, capacity)
    grouped = (rows_second[slot_token] * slot_valid[:, None].astype(jnp.bfloat16)).reshape(
        experts, capacity, local_width
    )
    expert_part = jnp.einsum(
        "ecd,edf->ecf",
        grouped,
        expert_in.reshape(experts, local_width, -1),
        preferred_element_type=jnp.float32,
    )
    router_part = jnp.einsum(
        "ecd,de->ec", grouped, router_weight, preferred_element_type=jnp.float32
    )
    shared_part = jnp.dot(
        rows_second, shared_in.reshape(local_width, -1), preferred_element_type=jnp.float32
    )
    expert_gu, router_logit, shared_gu = (
        lax.psum_scatter(
            expert_part.reshape(slot_count, -1), "gy", scatter_dimension=0, tiled=True
        ),
        lax.psum_scatter(router_part.reshape(slot_count), "gy", scatter_dimension=0, tiled=True),
        lax.psum_scatter(shared_part, "gy", scatter_dimension=0, tiled=True),
    )
    hidden_rows, shared_rows = gather_hidden(
        expert_act(expert_gu, router_logit).astype(jnp.bfloat16),
        shared_act(shared_gu).astype(jnp.bfloat16),
    )
    expert_result = jnp.einsum(
        "ecf,efd->ecd",
        hidden_rows.reshape(experts, capacity, -1),
        expert_down,
        preferred_element_type=jnp.float32,
    ).reshape(slot_count, local_width)
    branch = (
        expert_result[route_slot[:, 0]]
        + expert_result[route_slot[:, 1]]
        + jnp.dot(shared_rows, shared_down, preferred_element_type=jnp.float32)
    )
    result = middle + output_rows(branch)
    kept_items = (
        stream,
        inverse_first,
        rows_first,
        queries,
        keys_part,
        values_part,
        log_total,
        attended_rows,
        middle,
        inverse_second,
        rows_second,
        expert_gu,
        router_logit,
        shared_gu,
    )
    return (result, kept_items)


def layer_backward(grad_out, kept_items, weights, route_ids):
    (
        attention_gain,
        attention_in,
        attention_out,
        feed_gain,
        router_weight,
        expert_in,
        expert_down,
        shared_in,
        shared_down,
    ) = weights
    (
        stream,
        inverse_first,
        rows_first,
        queries,
        keys_part,
        values_part,
        log_total,
        attended_rows,
        middle,
        inverse_second,
        rows_second,
        expert_gu,
        router_logit,
        shared_gu,
    ) = kept_items[:14]
    local_width = stream.shape[1]
    experts = expert_in.shape[0]
    tokens = rows_second.shape[0]
    capacity = 5 * tokens // (2 * experts)
    slot_count = experts * capacity
    hidden_rows, shared_rows = gather_hidden(
        expert_act(expert_gu, router_logit).astype(jnp.bfloat16),
        shared_act(shared_gu).astype(jnp.bfloat16),
    )
    route_slot, slot_token, slot_valid = slot_table(route_ids, experts, capacity)
    valid_rows = slot_valid[:, None].astype(jnp.bfloat16)
    grouped = (rows_second[slot_token] * valid_rows).reshape(experts, capacity, local_width)
    grad_rows = token_rows(grad_out.astype(jnp.bfloat16))
    slot_grad = (grad_rows[slot_token] * valid_rows).reshape(experts, capacity, local_width)
    down_grad = jnp.einsum(
        "ecf,ecd->efd",
        hidden_rows.reshape(experts, capacity, -1),
        slot_grad,
        preferred_element_type=jnp.float32,
    )
    shared_down_grad = jnp.einsum(
        "tf,td->fd", shared_rows, grad_rows, preferred_element_type=jnp.float32
    )
    hidden_part = jnp.einsum(
        "ecd,efd->ecf", slot_grad, expert_down, preferred_element_type=jnp.float32
    ).reshape(slot_count, -1)
    shared_part = jnp.einsum(
        "td,fd->tf", grad_rows, shared_down, preferred_element_type=jnp.float32
    )
    grad_hidden, grad_shared = (
        lax.psum_scatter(
            hidden_part.astype(jnp.bfloat16), "gy", scatter_dimension=0, tiled=True
        ).astype(jnp.float32),
        lax.psum_scatter(
            shared_part.astype(jnp.bfloat16), "gy", scatter_dimension=0, tiled=True
        ).astype(jnp.float32),
    )
    unused_expert, expert_back = jax.vjp(expert_act, expert_gu, router_logit)
    grad_gu, grad_logit = expert_back(grad_hidden)
    unused_shared, shared_back = jax.vjp(shared_act, shared_gu)
    (grad_shared_gu,) = shared_back(grad_shared)
    gu_rows, shared_gu_rows = (
        lax.all_gather(grad_gu.astype(jnp.bfloat16), "gy", axis=0, tiled=True),
        lax.all_gather(grad_shared_gu.astype(jnp.bfloat16), "gy", axis=0, tiled=True),
    )
    logit_rows = lax.all_gather(grad_logit, "gy", axis=0, tiled=True).reshape(experts, capacity)
    gu_grouped = gu_rows.reshape(experts, capacity, -1)
    in_grad = jnp.einsum("ecd,ecf->edf", grouped, gu_grouped, preferred_element_type=jnp.float32)
    router_grad = jnp.einsum(
        "ecd,ec->de", grouped.astype(jnp.float32), logit_rows, precision=highest
    )
    shared_in_grad = jnp.einsum(
        "td,tf->df", rows_second, shared_gu_rows, preferred_element_type=jnp.float32
    )
    slot_back = jnp.einsum(
        "ecf,edf->ecd",
        gu_grouped,
        expert_in.reshape(experts, local_width, -1),
        preferred_element_type=jnp.float32,
    )
    slot_back = slot_back + logit_rows[:, :, None] * router_weight.T.astype(jnp.float32)[:, None, :]
    slot_back = slot_back.reshape(slot_count, local_width)
    rows_back = (
        slot_back[route_slot[:, 0]]
        + slot_back[route_slot[:, 1]]
        + jnp.einsum(
            "tf,df->td",
            shared_gu_rows,
            shared_in.reshape(local_width, -1),
            preferred_element_type=jnp.float32,
        )
    )
    grad_middle_norm, feed_gain_grad = norm_backward(
        middle, inverse_second, feed_gain, output_rows(rows_back)
    )
    grad_middle = grad_out + grad_middle_norm
    middle_rows = token_rows(grad_middle.astype(jnp.bfloat16))
    out_weight_grad = jnp.einsum(
        "tf,td->fd", attended_rows, middle_rows, preferred_element_type=jnp.float32
    )
    grad_attended = sequence_sums(
        jnp.einsum("td,fd->tf", middle_rows, attention_out, preferred_element_type=jnp.float32)
    )
    length = grad_attended.shape[0]
    positions = jnp.arange(length, dtype=jnp.float32)
    grad_queries, grad_keys, grad_values = attend_backward(
        queries,
        keys_part,
        values_part,
        log_total,
        grad_attended.astype(jnp.bfloat16).reshape(queries.shape),
    )
    grad_projected = jnp.stack(
        [
            rope_turn(grad_queries, positions, -1.0),
            rope_turn(grad_keys, positions, -1.0),
            grad_values,
        ],
        axis=1,
    )
    grad_projected = grad_projected.astype(jnp.bfloat16).reshape(length, -1)
    projected_rows = sequence_rows(grad_projected)
    in_weight_grad = jnp.einsum(
        "td,tf->df", rows_first, projected_rows, preferred_element_type=jnp.float32
    )
    grad_normed = output_rows(
        jnp.einsum(
            "tf,df->td",
            projected_rows,
            attention_in.reshape(local_width, -1),
            preferred_element_type=jnp.float32,
        )
    )
    grad_stream_norm, attention_gain_grad = norm_backward(
        stream, inverse_first, attention_gain, grad_normed
    )
    layer_grads = (
        attention_gain_grad,
        in_weight_grad.reshape(attention_in.shape),
        out_weight_grad,
        feed_gain_grad,
        router_grad,
        in_grad.reshape(expert_in.shape),
        down_grad,
        shared_in_grad.reshape(shared_in.shape),
        shared_down_grad,
    )
    return (grad_middle + grad_stream_norm, layer_grads)


def put_item(buffer, value, batch_index, is_valid):
    current = lax.dynamic_index_in_dim(buffer, batch_index, 0, keepdims=False)
    return lax.dynamic_update_index_in_dim(
        buffer, jnp.where(is_valid, value, current), batch_index, 0
    )


def on_device(
    block_input,
    output_grad,
    attention_gain,
    attention_in,
    attention_out,
    feed_gain,
    router_weight,
    expert_in,
    expert_down,
    shared_in,
    shared_down,
    routes,
):
    section_index = lax.axis_index("section")
    batches = block_input.shape[0]
    weights = tuple(
        (
            member[0]
            for member in (
                attention_gain,
                attention_in,
                attention_out,
                feed_gain,
                router_weight,
                expert_in,
                expert_down,
                shared_in,
                shared_down,
            )
        )
    )
    route_table = routes[0]
    outputs = jnp.zeros(block_input.shape, jnp.bfloat16)
    received = jnp.zeros(block_input.shape[1:], jnp.bfloat16)
    stored = None
    for tick_step in range(batches + 1):
        micro_index = tick_step - section_index
        is_valid = (micro_index >= 0) & (micro_index < batches)
        batch_index = jnp.clip(micro_index, 0, batches - 1)
        fresh_input = lax.dynamic_index_in_dim(block_input, batch_index, 0, keepdims=False)
        incoming = jnp.where(section_index == 0, fresh_input, received).astype(jnp.float32)
        route_ids = lax.dynamic_index_in_dim(route_table, batch_index, 0, keepdims=False)
        result, kept_items = layer_forward(incoming, weights, route_ids)
        result_low = result.astype(jnp.bfloat16)
        outputs = put_item(outputs, result_low, batch_index, is_valid)
        if stored is None:
            stored = tuple(
                (jnp.zeros((batches,) + member.shape, member.dtype) for member in kept_items)
            )
        stored = tuple(
            (
                put_item(buffer, member, batch_index, is_valid)
                for buffer, member in zip(stored, kept_items)
            )
        )
        if tick_step < batches:
            received = pass_section(result_low)
    grads_in = jnp.zeros(block_input.shape, jnp.bfloat16)
    received = jnp.zeros(block_input.shape[1:], jnp.bfloat16)
    totals = tuple((jnp.zeros(member.shape, jnp.float32) for member in weights))
    for tick_step in range(batches + 1):
        micro_index = batches - tick_step - section_index
        is_valid = (micro_index >= 0) & (micro_index < batches)
        batch_index = jnp.clip(micro_index, 0, batches - 1)
        given_grad = lax.dynamic_index_in_dim(output_grad, batch_index, 0, keepdims=False)
        incoming = jnp.where(section_index == 1, given_grad, received).astype(jnp.float32)
        kept_items = tuple(
            (lax.dynamic_index_in_dim(buffer, batch_index, 0, keepdims=False) for buffer in stored)
        )
        route_ids = lax.dynamic_index_in_dim(route_table, batch_index, 0, keepdims=False)
        grad_input, layer_grads = layer_backward(incoming, kept_items, weights, route_ids)
        grad_low = grad_input.astype(jnp.bfloat16)
        grads_in = put_item(grads_in, grad_low, batch_index, is_valid)
        totals = tuple(
            (total + jnp.where(is_valid, member, 0.0) for total, member in zip(totals, layer_grads))
        )
        if tick_step < batches:
            received = pass_section(grad_low)
    gain_first, gain_second, router_total = lax.psum((totals[0], totals[3], totals[4]), "gx")
    return (
        outputs[None],
        grads_in[None],
        gain_first[None],
        totals[1][None],
        totals[2][None],
        gain_second[None],
        router_total[None],
        totals[5][None],
        totals[6][None],
        totals[7][None],
        totals[8][None],
    )


def lanes_up(n):
    return -(-n // 128) * 128


def rot_columns(w):
    shape = w.shape
    w = w.reshape(shape[:-1] + (-1, 2, DH // 2))
    w = jnp.stack([-w[..., 1, :], w[..., 0, :]], axis=-2)
    return w.reshape(shape)


def pad_to(v, axis, n):
    pads = [(0, 0)] * v.ndim
    pads[axis] = (0, n - v.shape[axis])
    return jnp.pad(v, pads)


def mm(a, b, dims=((1,), (0,))):
    return lax.dot_general(a, b, (dims, ((), ())), preferred_element_type=jnp.float32)


def bf(v):
    return v.astype(jnp.bfloat16)


def emu_gather_gx(v, mbs):
    rows = v.shape[0] // mbs
    g = lax.all_gather(v.reshape(mbs, rows, -1), "gx")
    return jnp.moveaxis(g, 0, 1).reshape(mbs * 4 * rows, -1)


def emu_scatter_gx(v, mbs):
    n = lax.axis_size("gx")
    rows = v.shape[0] // mbs // n
    v = bf(v).astype(jnp.float32).reshape(mbs, n, rows, -1)
    v = lax.psum_scatter(v, "gx", scatter_dimension=1, tiled=False)
    return v.reshape(mbs * rows, -1)


def head_mask(pw, h):
    lane = lax.broadcasted_iota(jnp.int32, (1, pw), 1)
    return (lane >= h * DH) & (lane < (h + 1) * DH)


def rms(x, features):
    return lax.rsqrt(jnp.sum(x * x, axis=1, keepdims=True) / features + epsilon)


def norm_back(x, inv, gain, d, features):
    u = d * gain
    inner = jnp.sum(u * x, axis=1, keepdims=True) / features
    dx = inv * u - x * (inv * inv * inv * inner)
    return dx, jnp.sum(d * x * inv, axis=0, keepdims=True)


def emu_attn_fwd(x, gain, wqkv, wout, fgain, rwx, cos, sin, mbs, heads, features):
    pw = cos.shape[1]
    n1 = bf(x * rms(x, features) * gain)
    rows = emu_gather_gx(n1, mbs)
    proj = mm(rows, wqkv)
    length = rows.shape[0] // mbs
    cos2 = jnp.concatenate([cos] * mbs, 0)
    sin2 = jnp.concatenate([sin] * mbs, 0)
    q = bf(proj[:, :pw] * cos2 + proj[:, 3 * pw : 4 * pw] * sin2)
    k = bf(proj[:, pw : 2 * pw] * cos2 + proj[:, 4 * pw : 5 * pw] * sin2)
    v = bf(proj[:, 2 * pw : 3 * pw])
    outs = []
    for m in range(mbs):
        rs = slice(m * length, (m + 1) * length)
        acc = jnp.zeros((length, pw), jnp.float32)
        for h in range(heads):
            mask = head_mask(pw, h)
            p = probs_of(jnp.where(mask, q[rs], 0), k[rs])
            acc = acc + mm(bf(p), jnp.where(mask, v[rs], 0))
        outs.append(acc)
    att = bf(jnp.concatenate(outs, 0))
    mid = x + emu_scatter_gx(mm(att, wout), mbs)
    n2 = bf(mid * rms(mid, features) * fgain)
    rx = mm(n2, rwx)
    return mid, n2, rx, rows, q, k, v, att


def probs_of(q, k):
    s = mm(q, k, ((1,), (1,))) * DH ** -0.5
    n = s.shape[0]
    causal = lax.broadcasted_iota(jnp.int32, (n, n), 0) >= lax.broadcasted_iota(jnp.int32, (n, n), 1)
    s = jnp.where(causal, s, -1e30)
    e = jnp.exp(s - jnp.max(s, axis=1, keepdims=True))
    return e / jnp.sum(e, axis=1, keepdims=True)


def emu_attn_bwd(dn2, g, mid, fgain, x, gain, rows, q, k, v, att, wqkv, wout, cos, sin, rot, mbs, heads, features):
    pw = cos.shape[1]
    dx2, fgain_grad = norm_back(mid, rms(mid, features), fgain, dn2, features)
    dm = g + dx2
    dmr = emu_gather_gx(bf(dm), mbs)
    wout_grad = mm(att, dmr, ((0,), (0,)))
    datt = bf(mm(dmr, wout, ((1,), (1,))))
    length = rows.shape[0] // mbs
    parts = []
    for m in range(mbs):
        rs = slice(m * length, (m + 1) * length)
        dq = jnp.zeros((length, pw), jnp.float32)
        dk = dq
        dv = dq
        for h in range(heads):
            mask = head_mask(pw, h)
            qh = jnp.where(mask, q[rs], 0)
            kh = jnp.where(mask, k[rs], 0)
            da = jnp.where(mask, datt[rs], 0)
            p = probs_of(qh, k[rs])
            dp = mm(da, v[rs], ((1,), (1,)))
            ds = bf(p * (dp - jnp.sum(dp * p, axis=1, keepdims=True)))
            dv = dv + mm(bf(p), da, ((0,), (0,)))
            dq = dq + mm(ds, kh) * DH ** -0.5
            dk = dk + mm(ds, qh, ((0,), (0,))) * DH ** -0.5

        def back(t):
            hi = bf(t)
            lo = bf(t - hi.astype(jnp.float32))
            return t * cos - (mm(hi, rot) + mm(lo, rot)) * sin

        parts.append(jnp.concatenate([bf(back(dq)), bf(back(dk)), bf(dv)], 1))
    dqkv = jnp.concatenate(parts, 0)
    wqkv_grad = mm(rows, dqkv, ((0,), (0,)))
    dn1 = emu_scatter_gx(mm(dqkv, wqkv[:, : 3 * pw], ((1,), (1,))), mbs)
    dx1, gain_grad = norm_back(x, rms(x, features), gain, dn1, features)
    return dm + dx1, wqkv_grad, wout_grad, gain_grad, fgain_grad


def emu_spread(v, mbs, pw):
    n = lax.axis_size("gy")
    rows = v.shape[0] // mbs
    t = lax.all_to_all(v.reshape(mbs, rows, n, pw), "gy", split_axis=2, concat_axis=0, tiled=False)
    t = lax.all_gather(t, "gx")
    return t.transpose(2, 1, 0, 3, 4).reshape(mbs, -1, pw)


def emu_return(v, mbs):
    nx, ny = lax.axis_size("gx"), lax.axis_size("gy")
    pw = v.shape[-1]
    t = bf(v).astype(jnp.float32).reshape(mbs, ny, nx, -1, pw)
    t = lax.psum_scatter(t, "gx", scatter_dimension=2, tiled=False)
    rows = t.shape[2]
    t = lax.all_to_all(t, "gy", split_axis=1, concat_axis=0, tiled=False)
    return t.transpose(1, 2, 0, 3).reshape(mbs * rows, ny * pw)


def place_matrix(place_row, slots):
    i = lax.broadcasted_iota(jnp.int32, (slots, place_row.shape[1]), 0)
    return bf(((place_row[0:1] == i) | (place_row[1:2] == i)).astype(jnp.float32))


def ext_block(n2, rx, j, width, pw, experts):
    lane = lax.broadcasted_iota(jnp.int32, (1, pw), 1)
    hi = bf(rx)
    lo = bf(rx - hi.astype(jnp.float32))
    v = jnp.where(lane < width + experts, hi, lo)
    return jnp.where(lane < width, n2[:, j * pw : (j + 1) * pw], v)


def emu_ff_fwd(mid, n2, rx, place, win, wdt, sin_w, sdt, mbs, dims):
    width, pw, experts, cap = dims
    f = wdt.shape[-1]
    xe = jnp.concatenate([ext_block(n2, rx, j, width, pw, experts) for j in range(4)], 1)
    xs_all = emu_spread(xe, mbs, pw)
    slots_all, gu_all, hid_all, branch = [], [], [], []
    for m in range(mbs):
        pm = place_matrix(place[m], experts * cap)
        slots = bf(mm(pm, xs_all[m]))
        se = slots.reshape(experts, cap, pw)
        gu = jnp.einsum("ecd,edf->ecf", se[..., :width], win, preferred_element_type=jnp.float32)
        gu = lax.psum(bf(gu).astype(jnp.float32), "gy")
        lane = lax.broadcasted_iota(jnp.int32, (experts, 1, pw), 2)
        ex = lax.broadcasted_iota(jnp.int32, (experts, 1, pw), 0)
        rmask = (lane == width + ex) | (lane == width + experts + ex)
        r = jnp.sum(jnp.where(rmask, se.astype(jnp.float32), 0), -1, keepdims=True)
        hid = bf(jax.nn.silu(gu[..., :f]) * gu[..., f:] * jax.nn.sigmoid(r))
        eo = bf(jnp.einsum("ecf,edf->ecd", hid, wdt, preferred_element_type=jnp.float32)).reshape(-1, width)
        branch.append(pad_to(mm(pm, eo, ((0,), (0,))), 1, pw))
        slots_all.append(se)
        gu_all.append(bf(gu))
        hid_all.append(hid)
    ret = emu_return(jnp.stack(branch), mbs)
    rows2 = emu_gather_gx(n2, mbs)
    sgu = mm(rows2, sin_w)
    shid = bf(jax.nn.silu(sgu[:, :f]) * sgu[:, f:])
    sout = emu_scatter_gx(mm(shid, sdt, ((1,), (1,))), mbs)
    out = mid + ret + sout
    return out, (jnp.stack(slots_all), jnp.stack(gu_all), jnp.stack(hid_all), rows2, bf(sgu), shid)


def emu_ff_bwd(g, kept, n2, place, win, wdt, sin_w, sdt, rwx, mbs, dims):
    width, pw, experts, cap = dims
    slots_all, gu_all, hid_all, rows2, sgu, shid = kept
    f = wdt.shape[-1]
    gb = bf(g)
    g_all = emu_spread(gb, mbs, pw)
    comb = []
    win_grad = jnp.zeros((experts, width, 2 * f), jnp.float32)
    wdt_grad = jnp.zeros((experts, width, f), jnp.float32)
    for m in range(mbs):
        pm = place_matrix(place[m], experts * cap)
        gs = bf(mm(pm, g_all[m])).reshape(experts, cap, pw)[..., :width]
        dh = jnp.einsum("ecd,edf->ecf", gs, wdt, preferred_element_type=jnp.float32)
        dh = lax.psum(bf(dh).astype(jnp.float32), "gy")
        gu = gu_all[m].astype(jnp.float32)
        se = slots_all[m]
        lane = lax.broadcasted_iota(jnp.int32, (experts, 1, pw), 2)
        ex = lax.broadcasted_iota(jnp.int32, (experts, 1, pw), 0)
        rmask = (lane == width + ex) | (lane == width + experts + ex)
        r = jnp.sum(jnp.where(rmask, se.astype(jnp.float32), 0), -1, keepdims=True)
        gate, up = gu[..., :f], gu[..., f:]
        dgate, dup, dr = act_back(gate, up, dh, jax.nn.sigmoid(r))
        dgu = jnp.concatenate([bf(dgate), bf(dup)], -1)
        dslot = jnp.einsum("ecf,edf->ecd", dgu, win, preferred_element_type=jnp.float32)
        dslot = pad_to(dslot, 2, pw)
        hi = bf(dr).astype(jnp.float32)
        owner = (lax.axis_index("gy") == 0).astype(jnp.float32)
        dslot = dslot + owner * jnp.where(lane == width + ex, hi, jnp.where(lane == width + experts + ex, dr - hi, 0.0))
        comb.append(mm(pm, bf(dslot).reshape(-1, pw), ((0,), (0,))))
        win_grad = win_grad + jnp.einsum("ecd,ecf->edf", se[..., :width], dgu, preferred_element_type=jnp.float32)
        wdt_grad = wdt_grad + jnp.einsum("ecd,ecf->edf", gs, hid_all[m], preferred_element_type=jnp.float32)
    ret = emu_return(jnp.stack(comb), mbs)
    g_rows = emu_gather_gx(gb, mbs)
    dsh = mm(g_rows, sdt)
    sgu_f = sgu.astype(jnp.float32)
    dsg, dsu, _ = act_back(sgu_f[:, :f], sgu_f[:, f:], dsh, None)
    dsgu = jnp.concatenate([bf(dsg), bf(dsu)], 1)
    sin_grad = mm(rows2, dsgu, ((0,), (0,)))
    sdt_grad = mm(g_rows, shid, ((0,), (0,)))
    sback = emu_scatter_gx(mm(dsgu, sin_w, ((1,), (1,))), mbs)
    dn2, rw_grad = router_back(ret, n2, rwx, width, pw)
    return dn2 + sback, win_grad, wdt_grad, sin_grad, sdt_grad, rw_grad


def router_back(ret, n2, rwx, width, pw):
    lane = lax.broadcasted_iota(jnp.int32, (1, ret.shape[1]), 1)
    ret_x = sum(ret[:, j * pw : (j + 1) * pw] for j in range(ret.shape[1] // pw))
    lane1 = lax.broadcasted_iota(jnp.int32, (1, pw), 1)
    dlog = jnp.where(lane1 >= width, ret_x, 0.0)
    hi = bf(dlog)
    lo = bf(dlog - hi.astype(jnp.float32))
    main = jnp.where(lane % pw < width, ret, 0.0)
    dn2 = main + mm(hi, rwx, ((1,), (1,))) + mm(lo, rwx, ((1,), (1,)))
    rw_grad = mm(n2, hi, ((0,), (0,))) + mm(n2, lo, ((0,), (0,)))
    return dn2, rw_grad


def act_back(gate, up, dh, s):
    sg = jax.nn.sigmoid(gate)
    silu = gate * sg
    if s is None:
        return dh * up * (sg * (1.0 + gate * (1.0 - sg))), dh * silu, None
    dr = jnp.sum(dh * silu * up, axis=-1, keepdims=True) * s * (1.0 - s)
    ds = dh * s
    return ds * up * (sg * (1.0 + gate * (1.0 - sg))), ds * silu, dr


def places_of(routes, experts, capacity):
    lead = routes.shape[:-2]
    ids = routes.reshape((-1, routes.shape[-2] * 2))
    n = ids.shape[1]
    hot = (ids[..., None] == jnp.arange(experts, dtype=jnp.int32)).astype(jnp.bfloat16)
    before = (jnp.arange(n)[:, None] > jnp.arange(n)[None, :]).astype(jnp.bfloat16)
    earlier = jnp.einsum("ij,bje->bie", before, hot, preferred_element_type=jnp.float32)
    rank = jnp.sum(earlier * hot.astype(jnp.float32), -1).astype(jnp.int32)
    place = (ids * capacity + rank).reshape(lead + (-1, 2))
    return jnp.moveaxis(place, -1, -2)


def fast_device(block_input, output_grad, attention_gain, attention_in, attention_out, feed_gain,
                router_weight, expert_in, expert_down, shared_in, shared_down, routes):
    s = lax.axis_index("section")
    a = lax.axis_index("gx")
    b = lax.axis_index("gy")
    ny = lax.axis_size("gy")
    nx = lax.axis_size("gx")
    mbs = block_input.shape[0] // 2
    width = block_input.shape[2]
    features = width * ny
    experts = expert_in.shape[1]
    f = expert_in.shape[-1]
    pw = lanes_up(width + 2 * experts)
    tokens = routes.shape[2]
    cap = 5 * tokens // (2 * experts)
    sub = tokens // (nx * ny)
    heads = attention_in.shape[-1] // DH
    dims = (width, pw, experts, cap)
    length = sub * nx

    def both(v):
        other = pass_section(v)
        return jnp.where(s == 0, v, other), jnp.where(s == 0, other, v)

    def wide(v, axis):
        v = pad_to(v, axis, pw)
        return lax.all_gather(v, "gy", axis=axis, tiled=True)

    ai = wide(attention_in[0], 0)
    rotq = rot_columns(ai[:, :2])
    ai = pad_to(jnp.concatenate([ai, rotq], 1), 2, pw).reshape(ny * pw, 5 * pw)
    wqkv = both(ai)
    wout = both(pad_to(wide(attention_out[0], 1), 0, pw))
    gain = both(wide(attention_gain, 1))
    fgain = both(wide(feed_gain, 1))
    rwx = wide(router_weight[0], 0)
    rwx = jnp.concatenate([jnp.zeros((ny * pw, width), jnp.bfloat16), rwx, rwx], 1)
    rwx = both(pad_to(rwx, 1, pw))
    win_pair = (expert_in[0].reshape(experts, width, 2 * f),)
    win_pair = win_pair + (pass_section(win_pair[0]),)
    wdt_pair = (expert_down[0].transpose(0, 2, 1),)
    wdt_pair = wdt_pair + (pass_section(wdt_pair[0]),)
    sin_w = both(wide(shared_in[0].reshape(width, 2 * f), 0))
    sdt = both(wide(shared_down[0].T, 0))
    place = places_of(jnp.stack([lax.dynamic_slice_in_dim(r, s * mbs, mbs, 0) for r in both(routes[0])]), experts, cap)

    def tokens_in(v):
        t = lax.dynamic_slice_in_dim(v, s * mbs, mbs, 0)
        t = lax.all_gather(t, "gx", axis=1, tiled=True)
        t = lax.all_gather(pad_to(t, 2, pw), "gy", axis=2, tiled=True)
        t = lax.dynamic_slice_in_dim(t, b * length + a * sub, sub, 1)
        return t.reshape(mbs * sub, ny * pw).astype(jnp.float32)

    def tokens_out(pair):
        v0, v1 = pair
        keep = jnp.where(s == 0, v0, v1)
        send = jnp.where(s == 0, v1, v0)
        got = pass_section(send)
        both_mb = jnp.where(s == 0, jnp.stack([keep, got]), jnp.stack([got, keep]))
        t = bf(both_mb).reshape(2 * mbs, sub, ny, pw)[..., :width]
        t = lax.all_gather(t, "gx", axis=1, tiled=True)
        t = lax.all_gather(t, "gy", axis=1, tiled=True)
        t = lax.dynamic_slice_in_dim(t, a * (tokens // nx), tokens // nx, 1)
        return lax.dynamic_index_in_dim(t, b, 2, keepdims=False)[None]

    half = DH // 2
    freq = 10000.0 ** (-jnp.arange(half, dtype=jnp.float32) / half)
    ang = jnp.arange(length, dtype=jnp.float32)[:, None] * freq[None]
    lanes = jnp.tile(ang, (1, 2 * heads))
    cos = pad_to(jnp.cos(lanes), 1, pw)
    sin = pad_to(jnp.sin(lanes), 1, pw)
    rot = pad_to(pad_to(rot_columns(jnp.eye(heads * DH, dtype=jnp.float32)), 0, pw), 1, pw).astype(jnp.bfloat16)

    x = tokens_in(block_input)
    kept, outs = [], []
    for l in range(2):
        mid, n2, rx, rows, q, k, v, att = emu_attn_fwd(
            x, gain[l], wqkv[l], wout[l], fgain[l], rwx[l], cos, sin, mbs, heads, features)
        out, ff = ff_fwd(l, mid, n2, rx, place[l], win_pair, wdt_pair, sin_w[l], sdt[l], mbs, dims, l)
        kept.append((x, mid, n2, rows, q, k, v, att, ff))
        x = bf(out).astype(jnp.float32)
        outs.append(x)
    g = tokens_in(output_grad)
    gouts, grads = [None, None], [None, None]
    expert_grads = (jnp.zeros((experts, width, 2 * f), jnp.float32), jnp.zeros((experts, width, f), jnp.float32))
    for l in (1, 0):
        x, mid, n2, rows, q, k, v, att, ff = kept[l]
        dn2, expert_grads, sin_g, sdt_g, rw_g = ff_bwd(
            l, g, ff, n2, place[l], win_pair, wdt_pair, sin_w[l], sdt[l], rwx[l], expert_grads, mbs, dims, 2 + l)
        dx, wqkv_g, wout_g, gain_g, fgain_g = emu_attn_bwd(
            dn2, g, mid, fgain[l], x, gain[l], rows, q, k, v, att, wqkv[l], wout[l], cos, sin, rot, mbs, heads, features)
        g = bf(dx).astype(jnp.float32)
        gouts[l] = g
        grads[l] = (gain_g, wqkv_g, wout_g, fgain_g, rw_g, sin_g.astype(jnp.float32), sdt_g.astype(jnp.float32))

    own = [jnp.where(s == 0, p, q_) for p, q_ in zip(*grads)]
    other = [jnp.where(s == 0, q_, p) for p, q_ in zip(*grads)]
    own = [p + pass_section(q_) for p, q_ in zip(own, other)]
    gain_g, wqkv_g, wout_g, fgain_g, rw_g, sin_g, sdt_g = own
    win_g, wdt_g = expert_grads

    def narrow(v, axis):
        v = lax.psum_scatter(v, "gy", scatter_dimension=axis, tiled=True)
        return lax.slice_in_dim(v, 0, width, axis=axis)

    gain_g, fgain_g, rw_g = lax.psum((gain_g, fgain_g, rw_g), "gx")
    rw_g = rw_g[:, width : width + experts] + rw_g[:, width + experts : width + 2 * experts]
    hd = heads * DH
    return (
        tokens_out(outs),
        tokens_out(gouts),
        narrow(gain_g, 1),
        narrow(wqkv_g, 0).reshape(width, 3, pw)[..., :hd][None],
        narrow(wout_g, 1)[:hd][None],
        narrow(fgain_g, 1),
        narrow(rw_g, 0)[None],
        win_g.reshape(experts, width, 2, f)[None],
        wdt_g.transpose(0, 2, 1)[None],
        narrow(sin_g, 0).reshape(width, 2, f)[None],
        narrow(sdt_g, 0).T[None],
    )


MESH = pl.DeviceIdType.MESH
VMEM_BYTES = 60 * 2**20


def greet(targets):
    barrier = pltpu.get_barrier_semaphore()
    for target in targets:
        pl.semaphore_signal(barrier, inc=1, device_id=target, device_id_type=MESH)
    return barrier


def remote(src, dst, send, recv, target):
    return pltpu.make_async_remote_copy(
        src_ref=src, dst_ref=dst, send_sem=send, recv_sem=recv, device_id=target, device_id_type=MESH
    )


def router_column(rows, e, width, experts):
    lane = lax.broadcasted_iota(jnp.int32, rows.shape, rows.ndim - 1)
    mask = (lane == width + e) | (lane == width + experts + e)
    return jnp.sum(jnp.where(mask, rows.astype(jnp.float32), 0.0), axis=-1, keepdims=True)


class Position:
    def __init__(self, nx, ny):
        self.s = lax.axis_index("section")
        self.a = lax.axis_index("gx")
        self.b = lax.axis_index("gy")
        self.nx, self.ny = nx, ny
        self.n = nx * ny
        self.me = self.a * ny + self.b

    def device(self, index):
        return (self.s, index // self.ny, lax.rem(index, self.ny))

    def others(self, do):
        def step(i, c):
            index = lax.rem(self.me + i, self.n)
            do(index, index // self.ny, lax.rem(index, self.ny))
            return c

        lax.fori_loop(1, self.n, step, 0)

    def peers(self, do):
        for i in range(1, self.nx):
            do(lax.rem(self.a + i, self.nx))


def greet_section(pos):
    barrier = pltpu.get_barrier_semaphore()

    def one(index, ai, bi):
        pl.semaphore_signal(barrier, inc=1, device_id=(pos.s, ai, bi), device_id_type=MESH)

    pos.others(one)
    return barrier


def ff_fwd_kernel(cfg, mid, n2, rx, place, place_t, win_a, win_b, wdt_a, wdt_b, sin_w, sdt,
                  out, slots_o, gu_o, hid_o, rows_o, sgu_o, shid_o,
                  win, wdt, xsend, xall, nrows, pm, pt, slots, acc, gu, hid, eo, shid, rsend, rrecv, ssend, srecv,
                  w_sem, x_send, x_recv, n_send, n_recv, rs_send, rs_recv, ag_send, ag_recv,
                  r_send, r_recv, s_send, s_recv, o_sem):
    layer, nx, ny, mbs, sub, width, pw, experts, cap, f, sk, ak = cfg
    pos = Position(nx, ny)
    s, a, b, me = pos.s, pos.a, pos.b, pos.me
    slots_n = experts * cap
    tokens = nx * ny * sub
    d = ny * pw
    barrier = greet_section(pos)

    for j, (dst, own, oth) in enumerate(((win, win_a, win_b), (wdt, wdt_a, wdt_b))):
        @pl.when(s == layer)
        def _():
            pltpu.make_async_copy(own, dst, w_sem.at[j]).start()

        @pl.when(s != layer)
        def _():
            pltpu.make_async_copy(oth, dst, w_sem.at[j]).start()

    lane = lax.broadcasted_iota(jnp.int32, (1, pw), 1)
    rv = rx[...]
    hi = bf(rv)
    lo = bf(rv - hi.astype(jnp.float32))
    tail = jnp.where(lane < width + experts, hi, lo)
    for j in range(ny):
        block = jnp.where(lane < width, n2[...].reshape(mbs * sub, d)[:, j * pw : (j + 1) * pw], tail)
        xsend[j] = block.reshape(mbs, sub, pw)
    pl.semaphore_wait(barrier, pos.n - 1)

    def send_x(index, ai, bi):
        remote(xsend.at[bi], xall.at[:, b, a], x_send.at[index], x_recv.at[me], (s, ai, bi)).start()

    pos.others(send_x)

    def send_n(ai):
        remote(n2, nrows.at[:, a], n_send.at[ai], n_recv.at[a], (s, ai, b)).start()

    pos.peers(send_n)
    xall[:, b, a] = xsend[b]
    nrows[:, a] = n2[...]

    for m in range(mbs):
        i0 = lax.broadcasted_iota(jnp.int32, (slots_n, tokens), 0)
        pm[m] = bf(((place[m, 0:1] == i0) | (place[m, 1:2] == i0)).astype(jnp.float32))
        i1 = lax.broadcasted_iota(jnp.int32, (tokens, slots_n), 1)
        pt[m] = bf(((place_t[m, :, 0:1] == i1) | (place_t[m, :, 1:2] == i1)).astype(jnp.float32))

    def wait_x(index, ai, bi):
        remote(xsend.at[0], xall.at[:, bi, ai], x_send.at[index], x_recv.at[index], (s, ai, bi)).wait()

    pos.others(wait_x)
    for m in range(mbs):
        slots[m] = bf(mm(pm[m], xall[m].reshape(tokens, pw))).reshape(experts, cap, pw)
    for j, (dst, own) in enumerate(((win, win_a), (wdt, wdt_a))):
        pltpu.make_async_copy(own, dst, w_sem.at[j]).wait()
    pltpu.make_async_copy(slots, slots_o, o_sem.at[0]).start()

    def gu_copy(m, e):
        to = b - 1 if m == 0 else b + 1
        return remote(gu.at[m, e], gu.at[m, e], rs_send.at[m, e], rs_recv.at[m, e], (s, a, to))

    def hid_copy(m, e):
        to = b + 1 if m == 0 else b - 1
        return remote(hid.at[m, e], hid.at[m, e], ag_send.at[m, e], ag_recv.at[m, e], (s, a, to))

    first = (b == ny - 1, b == 0)
    last = (b == 0, b == ny - 1)

    up = (ny - 1 - b, b)
    down = (b, ny - 1 - b)

    def step(i, c):
        for m in range(mbs):
            e0 = i - sk * up[m]

            @pl.when((e0 >= 0) & (e0 < experts))
            def _():
                e = jnp.clip(e0, 0, experts - 1)
                acc[m] = mm(slots[m, e, :, :width], win[e])

                @pl.when(jnp.logical_not(first[m]))
                def _():
                    gu_copy(m, e).wait_recv()
                    acc[m] += gu[m, e].astype(jnp.float32)

                gu[m, e] = bf(acc[m])

                @pl.when(jnp.logical_not(last[m]))
                def _():
                    gu_copy(m, e).start()

                @pl.when(last[m])
                def _():
                    r = router_column(slots[m, e], e, width, experts)
                    gate = acc[m, :, :f]
                    hid[m, e] = bf(gate * jax.nn.sigmoid(gate) * acc[m, :, f:] * jax.nn.sigmoid(r))
                    hid_copy(m, e).start()

        for m in range(mbs):
            e1 = i - sk * (ny - 1) - ak * down[m]

            @pl.when((e1 >= 0) & (e1 < experts))
            def _():
                e = jnp.clip(e1, 0, experts - 1)

                @pl.when(jnp.logical_not(last[m]))
                def _():
                    hid_copy(m, e).wait_recv()

                    @pl.when(jnp.logical_not(first[m]))
                    def _():
                        hid_copy(m, e).start()

                eo[m, e] = bf(mm(hid[m, e], wdt[e], ((1,), (1,))))

        return c

    lax.fori_loop(0, experts + (sk + ak) * (ny - 1), step, 0)

    def wait_n(ai):
        remote(n2, nrows.at[:, ai], n_send.at[ai], n_recv.at[ai], (s, ai, b)).wait()

    for m in range(mbs):
        @pl.when(last[m])
        def _():
            pltpu.make_async_copy(gu.at[m], gu_o.at[m], o_sem.at[1]).start()

    pltpu.make_async_copy(hid, hid_o, o_sem.at[2]).start()
    for m in range(mbs):
        br = mm(pt[m], eo[m].reshape(slots_n, width))
        rsend[m, ..., :width] = bf(br).reshape(ny, nx, sub, width)

    def send_r(index, ai, bi):
        remote(rsend.at[:, bi, ai], rrecv.at[a, b], r_send.at[index], r_recv.at[me], (s, ai, bi)).start()

    pos.others(send_r)
    rrecv[a, b] = rsend[:, b, a]

    pos.peers(wait_n)
    sgu = mm(nrows[...].reshape(mbs * nx * sub, d), sin_w[...])
    sgu_o[...] = bf(sgu)
    gate = sgu[:, :f]
    shid[...] = bf(gate * jax.nn.sigmoid(gate) * sgu[:, f:])
    shid_o[...] = shid[...]
    rows_o[...] = nrows[...]
    ssend[...] = bf(mm(shid[...], sdt[...], ((1,), (1,)))).reshape(mbs, nx, sub, d)

    def send_s(ai):
        remote(ssend.at[:, ai], srecv.at[a], s_send.at[ai], s_recv.at[a], (s, ai, b)).start()

    pos.peers(send_s)
    srecv[a] = ssend[:, a]

    def wait_s(ai):
        remote(ssend.at[:, ai], srecv.at[ai], s_send.at[ai], s_recv.at[ai], (s, ai, b)).wait()

    pos.peers(wait_s)

    def wait_r(index, ai, bi):
        remote(rsend.at[:, bi, ai], rrecv.at[ai, bi], r_send.at[index], r_recv.at[index], (s, ai, bi)).wait()

    pos.others(wait_r)
    total = mid[...]
    for ai in range(nx):
        total = total + srecv[ai].astype(jnp.float32)
    for j in range(ny):
        part = total[:, :, j * pw : (j + 1) * pw]
        for ai in range(nx):
            part = part + jnp.where(lane < width, rrecv[ai, j].astype(jnp.float32), 0.0)
        out[:, :, j * pw : (j + 1) * pw] = part

    def finish(e, c):
        for m in range(mbs):
            @pl.when(jnp.logical_not(last[m]))
            def _():
                gu_copy(m, e).wait_send()

            @pl.when(jnp.logical_not(first[m]))
            def _():
                hid_copy(m, e).wait_send()

        return c

    lax.fori_loop(0, experts, finish, 0)
    for m in range(mbs):
        @pl.when(last[m])
        def _():
            pltpu.make_async_copy(gu.at[m], gu_o.at[m], o_sem.at[1]).wait()

    pltpu.make_async_copy(hid, hid_o, o_sem.at[2]).wait()
    pltpu.make_async_copy(slots, slots_o, o_sem.at[0]).wait()


def ff_fwd(layer, mid, n2, rx, place, win, wdt, sin_w, sdt, mbs, dims, ids):
    width, pw, experts, cap = dims
    nx, ny = lax.axis_size("gx"), lax.axis_size("gy")
    f = wdt[0].shape[-1]
    d = ny * pw
    sub = n2.shape[0] // mbs
    tokens = nx * ny * sub
    slots = experts * cap
    cfg = (layer, nx, ny, mbs, sub, width, pw, experts, cap, f, *FWD_SKEW)
    vm = pl.BlockSpec(memory_space=pltpu.VMEM)
    hbm = pl.BlockSpec(memory_space=pl.ANY)
    b16, f32 = jnp.bfloat16, jnp.float32
    dma = pltpu.SemaphoreType.DMA
    n = nx * ny
    outs = pl.pallas_call(
        functools.partial(ff_fwd_kernel, cfg),
        out_shape=(
            jax.ShapeDtypeStruct((mbs, sub, d), f32),
            jax.ShapeDtypeStruct((mbs, experts, cap, pw), b16),
            jax.ShapeDtypeStruct((mbs, experts, cap, 2 * f), b16),
            jax.ShapeDtypeStruct((mbs, experts, cap, f), b16),
            jax.ShapeDtypeStruct((mbs, nx, sub, d), b16),
            jax.ShapeDtypeStruct((mbs * nx * sub, 2 * f), b16),
            jax.ShapeDtypeStruct((mbs * nx * sub, f), b16),
        ),
        in_specs=[vm] * 5 + [hbm] * 4 + [vm] * 2,
        out_specs=(vm, hbm, hbm, hbm, vm, vm, vm),
        scratch_shapes=[
            pltpu.VMEM((experts, width, 2 * f), b16),
            pltpu.VMEM((experts, width, f), b16),
            pltpu.VMEM((ny, mbs, sub, pw), b16),
            pltpu.VMEM((mbs, ny, nx, sub, pw), b16),
            pltpu.VMEM((mbs, nx, sub, d), b16),
            pltpu.VMEM((mbs, slots, tokens), b16),
            pltpu.VMEM((mbs, tokens, slots), b16),
            pltpu.VMEM((mbs, experts, cap, pw), b16),
            pltpu.VMEM((mbs, cap, 2 * f), f32),
            pltpu.VMEM((mbs, experts, cap, 2 * f), b16),
            pltpu.VMEM((mbs, experts, cap, f), b16),
            pltpu.VMEM((mbs, experts, cap, width), b16),
            pltpu.VMEM((mbs * nx * sub, f), b16),
            pltpu.VMEM((mbs, ny, nx, sub, pw), b16),
            pltpu.VMEM((nx, ny, mbs, sub, pw), b16),
            pltpu.VMEM((mbs, nx, sub, d), b16),
            pltpu.VMEM((nx, mbs, sub, d), b16),
            dma((2,)), dma((n,)), dma((n,)), dma((nx,)), dma((nx,)),
            dma((mbs, experts)), dma((mbs, experts)), dma((mbs, experts)), dma((mbs, experts)),
            dma((n,)), dma((n,)), dma((nx,)), dma((nx,)), dma((3,)),
        ],
        compiler_params=pltpu.CompilerParams(collective_id=ids, has_side_effects=True, vmem_limit_bytes=VMEM_BYTES),
        cost_estimate=pl.CostEstimate(flops=4 * 10**9, bytes_accessed=30 * 10**6, transcendentals=10**6),
        name="experts_forward",
    )(
        mid.reshape(mbs, sub, d), n2.reshape(mbs, sub, d), rx, place, jnp.swapaxes(place, 1, 2),
        win[0], win[1], wdt[0], wdt[1], sin_w, sdt,
    )
    out, slots_k, gu, hid, rows2, sgu, shid = outs
    return out.reshape(mbs * sub, d), (slots_k, gu, hid, rows2.reshape(-1, d), sgu, shid)


FWD_SKEW = (1, 1)


def ff_bwd_kernel(cfg, g, n2, place, place_t, rwx, slots_i, gu_i, hid_i, rows2, sgu, shid,
                  win_a, win_b, wdt_a, wdt_b, sin_w, sdt, win_g_i, wdt_g_i,
                  out, rw_g, sin_g, sdt_g, win_g, wdt_g,
                  win, wdt, gsend, gall, grows, pm, pt, slots, gslots, gown, hid, acc, dh, dgu, deo,
                  wxi, wxd, sti, std, dsgu, rsend, rrecv, ssend, srecv,
                  w_sem, x_send, x_recv, n_send, n_recv, rs_send, rs_recv, ag_send, ag_recv,
                  wi_send, wi_recv, wd_send, wd_recv, r_send, r_recv, s_send, s_recv, l_sem, st_sem):
    layer, nx, ny, mbs, sub, width, pw, experts, cap, f, sk, ak = cfg
    pos = Position(nx, ny)
    s, a, b, me = pos.s, pos.a, pos.b, pos.me
    keeper = s == layer
    slots_n = experts * cap
    tokens = nx * ny * sub
    d = ny * pw
    first = (b == ny - 1, b == 0)
    last = (b == 0, b == ny - 1)
    barrier = greet_section(pos)

    @pl.when(keeper)
    def _():
        pl.semaphore_signal(barrier, inc=1, device_id=(1 - s, a, b), device_id_type=MESH)

    for j, (dst, own, oth) in enumerate(((win, win_a, win_b), (wdt, wdt_a, wdt_b))):
        @pl.when(keeper)
        def _():
            pltpu.make_async_copy(own, dst, w_sem.at[j]).start()

        @pl.when(jnp.logical_not(keeper))
        def _():
            pltpu.make_async_copy(oth, dst, w_sem.at[j]).start()

    pltpu.make_async_copy(slots_i, slots, l_sem.at[0]).start()
    pltpu.make_async_copy(hid_i, hid, l_sem.at[1]).start()
    for m in range(mbs):
        @pl.when(last[m])
        def _():
            pltpu.make_async_copy(gu_i.at[m], gown, l_sem.at[2]).start()

    lane = lax.broadcasted_iota(jnp.int32, (1, pw), 1)
    for j in range(ny):
        gsend[j] = g[:, :, j * pw : (j + 1) * pw]

    @pl.when(keeper)
    def _():
        pl.semaphore_wait(barrier, pos.n - 1)

    @pl.when(jnp.logical_not(keeper))
    def _():
        pl.semaphore_wait(barrier, pos.n)

    def send_x(index, ai, bi):
        remote(gsend.at[bi], gall.at[:, b, a], x_send.at[index], x_recv.at[me], (s, ai, bi)).start()

    pos.others(send_x)

    def send_n(ai):
        remote(g, grows.at[:, a], n_send.at[ai], n_recv.at[a], (s, ai, b)).start()

    pos.peers(send_n)
    gall[:, b, a] = gsend[b]
    grows[:, a] = g[...]
    deo[...] = jnp.zeros_like(deo)

    def wait_x(index, ai, bi):
        remote(gsend.at[0], gall.at[:, bi, ai], x_send.at[index], x_recv.at[index], (s, ai, bi)).wait()

    i0 = lax.broadcasted_iota(jnp.int32, (slots_n, tokens), 0)
    pm[...] = bf(((place[0, 0:1] == i0) | (place[0, 1:2] == i0)).astype(jnp.float32))
    pos.others(wait_x)
    for m in range(mbs):
        if m:
            pm[...] = bf(((place[m, 0:1] == i0) | (place[m, 1:2] == i0)).astype(jnp.float32))
        gslots[m] = bf(mm(pm[...], gall[m].reshape(tokens, pw))).reshape(experts, cap, pw)
    for j, (dst, own) in enumerate(((win, win_a), (wdt, wdt_a))):
        pltpu.make_async_copy(own, dst, w_sem.at[j]).wait()
    pltpu.make_async_copy(slots_i, slots, l_sem.at[0]).wait()
    pltpu.make_async_copy(hid_i, hid, l_sem.at[1]).wait()
    for m in range(mbs):
        @pl.when(last[m])
        def _():
            pltpu.make_async_copy(gu_i.at[m], gown, l_sem.at[2]).wait()

    def dh_copy(m, e):
        to = b - 1 if m == 0 else b + 1
        return remote(dh.at[m, e], dh.at[m, e], rs_send.at[m, e], rs_recv.at[m, e], (s, a, to))

    def dgu_copy(m, e):
        to = b + 1 if m == 0 else b - 1
        return remote(dgu.at[m, e], dgu.at[m, e], ag_send.at[m, e], ag_recv.at[m, e], (s, a, to))

    def wi_copy(e):
        return remote(wxi.at[e], wxi.at[e], wi_send.at[e], wi_recv.at[e], (layer, a, b))

    def wd_copy(e):
        return remote(wxd.at[e], wxd.at[e], wd_send.at[e], wd_recv.at[e], (layer, a, b))

    def st_copies(e, slot):
        return (pltpu.make_async_copy(sti.at[slot], win_g.at[e], st_sem.at[0, slot]),
                pltpu.make_async_copy(std.at[slot], wdt_g.at[e], st_sem.at[1, slot]))

    def weight_grads(e):
        gi = mm(slots[:, e, :, :width].reshape(mbs * cap, width), dgu[:, e].reshape(mbs * cap, 2 * f), ((0,), (0,)))
        gd = mm(gslots[:, e, :, :width].reshape(mbs * cap, width), hid[:, e].reshape(mbs * cap, f), ((0,), (0,)))
        return gi, gd

    up = (ny - 1 - b, b)
    down = (b, ny - 1 - b)
    full = (sk + ak) * (ny - 1)
    late = 2

    def step(i, c):
        for m in range(mbs):
            e0 = i - sk * up[m]

            @pl.when((e0 >= 0) & (e0 < experts))
            def _():
                e = jnp.clip(e0, 0, experts - 1)
                acc[m] = mm(gslots[m, e, :, :width], wdt[e])

                @pl.when(jnp.logical_not(first[m]))
                def _():
                    dh_copy(m, e).wait_recv()
                    acc[m] += dh[m, e].astype(jnp.float32)

                @pl.when(jnp.logical_not(last[m]))
                def _():
                    dh[m, e] = bf(acc[m])
                    dh_copy(m, e).start()

                @pl.when(last[m])
                def _():
                    r = router_column(slots[m, e], e, width, experts)
                    gate = gown[e, :, :f].astype(jnp.float32)
                    upv = gown[e, :, f:].astype(jnp.float32)
                    dgate, dup, dr = act_back(gate, upv, acc[m], jax.nn.sigmoid(r))
                    dgu[m, e, :, :f] = bf(dgate)
                    dgu[m, e, :, f:] = bf(dup)
                    dgu_copy(m, e).start()
                    hi = bf(dr).astype(jnp.float32)
                    deo[m, e] = bf(jnp.where(lane == width + e, hi, jnp.where(lane == width + experts + e, dr - hi, 0.0)))

        for m in range(mbs):
            e1 = i - sk * (ny - 1) - ak * down[m]

            @pl.when((e1 >= 0) & (e1 < experts))
            def _():
                e = jnp.clip(e1, 0, experts - 1)

                @pl.when(jnp.logical_not(last[m]))
                def _():
                    dgu_copy(m, e).wait_recv()

                    @pl.when(jnp.logical_not(first[m]))
                    def _():
                        dgu_copy(m, e).start()

                deo[m, e, :, :width] = bf(mm(dgu[m, e], win[e], ((1,), (1,))))

        e2 = i - full

        @pl.when((e2 >= 0) & (e2 < experts) & jnp.logical_not(keeper))
        def _():
            e = jnp.clip(e2, 0, experts - 1)
            gi, gd = weight_grads(e)
            wxi[e] = bf(gi)
            wi_copy(e).start()
            wxd[e] = bf(gd)
            wd_copy(e).start()

        e3 = i - full - late

        @pl.when((e3 >= 0) & (e3 < experts) & keeper)
        def _():
            e = jnp.clip(e3, 0, experts - 1)
            slot = lax.rem(e, 2)

            @pl.when(e >= 2)
            def _():
                for copy in st_copies(e - 2, slot):
                    copy.wait()

            gi, gd = weight_grads(e)
            wi_copy(e).wait_recv()
            sti[slot] = gi + wxi[e].astype(jnp.float32)
            wd_copy(e).wait_recv()
            std[slot] = gd + wxd[e].astype(jnp.float32)
            for copy in st_copies(e, slot):
                copy.start()

        return c

    lax.fori_loop(0, experts + full + late, step, 0)

    for m in range(mbs):
        i1 = lax.broadcasted_iota(jnp.int32, (tokens, slots_n), 1)
        pt[...] = bf(((place_t[m, :, 0:1] == i1) | (place_t[m, :, 1:2] == i1)).astype(jnp.float32))
        br = mm(pt[...], deo[m].reshape(slots_n, pw))
        rsend[m] = bf(br).reshape(ny, nx, sub, pw)

    def send_r(index, ai, bi):
        remote(rsend.at[:, bi, ai], rrecv.at[a, b], r_send.at[index], r_recv.at[me], (s, ai, bi)).start()

    pos.others(send_r)
    rrecv[a, b] = rsend[:, b, a]

    def wait_n(ai):
        remote(g, grows.at[:, ai], n_send.at[ai], n_recv.at[ai], (s, ai, b)).wait()

    pos.peers(wait_n)
    gr = grows[...].reshape(mbs * nx * sub, d)
    dsg, dsu, _ = act_back(sgu[:, :f].astype(jnp.float32), sgu[:, f:].astype(jnp.float32), mm(gr, sdt[...]), None)
    dsgu[:, :f] = bf(dsg)
    dsgu[:, f:] = bf(dsu)
    ssend[...] = bf(mm(dsgu[...], sin_w[...], ((1,), (1,)))).reshape(mbs, nx, sub, d)

    def send_s(ai):
        remote(ssend.at[:, ai], srecv.at[a], s_send.at[ai], s_recv.at[a], (s, ai, b)).start()

    pos.peers(send_s)
    srecv[a] = ssend[:, a]
    sin_g[...] = bf(mm(rows2[...], dsgu[...], ((0,), (0,))))
    sdt_g[...] = bf(mm(gr, shid[...], ((0,), (0,))))

    def wait_s(ai):
        remote(ssend.at[:, ai], srecv.at[ai], s_send.at[ai], s_recv.at[ai], (s, ai, b)).wait()

    pos.peers(wait_s)

    def wait_r(index, ai, bi):
        remote(rsend.at[:, bi, ai], rrecv.at[ai, bi], r_send.at[index], r_recv.at[index], (s, ai, bi)).wait()

    pos.others(wait_r)
    dlog = jnp.zeros((mbs * sub, pw), jnp.float32)
    parts = []
    for j in range(ny):
        part = jnp.zeros((mbs, sub, pw), jnp.float32)
        for ai in range(nx):
            part = part + rrecv[ai, j].astype(jnp.float32)
        part = part.reshape(mbs * sub, pw)
        dlog = dlog + jnp.where(lane >= width, part, 0.0)
        parts.append(jnp.where(lane < width, part, 0.0))
    hi = bf(dlog)
    lo = bf(dlog - hi.astype(jnp.float32))
    total = mm(hi, rwx[...], ((1,), (1,))) + mm(lo, rwx[...], ((1,), (1,)))
    for ai in range(nx):
        total = total + srecv[ai].astype(jnp.float32).reshape(mbs * sub, d)
    for j in range(ny):
        out[:, j * pw : (j + 1) * pw] = total[:, j * pw : (j + 1) * pw] + parts[j]
    n2v = n2[...].reshape(mbs * sub, d)
    rw_g[...] = mm(n2v, hi, ((0,), (0,))) + mm(n2v, lo, ((0,), (0,)))

    def finish(e, c):
        for m in range(mbs):
            @pl.when(jnp.logical_not(last[m]))
            def _():
                dh_copy(m, e).wait_send()

            @pl.when(jnp.logical_not(first[m]))
            def _():
                dgu_copy(m, e).wait_send()

        @pl.when(jnp.logical_not(keeper))
        def _():
            wi_copy(e).wait_send()
            wd_copy(e).wait_send()

        return c

    lax.fori_loop(0, experts, finish, 0)

    @pl.when(keeper)
    def _():
        for e in (experts - 2, experts - 1):
            for copy in st_copies(e, e % 2):
                copy.wait()


def ff_bwd(layer, g, kept, n2, place, win, wdt, sin_w, sdt, rwx, grads, mbs, dims, ids):
    width, pw, experts, cap = dims
    slots_k, gu, hid, rows2, sgu, shid = kept
    nx, ny = lax.axis_size("gx"), lax.axis_size("gy")
    f = wdt[0].shape[-1]
    d = ny * pw
    sub = n2.shape[0] // mbs
    tokens = nx * ny * sub
    slots = experts * cap
    cfg = (layer, nx, ny, mbs, sub, width, pw, experts, cap, f, *BWD_SKEW)
    vm = pl.BlockSpec(memory_space=pltpu.VMEM)
    hbm = pl.BlockSpec(memory_space=pl.ANY)
    b16, f32 = jnp.bfloat16, jnp.float32
    dma = pltpu.SemaphoreType.DMA
    n = nx * ny
    out, rw_g, sin_g, sdt_g, win_g, wdt_g = pl.pallas_call(
        functools.partial(ff_bwd_kernel, cfg),
        out_shape=(
            jax.ShapeDtypeStruct((mbs * sub, d), f32),
            jax.ShapeDtypeStruct((d, pw), f32),
            jax.ShapeDtypeStruct((d, 2 * f), b16),
            jax.ShapeDtypeStruct((d, f), b16),
            jax.ShapeDtypeStruct((experts, width, 2 * f), f32),
            jax.ShapeDtypeStruct((experts, width, f), f32),
        ),
        in_specs=[vm] * 5 + [hbm] * 3 + [vm] * 3 + [hbm] * 4 + [vm] * 2 + [hbm] * 2,
        out_specs=(vm, vm, vm, vm, hbm, hbm),
        scratch_shapes=[
            pltpu.VMEM((experts, width, 2 * f), b16),
            pltpu.VMEM((experts, width, f), b16),
            pltpu.VMEM((ny, mbs, sub, pw), b16),
            pltpu.VMEM((mbs, ny, nx, sub, pw), b16),
            pltpu.VMEM((mbs, nx, sub, d), b16),
            pltpu.VMEM((slots, tokens), b16),
            pltpu.VMEM((tokens, slots), b16),
            pltpu.VMEM((mbs, experts, cap, pw), b16),
            pltpu.VMEM((mbs, experts, cap, pw), b16),
            pltpu.VMEM((experts, cap, 2 * f), b16),
            pltpu.VMEM((mbs, experts, cap, f), b16),
            pltpu.VMEM((mbs, cap, f), f32),
            pltpu.VMEM((mbs, experts, cap, f), b16),
            pltpu.VMEM((mbs, experts, cap, 2 * f), b16),
            pltpu.VMEM((mbs, experts, cap, pw), b16),
            pltpu.VMEM((experts, width, 2 * f), b16),
            pltpu.VMEM((experts, width, f), b16),
            pltpu.VMEM((2, width, 2 * f), f32),
            pltpu.VMEM((2, width, f), f32),
            pltpu.VMEM((mbs * nx * sub, 2 * f), b16),
            pltpu.VMEM((mbs, ny, nx, sub, pw), b16),
            pltpu.VMEM((nx, ny, mbs, sub, pw), b16),
            pltpu.VMEM((mbs, nx, sub, d), b16),
            pltpu.VMEM((nx, mbs, sub, d), b16),
            dma((2,)), dma((n,)), dma((n,)), dma((nx,)), dma((nx,)),
            dma((mbs, experts)), dma((mbs, experts)), dma((mbs, experts)), dma((mbs, experts)),
            dma((experts,)), dma((experts,)), dma((experts,)), dma((experts,)),
            dma((n,)), dma((n,)), dma((nx,)), dma((nx,)), dma((3,)), dma((2, 2)),
        ],
        input_output_aliases={17: 4, 18: 5},
        compiler_params=pltpu.CompilerParams(collective_id=ids, has_side_effects=True, vmem_limit_bytes=VMEM_BYTES),
        cost_estimate=pl.CostEstimate(flops=8 * 10**9, bytes_accessed=60 * 10**6, transcendentals=10**6),
        name="experts_backward",
    )(
        bf(g).reshape(mbs, sub, d), n2.reshape(mbs, sub, d), place, jnp.swapaxes(place, 1, 2), rwx,
        slots_k, gu, hid, rows2, sgu, shid, win[0], win[1], wdt[0], wdt[1], sin_w, sdt, *grads,
    )
    return out, (win_g, wdt_g), sin_g, sdt_g, rw_g


BWD_SKEW = (2, 2)


def solution(mesh):
    in_specs = (
        P(None, "gx", "gy"),
        P(None, "gx", "gy"),
        P("section", "gy"),
        P("section", "gy", None, "gx"),
        P("section", "gx", "gy"),
        P("section", "gy"),
        P("section", "gy", None),
        P("section", None, "gy", None, "gx"),
        P("section", None, "gx", "gy"),
        P("section", "gy", None, "gx"),
        P("section", "gx", "gy"),
        P("section", None, None, None),
    )
    out_specs = (
        P("section", None, "gx", "gy"),
        P("section", None, "gx", "gy"),
        P("section", "gy"),
        P("section", "gy", None, "gx"),
        P("section", "gx", "gy"),
        P("section", "gy"),
        P("section", "gy", None),
        P("section", None, "gy", None, "gx"),
        P("section", None, "gx", "gy"),
        P("section", "gy", None, "gx"),
        P("section", "gx", "gy"),
    )
    fast = mesh.shape["gx"] == mesh.shape["gy"]
    return jax.shard_map(
        fast_device if fast else on_device, mesh=mesh, in_specs=in_specs, out_specs=out_specs, check_vma=False
    )
```

```python
import functools

import jax
import jax.numpy as jnp
from jax import lax
from jax.experimental import pallas as pl
from jax.experimental.pallas import tpu as pltpu
from jax.sharding import PartitionSpec as P

DH = 64


epsilon = 1e-06
highest = lax.Precision.HIGHEST


def from_partner(array, axis, apart):
    return lax.ppermute(array, axis, [(i, i ^ 1 << apart) for i in range(lax.axis_size(axis))])


def token_rows(values):
    return lax.all_gather(values, "gx", axis=0, tiled=True)


def output_rows(values):
    return lax.psum_scatter(values, "gx", scatter_dimension=0, tiled=True)


def width_sum(values):
    return lax.psum(values, "gy")


def pass_section(values):
    return from_partner(values, "section", 0)


def sequence_sums(values):
    return lax.psum_scatter(values, "gy", scatter_dimension=0, tiled=True)


def sequence_rows(values):
    return lax.all_gather(values, "gy", axis=0, tiled=True)


def gather_hidden(hidden, shared_hidden):
    return (
        lax.all_gather(hidden, "gy", axis=0, tiled=True),
        lax.all_gather(shared_hidden, "gy", axis=0, tiled=True),
    )


def rope_turn(values, positions, turn_sign):
    half_size = values.shape[-1] // 2
    frequency = 10000.0 ** (-jnp.arange(half_size, dtype=jnp.float32) / half_size)
    angles = positions[:, None] * frequency[None, :]
    cosine = jnp.cos(angles)[:, None, :]
    sine_part = turn_sign * jnp.sin(angles)[:, None, :]
    first_half = values[..., :half_size]
    second_half = values[..., half_size:]
    return jnp.concatenate(
        [
            first_half * cosine - second_half * sine_part,
            first_half * sine_part + second_half * cosine,
        ],
        axis=-1,
    )


def norm_forward(stream, gain):
    full_width = stream.shape[1] * lax.axis_size("gy")
    square_sum = width_sum(jnp.sum(stream * stream, axis=1))
    inverse_rms = lax.rsqrt(square_sum / full_width + epsilon)
    return ((stream * inverse_rms[:, None] * gain[None, :]).astype(jnp.bfloat16), inverse_rms)


def norm_backward(stream, inverse_rms, gain, grad_normed):
    full_width = stream.shape[1] * lax.axis_size("gy")
    scaled = grad_normed * gain[None, :]
    inner_sum = width_sum(jnp.sum(scaled * stream, axis=1))
    cubed = inverse_rms * inverse_rms * inverse_rms
    grad_stream = inverse_rms[:, None] * scaled - stream * (cubed * inner_sum / full_width)[:, None]
    grad_gain = jnp.sum(grad_normed * stream * inverse_rms[:, None], axis=0)
    return (grad_stream, grad_gain)


def slot_table(route_ids, experts, capacity):
    flat_ids = route_ids.reshape(-1)
    assigned = (flat_ids[:, None] == jnp.arange(experts, dtype=jnp.int32)[None, :]).astype(
        jnp.int32
    )
    earlier = jnp.cumsum(assigned, axis=0) - assigned
    places = flat_ids * capacity + jnp.sum(earlier * assigned, axis=1)
    owners = jnp.arange(flat_ids.shape[0], dtype=jnp.int32) // 2
    slot_token = jnp.zeros((experts * capacity,), jnp.int32).at[places].set(owners)
    slot_valid = jnp.zeros((experts * capacity,), jnp.int32).at[places].set(jnp.ones_like(owners))
    return (places.reshape(-1, 2), slot_token, slot_valid)


def expert_act(gate_up, logits):
    half_size = gate_up.shape[1] // 2
    return (
        jax.nn.silu(gate_up[:, :half_size])
        * gate_up[:, half_size:]
        * jax.nn.sigmoid(logits)[:, None]
    )


def shared_act(gate_up):
    half_size = gate_up.shape[1] // 2
    return jax.nn.silu(gate_up[:, :half_size]) * gate_up[:, half_size:]


def causal_scores(queries, keys_part):
    score_scale = queries.shape[-1] ** (-0.5)
    scores = (
        jnp.einsum("qhd,khd->hqk", queries, keys_part, preferred_element_type=jnp.float32)
        * score_scale
    )
    length = queries.shape[0]
    causal = jnp.arange(length)[:, None] >= jnp.arange(length)[None, :]
    return jnp.where(causal[None], scores, -1e30)


def attend_forward(queries, keys_part, values_part):
    scores = causal_scores(queries, keys_part)
    row_max = jnp.max(scores, axis=-1, keepdims=True)
    exponent = jnp.exp(scores - row_max)
    row_total = jnp.sum(exponent, axis=-1, keepdims=True)
    probabilities = (exponent / row_total).astype(jnp.bfloat16)
    attended = jnp.einsum(
        "hqk,khd->qhd", probabilities, values_part, preferred_element_type=jnp.float32
    )
    return (attended, row_max + jnp.log(row_total))


def attend_backward(queries, keys_part, values_part, log_total, grad_attended):
    score_scale = queries.shape[-1] ** (-0.5)
    probabilities = jnp.exp(causal_scores(queries, keys_part) - log_total)
    grad_values = jnp.einsum(
        "hqk,qhd->khd",
        probabilities.astype(jnp.bfloat16),
        grad_attended,
        preferred_element_type=jnp.float32,
    )
    grad_probs = jnp.einsum(
        "qhd,khd->hqk", grad_attended, values_part, preferred_element_type=jnp.float32
    )
    grad_scores = (
        probabilities * (grad_probs - jnp.sum(grad_probs * probabilities, axis=-1, keepdims=True))
    ).astype(jnp.bfloat16)
    grad_queries = (
        jnp.einsum("hqk,khd->qhd", grad_scores, keys_part, preferred_element_type=jnp.float32)
        * score_scale
    )
    grad_keys = (
        jnp.einsum("hqk,qhd->khd", grad_scores, queries, preferred_element_type=jnp.float32)
        * score_scale
    )
    return (grad_queries, grad_keys, grad_values)


def layer_forward(stream, weights, route_ids):
    (
        attention_gain,
        attention_in,
        attention_out,
        feed_gain,
        router_weight,
        expert_in,
        expert_down,
        shared_in,
        shared_down,
    ) = weights
    local_width = stream.shape[1]
    experts = expert_in.shape[0]
    normed, inverse_first = norm_forward(stream, attention_gain)
    rows_first = token_rows(normed)
    tokens = rows_first.shape[0]
    capacity = 5 * tokens // (2 * experts)
    slot_count = experts * capacity
    projected = sequence_sums(
        jnp.dot(
            rows_first, attention_in.reshape(local_width, -1), preferred_element_type=jnp.float32
        )
    )
    length = projected.shape[0]
    projected = projected.reshape(length, 3, -1, DH)
    positions = jnp.arange(length, dtype=jnp.float32)
    queries = rope_turn(projected[:, 0], positions, 1.0).astype(jnp.bfloat16)
    keys_part = rope_turn(projected[:, 1], positions, 1.0).astype(jnp.bfloat16)
    values_part = projected[:, 2].astype(jnp.bfloat16)
    attended, log_total = attend_forward(queries, keys_part, values_part)
    attended_rows = sequence_rows(attended.astype(jnp.bfloat16).reshape(length, -1))
    middle = stream + output_rows(
        jnp.dot(attended_rows, attention_out, preferred_element_type=jnp.float32)
    )
    normed_feed, inverse_second = norm_forward(middle, feed_gain)
    rows_second = token_rows(normed_feed)
    route_slot, slot_token, slot_valid = slot_table(route_ids, experts, capacity)
    grouped = (rows_second[slot_token] * slot_valid[:, None].astype(jnp.bfloat16)).reshape(
        experts, capacity, local_width
    )
    expert_part = jnp.einsum(
        "ecd,edf->ecf",
        grouped,
        expert_in.reshape(experts, local_width, -1),
        preferred_element_type=jnp.float32,
    )
    router_part = jnp.einsum(
        "ecd,de->ec", grouped, router_weight, preferred_element_type=jnp.float32
    )
    shared_part = jnp.dot(
        rows_second, shared_in.reshape(local_width, -1), preferred_element_type=jnp.float32
    )
    expert_gu, router_logit, shared_gu = (
        lax.psum_scatter(
            expert_part.reshape(slot_count, -1), "gy", scatter_dimension=0, tiled=True
        ),
        lax.psum_scatter(router_part.reshape(slot_count), "gy", scatter_dimension=0, tiled=True),
        lax.psum_scatter(shared_part, "gy", scatter_dimension=0, tiled=True),
    )
    hidden_rows, shared_rows = gather_hidden(
        expert_act(expert_gu, router_logit).astype(jnp.bfloat16),
        shared_act(shared_gu).astype(jnp.bfloat16),
    )
    expert_result = jnp.einsum(
        "ecf,efd->ecd",
        hidden_rows.reshape(experts, capacity, -1),
        expert_down,
        preferred_element_type=jnp.float32,
    ).reshape(slot_count, local_width)
    branch = (
        expert_result[route_slot[:, 0]]
        + expert_result[route_slot[:, 1]]
        + jnp.dot(shared_rows, shared_down, preferred_element_type=jnp.float32)
    )
    result = middle + output_rows(branch)
    kept_items = (
        stream,
        inverse_first,
        rows_first,
        queries,
        keys_part,
        values_part,
        log_total,
        attended_rows,
        middle,
        inverse_second,
        rows_second,
        expert_gu,
        router_logit,
        shared_gu,
    )
    return (result, kept_items)


def layer_backward(grad_out, kept_items, weights, route_ids):
    (
        attention_gain,
        attention_in,
        attention_out,
        feed_gain,
        router_weight,
        expert_in,
        expert_down,
        shared_in,
        shared_down,
    ) = weights
    (
        stream,
        inverse_first,
        rows_first,
        queries,
        keys_part,
        values_part,
        log_total,
        attended_rows,
        middle,
        inverse_second,
        rows_second,
        expert_gu,
        router_logit,
        shared_gu,
    ) = kept_items[:14]
    local_width = stream.shape[1]
    experts = expert_in.shape[0]
    tokens = rows_second.shape[0]
    capacity = 5 * tokens // (2 * experts)
    slot_count = experts * capacity
    hidden_rows, shared_rows = gather_hidden(
        expert_act(expert_gu, router_logit).astype(jnp.bfloat16),
        shared_act(shared_gu).astype(jnp.bfloat16),
    )
    route_slot, slot_token, slot_valid = slot_table(route_ids, experts, capacity)
    valid_rows = slot_valid[:, None].astype(jnp.bfloat16)
    grouped = (rows_second[slot_token] * valid_rows).reshape(experts, capacity, local_width)
    grad_rows = token_rows(grad_out.astype(jnp.bfloat16))
    slot_grad = (grad_rows[slot_token] * valid_rows).reshape(experts, capacity, local_width)
    down_grad = jnp.einsum(
        "ecf,ecd->efd",
        hidden_rows.reshape(experts, capacity, -1),
        slot_grad,
        preferred_element_type=jnp.float32,
    )
    shared_down_grad = jnp.einsum(
        "tf,td->fd", shared_rows, grad_rows, preferred_element_type=jnp.float32
    )
    hidden_part = jnp.einsum(
        "ecd,efd->ecf", slot_grad, expert_down, preferred_element_type=jnp.float32
    ).reshape(slot_count, -1)
    shared_part = jnp.einsum(
        "td,fd->tf", grad_rows, shared_down, preferred_element_type=jnp.float32
    )
    grad_hidden, grad_shared = (
        lax.psum_scatter(
            hidden_part.astype(jnp.bfloat16), "gy", scatter_dimension=0, tiled=True
        ).astype(jnp.float32),
        lax.psum_scatter(
            shared_part.astype(jnp.bfloat16), "gy", scatter_dimension=0, tiled=True
        ).astype(jnp.float32),
    )
    unused_expert, expert_back = jax.vjp(expert_act, expert_gu, router_logit)
    grad_gu, grad_logit = expert_back(grad_hidden)
    unused_shared, shared_back = jax.vjp(shared_act, shared_gu)
    (grad_shared_gu,) = shared_back(grad_shared)
    gu_rows, shared_gu_rows = (
        lax.all_gather(grad_gu.astype(jnp.bfloat16), "gy", axis=0, tiled=True),
        lax.all_gather(grad_shared_gu.astype(jnp.bfloat16), "gy", axis=0, tiled=True),
    )
    logit_rows = lax.all_gather(grad_logit, "gy", axis=0, tiled=True).reshape(experts, capacity)
    gu_grouped = gu_rows.reshape(experts, capacity, -1)
    in_grad = jnp.einsum("ecd,ecf->edf", grouped, gu_grouped, preferred_element_type=jnp.float32)
    router_grad = jnp.einsum(
        "ecd,ec->de", grouped.astype(jnp.float32), logit_rows, precision=highest
    )
    shared_in_grad = jnp.einsum(
        "td,tf->df", rows_second, shared_gu_rows, preferred_element_type=jnp.float32
    )
    slot_back = jnp.einsum(
        "ecf,edf->ecd",
        gu_grouped,
        expert_in.reshape(experts, local_width, -1),
        preferred_element_type=jnp.float32,
    )
    slot_back = slot_back + logit_rows[:, :, None] * router_weight.T.astype(jnp.float32)[:, None, :]
    slot_back = slot_back.reshape(slot_count, local_width)
    rows_back = (
        slot_back[route_slot[:, 0]]
        + slot_back[route_slot[:, 1]]
        + jnp.einsum(
            "tf,df->td",
            shared_gu_rows,
            shared_in.reshape(local_width, -1),
            preferred_element_type=jnp.float32,
        )
    )
    grad_middle_norm, feed_gain_grad = norm_backward(
        middle, inverse_second, feed_gain, output_rows(rows_back)
    )
    grad_middle = grad_out + grad_middle_norm
    middle_rows = token_rows(grad_middle.astype(jnp.bfloat16))
    out_weight_grad = jnp.einsum(
        "tf,td->fd", attended_rows, middle_rows, preferred_element_type=jnp.float32
    )
    grad_attended = sequence_sums(
        jnp.einsum("td,fd->tf", middle_rows, attention_out, preferred_element_type=jnp.float32)
    )
    length = grad_attended.shape[0]
    positions = jnp.arange(length, dtype=jnp.float32)
    grad_queries, grad_keys, grad_values = attend_backward(
        queries,
        keys_part,
        values_part,
        log_total,
        grad_attended.astype(jnp.bfloat16).reshape(queries.shape),
    )
    grad_projected = jnp.stack(
        [
            rope_turn(grad_queries, positions, -1.0),
            rope_turn(grad_keys, positions, -1.0),
            grad_values,
        ],
        axis=1,
    )
    grad_projected = grad_projected.astype(jnp.bfloat16).reshape(length, -1)
    projected_rows = sequence_rows(grad_projected)
    in_weight_grad = jnp.einsum(
        "td,tf->df", rows_first, projected_rows, preferred_element_type=jnp.float32
    )
    grad_normed = output_rows(
        jnp.einsum(
            "tf,df->td",
            projected_rows,
            attention_in.reshape(local_width, -1),
            preferred_element_type=jnp.float32,
        )
    )
    grad_stream_norm, attention_gain_grad = norm_backward(
        stream, inverse_first, attention_gain, grad_normed
    )
    layer_grads = (
        attention_gain_grad,
        in_weight_grad.reshape(attention_in.shape),
        out_weight_grad,
        feed_gain_grad,
        router_grad,
        in_grad.reshape(expert_in.shape),
        down_grad,
        shared_in_grad.reshape(shared_in.shape),
        shared_down_grad,
    )
    return (grad_middle + grad_stream_norm, layer_grads)


def put_item(buffer, value, batch_index, is_valid):
    current = lax.dynamic_index_in_dim(buffer, batch_index, 0, keepdims=False)
    return lax.dynamic_update_index_in_dim(
        buffer, jnp.where(is_valid, value, current), batch_index, 0
    )


def on_device(
    block_input,
    output_grad,
    attention_gain,
    attention_in,
    attention_out,
    feed_gain,
    router_weight,
    expert_in,
    expert_down,
    shared_in,
    shared_down,
    routes,
):
    section_index = lax.axis_index("section")
    batches = block_input.shape[0]
    weights = tuple(
        (
            member[0]
            for member in (
                attention_gain,
                attention_in,
                attention_out,
                feed_gain,
                router_weight,
                expert_in,
                expert_down,
                shared_in,
                shared_down,
            )
        )
    )
    route_table = routes[0]
    outputs = jnp.zeros(block_input.shape, jnp.bfloat16)
    received = jnp.zeros(block_input.shape[1:], jnp.bfloat16)
    stored = None
    for tick_step in range(batches + 1):
        micro_index = tick_step - section_index
        is_valid = (micro_index >= 0) & (micro_index < batches)
        batch_index = jnp.clip(micro_index, 0, batches - 1)
        fresh_input = lax.dynamic_index_in_dim(block_input, batch_index, 0, keepdims=False)
        incoming = jnp.where(section_index == 0, fresh_input, received).astype(jnp.float32)
        route_ids = lax.dynamic_index_in_dim(route_table, batch_index, 0, keepdims=False)
        result, kept_items = layer_forward(incoming, weights, route_ids)
        result_low = result.astype(jnp.bfloat16)
        outputs = put_item(outputs, result_low, batch_index, is_valid)
        if stored is None:
            stored = tuple(
                (jnp.zeros((batches,) + member.shape, member.dtype) for member in kept_items)
            )
        stored = tuple(
            (
                put_item(buffer, member, batch_index, is_valid)
                for buffer, member in zip(stored, kept_items)
            )
        )
        if tick_step < batches:
            received = pass_section(result_low)
    grads_in = jnp.zeros(block_input.shape, jnp.bfloat16)
    received = jnp.zeros(block_input.shape[1:], jnp.bfloat16)
    totals = tuple((jnp.zeros(member.shape, jnp.float32) for member in weights))
    for tick_step in range(batches + 1):
        micro_index = batches - tick_step - section_index
        is_valid = (micro_index >= 0) & (micro_index < batches)
        batch_index = jnp.clip(micro_index, 0, batches - 1)
        given_grad = lax.dynamic_index_in_dim(output_grad, batch_index, 0, keepdims=False)
        incoming = jnp.where(section_index == 1, given_grad, received).astype(jnp.float32)
        kept_items = tuple(
            (lax.dynamic_index_in_dim(buffer, batch_index, 0, keepdims=False) for buffer in stored)
        )
        route_ids = lax.dynamic_index_in_dim(route_table, batch_index, 0, keepdims=False)
        grad_input, layer_grads = layer_backward(incoming, kept_items, weights, route_ids)
        grad_low = grad_input.astype(jnp.bfloat16)
        grads_in = put_item(grads_in, grad_low, batch_index, is_valid)
        totals = tuple(
            (total + jnp.where(is_valid, member, 0.0) for total, member in zip(totals, layer_grads))
        )
        if tick_step < batches:
            received = pass_section(grad_low)
    gain_first, gain_second, router_total = lax.psum((totals[0], totals[3], totals[4]), "gx")
    return (
        outputs[None],
        grads_in[None],
        gain_first[None],
        totals[1][None],
        totals[2][None],
        gain_second[None],
        router_total[None],
        totals[5][None],
        totals[6][None],
        totals[7][None],
        totals[8][None],
    )


def lanes_up(n):
    return -(-n // 128) * 128


def rot_columns(w):
    shape = w.shape
    w = w.reshape(shape[:-1] + (-1, 2, DH // 2))
    w = jnp.stack([-w[..., 1, :], w[..., 0, :]], axis=-2)
    return w.reshape(shape)


def pad_to(v, axis, n):
    pads = [(0, 0)] * v.ndim
    pads[axis] = (0, n - v.shape[axis])
    return jnp.pad(v, pads)


def mm(a, b, dims=((1,), (0,))):
    return lax.dot_general(a, b, (dims, ((), ())), preferred_element_type=jnp.float32)


def bf(v):
    return v.astype(jnp.bfloat16)


def emu_gather_gx(v, mbs):
    rows = v.shape[0] // mbs
    g = lax.all_gather(v.reshape(mbs, rows, -1), "gx")
    return jnp.moveaxis(g, 0, 1).reshape(mbs * 4 * rows, -1)


def emu_scatter_gx(v, mbs):
    n = lax.axis_size("gx")
    rows = v.shape[0] // mbs // n
    v = bf(v).astype(jnp.float32).reshape(mbs, n, rows, -1)
    v = lax.psum_scatter(v, "gx", scatter_dimension=1, tiled=False)
    return v.reshape(mbs * rows, -1)


def head_mask(pw, h):
    lane = lax.broadcasted_iota(jnp.int32, (1, pw), 1)
    return (lane >= h * DH) & (lane < (h + 1) * DH)


def rms(x, features):
    return lax.rsqrt(jnp.sum(x * x, axis=1, keepdims=True) / features + epsilon)


def norm_back(x, inv, gain, d, features):
    u = d * gain
    inner = jnp.sum(u * x, axis=1, keepdims=True) / features
    dx = inv * u - x * (inv * inv * inv * inner)
    return dx, jnp.sum(d * x * inv, axis=0, keepdims=True)


def emu_attn_fwd(x, gain, wqkv, wout, fgain, rwx, cos, sin, mbs, heads, features):
    pw = cos.shape[1]
    n1 = bf(x * rms(x, features) * gain)
    rows = emu_gather_gx(n1, mbs)
    proj = mm(rows, wqkv)
    length = rows.shape[0] // mbs
    cos2 = jnp.concatenate([cos] * mbs, 0)
    sin2 = jnp.concatenate([sin] * mbs, 0)
    q = bf(proj[:, :pw] * cos2 + proj[:, 3 * pw : 4 * pw] * sin2)
    k = bf(proj[:, pw : 2 * pw] * cos2 + proj[:, 4 * pw : 5 * pw] * sin2)
    v = bf(proj[:, 2 * pw : 3 * pw])
    outs = []
    for m in range(mbs):
        rs = slice(m * length, (m + 1) * length)
        acc = jnp.zeros((length, pw), jnp.float32)
        for h in range(heads):
            mask = head_mask(pw, h)
            p = probs_of(jnp.where(mask, q[rs], 0), k[rs])
            acc = acc + mm(bf(p), jnp.where(mask, v[rs], 0))
        outs.append(acc)
    att = bf(jnp.concatenate(outs, 0))
    mid = x + emu_scatter_gx(mm(att, wout), mbs)
    n2 = bf(mid * rms(mid, features) * fgain)
    rx = mm(n2, rwx)
    return mid, n2, rx, rows, q, k, v, att


def probs_of(q, k):
    s = mm(q, k, ((1,), (1,))) * DH ** -0.5
    n = s.shape[0]
    causal = lax.broadcasted_iota(jnp.int32, (n, n), 0) >= lax.broadcasted_iota(jnp.int32, (n, n), 1)
    s = jnp.where(causal, s, -1e30)
    e = jnp.exp(s - jnp.max(s, axis=1, keepdims=True))
    return e / jnp.sum(e, axis=1, keepdims=True)


def emu_attn_bwd(dn2, g, mid, fgain, x, gain, rows, q, k, v, att, wqkv, wout, cos, sin, rot, mbs, heads, features):
    pw = cos.shape[1]
    dx2, fgain_grad = norm_back(mid, rms(mid, features), fgain, dn2, features)
    dm = g + dx2
    dmr = emu_gather_gx(bf(dm), mbs)
    wout_grad = mm(att, dmr, ((0,), (0,)))
    datt = bf(mm(dmr, wout, ((1,), (1,))))
    length = rows.shape[0] // mbs
    parts = []
    for m in range(mbs):
        rs = slice(m * length, (m + 1) * length)
        dq = jnp.zeros((length, pw), jnp.float32)
        dk = dq
        dv = dq
        for h in range(heads):
            mask = head_mask(pw, h)
            qh = jnp.where(mask, q[rs], 0)
            kh = jnp.where(mask, k[rs], 0)
            da = jnp.where(mask, datt[rs], 0)
            p = probs_of(qh, k[rs])
            dp = mm(da, v[rs], ((1,), (1,)))
            ds = bf(p * (dp - jnp.sum(dp * p, axis=1, keepdims=True)))
            dv = dv + mm(bf(p), da, ((0,), (0,)))
            dq = dq + mm(ds, kh) * DH ** -0.5
            dk = dk + mm(ds, qh, ((0,), (0,))) * DH ** -0.5

        def back(t):
            hi = bf(t)
            lo = bf(t - hi.astype(jnp.float32))
            return t * cos - (mm(hi, rot) + mm(lo, rot)) * sin

        parts.append(jnp.concatenate([bf(back(dq)), bf(back(dk)), bf(dv)], 1))
    dqkv = jnp.concatenate(parts, 0)
    wqkv_grad = mm(rows, dqkv, ((0,), (0,)))
    dn1 = emu_scatter_gx(mm(dqkv, wqkv[:, : 3 * pw], ((1,), (1,))), mbs)
    dx1, gain_grad = norm_back(x, rms(x, features), gain, dn1, features)
    return dm + dx1, wqkv_grad, wout_grad, gain_grad, fgain_grad


def emu_spread(v, mbs, pw):
    n = lax.axis_size("gy")
    rows = v.shape[0] // mbs
    t = lax.all_to_all(v.reshape(mbs, rows, n, pw), "gy", split_axis=2, concat_axis=0, tiled=False)
    t = lax.all_gather(t, "gx")
    return t.transpose(2, 1, 0, 3, 4).reshape(mbs, -1, pw)


def emu_return(v, mbs):
    nx, ny = lax.axis_size("gx"), lax.axis_size("gy")
    pw = v.shape[-1]
    t = bf(v).astype(jnp.float32).reshape(mbs, ny, nx, -1, pw)
    t = lax.psum_scatter(t, "gx", scatter_dimension=2, tiled=False)
    rows = t.shape[2]
    t = lax.all_to_all(t, "gy", split_axis=1, concat_axis=0, tiled=False)
    return t.transpose(1, 2, 0, 3).reshape(mbs * rows, ny * pw)


def place_matrix(place_row, slots):
    i = lax.broadcasted_iota(jnp.int32, (slots, place_row.shape[1]), 0)
    return bf(((place_row[0:1] == i) | (place_row[1:2] == i)).astype(jnp.float32))


def ext_block(n2, rx, j, width, pw, experts):
    lane = lax.broadcasted_iota(jnp.int32, (1, pw), 1)
    hi = bf(rx)
    lo = bf(rx - hi.astype(jnp.float32))
    v = jnp.where(lane < width + experts, hi, lo)
    return jnp.where(lane < width, n2[:, j * pw : (j + 1) * pw], v)


def emu_ff_fwd(mid, n2, rx, place, win, wdt, sin_w, sdt, mbs, dims):
    width, pw, experts, cap = dims
    f = wdt.shape[-1]
    xe = jnp.concatenate([ext_block(n2, rx, j, width, pw, experts) for j in range(4)], 1)
    xs_all = emu_spread(xe, mbs, pw)
    slots_all, gu_all, hid_all, branch = [], [], [], []
    for m in range(mbs):
        pm = place_matrix(place[m], experts * cap)
        slots = bf(mm(pm, xs_all[m]))
        se = slots.reshape(experts, cap, pw)
        gu = jnp.einsum("ecd,edf->ecf", se[..., :width], win, preferred_element_type=jnp.float32)
        gu = lax.psum(bf(gu).astype(jnp.float32), "gy")
        lane = lax.broadcasted_iota(jnp.int32, (experts, 1, pw), 2)
        ex = lax.broadcasted_iota(jnp.int32, (experts, 1, pw), 0)
        rmask = (lane == width + ex) | (lane == width + experts + ex)
        r = jnp.sum(jnp.where(rmask, se.astype(jnp.float32), 0), -1, keepdims=True)
        hid = bf(jax.nn.silu(gu[..., :f]) * gu[..., f:] * jax.nn.sigmoid(r))
        eo = bf(jnp.einsum("ecf,edf->ecd", hid, wdt, preferred_element_type=jnp.float32)).reshape(-1, width)
        branch.append(pad_to(mm(pm, eo, ((0,), (0,))), 1, pw))
        slots_all.append(se)
        gu_all.append(bf(gu))
        hid_all.append(hid)
    ret = emu_return(jnp.stack(branch), mbs)
    rows2 = emu_gather_gx(n2, mbs)
    sgu = mm(rows2, sin_w)
    shid = bf(jax.nn.silu(sgu[:, :f]) * sgu[:, f:])
    sout = emu_scatter_gx(mm(shid, sdt, ((1,), (1,))), mbs)
    out = mid + ret + sout
    return out, (jnp.stack(slots_all), jnp.stack(gu_all), jnp.stack(hid_all), rows2, bf(sgu), shid)


def emu_ff_bwd(g, kept, n2, place, win, wdt, sin_w, sdt, rwx, mbs, dims):
    width, pw, experts, cap = dims
    slots_all, gu_all, hid_all, rows2, sgu, shid = kept
    f = wdt.shape[-1]
    gb = bf(g)
    g_all = emu_spread(gb, mbs, pw)
    comb = []
    win_grad = jnp.zeros((experts, width, 2 * f), jnp.float32)
    wdt_grad = jnp.zeros((experts, width, f), jnp.float32)
    for m in range(mbs):
        pm = place_matrix(place[m], experts * cap)
        gs = bf(mm(pm, g_all[m])).reshape(experts, cap, pw)[..., :width]
        dh = jnp.einsum("ecd,edf->ecf", gs, wdt, preferred_element_type=jnp.float32)
        dh = lax.psum(bf(dh).astype(jnp.float32), "gy")
        gu = gu_all[m].astype(jnp.float32)
        se = slots_all[m]
        lane = lax.broadcasted_iota(jnp.int32, (experts, 1, pw), 2)
        ex = lax.broadcasted_iota(jnp.int32, (experts, 1, pw), 0)
        rmask = (lane == width + ex) | (lane == width + experts + ex)
        r = jnp.sum(jnp.where(rmask, se.astype(jnp.float32), 0), -1, keepdims=True)
        gate, up = gu[..., :f], gu[..., f:]
        dgate, dup, dr = act_back(gate, up, dh, jax.nn.sigmoid(r))
        dgu = jnp.concatenate([bf(dgate), bf(dup)], -1)
        dslot = jnp.einsum("ecf,edf->ecd", dgu, win, preferred_element_type=jnp.float32)
        dslot = pad_to(dslot, 2, pw)
        hi = bf(dr).astype(jnp.float32)
        owner = (lax.axis_index("gy") == 0).astype(jnp.float32)
        dslot = dslot + owner * jnp.where(lane == width + ex, hi, jnp.where(lane == width + experts + ex, dr - hi, 0.0))
        comb.append(mm(pm, bf(dslot).reshape(-1, pw), ((0,), (0,))))
        win_grad = win_grad + jnp.einsum("ecd,ecf->edf", se[..., :width], dgu, preferred_element_type=jnp.float32)
        wdt_grad = wdt_grad + jnp.einsum("ecd,ecf->edf", gs, hid_all[m], preferred_element_type=jnp.float32)
    ret = emu_return(jnp.stack(comb), mbs)
    g_rows = emu_gather_gx(gb, mbs)
    dsh = mm(g_rows, sdt)
    sgu_f = sgu.astype(jnp.float32)
    dsg, dsu, _ = act_back(sgu_f[:, :f], sgu_f[:, f:], dsh, None)
    dsgu = jnp.concatenate([bf(dsg), bf(dsu)], 1)
    sin_grad = mm(rows2, dsgu, ((0,), (0,)))
    sdt_grad = mm(g_rows, shid, ((0,), (0,)))
    sback = emu_scatter_gx(mm(dsgu, sin_w, ((1,), (1,))), mbs)
    dn2, rw_grad = router_back(ret, n2, rwx, width, pw)
    return dn2 + sback, win_grad, wdt_grad, sin_grad, sdt_grad, rw_grad


def router_back(ret, n2, rwx, width, pw):
    lane = lax.broadcasted_iota(jnp.int32, (1, ret.shape[1]), 1)
    ret_x = sum(ret[:, j * pw : (j + 1) * pw] for j in range(ret.shape[1] // pw))
    lane1 = lax.broadcasted_iota(jnp.int32, (1, pw), 1)
    dlog = jnp.where(lane1 >= width, ret_x, 0.0)
    hi = bf(dlog)
    lo = bf(dlog - hi.astype(jnp.float32))
    main = jnp.where(lane % pw < width, ret, 0.0)
    dn2 = main + mm(hi, rwx, ((1,), (1,))) + mm(lo, rwx, ((1,), (1,)))
    rw_grad = mm(n2, hi, ((0,), (0,))) + mm(n2, lo, ((0,), (0,)))
    return dn2, rw_grad


def act_back(gate, up, dh, s):
    sg = jax.nn.sigmoid(gate)
    silu = gate * sg
    if s is None:
        return dh * up * (sg * (1.0 + gate * (1.0 - sg))), dh * silu, None
    dr = jnp.sum(dh * silu * up, axis=-1, keepdims=True) * s * (1.0 - s)
    ds = dh * s
    return ds * up * (sg * (1.0 + gate * (1.0 - sg))), ds * silu, dr


def places_of(routes, experts, capacity):
    lead = routes.shape[:-2]
    ids = routes.reshape((-1, routes.shape[-2] * 2))
    n = ids.shape[1]
    hot = (ids[..., None] == jnp.arange(experts, dtype=jnp.int32)).astype(jnp.bfloat16)
    before = (jnp.arange(n)[:, None] > jnp.arange(n)[None, :]).astype(jnp.bfloat16)
    earlier = jnp.einsum("ij,bje->bie", before, hot, preferred_element_type=jnp.float32)
    rank = jnp.sum(earlier * hot.astype(jnp.float32), -1).astype(jnp.int32)
    place = (ids * capacity + rank).reshape(lead + (-1, 2))
    return jnp.moveaxis(place, -1, -2)


def fast_device(block_input, output_grad, attention_gain, attention_in, attention_out, feed_gain,
                router_weight, expert_in, expert_down, shared_in, shared_down, routes):
    s = lax.axis_index("section")
    a = lax.axis_index("gx")
    b = lax.axis_index("gy")
    ny = lax.axis_size("gy")
    nx = lax.axis_size("gx")
    mbs = block_input.shape[0] // 2
    width = block_input.shape[2]
    features = width * ny
    experts = expert_in.shape[1]
    f = expert_in.shape[-1]
    pw = lanes_up(width + 2 * experts)
    tokens = routes.shape[2]
    cap = 5 * tokens // (2 * experts)
    sub = tokens // (nx * ny)
    heads = attention_in.shape[-1] // DH
    dims = (width, pw, experts, cap)
    length = sub * nx

    def both(v):
        other = pass_section(v)
        return jnp.where(s == 0, v, other), jnp.where(s == 0, other, v)

    def wide(v, axis):
        v = pad_to(v, axis, pw)
        return lax.all_gather(v, "gy", axis=axis, tiled=True)

    ai = wide(attention_in[0], 0)
    rotq = rot_columns(ai[:, :2])
    ai = pad_to(jnp.concatenate([ai, rotq], 1), 2, pw).reshape(ny * pw, 5 * pw)
    wqkv = both(ai)
    wout = both(pad_to(wide(attention_out[0], 1), 0, pw))
    gain = both(wide(attention_gain, 1))
    fgain = both(wide(feed_gain, 1))
    rwx = wide(router_weight[0], 0)
    rwx = jnp.concatenate([jnp.zeros((ny * pw, width), jnp.bfloat16), rwx, rwx], 1)
    rwx = both(pad_to(rwx, 1, pw))
    win_pair = (expert_in[0].reshape(experts, width, 2 * f),)
    win_pair = win_pair + (pass_section(win_pair[0]),)
    wdt_pair = (expert_down[0].transpose(0, 2, 1),)
    wdt_pair = wdt_pair + (pass_section(wdt_pair[0]),)
    sin_w = both(wide(shared_in[0].reshape(width, 2 * f), 0))
    sdt = both(wide(shared_down[0].T, 0))
    place = places_of(jnp.stack([lax.dynamic_slice_in_dim(r, s * mbs, mbs, 0) for r in both(routes[0])]), experts, cap)

    def tokens_in(v):
        t = lax.dynamic_slice_in_dim(v, s * mbs, mbs, 0)
        t = lax.all_gather(t, "gx", axis=1, tiled=True)
        t = lax.all_gather(pad_to(t, 2, pw), "gy", axis=2, tiled=True)
        t = lax.dynamic_slice_in_dim(t, b * length + a * sub, sub, 1)
        return t.reshape(mbs * sub, ny * pw).astype(jnp.float32)

    def tokens_out(pair):
        v0, v1 = pair
        keep = jnp.where(s == 0, v0, v1)
        send = jnp.where(s == 0, v1, v0)
        got = pass_section(send)
        both_mb = jnp.where(s == 0, jnp.stack([keep, got]), jnp.stack([got, keep]))
        t = bf(both_mb).reshape(2 * mbs, sub, ny, pw)[..., :width]
        t = lax.all_gather(t, "gx", axis=1, tiled=True)
        t = lax.all_gather(t, "gy", axis=1, tiled=True)
        t = lax.dynamic_slice_in_dim(t, a * (tokens // nx), tokens // nx, 1)
        return lax.dynamic_index_in_dim(t, b, 2, keepdims=False)[None]

    half = DH // 2
    freq = 10000.0 ** (-jnp.arange(half, dtype=jnp.float32) / half)
    ang = jnp.arange(length, dtype=jnp.float32)[:, None] * freq[None]
    lanes = jnp.tile(ang, (1, 2 * heads))
    cos = pad_to(jnp.cos(lanes), 1, pw)
    sin = pad_to(jnp.sin(lanes), 1, pw)
    rot = pad_to(pad_to(rot_columns(jnp.eye(heads * DH, dtype=jnp.float32)), 0, pw), 1, pw).astype(jnp.bfloat16)

    x = tokens_in(block_input)
    kept, outs = [], []
    for l in range(2):
        mid, n2, rx, rows, q, k, v, att = attn_fwd(
            x, gain[l], wqkv[l], wout[l], fgain[l], rwx[l], cos, sin, mbs, heads, features, 4)
        out, ff = ff_fwd(l, mid, n2, rx, place[l], win_pair, wdt_pair, sin_w[l], sdt[l], mbs, dims, l)
        kept.append((x, mid, n2, rows, q, k, v, att, ff))
        x = bf(out).astype(jnp.float32)
        outs.append(x)
    g = tokens_in(output_grad)
    gouts = [None, None]
    dense_grads = tuple(jnp.zeros(v.shape, v.dtype) for v in grad_shapes(experts, width, pw, f))
    expert_grads = (jnp.zeros((experts, width, 2 * f), jnp.float32), jnp.zeros((experts, width, f), jnp.float32))
    for l in (1, 0):
        x, mid, n2, rows, q, k, v, att, ff = kept[l]
        dn2, expert_grads, sin_g, sdt_g, rw_g = ff_bwd(
            l, g, ff, n2, place[l], win_pair, wdt_pair, sin_w[l], sdt[l], rwx[l], expert_grads, mbs, dims, 2 + l)
        dx, dense_grads = attn_bwd(
            l, dn2, g, mid, fgain[l], x, gain[l], rows, q, k, v, att, wqkv[l], wout[l], cos, sin, rot,
            sin_g, sdt_g, rw_g, dense_grads, mbs, heads, features, 5 + l)
        g = bf(dx).astype(jnp.float32)
        gouts[l] = g

    wqkv_g, wout_g, sin_g, sdt_g, small_g = dense_grads
    win_g, wdt_g = expert_grads

    hd = heads * DH
    return (
        tokens_out(outs),
        tokens_out(gouts),
        small_g[experts + 1 : experts + 2, :width],
        wqkv_g.reshape(width, 3, pw)[..., :hd][None],
        wout_g[:hd, :width][None],
        small_g[experts : experts + 1, :width],
        small_g[:experts, :width].T[None],
        win_g.reshape(experts, width, 2, f)[None],
        wdt_g.transpose(0, 2, 1)[None],
        sin_g.reshape(width, 2, f)[None],
        sdt_g.T[None],
    )


MESH = pl.DeviceIdType.MESH
VMEM_BYTES = 60 * 2**20


def greet(targets):
    barrier = pltpu.get_barrier_semaphore()
    for target in targets:
        pl.semaphore_signal(barrier, inc=1, device_id=target, device_id_type=MESH)
    return barrier


def remote(src, dst, send, recv, target):
    return pltpu.make_async_remote_copy(
        src_ref=src, dst_ref=dst, send_sem=send, recv_sem=recv, device_id=target, device_id_type=MESH
    )


def router_column(rows, e, width, experts):
    lane = lax.broadcasted_iota(jnp.int32, rows.shape, rows.ndim - 1)
    mask = (lane == width + e) | (lane == width + experts + e)
    return jnp.sum(jnp.where(mask, rows.astype(jnp.float32), 0.0), axis=-1, keepdims=True)


class Position:
    def __init__(self, nx, ny):
        self.s = lax.axis_index("section")
        self.a = lax.axis_index("gx")
        self.b = lax.axis_index("gy")
        self.nx, self.ny = nx, ny
        self.n = nx * ny
        self.me = self.a * ny + self.b

    def device(self, index):
        return (self.s, index // self.ny, lax.rem(index, self.ny))

    def others(self, do):
        def step(i, c):
            index = lax.rem(self.me + i, self.n)
            do(index, index // self.ny, lax.rem(index, self.ny))
            return c

        lax.fori_loop(1, self.n, step, 0)

    def peers(self, do):
        for i in range(1, self.nx):
            do(lax.rem(self.a + i, self.nx))


def greet_section(pos):
    barrier = pltpu.get_barrier_semaphore()

    def one(index, ai, bi):
        pl.semaphore_signal(barrier, inc=1, device_id=(pos.s, ai, bi), device_id_type=MESH)

    pos.others(one)
    return barrier


def ff_fwd_kernel(cfg, mid, n2, rx, place, place_t, win_a, win_b, wdt_a, wdt_b, sin_w, sdt,
                  out, slots_o, gu_o, hid_o, rows_o, sgu_o, shid_o,
                  win, wdt, xsend, xall, nrows, pm, pt, slots, acc, gu, hid, eo, shid, rsend, rrecv, ssend, srecv,
                  w_sem, x_send, x_recv, n_send, n_recv, rs_send, rs_recv, ag_send, ag_recv,
                  r_send, r_recv, s_send, s_recv, o_sem):
    layer, nx, ny, mbs, sub, width, pw, experts, cap, f, sk, ak = cfg
    pos = Position(nx, ny)
    s, a, b, me = pos.s, pos.a, pos.b, pos.me
    slots_n = experts * cap
    tokens = nx * ny * sub
    d = ny * pw
    barrier = greet_section(pos)

    for j, (dst, own, oth) in enumerate(((win, win_a, win_b), (wdt, wdt_a, wdt_b))):
        @pl.when(s == layer)
        def _():
            pltpu.make_async_copy(own, dst, w_sem.at[j]).start()

        @pl.when(s != layer)
        def _():
            pltpu.make_async_copy(oth, dst, w_sem.at[j]).start()

    lane = lax.broadcasted_iota(jnp.int32, (1, pw), 1)
    rv = rx[...]
    hi = bf(rv)
    lo = bf(rv - hi.astype(jnp.float32))
    tail = jnp.where(lane < width + experts, hi, lo)
    for j in range(ny):
        block = jnp.where(lane < width, n2[...].reshape(mbs * sub, d)[:, j * pw : (j + 1) * pw], tail)
        xsend[j] = block.reshape(mbs, sub, pw)
    pl.semaphore_wait(barrier, pos.n - 1)

    def send_x(index, ai, bi):
        remote(xsend.at[bi], xall.at[:, b, a], x_send.at[index], x_recv.at[me], (s, ai, bi)).start()

    pos.others(send_x)

    def send_n(ai):
        remote(n2, nrows.at[:, a], n_send.at[ai], n_recv.at[a], (s, ai, b)).start()

    pos.peers(send_n)
    xall[:, b, a] = xsend[b]
    nrows[:, a] = n2[...]

    for m in range(mbs):
        i0 = lax.broadcasted_iota(jnp.int32, (slots_n, tokens), 0)
        pm[m] = bf(((place[m, 0:1] == i0) | (place[m, 1:2] == i0)).astype(jnp.float32))
        i1 = lax.broadcasted_iota(jnp.int32, (tokens, slots_n), 1)
        pt[m] = bf(((place_t[m, :, 0:1] == i1) | (place_t[m, :, 1:2] == i1)).astype(jnp.float32))

    def wait_x(index, ai, bi):
        remote(xsend.at[0], xall.at[:, bi, ai], x_send.at[index], x_recv.at[index], (s, ai, bi)).wait()

    pos.others(wait_x)
    for m in range(mbs):
        slots[m] = bf(mm(pm[m], xall[m].reshape(tokens, pw))).reshape(experts, cap, pw)
    for j, (dst, own) in enumerate(((win, win_a), (wdt, wdt_a))):
        pltpu.make_async_copy(own, dst, w_sem.at[j]).wait()
    pltpu.make_async_copy(slots, slots_o, o_sem.at[0]).start()

    def gu_copy(m, e):
        to = b - 1 if m == 0 else b + 1
        return remote(gu.at[m, e], gu.at[m, e], rs_send.at[m, e], rs_recv.at[m, e], (s, a, to))

    def hid_copy(m, e):
        to = b + 1 if m == 0 else b - 1
        return remote(hid.at[m, e], hid.at[m, e], ag_send.at[m, e], ag_recv.at[m, e], (s, a, to))

    first = (b == ny - 1, b == 0)
    last = (b == 0, b == ny - 1)

    up = (ny - 1 - b, b)
    down = (b, ny - 1 - b)

    def step(i, c):
        for m in range(mbs):
            e0 = i - sk * up[m]

            @pl.when((e0 >= 0) & (e0 < experts))
            def _():
                e = jnp.clip(e0, 0, experts - 1)
                acc[m] = mm(slots[m, e, :, :width], win[e])

                @pl.when(jnp.logical_not(first[m]))
                def _():
                    gu_copy(m, e).wait_recv()
                    acc[m] += gu[m, e].astype(jnp.float32)

                gu[m, e] = bf(acc[m])

                @pl.when(jnp.logical_not(last[m]))
                def _():
                    gu_copy(m, e).start()

                @pl.when(last[m])
                def _():
                    r = router_column(slots[m, e], e, width, experts)
                    gate = acc[m, :, :f]
                    hid[m, e] = bf(gate * jax.nn.sigmoid(gate) * acc[m, :, f:] * jax.nn.sigmoid(r))
                    hid_copy(m, e).start()

        for m in range(mbs):
            e1 = i - sk * (ny - 1) - ak * down[m]

            @pl.when((e1 >= 0) & (e1 < experts))
            def _():
                e = jnp.clip(e1, 0, experts - 1)

                @pl.when(jnp.logical_not(last[m]))
                def _():
                    hid_copy(m, e).wait_recv()

                    @pl.when(jnp.logical_not(first[m]))
                    def _():
                        hid_copy(m, e).start()

                eo[m, e] = bf(mm(hid[m, e], wdt[e], ((1,), (1,))))

        return c

    lax.fori_loop(0, experts + (sk + ak) * (ny - 1), step, 0)

    def wait_n(ai):
        remote(n2, nrows.at[:, ai], n_send.at[ai], n_recv.at[ai], (s, ai, b)).wait()

    for m in range(mbs):
        @pl.when(last[m])
        def _():
            pltpu.make_async_copy(gu.at[m], gu_o.at[m], o_sem.at[1]).start()

    pltpu.make_async_copy(hid, hid_o, o_sem.at[2]).start()
    for m in range(mbs):
        br = mm(pt[m], eo[m].reshape(slots_n, width))
        rsend[m, ..., :width] = bf(br).reshape(ny, nx, sub, width)

    def send_r(index, ai, bi):
        remote(rsend.at[:, bi, ai], rrecv.at[a, b], r_send.at[index], r_recv.at[me], (s, ai, bi)).start()

    pos.others(send_r)
    rrecv[a, b] = rsend[:, b, a]

    pos.peers(wait_n)
    sgu = mm(nrows[...].reshape(mbs * nx * sub, d), sin_w[...])
    sgu_o[...] = bf(sgu)
    gate = sgu[:, :f]
    shid[...] = bf(gate * jax.nn.sigmoid(gate) * sgu[:, f:])
    shid_o[...] = shid[...]
    rows_o[...] = nrows[...]
    ssend[...] = bf(mm(shid[...], sdt[...], ((1,), (1,)))).reshape(mbs, nx, sub, d)

    def send_s(ai):
        remote(ssend.at[:, ai], srecv.at[a], s_send.at[ai], s_recv.at[a], (s, ai, b)).start()

    pos.peers(send_s)
    srecv[a] = ssend[:, a]

    def wait_s(ai):
        remote(ssend.at[:, ai], srecv.at[ai], s_send.at[ai], s_recv.at[ai], (s, ai, b)).wait()

    pos.peers(wait_s)

    def wait_r(index, ai, bi):
        remote(rsend.at[:, bi, ai], rrecv.at[ai, bi], r_send.at[index], r_recv.at[index], (s, ai, bi)).wait()

    pos.others(wait_r)
    total = mid[...]
    for ai in range(nx):
        total = total + srecv[ai].astype(jnp.float32)
    for j in range(ny):
        part = total[:, :, j * pw : (j + 1) * pw]
        for ai in range(nx):
            part = part + jnp.where(lane < width, rrecv[ai, j].astype(jnp.float32), 0.0)
        out[:, :, j * pw : (j + 1) * pw] = part

    def finish(e, c):
        for m in range(mbs):
            @pl.when(jnp.logical_not(last[m]))
            def _():
                gu_copy(m, e).wait_send()

            @pl.when(jnp.logical_not(first[m]))
            def _():
                hid_copy(m, e).wait_send()

        return c

    lax.fori_loop(0, experts, finish, 0)
    for m in range(mbs):
        @pl.when(last[m])
        def _():
            pltpu.make_async_copy(gu.at[m], gu_o.at[m], o_sem.at[1]).wait()

    pltpu.make_async_copy(hid, hid_o, o_sem.at[2]).wait()
    pltpu.make_async_copy(slots, slots_o, o_sem.at[0]).wait()


def ff_fwd(layer, mid, n2, rx, place, win, wdt, sin_w, sdt, mbs, dims, ids):
    width, pw, experts, cap = dims
    nx, ny = lax.axis_size("gx"), lax.axis_size("gy")
    f = wdt[0].shape[-1]
    d = ny * pw
    sub = n2.shape[0] // mbs
    tokens = nx * ny * sub
    slots = experts * cap
    cfg = (layer, nx, ny, mbs, sub, width, pw, experts, cap, f, *FWD_SKEW)
    vm = pl.BlockSpec(memory_space=pltpu.VMEM)
    hbm = pl.BlockSpec(memory_space=pl.ANY)
    b16, f32 = jnp.bfloat16, jnp.float32
    dma = pltpu.SemaphoreType.DMA
    n = nx * ny
    outs = pl.pallas_call(
        functools.partial(ff_fwd_kernel, cfg),
        out_shape=(
            jax.ShapeDtypeStruct((mbs, sub, d), f32),
            jax.ShapeDtypeStruct((mbs, experts, cap, pw), b16),
            jax.ShapeDtypeStruct((mbs, experts, cap, 2 * f), b16),
            jax.ShapeDtypeStruct((mbs, experts, cap, f), b16),
            jax.ShapeDtypeStruct((mbs, nx, sub, d), b16),
            jax.ShapeDtypeStruct((mbs * nx * sub, 2 * f), b16),
            jax.ShapeDtypeStruct((mbs * nx * sub, f), b16),
        ),
        in_specs=[vm] * 5 + [hbm] * 4 + [vm] * 2,
        out_specs=(vm, hbm, hbm, hbm, vm, vm, vm),
        scratch_shapes=[
            pltpu.VMEM((experts, width, 2 * f), b16),
            pltpu.VMEM((experts, width, f), b16),
            pltpu.VMEM((ny, mbs, sub, pw), b16),
            pltpu.VMEM((mbs, ny, nx, sub, pw), b16),
            pltpu.VMEM((mbs, nx, sub, d), b16),
            pltpu.VMEM((mbs, slots, tokens), b16),
            pltpu.VMEM((mbs, tokens, slots), b16),
            pltpu.VMEM((mbs, experts, cap, pw), b16),
            pltpu.VMEM((mbs, cap, 2 * f), f32),
            pltpu.VMEM((mbs, experts, cap, 2 * f), b16),
            pltpu.VMEM((mbs, experts, cap, f), b16),
            pltpu.VMEM((mbs, experts, cap, width), b16),
            pltpu.VMEM((mbs * nx * sub, f), b16),
            pltpu.VMEM((mbs, ny, nx, sub, pw), b16),
            pltpu.VMEM((nx, ny, mbs, sub, pw), b16),
            pltpu.VMEM((mbs, nx, sub, d), b16),
            pltpu.VMEM((nx, mbs, sub, d), b16),
            dma((2,)), dma((n,)), dma((n,)), dma((nx,)), dma((nx,)),
            dma((mbs, experts)), dma((mbs, experts)), dma((mbs, experts)), dma((mbs, experts)),
            dma((n,)), dma((n,)), dma((nx,)), dma((nx,)), dma((3,)),
        ],
        compiler_params=pltpu.CompilerParams(collective_id=ids, has_side_effects=True, vmem_limit_bytes=VMEM_BYTES),
        cost_estimate=pl.CostEstimate(flops=4 * 10**9, bytes_accessed=30 * 10**6, transcendentals=10**6),
        name="experts_forward",
    )(
        mid.reshape(mbs, sub, d), n2.reshape(mbs, sub, d), rx, place, jnp.swapaxes(place, 1, 2),
        win[0], win[1], wdt[0], wdt[1], sin_w, sdt,
    )
    out, slots_k, gu, hid, rows2, sgu, shid = outs
    return out.reshape(mbs * sub, d), (slots_k, gu, hid, rows2.reshape(-1, d), sgu, shid)


FWD_SKEW = (1, 1)


def ff_bwd_kernel(cfg, g, n2, place, place_t, rwx, slots_i, gu_i, hid_i, rows2, sgu, shid,
                  win_a, win_b, wdt_a, wdt_b, sin_w, sdt, win_g_i, wdt_g_i,
                  out, rw_g, sin_g, sdt_g, win_g, wdt_g,
                  win, wdt, gsend, gall, grows, pm, pt, slots, gslots, gown, hid, acc, dh, dgu, deo,
                  wxi, wxd, sti, std, dsgu, rsend, rrecv, ssend, srecv,
                  w_sem, x_send, x_recv, n_send, n_recv, rs_send, rs_recv, ag_send, ag_recv,
                  wi_send, wi_recv, wd_send, wd_recv, r_send, r_recv, s_send, s_recv, l_sem, st_sem):
    layer, nx, ny, mbs, sub, width, pw, experts, cap, f, sk, ak = cfg
    pos = Position(nx, ny)
    s, a, b, me = pos.s, pos.a, pos.b, pos.me
    keeper = s == layer
    slots_n = experts * cap
    tokens = nx * ny * sub
    d = ny * pw
    first = (b == ny - 1, b == 0)
    last = (b == 0, b == ny - 1)
    barrier = greet_section(pos)

    @pl.when(keeper)
    def _():
        pl.semaphore_signal(barrier, inc=1, device_id=(1 - s, a, b), device_id_type=MESH)

    for j, (dst, own, oth) in enumerate(((win, win_a, win_b), (wdt, wdt_a, wdt_b))):
        @pl.when(keeper)
        def _():
            pltpu.make_async_copy(own, dst, w_sem.at[j]).start()

        @pl.when(jnp.logical_not(keeper))
        def _():
            pltpu.make_async_copy(oth, dst, w_sem.at[j]).start()

    pltpu.make_async_copy(slots_i, slots, l_sem.at[0]).start()
    pltpu.make_async_copy(hid_i, hid, l_sem.at[1]).start()
    for m in range(mbs):
        @pl.when(last[m])
        def _():
            pltpu.make_async_copy(gu_i.at[m], gown, l_sem.at[2]).start()

    lane = lax.broadcasted_iota(jnp.int32, (1, pw), 1)
    for j in range(ny):
        gsend[j] = g[:, :, j * pw : (j + 1) * pw]

    @pl.when(keeper)
    def _():
        pl.semaphore_wait(barrier, pos.n - 1)

    @pl.when(jnp.logical_not(keeper))
    def _():
        pl.semaphore_wait(barrier, pos.n)

    def send_x(index, ai, bi):
        remote(gsend.at[bi], gall.at[:, b, a], x_send.at[index], x_recv.at[me], (s, ai, bi)).start()

    pos.others(send_x)

    def send_n(ai):
        remote(g, grows.at[:, a], n_send.at[ai], n_recv.at[a], (s, ai, b)).start()

    pos.peers(send_n)
    gall[:, b, a] = gsend[b]
    grows[:, a] = g[...]
    deo[...] = jnp.zeros_like(deo)

    def wait_x(index, ai, bi):
        remote(gsend.at[0], gall.at[:, bi, ai], x_send.at[index], x_recv.at[index], (s, ai, bi)).wait()

    i0 = lax.broadcasted_iota(jnp.int32, (slots_n, tokens), 0)
    pm[...] = bf(((place[0, 0:1] == i0) | (place[0, 1:2] == i0)).astype(jnp.float32))
    pos.others(wait_x)
    for m in range(mbs):
        if m:
            pm[...] = bf(((place[m, 0:1] == i0) | (place[m, 1:2] == i0)).astype(jnp.float32))
        gslots[m] = bf(mm(pm[...], gall[m].reshape(tokens, pw))).reshape(experts, cap, pw)
    for j, (dst, own) in enumerate(((win, win_a), (wdt, wdt_a))):
        pltpu.make_async_copy(own, dst, w_sem.at[j]).wait()
    pltpu.make_async_copy(slots_i, slots, l_sem.at[0]).wait()
    pltpu.make_async_copy(hid_i, hid, l_sem.at[1]).wait()
    for m in range(mbs):
        @pl.when(last[m])
        def _():
            pltpu.make_async_copy(gu_i.at[m], gown, l_sem.at[2]).wait()

    def dh_copy(m, e):
        to = b - 1 if m == 0 else b + 1
        return remote(dh.at[m, e], dh.at[m, e], rs_send.at[m, e], rs_recv.at[m, e], (s, a, to))

    def dgu_copy(m, e):
        to = b + 1 if m == 0 else b - 1
        return remote(dgu.at[m, e], dgu.at[m, e], ag_send.at[m, e], ag_recv.at[m, e], (s, a, to))

    def wi_copy(e):
        return remote(wxi.at[e], wxi.at[e], wi_send.at[e], wi_recv.at[e], (layer, a, b))

    def wd_copy(e):
        return remote(wxd.at[e], wxd.at[e], wd_send.at[e], wd_recv.at[e], (layer, a, b))

    def st_copies(e, slot):
        return (pltpu.make_async_copy(sti.at[slot], win_g.at[e], st_sem.at[0, slot]),
                pltpu.make_async_copy(std.at[slot], wdt_g.at[e], st_sem.at[1, slot]))

    def weight_grads(e):
        gi = mm(slots[:, e, :, :width].reshape(mbs * cap, width), dgu[:, e].reshape(mbs * cap, 2 * f), ((0,), (0,)))
        gd = mm(gslots[:, e, :, :width].reshape(mbs * cap, width), hid[:, e].reshape(mbs * cap, f), ((0,), (0,)))
        return gi, gd

    up = (ny - 1 - b, b)
    down = (b, ny - 1 - b)
    full = (sk + ak) * (ny - 1)
    late = 2

    def step(i, c):
        for m in range(mbs):
            e0 = i - sk * up[m]

            @pl.when((e0 >= 0) & (e0 < experts))
            def _():
                e = jnp.clip(e0, 0, experts - 1)
                acc[m] = mm(gslots[m, e, :, :width], wdt[e])

                @pl.when(jnp.logical_not(first[m]))
                def _():
                    dh_copy(m, e).wait_recv()
                    acc[m] += dh[m, e].astype(jnp.float32)

                @pl.when(jnp.logical_not(last[m]))
                def _():
                    dh[m, e] = bf(acc[m])
                    dh_copy(m, e).start()

                @pl.when(last[m])
                def _():
                    r = router_column(slots[m, e], e, width, experts)
                    gate = gown[e, :, :f].astype(jnp.float32)
                    upv = gown[e, :, f:].astype(jnp.float32)
                    dgate, dup, dr = act_back(gate, upv, acc[m], jax.nn.sigmoid(r))
                    dgu[m, e, :, :f] = bf(dgate)
                    dgu[m, e, :, f:] = bf(dup)
                    dgu_copy(m, e).start()
                    hi = bf(dr).astype(jnp.float32)
                    deo[m, e] = bf(jnp.where(lane == width + e, hi, jnp.where(lane == width + experts + e, dr - hi, 0.0)))

        for m in range(mbs):
            e1 = i - sk * (ny - 1) - ak * down[m]

            @pl.when((e1 >= 0) & (e1 < experts))
            def _():
                e = jnp.clip(e1, 0, experts - 1)

                @pl.when(jnp.logical_not(last[m]))
                def _():
                    dgu_copy(m, e).wait_recv()

                    @pl.when(jnp.logical_not(first[m]))
                    def _():
                        dgu_copy(m, e).start()

                deo[m, e, :, :width] = bf(mm(dgu[m, e], win[e], ((1,), (1,))))

        e2 = i - full

        @pl.when((e2 >= 0) & (e2 < experts) & jnp.logical_not(keeper))
        def _():
            e = jnp.clip(e2, 0, experts - 1)
            gi, gd = weight_grads(e)
            wxi[e] = bf(gi)
            wi_copy(e).start()
            wxd[e] = bf(gd)
            wd_copy(e).start()

        e3 = i - full - late

        @pl.when((e3 >= 0) & (e3 < experts) & keeper)
        def _():
            e = jnp.clip(e3, 0, experts - 1)
            slot = lax.rem(e, 2)

            @pl.when(e >= 2)
            def _():
                for copy in st_copies(e - 2, slot):
                    copy.wait()

            gi, gd = weight_grads(e)
            wi_copy(e).wait_recv()
            sti[slot] = gi + wxi[e].astype(jnp.float32)
            wd_copy(e).wait_recv()
            std[slot] = gd + wxd[e].astype(jnp.float32)
            for copy in st_copies(e, slot):
                copy.start()

        return c

    lax.fori_loop(0, experts + full + late, step, 0)

    for m in range(mbs):
        i1 = lax.broadcasted_iota(jnp.int32, (tokens, slots_n), 1)
        pt[...] = bf(((place_t[m, :, 0:1] == i1) | (place_t[m, :, 1:2] == i1)).astype(jnp.float32))
        br = mm(pt[...], deo[m].reshape(slots_n, pw))
        rsend[m] = bf(br).reshape(ny, nx, sub, pw)

    def send_r(index, ai, bi):
        remote(rsend.at[:, bi, ai], rrecv.at[a, b], r_send.at[index], r_recv.at[me], (s, ai, bi)).start()

    pos.others(send_r)
    rrecv[a, b] = rsend[:, b, a]

    def wait_n(ai):
        remote(g, grows.at[:, ai], n_send.at[ai], n_recv.at[ai], (s, ai, b)).wait()

    pos.peers(wait_n)
    gr = grows[...].reshape(mbs * nx * sub, d)
    dsg, dsu, _ = act_back(sgu[:, :f].astype(jnp.float32), sgu[:, f:].astype(jnp.float32), mm(gr, sdt[...]), None)
    dsgu[:, :f] = bf(dsg)
    dsgu[:, f:] = bf(dsu)
    ssend[...] = bf(mm(dsgu[...], sin_w[...], ((1,), (1,)))).reshape(mbs, nx, sub, d)

    def send_s(ai):
        remote(ssend.at[:, ai], srecv.at[a], s_send.at[ai], s_recv.at[a], (s, ai, b)).start()

    pos.peers(send_s)
    srecv[a] = ssend[:, a]
    sin_g[...] = bf(mm(rows2[...], dsgu[...], ((0,), (0,))))
    sdt_g[...] = bf(mm(gr, shid[...], ((0,), (0,))))

    def wait_s(ai):
        remote(ssend.at[:, ai], srecv.at[ai], s_send.at[ai], s_recv.at[ai], (s, ai, b)).wait()

    pos.peers(wait_s)

    def wait_r(index, ai, bi):
        remote(rsend.at[:, bi, ai], rrecv.at[ai, bi], r_send.at[index], r_recv.at[index], (s, ai, bi)).wait()

    pos.others(wait_r)
    dlog = jnp.zeros((mbs * sub, pw), jnp.float32)
    parts = []
    for j in range(ny):
        part = jnp.zeros((mbs, sub, pw), jnp.float32)
        for ai in range(nx):
            part = part + rrecv[ai, j].astype(jnp.float32)
        part = part.reshape(mbs * sub, pw)
        dlog = dlog + jnp.where(lane >= width, part, 0.0)
        parts.append(jnp.where(lane < width, part, 0.0))
    hi = bf(dlog)
    lo = bf(dlog - hi.astype(jnp.float32))
    total = mm(hi, rwx[...], ((1,), (1,))) + mm(lo, rwx[...], ((1,), (1,)))
    for ai in range(nx):
        total = total + srecv[ai].astype(jnp.float32).reshape(mbs * sub, d)
    for j in range(ny):
        out[:, j * pw : (j + 1) * pw] = total[:, j * pw : (j + 1) * pw] + parts[j]
    n2v = n2[...].reshape(mbs * sub, d)
    rw_t = mm(hi, n2v, ((0,), (0,))) + mm(lo, n2v, ((0,), (0,)))
    rw_g[...] = rw_t[width : width + experts] + rw_t[width + experts : width + 2 * experts]

    def finish(e, c):
        for m in range(mbs):
            @pl.when(jnp.logical_not(last[m]))
            def _():
                dh_copy(m, e).wait_send()

            @pl.when(jnp.logical_not(first[m]))
            def _():
                dgu_copy(m, e).wait_send()

        @pl.when(jnp.logical_not(keeper))
        def _():
            wi_copy(e).wait_send()
            wd_copy(e).wait_send()

        return c

    lax.fori_loop(0, experts, finish, 0)

    @pl.when(keeper)
    def _():
        for e in (experts - 2, experts - 1):
            for copy in st_copies(e, e % 2):
                copy.wait()


def ff_bwd(layer, g, kept, n2, place, win, wdt, sin_w, sdt, rwx, grads, mbs, dims, ids):
    width, pw, experts, cap = dims
    slots_k, gu, hid, rows2, sgu, shid = kept
    nx, ny = lax.axis_size("gx"), lax.axis_size("gy")
    f = wdt[0].shape[-1]
    d = ny * pw
    sub = n2.shape[0] // mbs
    tokens = nx * ny * sub
    slots = experts * cap
    cfg = (layer, nx, ny, mbs, sub, width, pw, experts, cap, f, *BWD_SKEW)
    vm = pl.BlockSpec(memory_space=pltpu.VMEM)
    hbm = pl.BlockSpec(memory_space=pl.ANY)
    b16, f32 = jnp.bfloat16, jnp.float32
    dma = pltpu.SemaphoreType.DMA
    n = nx * ny
    out, rw_g, sin_g, sdt_g, win_g, wdt_g = pl.pallas_call(
        functools.partial(ff_bwd_kernel, cfg),
        out_shape=(
            jax.ShapeDtypeStruct((mbs * sub, d), f32),
            jax.ShapeDtypeStruct((experts, d), f32),
            jax.ShapeDtypeStruct((d, 2 * f), b16),
            jax.ShapeDtypeStruct((d, f), b16),
            jax.ShapeDtypeStruct((experts, width, 2 * f), f32),
            jax.ShapeDtypeStruct((experts, width, f), f32),
        ),
        in_specs=[vm] * 5 + [hbm] * 3 + [vm] * 3 + [hbm] * 4 + [vm] * 2 + [hbm] * 2,
        out_specs=(vm, vm, vm, vm, hbm, hbm),
        scratch_shapes=[
            pltpu.VMEM((experts, width, 2 * f), b16),
            pltpu.VMEM((experts, width, f), b16),
            pltpu.VMEM((ny, mbs, sub, pw), b16),
            pltpu.VMEM((mbs, ny, nx, sub, pw), b16),
            pltpu.VMEM((mbs, nx, sub, d), b16),
            pltpu.VMEM((slots, tokens), b16),
            pltpu.VMEM((tokens, slots), b16),
            pltpu.VMEM((mbs, experts, cap, pw), b16),
            pltpu.VMEM((mbs, experts, cap, pw), b16),
            pltpu.VMEM((experts, cap, 2 * f), b16),
            pltpu.VMEM((mbs, experts, cap, f), b16),
            pltpu.VMEM((mbs, cap, f), f32),
            pltpu.VMEM((mbs, experts, cap, f), b16),
            pltpu.VMEM((mbs, experts, cap, 2 * f), b16),
            pltpu.VMEM((mbs, experts, cap, pw), b16),
            pltpu.VMEM((experts, width, 2 * f), b16),
            pltpu.VMEM((experts, width, f), b16),
            pltpu.VMEM((2, width, 2 * f), f32),
            pltpu.VMEM((2, width, f), f32),
            pltpu.VMEM((mbs * nx * sub, 2 * f), b16),
            pltpu.VMEM((mbs, ny, nx, sub, pw), b16),
            pltpu.VMEM((nx, ny, mbs, sub, pw), b16),
            pltpu.VMEM((mbs, nx, sub, d), b16),
            pltpu.VMEM((nx, mbs, sub, d), b16),
            dma((2,)), dma((n,)), dma((n,)), dma((nx,)), dma((nx,)),
            dma((mbs, experts)), dma((mbs, experts)), dma((mbs, experts)), dma((mbs, experts)),
            dma((experts,)), dma((experts,)), dma((experts,)), dma((experts,)),
            dma((n,)), dma((n,)), dma((nx,)), dma((nx,)), dma((3,)), dma((2, 2)),
        ],
        input_output_aliases={17: 4, 18: 5},
        compiler_params=pltpu.CompilerParams(collective_id=ids, has_side_effects=True, vmem_limit_bytes=VMEM_BYTES),
        cost_estimate=pl.CostEstimate(flops=8 * 10**9, bytes_accessed=60 * 10**6, transcendentals=10**6),
        name="experts_backward",
    )(
        bf(g).reshape(mbs, sub, d), n2.reshape(mbs, sub, d), place, jnp.swapaxes(place, 1, 2), rwx,
        slots_k, gu, hid, rows2, sgu, shid, win[0], win[1], wdt[0], wdt[1], sin_w, sdt, *grads,
    )
    return out, (win_g, wdt_g), sin_g, sdt_g, rw_g


BWD_SKEW = (2, 2)


def attn_fwd_kernel(cfg, x, gain, fgain, wqkv, wout, rwx, cos, sin,
                    mid, n2, rx, rows_o, q, k, v, att,
                    nsend, nall, proj, osend, orecv, n_send, n_recv, o_send, o_recv):
    nx, ny, mbs, sub, pw, heads, features = cfg
    pos = Position(nx, ny)
    s, a, b = pos.s, pos.a, pos.b
    d = ny * pw
    length = nx * sub
    barrier = pltpu.get_barrier_semaphore()
    pos.peers(lambda ai: pl.semaphore_signal(barrier, inc=1, device_id=(s, ai, b), device_id_type=MESH))
    xv = x[...].reshape(mbs * sub, d)
    nsend[...] = bf(xv * rms(xv, features) * gain[...]).reshape(mbs, sub, d)
    pl.semaphore_wait(barrier, nx - 1)

    def copy_n(ai, slot):
        return remote(nsend, nall.at[:, slot], n_send.at[ai], n_recv.at[slot], (s, ai, b))

    pos.peers(lambda ai: copy_n(ai, a).start())
    nall[:, a] = nsend[...]
    pos.peers(lambda ai: copy_n(ai, ai).wait())
    rows = nall[...].reshape(mbs * length, d)
    proj[...] = mm(rows, wqkv[...])
    rows_o[...] = nall[...]
    v[...] = bf(proj[:, 2 * pw : 3 * pw])
    for m in range(mbs):
        rs = slice(m * length, (m + 1) * length)
        q[rs] = bf(proj[rs, :pw] * cos[...] + proj[rs, 3 * pw : 4 * pw] * sin[...])
        k[rs] = bf(proj[rs, pw : 2 * pw] * cos[...] + proj[rs, 4 * pw : 5 * pw] * sin[...])
        acc = jnp.zeros((length, pw), jnp.float32)
        for h in range(heads):
            mask = head_mask(pw, h)
            p = probs_of(jnp.where(mask, q[rs], 0), k[rs])
            acc = acc + mm(bf(p), jnp.where(mask, v[rs], 0))
        att[rs] = bf(acc)
    osend[...] = bf(mm(att[...], wout[...])).reshape(mbs, nx, sub, d)

    def copy_o(ai, slot):
        return remote(osend.at[:, ai], orecv.at[slot], o_send.at[ai], o_recv.at[slot], (s, ai, b))

    pos.peers(lambda ai: copy_o(ai, a).start())
    orecv[a] = osend[:, a]
    pos.peers(lambda ai: copy_o(ai, ai).wait())
    mv = x[...]
    for ai in range(nx):
        mv = mv + orecv[ai].astype(jnp.float32)
    mv = mv.reshape(mbs * sub, d)
    mid[...] = mv
    n2v = bf(mv * rms(mv, features) * fgain[...])
    n2[...] = n2v
    rx[...] = mm(n2v, rwx[...])


def attn_fwd(x, gain, wqkv, wout, fgain, rwx, cos, sin, mbs, heads, features, ids):
    nx, ny = lax.axis_size("gx"), lax.axis_size("gy")
    pw = cos.shape[1]
    d = ny * pw
    sub = x.shape[0] // mbs
    length = nx * sub
    b16, f32 = jnp.bfloat16, jnp.float32
    dma = pltpu.SemaphoreType.DMA
    vm = pl.BlockSpec(memory_space=pltpu.VMEM)
    outs = pl.pallas_call(
        functools.partial(attn_fwd_kernel, (nx, ny, mbs, sub, pw, heads, features)),
        out_shape=(
            jax.ShapeDtypeStruct((mbs * sub, d), f32),
            jax.ShapeDtypeStruct((mbs * sub, d), b16),
            jax.ShapeDtypeStruct((mbs * sub, pw), f32),
            jax.ShapeDtypeStruct((mbs, nx, sub, d), b16),
            jax.ShapeDtypeStruct((mbs * length, pw), b16),
            jax.ShapeDtypeStruct((mbs * length, pw), b16),
            jax.ShapeDtypeStruct((mbs * length, pw), b16),
            jax.ShapeDtypeStruct((mbs * length, pw), b16),
        ),
        in_specs=[vm] * 8,
        out_specs=(vm,) * 8,
        scratch_shapes=[
            pltpu.VMEM((mbs, sub, d), b16),
            pltpu.VMEM((mbs, nx, sub, d), b16),
            pltpu.VMEM((mbs * length, 5 * pw), f32),
            pltpu.VMEM((mbs, nx, sub, d), b16),
            pltpu.VMEM((nx, mbs, sub, d), b16),
            dma((nx,)), dma((nx,)), dma((nx,)), dma((nx,)),
        ],
        compiler_params=pltpu.CompilerParams(collective_id=ids, has_side_effects=True, vmem_limit_bytes=VMEM_BYTES),
        cost_estimate=pl.CostEstimate(flops=10**9, bytes_accessed=10**7, transcendentals=10**6),
        name="attention_forward",
    )(x.reshape(mbs, sub, d), gain, fgain, wqkv, wout, rwx, cos, sin)
    mid, n2, rx, rows, q, k, v, att = outs
    return mid, n2, rx, rows.reshape(mbs * length, d), q, k, v, att


def attn_bwd_kernel(cfg, dn2, g, mid, x, gain, fgain, rows, q, k, v, att, wqkv, wout, cos, sin, rot,
                    sin_p, sdt_p, rw_p, wqkv_i, wout_i, sin_i, sdt_i, small_i,
                    dx_o, wqkv_o, wout_o, sin_o, sdt_o, small_o,
                    msend, mall, dqkv, dsend, drecv, datt,
                    wqkv_p, wout_p, small_p, wqkv_x, wout_x, sin_x, sdt_x, small_x,
                    wqkv_t, wout_t, sin_t, sdt_t, small_t, wqkv_r, wout_r, sin_r, sdt_r, small_r,
                    wqkv_f, wout_f, sin_f, sdt_f, small_f, small_a,
                    m_send, m_recv, d_send, d_recv, c_send, c_recv, r_send, r_recv, a_send, a_recv, f_sem):
    layer, nx, ny, mbs, sub, width, pw, heads, features, experts = cfg
    pos = Position(nx, ny)
    s, a, b = pos.s, pos.a, pos.b
    keeper = s == layer
    helper = jnp.logical_not(keeper)
    d = ny * pw
    length = nx * sub
    scale = DH ** -0.5
    barrier = pltpu.get_barrier_semaphore()
    pos.peers(lambda ai: pl.semaphore_signal(barrier, inc=1, device_id=(s, ai, b), device_id_type=MESH))

    def line(do):
        for i in range(1, ny):
            do(lax.rem(b + i, ny))

    @pl.when(keeper)
    def _():
        line(lambda bi: pl.semaphore_signal(barrier, inc=1, device_id=(s, a, bi), device_id_type=MESH))
        pl.semaphore_signal(barrier, inc=1, device_id=(1 - s, a, b), device_id_type=MESH)

    xv = x[...]
    mv = mid[...]
    dx2, fgain_g = norm_back(mv, rms(mv, features), fgain[...], dn2[...], features)
    dm = g[...] + dx2
    msend[...] = bf(dm).reshape(mbs, sub, d)
    dx_o[...] = dm

    @pl.when(keeper)
    def _():
        pl.semaphore_wait(barrier, nx - 1 + ny - 1)

    @pl.when(helper)
    def _():
        pl.semaphore_wait(barrier, nx)

    def copy_m(ai, slot):
        return remote(msend, mall.at[:, slot], m_send.at[ai], m_recv.at[slot], (s, ai, b))

    pos.peers(lambda ai: copy_m(ai, a).start())

    crossing = ((sin_p, sin_x), (sdt_p, sdt_x), (wqkv_p, wqkv_x), (wout_p, wout_x), (small_p, small_x))

    def cross(i):
        return remote(crossing[i][0], crossing[i][1], c_send.at[i], c_recv.at[i], (layer, a, b))

    def rows_of(ref, bi, n):
        return ref.at[pl.ds(pl.multiple_of(bi * pw, pw), n)]

    def lanes_of(ref, bi):
        return ref.at[:, pl.ds(pl.multiple_of(bi * pw, pw), pw)]

    blocks = (
        lambda bi: rows_of(sin_t, bi, width), lambda bi: rows_of(sdt_t, bi, width),
        lambda bi: rows_of(wqkv_t, bi, width), lambda bi: lanes_of(wout_t, bi), lambda bi: lanes_of(small_t, bi),
    )
    totals = (sin_t, sdt_t, wqkv_t, wout_t, small_t)
    places = (sin_r, sdt_r, wqkv_r, wout_r, small_r)
    finals = (sin_f, sdt_f, wqkv_f, wout_f, small_f)
    results = (sin_o, sdt_o, wqkv_o, wout_o, small_o)

    def spread(i, bi, slot):
        return remote(blocks[i](bi), places[i].at[slot], r_send.at[i, bi], r_recv.at[i, slot], (s, a, bi))

    def join(i):
        cross(i).wait_recv()
        part, other = crossing[i]
        totals[i][...] = (part[...].astype(jnp.float32) + other[...].astype(jnp.float32)).astype(totals[i].dtype)
        line(lambda bi: spread(i, bi, b).start())

    @pl.when(helper)
    def _():
        cross(0).start()
        cross(1).start()

    mall[:, a] = msend[...]
    pos.peers(lambda ai: copy_m(ai, ai).wait())
    dmr = mall[...].reshape(mbs * length, d)
    datt[...] = bf(mm(dmr, wout[...], ((1,), (1,))))
    wout_p[...] = bf(mm(att[...], dmr, ((0,), (0,))))

    @pl.when(keeper)
    def _():
        join(0)
        join(1)

    def back(t):
        hi = bf(t)
        lo = bf(t - hi.astype(jnp.float32))
        return bf(t * cos[...] - (mm(hi, rot[...]) + mm(lo, rot[...])) * sin[...])

    for m in range(mbs):
        rs = slice(m * length, (m + 1) * length)
        dq = jnp.zeros((length, pw), jnp.float32)
        dk = dq
        dv = dq
        for h in range(heads):
            mask = head_mask(pw, h)
            qh = jnp.where(mask, q[rs], 0)
            kh = jnp.where(mask, k[rs], 0)
            da = jnp.where(mask, datt[rs], 0)
            p = probs_of(qh, k[rs])
            dp = mm(da, v[rs], ((1,), (1,)))
            ds = bf(p * (dp - jnp.sum(dp * p, axis=1, keepdims=True)))
            dv = dv + mm(bf(p), da, ((0,), (0,)))
            dq = dq + mm(ds, kh)
            dk = dk + mm(ds, qh, ((0,), (0,)))
        dqkv[rs, :pw] = back(dq * scale)
        dqkv[rs, pw : 2 * pw] = back(dk * scale)
        dqkv[rs, 2 * pw :] = bf(dv)
    dsend[...] = bf(mm(dqkv[...], wqkv[:, : 3 * pw], ((1,), (1,)))).reshape(mbs, nx, sub, d)

    def copy_d(ai, slot):
        return remote(dsend.at[:, ai], drecv.at[slot], d_send.at[ai], d_recv.at[slot], (s, ai, b))

    pos.peers(lambda ai: copy_d(ai, a).start())
    drecv[a] = dsend[:, a]
    wqkv_p[...] = bf(mm(rows[...], dqkv[...], ((0,), (0,))))

    @pl.when(helper)
    def _():
        cross(2).start()
        cross(3).start()

    pos.peers(lambda ai: copy_d(ai, ai).wait())
    dn1 = drecv[0].astype(jnp.float32)
    for ai in range(1, nx):
        dn1 = dn1 + drecv[ai].astype(jnp.float32)
    dn1 = dn1.reshape(mbs * sub, d)
    dx1, gain_g = norm_back(xv, rms(xv, features), gain[...], dn1, features)
    dx_o[...] += dx1
    small_p[: experts] = rw_p[...]
    row = lax.broadcasted_iota(jnp.int32, (8, d), 0)
    small_p[experts:] = jnp.where(row == 0, fgain_g, jnp.where(row == 1, gain_g, 0.0))

    @pl.when(helper)
    def _():
        cross(4).start()
        for i in range(5):
            cross(i).wait_send()

    @pl.when(keeper)
    def _():
        join(2)
        join(3)
        join(4)
        for i in range(5):
            line(lambda bi: spread(i, bi, bi).wait())
            total = blocks[i](b)[...].astype(jnp.float32)
            for k in range(1, ny):
                total = total + places[i][lax.rem(b + k, ny)].astype(jnp.float32)
            finals[i][...] = total
            if i < 4:
                pltpu.make_async_copy(finals[i], results[i], f_sem.at[i]).start()

        def copy_a(ai, slot):
            return remote(small_f, small_a.at[slot], a_send.at[ai], a_recv.at[slot], (s, ai, b))

        pos.peers(lambda ai: copy_a(ai, a).start())
        small_a[a] = small_f[...]
        pos.peers(lambda ai: copy_a(ai, ai).wait())
        total = small_a[0]
        for ai in range(1, nx):
            total = total + small_a[ai]
        small_f[...] = total
        pltpu.make_async_copy(small_f, small_o, f_sem.at[4]).start()
        for i in range(5):
            pltpu.make_async_copy(finals[i], results[i], f_sem.at[i]).wait()


def grad_shapes(experts, width, pw, f):
    return (
        jax.ShapeDtypeStruct((width, 3 * pw), jnp.float32),
        jax.ShapeDtypeStruct((pw, pw), jnp.float32),
        jax.ShapeDtypeStruct((width, 2 * f), jnp.float32),
        jax.ShapeDtypeStruct((width, f), jnp.float32),
        jax.ShapeDtypeStruct((experts + 8, pw), jnp.float32),
    )


def attn_bwd(layer, dn2, g, mid, fgain, x, gain, rows, q, k, v, att, wqkv, wout, cos, sin, rot,
             sin_g, sdt_g, rw_g, grads, mbs, heads, features, ids):
    nx, ny = lax.axis_size("gx"), lax.axis_size("gy")
    pw = cos.shape[1]
    d = ny * pw
    width = features // ny
    sub = x.shape[0] // mbs
    length = nx * sub
    f = sdt_g.shape[1]
    experts = rw_g.shape[0]
    b16, f32 = jnp.bfloat16, jnp.float32
    dma = pltpu.SemaphoreType.DMA
    vm = pl.BlockSpec(memory_space=pltpu.VMEM)
    hbm = pl.BlockSpec(memory_space=pl.ANY)
    shapes = grad_shapes(experts, width, pw, f)
    n = experts + 8
    outs = pl.pallas_call(
        functools.partial(attn_bwd_kernel, (layer, nx, ny, mbs, sub, width, pw, heads, features, experts)),
        out_shape=(jax.ShapeDtypeStruct((mbs * sub, d), f32),) + shapes,
        in_specs=[vm] * 19 + [hbm] * 5,
        out_specs=(vm,) + (hbm,) * 5,
        scratch_shapes=[
            pltpu.VMEM((mbs, sub, d), b16),
            pltpu.VMEM((mbs, nx, sub, d), b16),
            pltpu.VMEM((mbs * length, 3 * pw), b16),
            pltpu.VMEM((mbs, nx, sub, d), b16),
            pltpu.VMEM((nx, mbs, sub, d), b16),
            pltpu.VMEM((mbs * length, pw), b16),
            pltpu.VMEM((d, 3 * pw), b16), pltpu.VMEM((pw, d), b16), pltpu.VMEM((n, d), f32),
            pltpu.VMEM((d, 3 * pw), b16), pltpu.VMEM((pw, d), b16), pltpu.VMEM((d, 2 * f), b16),
            pltpu.VMEM((d, f), b16), pltpu.VMEM((n, d), f32),
            pltpu.VMEM((d, 3 * pw), b16), pltpu.VMEM((pw, d), b16), pltpu.VMEM((d, 2 * f), b16),
            pltpu.VMEM((d, f), b16), pltpu.VMEM((n, d), f32),
            pltpu.VMEM((ny, width, 3 * pw), b16), pltpu.VMEM((ny, pw, pw), b16), pltpu.VMEM((ny, width, 2 * f), b16),
            pltpu.VMEM((ny, width, f), b16), pltpu.VMEM((ny, n, pw), f32),
            pltpu.VMEM((width, 3 * pw), f32), pltpu.VMEM((pw, pw), f32), pltpu.VMEM((width, 2 * f), f32),
            pltpu.VMEM((width, f), f32), pltpu.VMEM((n, pw), f32),
            pltpu.VMEM((nx, n, pw), f32),
            dma((nx,)), dma((nx,)), dma((nx,)), dma((nx,)), dma((5,)), dma((5,)),
            dma((5, ny)), dma((5, ny)), dma((nx,)), dma((nx,)), dma((5,)),
        ],
        input_output_aliases={19 + i: 1 + i for i in range(5)},
        compiler_params=pltpu.CompilerParams(collective_id=ids, has_side_effects=True, vmem_limit_bytes=VMEM_BYTES),
        cost_estimate=pl.CostEstimate(flops=2 * 10**9, bytes_accessed=2 * 10**7, transcendentals=10**6),
        name="attention_backward",
    )(dn2, g, mid, x, gain, fgain, rows, q, k, v, att, wqkv, wout, cos, sin, rot, sin_g, sdt_g, rw_g, *grads)
    return outs[0], outs[1:]


def solution(mesh):
    in_specs = (
        P(None, "gx", "gy"),
        P(None, "gx", "gy"),
        P("section", "gy"),
        P("section", "gy", None, "gx"),
        P("section", "gx", "gy"),
        P("section", "gy"),
        P("section", "gy", None),
        P("section", None, "gy", None, "gx"),
        P("section", None, "gx", "gy"),
        P("section", "gy", None, "gx"),
        P("section", "gx", "gy"),
        P("section", None, None, None),
    )
    out_specs = (
        P("section", None, "gx", "gy"),
        P("section", None, "gx", "gy"),
        P("section", "gy"),
        P("section", "gy", None, "gx"),
        P("section", "gx", "gy"),
        P("section", "gy"),
        P("section", "gy", None),
        P("section", None, "gy", None, "gx"),
        P("section", None, "gx", "gy"),
        P("section", "gy", None, "gx"),
        P("section", "gx", "gy"),
    )
    fast = mesh.shape["gx"] == mesh.shape["gy"]
    return jax.shard_map(
        fast_device if fast else on_device, mesh=mesh, in_specs=in_specs, out_specs=out_specs, check_vma=False
    )
```

```python
import functools

import jax
import jax.numpy as jnp
from jax import lax
from jax.experimental import pallas as pl
from jax.experimental.pallas import tpu as pltpu
from jax.sharding import PartitionSpec as P

DH = 64


epsilon = 1e-06
highest = lax.Precision.HIGHEST


def from_partner(array, axis, apart):
    return lax.ppermute(array, axis, [(i, i ^ 1 << apart) for i in range(lax.axis_size(axis))])


def token_rows(values):
    return lax.all_gather(values, "gx", axis=0, tiled=True)


def output_rows(values):
    return lax.psum_scatter(values, "gx", scatter_dimension=0, tiled=True)


def width_sum(values):
    return lax.psum(values, "gy")


def pass_section(values):
    return from_partner(values, "section", 0)


def sequence_sums(values):
    return lax.psum_scatter(values, "gy", scatter_dimension=0, tiled=True)


def sequence_rows(values):
    return lax.all_gather(values, "gy", axis=0, tiled=True)


def gather_hidden(hidden, shared_hidden):
    return (
        lax.all_gather(hidden, "gy", axis=0, tiled=True),
        lax.all_gather(shared_hidden, "gy", axis=0, tiled=True),
    )


def rope_turn(values, positions, turn_sign):
    half_size = values.shape[-1] // 2
    frequency = 10000.0 ** (-jnp.arange(half_size, dtype=jnp.float32) / half_size)
    angles = positions[:, None] * frequency[None, :]
    cosine = jnp.cos(angles)[:, None, :]
    sine_part = turn_sign * jnp.sin(angles)[:, None, :]
    first_half = values[..., :half_size]
    second_half = values[..., half_size:]
    return jnp.concatenate(
        [
            first_half * cosine - second_half * sine_part,
            first_half * sine_part + second_half * cosine,
        ],
        axis=-1,
    )


def norm_forward(stream, gain):
    full_width = stream.shape[1] * lax.axis_size("gy")
    square_sum = width_sum(jnp.sum(stream * stream, axis=1))
    inverse_rms = lax.rsqrt(square_sum / full_width + epsilon)
    return ((stream * inverse_rms[:, None] * gain[None, :]).astype(jnp.bfloat16), inverse_rms)


def norm_backward(stream, inverse_rms, gain, grad_normed):
    full_width = stream.shape[1] * lax.axis_size("gy")
    scaled = grad_normed * gain[None, :]
    inner_sum = width_sum(jnp.sum(scaled * stream, axis=1))
    cubed = inverse_rms * inverse_rms * inverse_rms
    grad_stream = inverse_rms[:, None] * scaled - stream * (cubed * inner_sum / full_width)[:, None]
    grad_gain = jnp.sum(grad_normed * stream * inverse_rms[:, None], axis=0)
    return (grad_stream, grad_gain)


def slot_table(route_ids, experts, capacity):
    flat_ids = route_ids.reshape(-1)
    assigned = (flat_ids[:, None] == jnp.arange(experts, dtype=jnp.int32)[None, :]).astype(
        jnp.int32
    )
    earlier = jnp.cumsum(assigned, axis=0) - assigned
    places = flat_ids * capacity + jnp.sum(earlier * assigned, axis=1)
    owners = jnp.arange(flat_ids.shape[0], dtype=jnp.int32) // 2
    slot_token = jnp.zeros((experts * capacity,), jnp.int32).at[places].set(owners)
    slot_valid = jnp.zeros((experts * capacity,), jnp.int32).at[places].set(jnp.ones_like(owners))
    return (places.reshape(-1, 2), slot_token, slot_valid)


def expert_act(gate_up, logits):
    half_size = gate_up.shape[1] // 2
    return (
        jax.nn.silu(gate_up[:, :half_size])
        * gate_up[:, half_size:]
        * jax.nn.sigmoid(logits)[:, None]
    )


def shared_act(gate_up):
    half_size = gate_up.shape[1] // 2
    return jax.nn.silu(gate_up[:, :half_size]) * gate_up[:, half_size:]


def causal_scores(queries, keys_part):
    score_scale = queries.shape[-1] ** (-0.5)
    scores = (
        jnp.einsum("qhd,khd->hqk", queries, keys_part, preferred_element_type=jnp.float32)
        * score_scale
    )
    length = queries.shape[0]
    causal = jnp.arange(length)[:, None] >= jnp.arange(length)[None, :]
    return jnp.where(causal[None], scores, -1e30)


def attend_forward(queries, keys_part, values_part):
    scores = causal_scores(queries, keys_part)
    row_max = jnp.max(scores, axis=-1, keepdims=True)
    exponent = jnp.exp(scores - row_max)
    row_total = jnp.sum(exponent, axis=-1, keepdims=True)
    probabilities = (exponent / row_total).astype(jnp.bfloat16)
    attended = jnp.einsum(
        "hqk,khd->qhd", probabilities, values_part, preferred_element_type=jnp.float32
    )
    return (attended, row_max + jnp.log(row_total))


def attend_backward(queries, keys_part, values_part, log_total, grad_attended):
    score_scale = queries.shape[-1] ** (-0.5)
    probabilities = jnp.exp(causal_scores(queries, keys_part) - log_total)
    grad_values = jnp.einsum(
        "hqk,qhd->khd",
        probabilities.astype(jnp.bfloat16),
        grad_attended,
        preferred_element_type=jnp.float32,
    )
    grad_probs = jnp.einsum(
        "qhd,khd->hqk", grad_attended, values_part, preferred_element_type=jnp.float32
    )
    grad_scores = (
        probabilities * (grad_probs - jnp.sum(grad_probs * probabilities, axis=-1, keepdims=True))
    ).astype(jnp.bfloat16)
    grad_queries = (
        jnp.einsum("hqk,khd->qhd", grad_scores, keys_part, preferred_element_type=jnp.float32)
        * score_scale
    )
    grad_keys = (
        jnp.einsum("hqk,qhd->khd", grad_scores, queries, preferred_element_type=jnp.float32)
        * score_scale
    )
    return (grad_queries, grad_keys, grad_values)


def layer_forward(stream, weights, route_ids):
    (
        attention_gain,
        attention_in,
        attention_out,
        feed_gain,
        router_weight,
        expert_in,
        expert_down,
        shared_in,
        shared_down,
    ) = weights
    local_width = stream.shape[1]
    experts = expert_in.shape[0]
    normed, inverse_first = norm_forward(stream, attention_gain)
    rows_first = token_rows(normed)
    tokens = rows_first.shape[0]
    capacity = 5 * tokens // (2 * experts)
    slot_count = experts * capacity
    projected = sequence_sums(
        jnp.dot(
            rows_first, attention_in.reshape(local_width, -1), preferred_element_type=jnp.float32
        )
    )
    length = projected.shape[0]
    projected = projected.reshape(length, 3, -1, DH)
    positions = jnp.arange(length, dtype=jnp.float32)
    queries = rope_turn(projected[:, 0], positions, 1.0).astype(jnp.bfloat16)
    keys_part = rope_turn(projected[:, 1], positions, 1.0).astype(jnp.bfloat16)
    values_part = projected[:, 2].astype(jnp.bfloat16)
    attended, log_total = attend_forward(queries, keys_part, values_part)
    attended_rows = sequence_rows(attended.astype(jnp.bfloat16).reshape(length, -1))
    middle = stream + output_rows(
        jnp.dot(attended_rows, attention_out, preferred_element_type=jnp.float32)
    )
    normed_feed, inverse_second = norm_forward(middle, feed_gain)
    rows_second = token_rows(normed_feed)
    route_slot, slot_token, slot_valid = slot_table(route_ids, experts, capacity)
    grouped = (rows_second[slot_token] * slot_valid[:, None].astype(jnp.bfloat16)).reshape(
        experts, capacity, local_width
    )
    expert_part = jnp.einsum(
        "ecd,edf->ecf",
        grouped,
        expert_in.reshape(experts, local_width, -1),
        preferred_element_type=jnp.float32,
    )
    router_part = jnp.einsum(
        "ecd,de->ec", grouped, router_weight, preferred_element_type=jnp.float32
    )
    shared_part = jnp.dot(
        rows_second, shared_in.reshape(local_width, -1), preferred_element_type=jnp.float32
    )
    expert_gu, router_logit, shared_gu = (
        lax.psum_scatter(
            expert_part.reshape(slot_count, -1), "gy", scatter_dimension=0, tiled=True
        ),
        lax.psum_scatter(router_part.reshape(slot_count), "gy", scatter_dimension=0, tiled=True),
        lax.psum_scatter(shared_part, "gy", scatter_dimension=0, tiled=True),
    )
    hidden_rows, shared_rows = gather_hidden(
        expert_act(expert_gu, router_logit).astype(jnp.bfloat16),
        shared_act(shared_gu).astype(jnp.bfloat16),
    )
    expert_result = jnp.einsum(
        "ecf,efd->ecd",
        hidden_rows.reshape(experts, capacity, -1),
        expert_down,
        preferred_element_type=jnp.float32,
    ).reshape(slot_count, local_width)
    branch = (
        expert_result[route_slot[:, 0]]
        + expert_result[route_slot[:, 1]]
        + jnp.dot(shared_rows, shared_down, preferred_element_type=jnp.float32)
    )
    result = middle + output_rows(branch)
    kept_items = (
        stream,
        inverse_first,
        rows_first,
        queries,
        keys_part,
        values_part,
        log_total,
        attended_rows,
        middle,
        inverse_second,
        rows_second,
        expert_gu,
        router_logit,
        shared_gu,
    )
    return (result, kept_items)


def layer_backward(grad_out, kept_items, weights, route_ids):
    (
        attention_gain,
        attention_in,
        attention_out,
        feed_gain,
        router_weight,
        expert_in,
        expert_down,
        shared_in,
        shared_down,
    ) = weights
    (
        stream,
        inverse_first,
        rows_first,
        queries,
        keys_part,
        values_part,
        log_total,
        attended_rows,
        middle,
        inverse_second,
        rows_second,
        expert_gu,
        router_logit,
        shared_gu,
    ) = kept_items[:14]
    local_width = stream.shape[1]
    experts = expert_in.shape[0]
    tokens = rows_second.shape[0]
    capacity = 5 * tokens // (2 * experts)
    slot_count = experts * capacity
    hidden_rows, shared_rows = gather_hidden(
        expert_act(expert_gu, router_logit).astype(jnp.bfloat16),
        shared_act(shared_gu).astype(jnp.bfloat16),
    )
    route_slot, slot_token, slot_valid = slot_table(route_ids, experts, capacity)
    valid_rows = slot_valid[:, None].astype(jnp.bfloat16)
    grouped = (rows_second[slot_token] * valid_rows).reshape(experts, capacity, local_width)
    grad_rows = token_rows(grad_out.astype(jnp.bfloat16))
    slot_grad = (grad_rows[slot_token] * valid_rows).reshape(experts, capacity, local_width)
    down_grad = jnp.einsum(
        "ecf,ecd->efd",
        hidden_rows.reshape(experts, capacity, -1),
        slot_grad,
        preferred_element_type=jnp.float32,
    )
    shared_down_grad = jnp.einsum(
        "tf,td->fd", shared_rows, grad_rows, preferred_element_type=jnp.float32
    )
    hidden_part = jnp.einsum(
        "ecd,efd->ecf", slot_grad, expert_down, preferred_element_type=jnp.float32
    ).reshape(slot_count, -1)
    shared_part = jnp.einsum(
        "td,fd->tf", grad_rows, shared_down, preferred_element_type=jnp.float32
    )
    grad_hidden, grad_shared = (
        lax.psum_scatter(
            hidden_part.astype(jnp.bfloat16), "gy", scatter_dimension=0, tiled=True
        ).astype(jnp.float32),
        lax.psum_scatter(
            shared_part.astype(jnp.bfloat16), "gy", scatter_dimension=0, tiled=True
        ).astype(jnp.float32),
    )
    unused_expert, expert_back = jax.vjp(expert_act, expert_gu, router_logit)
    grad_gu, grad_logit = expert_back(grad_hidden)
    unused_shared, shared_back = jax.vjp(shared_act, shared_gu)
    (grad_shared_gu,) = shared_back(grad_shared)
    gu_rows, shared_gu_rows = (
        lax.all_gather(grad_gu.astype(jnp.bfloat16), "gy", axis=0, tiled=True),
        lax.all_gather(grad_shared_gu.astype(jnp.bfloat16), "gy", axis=0, tiled=True),
    )
    logit_rows = lax.all_gather(grad_logit, "gy", axis=0, tiled=True).reshape(experts, capacity)
    gu_grouped = gu_rows.reshape(experts, capacity, -1)
    in_grad = jnp.einsum("ecd,ecf->edf", grouped, gu_grouped, preferred_element_type=jnp.float32)
    router_grad = jnp.einsum(
        "ecd,ec->de", grouped.astype(jnp.float32), logit_rows, precision=highest
    )
    shared_in_grad = jnp.einsum(
        "td,tf->df", rows_second, shared_gu_rows, preferred_element_type=jnp.float32
    )
    slot_back = jnp.einsum(
        "ecf,edf->ecd",
        gu_grouped,
        expert_in.reshape(experts, local_width, -1),
        preferred_element_type=jnp.float32,
    )
    slot_back = slot_back + logit_rows[:, :, None] * router_weight.T.astype(jnp.float32)[:, None, :]
    slot_back = slot_back.reshape(slot_count, local_width)
    rows_back = (
        slot_back[route_slot[:, 0]]
        + slot_back[route_slot[:, 1]]
        + jnp.einsum(
            "tf,df->td",
            shared_gu_rows,
            shared_in.reshape(local_width, -1),
            preferred_element_type=jnp.float32,
        )
    )
    grad_middle_norm, feed_gain_grad = norm_backward(
        middle, inverse_second, feed_gain, output_rows(rows_back)
    )
    grad_middle = grad_out + grad_middle_norm
    middle_rows = token_rows(grad_middle.astype(jnp.bfloat16))
    out_weight_grad = jnp.einsum(
        "tf,td->fd", attended_rows, middle_rows, preferred_element_type=jnp.float32
    )
    grad_attended = sequence_sums(
        jnp.einsum("td,fd->tf", middle_rows, attention_out, preferred_element_type=jnp.float32)
    )
    length = grad_attended.shape[0]
    positions = jnp.arange(length, dtype=jnp.float32)
    grad_queries, grad_keys, grad_values = attend_backward(
        queries,
        keys_part,
        values_part,
        log_total,
        grad_attended.astype(jnp.bfloat16).reshape(queries.shape),
    )
    grad_projected = jnp.stack(
        [
            rope_turn(grad_queries, positions, -1.0),
            rope_turn(grad_keys, positions, -1.0),
            grad_values,
        ],
        axis=1,
    )
    grad_projected = grad_projected.astype(jnp.bfloat16).reshape(length, -1)
    projected_rows = sequence_rows(grad_projected)
    in_weight_grad = jnp.einsum(
        "td,tf->df", rows_first, projected_rows, preferred_element_type=jnp.float32
    )
    grad_normed = output_rows(
        jnp.einsum(
            "tf,df->td",
            projected_rows,
            attention_in.reshape(local_width, -1),
            preferred_element_type=jnp.float32,
        )
    )
    grad_stream_norm, attention_gain_grad = norm_backward(
        stream, inverse_first, attention_gain, grad_normed
    )
    layer_grads = (
        attention_gain_grad,
        in_weight_grad.reshape(attention_in.shape),
        out_weight_grad,
        feed_gain_grad,
        router_grad,
        in_grad.reshape(expert_in.shape),
        down_grad,
        shared_in_grad.reshape(shared_in.shape),
        shared_down_grad,
    )
    return (grad_middle + grad_stream_norm, layer_grads)


def put_item(buffer, value, batch_index, is_valid):
    current = lax.dynamic_index_in_dim(buffer, batch_index, 0, keepdims=False)
    return lax.dynamic_update_index_in_dim(
        buffer, jnp.where(is_valid, value, current), batch_index, 0
    )


def on_device(
    block_input,
    output_grad,
    attention_gain,
    attention_in,
    attention_out,
    feed_gain,
    router_weight,
    expert_in,
    expert_down,
    shared_in,
    shared_down,
    routes,
):
    section_index = lax.axis_index("section")
    batches = block_input.shape[0]
    weights = tuple(
        (
            member[0]
            for member in (
                attention_gain,
                attention_in,
                attention_out,
                feed_gain,
                router_weight,
                expert_in,
                expert_down,
                shared_in,
                shared_down,
            )
        )
    )
    route_table = routes[0]
    outputs = jnp.zeros(block_input.shape, jnp.bfloat16)
    received = jnp.zeros(block_input.shape[1:], jnp.bfloat16)
    stored = None
    for tick_step in range(batches + 1):
        micro_index = tick_step - section_index
        is_valid = (micro_index >= 0) & (micro_index < batches)
        batch_index = jnp.clip(micro_index, 0, batches - 1)
        fresh_input = lax.dynamic_index_in_dim(block_input, batch_index, 0, keepdims=False)
        incoming = jnp.where(section_index == 0, fresh_input, received).astype(jnp.float32)
        route_ids = lax.dynamic_index_in_dim(route_table, batch_index, 0, keepdims=False)
        result, kept_items = layer_forward(incoming, weights, route_ids)
        result_low = result.astype(jnp.bfloat16)
        outputs = put_item(outputs, result_low, batch_index, is_valid)
        if stored is None:
            stored = tuple(
                (jnp.zeros((batches,) + member.shape, member.dtype) for member in kept_items)
            )
        stored = tuple(
            (
                put_item(buffer, member, batch_index, is_valid)
                for buffer, member in zip(stored, kept_items)
            )
        )
        if tick_step < batches:
            received = pass_section(result_low)
    grads_in = jnp.zeros(block_input.shape, jnp.bfloat16)
    received = jnp.zeros(block_input.shape[1:], jnp.bfloat16)
    totals = tuple((jnp.zeros(member.shape, jnp.float32) for member in weights))
    for tick_step in range(batches + 1):
        micro_index = batches - tick_step - section_index
        is_valid = (micro_index >= 0) & (micro_index < batches)
        batch_index = jnp.clip(micro_index, 0, batches - 1)
        given_grad = lax.dynamic_index_in_dim(output_grad, batch_index, 0, keepdims=False)
        incoming = jnp.where(section_index == 1, given_grad, received).astype(jnp.float32)
        kept_items = tuple(
            (lax.dynamic_index_in_dim(buffer, batch_index, 0, keepdims=False) for buffer in stored)
        )
        route_ids = lax.dynamic_index_in_dim(route_table, batch_index, 0, keepdims=False)
        grad_input, layer_grads = layer_backward(incoming, kept_items, weights, route_ids)
        grad_low = grad_input.astype(jnp.bfloat16)
        grads_in = put_item(grads_in, grad_low, batch_index, is_valid)
        totals = tuple(
            (total + jnp.where(is_valid, member, 0.0) for total, member in zip(totals, layer_grads))
        )
        if tick_step < batches:
            received = pass_section(grad_low)
    gain_first, gain_second, router_total = lax.psum((totals[0], totals[3], totals[4]), "gx")
    return (
        outputs[None],
        grads_in[None],
        gain_first[None],
        totals[1][None],
        totals[2][None],
        gain_second[None],
        router_total[None],
        totals[5][None],
        totals[6][None],
        totals[7][None],
        totals[8][None],
    )


def lanes_up(n):
    return -(-n // 128) * 128


def rot_columns(w):
    shape = w.shape
    w = w.reshape(shape[:-1] + (-1, 2, DH // 2))
    w = jnp.stack([-w[..., 1, :], w[..., 0, :]], axis=-2)
    return w.reshape(shape)


def pad_to(v, axis, n):
    pads = [(0, 0)] * v.ndim
    pads[axis] = (0, n - v.shape[axis])
    return jnp.pad(v, pads)


def mm(a, b, dims=((1,), (0,))):
    return lax.dot_general(a, b, (dims, ((), ())), preferred_element_type=jnp.float32)


def bf(v):
    return v.astype(jnp.bfloat16)


def head_mask(pw, h):
    lane = lax.broadcasted_iota(jnp.int32, (1, pw), 1)
    return (lane >= h * DH) & (lane < (h + 1) * DH)


def rms(x, features):
    return lax.rsqrt(jnp.sum(x * x, axis=1, keepdims=True) / features + epsilon)


def norm_back(x, inv, gain, d, features):
    u = d * gain
    inner = jnp.sum(u * x, axis=1, keepdims=True) / features
    dx = inv * u - x * (inv * inv * inv * inner)
    return dx, jnp.sum(d * x * inv, axis=0, keepdims=True)


def probs_of(q, k):
    s = mm(q, k, ((1,), (1,))) * DH ** -0.5
    n = s.shape[0]
    causal = lax.broadcasted_iota(jnp.int32, (n, n), 0) >= lax.broadcasted_iota(jnp.int32, (n, n), 1)
    s = jnp.where(causal, s, -1e30)
    e = jnp.exp(s - jnp.max(s, axis=1, keepdims=True))
    return e / jnp.sum(e, axis=1, keepdims=True)


def act_back(gate, up, dh, s):
    sg = jax.nn.sigmoid(gate)
    silu = gate * sg
    if s is None:
        return dh * up * (sg * (1.0 + gate * (1.0 - sg))), dh * silu, None
    dr = jnp.sum(dh * silu * up, axis=-1, keepdims=True) * s * (1.0 - s)
    ds = dh * s
    return ds * up * (sg * (1.0 + gate * (1.0 - sg))), ds * silu, dr


def places_of(routes, experts, capacity):
    lead = routes.shape[:-2]
    ids = routes.reshape((-1, routes.shape[-2] * 2))
    n = ids.shape[1]
    hot = (ids[..., None] == jnp.arange(experts, dtype=jnp.int32)).astype(jnp.bfloat16)
    before = (jnp.arange(n)[:, None] > jnp.arange(n)[None, :]).astype(jnp.bfloat16)
    earlier = jnp.einsum("ij,bje->bie", before, hot, preferred_element_type=jnp.float32)
    rank = jnp.sum(earlier * hot.astype(jnp.float32), -1).astype(jnp.int32)
    place = (ids * capacity + rank).reshape(lead + (-1, 2))
    return jnp.moveaxis(place, -1, -2)


MESH = pl.DeviceIdType.MESH
VMEM_BYTES = 60 * 2**20


def remote(src, dst, send, recv, target):
    return pltpu.make_async_remote_copy(
        src_ref=src, dst_ref=dst, send_sem=send, recv_sem=recv, device_id=target, device_id_type=MESH
    )


def router_column(rows, e, width, experts):
    lane = lax.broadcasted_iota(jnp.int32, rows.shape, rows.ndim - 1)
    mask = (lane == width + e) | (lane == width + experts + e)
    return jnp.sum(jnp.where(mask, rows.astype(jnp.float32), 0.0), axis=-1, keepdims=True)


class Position:
    def __init__(self, nx, ny):
        self.s = lax.axis_index("section")
        self.a = lax.axis_index("gx")
        self.b = lax.axis_index("gy")
        self.nx, self.ny = nx, ny
        self.n = nx * ny
        self.me = self.a * ny + self.b

    def device(self, index):
        return (self.s, index // self.ny, lax.rem(index, self.ny))

    def others(self, do):
        def step(i, c):
            index = lax.rem(self.me + i, self.n)
            do(index, index // self.ny, lax.rem(index, self.ny))
            return c

        lax.fori_loop(1, self.n, step, 0)

    def peers(self, do):
        for i in range(1, self.nx):
            do(lax.rem(self.a + i, self.nx))


def greet_section(pos):
    barrier = pltpu.get_barrier_semaphore()

    def one(index, ai, bi):
        pl.semaphore_signal(barrier, inc=1, device_id=(pos.s, ai, bi), device_id_type=MESH)

    pos.others(one)
    return barrier


def flags(count):
    return pltpu.SemaphoreType.DMA(count)


class Share:
    def __init__(self, pos, layer, block, full, sems):
        self.pos, self.layer, self.block, self.full = pos, layer, block, full
        self.sems = sems
        self.source = pos.s == layer

    def line(self, do):
        for i in range(1, self.pos.ny):
            do(lax.rem(self.pos.b + i, self.pos.ny))

    def signal(self, barrier, with_line):
        pos = self.pos
        if with_line:
            @pl.when(self.source)
            def _():
                self.line(lambda bi: pl.semaphore_signal(
                    barrier, inc=1, device_id=(pos.s, pos.a, bi), device_id_type=MESH))

        @pl.when(jnp.logical_not(self.source))
        def _():
            pl.semaphore_signal(barrier, inc=1, device_id=(1 - pos.s, pos.a, pos.b), device_id_type=MESH)

    def wait_barrier(self, barrier, count, with_line):
        @pl.when(self.source)
        def _():
            pl.semaphore_wait(barrier, count + 1 + (self.pos.ny - 1 if with_line else 0))

        @pl.when(jnp.logical_not(self.source))
        def _():
            pl.semaphore_wait(barrier, count)

    def along(self, bi, slot):
        pos = self.pos
        return remote(self.block, self.full.at[slot], self.sems[0].at[bi], self.sems[1].at[slot], (pos.s, pos.a, bi))

    def across(self, src, slot):
        pos = self.pos
        return remote(src, self.full.at[slot], self.sems[2].at[slot], self.sems[3].at[slot], (1 - pos.s, pos.a, pos.b))

    def start(self):
        b = self.pos.b

        @pl.when(self.source)
        def _():
            self.line(lambda bi: self.along(bi, b).start())
            self.across(self.block, b).start()
            self.full[b] = self.block[...]

    def forward(self):
        @pl.when(self.source)
        def _():
            def one(bi):
                self.along(bi, bi).wait_recv()
                self.across(self.full.at[bi], bi).start()

            self.line(one)

    def finish(self):
        b = self.pos.b

        @pl.when(self.source)
        def _():
            def one(bi):
                self.along(bi, bi).wait_send()
                self.across(self.full.at[bi], bi).wait_send()

            self.line(one)
            self.across(self.block, b).wait_send()

        @pl.when(jnp.logical_not(self.source))
        def _():
            for j in range(self.pos.ny):
                self.across(self.full.at[j], j).wait_recv()


def share_sems(ny):
    return [flags((ny,))] * 4


def params(ids):
    return pltpu.CompilerParams(collective_id=ids, has_side_effects=True, vmem_limit_bytes=VMEM_BYTES)


def greet_all(pos):
    barrier = pltpu.get_barrier_semaphore()
    total = 2 * pos.n
    mine = pos.s * pos.n + pos.me

    def one(i, c):
        index = lax.rem(mine + i, total)
        rest = lax.rem(index, pos.n)
        pl.semaphore_signal(
            barrier, inc=1, device_id=(index // pos.n, rest // pos.ny, lax.rem(rest, pos.ny)), device_id_type=MESH)
        return c

    lax.fori_loop(1, total, one, 0)
    pl.semaphore_wait(barrier, total - 1)


def entry_kernel(cfg, tin, watt, small, tok, watt0, small_o, tbuf, wbuf, sbuf,
                 t_send, t_recv, s_send, s_recv, *w_sems):
    nx, ny, mbs, sub, pw = cfg
    pos = Position(nx, ny)
    s, a, b = pos.s, pos.a, pos.b
    greet_all(pos)
    share = Share(pos, 0, watt, wbuf, w_sems)

    def tokens(i, slot, seq):
        src = tin.at[:, :, pl.ds(pl.multiple_of(i * sub, sub), sub), :]
        return remote(src, tbuf.at[slot], t_send.at[i], t_recv.at[slot], (s, i, seq))

    for k in range(nx):
        i = lax.rem(a + k, nx)

        @pl.when(jnp.logical_or(i != a, a != b))
        def _():
            tokens(i, b, a).start()

    @pl.when(a == b)
    def _():
        tbuf[b] = tin[:, :, pl.ds(pl.multiple_of(a * sub, sub), sub), :]

    def gains(so, bi, s_slot, b_slot):
        return remote(small, sbuf.at[s_slot, b_slot], s_send.at[so, bi], s_recv.at[s_slot, b_slot], (so, a, bi))

    def each_gain(do):
        for so in range(2):
            for bi in range(ny):
                @pl.when(jnp.logical_or(s != so, b != bi))
                def _():
                    do(so, bi)

    each_gain(lambda so, bi: gains(so, bi, s, b).start())
    sbuf[s, b] = small[...]
    share.start()
    share.forward()
    each_gain(lambda so, bi: gains(so, bi, so, bi).wait())
    for l in range(2):
        for j in range(ny):
            small_o[l, :, j * pw : (j + 1) * pw] = sbuf[l, j]
    for k in range(nx):
        i = lax.rem(a + k, nx)

        @pl.when(jnp.logical_or(i != a, a != b))
        def _():
            tokens(i, b, a).wait_send()

    for j in range(ny):
        @pl.when(jnp.logical_or(a != b, b != j))
        def _():
            tokens(a, j, j).wait_recv()

        tok[:, :, :, j * pw : (j + 1) * pw] = tbuf[j]
    share.finish()
    watt0[...] = wbuf[...]


def entry(tin, watt, small, ids):
    nx, ny = lax.axis_size("gx"), lax.axis_size("gy")
    kinds, mbs, length, pw = tin.shape
    sub = length // nx
    width, cols = watt.shape
    vm = pl.BlockSpec(memory_space=pltpu.VMEM)
    b16, f32 = jnp.bfloat16, jnp.float32
    return pl.pallas_call(
        functools.partial(entry_kernel, (nx, ny, mbs, sub, pw)),
        out_shape=(
            jax.ShapeDtypeStruct((kinds, mbs, sub, ny * pw), b16),
            jax.ShapeDtypeStruct((ny, width, cols), b16),
            jax.ShapeDtypeStruct((2, small.shape[0], ny * pw), f32),
        ),
        in_specs=[vm] * 3,
        out_specs=(vm,) * 3,
        scratch_shapes=[
            pltpu.VMEM((ny, kinds, mbs, sub, pw), b16),
            pltpu.VMEM((ny, width, cols), b16),
            pltpu.VMEM((2, ny, small.shape[0], pw), f32),
            flags((nx,)), flags((ny,)), flags((2, ny)), flags((2, ny)),
        ] + share_sems(ny),
        compiler_params=params(ids),
        name="entry",
    )(tin, watt, small)


def leave_kernel(cfg, pair0, pair1, out, buf, t_send, t_recv):
    nx, ny, mbs, sub, pw = cfg
    pos = Position(nx, ny)
    s, a, b = pos.s, pos.a, pos.b
    greet_all(pos)
    pairs = (pair0, pair1)

    def copy(l, j, s_slot, a_slot, seq):
        src = pairs[l].at[:, :, :, pl.ds(pl.multiple_of(j * pw, pw), pw)]
        return remote(src, buf.at[s_slot, a_slot], t_send.at[l, j], t_recv.at[s_slot, a_slot], (l, seq, j))

    for l in range(2):
        for j in range(ny):
            @pl.when((l != s) | (a != b) | (j != b))
            def _():
                copy(l, j, s, a, b).start()

        @pl.when((l == s) & (a == b))
        def _():
            buf[s, a] = pairs[l][:, :, :, pl.ds(pl.multiple_of(b * pw, pw), pw)]

    for so in range(2):
        for i in range(nx):
            @pl.when((so != s) | (a != b) | (i != a))
            def _():
                copy(0, 0, so, i, i).wait_recv()

            out[:, so * mbs : (so + 1) * mbs, i * sub : (i + 1) * sub, :] = buf[so, i]
    for l in range(2):
        for j in range(ny):
            @pl.when((l != s) | (a != b) | (j != b))
            def _():
                copy(l, j, s, a, b).wait_send()


def leave(pair0, pair1, pw, ids):
    nx, ny = lax.axis_size("gx"), lax.axis_size("gy")
    kinds, mbs, sub, d = pair0.shape
    vm = pl.BlockSpec(memory_space=pltpu.VMEM)
    return pl.pallas_call(
        functools.partial(leave_kernel, (nx, ny, mbs, sub, pw)),
        out_shape=jax.ShapeDtypeStruct((kinds, 2 * mbs, nx * sub, pw), jnp.bfloat16),
        in_specs=[vm] * 2,
        out_specs=vm,
        scratch_shapes=[
            pltpu.VMEM((2, nx, kinds, mbs, sub, pw), jnp.bfloat16),
            flags((2, ny)), flags((2, nx)),
        ],
        compiler_params=params(ids),
        name="leave",
    )(pair0, pair1)


def turn(t, cos, sin, rot, sign):
    hi = bf(t)
    lo = bf(t - hi.astype(jnp.float32))
    return bf(t * cos + sign * ((mm(hi, rot) + mm(lo, rot)) * sin))


def by_blocks(rows, full, cols, width, pw):
    total = None
    for j in range(full.shape[0]):
        part = mm(rows[:, j * pw : j * pw + width], full[j, :, cols])
        total = part if total is None else total + part
    return total


def attn_fwd_kernel(cfg, x, small, watt, shw, cos, sin, rot,
                    mid, n2, rx, rows_o, q, k, v, att, shw_o,
                    nsend, nall, proj, osend, orecv, rwx, shfull,
                    n_send, n_recv, o_send, o_recv, w_sem, *w_sems):
    layer, nx, ny, mbs, sub, width, pw, heads, features, experts = cfg
    pos = Position(nx, ny)
    s, a, b = pos.s, pos.a, pos.b
    d = ny * pw
    length = nx * sub
    barrier = pltpu.get_barrier_semaphore()
    share = Share(pos, layer, shw, shfull, w_sems)
    pos.peers(lambda ai: pl.semaphore_signal(barrier, inc=1, device_id=(s, ai, b), device_id_type=MESH))
    share.signal(barrier, True)
    xv = x[...].reshape(mbs * sub, d).astype(jnp.float32)
    gain = small[experts + 1 : experts + 2]
    fgain = small[experts : experts + 1]
    nsend[...] = bf(xv * rms(xv, features) * gain).reshape(mbs, sub, d)
    share.wait_barrier(barrier, nx - 1, True)

    def copy_n(ai, slot):
        return remote(nsend, nall.at[:, slot], n_send.at[ai], n_recv.at[slot], (s, ai, b))

    pos.peers(lambda ai: copy_n(ai, a).start())
    share.start()
    nall[:, a] = nsend[...]
    osend[...] = jnp.zeros_like(osend)
    rwx[...] = jnp.zeros_like(rwx)
    rwx[width : width + experts] = bf(small[:experts])
    rwx[width + experts : width + 2 * experts] = bf(small[:experts])
    pos.peers(lambda ai: copy_n(ai, ai).wait())
    rows = nall[...].reshape(mbs * length, d)
    proj[...] = by_blocks(rows, watt, slice(0, 3 * pw), width, pw)
    rows_o[...] = nall[...]
    v[...] = bf(proj[:, 2 * pw : 3 * pw])
    for m in range(mbs):
        rs = slice(m * length, (m + 1) * length)
        q[rs] = turn(proj[rs, :pw], cos[...], sin[...], rot[...], 1.0)
        k[rs] = turn(proj[rs, pw : 2 * pw], cos[...], sin[...], rot[...], 1.0)
        acc = jnp.zeros((length, pw), jnp.float32)
        for h in range(heads):
            mask = head_mask(pw, h)
            p = probs_of(jnp.where(mask, q[rs], 0), k[rs])
            acc = acc + mm(bf(p), jnp.where(mask, v[rs], 0))
        att[rs] = bf(acc)
    for j in range(ny):
        part = mm(att[...], watt[j, :, 3 * pw : 4 * pw], ((1,), (1,)))
        osend[..., j * pw : j * pw + width] = bf(part).reshape(mbs, nx, sub, width)

    def copy_o(ai, slot):
        return remote(osend.at[:, ai], orecv.at[slot], o_send.at[ai], o_recv.at[slot], (s, ai, b))

    pos.peers(lambda ai: copy_o(ai, a).start())
    orecv[a] = osend[:, a]
    share.forward()
    pos.peers(lambda ai: copy_o(ai, ai).wait())
    mv = xv.reshape(mbs, sub, d)
    for ai in range(nx):
        mv = mv + orecv[ai].astype(jnp.float32)
    mv = mv.reshape(mbs * sub, d)
    mid[...] = mv
    n2v = bf(mv * rms(mv, features) * fgain)
    n2[...] = n2v
    rx[...] = mm(n2v, rwx[...], ((1,), (1,)))
    share.finish()
    keep = pltpu.make_async_copy(shfull, shw_o, w_sem)
    keep.start()
    keep.wait()


def attn_fwd(layer, x, small, watt, shw, cos, sin, rot, dims, heads, features, ids):
    width, pw, experts, cap = dims
    nx, ny = lax.axis_size("gx"), lax.axis_size("gy")
    d = ny * pw
    mbs, sub = x.shape[:2]
    length = nx * sub
    b16, f32 = jnp.bfloat16, jnp.float32
    vm = pl.BlockSpec(memory_space=pltpu.VMEM)
    hbm = pl.BlockSpec(memory_space=pl.ANY)
    return pl.pallas_call(
        functools.partial(attn_fwd_kernel, (layer, nx, ny, mbs, sub, width, pw, heads, features, experts)),
        out_shape=(
            jax.ShapeDtypeStruct((mbs * sub, d), f32),
            jax.ShapeDtypeStruct((mbs * sub, d), b16),
            jax.ShapeDtypeStruct((mbs * sub, pw), f32),
            jax.ShapeDtypeStruct((mbs, nx, sub, d), b16),
            jax.ShapeDtypeStruct((mbs * length, pw), b16),
            jax.ShapeDtypeStruct((mbs * length, pw), b16),
            jax.ShapeDtypeStruct((mbs * length, pw), b16),
            jax.ShapeDtypeStruct((mbs * length, pw), b16),
            jax.ShapeDtypeStruct((ny,) + shw.shape, b16),
        ),
        in_specs=[vm] * 7,
        out_specs=(vm,) * 8 + (hbm,),
        scratch_shapes=[
            pltpu.VMEM((mbs, sub, d), b16),
            pltpu.VMEM((mbs, nx, sub, d), b16),
            pltpu.VMEM((mbs * length, 3 * pw), f32),
            pltpu.VMEM((mbs, nx, sub, d), b16),
            pltpu.VMEM((nx, mbs, sub, d), b16),
            pltpu.VMEM((pw, d), b16),
            pltpu.VMEM((ny,) + shw.shape, b16),
            flags((nx,)), flags((nx,)), flags((nx,)), flags((nx,)), pltpu.SemaphoreType.DMA,
        ] + share_sems(ny),
        compiler_params=params(ids),
        cost_estimate=pl.CostEstimate(flops=10**9, bytes_accessed=10**7, transcendentals=10**6),
        name="attention_forward",
    )(x, small, watt, shw, cos, sin, rot)


def attn_bwd_kernel(cfg, *refs):
    layer, nx, ny, mbs, sub, width, pw, heads, features, experts = cfg
    (dn2, g, mid, x, small, rows, q, k, v, att, watt, cos, sin, rot, sh_p, rw_p) = refs[:16]
    refs = refs[16 + (0 if layer else 3) :]
    (dx_o, att_o, sh_o, small_o,
     msend, mall, dqkv, dsend, drecv, datt,
     att_p, small_p, sh_x, att_x, small_x, sh_t, att_t, small_t, sh_r, att_r, small_r,
     sh_f, att_f, small_f, small_a,
     m_send, m_recv, d_send, d_recv, c_send, c_recv, r_send, r_recv, a_send, a_recv, f_sem) = refs
    pos = Position(nx, ny)
    s, a, b = pos.s, pos.a, pos.b
    keeper = s == layer
    helper = jnp.logical_not(keeper)
    d = ny * pw
    length = nx * sub
    scale = DH ** -0.5
    barrier = pltpu.get_barrier_semaphore()
    pos.peers(lambda ai: pl.semaphore_signal(barrier, inc=1, device_id=(s, ai, b), device_id_type=MESH))

    def line(do):
        for i in range(1, ny):
            do(lax.rem(b + i, ny))

    @pl.when(keeper)
    def _():
        line(lambda bi: pl.semaphore_signal(barrier, inc=1, device_id=(s, a, bi), device_id_type=MESH))
        pl.semaphore_signal(barrier, inc=1, device_id=(1 - s, a, b), device_id_type=MESH)

    xv = x[...].reshape(mbs * sub, d).astype(jnp.float32)
    mv = mid[...]
    gain = small[experts + 1 : experts + 2]
    fgain = small[experts : experts + 1]
    dx2, fgain_g = norm_back(mv, rms(mv, features), fgain, dn2[...], features)
    dm = g[...].reshape(mbs * sub, d).astype(jnp.float32) + dx2
    msend[...] = bf(dm).reshape(mbs, sub, d)

    @pl.when(keeper)
    def _():
        pl.semaphore_wait(barrier, nx - 1 + ny - 1)

    @pl.when(helper)
    def _():
        pl.semaphore_wait(barrier, nx)

    def copy_m(ai, slot):
        return remote(msend, mall.at[:, slot], m_send.at[ai], m_recv.at[slot], (s, ai, b))

    pos.peers(lambda ai: copy_m(ai, a).start())

    crossing = ((sh_p, sh_x), (att_p, att_x), (small_p, small_x))
    totals = (sh_t, att_t, small_t)
    places = (sh_r, att_r, small_r)
    finals = (sh_f, att_f, small_f)
    results = (sh_o, att_o, small_o)

    def cross(i):
        return remote(crossing[i][0], crossing[i][1], c_send.at[i], c_recv.at[i], (layer, a, b))

    def block(i, bi):
        if i == 2:
            return small_t.at[:, pl.ds(pl.multiple_of(bi * pw, pw), pw)]
        return totals[i].at[bi]

    def spread(i, bi, slot):
        return remote(block(i, bi), places[i].at[slot], r_send.at[i, bi], r_recv.at[i, slot], (s, a, bi))

    def copy_a(ai, slot):
        return remote(small_f, small_a.at[slot], a_send.at[ai], a_recv.at[slot], (s, ai, b))

    def join(i):
        cross(i).wait_recv()
        part, other = crossing[i]
        totals[i][...] = (part[...].astype(jnp.float32) + other[...].astype(jnp.float32)).astype(totals[i].dtype)
        line(lambda bi: spread(i, bi, b).start())

    @pl.when(helper)
    def _():
        cross(0).start()

    mall[:, a] = msend[...]
    dsend[...] = jnp.zeros_like(dsend)
    pos.peers(lambda ai: copy_m(ai, ai).wait())
    dmr = mall[...].reshape(mbs * length, d)
    datt[...] = bf(by_blocks(dmr, watt, slice(3 * pw, 4 * pw), width, pw))
    for j in range(ny):
        att_p[j, :, 3 * pw :] = bf(mm(dmr[:, j * pw : j * pw + width], att[...], ((0,), (0,))))

    @pl.when(keeper)
    def _():
        join(0)

    for m in range(mbs):
        rs = slice(m * length, (m + 1) * length)
        dq = jnp.zeros((length, pw), jnp.float32)
        dk = dq
        dv = dq
        for h in range(heads):
            mask = head_mask(pw, h)
            qh = jnp.where(mask, q[rs], 0)
            kh = jnp.where(mask, k[rs], 0)
            da = jnp.where(mask, datt[rs], 0)
            p = probs_of(qh, k[rs])
            dp = mm(da, v[rs], ((1,), (1,)))
            ds = bf(p * (dp - jnp.sum(dp * p, axis=1, keepdims=True)))
            dv = dv + mm(bf(p), da, ((0,), (0,)))
            dq = dq + mm(ds, kh)
            dk = dk + mm(ds, qh, ((0,), (0,)))
        dqkv[rs, :pw] = turn(dq * scale, cos[...], sin[...], rot[...], -1.0)
        dqkv[rs, pw : 2 * pw] = turn(dk * scale, cos[...], sin[...], rot[...], -1.0)
        dqkv[rs, 2 * pw :] = bf(dv)
    for j in range(ny):
        part = mm(dqkv[...], watt[j, :, : 3 * pw], ((1,), (1,)))
        dsend[..., j * pw : j * pw + width] = bf(part).reshape(mbs, nx, sub, width)

    def copy_d(ai, slot):
        return remote(dsend.at[:, ai], drecv.at[slot], d_send.at[ai], d_recv.at[slot], (s, ai, b))

    pos.peers(lambda ai: copy_d(ai, a).start())
    drecv[a] = dsend[:, a]
    rv = rows[...].reshape(mbs * length, d)
    for j in range(ny):
        att_p[j, :, : 3 * pw] = bf(mm(rv[:, j * pw : j * pw + width], dqkv[...], ((0,), (0,))))

    @pl.when(helper)
    def _():
        cross(1).start()

    @pl.when(keeper)
    def _():
        join(1)

    pos.peers(lambda ai: copy_d(ai, ai).wait())
    dn1 = drecv[0].astype(jnp.float32)
    for ai in range(1, nx):
        dn1 = dn1 + drecv[ai].astype(jnp.float32)
    dn1 = dn1.reshape(mbs * sub, d)
    dx1, gain_g = norm_back(xv, rms(xv, features), gain, dn1, features)
    dx_o[...] = bf(dm + dx1).reshape(mbs, sub, d)
    small_p[: experts] = rw_p[...]
    row = lax.broadcasted_iota(jnp.int32, (8, d), 0)
    small_p[experts:] = jnp.where(row == 0, fgain_g, jnp.where(row == 1, gain_g, 0.0))

    @pl.when(helper)
    def _():
        cross(2).start()
        for i in range(3):
            cross(i).wait_send()

    @pl.when(keeper)
    def _():
        join(2)
        for i in (2, 0, 1):
            line(lambda bi: spread(i, bi, bi).wait())
            total = block(i, b)[...].astype(jnp.float32)
            for c in range(1, ny):
                total = total + places[i][lax.rem(b + c, ny)].astype(jnp.float32)
            finals[i][...] = total
            if i < 2:
                pltpu.make_async_copy(finals[i], results[i], f_sem.at[i]).start()
            else:
                pos.peers(lambda ai: copy_a(ai, a).start())
        small_a[a] = small_f[...]
        pos.peers(lambda ai: copy_a(ai, ai).wait())
        total = small_a[0]
        for ai in range(1, nx):
            total = total + small_a[ai]
        small_f[...] = total
        pltpu.make_async_copy(small_f, small_o, f_sem.at[2]).start()
        for i in range(3):
            pltpu.make_async_copy(finals[i], results[i], f_sem.at[i]).wait()


def attn_bwd(layer, dn2, g, mid, x, small, rows, q, k, v, att, watt, cos, sin, rot, sh_g, rw_g, grads, dims,
             heads, features, ids):
    width, pw, experts, cap = dims
    nx, ny = lax.axis_size("gx"), lax.axis_size("gy")
    d = ny * pw
    mbs, sub = x.shape[:2]
    length = nx * sub
    b16, f32 = jnp.bfloat16, jnp.float32
    vm = pl.BlockSpec(memory_space=pltpu.VMEM)
    hbm = pl.BlockSpec(memory_space=pl.ANY)
    ac, sc, n = watt.shape[2], sh_g.shape[2], small.shape[0]
    outs = pl.pallas_call(
        functools.partial(attn_bwd_kernel, (layer, nx, ny, mbs, sub, width, pw, heads, features, experts)),
        out_shape=(
            jax.ShapeDtypeStruct((mbs, sub, d), b16),
            jax.ShapeDtypeStruct((width, ac), f32),
            jax.ShapeDtypeStruct((width, sc), f32),
            jax.ShapeDtypeStruct((n, pw), f32),
        ),
        in_specs=[vm] * 16 + [hbm] * len(grads),
        out_specs=(vm,) + (hbm,) * 3,
        scratch_shapes=[
            pltpu.VMEM((mbs, sub, d), b16),
            pltpu.VMEM((mbs, nx, sub, d), b16),
            pltpu.VMEM((mbs * length, 3 * pw), b16),
            pltpu.VMEM((mbs, nx, sub, d), b16),
            pltpu.VMEM((nx, mbs, sub, d), b16),
            pltpu.VMEM((mbs * length, pw), b16),
            pltpu.VMEM((ny, width, ac), b16), pltpu.VMEM((n, d), f32),
            pltpu.VMEM((ny, width, sc), b16), pltpu.VMEM((ny, width, ac), b16), pltpu.VMEM((n, d), f32),
            pltpu.VMEM((ny, width, sc), b16), pltpu.VMEM((ny, width, ac), b16), pltpu.VMEM((n, d), f32),
            pltpu.VMEM((ny, width, sc), b16), pltpu.VMEM((ny, width, ac), b16), pltpu.VMEM((ny, n, pw), f32),
            pltpu.VMEM((width, sc), f32), pltpu.VMEM((width, ac), f32), pltpu.VMEM((n, pw), f32),
            pltpu.VMEM((nx, n, pw), f32),
            flags((nx,)), flags((nx,)), flags((nx,)), flags((nx,)), flags((3,)), flags((3,)),
            flags((3, ny)), flags((3, ny)), flags((nx,)), flags((nx,)), flags((3,)),
        ],
        input_output_aliases={16 + i: 1 + i for i in range(len(grads))},
        compiler_params=params(ids),
        cost_estimate=pl.CostEstimate(flops=2 * 10**9, bytes_accessed=2 * 10**7, transcendentals=10**6),
        name="attention_backward",
    )(dn2, g, mid, x, small, rows, q, k, v, att, watt, cos, sin, rot, sh_g, rw_g, *grads)
    return outs[0], outs[1:]


def ff_fwd_kernel(cfg, *refs):
    layer, nx, ny, mbs, sub, width, pw, experts, cap, f, sk, ak = cfg
    (mid, n2, rx, place, place_t, win_a, win_b, wdt_a, wdt_b, shw) = refs[:10]
    refs = refs[10:]
    if layer == 0:
        watt1, refs = refs[0], refs[1:]
    (out, slots_o, gu_o, hid_o, rows_o, sgu_o, shid_o), refs = refs[:7], refs[7:]
    if layer == 0:
        watt_o, refs = refs[0], refs[1:]
    (win, wdt, xsend, xall, nrows, pm, pt, slots, acc, gu, hid, eo, rsend, rrecv, ssend, srecv,
     w_sem, x_send, x_recv, n_send, n_recv, rs_send, rs_recv, ag_send, ag_recv,
     r_send, r_recv, s_send, s_recv, o_sem) = refs[:30]
    refs = refs[30:]
    pos = Position(nx, ny)
    s, a, b, me = pos.s, pos.a, pos.b, pos.me
    slots_n = experts * cap
    tokens = nx * ny * sub
    d = ny * pw
    barrier = greet_section(pos)
    if layer == 0:
        wfull, *w_sems = refs
        share = Share(pos, 1, watt1, wfull, w_sems)
        share.signal(barrier, False)

    for j, (dst, own, oth) in enumerate(((win, win_a, win_b), (wdt, wdt_a, wdt_b))):
        @pl.when(s == layer)
        def _():
            pltpu.make_async_copy(own, dst, w_sem.at[j]).start()

        @pl.when(s != layer)
        def _():
            pltpu.make_async_copy(oth, dst, w_sem.at[j]).start()

    lane = lax.broadcasted_iota(jnp.int32, (1, pw), 1)
    rv = rx[...]
    hi = bf(rv)
    lo = bf(rv - hi.astype(jnp.float32))
    tail = jnp.where(lane < width + experts, hi, lo)
    n2v = n2[...].reshape(mbs * sub, d)
    for j in range(ny):
        xsend[j] = jnp.where(lane < width, n2v[:, j * pw : (j + 1) * pw], tail).reshape(mbs, sub, pw)
    if layer == 0:
        share.wait_barrier(barrier, pos.n - 1, False)
    else:
        pl.semaphore_wait(barrier, pos.n - 1)

    def send_x(index, ai, bi):
        remote(xsend.at[bi], xall.at[:, b, a], x_send.at[index], x_recv.at[me], (s, ai, bi)).start()

    pos.others(send_x)

    def copy_n(ai, slot):
        return remote(n2, nrows.at[:, slot], n_send.at[ai], n_recv.at[slot], (s, ai, b))

    pos.peers(lambda ai: copy_n(ai, a).start())
    if layer == 0:
        share.start()
    xall[:, b, a] = xsend[b]
    nrows[:, a] = n2[...]

    for m in range(mbs):
        i0 = lax.broadcasted_iota(jnp.int32, (slots_n, tokens), 0)
        pm[m] = bf(((place[m, 0:1] == i0) | (place[m, 1:2] == i0)).astype(jnp.float32))
        i1 = lax.broadcasted_iota(jnp.int32, (tokens, slots_n), 1)
        pt[m] = bf(((place_t[m, :, 0:1] == i1) | (place_t[m, :, 1:2] == i1)).astype(jnp.float32))

    def wait_x(index, ai, bi):
        remote(xsend.at[0], xall.at[:, bi, ai], x_send.at[index], x_recv.at[index], (s, ai, bi)).wait()

    pos.others(wait_x)
    for m in range(mbs):
        slots[m] = bf(mm(pm[m], xall[m].reshape(tokens, pw))).reshape(experts, cap, pw)
    for j, (dst, own) in enumerate(((win, win_a), (wdt, wdt_a))):
        pltpu.make_async_copy(own, dst, w_sem.at[j]).wait()
    pltpu.make_async_copy(slots, slots_o, o_sem.at[0]).start()

    def gu_copy(m, e):
        to = b - 1 if m == 0 else b + 1
        return remote(gu.at[m, e], gu.at[m, e], rs_send.at[m, e], rs_recv.at[m, e], (s, a, to))

    def hid_copy(m, e):
        to = b + 1 if m == 0 else b - 1
        return remote(hid.at[m, e], hid.at[m, e], ag_send.at[m, e], ag_recv.at[m, e], (s, a, to))

    first = (b == ny - 1, b == 0)
    last = (b == 0, b == ny - 1)
    up = (ny - 1 - b, b)
    down = (b, ny - 1 - b)

    def shared_part(i):
        @pl.when(i == 2)
        def _():
            pos.peers(lambda ai: copy_n(ai, ai).wait())
            rows_o[...] = nrows[...]
            sgu_o[...] = bf(by_blocks(nrows[...].reshape(mbs * nx * sub, d), shw, slice(0, 2 * f), width, pw))

        @pl.when(i == 4)
        def _():
            gate = sgu_o[:, :f].astype(jnp.float32)
            shid_o[...] = bf(gate * jax.nn.sigmoid(gate) * sgu_o[:, f:].astype(jnp.float32))
            ssend[...] = jnp.zeros_like(ssend)

        @pl.when(i == 6)
        def _():
            for j in range(ny):
                part = mm(shid_o[...], shw[j, :, 2 * f :], ((1,), (1,)))
                ssend[..., j * pw : j * pw + width] = bf(part).reshape(mbs, nx, sub, width)
            pos.peers(lambda ai: copy_s(ai, a).start())
            srecv[a] = ssend[:, a]

        if layer == 0:
            @pl.when(i == 8)
            def _():
                share.forward()

    def copy_s(ai, slot):
        return remote(ssend.at[:, ai], srecv.at[slot], s_send.at[ai], s_recv.at[slot], (s, ai, b))

    def step(i, c):
        for m in range(mbs):
            e0 = i - sk * up[m]

            @pl.when((e0 >= 0) & (e0 < experts))
            def _():
                e = jnp.clip(e0, 0, experts - 1)
                acc[m] = mm(slots[m, e, :, :width], win[e])

                @pl.when(jnp.logical_not(first[m]))
                def _():
                    gu_copy(m, e).wait_recv()
                    acc[m] += gu[m, e].astype(jnp.float32)

                gu[m, e] = bf(acc[m])

                @pl.when(jnp.logical_not(last[m]))
                def _():
                    gu_copy(m, e).start()

                @pl.when(last[m])
                def _():
                    r = router_column(slots[m, e], e, width, experts)
                    gate = acc[m, :, :f]
                    hid[m, e] = bf(gate * jax.nn.sigmoid(gate) * acc[m, :, f:] * jax.nn.sigmoid(r))
                    hid_copy(m, e).start()

        for m in range(mbs):
            e1 = i - sk * (ny - 1) - ak * down[m]

            @pl.when((e1 >= 0) & (e1 < experts))
            def _():
                e = jnp.clip(e1, 0, experts - 1)

                @pl.when(jnp.logical_not(last[m]))
                def _():
                    hid_copy(m, e).wait_recv()

                    @pl.when(jnp.logical_not(first[m]))
                    def _():
                        hid_copy(m, e).start()

                eo[m, e] = bf(mm(hid[m, e], wdt[e], ((1,), (1,))))

        shared_part(i)
        return c

    lax.fori_loop(0, experts + (sk + ak) * (ny - 1), step, 0)

    for m in range(mbs):
        @pl.when(last[m])
        def _():
            pltpu.make_async_copy(gu.at[m], gu_o.at[m], o_sem.at[1]).start()

    pltpu.make_async_copy(hid, hid_o, o_sem.at[2]).start()
    for m in range(mbs):
        br = mm(pt[m], eo[m].reshape(slots_n, width))
        rsend[m, ..., :width] = bf(br).reshape(ny, nx, sub, width)

    def send_r(index, ai, bi):
        remote(rsend.at[:, bi, ai], rrecv.at[a, b], r_send.at[index], r_recv.at[me], (s, ai, bi)).start()

    pos.others(send_r)
    rrecv[a, b] = rsend[:, b, a]
    if layer == 0:
        share.finish()
        pltpu.make_async_copy(wfull, watt_o, o_sem.at[3]).start()
    pos.peers(lambda ai: copy_s(ai, ai).wait())

    def wait_r(index, ai, bi):
        remote(rsend.at[:, bi, ai], rrecv.at[ai, bi], r_send.at[index], r_recv.at[index], (s, ai, bi)).wait()

    pos.others(wait_r)
    total = mid[...]
    for ai in range(nx):
        total = total + srecv[ai].astype(jnp.float32)
    for j in range(ny):
        part = total[:, :, j * pw : (j + 1) * pw]
        for ai in range(nx):
            part = part + jnp.where(lane < width, rrecv[ai, j].astype(jnp.float32), 0.0)
        out[:, :, j * pw : (j + 1) * pw] = bf(part)

    def finish(e, c):
        for m in range(mbs):
            @pl.when(jnp.logical_not(last[m]))
            def _():
                gu_copy(m, e).wait_send()

            @pl.when(jnp.logical_not(first[m]))
            def _():
                hid_copy(m, e).wait_send()

        return c

    lax.fori_loop(0, experts, finish, 0)
    for m in range(mbs):
        @pl.when(last[m])
        def _():
            pltpu.make_async_copy(gu.at[m], gu_o.at[m], o_sem.at[1]).wait()

    pltpu.make_async_copy(hid, hid_o, o_sem.at[2]).wait()
    pltpu.make_async_copy(slots, slots_o, o_sem.at[0]).wait()
    if layer == 0:
        pltpu.make_async_copy(wfull, watt_o, o_sem.at[3]).wait()


def ff_fwd(layer, mid, n2, rx, place, win, wdt, shw, watt1, mbs, dims, ids):
    width, pw, experts, cap = dims
    nx, ny = lax.axis_size("gx"), lax.axis_size("gy")
    f = wdt[0].shape[-1]
    d = ny * pw
    sub = n2.shape[0] // mbs
    tokens = nx * ny * sub
    slots = experts * cap
    cfg = (layer, nx, ny, mbs, sub, width, pw, experts, cap, f, *FWD_SKEW)
    vm = pl.BlockSpec(memory_space=pltpu.VMEM)
    hbm = pl.BlockSpec(memory_space=pl.ANY)
    b16, f32 = jnp.bfloat16, jnp.float32
    n = nx * ny
    extra = [watt1] if layer == 0 else []
    wide = [jax.ShapeDtypeStruct((ny,) + v.shape, b16) for v in extra]
    outs = pl.pallas_call(
        functools.partial(ff_fwd_kernel, cfg),
        out_shape=(
            jax.ShapeDtypeStruct((mbs, sub, d), b16),
            jax.ShapeDtypeStruct((mbs, experts, cap, pw), b16),
            jax.ShapeDtypeStruct((mbs, experts, cap, 2 * f), b16),
            jax.ShapeDtypeStruct((mbs, experts, cap, f), b16),
            jax.ShapeDtypeStruct((mbs, nx, sub, d), b16),
            jax.ShapeDtypeStruct((mbs * nx * sub, 2 * f), b16),
            jax.ShapeDtypeStruct((mbs * nx * sub, f), b16),
            *wide,
        ),
        in_specs=[vm] * 5 + [hbm] * 4 + [vm] + [vm] * len(extra),
        out_specs=(vm, hbm, hbm, hbm, vm, vm, vm) + (hbm,) * len(extra),
        scratch_shapes=[
            pltpu.VMEM((experts, width, 2 * f), b16),
            pltpu.VMEM((experts, width, f), b16),
            pltpu.VMEM((ny, mbs, sub, pw), b16),
            pltpu.VMEM((mbs, ny, nx, sub, pw), b16),
            pltpu.VMEM((mbs, nx, sub, d), b16),
            pltpu.VMEM((mbs, slots, tokens), b16),
            pltpu.VMEM((mbs, tokens, slots), b16),
            pltpu.VMEM((mbs, experts, cap, pw), b16),
            pltpu.VMEM((mbs, cap, 2 * f), f32),
            pltpu.VMEM((mbs, experts, cap, 2 * f), b16),
            pltpu.VMEM((mbs, experts, cap, f), b16),
            pltpu.VMEM((mbs, experts, cap, width), b16),
            pltpu.VMEM((mbs, ny, nx, sub, pw), b16),
            pltpu.VMEM((nx, ny, mbs, sub, pw), b16),
            pltpu.VMEM((mbs, nx, sub, d), b16),
            pltpu.VMEM((nx, mbs, sub, d), b16),
            flags((2,)), flags((n,)), flags((n,)), flags((nx,)), flags((nx,)),
            flags((mbs, experts)), flags((mbs, experts)), flags((mbs, experts)), flags((mbs, experts)),
            flags((n,)), flags((n,)), flags((nx,)), flags((nx,)), flags((4,)),
        ] + ([pltpu.VMEM(wide[0].shape, b16)] + share_sems(ny) if extra else []),
        compiler_params=params(ids),
        cost_estimate=pl.CostEstimate(flops=4 * 10**9, bytes_accessed=30 * 10**6, transcendentals=10**6),
        name="experts_forward",
    )(
        mid.reshape(mbs, sub, d), n2.reshape(mbs, sub, d), rx, place, jnp.swapaxes(place, 1, 2),
        win[0], win[1], wdt[0], wdt[1], shw, *extra,
    )
    return outs[0], outs[1:7], outs[7] if extra else None


FWD_SKEW = (2, 2)


def ff_bwd_kernel(cfg, *refs):
    layer, nx, ny, mbs, sub, width, pw, experts, cap, f, sk, ak = cfg
    (g, n2, place, place_t, small, slots_i, gu_i, hid_i, rows2, sgu, shid,
     win_a, win_b, wdt_a, wdt_b, shw) = refs[:16]
    refs = refs[16 + (0 if layer else 2) :]
    (out, rw_g, sh_g, win_g, wdt_g,
     win, wdt, gsend, gall, grows, pm, pt, slots, gslots, gown, hid, acc, dh, dgu, deo,
     wxi, wxd, sti, std, dsgu, rsend, rrecv, ssend, srecv, rwx,
     w_sem, x_send, x_recv, n_send, n_recv, rs_send, rs_recv, ag_send, ag_recv,
     wi_send, wi_recv, wd_send, wd_recv, r_send, r_recv, s_send, s_recv, l_sem, st_sem) = refs
    pos = Position(nx, ny)
    s, a, b, me = pos.s, pos.a, pos.b, pos.me
    keeper = s == layer
    slots_n = experts * cap
    tokens = nx * ny * sub
    d = ny * pw
    first = (b == ny - 1, b == 0)
    last = (b == 0, b == ny - 1)
    barrier = greet_section(pos)

    @pl.when(keeper)
    def _():
        pl.semaphore_signal(barrier, inc=1, device_id=(1 - s, a, b), device_id_type=MESH)

    for j, (dst, own, oth) in enumerate(((win, win_a, win_b), (wdt, wdt_a, wdt_b))):
        @pl.when(keeper)
        def _():
            pltpu.make_async_copy(own, dst, w_sem.at[j]).start()

        @pl.when(jnp.logical_not(keeper))
        def _():
            pltpu.make_async_copy(oth, dst, w_sem.at[j]).start()

    pltpu.make_async_copy(slots_i, slots, l_sem.at[0]).start()
    pltpu.make_async_copy(hid_i, hid, l_sem.at[1]).start()
    for m in range(mbs):
        @pl.when(last[m])
        def _():
            pltpu.make_async_copy(gu_i.at[m], gown, l_sem.at[2]).start()

    lane = lax.broadcasted_iota(jnp.int32, (1, pw), 1)
    for j in range(ny):
        gsend[j] = g[:, :, j * pw : (j + 1) * pw]

    @pl.when(keeper)
    def _():
        pl.semaphore_wait(barrier, pos.n - 1)

    @pl.when(jnp.logical_not(keeper))
    def _():
        pl.semaphore_wait(barrier, pos.n)

    def send_x(index, ai, bi):
        remote(gsend.at[bi], gall.at[:, b, a], x_send.at[index], x_recv.at[me], (s, ai, bi)).start()

    pos.others(send_x)

    def copy_n(ai, slot):
        return remote(g, grows.at[:, slot], n_send.at[ai], n_recv.at[slot], (s, ai, b))

    pos.peers(lambda ai: copy_n(ai, a).start())
    gall[:, b, a] = gsend[b]
    grows[:, a] = g[...]
    deo[...] = jnp.zeros_like(deo)
    rwx[...] = jnp.zeros_like(rwx)
    rwx[width : width + experts] = bf(small[:experts])
    rwx[width + experts : width + 2 * experts] = bf(small[:experts])

    def wait_x(index, ai, bi):
        remote(gsend.at[0], gall.at[:, bi, ai], x_send.at[index], x_recv.at[index], (s, ai, bi)).wait()

    i0 = lax.broadcasted_iota(jnp.int32, (slots_n, tokens), 0)
    pm[...] = bf(((place[0, 0:1] == i0) | (place[0, 1:2] == i0)).astype(jnp.float32))
    pos.others(wait_x)
    for m in range(mbs):
        if m:
            pm[...] = bf(((place[m, 0:1] == i0) | (place[m, 1:2] == i0)).astype(jnp.float32))
        gslots[m] = bf(mm(pm[...], gall[m].reshape(tokens, pw))).reshape(experts, cap, pw)
    for j, (dst, own) in enumerate(((win, win_a), (wdt, wdt_a))):
        pltpu.make_async_copy(own, dst, w_sem.at[j]).wait()
    pltpu.make_async_copy(slots_i, slots, l_sem.at[0]).wait()
    pltpu.make_async_copy(hid_i, hid, l_sem.at[1]).wait()
    for m in range(mbs):
        @pl.when(last[m])
        def _():
            pltpu.make_async_copy(gu_i.at[m], gown, l_sem.at[2]).wait()

    def dh_copy(m, e):
        to = b - 1 if m == 0 else b + 1
        return remote(dh.at[m, e], dh.at[m, e], rs_send.at[m, e], rs_recv.at[m, e], (s, a, to))

    def dgu_copy(m, e):
        to = b + 1 if m == 0 else b - 1
        return remote(dgu.at[m, e], dgu.at[m, e], ag_send.at[m, e], ag_recv.at[m, e], (s, a, to))

    def wi_copy(e):
        return remote(wxi.at[e], wxi.at[e], wi_send.at[e], wi_recv.at[e], (layer, a, b))

    def wd_copy(e):
        return remote(wxd.at[e], wxd.at[e], wd_send.at[e], wd_recv.at[e], (layer, a, b))

    def st_copies(e, slot):
        return (pltpu.make_async_copy(sti.at[slot], win_g.at[e], st_sem.at[0, slot]),
                pltpu.make_async_copy(std.at[slot], wdt_g.at[e], st_sem.at[1, slot]))

    def weight_grads(e):
        gi = mm(slots[:, e, :, :width].reshape(mbs * cap, width), dgu[:, e].reshape(mbs * cap, 2 * f), ((0,), (0,)))
        gd = mm(gslots[:, e, :, :width].reshape(mbs * cap, width), hid[:, e].reshape(mbs * cap, f), ((0,), (0,)))
        return gi, gd

    up = (ny - 1 - b, b)
    down = (b, ny - 1 - b)
    full = (sk + ak) * (ny - 1)
    late = 2

    def copy_s(ai, slot):
        return remote(ssend.at[:, ai], srecv.at[slot], s_send.at[ai], s_recv.at[slot], (s, ai, b))

    def shared_part(i):
        @pl.when(i == 2)
        def _():
            pos.peers(lambda ai: copy_n(ai, ai).wait())
            ssend[...] = jnp.zeros_like(ssend)
            dsh = by_blocks(grows[...].reshape(mbs * nx * sub, d), shw, slice(2 * f, 3 * f), width, pw)
            dsg, dsu, _ = act_back(sgu[:, :f].astype(jnp.float32), sgu[:, f:].astype(jnp.float32), dsh, None)
            dsgu[:, :f] = bf(dsg)
            dsgu[:, f:] = bf(dsu)

        @pl.when(i == 4)
        def _():
            for j in range(ny):
                part = mm(dsgu[...], shw[j, :, : 2 * f], ((1,), (1,)))
                ssend[..., j * pw : j * pw + width] = bf(part).reshape(mbs, nx, sub, width)
            pos.peers(lambda ai: copy_s(ai, a).start())
            srecv[a] = ssend[:, a]

        @pl.when(i == 6)
        def _():
            for j in range(ny):
                rj = rows2[:, :, :, j * pw : j * pw + width].reshape(mbs * nx * sub, width)
                sh_g[j, :, : 2 * f] = bf(mm(rj, dsgu[...], ((0,), (0,))))

        @pl.when(i == 8)
        def _():
            for j in range(ny):
                gj = grows[:, :, :, j * pw : j * pw + width].reshape(mbs * nx * sub, width)
                sh_g[j, :, 2 * f :] = bf(mm(gj, shid[...], ((0,), (0,))))

    def step(i, c):
        for m in range(mbs):
            e0 = i - sk * up[m]

            @pl.when((e0 >= 0) & (e0 < experts))
            def _():
                e = jnp.clip(e0, 0, experts - 1)
                acc[m] = mm(gslots[m, e, :, :width], wdt[e])

                @pl.when(jnp.logical_not(first[m]))
                def _():
                    dh_copy(m, e).wait_recv()
                    acc[m] += dh[m, e].astype(jnp.float32)

                @pl.when(jnp.logical_not(last[m]))
                def _():
                    dh[m, e] = bf(acc[m])
                    dh_copy(m, e).start()

                @pl.when(last[m])
                def _():
                    r = router_column(slots[m, e], e, width, experts)
                    gate = gown[e, :, :f].astype(jnp.float32)
                    upv = gown[e, :, f:].astype(jnp.float32)
                    dgate, dup, dr = act_back(gate, upv, acc[m], jax.nn.sigmoid(r))
                    dgu[m, e, :, :f] = bf(dgate)
                    dgu[m, e, :, f:] = bf(dup)
                    dgu_copy(m, e).start()
                    hi = bf(dr).astype(jnp.float32)
                    deo[m, e] = bf(jnp.where(lane == width + e, hi, jnp.where(lane == width + experts + e, dr - hi, 0.0)))

        for m in range(mbs):
            e1 = i - sk * (ny - 1) - ak * down[m]

            @pl.when((e1 >= 0) & (e1 < experts))
            def _():
                e = jnp.clip(e1, 0, experts - 1)

                @pl.when(jnp.logical_not(last[m]))
                def _():
                    dgu_copy(m, e).wait_recv()

                    @pl.when(jnp.logical_not(first[m]))
                    def _():
                        dgu_copy(m, e).start()

                deo[m, e, :, :width] = bf(mm(dgu[m, e], win[e], ((1,), (1,))))

        e2 = i - full

        @pl.when((e2 >= 0) & (e2 < experts) & jnp.logical_not(keeper))
        def _():
            e = jnp.clip(e2, 0, experts - 1)
            gi, gd = weight_grads(e)
            wxi[e] = bf(gi)
            wi_copy(e).start()
            wxd[e] = bf(gd)
            wd_copy(e).start()

        e3 = i - full - late

        @pl.when((e3 >= 0) & (e3 < experts) & keeper)
        def _():
            e = jnp.clip(e3, 0, experts - 1)
            slot = lax.rem(e, 2)

            @pl.when(e >= 2)
            def _():
                for copy in st_copies(e - 2, slot):
                    copy.wait()

            gi, gd = weight_grads(e)
            wi_copy(e).wait_recv()
            sti[slot] = gi + wxi[e].astype(jnp.float32)
            wd_copy(e).wait_recv()
            std[slot] = gd + wxd[e].astype(jnp.float32)
            for copy in st_copies(e, slot):
                copy.start()

        shared_part(i)
        return c

    lax.fori_loop(0, experts + full + late, step, 0)

    for m in range(mbs):
        i1 = lax.broadcasted_iota(jnp.int32, (tokens, slots_n), 1)
        pt[...] = bf(((place_t[m, :, 0:1] == i1) | (place_t[m, :, 1:2] == i1)).astype(jnp.float32))
        br = mm(pt[...], deo[m].reshape(slots_n, pw))
        rsend[m] = bf(br).reshape(ny, nx, sub, pw)

    def send_r(index, ai, bi):
        remote(rsend.at[:, bi, ai], rrecv.at[a, b], r_send.at[index], r_recv.at[me], (s, ai, bi)).start()

    pos.others(send_r)
    rrecv[a, b] = rsend[:, b, a]

    pos.peers(lambda ai: copy_s(ai, ai).wait())

    def wait_r(index, ai, bi):
        remote(rsend.at[:, bi, ai], rrecv.at[ai, bi], r_send.at[index], r_recv.at[index], (s, ai, bi)).wait()

    pos.others(wait_r)
    dlog = jnp.zeros((mbs * sub, pw), jnp.float32)
    parts = []
    for j in range(ny):
        part = jnp.zeros((mbs, sub, pw), jnp.float32)
        for ai in range(nx):
            part = part + rrecv[ai, j].astype(jnp.float32)
        part = part.reshape(mbs * sub, pw)
        dlog = dlog + jnp.where(lane >= width, part, 0.0)
        parts.append(jnp.where(lane < width, part, 0.0))
    hi = bf(dlog)
    lo = bf(dlog - hi.astype(jnp.float32))
    total = mm(hi, rwx[...]) + mm(lo, rwx[...])
    for ai in range(nx):
        total = total + srecv[ai].astype(jnp.float32).reshape(mbs * sub, d)
    for j in range(ny):
        out[:, j * pw : (j + 1) * pw] = total[:, j * pw : (j + 1) * pw] + parts[j]
    n2v = n2[...].reshape(mbs * sub, d)
    rw_t = mm(hi, n2v, ((0,), (0,))) + mm(lo, n2v, ((0,), (0,)))
    rw_g[...] = rw_t[width : width + experts] + rw_t[width + experts : width + 2 * experts]

    def finish(e, c):
        for m in range(mbs):
            @pl.when(jnp.logical_not(last[m]))
            def _():
                dh_copy(m, e).wait_send()

            @pl.when(jnp.logical_not(first[m]))
            def _():
                dgu_copy(m, e).wait_send()

        @pl.when(jnp.logical_not(keeper))
        def _():
            wi_copy(e).wait_send()
            wd_copy(e).wait_send()

        return c

    lax.fori_loop(0, experts, finish, 0)

    @pl.when(keeper)
    def _():
        for e in (experts - 2, experts - 1):
            for copy in st_copies(e, e % 2):
                copy.wait()


def ff_bwd(layer, g, kept, n2, place, win, wdt, shw, small, grads, mbs, dims, ids):
    width, pw, experts, cap = dims
    slots_k, gu, hid, rows2, sgu, shid = kept
    nx, ny = lax.axis_size("gx"), lax.axis_size("gy")
    f = wdt[0].shape[-1]
    d = ny * pw
    sub = n2.shape[0] // mbs
    tokens = nx * ny * sub
    slots = experts * cap
    cfg = (layer, nx, ny, mbs, sub, width, pw, experts, cap, f, *BWD_SKEW)
    vm = pl.BlockSpec(memory_space=pltpu.VMEM)
    hbm = pl.BlockSpec(memory_space=pl.ANY)
    b16, f32 = jnp.bfloat16, jnp.float32
    n = nx * ny
    out, rw_g, sh_g, win_g, wdt_g = pl.pallas_call(
        functools.partial(ff_bwd_kernel, cfg),
        out_shape=(
            jax.ShapeDtypeStruct((mbs * sub, d), f32),
            jax.ShapeDtypeStruct((experts, d), f32),
            jax.ShapeDtypeStruct(shw.shape, b16),
            jax.ShapeDtypeStruct((experts, width, 2 * f), f32),
            jax.ShapeDtypeStruct((experts, width, f), f32),
        ),
        in_specs=[vm] * 5 + [hbm] * 3 + [vm] * 3 + [hbm] * 4 + [vm] + [hbm] * len(grads),
        out_specs=(vm, vm, vm, hbm, hbm),
        scratch_shapes=[
            pltpu.VMEM((experts, width, 2 * f), b16),
            pltpu.VMEM((experts, width, f), b16),
            pltpu.VMEM((ny, mbs, sub, pw), b16),
            pltpu.VMEM((mbs, ny, nx, sub, pw), b16),
            pltpu.VMEM((mbs, nx, sub, d), b16),
            pltpu.VMEM((slots, tokens), b16),
            pltpu.VMEM((tokens, slots), b16),
            pltpu.VMEM((mbs, experts, cap, pw), b16),
            pltpu.VMEM((mbs, experts, cap, pw), b16),
            pltpu.VMEM((experts, cap, 2 * f), b16),
            pltpu.VMEM((mbs, experts, cap, f), b16),
            pltpu.VMEM((mbs, cap, f), f32),
            pltpu.VMEM((mbs, experts, cap, f), b16),
            pltpu.VMEM((mbs, experts, cap, 2 * f), b16),
            pltpu.VMEM((mbs, experts, cap, pw), b16),
            pltpu.VMEM((experts, width, 2 * f), b16),
            pltpu.VMEM((experts, width, f), b16),
            pltpu.VMEM((2, width, 2 * f), f32),
            pltpu.VMEM((2, width, f), f32),
            pltpu.VMEM((mbs * nx * sub, 2 * f), b16),
            pltpu.VMEM((mbs, ny, nx, sub, pw), b16),
            pltpu.VMEM((nx, ny, mbs, sub, pw), b16),
            pltpu.VMEM((mbs, nx, sub, d), b16),
            pltpu.VMEM((nx, mbs, sub, d), b16),
            pltpu.VMEM((pw, d), b16),
            flags((2,)), flags((n,)), flags((n,)), flags((nx,)), flags((nx,)),
            flags((mbs, experts)), flags((mbs, experts)), flags((mbs, experts)), flags((mbs, experts)),
            flags((experts,)), flags((experts,)), flags((experts,)), flags((experts,)),
            flags((n,)), flags((n,)), flags((nx,)), flags((nx,)), flags((3,)), flags((2, 2)),
        ],
        input_output_aliases={16 + i: 3 + i for i in range(len(grads))},
        compiler_params=params(ids),
        cost_estimate=pl.CostEstimate(flops=8 * 10**9, bytes_accessed=60 * 10**6, transcendentals=10**6),
        name="experts_backward",
    )(
        g, n2.reshape(mbs, sub, d), place, jnp.swapaxes(place, 1, 2), small,
        slots_k, gu, hid, rows2, sgu, shid, win[0], win[1], wdt[0], wdt[1], shw, *grads,
    )
    return out, (win_g, wdt_g), sh_g, rw_g


BWD_SKEW = (2, 2)


def fast_device(block_input, output_grad, attention_gain, attention_in, attention_out, feed_gain,
                router_weight, expert_in, expert_down, shared_in, shared_down, routes):
    s = lax.axis_index("section")
    ny = lax.axis_size("gy")
    nx = lax.axis_size("gx")
    mbs = block_input.shape[0] // 2
    width = block_input.shape[2]
    features = width * ny
    experts = expert_in.shape[1]
    f = expert_in.shape[-1]
    pw = lanes_up(width + 2 * experts)
    tokens = routes.shape[2]
    cap = 5 * tokens // (2 * experts)
    length = tokens // ny
    heads = attention_in.shape[-1] // DH
    dims = (width, pw, experts, cap)

    att_block = jnp.concatenate([
        pad_to(attention_in[0], 2, pw).reshape(width, 3 * pw), pad_to(attention_out[0].T, 1, pw)], 1)
    sh_block = jnp.concatenate([shared_in[0].reshape(width, 2 * f), shared_down[0].T], 1)
    small = jnp.concatenate([
        router_weight[0].T.astype(jnp.float32), feed_gain, attention_gain, jnp.zeros((6, width), jnp.float32)], 0)
    tin = lax.dynamic_slice_in_dim(jnp.stack([block_input, output_grad]), s * mbs, mbs, 1)
    tok, watt0, small = entry(pad_to(tin, 3, pw), att_block, pad_to(small, 1, pw), 0)

    win = expert_in[0].reshape(experts, width, 2 * f)
    win = (win, pass_section(win))
    wdt = expert_down[0].transpose(0, 2, 1)
    wdt = (wdt, pass_section(wdt))
    other = pass_section(routes[0])
    pair = jnp.stack([jnp.where(s == 0, routes[0], other), jnp.where(s == 0, other, routes[0])])
    place = places_of(lax.dynamic_slice_in_dim(pair, s * mbs, mbs, 1), experts, cap)

    half = DH // 2
    freq = 10000.0 ** (-jnp.arange(half, dtype=jnp.float32) / half)
    ang = jnp.arange(length, dtype=jnp.float32)[:, None] * freq[None]
    lanes = jnp.tile(ang, (1, 2 * heads))
    cos = pad_to(jnp.cos(lanes), 1, pw)
    sin = pad_to(jnp.sin(lanes), 1, pw)
    rot = pad_to(pad_to(rot_columns(jnp.eye(heads * DH, dtype=jnp.float32)), 0, pw), 1, pw).astype(jnp.bfloat16)

    x, watt = tok[0], [watt0, None]
    kept, outs = [], []
    for l in range(2):
        mid, n2, rx, rows, q, k, v, att, shw = attn_fwd(
            l, x, small[l], watt[l], sh_block, cos, sin, rot, dims, heads, features, 1 + l)
        out, ff, wide = ff_fwd(l, mid, n2, rx, place[l], win, wdt, shw, att_block, mbs, dims, 3 + l)
        watt[1] = wide if l == 0 else watt[1]
        kept.append((x, mid, n2, rows, q, k, v, att, shw, ff))
        x = out
        outs.append(x)
    g = tok[1]
    gouts = [None, None]
    expert_grads = dense_grads = ()
    for l in (1, 0):
        x, mid, n2, rows, q, k, v, att, shw, ff = kept[l]
        dn2, expert_grads, sh_g, rw_g = ff_bwd(
            l, g, ff, n2, place[l], win, wdt, shw, small[l], expert_grads, mbs, dims, 5 + l)
        g, dense_grads = attn_bwd(
            l, dn2, g, mid, x, small[l], rows, q, k, v, att, watt[l], cos, sin, rot, sh_g, rw_g, dense_grads,
            dims, heads, features, 7 + l)
        gouts[l] = g

    both = leave(jnp.stack([outs[0], gouts[0]]), jnp.stack([outs[1], gouts[1]]), pw, 9)[..., :width]
    att_g, sh_g, small_g = dense_grads
    win_g, wdt_g = expert_grads
    hd = heads * DH
    return (
        both[0][None],
        both[1][None],
        small_g[experts + 1 : experts + 2, :width],
        att_g[:, : 3 * pw].reshape(width, 3, pw)[..., :hd][None],
        att_g[:, 3 * pw : 3 * pw + hd].T[None],
        small_g[experts : experts + 1, :width],
        small_g[:experts, :width].T[None],
        win_g.reshape(experts, width, 2, f)[None],
        wdt_g.transpose(0, 2, 1)[None],
        sh_g[:, : 2 * f].reshape(width, 2, f)[None],
        sh_g[:, 2 * f :].T[None],
    )


def solution(mesh):
    in_specs = (
        P(None, "gx", "gy"),
        P(None, "gx", "gy"),
        P("section", "gy"),
        P("section", "gy", None, "gx"),
        P("section", "gx", "gy"),
        P("section", "gy"),
        P("section", "gy", None),
        P("section", None, "gy", None, "gx"),
        P("section", None, "gx", "gy"),
        P("section", "gy", None, "gx"),
        P("section", "gx", "gy"),
        P("section", None, None, None),
    )
    out_specs = (
        P("section", None, "gx", "gy"),
        P("section", None, "gx", "gy"),
        P("section", "gy"),
        P("section", "gy", None, "gx"),
        P("section", "gx", "gy"),
        P("section", "gy"),
        P("section", "gy", None),
        P("section", None, "gy", None, "gx"),
        P("section", None, "gx", "gy"),
        P("section", "gy", None, "gx"),
        P("section", "gx", "gy"),
    )
    fast = mesh.shape["gx"] == mesh.shape["gy"]
    return jax.shard_map(
        fast_device if fast else on_device, mesh=mesh, in_specs=in_specs, out_specs=out_specs, check_vma=False
    )
```

```python
import functools

import jax
import jax.numpy as jnp
from jax import lax
from jax.experimental import pallas as pl
from jax.experimental.pallas import tpu as pltpu
from jax.sharding import PartitionSpec as P

DH = 64


epsilon = 1e-06
highest = lax.Precision.HIGHEST


def from_partner(array, axis, apart):
    return lax.ppermute(array, axis, [(i, i ^ 1 << apart) for i in range(lax.axis_size(axis))])


def token_rows(values):
    return lax.all_gather(values, "gx", axis=0, tiled=True)


def output_rows(values):
    return lax.psum_scatter(values, "gx", scatter_dimension=0, tiled=True)


def width_sum(values):
    return lax.psum(values, "gy")


def pass_section(values):
    return from_partner(values, "section", 0)


def sequence_sums(values):
    return lax.psum_scatter(values, "gy", scatter_dimension=0, tiled=True)


def sequence_rows(values):
    return lax.all_gather(values, "gy", axis=0, tiled=True)


def gather_hidden(hidden, shared_hidden):
    return (
        lax.all_gather(hidden, "gy", axis=0, tiled=True),
        lax.all_gather(shared_hidden, "gy", axis=0, tiled=True),
    )


def rope_turn(values, positions, turn_sign):
    half_size = values.shape[-1] // 2
    frequency = 10000.0 ** (-jnp.arange(half_size, dtype=jnp.float32) / half_size)
    angles = positions[:, None] * frequency[None, :]
    cosine = jnp.cos(angles)[:, None, :]
    sine_part = turn_sign * jnp.sin(angles)[:, None, :]
    first_half = values[..., :half_size]
    second_half = values[..., half_size:]
    return jnp.concatenate(
        [
            first_half * cosine - second_half * sine_part,
            first_half * sine_part + second_half * cosine,
        ],
        axis=-1,
    )


def norm_forward(stream, gain):
    full_width = stream.shape[1] * lax.axis_size("gy")
    square_sum = width_sum(jnp.sum(stream * stream, axis=1))
    inverse_rms = lax.rsqrt(square_sum / full_width + epsilon)
    return ((stream * inverse_rms[:, None] * gain[None, :]).astype(jnp.bfloat16), inverse_rms)


def norm_backward(stream, inverse_rms, gain, grad_normed):
    full_width = stream.shape[1] * lax.axis_size("gy")
    scaled = grad_normed * gain[None, :]
    inner_sum = width_sum(jnp.sum(scaled * stream, axis=1))
    cubed = inverse_rms * inverse_rms * inverse_rms
    grad_stream = inverse_rms[:, None] * scaled - stream * (cubed * inner_sum / full_width)[:, None]
    grad_gain = jnp.sum(grad_normed * stream * inverse_rms[:, None], axis=0)
    return (grad_stream, grad_gain)


def slot_table(route_ids, experts, capacity):
    flat_ids = route_ids.reshape(-1)
    assigned = (flat_ids[:, None] == jnp.arange(experts, dtype=jnp.int32)[None, :]).astype(
        jnp.int32
    )
    earlier = jnp.cumsum(assigned, axis=0) - assigned
    places = flat_ids * capacity + jnp.sum(earlier * assigned, axis=1)
    owners = jnp.arange(flat_ids.shape[0], dtype=jnp.int32) // 2
    slot_token = jnp.zeros((experts * capacity,), jnp.int32).at[places].set(owners)
    slot_valid = jnp.zeros((experts * capacity,), jnp.int32).at[places].set(jnp.ones_like(owners))
    return (places.reshape(-1, 2), slot_token, slot_valid)


def expert_act(gate_up, logits):
    half_size = gate_up.shape[1] // 2
    return (
        jax.nn.silu(gate_up[:, :half_size])
        * gate_up[:, half_size:]
        * jax.nn.sigmoid(logits)[:, None]
    )


def shared_act(gate_up):
    half_size = gate_up.shape[1] // 2
    return jax.nn.silu(gate_up[:, :half_size]) * gate_up[:, half_size:]


def causal_scores(queries, keys_part):
    score_scale = queries.shape[-1] ** (-0.5)
    scores = (
        jnp.einsum("qhd,khd->hqk", queries, keys_part, preferred_element_type=jnp.float32)
        * score_scale
    )
    length = queries.shape[0]
    causal = jnp.arange(length)[:, None] >= jnp.arange(length)[None, :]
    return jnp.where(causal[None], scores, -1e30)


def attend_forward(queries, keys_part, values_part):
    scores = causal_scores(queries, keys_part)
    row_max = jnp.max(scores, axis=-1, keepdims=True)
    exponent = jnp.exp(scores - row_max)
    row_total = jnp.sum(exponent, axis=-1, keepdims=True)
    probabilities = (exponent / row_total).astype(jnp.bfloat16)
    attended = jnp.einsum(
        "hqk,khd->qhd", probabilities, values_part, preferred_element_type=jnp.float32
    )
    return (attended, row_max + jnp.log(row_total))


def attend_backward(queries, keys_part, values_part, log_total, grad_attended):
    score_scale = queries.shape[-1] ** (-0.5)
    probabilities = jnp.exp(causal_scores(queries, keys_part) - log_total)
    grad_values = jnp.einsum(
        "hqk,qhd->khd",
        probabilities.astype(jnp.bfloat16),
        grad_attended,
        preferred_element_type=jnp.float32,
    )
    grad_probs = jnp.einsum(
        "qhd,khd->hqk", grad_attended, values_part, preferred_element_type=jnp.float32
    )
    grad_scores = (
        probabilities * (grad_probs - jnp.sum(grad_probs * probabilities, axis=-1, keepdims=True))
    ).astype(jnp.bfloat16)
    grad_queries = (
        jnp.einsum("hqk,khd->qhd", grad_scores, keys_part, preferred_element_type=jnp.float32)
        * score_scale
    )
    grad_keys = (
        jnp.einsum("hqk,qhd->khd", grad_scores, queries, preferred_element_type=jnp.float32)
        * score_scale
    )
    return (grad_queries, grad_keys, grad_values)


def layer_forward(stream, weights, route_ids):
    (
        attention_gain,
        attention_in,
        attention_out,
        feed_gain,
        router_weight,
        expert_in,
        expert_down,
        shared_in,
        shared_down,
    ) = weights
    local_width = stream.shape[1]
    experts = expert_in.shape[0]
    normed, inverse_first = norm_forward(stream, attention_gain)
    rows_first = token_rows(normed)
    tokens = rows_first.shape[0]
    capacity = 5 * tokens // (2 * experts)
    slot_count = experts * capacity
    projected = sequence_sums(
        jnp.dot(
            rows_first, attention_in.reshape(local_width, -1), preferred_element_type=jnp.float32
        )
    )
    length = projected.shape[0]
    projected = projected.reshape(length, 3, -1, DH)
    positions = jnp.arange(length, dtype=jnp.float32)
    queries = rope_turn(projected[:, 0], positions, 1.0).astype(jnp.bfloat16)
    keys_part = rope_turn(projected[:, 1], positions, 1.0).astype(jnp.bfloat16)
    values_part = projected[:, 2].astype(jnp.bfloat16)
    attended, log_total = attend_forward(queries, keys_part, values_part)
    attended_rows = sequence_rows(attended.astype(jnp.bfloat16).reshape(length, -1))
    middle = stream + output_rows(
        jnp.dot(attended_rows, attention_out, preferred_element_type=jnp.float32)
    )
    normed_feed, inverse_second = norm_forward(middle, feed_gain)
    rows_second = token_rows(normed_feed)
    route_slot, slot_token, slot_valid = slot_table(route_ids, experts, capacity)
    grouped = (rows_second[slot_token] * slot_valid[:, None].astype(jnp.bfloat16)).reshape(
        experts, capacity, local_width
    )
    expert_part = jnp.einsum(
        "ecd,edf->ecf",
        grouped,
        expert_in.reshape(experts, local_width, -1),
        preferred_element_type=jnp.float32,
    )
    router_part = jnp.einsum(
        "ecd,de->ec", grouped, router_weight, preferred_element_type=jnp.float32
    )
    shared_part = jnp.dot(
        rows_second, shared_in.reshape(local_width, -1), preferred_element_type=jnp.float32
    )
    expert_gu, router_logit, shared_gu = (
        lax.psum_scatter(
            expert_part.reshape(slot_count, -1), "gy", scatter_dimension=0, tiled=True
        ),
        lax.psum_scatter(router_part.reshape(slot_count), "gy", scatter_dimension=0, tiled=True),
        lax.psum_scatter(shared_part, "gy", scatter_dimension=0, tiled=True),
    )
    hidden_rows, shared_rows = gather_hidden(
        expert_act(expert_gu, router_logit).astype(jnp.bfloat16),
        shared_act(shared_gu).astype(jnp.bfloat16),
    )
    expert_result = jnp.einsum(
        "ecf,efd->ecd",
        hidden_rows.reshape(experts, capacity, -1),
        expert_down,
        preferred_element_type=jnp.float32,
    ).reshape(slot_count, local_width)
    branch = (
        expert_result[route_slot[:, 0]]
        + expert_result[route_slot[:, 1]]
        + jnp.dot(shared_rows, shared_down, preferred_element_type=jnp.float32)
    )
    result = middle + output_rows(branch)
    kept_items = (
        stream,
        inverse_first,
        rows_first,
        queries,
        keys_part,
        values_part,
        log_total,
        attended_rows,
        middle,
        inverse_second,
        rows_second,
        expert_gu,
        router_logit,
        shared_gu,
    )
    return (result, kept_items)


def layer_backward(grad_out, kept_items, weights, route_ids):
    (
        attention_gain,
        attention_in,
        attention_out,
        feed_gain,
        router_weight,
        expert_in,
        expert_down,
        shared_in,
        shared_down,
    ) = weights
    (
        stream,
        inverse_first,
        rows_first,
        queries,
        keys_part,
        values_part,
        log_total,
        attended_rows,
        middle,
        inverse_second,
        rows_second,
        expert_gu,
        router_logit,
        shared_gu,
    ) = kept_items[:14]
    local_width = stream.shape[1]
    experts = expert_in.shape[0]
    tokens = rows_second.shape[0]
    capacity = 5 * tokens // (2 * experts)
    slot_count = experts * capacity
    hidden_rows, shared_rows = gather_hidden(
        expert_act(expert_gu, router_logit).astype(jnp.bfloat16),
        shared_act(shared_gu).astype(jnp.bfloat16),
    )
    route_slot, slot_token, slot_valid = slot_table(route_ids, experts, capacity)
    valid_rows = slot_valid[:, None].astype(jnp.bfloat16)
    grouped = (rows_second[slot_token] * valid_rows).reshape(experts, capacity, local_width)
    grad_rows = token_rows(grad_out.astype(jnp.bfloat16))
    slot_grad = (grad_rows[slot_token] * valid_rows).reshape(experts, capacity, local_width)
    down_grad = jnp.einsum(
        "ecf,ecd->efd",
        hidden_rows.reshape(experts, capacity, -1),
        slot_grad,
        preferred_element_type=jnp.float32,
    )
    shared_down_grad = jnp.einsum(
        "tf,td->fd", shared_rows, grad_rows, preferred_element_type=jnp.float32
    )
    hidden_part = jnp.einsum(
        "ecd,efd->ecf", slot_grad, expert_down, preferred_element_type=jnp.float32
    ).reshape(slot_count, -1)
    shared_part = jnp.einsum(
        "td,fd->tf", grad_rows, shared_down, preferred_element_type=jnp.float32
    )
    grad_hidden, grad_shared = (
        lax.psum_scatter(
            hidden_part.astype(jnp.bfloat16), "gy", scatter_dimension=0, tiled=True
        ).astype(jnp.float32),
        lax.psum_scatter(
            shared_part.astype(jnp.bfloat16), "gy", scatter_dimension=0, tiled=True
        ).astype(jnp.float32),
    )
    unused_expert, expert_back = jax.vjp(expert_act, expert_gu, router_logit)
    grad_gu, grad_logit = expert_back(grad_hidden)
    unused_shared, shared_back = jax.vjp(shared_act, shared_gu)
    (grad_shared_gu,) = shared_back(grad_shared)
    gu_rows, shared_gu_rows = (
        lax.all_gather(grad_gu.astype(jnp.bfloat16), "gy", axis=0, tiled=True),
        lax.all_gather(grad_shared_gu.astype(jnp.bfloat16), "gy", axis=0, tiled=True),
    )
    logit_rows = lax.all_gather(grad_logit, "gy", axis=0, tiled=True).reshape(experts, capacity)
    gu_grouped = gu_rows.reshape(experts, capacity, -1)
    in_grad = jnp.einsum("ecd,ecf->edf", grouped, gu_grouped, preferred_element_type=jnp.float32)
    router_grad = jnp.einsum(
        "ecd,ec->de", grouped.astype(jnp.float32), logit_rows, precision=highest
    )
    shared_in_grad = jnp.einsum(
        "td,tf->df", rows_second, shared_gu_rows, preferred_element_type=jnp.float32
    )
    slot_back = jnp.einsum(
        "ecf,edf->ecd",
        gu_grouped,
        expert_in.reshape(experts, local_width, -1),
        preferred_element_type=jnp.float32,
    )
    slot_back = slot_back + logit_rows[:, :, None] * router_weight.T.astype(jnp.float32)[:, None, :]
    slot_back = slot_back.reshape(slot_count, local_width)
    rows_back = (
        slot_back[route_slot[:, 0]]
        + slot_back[route_slot[:, 1]]
        + jnp.einsum(
            "tf,df->td",
            shared_gu_rows,
            shared_in.reshape(local_width, -1),
            preferred_element_type=jnp.float32,
        )
    )
    grad_middle_norm, feed_gain_grad = norm_backward(
        middle, inverse_second, feed_gain, output_rows(rows_back)
    )
    grad_middle = grad_out + grad_middle_norm
    middle_rows = token_rows(grad_middle.astype(jnp.bfloat16))
    out_weight_grad = jnp.einsum(
        "tf,td->fd", attended_rows, middle_rows, preferred_element_type=jnp.float32
    )
    grad_attended = sequence_sums(
        jnp.einsum("td,fd->tf", middle_rows, attention_out, preferred_element_type=jnp.float32)
    )
    length = grad_attended.shape[0]
    positions = jnp.arange(length, dtype=jnp.float32)
    grad_queries, grad_keys, grad_values = attend_backward(
        queries,
        keys_part,
        values_part,
        log_total,
        grad_attended.astype(jnp.bfloat16).reshape(queries.shape),
    )
    grad_projected = jnp.stack(
        [
            rope_turn(grad_queries, positions, -1.0),
            rope_turn(grad_keys, positions, -1.0),
            grad_values,
        ],
        axis=1,
    )
    grad_projected = grad_projected.astype(jnp.bfloat16).reshape(length, -1)
    projected_rows = sequence_rows(grad_projected)
    in_weight_grad = jnp.einsum(
        "td,tf->df", rows_first, projected_rows, preferred_element_type=jnp.float32
    )
    grad_normed = output_rows(
        jnp.einsum(
            "tf,df->td",
            projected_rows,
            attention_in.reshape(local_width, -1),
            preferred_element_type=jnp.float32,
        )
    )
    grad_stream_norm, attention_gain_grad = norm_backward(
        stream, inverse_first, attention_gain, grad_normed
    )
    layer_grads = (
        attention_gain_grad,
        in_weight_grad.reshape(attention_in.shape),
        out_weight_grad,
        feed_gain_grad,
        router_grad,
        in_grad.reshape(expert_in.shape),
        down_grad,
        shared_in_grad.reshape(shared_in.shape),
        shared_down_grad,
    )
    return (grad_middle + grad_stream_norm, layer_grads)


def put_item(buffer, value, batch_index, is_valid):
    current = lax.dynamic_index_in_dim(buffer, batch_index, 0, keepdims=False)
    return lax.dynamic_update_index_in_dim(
        buffer, jnp.where(is_valid, value, current), batch_index, 0
    )


def on_device(
    block_input,
    output_grad,
    attention_gain,
    attention_in,
    attention_out,
    feed_gain,
    router_weight,
    expert_in,
    expert_down,
    shared_in,
    shared_down,
    routes,
):
    section_index = lax.axis_index("section")
    batches = block_input.shape[0]
    weights = tuple(
        (
            member[0]
            for member in (
                attention_gain,
                attention_in,
                attention_out,
                feed_gain,
                router_weight,
                expert_in,
                expert_down,
                shared_in,
                shared_down,
            )
        )
    )
    route_table = routes[0]
    outputs = jnp.zeros(block_input.shape, jnp.bfloat16)
    received = jnp.zeros(block_input.shape[1:], jnp.bfloat16)
    stored = None
    for tick_step in range(batches + 1):
        micro_index = tick_step - section_index
        is_valid = (micro_index >= 0) & (micro_index < batches)
        batch_index = jnp.clip(micro_index, 0, batches - 1)
        fresh_input = lax.dynamic_index_in_dim(block_input, batch_index, 0, keepdims=False)
        incoming = jnp.where(section_index == 0, fresh_input, received).astype(jnp.float32)
        route_ids = lax.dynamic_index_in_dim(route_table, batch_index, 0, keepdims=False)
        result, kept_items = layer_forward(incoming, weights, route_ids)
        result_low = result.astype(jnp.bfloat16)
        outputs = put_item(outputs, result_low, batch_index, is_valid)
        if stored is None:
            stored = tuple(
                (jnp.zeros((batches,) + member.shape, member.dtype) for member in kept_items)
            )
        stored = tuple(
            (
                put_item(buffer, member, batch_index, is_valid)
                for buffer, member in zip(stored, kept_items)
            )
        )
        if tick_step < batches:
            received = pass_section(result_low)
    grads_in = jnp.zeros(block_input.shape, jnp.bfloat16)
    received = jnp.zeros(block_input.shape[1:], jnp.bfloat16)
    totals = tuple((jnp.zeros(member.shape, jnp.float32) for member in weights))
    for tick_step in range(batches + 1):
        micro_index = batches - tick_step - section_index
        is_valid = (micro_index >= 0) & (micro_index < batches)
        batch_index = jnp.clip(micro_index, 0, batches - 1)
        given_grad = lax.dynamic_index_in_dim(output_grad, batch_index, 0, keepdims=False)
        incoming = jnp.where(section_index == 1, given_grad, received).astype(jnp.float32)
        kept_items = tuple(
            (lax.dynamic_index_in_dim(buffer, batch_index, 0, keepdims=False) for buffer in stored)
        )
        route_ids = lax.dynamic_index_in_dim(route_table, batch_index, 0, keepdims=False)
        grad_input, layer_grads = layer_backward(incoming, kept_items, weights, route_ids)
        grad_low = grad_input.astype(jnp.bfloat16)
        grads_in = put_item(grads_in, grad_low, batch_index, is_valid)
        totals = tuple(
            (total + jnp.where(is_valid, member, 0.0) for total, member in zip(totals, layer_grads))
        )
        if tick_step < batches:
            received = pass_section(grad_low)
    gain_first, gain_second, router_total = lax.psum((totals[0], totals[3], totals[4]), "gx")
    return (
        outputs[None],
        grads_in[None],
        gain_first[None],
        totals[1][None],
        totals[2][None],
        gain_second[None],
        router_total[None],
        totals[5][None],
        totals[6][None],
        totals[7][None],
        totals[8][None],
    )


def lanes_up(n):
    return -(-n // 128) * 128


def rot_columns(w):
    shape = w.shape
    w = w.reshape(shape[:-1] + (-1, 2, DH // 2))
    w = jnp.stack([-w[..., 1, :], w[..., 0, :]], axis=-2)
    return w.reshape(shape)


def pad_to(v, axis, n):
    pads = [(0, 0)] * v.ndim
    pads[axis] = (0, n - v.shape[axis])
    return jnp.pad(v, pads)


def mm(a, b, dims=((1,), (0,))):
    return lax.dot_general(a, b, (dims, ((), ())), preferred_element_type=jnp.float32)


def bf(v):
    return v.astype(jnp.bfloat16)


def head_mask(pw, h):
    lane = lax.broadcasted_iota(jnp.int32, (1, pw), 1)
    return (lane >= h * DH) & (lane < (h + 1) * DH)


def rms(x, features):
    return lax.rsqrt(jnp.sum(x * x, axis=1, keepdims=True) / features + epsilon)


def norm_back(x, inv, gain, d, features):
    u = d * gain
    inner = jnp.sum(u * x, axis=1, keepdims=True) / features
    dx = inv * u - x * (inv * inv * inv * inner)
    return dx, jnp.sum(d * x * inv, axis=0, keepdims=True)


def probs_of(q, k):
    s = mm(q, k, ((1,), (1,))) * DH ** -0.5
    n = s.shape[0]
    causal = lax.broadcasted_iota(jnp.int32, (n, n), 0) >= lax.broadcasted_iota(jnp.int32, (n, n), 1)
    s = jnp.where(causal, s, -1e30)
    e = jnp.exp(s - jnp.max(s, axis=1, keepdims=True))
    return e / jnp.sum(e, axis=1, keepdims=True)


def act_back(gate, up, dh, s):
    sg = jax.nn.sigmoid(gate)
    silu = gate * sg
    if s is None:
        return dh * up * (sg * (1.0 + gate * (1.0 - sg))), dh * silu, None
    dr = jnp.sum(dh * silu * up, axis=-1, keepdims=True) * s * (1.0 - s)
    ds = dh * s
    return ds * up * (sg * (1.0 + gate * (1.0 - sg))), ds * silu, dr


MESH = pl.DeviceIdType.MESH
VMEM_BYTES = 62 * 2**20


def remote(src, dst, send, recv, target):
    return pltpu.make_async_remote_copy(
        src_ref=src, dst_ref=dst, send_sem=send, recv_sem=recv, device_id=target, device_id_type=MESH
    )


def router_column(rows, e, width, experts):
    lane = lax.broadcasted_iota(jnp.int32, rows.shape, rows.ndim - 1)
    mask = (lane == width + e) | (lane == width + experts + e)
    return jnp.sum(jnp.where(mask, rows.astype(jnp.float32), 0.0), axis=-1, keepdims=True)


class Position:
    def __init__(self, nx, ny):
        self.s = lax.axis_index("section")
        self.a = lax.axis_index("gx")
        self.b = lax.axis_index("gy")
        self.nx, self.ny = nx, ny
        self.n = nx * ny
        self.me = self.a * ny + self.b

    def device(self, index):
        return (self.s, index // self.ny, lax.rem(index, self.ny))

    def others(self, do):
        def step(i, c):
            index = lax.rem(self.me + i, self.n)
            do(index, index // self.ny, lax.rem(index, self.ny))
            return c

        lax.fori_loop(1, self.n, step, 0)

    def peers(self, do):
        for i in range(1, self.nx):
            do(lax.rem(self.a + i, self.nx))

    def line(self, do):
        for i in range(1, self.ny):
            do(lax.rem(self.b + i, self.ny))


def greet_section(pos):
    barrier = pltpu.get_barrier_semaphore()

    def one(index, ai, bi):
        pl.semaphore_signal(barrier, inc=1, device_id=(pos.s, ai, bi), device_id_type=MESH)

    pos.others(one)
    return barrier


def flags(count):
    return pltpu.SemaphoreType.DMA(count)


class Share:
    def __init__(self, pos, layer, block, full, sems):
        self.pos, self.layer, self.block, self.full = pos, layer, block, full
        self.sems = sems
        self.source = pos.s == layer

    def along(self, way, h):
        pos = self.pos
        j = pos.b - way * h
        to = pos.b + way
        real = (j >= 0) & (j < pos.ny) & (to >= 0) & (to < pos.ny)
        j = jnp.clip(j, 0, pos.ny - 1)
        src = self.block if h == 0 else self.full.at[j]
        copy = remote(src, self.full.at[j], self.sems[0].at[(way + 1) // 2, h], self.sems[1].at[j], (pos.s, pos.a, to))
        return real, j, copy

    def across(self, src, slot):
        pos = self.pos
        return remote(src, self.full.at[slot], self.sems[2].at[slot], self.sems[3].at[slot], (1 - pos.s, pos.a, pos.b))

    def start(self):
        b = self.pos.b

        @pl.when(self.source)
        def _():
            self.full[b] = self.block[...]
            for way in (-1, 1):
                real, _, copy = self.along(way, 0)
                pl.when(real)(copy.start)
            self.across(self.block, b).start()

    def hop(self, h):
        pos = self.pos

        @pl.when(self.source)
        def _():
            for way in (-1, 1):
                j = pos.b - way * h

                @pl.when((j >= 0) & (j < pos.ny))
                def _():
                    real, jc, copy = self.along(way, h)
                    copy.wait_recv()
                    pl.when(real)(copy.start)
                    self.across(self.full.at[jc], jc).start()

    def finish(self):
        pos = self.pos

        @pl.when(self.source)
        def _():
            for h in range(pos.ny - 1):
                for way in (-1, 1):
                    real, _, copy = self.along(way, h)
                    pl.when(real)(copy.wait_send)
            for j in range(pos.ny):
                self.across(self.block, j).wait_send()

        @pl.when(jnp.logical_not(self.source))
        def _():
            for j in range(pos.ny):
                self.across(self.full.at[j], j).wait_recv()


def share_sems(ny):
    return [flags((2, ny)), flags((ny,)), flags((ny,)), flags((ny,))]


def params(ids):
    return pltpu.CompilerParams(collective_id=ids, has_side_effects=True, vmem_limit_bytes=VMEM_BYTES)


def greet_all(pos):
    barrier = pltpu.get_barrier_semaphore()
    total = 2 * pos.n
    mine = pos.s * pos.n + pos.me

    def one(i, c):
        index = lax.rem(mine + i, total)
        rest = lax.rem(index, pos.n)
        pl.semaphore_signal(
            barrier, inc=1, device_id=(index // pos.n, rest // pos.ny, lax.rem(rest, pos.ny)), device_id_type=MESH)
        return c

    lax.fori_loop(1, total, one, 0)
    pl.semaphore_wait(barrier, total - 1)


def leave_kernel(cfg, pair0, pair1, out, buf, t_send, t_recv):
    nx, ny, mbs, sub, pw = cfg
    pos = Position(nx, ny)
    s, a, b = pos.s, pos.a, pos.b
    greet_all(pos)
    pairs = (pair0, pair1)

    def copy(l, j, s_slot, a_slot, seq):
        src = pairs[l].at[:, :, :, pl.ds(pl.multiple_of(j * pw, pw), pw)]
        return remote(src, buf.at[s_slot, a_slot], t_send.at[l, j], t_recv.at[s_slot, a_slot], (l, seq, j))

    for l in range(2):
        for j in range(ny):
            @pl.when((l != s) | (a != b) | (j != b))
            def _():
                copy(l, j, s, a, b).start()

        @pl.when((l == s) & (a == b))
        def _():
            buf[s, a] = pairs[l][:, :, :, pl.ds(pl.multiple_of(b * pw, pw), pw)]

    for so in range(2):
        for i in range(nx):
            @pl.when((so != s) | (a != b) | (i != a))
            def _():
                copy(0, 0, so, i, i).wait_recv()

            out[:, so * mbs : (so + 1) * mbs, i * sub : (i + 1) * sub, :] = buf[so, i]
    for l in range(2):
        for j in range(ny):
            @pl.when((l != s) | (a != b) | (j != b))
            def _():
                copy(l, j, s, a, b).wait_send()


def leave(pair0, pair1, pw, ids):
    nx, ny = lax.axis_size("gx"), lax.axis_size("gy")
    kinds, mbs, sub, d = pair0.shape
    vm = pl.BlockSpec(memory_space=pltpu.VMEM)
    return pl.pallas_call(
        functools.partial(leave_kernel, (nx, ny, mbs, sub, pw)),
        out_shape=jax.ShapeDtypeStruct((kinds, 2 * mbs, nx * sub, pw), jnp.bfloat16),
        in_specs=[vm] * 2,
        out_specs=vm,
        scratch_shapes=[
            pltpu.VMEM((2, nx, kinds, mbs, sub, pw), jnp.bfloat16),
            flags((2, ny)), flags((2, nx)),
        ],
        compiler_params=params(ids),
        name="leave",
    )(pair0, pair1)


def turn(t, cos, sin, rot, sign):
    hi = bf(t)
    lo = bf(t - hi.astype(jnp.float32))
    return bf(t * cos + sign * ((mm(hi, rot) + mm(lo, rot)) * sin))


def by_blocks(rows, full, cols, width, pw):
    total = None
    for j in range(full.shape[0]):
        part = mm(rows[:, j * pw : j * pw + width], full[j, :, cols])
        total = part if total is None else total + part
    return total


def forward_kernel(cfg, *refs):
    nx, ny, mbs, sub, width, pw, heads, features, experts, cap, f, sk, ak = cfg
    (tin, small_b, att_b, sh_b, routes, cos, sin, rot, win_a, win_b, wdt_a, wdt_b,
     tok_o, small_o, place_o, place_to, watt0_o, y_o, mid_o, n2_o, rows_o, q_o, k_o, v_o, att_o, slots_o, gu_o, hid_o, rows2_o, sgu_o, shid_o, shw_o, watt_o,
     y, mid, n2, rx, nsend, nall, proj, q, k, v, att, osend, orecv, rwx,
     xsend, xline, xall, nrows, pm, pt, slots, acc, gu, hid, eo, sgu, shid, ssend, srecv, rsend, rpeer, rline, rrecv,
     win, wdt, shw0, shw1, watt0, watt1, tbuf, tok, rts, place, place_t, sm0, sm1, small,
     n_send, n_recv, o_send, o_recv, x_send, x_recv, u_send, u_recv, t_send, t_recv, s_send, s_recv, g_send, g_recv, r_send, r_recv,
     rs_send, rs_recv, ag_send, ag_recv, wi_sem, wd_sem, g_sem, k_sem, i_send, i_recv, q_send, q_recv, *w_sems) = refs
    pos = Position(nx, ny)
    s, a, b, me = pos.s, pos.a, pos.b, pos.me
    slots_n = experts * cap
    tokens = nx * ny * sub
    d = ny * pw
    length = nx * sub
    half = experts // 2
    lane = lax.broadcasted_iota(jnp.int32, (1, pw), 1)
    shares = (
        Share(pos, 0, sh_b, shw0, w_sems[0:4]),
        Share(pos, 1, att_b, watt1, w_sems[4:8]),
        Share(pos, 1, sh_b, shw1, w_sems[8:12]),
    )
    entry_shares = (
        Share(pos, 0, small_b, sm0, w_sems[12:16]),
        Share(pos, 1, small_b, sm1, w_sems[16:20]),
        Share(pos, 0, att_b, watt0, w_sems[20:24]),
    )
    watts, shws = (watt0, watt1), (shw0, shw1)
    barrier = pltpu.get_barrier_semaphore()
    pos.peers(lambda ai: pl.semaphore_signal(barrier, inc=1, device_id=(s, ai, b), device_id_type=MESH))
    pos.line(lambda bi: pl.semaphore_signal(barrier, inc=1, device_id=(s, a, bi), device_id_type=MESH))
    pl.semaphore_signal(barrier, inc=1, device_id=(1 - s, a, b), device_id_type=MESH)
    for j in range(ny):
        @pl.when((a != b) | (b != j))
        def _():
            pl.semaphore_signal(barrier, inc=1, device_id=(s, b, j), device_id_type=MESH)

    def weight_copy(layer, e, which):
        own, oth, dst, sem = ((win_a, win_b, win, wi_sem), (wdt_a, wdt_b, wdt, wd_sem))[which]
        return own.at[e], oth.at[e], dst.at[e], sem.at[e]

    def start_weight(layer, e, which):
        own, oth, dst, sem = weight_copy(layer, e, which)

        @pl.when(s == layer)
        def _():
            pltpu.make_async_copy(own, dst, sem).start()

        @pl.when(s != layer)
        def _():
            pltpu.make_async_copy(oth, dst, sem).start()

    def wait_weight(layer, e, which):
        own, oth, dst, sem = weight_copy(layer, e, which)
        pltpu.make_async_copy(own, dst, sem).wait()

    def first_weights(e, c):
        start_weight(0, e, 0)
        start_weight(0, e, 1)
        return c

    lax.fori_loop(0, experts, first_weights, 0)

    @pl.when(a == b)
    def _():
        pl.semaphore_wait(barrier, nx - 1 + ny - 1 + 1 + nx - 1)

    @pl.when(a != b)
    def _():
        pl.semaphore_wait(barrier, nx - 1 + ny - 1 + 1 + nx)

    def tokens_copy(i, slot, seq):
        src = tin.at[:, :, pl.ds(pl.multiple_of(i * sub, sub), sub), :]
        return remote(src, tbuf.at[slot], i_send.at[i], i_recv.at[slot], (s, i, seq))

    def token_targets(do):
        for c in range(nx):
            i = lax.rem(a + c, nx)

            @pl.when((i != a) | (a != b))
            def _():
                do(tokens_copy(i, b, a))

    def routes_copy(src, slot):
        return remote(routes.at[pl.ds(src * mbs, mbs)], rts.at[slot], q_send, q_recv, (1 - s, a, b))

    token_targets(lambda copy: copy.start())
    routes_copy(1 - s, s).start()
    for share in entry_shares:
        share.start()
    rts[s] = routes[pl.ds(s * mbs, mbs)]

    @pl.when(a == b)
    def _():
        tbuf[b] = tin[:, :, pl.ds(pl.multiple_of(a * sub, sub), sub), :]

    routes_copy(0, 1 - s).wait()

    def places():
        t0 = lax.broadcasted_iota(jnp.int32, (tokens, tokens), 0)
        t1 = lax.broadcasted_iota(jnp.int32, (tokens, tokens), 1)
        before = bf((t1 < t0).astype(jnp.float32))
        after = bf((t0 < t1).astype(jnp.float32))
        er = lax.broadcasted_iota(jnp.int32, (experts, tokens), 0).astype(jnp.float32)
        ec = lax.broadcasted_iota(jnp.int32, (tokens, 128), 1).astype(jnp.float32)
        sub8 = lax.broadcasted_iota(jnp.int32, (128, tokens), 0)
        for l in range(2):
            for m in range(mbs):
                r = rts[l, m].astype(jnp.float32)
                rows = [r[c : c + 1] for c in range(2)]
                hot = [(row == er).astype(jnp.float32) for row in rows]
                count = mm(bf(hot[0] + hot[1]), after)
                cols = jnp.where(sub8 == 0, rows[0], jnp.where(sub8 == 1, rows[1], 0.0)).T
                cols = [cols[:, c : c + 1] for c in range(2)]
                hot_t = [(col == ec).astype(jnp.float32) for col in cols]
                count_t = mm(before, bf(hot_t[0] + hot_t[1]))
                for c in range(2):
                    rank = jnp.sum(hot[c] * count, axis=0, keepdims=True)
                    place[l, m, c : c + 1] = (rows[c] * cap + rank).astype(jnp.int32)
                    rank_t = jnp.sum(hot_t[c] * count_t, axis=1, keepdims=True)
                    place_t[l, m, :, c : c + 1] = (cols[c] * cap + rank_t).astype(jnp.int32)

    def tokens_ready():
        for j in range(ny):
            @pl.when((a != b) | (b != j))
            def _():
                tokens_copy(a, j, j).wait_recv()

            for kind in range(2):
                tok[kind, :, :, j * pw : (j + 1) * pw] = tbuf[j, kind]
        token_targets(lambda copy: copy.wait_send())

    def stream(l, m):
        return (tok[0, m] if l == 0 else y[0, m]).astype(jnp.float32)

    def copy_n(l, m, ai, slot):
        return remote(nsend.at[l, m], nall.at[l, m, slot], n_send.at[l, m, ai], n_recv.at[l, m, slot], (s, ai, b))

    def norm_first(l, m):
        xv = stream(l, m)
        nsend[l, m] = bf(xv * rms(xv, features) * small[l, experts + 1 : experts + 2])
        pos.peers(lambda ai: copy_n(l, m, ai, a).start())
        nall[l, m, a] = nsend[l, m]

    def copy_o(l, m, ai, slot):
        return remote(osend.at[l, m, ai], orecv.at[l, m, slot], o_send.at[l, m, ai], o_recv.at[l, m, slot], (s, ai, b))

    def attention(l, m):
        watt = watts[l]
        pos.peers(lambda ai: copy_n(l, m, ai, ai).wait())
        proj[...] = by_blocks(nall[l, m].reshape(length, d), watt, slice(0, 3 * pw), width, pw)
        v[l, m] = bf(proj[:, 2 * pw : 3 * pw])
        q[l, m] = turn(proj[:, :pw], cos[...], sin[...], rot[...], 1.0)
        k[l, m] = turn(proj[:, pw : 2 * pw], cos[...], sin[...], rot[...], 1.0)
        total = jnp.zeros((length, pw), jnp.float32)
        for h in range(heads):
            mask = head_mask(pw, h)
            p = probs_of(jnp.where(mask, q[l, m], 0), k[l, m])
            total = total + mm(bf(p), jnp.where(mask, v[l, m], 0))
        att[l, m] = bf(total)
        for j in range(ny):
            part = mm(att[l, m], watt[j, :, 3 * pw : 4 * pw], ((1,), (1,)))
            osend[l, m, :, :, j * pw : j * pw + width] = bf(part).reshape(nx, sub, width)
        pos.peers(lambda ai: copy_o(l, m, ai, a).start())
        orecv[l, m, a] = osend[l, m, a]

    def copy_x(l, m, bi, slot):
        return remote(xsend.at[l, m, bi], xline.at[l, m, slot], x_send.at[l, m, bi], x_recv.at[l, m, slot], (s, a, bi))

    def copy_w(l, m, ai, slot):
        return remote(xline.at[l, m], xall.at[l, m, :, slot], u_send.at[l, m, ai], u_recv.at[l, m, slot], (s, ai, b))

    def copy_t(l, m, ai, slot):
        return remote(n2.at[l, m], nrows.at[l, m, slot], t_send.at[l, m, ai], t_recv.at[l, m, slot], (s, ai, b))

    def norm_second(l, m):
        pos.peers(lambda ai: copy_o(l, m, ai, ai).wait())
        mv = stream(l, m)
        for ai in range(nx):
            mv = mv + orecv[l, m, ai].astype(jnp.float32)
        mid[l, m] = mv
        n2v = bf(mv * rms(mv, features) * small[l, experts : experts + 1])
        n2[l, m] = n2v
        rv = mm(n2v, rwx[l], ((1,), (1,)))
        hi = bf(rv)
        lo = bf(rv - hi.astype(jnp.float32))
        tail = jnp.where(lane < width + experts, hi, lo)
        for j in range(ny):
            xsend[l, m, j] = jnp.where(lane < width, n2v[:, j * pw : (j + 1) * pw], tail)
        pos.line(lambda bi: copy_x(l, m, bi, b).start())
        xline[l, m, b] = xsend[l, m, b]
        pos.peers(lambda ai: copy_t(l, m, ai, a).start())
        nrows[l, m, a] = n2[l, m]

    def spread(l, m):
        pos.line(lambda bi: copy_x(l, m, bi, bi).wait())
        pos.peers(lambda ai: copy_w(l, m, ai, a).start())
        xall[l, m, :, a] = xline[l, m]

    def dispatch(l, m):
        i0 = lax.broadcasted_iota(jnp.int32, (slots_n, tokens), 0)
        pm[...] = bf(((place[l, m, 0:1] == i0) | (place[l, m, 1:2] == i0)).astype(jnp.float32))
        pos.peers(lambda ai: copy_w(l, m, ai, ai).wait())
        slots[l, m] = bf(mm(pm[...], xall[l, m].reshape(tokens, pw))).reshape(experts, cap, pw)

    def shared_in_part(l, m):
        pos.peers(lambda ai: copy_t(l, m, ai, ai).wait())
        shw = shws[l]
        gu_s = by_blocks(nrows[l, m].reshape(length, d), shw, slice(0, 2 * f), width, pw)
        sgu[l, m] = bf(gu_s)
        gate = gu_s[:, :f]
        shid[l, m] = bf(gate * jax.nn.sigmoid(gate) * gu_s[:, f:])

    def copy_s(l, m, ai, slot):
        return remote(ssend.at[l, m, ai], srecv.at[l, m, slot], s_send.at[l, m, ai], s_recv.at[l, m, slot], (s, ai, b))

    def shared_out_part(l, m):
        for j in range(ny):
            part = mm(shid[l, m], shws[l][j, :, 2 * f :], ((1,), (1,)))
            ssend[l, m, :, :, j * pw : j * pw + width] = bf(part).reshape(nx, sub, width)
        pos.peers(lambda ai: copy_s(l, m, ai, a).start())
        srecv[l, m, a] = ssend[l, m, a]

    def copy_g(l, m, ai, slot):
        return remote(rsend.at[l, m, ai], rpeer.at[l, m, slot], g_send.at[l, m, ai], g_recv.at[l, m, slot], (s, ai, b))

    def copy_r(l, m, bi, slot):
        return remote(rline.at[l, m, bi], rrecv.at[l, m, slot], r_send.at[l, m, bi], r_recv.at[l, m, slot], (s, a, bi))

    def combine(l, m):
        i1 = lax.broadcasted_iota(jnp.int32, (tokens, slots_n), 1)
        pt[...] = bf(((place_t[l, m, :, 0:1] == i1) | (place_t[l, m, :, 1:2] == i1)).astype(jnp.float32))
        br = mm(pt[...], eo[m].reshape(slots_n, width))
        for ai in range(nx):
            rsend[l, m, ai, :, :, :width] = bf(br).reshape(ny, nx, sub, width)[:, ai]
        pos.peers(lambda ai: copy_g(l, m, ai, a).start())
        rpeer[l, m, a] = rsend[l, m, a]

    def combine_line(l, m):
        pos.peers(lambda ai: copy_g(l, m, ai, ai).wait())
        total = rpeer[l, m, 0].astype(jnp.float32)
        for ai in range(1, nx):
            total = total + rpeer[l, m, ai].astype(jnp.float32)
        rline[l, m] = bf(total)
        pos.line(lambda bi: copy_r(l, m, bi, b).start())
        rrecv[l, m, b] = rline[l, m, b]

    def layer_out(l, m):
        pos.peers(lambda ai: copy_s(l, m, ai, ai).wait())
        pos.line(lambda bi: copy_r(l, m, bi, bi).wait())
        total = mid[l, m]
        for ai in range(nx):
            total = total + srecv[l, m, ai].astype(jnp.float32)
        for j in range(ny):
            part = total[:, j * pw : (j + 1) * pw]
            part = part + jnp.where(lane < width, rrecv[l, m, j].astype(jnp.float32), 0.0)
            y[l, m, :, j * pw : (j + 1) * pw] = bf(part)

    first = (b == ny - 1, b == 0)
    last = (b == 0, b == ny - 1)
    up = (ny - 1 - b, b)
    down = (b, ny - 1 - b)
    lag = (sk + ak) * (ny - 1)
    apart = STAGE_STEPS
    gap = max(half - 1 + lag + 6 * apart + 1 - 2 * half, 0)
    starts = (0, half, 2 * half + gap, 3 * half + gap)
    steps = starts[3] + half + lag

    def unit(t, dd):
        early = (t >= 0) & (t < 2 * half)
        late = (t >= starts[2]) & (t < starts[2] + 2 * half)
        u = jnp.clip(jnp.where(t < starts[2], jnp.minimum(t, 2 * half - 1), t - gap), 0, 4 * half - 1)
        job = u // half
        return early | late, job // 2, lax.rem(job, 2), lax.rem(u, half) + dd * half

    def gu_copy(dd, l, m, e):
        to = b - 1 if dd == 0 else b + 1
        return remote(gu.at[l, m, e], gu.at[l, m, e], rs_send.at[l, m, e], rs_recv.at[l, m, e], (s, a, to))

    def hid_copy(dd, l, m, e):
        to = b + 1 if dd == 0 else b - 1
        return remote(hid.at[l, m, e], hid.at[l, m, e], ag_send.at[l, m, e], ag_recv.at[l, m, e], (s, a, to))

    def chain(i):
        reduce = [unit(i - sk * up[dd], dd) for dd in range(2)]
        spreads = [unit(i - sk * (ny - 1) - ak * down[dd], dd) for dd in range(2)]
        for dd in range(2):
            valid, l, m, e = reduce[dd]

            @pl.when(valid)
            def _():
                @pl.when(m == 0)
                def _():
                    wait_weight(0, e, 0)

                acc[dd] = mm(slots[l, m, e, :, :width], win[e])

                @pl.when((l == 0) & (m == 1))
                def _():
                    start_weight(1, e, 0)

        for dd in range(2):
            valid, l, m, e = reduce[dd]

            @pl.when(valid & first[dd])
            def _():
                gu[l, m, e] = bf(acc[dd])
                gu_copy(dd, l, m, e).start()

            @pl.when(valid & jnp.logical_not(first[dd] | last[dd]))
            def _():
                gu_copy(dd, l, m, e).wait_recv()
                gu[l, m, e] = bf(acc[dd] + gu[l, m, e].astype(jnp.float32))
                gu_copy(dd, l, m, e).start()

            @pl.when(valid & last[dd])
            def _():
                gu_copy(dd, l, m, e).wait_recv()
                total = acc[dd] + gu[l, m, e].astype(jnp.float32)
                r = router_column(slots[l, m, e], e, width, experts)
                gate = total[:, :f]
                hid[l, m, e] = bf(gate * jax.nn.sigmoid(gate) * total[:, f:] * jax.nn.sigmoid(r))
                hid_copy(dd, l, m, e).start()
                gu[l, m, e] = bf(total)
                pltpu.make_async_copy(gu.at[l, m, e], gu_o.at[l, m, e], g_sem.at[l, m, e]).start()

        for dd in range(2):
            valid, l, m, e = spreads[dd]

            @pl.when(valid & jnp.logical_not(last[dd]))
            def _():
                hid_copy(dd, l, m, e).wait_recv()

                @pl.when(jnp.logical_not(first[dd]))
                def _():
                    hid_copy(dd, l, m, e).start()

        for dd in range(2):
            valid, l, m, e = spreads[dd]

            @pl.when(valid)
            def _():
                @pl.when(m == 0)
                def _():
                    wait_weight(0, e, 1)

                eo[m, e] = bf(mm(hid[l, m, e], wdt[e], ((1,), (1,))))

                @pl.when((l == 0) & (m == 1))
                def _():
                    start_weight(1, e, 1)

    kept = [
        (mid, mid_o), (n2, n2_o), (nall, rows_o), (q, q_o), (k, k_o), (v, v_o), (att, att_o), (slots, slots_o),
        (hid, hid_o), (nrows, rows2_o), (sgu, sgu_o), (shid, shid_o), (y, y_o),
    ]
    stages = {}

    def at(step, do):
        stages.setdefault(step, []).append(do)

    def stage(do, l, m):
        return lambda: do(l, m)

    osend[...] = jnp.zeros_like(osend)
    ssend[...] = jnp.zeros_like(ssend)
    rwx[...] = jnp.zeros_like(rwx)
    for h in range(1, ny):
        for share in entry_shares:
            share.hop(h)
    for share in entry_shares[:2]:
        share.finish()
    tokens_ready()
    for l, full in enumerate((sm0, sm1)):
        for j in range(ny):
            small[l, :, j * pw : (j + 1) * pw] = full[j]
    for l in range(2):
        rwx[l, width : width + experts] = bf(small[l, :experts])
        rwx[l, width + experts : width + 2 * experts] = bf(small[l, :experts])
    norm_first(0, 0)
    norm_first(0, 1)
    places()
    entry_shares[2].finish()
    shares[0].start()
    shares[1].start()
    attention(0, 0)
    norm_second(0, 0)
    attention(0, 1)
    spread(0, 0)
    norm_second(0, 1)
    dispatch(0, 0)
    for h in range(1, ny):
        at(h - 1, lambda h=h: (shares[0].hop(h), shares[1].hop(h)))
    at(1, stage(spread, 0, 1))
    at(3, stage(dispatch, 0, 1))
    at(4, lambda: (shares[0].finish(), shares[1].finish()))
    at(5, stage(shared_in_part, 0, 0))
    at(6, stage(shared_out_part, 0, 0))
    at(half, stage(shared_in_part, 0, 1))
    at(half + 1, stage(shared_out_part, 0, 1))
    for m in range(2):
        done = starts[m] + half - 1 + lag
        for c, do in enumerate((combine, combine_line)):
            at(done + c * apart, stage(do, 0, m))
        at(done + 2 * apart, stage(layer_out, 0, m))
        for c, do in enumerate((norm_first, attention, norm_second, spread, dispatch)):
            at(done + (2 + c) * apart, stage(do, 1, m))
        at(starts[2 + m] + 2, stage(shared_in_part, 1, m))
        at(starts[2 + m] + 4, stage(shared_out_part, 1, m))
        done = starts[2 + m] + half - 1 + lag
        for c, do in enumerate((combine, combine_line, layer_out)):
            at(done + c * apart, stage(do, 1, m))
    at(half + lag, shares[2].start)
    for h in range(1, ny):
        at(half + lag + h, lambda h=h: shares[2].hop(h))
    at(half + lag + ny, shares[2].finish)

    def step(i, c):
        chain(i)
        for when in sorted(stages):
            if when < steps:
                @pl.when(i == when)
                def _():
                    for do in stages[when]:
                        do()

        return c

    lax.fori_loop(0, steps, step, 0)
    for when in sorted(stages):
        if when >= steps:
            for do in stages[when]:
                do()
    kept += [(shw0, shw_o.at[0]), (shw1, shw_o.at[1]), (watt1, watt_o), (watt0, watt0_o), (tok, tok_o), (small, small_o)]
    kept += [(place, place_o), (place_t, place_to)]
    saves = [pltpu.make_async_copy(src, dst, k_sem.at[i]) for i, (src, dst) in enumerate(kept)]
    for copy in saves:
        copy.start()

    def finish(index, c):
        l = index // (mbs * half)
        m = lax.rem(index // half, mbs)
        for dd in range(2):
            e = lax.rem(index, half) + dd * half

            @pl.when(jnp.logical_not(last[dd]))
            def _():
                gu_copy(dd, l, m, e).wait_send()

            @pl.when(jnp.logical_not(first[dd]))
            def _():
                hid_copy(dd, l, m, e).wait_send()

            @pl.when(last[dd])
            def _():
                pltpu.make_async_copy(gu.at[l, m, e], gu_o.at[l, m, e], g_sem.at[l, m, e]).wait()

        return c

    lax.fori_loop(0, 2 * mbs * half, finish, 0)
    for copy in saves:
        copy.wait()


def forward(tin, small_b, att_block, sh_block, routes, cos, sin, rot, win, wdt, dims, heads, features, ids):
    width, pw, experts, cap = dims
    nx, ny = lax.axis_size("gx"), lax.axis_size("gy")
    mbs, length = tin.shape[1:3]
    sub, d = length // nx, ny * pw
    f = wdt[0].shape[-1]
    length, tokens, n, slots = nx * sub, nx * ny * sub, nx * ny, experts * cap
    b16, f32 = jnp.bfloat16, jnp.float32
    vm = pl.BlockSpec(memory_space=pltpu.VMEM)
    hbm = pl.BlockSpec(memory_space=pl.ANY)
    lm = (2, mbs)
    rows_shape = lm + (nx, sub, d)
    spread_shape = lm + (ny, nx, sub, pw)
    entry = (
        ((2, mbs, sub, d), b16), ((2, small_b.shape[0], d), f32), (lm + (2, tokens), jnp.int32),
        (lm + (tokens, 2), jnp.int32), ((ny,) + att_block.shape, b16),
    )
    kept = entry + (
        (lm + (sub, d), b16), (lm + (sub, d), f32), (lm + (sub, d), b16), (rows_shape, b16),
        (lm + (length, pw), b16), (lm + (length, pw), b16), (lm + (length, pw), b16), (lm + (length, pw), b16),
        (lm + (experts, cap, pw), b16), (lm + (experts, cap, 2 * f), b16), (lm + (experts, cap, f), b16),
        (rows_shape, b16), (lm + (length, 2 * f), b16), (lm + (length, f), b16),
        ((2, ny) + sh_block.shape, b16), ((ny,) + att_block.shape, b16),
    )
    scratch = (
        (lm + (sub, d), b16), (lm + (sub, d), f32), (lm + (sub, d), b16), None,
        (lm + (sub, d), b16), (rows_shape, b16), ((length, 3 * pw), f32),
        (lm + (length, pw), b16), (lm + (length, pw), b16), (lm + (length, pw), b16), (lm + (length, pw), b16),
        (rows_shape, b16), (rows_shape, b16), ((2, pw, d), b16),
        (lm + (ny, sub, pw), b16), (lm + (ny, sub, pw), b16), (spread_shape, b16), (rows_shape, b16),
        ((slots, tokens), b16), ((tokens, slots), b16), (lm + (experts, cap, pw), b16), ((2, cap, 2 * f), f32),
        (lm + (experts, cap, 2 * f), b16), (lm + (experts, cap, f), b16), ((mbs, experts, cap, width), b16),
        (lm + (length, 2 * f), b16), (lm + (length, f), b16), (rows_shape, b16), (rows_shape, b16),
        (lm + (nx, ny, sub, pw), b16), (lm + (nx, ny, sub, pw), b16), (lm + (ny, sub, pw), b16), (lm + (ny, sub, pw), b16),
        ((experts, width, 2 * f), b16), ((experts, width, f), b16),
        ((ny,) + sh_block.shape, b16), ((ny,) + sh_block.shape, b16), ((ny,) + att_block.shape, b16), ((ny,) + att_block.shape, b16),
        ((ny, 2, mbs, sub, pw), b16), ((2, mbs, sub, d), b16), (lm + (2, tokens), jnp.int32),
        (lm + (2, tokens), jnp.int32), (lm + (tokens, 2), jnp.int32),
        ((ny,) + small_b.shape, f32), ((ny,) + small_b.shape, f32), ((2, small_b.shape[0], d), f32),
    )
    outs = pl.pallas_call(
        functools.partial(forward_kernel, (nx, ny, mbs, sub, width, pw, heads, features, experts, cap, f, *FWD_SKEW)),
        out_shape=tuple(jax.ShapeDtypeStruct(*v) for v in kept),
        in_specs=[vm] * 8 + [hbm] * 4,
        out_specs=(hbm,) * len(kept),
        scratch_shapes=[pltpu.VMEM(*(v or ((8, 128), f32))) for v in scratch] + [
            flags(lm + (nx,)), flags(lm + (nx,)), flags(lm + (nx,)), flags(lm + (nx,)),
            flags(lm + (ny,)), flags(lm + (ny,)), flags(lm + (nx,)), flags(lm + (nx,)), flags(lm + (nx,)), flags(lm + (nx,)),
            flags(lm + (nx,)), flags(lm + (nx,)), flags(lm + (nx,)), flags(lm + (nx,)), flags(lm + (ny,)), flags(lm + (ny,)),
            flags(lm + (experts,)), flags(lm + (experts,)), flags(lm + (experts,)), flags(lm + (experts,)),
            flags((experts,)), flags((experts,)), flags(lm + (experts,)), flags((24,)),
            flags((nx,)), flags((ny,)), pltpu.SemaphoreType.DMA, pltpu.SemaphoreType.DMA,
        ] + share_sems(ny) * 6,
        compiler_params=params(ids),
        cost_estimate=pl.CostEstimate(flops=10**10, bytes_accessed=8 * 10**7, transcendentals=10**6),
        name="forward",
    )(tin, small_b, att_block, sh_block, routes, cos, sin, rot, *win, *wdt)
    names = ("tok", "small", "place", "place_t", "watt0", "y", "mid", "n2", "rows", "q", "k", "v", "att", "slots", "gu", "hid", "rows2", "sgu", "shid", "shw", "watt1")
    return dict(zip(names, outs))


FWD_SKEW = (1, 1)
STAGE_STEPS = 1


def backward_kernel(cfg, *refs):
    layer, nx, ny, mbs, sub, width, pw, heads, features, experts, cap, f, sk, ak = cfg
    n_by = 16
    by_layer, refs = refs[:n_by], refs[n_by:]
    (watt, cos, sin, rot, slots_i, gu_i, hid_i, win_a, win_b, wdt_a, wdt_b) = refs[:11]
    refs = refs[11 + (0 if layer else 5) :]
    (gx_o, win_g, wdt_g, att_g, sh_g, small_g,
     win, wdt, xsend, xline, xall, grows, pm, pt, slots, gslots, gown, hid, acc, dh, dgu, deo, sti, std,
     dsgu, ssend, srecv, rsend, rpeer, rline, rrecv, rwx, dm, msend, mall, datt, dqkv, dsend, drecv,
     rw_p, gains, sh_p, att_p, small_p, sh_x, att_x, small_x, sh_r, att_r, small_r, sh_f, att_f, small_f, small_a,
     x, g, small, mid, n2, rows, q, k, v, att, rows2, sgu, shid, shw, place, place_t,
     w_sem, x_send, x_recv, u_send, u_recv, t_send, t_recv, s_send, s_recv, g_send, g_recv, r_send, r_recv,
     m_send, m_recv, d_send, d_recv, rs_send, rs_recv, ag_send, ag_recv, wi_send, wi_recv, wd_send, wd_recv,
     c_send, c_recv, e_send, e_recv, a_send, a_recv, l_sem, st_sem, f_sem, y_sem, free) = refs
    resident = (g, small, place, place_t, x, mid, n2, rows, q, k, v, att, rows2, sgu, shid, shw)
    pos = Position(nx, ny)
    s, a, b = pos.s, pos.a, pos.b
    keeper = s == layer
    helper = jnp.logical_not(keeper)
    slots_n = experts * cap
    tokens = nx * ny * sub
    d = ny * pw
    length = nx * sub
    half = experts // 2
    scale = DH ** -0.5
    lane = lax.broadcasted_iota(jnp.int32, (1, pw), 1)
    first = (b == ny - 1, b == 0)
    last = (b == 0, b == ny - 1)
    up = (ny - 1 - b, b)
    down = (b, ny - 1 - b)
    barrier = pltpu.get_barrier_semaphore()
    pos.peers(lambda ai: pl.semaphore_signal(barrier, inc=1, device_id=(s, ai, b), device_id_type=MESH))
    pos.line(lambda bi: pl.semaphore_signal(barrier, inc=1, device_id=(s, a, bi), device_id_type=MESH))
    pl.semaphore_signal(barrier, inc=1, device_id=(1 - s, a, b), device_id_type=MESH)

    for j, (dst, own, oth) in enumerate(((win, win_a, win_b), (wdt, wdt_a, wdt_b))):
        @pl.when(keeper)
        def _():
            pltpu.make_async_copy(own, dst, w_sem.at[j]).start()

        @pl.when(helper)
        def _():
            pltpu.make_async_copy(oth, dst, w_sem.at[j]).start()

    picks = (-1, layer, layer, layer, 0) + (layer,) * 11
    fills = [
        pltpu.make_async_copy(src.at[src.shape[0] - 1 if at < 0 else at], dst, y_sem.at[c])
        for c, (src, dst, at) in enumerate(zip(by_layer, resident, picks))
    ]
    for copy in fills:
        copy.start()
    loads = fills[4:] + [pltpu.make_async_copy(slots_i.at[layer], slots, l_sem.at[0]), pltpu.make_async_copy(hid_i.at[layer], hid, l_sem.at[1])]
    for copy in loads[-2:]:
        copy.start()

    def own_gates(dd):
        part = pl.ds(dd * half, half)
        return pltpu.make_async_copy(gu_i.at[layer, :, part], gown, l_sem.at[2])

    for dd in range(2):
        pl.when(last[dd])(own_gates(dd).start)

    def copy_x(m, bi, slot):
        return remote(xsend.at[m, bi], xline.at[m, slot], x_send.at[m, bi], x_recv.at[m, slot], (s, a, bi))

    def copy_w(m, ai, slot):
        return remote(xline.at[m], xall.at[m, :, slot], u_send.at[m, ai], u_recv.at[m, slot], (s, ai, b))

    def copy_t(m, ai, slot):
        return remote(g.at[m], grows.at[m, slot], t_send.at[m, ai], t_recv.at[m, slot], (s, ai, b))

    for copy in fills[:4]:
        copy.wait()
    for m in range(mbs):
        for j in range(ny):
            xsend[m, j] = g[m, :, j * pw : (j + 1) * pw]
    pl.semaphore_wait(barrier, nx - 1 + ny - 1 + 1)
    for m in range(mbs):
        pos.line(lambda bi: copy_x(m, bi, b).start())
        xline[m, b] = xsend[m, b]
    for m in range(mbs):
        pos.peers(lambda ai: copy_t(m, ai, a).start())
        grows[m, a] = g[m]
    deo[...] = jnp.zeros_like(deo)
    ssend[...] = jnp.zeros_like(ssend)
    dsend[...] = jnp.zeros_like(dsend)
    rwx[...] = jnp.zeros_like(rwx)
    rwx[width : width + experts] = bf(small[:experts])
    rwx[width + experts : width + 2 * experts] = bf(small[:experts])
    rw_p[...] = jnp.zeros_like(rw_p)
    gains[...] = jnp.zeros_like(gains)

    def spread(m):
        pos.line(lambda bi: copy_x(m, bi, bi).wait())
        pos.peers(lambda ai: copy_w(m, ai, a).start())
        xall[m, :, a] = xline[m]

    def dispatch(m):
        i0 = lax.broadcasted_iota(jnp.int32, (slots_n, tokens), 0)
        pm[...] = bf(((place[m, 0:1] == i0) | (place[m, 1:2] == i0)).astype(jnp.float32))
        pos.peers(lambda ai: copy_w(m, ai, ai).wait())
        gslots[m] = bf(mm(pm[...], xall[m].reshape(tokens, pw))).reshape(experts, cap, pw)

    def shared_act(m):
        pos.peers(lambda ai: copy_t(m, ai, ai).wait())
        dsh = by_blocks(grows[m].reshape(length, d), shw, slice(2 * f, 3 * f), width, pw)
        dsg, dsu, _ = act_back(sgu[m, :, :f].astype(jnp.float32), sgu[m, :, f:].astype(jnp.float32), dsh, None)
        dsgu[m, :, :f] = bf(dsg)
        dsgu[m, :, f:] = bf(dsu)

    def copy_s(m, ai, slot):
        return remote(ssend.at[m, ai], srecv.at[m, slot], s_send.at[m, ai], s_recv.at[m, slot], (s, ai, b))

    def shared_back(m):
        for j in range(ny):
            part = mm(dsgu[m], shw[j, :, : 2 * f], ((1,), (1,)))
            ssend[m, :, :, j * pw : j * pw + width] = bf(part).reshape(nx, sub, width)
        pos.peers(lambda ai: copy_s(m, ai, a).start())
        srecv[m, a] = ssend[m, a]

    crossing = ((sh_p, sh_x), (att_p, att_x), (small_p, small_x))
    places = (sh_r, att_r, small_r)
    finals = (sh_f, att_f, small_f)
    results = (sh_g, att_g, small_g)

    def cross(i):
        return remote(crossing[i][0], crossing[i][1], c_send.at[i], c_recv.at[i], (layer, a, b))

    def block(i, bi):
        if i == 2:
            return small_x.at[:, pl.ds(pl.multiple_of(bi * pw, pw), pw)]
        return crossing[i][1].at[bi]

    def along(i, bi, slot):
        return remote(block(i, bi), places[i].at[slot], e_send.at[i, bi], e_recv.at[i, slot], (s, a, bi))

    def give(i):
        pl.when(helper)(cross(i).start)

    def join(i):
        @pl.when(keeper)
        def _():
            cross(i).wait_recv()
            part, other = crossing[i]
            other[...] = (part[...].astype(jnp.float32) + other[...].astype(jnp.float32)).astype(other.dtype)
            pos.line(lambda bi: along(i, bi, b).start())

    def settle(i):
        @pl.when(keeper)
        def _():
            pos.line(lambda bi: along(i, bi, bi).wait())
            total = block(i, b)[...].astype(jnp.float32)
            for c in range(1, ny):
                total = total + places[i][lax.rem(b + c, ny)].astype(jnp.float32)
            finals[i][...] = total
            if i < 2:
                pltpu.make_async_copy(finals[i], results[i], f_sem.at[i]).start()

    def shared_grads():
        for j in range(ny):
            rj = rows2[:, :, :, j * pw : j * pw + width].reshape(mbs * length, width)
            sh_p[j, :, : 2 * f] = bf(mm(rj, dsgu[...].reshape(mbs * length, 2 * f), ((0,), (0,))))

    def down_grads():
        for j in range(ny):
            gj = grows[:, :, :, j * pw : j * pw + width].reshape(mbs * length, width)
            sh_p[j, :, 2 * f :] = bf(mm(gj, shid[...].reshape(mbs * length, f), ((0,), (0,))))
        give(0)

    def copy_g(m, ai, slot):
        return remote(rsend.at[m, ai], rpeer.at[m, slot], g_send.at[m, ai], g_recv.at[m, slot], (s, ai, b))

    def copy_r(m, bi, slot):
        return remote(rline.at[m, bi], rrecv.at[m, slot], r_send.at[m, bi], r_recv.at[m, slot], (s, a, bi))

    def combine(m):
        i1 = lax.broadcasted_iota(jnp.int32, (tokens, slots_n), 1)
        pt[...] = bf(((place_t[m, :, 0:1] == i1) | (place_t[m, :, 1:2] == i1)).astype(jnp.float32))
        br = bf(mm(pt[...], deo[m].reshape(slots_n, pw))).reshape(ny, nx, sub, pw)
        for ai in range(nx):
            rsend[m, ai] = br[:, ai]
        pos.peers(lambda ai: copy_g(m, ai, a).start())
        rpeer[m, a] = rsend[m, a]

    def combine_line(m):
        pos.peers(lambda ai: copy_g(m, ai, ai).wait())
        total = rpeer[m, 0].astype(jnp.float32)
        for ai in range(1, nx):
            total = total + rpeer[m, ai].astype(jnp.float32)
        rline[m] = bf(total)
        pos.line(lambda bi: copy_r(m, bi, b).start())
        rrecv[m, b] = rline[m, b]

    def copy_m(m, ai, slot):
        return remote(msend.at[m], mall.at[m, slot], m_send.at[m, ai], m_recv.at[m, slot], (s, ai, b))

    def second_norm(m):
        pos.peers(lambda ai: copy_s(m, ai, ai).wait())
        pos.line(lambda bi: copy_r(m, bi, bi).wait())
        dlog = jnp.zeros((sub, pw), jnp.float32)
        parts = []
        for j in range(ny):
            part = rrecv[m, j].astype(jnp.float32)
            dlog = dlog + jnp.where(lane >= width, part, 0.0)
            parts.append(jnp.where(lane < width, part, 0.0))
        hi = bf(dlog)
        lo = bf(dlog - hi.astype(jnp.float32))
        dn2 = jnp.concatenate(parts, 1) + mm(hi, rwx[...]) + mm(lo, rwx[...])
        for ai in range(nx):
            dn2 = dn2 + srecv[m, ai].astype(jnp.float32)
        rw_t = mm(hi, n2[m], ((0,), (0,))) + mm(lo, n2[m], ((0,), (0,)))
        rw_p[...] += rw_t[width : width + experts] + rw_t[width + experts : width + 2 * experts]
        mv = mid[m]
        dx2, gain_g = norm_back(mv, rms(mv, features), small[experts : experts + 1], dn2, features)
        gains[0:1] += gain_g
        dm[m] = g[m].astype(jnp.float32) + dx2
        msend[m] = bf(dm[m])
        pos.peers(lambda ai: copy_m(m, ai, a).start())
        mall[m, a] = msend[m]

    def copy_d(m, ai, slot):
        return remote(dsend.at[m, ai], drecv.at[m, slot], d_send.at[m, ai], d_recv.at[m, slot], (s, ai, b))

    def attention(m):
        pos.peers(lambda ai: copy_m(m, ai, ai).wait())
        datt[...] = bf(by_blocks(mall[m].reshape(length, d), watt, slice(3 * pw, 4 * pw), width, pw))
        dq = jnp.zeros((length, pw), jnp.float32)
        dk = dq
        dv = dq
        for h in range(heads):
            mask = head_mask(pw, h)
            qh = jnp.where(mask, q[m], 0)
            kh = jnp.where(mask, k[m], 0)
            da = jnp.where(mask, datt[...], 0)
            p = probs_of(qh, k[m])
            dp = mm(da, v[m], ((1,), (1,)))
            ds = bf(p * (dp - jnp.sum(dp * p, axis=1, keepdims=True)))
            dv = dv + mm(bf(p), da, ((0,), (0,)))
            dq = dq + mm(ds, kh)
            dk = dk + mm(ds, qh, ((0,), (0,)))
        dqkv[m, :, :pw] = turn(dq * scale, cos[...], sin[...], rot[...], -1.0)
        dqkv[m, :, pw : 2 * pw] = turn(dk * scale, cos[...], sin[...], rot[...], -1.0)
        dqkv[m, :, 2 * pw :] = bf(dv)
        for j in range(ny):
            part = mm(dqkv[m], watt[j, :, : 3 * pw], ((1,), (1,)))
            dsend[m, :, :, j * pw : j * pw + width] = bf(part).reshape(nx, sub, width)
        pos.peers(lambda ai: copy_d(m, ai, a).start())
        drecv[m, a] = dsend[m, a]

    def first_norm(m):
        pos.peers(lambda ai: copy_d(m, ai, ai).wait())
        dn1 = drecv[m, 0].astype(jnp.float32)
        for ai in range(1, nx):
            dn1 = dn1 + drecv[m, ai].astype(jnp.float32)
        xv = x[m].astype(jnp.float32)
        dx1, gain_g = norm_back(xv, rms(xv, features), small[experts + 1 : experts + 2], dn1, features)
        gains[1:2] += gain_g
        gx_o[m] = bf(dm[m] + dx1)

    def attention_grads():
        for j in range(ny):
            cols = slice(j * pw, j * pw + width)
            rj = rows[:, :, :, cols].reshape(mbs * length, width)
            mj = mall[:, :, :, cols].reshape(mbs * length, width)
            att_p[j, :, : 3 * pw] = bf(mm(rj, dqkv[...].reshape(mbs * length, 3 * pw), ((0,), (0,))))
            att_p[j, :, 3 * pw :] = bf(mm(mj, att[...].reshape(mbs * length, pw), ((0,), (0,))))
        give(1)

    def small_grads():
        small_p[:experts] = rw_p[...]
        small_p[experts:] = gains[...]
        give(2)

    lag = (sk + ak) * (ny - 1)
    apart = STAGE_STEPS
    starts = (0, half)

    def unit(t, dd):
        u = jnp.clip(t, 0, mbs * half - 1)
        return (t >= 0) & (t < mbs * half), u // half, lax.rem(u, half) + dd * half

    def dh_copy(dd, m, e):
        to = b - 1 if dd == 0 else b + 1
        return remote(dh.at[m, e], dh.at[m, e], rs_send.at[m, e], rs_recv.at[m, e], (s, a, to))

    def dgu_copy(dd, m, e):
        to = b + 1 if dd == 0 else b - 1
        return remote(dgu.at[m, e], dgu.at[m, e], ag_send.at[m, e], ag_recv.at[m, e], (s, a, to))

    def wi_copy(e):
        return remote(win.at[e], win.at[e], wi_send.at[e], wi_recv.at[e], (layer, a, b))

    def wd_copy(e):
        return remote(wdt.at[e], wdt.at[e], wd_send.at[e], wd_recv.at[e], (layer, a, b))

    def st_copies(e, slot):
        return (pltpu.make_async_copy(sti.at[slot], win_g.at[e], st_sem.at[0, slot]),
                pltpu.make_async_copy(std.at[slot], wdt_g.at[e], st_sem.at[1, slot]))

    def weight_grads(e):
        gi = mm(slots[:, e, :, :width].reshape(mbs * cap, width), dgu[:, e].reshape(mbs * cap, 2 * f), ((0,), (0,)))
        gd = mm(gslots[:, e, :, :width].reshape(mbs * cap, width), hid[:, e].reshape(mbs * cap, f), ((0,), (0,)))
        return gi, gd

    late = 2
    steps = starts[1] + half + lag + late

    def chain(i):
        reduce = [unit(i - sk * up[dd], dd) for dd in range(2)]
        spreads = [unit(i - sk * (ny - 1) - ak * down[dd], dd) for dd in range(2)]
        for dd in range(2):
            valid, m, e = reduce[dd]

            @pl.when(valid)
            def _():
                acc[dd] = mm(gslots[m, e, :, :width], wdt[e])

            @pl.when(valid & first[dd])
            def _():
                dh[m, e] = bf(acc[dd])
                dh_copy(dd, m, e).start()

            @pl.when(valid & jnp.logical_not(first[dd] | last[dd]))
            def _():
                dh_copy(dd, m, e).wait_recv()
                dh[m, e] = bf(acc[dd] + dh[m, e].astype(jnp.float32))
                dh_copy(dd, m, e).start()

            @pl.when(valid & last[dd])
            def _():
                dh_copy(dd, m, e).wait_recv()
                total = acc[dd] + dh[m, e].astype(jnp.float32)
                r = router_column(slots[m, e], e, width, experts)
                gate = gown[m, e - dd * half, :, :f].astype(jnp.float32)
                upv = gown[m, e - dd * half, :, f:].astype(jnp.float32)
                dgate, dup, dr = act_back(gate, upv, total, jax.nn.sigmoid(r))
                dgu[m, e, :, :f] = bf(dgate)
                dgu[m, e, :, f:] = bf(dup)
                dgu_copy(dd, m, e).start()
                hi = bf(dr).astype(jnp.float32)
                deo[m, e] = bf(jnp.where(lane == width + e, hi, jnp.where(lane == width + experts + e, dr - hi, 0.0)))

        for dd in range(2):
            valid, m, e = spreads[dd]

            @pl.when(valid & jnp.logical_not(last[dd]))
            def _():
                dgu_copy(dd, m, e).wait_recv()

                @pl.when(jnp.logical_not(first[dd]))
                def _():
                    dgu_copy(dd, m, e).start()

            @pl.when(valid)
            def _():
                deo[m, e, :, :width] = bf(mm(dgu[m, e], win[e], ((1,), (1,))))

        u = i - half - lag

        @pl.when((u >= 0) & (u < half) & keeper)
        def _():
            pl.semaphore_signal(free, inc=1, device_id=(1 - s, a, b), device_id_type=MESH)

        @pl.when((u >= 0) & (u < half) & helper)
        def _():
            pl.semaphore_wait(free, 1)
            for dd in range(2):
                e = jnp.clip(u, 0, half - 1) + dd * half
                gi, gd = weight_grads(e)
                win[e] = bf(gi)
                wi_copy(e).start()
                wdt[e] = bf(gd)
                wd_copy(e).start()

        w = u - late

        @pl.when((w >= 0) & (w < half) & keeper)
        def _():
            for dd in range(2):
                e = jnp.clip(w, 0, half - 1) + dd * half

                @pl.when(w >= 1)
                def _():
                    for copy in st_copies(e - 1, dd):
                        copy.wait()

                gi, gd = weight_grads(e)
                wi_copy(e).wait_recv()
                sti[dd] = gi + win[e].astype(jnp.float32)
                wd_copy(e).wait_recv()
                std[dd] = gd + wdt[e].astype(jnp.float32)
                for copy in st_copies(e, dd):
                    copy.start()

    stages = {}

    def at(step, do, *args):
        stages.setdefault(step, []).append(lambda: do(*args))

    spread(0)
    spread(1)
    dispatch(0)
    for j, (dst, own) in enumerate(((win, win_a), (wdt, wdt_a))):
        pltpu.make_async_copy(own, dst, w_sem.at[j]).wait()
    for copy in loads:
        copy.wait()
    for dd in range(2):
        pl.when(last[dd])(own_gates(dd).wait)
    at(1, dispatch, 1)
    at(2, shared_act, 0)
    at(3, shared_act, 1)
    at(4, shared_grads)
    at(5, down_grads)
    at(6, shared_back, 0)
    at(7, join, 0)
    at(8, shared_back, 1)
    for m in range(2):
        done = starts[m] + half - 1 + lag
        for c, do in enumerate((combine, combine_line, second_norm, attention, first_norm)):
            at(done + c * apart, do, m)
    end = starts[1] + half - 1 + lag
    at(end - 1, settle, 0)
    at(end + 3 * apart, attention_grads)
    at(end + 4 * apart, join, 1)
    at(end + 4 * apart, small_grads)
    at(end + 5 * apart, join, 2)
    at(end + 5 * apart, settle, 1)
    at(end + 5 * apart, settle, 2)

    def step(i, c):
        chain(i)
        for when in sorted(stages):
            if when < steps:
                @pl.when(i == when)
                def _():
                    for do in stages[when]:
                        do()

        return c

    lax.fori_loop(0, steps, step, 0)
    for when in sorted(stages):
        if when >= steps:
            for do in stages[when]:
                do()

    def copy_a(ai, slot):
        return remote(small_f, small_a.at[slot], a_send.at[ai], a_recv.at[slot], (s, ai, b))

    @pl.when(helper)
    def _():
        for i in range(3):
            cross(i).wait_send()

    @pl.when(keeper)
    def _():
        pos.peers(lambda ai: copy_a(ai, a).start())
        small_a[a] = small_f[...]
        pos.peers(lambda ai: copy_a(ai, ai).wait())
        total = small_a[0]
        for ai in range(1, nx):
            total = total + small_a[ai]
        small_f[...] = total
        pltpu.make_async_copy(small_f, small_g, f_sem.at[2]).start()
        for i in range(3):
            pltpu.make_async_copy(finals[i], results[i], f_sem.at[i]).wait()
        for dd in range(2):
            for copy in st_copies((dd + 1) * half - 1, dd):
                copy.wait()

    def finish(index, c):
        m = index // half
        for dd in range(2):
            e = lax.rem(index, half) + dd * half

            @pl.when(jnp.logical_not(last[dd]))
            def _():
                dh_copy(dd, m, e).wait_send()

            @pl.when(jnp.logical_not(first[dd]))
            def _():
                dgu_copy(dd, m, e).wait_send()

            @pl.when(helper & (m == 0))
            def _():
                wi_copy(e).wait_send()
                wd_copy(e).wait_send()

        return c

    lax.fori_loop(0, mbs * half, finish, 0)


def backward(layer, g, fwd, watt, cos, sin, rot, win, wdt, grads, dims, heads, features, ids):
    width, pw, experts, cap = dims
    nx, ny = lax.axis_size("gx"), lax.axis_size("gy")
    mbs, sub, d = g.shape[-3:]
    f = wdt[0].shape[-1]
    length, tokens, slots = nx * sub, nx * ny * sub, experts * cap
    b16, f32 = jnp.bfloat16, jnp.float32
    vm = pl.BlockSpec(memory_space=pltpu.VMEM)
    hbm = pl.BlockSpec(memory_space=pl.ANY)
    ac, sc, n, half = watt.shape[2], fwd["shw"].shape[3], fwd["small"].shape[1], experts // 2
    rows_shape = (mbs, nx, sub, d)
    dense = lambda c: ((ny, width, c), b16)
    scratch = (
        ((experts, width, 2 * f), b16), ((experts, width, f), b16),
        ((mbs, ny, sub, pw), b16), ((mbs, ny, sub, pw), b16), ((mbs, ny, nx, sub, pw), b16), (rows_shape, b16),
        ((slots, tokens), b16), ((tokens, slots), b16),
        ((mbs, experts, cap, pw), b16), ((mbs, experts, cap, pw), b16), ((mbs, half, cap, 2 * f), b16),
        ((mbs, experts, cap, f), b16), ((2, cap, f), f32), ((mbs, experts, cap, f), b16),
        ((mbs, experts, cap, 2 * f), b16), ((mbs, experts, cap, pw), b16),
        ((2, width, 2 * f), f32), ((2, width, f), f32),
        ((mbs, length, 2 * f), b16), (rows_shape, b16), (rows_shape, b16),
        ((mbs, nx, ny, sub, pw), b16), ((mbs, nx, ny, sub, pw), b16), ((mbs, ny, sub, pw), b16), ((mbs, ny, sub, pw), b16),
        ((pw, d), b16), ((mbs, sub, d), f32), ((mbs, sub, d), b16), (rows_shape, b16),
        ((length, pw), b16), ((mbs, length, 3 * pw), b16), (rows_shape, b16), (rows_shape, b16),
        ((experts, d), f32), ((8, d), f32),
        dense(sc), dense(ac), ((n, d), f32), dense(sc), dense(ac), ((n, d), f32),
        dense(sc), dense(ac), ((ny, n, pw), f32),
        ((width, sc), f32), ((width, ac), f32), ((n, pw), f32), ((nx, n, pw), f32),
    )
    by_m = lambda c: flags((mbs, c))

    names = ("mid", "n2", "rows", "q", "k", "v", "att", "rows2", "sgu", "shid", "shw")
    by_layer = [g, fwd["small"], fwd["place"], fwd["place_t"], fwd["tok"] if layer == 0 else fwd["y"]]
    by_layer += [fwd[name] for name in names]
    order = [4, 0, 1, *range(5, 16), 2, 3]
    resident = tuple((by_layer[c].shape[1:], by_layer[c].dtype) for c in order)
    outs = pl.pallas_call(
        functools.partial(
            backward_kernel,
            (layer, nx, ny, mbs, sub, width, pw, heads, features, experts, cap, f, *BWD_SKEW)),
        out_shape=(
            jax.ShapeDtypeStruct((mbs, sub, d), b16),
            jax.ShapeDtypeStruct((experts, width, 2 * f), f32),
            jax.ShapeDtypeStruct((experts, width, f), f32),
            jax.ShapeDtypeStruct((width, ac), f32),
            jax.ShapeDtypeStruct((width, sc), f32),
            jax.ShapeDtypeStruct((n, pw), f32),
        ),
        in_specs=[hbm] * 16 + [vm] * 4 + [hbm] * (7 + len(grads)),
        out_specs=(vm,) + (hbm,) * 5,
        scratch_shapes=[pltpu.VMEM(*v) for v in scratch + resident] + [
            flags((2,)), by_m(ny), by_m(ny), by_m(nx), by_m(nx), by_m(nx), by_m(nx), by_m(nx), by_m(nx),
            by_m(nx), by_m(nx), by_m(ny), by_m(ny), by_m(nx), by_m(nx), by_m(nx), by_m(nx),
            by_m(experts), by_m(experts), by_m(experts), by_m(experts),
            flags((experts,)), flags((experts,)), flags((experts,)), flags((experts,)),
            flags((3,)), flags((3,)), flags((3, ny)), flags((3, ny)), flags((nx,)), flags((nx,)),
            flags((3,)), flags((2, 2)), flags((3,)), flags((16,)), pltpu.SemaphoreType.REGULAR,
        ],
        input_output_aliases={27 + i: 1 + i for i in range(len(grads))},
        compiler_params=params(ids),
        cost_estimate=pl.CostEstimate(flops=10**10, bytes_accessed=6 * 10**7, transcendentals=10**6),
        name="backward",
    )(
        *by_layer, watt, cos, sin, rot,
        *(fwd[name] for name in ("slots", "gu", "hid")), *win, *wdt, *grads,
    )
    return outs[0], outs[1:]


BWD_SKEW = (1, 1)


def fast_device(block_input, output_grad, attention_gain, attention_in, attention_out, feed_gain,
                router_weight, expert_in, expert_down, shared_in, shared_down, routes):
    s = lax.axis_index("section")
    ny = lax.axis_size("gy")
    nx = lax.axis_size("gx")
    mbs = block_input.shape[0] // 2
    width = block_input.shape[2]
    features = width * ny
    experts = expert_in.shape[1]
    f = expert_in.shape[-1]
    pw = lanes_up(width + 2 * experts)
    tokens = routes.shape[2]
    cap = 5 * tokens // (2 * experts)
    length = tokens // ny
    heads = attention_in.shape[-1] // DH
    dims = (width, pw, experts, cap)

    att_block = jnp.concatenate([
        pad_to(attention_in[0], 2, pw).reshape(width, 3 * pw), pad_to(attention_out[0].T, 1, pw)], 1)
    sh_block = jnp.concatenate([shared_in[0].reshape(width, 2 * f), shared_down[0].T], 1)
    small = jnp.concatenate([
        router_weight[0].T.astype(jnp.float32), feed_gain, attention_gain, jnp.zeros((6, width), jnp.float32)], 0)
    tin = lax.dynamic_slice_in_dim(jnp.stack([block_input, output_grad]), s * mbs, mbs, 1)
    tin = pad_to(tin, 3, pw)
    small = pad_to(small, 1, pw)
    win = expert_in[0].reshape(experts, width, 2 * f)
    win = (win, pass_section(win))
    wdt = expert_down[0].transpose(0, 2, 1)
    wdt = (wdt, pass_section(wdt))
    pairs = jnp.swapaxes(routes[0], 1, 2)
    half = DH // 2
    freq = 10000.0 ** (-jnp.arange(half, dtype=jnp.float32) / half)
    ang = jnp.arange(length, dtype=jnp.float32)[:, None] * freq[None]
    lanes = jnp.tile(ang, (1, 2 * heads))
    cos = pad_to(jnp.cos(lanes), 1, pw)
    sin = pad_to(jnp.sin(lanes), 1, pw)
    rot = pad_to(pad_to(rot_columns(jnp.eye(heads * DH, dtype=jnp.float32)), 0, pw), 1, pw).astype(jnp.bfloat16)

    fwd = forward(tin, small, att_block, sh_block, pairs, cos, sin, rot, win, wdt, dims, heads, features, 0)
    outs, watt = fwd["y"], (fwd["watt0"], fwd["watt1"])
    g, gouts, grads = fwd["tok"], [None, None], ()
    for l in (1, 0):
        gouts[l], grads = backward(l, g, fwd, watt[l], cos, sin, rot, win, wdt, grads, dims, heads, features, 1 + l)
        g = gouts[l][None]

    both = leave(jnp.stack([outs[0], gouts[0]]), jnp.stack([outs[1], gouts[1]]), pw, 3)[..., :width]
    win_g, wdt_g, att_g, sh_g, small_g = grads
    hd = heads * DH
    return (
        both[0][None],
        both[1][None],
        small_g[experts + 1 : experts + 2, :width],
        att_g[:, : 3 * pw].reshape(width, 3, pw)[..., :hd][None],
        att_g[:, 3 * pw : 3 * pw + hd].T[None],
        small_g[experts : experts + 1, :width],
        small_g[:experts, :width].T[None],
        win_g.reshape(experts, width, 2, f)[None],
        wdt_g.transpose(0, 2, 1)[None],
        sh_g[:, : 2 * f].reshape(width, 2, f)[None],
        sh_g[:, 2 * f :].T[None],
    )


def solution(mesh):
    in_specs = (
        P(None, "gx", "gy"),
        P(None, "gx", "gy"),
        P("section", "gy"),
        P("section", "gy", None, "gx"),
        P("section", "gx", "gy"),
        P("section", "gy"),
        P("section", "gy", None),
        P("section", None, "gy", None, "gx"),
        P("section", None, "gx", "gy"),
        P("section", "gy", None, "gx"),
        P("section", "gx", "gy"),
        P("section", None, None, None),
    )
    out_specs = (
        P("section", None, "gx", "gy"),
        P("section", None, "gx", "gy"),
        P("section", "gy"),
        P("section", "gy", None, "gx"),
        P("section", "gx", "gy"),
        P("section", "gy"),
        P("section", "gy", None),
        P("section", None, "gy", None, "gx"),
        P("section", None, "gx", "gy"),
        P("section", "gy", None, "gx"),
        P("section", "gx", "gy"),
    )
    fast = mesh.shape["gx"] == mesh.shape["gy"]
    return jax.shard_map(
        fast_device if fast else on_device, mesh=mesh, in_specs=in_specs, out_specs=out_specs, check_vma=False
    )
```

```python
import functools

import jax
import jax.numpy as jnp
from jax import lax
from jax.experimental import pallas as pl
from jax.experimental.pallas import tpu as pltpu
from jax.sharding import PartitionSpec as P

DH = 64


epsilon = 1e-06
highest = lax.Precision.HIGHEST


def from_partner(array, axis, apart):
    return lax.ppermute(array, axis, [(i, i ^ 1 << apart) for i in range(lax.axis_size(axis))])


def token_rows(values):
    return lax.all_gather(values, "gx", axis=0, tiled=True)


def output_rows(values):
    return lax.psum_scatter(values, "gx", scatter_dimension=0, tiled=True)


def width_sum(values):
    return lax.psum(values, "gy")


def pass_section(values):
    return from_partner(values, "section", 0)


def sequence_sums(values):
    return lax.psum_scatter(values, "gy", scatter_dimension=0, tiled=True)


def sequence_rows(values):
    return lax.all_gather(values, "gy", axis=0, tiled=True)


def gather_hidden(hidden, shared_hidden):
    return (
        lax.all_gather(hidden, "gy", axis=0, tiled=True),
        lax.all_gather(shared_hidden, "gy", axis=0, tiled=True),
    )


def rope_turn(values, positions, turn_sign):
    half_size = values.shape[-1] // 2
    frequency = 10000.0 ** (-jnp.arange(half_size, dtype=jnp.float32) / half_size)
    angles = positions[:, None] * frequency[None, :]
    cosine = jnp.cos(angles)[:, None, :]
    sine_part = turn_sign * jnp.sin(angles)[:, None, :]
    first_half = values[..., :half_size]
    second_half = values[..., half_size:]
    return jnp.concatenate(
        [
            first_half * cosine - second_half * sine_part,
            first_half * sine_part + second_half * cosine,
        ],
        axis=-1,
    )


def norm_forward(stream, gain):
    full_width = stream.shape[1] * lax.axis_size("gy")
    square_sum = width_sum(jnp.sum(stream * stream, axis=1))
    inverse_rms = lax.rsqrt(square_sum / full_width + epsilon)
    return ((stream * inverse_rms[:, None] * gain[None, :]).astype(jnp.bfloat16), inverse_rms)


def norm_backward(stream, inverse_rms, gain, grad_normed):
    full_width = stream.shape[1] * lax.axis_size("gy")
    scaled = grad_normed * gain[None, :]
    inner_sum = width_sum(jnp.sum(scaled * stream, axis=1))
    cubed = inverse_rms * inverse_rms * inverse_rms
    grad_stream = inverse_rms[:, None] * scaled - stream * (cubed * inner_sum / full_width)[:, None]
    grad_gain = jnp.sum(grad_normed * stream * inverse_rms[:, None], axis=0)
    return (grad_stream, grad_gain)


def slot_table(route_ids, experts, capacity):
    flat_ids = route_ids.reshape(-1)
    assigned = (flat_ids[:, None] == jnp.arange(experts, dtype=jnp.int32)[None, :]).astype(
        jnp.int32
    )
    earlier = jnp.cumsum(assigned, axis=0) - assigned
    places = flat_ids * capacity + jnp.sum(earlier * assigned, axis=1)
    owners = jnp.arange(flat_ids.shape[0], dtype=jnp.int32) // 2
    slot_token = jnp.zeros((experts * capacity,), jnp.int32).at[places].set(owners)
    slot_valid = jnp.zeros((experts * capacity,), jnp.int32).at[places].set(jnp.ones_like(owners))
    return (places.reshape(-1, 2), slot_token, slot_valid)


def expert_act(gate_up, logits):
    half_size = gate_up.shape[1] // 2
    return (
        jax.nn.silu(gate_up[:, :half_size])
        * gate_up[:, half_size:]
        * jax.nn.sigmoid(logits)[:, None]
    )


def shared_act(gate_up):
    half_size = gate_up.shape[1] // 2
    return jax.nn.silu(gate_up[:, :half_size]) * gate_up[:, half_size:]


def causal_scores(queries, keys_part):
    score_scale = queries.shape[-1] ** (-0.5)
    scores = (
        jnp.einsum("qhd,khd->hqk", queries, keys_part, preferred_element_type=jnp.float32)
        * score_scale
    )
    length = queries.shape[0]
    causal = jnp.arange(length)[:, None] >= jnp.arange(length)[None, :]
    return jnp.where(causal[None], scores, -1e30)


def attend_forward(queries, keys_part, values_part):
    scores = causal_scores(queries, keys_part)
    row_max = jnp.max(scores, axis=-1, keepdims=True)
    exponent = jnp.exp(scores - row_max)
    row_total = jnp.sum(exponent, axis=-1, keepdims=True)
    probabilities = (exponent / row_total).astype(jnp.bfloat16)
    attended = jnp.einsum(
        "hqk,khd->qhd", probabilities, values_part, preferred_element_type=jnp.float32
    )
    return (attended, row_max + jnp.log(row_total))


def attend_backward(queries, keys_part, values_part, log_total, grad_attended):
    score_scale = queries.shape[-1] ** (-0.5)
    probabilities = jnp.exp(causal_scores(queries, keys_part) - log_total)
    grad_values = jnp.einsum(
        "hqk,qhd->khd",
        probabilities.astype(jnp.bfloat16),
        grad_attended,
        preferred_element_type=jnp.float32,
    )
    grad_probs = jnp.einsum(
        "qhd,khd->hqk", grad_attended, values_part, preferred_element_type=jnp.float32
    )
    grad_scores = (
        probabilities * (grad_probs - jnp.sum(grad_probs * probabilities, axis=-1, keepdims=True))
    ).astype(jnp.bfloat16)
    grad_queries = (
        jnp.einsum("hqk,khd->qhd", grad_scores, keys_part, preferred_element_type=jnp.float32)
        * score_scale
    )
    grad_keys = (
        jnp.einsum("hqk,qhd->khd", grad_scores, queries, preferred_element_type=jnp.float32)
        * score_scale
    )
    return (grad_queries, grad_keys, grad_values)


def layer_forward(stream, weights, route_ids):
    (
        attention_gain,
        attention_in,
        attention_out,
        feed_gain,
        router_weight,
        expert_in,
        expert_down,
        shared_in,
        shared_down,
    ) = weights
    local_width = stream.shape[1]
    experts = expert_in.shape[0]
    normed, inverse_first = norm_forward(stream, attention_gain)
    rows_first = token_rows(normed)
    tokens = rows_first.shape[0]
    capacity = 5 * tokens // (2 * experts)
    slot_count = experts * capacity
    projected = sequence_sums(
        jnp.dot(
            rows_first, attention_in.reshape(local_width, -1), preferred_element_type=jnp.float32
        )
    )
    length = projected.shape[0]
    projected = projected.reshape(length, 3, -1, DH)
    positions = jnp.arange(length, dtype=jnp.float32)
    queries = rope_turn(projected[:, 0], positions, 1.0).astype(jnp.bfloat16)
    keys_part = rope_turn(projected[:, 1], positions, 1.0).astype(jnp.bfloat16)
    values_part = projected[:, 2].astype(jnp.bfloat16)
    attended, log_total = attend_forward(queries, keys_part, values_part)
    attended_rows = sequence_rows(attended.astype(jnp.bfloat16).reshape(length, -1))
    middle = stream + output_rows(
        jnp.dot(attended_rows, attention_out, preferred_element_type=jnp.float32)
    )
    normed_feed, inverse_second = norm_forward(middle, feed_gain)
    rows_second = token_rows(normed_feed)
    route_slot, slot_token, slot_valid = slot_table(route_ids, experts, capacity)
    grouped = (rows_second[slot_token] * slot_valid[:, None].astype(jnp.bfloat16)).reshape(
        experts, capacity, local_width
    )
    expert_part = jnp.einsum(
        "ecd,edf->ecf",
        grouped,
        expert_in.reshape(experts, local_width, -1),
        preferred_element_type=jnp.float32,
    )
    router_part = jnp.einsum(
        "ecd,de->ec", grouped, router_weight, preferred_element_type=jnp.float32
    )
    shared_part = jnp.dot(
        rows_second, shared_in.reshape(local_width, -1), preferred_element_type=jnp.float32
    )
    expert_gu, router_logit, shared_gu = (
        lax.psum_scatter(
            expert_part.reshape(slot_count, -1), "gy", scatter_dimension=0, tiled=True
        ),
        lax.psum_scatter(router_part.reshape(slot_count), "gy", scatter_dimension=0, tiled=True),
        lax.psum_scatter(shared_part, "gy", scatter_dimension=0, tiled=True),
    )
    hidden_rows, shared_rows = gather_hidden(
        expert_act(expert_gu, router_logit).astype(jnp.bfloat16),
        shared_act(shared_gu).astype(jnp.bfloat16),
    )
    expert_result = jnp.einsum(
        "ecf,efd->ecd",
        hidden_rows.reshape(experts, capacity, -1),
        expert_down,
        preferred_element_type=jnp.float32,
    ).reshape(slot_count, local_width)
    branch = (
        expert_result[route_slot[:, 0]]
        + expert_result[route_slot[:, 1]]
        + jnp.dot(shared_rows, shared_down, preferred_element_type=jnp.float32)
    )
    result = middle + output_rows(branch)
    kept_items = (
        stream,
        inverse_first,
        rows_first,
        queries,
        keys_part,
        values_part,
        log_total,
        attended_rows,
        middle,
        inverse_second,
        rows_second,
        expert_gu,
        router_logit,
        shared_gu,
    )
    return (result, kept_items)


def layer_backward(grad_out, kept_items, weights, route_ids):
    (
        attention_gain,
        attention_in,
        attention_out,
        feed_gain,
        router_weight,
        expert_in,
        expert_down,
        shared_in,
        shared_down,
    ) = weights
    (
        stream,
        inverse_first,
        rows_first,
        queries,
        keys_part,
        values_part,
        log_total,
        attended_rows,
        middle,
        inverse_second,
        rows_second,
        expert_gu,
        router_logit,
        shared_gu,
    ) = kept_items[:14]
    local_width = stream.shape[1]
    experts = expert_in.shape[0]
    tokens = rows_second.shape[0]
    capacity = 5 * tokens // (2 * experts)
    slot_count = experts * capacity
    hidden_rows, shared_rows = gather_hidden(
        expert_act(expert_gu, router_logit).astype(jnp.bfloat16),
        shared_act(shared_gu).astype(jnp.bfloat16),
    )
    route_slot, slot_token, slot_valid = slot_table(route_ids, experts, capacity)
    valid_rows = slot_valid[:, None].astype(jnp.bfloat16)
    grouped = (rows_second[slot_token] * valid_rows).reshape(experts, capacity, local_width)
    grad_rows = token_rows(grad_out.astype(jnp.bfloat16))
    slot_grad = (grad_rows[slot_token] * valid_rows).reshape(experts, capacity, local_width)
    down_grad = jnp.einsum(
        "ecf,ecd->efd",
        hidden_rows.reshape(experts, capacity, -1),
        slot_grad,
        preferred_element_type=jnp.float32,
    )
    shared_down_grad = jnp.einsum(
        "tf,td->fd", shared_rows, grad_rows, preferred_element_type=jnp.float32
    )
    hidden_part = jnp.einsum(
        "ecd,efd->ecf", slot_grad, expert_down, preferred_element_type=jnp.float32
    ).reshape(slot_count, -1)
    shared_part = jnp.einsum(
        "td,fd->tf", grad_rows, shared_down, preferred_element_type=jnp.float32
    )
    grad_hidden, grad_shared = (
        lax.psum_scatter(
            hidden_part.astype(jnp.bfloat16), "gy", scatter_dimension=0, tiled=True
        ).astype(jnp.float32),
        lax.psum_scatter(
            shared_part.astype(jnp.bfloat16), "gy", scatter_dimension=0, tiled=True
        ).astype(jnp.float32),
    )
    unused_expert, expert_back = jax.vjp(expert_act, expert_gu, router_logit)
    grad_gu, grad_logit = expert_back(grad_hidden)
    unused_shared, shared_back = jax.vjp(shared_act, shared_gu)
    (grad_shared_gu,) = shared_back(grad_shared)
    gu_rows, shared_gu_rows = (
        lax.all_gather(grad_gu.astype(jnp.bfloat16), "gy", axis=0, tiled=True),
        lax.all_gather(grad_shared_gu.astype(jnp.bfloat16), "gy", axis=0, tiled=True),
    )
    logit_rows = lax.all_gather(grad_logit, "gy", axis=0, tiled=True).reshape(experts, capacity)
    gu_grouped = gu_rows.reshape(experts, capacity, -1)
    in_grad = jnp.einsum("ecd,ecf->edf", grouped, gu_grouped, preferred_element_type=jnp.float32)
    router_grad = jnp.einsum(
        "ecd,ec->de", grouped.astype(jnp.float32), logit_rows, precision=highest
    )
    shared_in_grad = jnp.einsum(
        "td,tf->df", rows_second, shared_gu_rows, preferred_element_type=jnp.float32
    )
    slot_back = jnp.einsum(
        "ecf,edf->ecd",
        gu_grouped,
        expert_in.reshape(experts, local_width, -1),
        preferred_element_type=jnp.float32,
    )
    slot_back = slot_back + logit_rows[:, :, None] * router_weight.T.astype(jnp.float32)[:, None, :]
    slot_back = slot_back.reshape(slot_count, local_width)
    rows_back = (
        slot_back[route_slot[:, 0]]
        + slot_back[route_slot[:, 1]]
        + jnp.einsum(
            "tf,df->td",
            shared_gu_rows,
            shared_in.reshape(local_width, -1),
            preferred_element_type=jnp.float32,
        )
    )
    grad_middle_norm, feed_gain_grad = norm_backward(
        middle, inverse_second, feed_gain, output_rows(rows_back)
    )
    grad_middle = grad_out + grad_middle_norm
    middle_rows = token_rows(grad_middle.astype(jnp.bfloat16))
    out_weight_grad = jnp.einsum(
        "tf,td->fd", attended_rows, middle_rows, preferred_element_type=jnp.float32
    )
    grad_attended = sequence_sums(
        jnp.einsum("td,fd->tf", middle_rows, attention_out, preferred_element_type=jnp.float32)
    )
    length = grad_attended.shape[0]
    positions = jnp.arange(length, dtype=jnp.float32)
    grad_queries, grad_keys, grad_values = attend_backward(
        queries,
        keys_part,
        values_part,
        log_total,
        grad_attended.astype(jnp.bfloat16).reshape(queries.shape),
    )
    grad_projected = jnp.stack(
        [
            rope_turn(grad_queries, positions, -1.0),
            rope_turn(grad_keys, positions, -1.0),
            grad_values,
        ],
        axis=1,
    )
    grad_projected = grad_projected.astype(jnp.bfloat16).reshape(length, -1)
    projected_rows = sequence_rows(grad_projected)
    in_weight_grad = jnp.einsum(
        "td,tf->df", rows_first, projected_rows, preferred_element_type=jnp.float32
    )
    grad_normed = output_rows(
        jnp.einsum(
            "tf,df->td",
            projected_rows,
            attention_in.reshape(local_width, -1),
            preferred_element_type=jnp.float32,
        )
    )
    grad_stream_norm, attention_gain_grad = norm_backward(
        stream, inverse_first, attention_gain, grad_normed
    )
    layer_grads = (
        attention_gain_grad,
        in_weight_grad.reshape(attention_in.shape),
        out_weight_grad,
        feed_gain_grad,
        router_grad,
        in_grad.reshape(expert_in.shape),
        down_grad,
        shared_in_grad.reshape(shared_in.shape),
        shared_down_grad,
    )
    return (grad_middle + grad_stream_norm, layer_grads)


def put_item(buffer, value, batch_index, is_valid):
    current = lax.dynamic_index_in_dim(buffer, batch_index, 0, keepdims=False)
    return lax.dynamic_update_index_in_dim(
        buffer, jnp.where(is_valid, value, current), batch_index, 0
    )


def on_device(
    block_input,
    output_grad,
    attention_gain,
    attention_in,
    attention_out,
    feed_gain,
    router_weight,
    expert_in,
    expert_down,
    shared_in,
    shared_down,
    routes,
):
    section_index = lax.axis_index("section")
    batches = block_input.shape[0]
    weights = tuple(
        (
            member[0]
            for member in (
                attention_gain,
                attention_in,
                attention_out,
                feed_gain,
                router_weight,
                expert_in,
                expert_down,
                shared_in,
                shared_down,
            )
        )
    )
    route_table = routes[0]
    outputs = jnp.zeros(block_input.shape, jnp.bfloat16)
    received = jnp.zeros(block_input.shape[1:], jnp.bfloat16)
    stored = None
    for tick_step in range(batches + 1):
        micro_index = tick_step - section_index
        is_valid = (micro_index >= 0) & (micro_index < batches)
        batch_index = jnp.clip(micro_index, 0, batches - 1)
        fresh_input = lax.dynamic_index_in_dim(block_input, batch_index, 0, keepdims=False)
        incoming = jnp.where(section_index == 0, fresh_input, received).astype(jnp.float32)
        route_ids = lax.dynamic_index_in_dim(route_table, batch_index, 0, keepdims=False)
        result, kept_items = layer_forward(incoming, weights, route_ids)
        result_low = result.astype(jnp.bfloat16)
        outputs = put_item(outputs, result_low, batch_index, is_valid)
        if stored is None:
            stored = tuple(
                (jnp.zeros((batches,) + member.shape, member.dtype) for member in kept_items)
            )
        stored = tuple(
            (
                put_item(buffer, member, batch_index, is_valid)
                for buffer, member in zip(stored, kept_items)
            )
        )
        if tick_step < batches:
            received = pass_section(result_low)
    grads_in = jnp.zeros(block_input.shape, jnp.bfloat16)
    received = jnp.zeros(block_input.shape[1:], jnp.bfloat16)
    totals = tuple((jnp.zeros(member.shape, jnp.float32) for member in weights))
    for tick_step in range(batches + 1):
        micro_index = batches - tick_step - section_index
        is_valid = (micro_index >= 0) & (micro_index < batches)
        batch_index = jnp.clip(micro_index, 0, batches - 1)
        given_grad = lax.dynamic_index_in_dim(output_grad, batch_index, 0, keepdims=False)
        incoming = jnp.where(section_index == 1, given_grad, received).astype(jnp.float32)
        kept_items = tuple(
            (lax.dynamic_index_in_dim(buffer, batch_index, 0, keepdims=False) for buffer in stored)
        )
        route_ids = lax.dynamic_index_in_dim(route_table, batch_index, 0, keepdims=False)
        grad_input, layer_grads = layer_backward(incoming, kept_items, weights, route_ids)
        grad_low = grad_input.astype(jnp.bfloat16)
        grads_in = put_item(grads_in, grad_low, batch_index, is_valid)
        totals = tuple(
            (total + jnp.where(is_valid, member, 0.0) for total, member in zip(totals, layer_grads))
        )
        if tick_step < batches:
            received = pass_section(grad_low)
    gain_first, gain_second, router_total = lax.psum((totals[0], totals[3], totals[4]), "gx")
    return (
        outputs[None],
        grads_in[None],
        gain_first[None],
        totals[1][None],
        totals[2][None],
        gain_second[None],
        router_total[None],
        totals[5][None],
        totals[6][None],
        totals[7][None],
        totals[8][None],
    )


def lanes_up(n):
    return -(-n // 128) * 128


def rot_columns(w):
    shape = w.shape
    w = w.reshape(shape[:-1] + (-1, 2, DH // 2))
    w = jnp.stack([-w[..., 1, :], w[..., 0, :]], axis=-2)
    return w.reshape(shape)


def pad_to(v, axis, n):
    pads = [(0, 0)] * v.ndim
    pads[axis] = (0, n - v.shape[axis])
    return jnp.pad(v, pads)


def mm(a, b, dims=((1,), (0,))):
    return lax.dot_general(a, b, (dims, ((), ())), preferred_element_type=jnp.float32)


def bf(v):
    return v.astype(jnp.bfloat16)


def head_mask(pw, h):
    lane = lax.broadcasted_iota(jnp.int32, (1, pw), 1)
    return (lane >= h * DH) & (lane < (h + 1) * DH)


def rms(x, features):
    return lax.rsqrt(jnp.sum(x * x, axis=1, keepdims=True) / features + epsilon)


def norm_back(x, inv, gain, d, features):
    u = d * gain
    inner = jnp.sum(u * x, axis=1, keepdims=True) / features
    dx = inv * u - x * (inv * inv * inv * inner)
    return dx, jnp.sum(d * x * inv, axis=0, keepdims=True)


def probs_of(q, k):
    s = mm(q, k, ((1,), (1,))) * DH ** -0.5
    n = s.shape[0]
    causal = lax.broadcasted_iota(jnp.int32, (n, n), 0) >= lax.broadcasted_iota(jnp.int32, (n, n), 1)
    s = jnp.where(causal, s, -1e30)
    e = jnp.exp(s - jnp.max(s, axis=1, keepdims=True))
    return e / jnp.sum(e, axis=1, keepdims=True)


def act_back(gate, up, dh, s):
    sg = jax.nn.sigmoid(gate)
    silu = gate * sg
    if s is None:
        return dh * up * (sg * (1.0 + gate * (1.0 - sg))), dh * silu, None
    dr = jnp.sum(dh * silu * up, axis=-1, keepdims=True) * s * (1.0 - s)
    ds = dh * s
    return ds * up * (sg * (1.0 + gate * (1.0 - sg))), ds * silu, dr


MESH = pl.DeviceIdType.MESH
VMEM_BYTES = 62 * 2**20


def remote(src, dst, send, recv, target):
    return pltpu.make_async_remote_copy(
        src_ref=src, dst_ref=dst, send_sem=send, recv_sem=recv, device_id=target, device_id_type=MESH
    )


def router_column(rows, e, width, experts):
    lane = lax.broadcasted_iota(jnp.int32, rows.shape, rows.ndim - 1)
    mask = (lane == width + e) | (lane == width + experts + e)
    return jnp.sum(jnp.where(mask, rows.astype(jnp.float32), 0.0), axis=-1, keepdims=True)


class Position:
    def __init__(self, nx, ny):
        self.s = lax.axis_index("section")
        self.a = lax.axis_index("gx")
        self.b = lax.axis_index("gy")
        self.nx, self.ny = nx, ny
        self.n = nx * ny
        self.me = self.a * ny + self.b

    def device(self, index):
        return (self.s, index // self.ny, lax.rem(index, self.ny))

    def others(self, do):
        def step(i, c):
            index = lax.rem(self.me + i, self.n)
            do(index, index // self.ny, lax.rem(index, self.ny))
            return c

        lax.fori_loop(1, self.n, step, 0)

    def peers(self, do):
        for i in range(1, self.nx):
            do(lax.rem(self.a + i, self.nx))

    def line(self, do):
        for i in range(1, self.ny):
            do(lax.rem(self.b + i, self.ny))


def greet_section(pos):
    barrier = pltpu.get_barrier_semaphore()

    def one(index, ai, bi):
        pl.semaphore_signal(barrier, inc=1, device_id=(pos.s, ai, bi), device_id_type=MESH)

    pos.others(one)
    return barrier


def flags(count):
    return pltpu.SemaphoreType.DMA(count)


class Share:
    def __init__(self, pos, layer, block, full, sems):
        self.pos, self.layer, self.block, self.full = pos, layer, block, full
        self.sems = sems
        self.source = pos.s == layer

    def along(self, way, h):
        pos = self.pos
        j = pos.b - way * h
        to = pos.b + way
        real = (j >= 0) & (j < pos.ny) & (to >= 0) & (to < pos.ny)
        j = jnp.clip(j, 0, pos.ny - 1)
        src = self.block if h == 0 else self.full.at[j]
        copy = remote(src, self.full.at[j], self.sems[0].at[(way + 1) // 2, h], self.sems[1].at[j], (pos.s, pos.a, to))
        return real, j, copy

    def across(self, src, slot):
        pos = self.pos
        return remote(src, self.full.at[slot], self.sems[2].at[slot], self.sems[3].at[slot], (1 - pos.s, pos.a, pos.b))

    def start(self):
        b = self.pos.b

        @pl.when(self.source)
        def _():
            self.full[b] = self.block[...]
            for way in (-1, 1):
                real, _, copy = self.along(way, 0)
                pl.when(real)(copy.start)
            self.across(self.block, b).start()

    def hop(self, h):
        pos = self.pos

        @pl.when(self.source)
        def _():
            for way in (-1, 1):
                j = pos.b - way * h

                @pl.when((j >= 0) & (j < pos.ny))
                def _():
                    real, jc, copy = self.along(way, h)
                    copy.wait_recv()
                    pl.when(real)(copy.start)
                    self.across(self.full.at[jc], jc).start()

    def finish(self):
        pos = self.pos

        @pl.when(self.source)
        def _():
            for h in range(pos.ny - 1):
                for way in (-1, 1):
                    real, _, copy = self.along(way, h)
                    pl.when(real)(copy.wait_send)
            for j in range(pos.ny):
                self.across(self.block, j).wait_send()

        @pl.when(jnp.logical_not(self.source))
        def _():
            for j in range(pos.ny):
                self.across(self.full.at[j], j).wait_recv()


def share_sems(ny):
    return [flags((2, ny)), flags((ny,)), flags((ny,)), flags((ny,))]


def params(ids):
    return pltpu.CompilerParams(collective_id=ids, has_side_effects=True, vmem_limit_bytes=VMEM_BYTES)


def greet_all(pos):
    barrier = pltpu.get_barrier_semaphore()
    total = 2 * pos.n
    mine = pos.s * pos.n + pos.me

    def one(i, c):
        index = lax.rem(mine + i, total)
        rest = lax.rem(index, pos.n)
        pl.semaphore_signal(
            barrier, inc=1, device_id=(index // pos.n, rest // pos.ny, lax.rem(rest, pos.ny)), device_id_type=MESH)
        return c

    lax.fori_loop(1, total, one, 0)
    pl.semaphore_wait(barrier, total - 1)


def leave_kernel(cfg, pair0, pair1, out, buf, t_send, t_recv):
    nx, ny, mbs, sub, pw = cfg
    pos = Position(nx, ny)
    s, a, b = pos.s, pos.a, pos.b
    greet_all(pos)
    pairs = (pair0, pair1)

    def copy(l, j, s_slot, a_slot, seq):
        src = pairs[l].at[:, :, :, pl.ds(pl.multiple_of(j * pw, pw), pw)]
        return remote(src, buf.at[s_slot, a_slot], t_send.at[l, j], t_recv.at[s_slot, a_slot], (l, seq, j))

    for l in range(2):
        for j in range(ny):
            @pl.when((l != s) | (a != b) | (j != b))
            def _():
                copy(l, j, s, a, b).start()

        @pl.when((l == s) & (a == b))
        def _():
            buf[s, a] = pairs[l][:, :, :, pl.ds(pl.multiple_of(b * pw, pw), pw)]

    for so in range(2):
        for i in range(nx):
            @pl.when((so != s) | (a != b) | (i != a))
            def _():
                copy(0, 0, so, i, i).wait_recv()

            out[:, so * mbs : (so + 1) * mbs, i * sub : (i + 1) * sub, :] = buf[so, i]
    for l in range(2):
        for j in range(ny):
            @pl.when((l != s) | (a != b) | (j != b))
            def _():
                copy(l, j, s, a, b).wait_send()


def leave(pair0, pair1, pw, ids):
    nx, ny = lax.axis_size("gx"), lax.axis_size("gy")
    kinds, mbs, sub, d = pair0.shape
    vm = pl.BlockSpec(memory_space=pltpu.VMEM)
    return pl.pallas_call(
        functools.partial(leave_kernel, (nx, ny, mbs, sub, pw)),
        out_shape=jax.ShapeDtypeStruct((kinds, 2 * mbs, nx * sub, pw), jnp.bfloat16),
        in_specs=[vm] * 2,
        out_specs=vm,
        scratch_shapes=[
            pltpu.VMEM((2, nx, kinds, mbs, sub, pw), jnp.bfloat16),
            flags((2, ny)), flags((2, nx)),
        ],
        compiler_params=params(ids),
        name="leave",
    )(pair0, pair1)


def turn(t, cos, sin, rot, sign):
    hi = bf(t)
    lo = bf(t - hi.astype(jnp.float32))
    return bf(t * cos + sign * ((mm(hi, rot) + mm(lo, rot)) * sin))


def by_blocks(rows, full, cols, width, pw):
    total = None
    for j in range(full.shape[0]):
        part = mm(rows[:, j * pw : j * pw + width], full[j, :, cols])
        total = part if total is None else total + part
    return total


def forward_kernel(cfg, *refs):
    nx, ny, mbs, sub, width, pw, heads, features, experts, cap, f, sk, ak = cfg
    (tin, small_b, att_b, sh_b, routes, cos, sin, rot, win_a, win_b, wdt_a, wdt_b,
     tok_o, small_o, place_o, place_to, watt0_o, y_o, mid_o, n2_o, rows_o, q_o, k_o, v_o, att_o, slots_o, gu_o, hid_o, rows2_o, sgu_o, shid_o, shw_o, watt_o,
     y, mid, n2, rx, nsend, nall, proj, q, k, v, att, osend, orecv, rwx,
     xsend, xline, xall, nrows, pm, pt, slots, acc, gu, hid, eo, sgu, shid, ssend, srecv, rsend, rpeer, rline, rrecv,
     win, wdt, shw0, shw1, watt0, watt1, tbuf, tok, rts, place, place_t, sm0, sm1, small,
     n_send, n_recv, o_send, o_recv, x_send, x_recv, u_send, u_recv, t_send, t_recv, s_send, s_recv, g_send, g_recv, r_send, r_recv,
     rs_send, rs_recv, ag_send, ag_recv, wi_sem, wd_sem, g_sem, k_sem, i_send, i_recv, q_send, q_recv, *w_sems) = refs
    pos = Position(nx, ny)
    s, a, b, me = pos.s, pos.a, pos.b, pos.me
    slots_n = experts * cap
    tokens = nx * ny * sub
    d = ny * pw
    length = nx * sub
    half = experts // 2
    lane = lax.broadcasted_iota(jnp.int32, (1, pw), 1)
    shares = (
        Share(pos, 0, sh_b, shw0, w_sems[0:4]),
        Share(pos, 1, att_b, watt1, w_sems[4:8]),
        Share(pos, 1, sh_b, shw1, w_sems[8:12]),
    )
    entry_shares = (
        Share(pos, 0, small_b, sm0, w_sems[12:16]),
        Share(pos, 1, small_b, sm1, w_sems[16:20]),
        Share(pos, 0, att_b, watt0, w_sems[20:24]),
    )
    watts, shws = (watt0, watt1), (shw0, shw1)
    barrier = pltpu.get_barrier_semaphore()
    pos.peers(lambda ai: pl.semaphore_signal(barrier, inc=1, device_id=(s, ai, b), device_id_type=MESH))
    pos.line(lambda bi: pl.semaphore_signal(barrier, inc=1, device_id=(s, a, bi), device_id_type=MESH))
    pl.semaphore_signal(barrier, inc=1, device_id=(1 - s, a, b), device_id_type=MESH)
    for j in range(ny):
        @pl.when((a != b) | (b != j))
        def _():
            pl.semaphore_signal(barrier, inc=1, device_id=(s, b, j), device_id_type=MESH)

    def weight_copy(layer, e, which):
        own, oth, dst, sem = ((win_a, win_b, win, wi_sem), (wdt_a, wdt_b, wdt, wd_sem))[which]
        return own.at[e], oth.at[e], dst.at[e], sem.at[e]

    def start_weight(layer, e, which):
        own, oth, dst, sem = weight_copy(layer, e, which)

        @pl.when(s == layer)
        def _():
            pltpu.make_async_copy(own, dst, sem).start()

        @pl.when(s != layer)
        def _():
            pltpu.make_async_copy(oth, dst, sem).start()

    def wait_weight(layer, e, which):
        own, oth, dst, sem = weight_copy(layer, e, which)
        pltpu.make_async_copy(own, dst, sem).wait()

    def first_weights(e, c):
        start_weight(0, e, 0)
        start_weight(0, e, 1)
        return c

    lax.fori_loop(0, experts, first_weights, 0)

    @pl.when(a == b)
    def _():
        pl.semaphore_wait(barrier, nx - 1 + ny - 1 + 1 + nx - 1)

    @pl.when(a != b)
    def _():
        pl.semaphore_wait(barrier, nx - 1 + ny - 1 + 1 + nx)

    def tokens_copy(i, slot, seq):
        src = tin.at[:, :, pl.ds(pl.multiple_of(i * sub, sub), sub), :]
        return remote(src, tbuf.at[slot], i_send.at[i], i_recv.at[slot], (s, i, seq))

    def token_targets(do):
        for c in range(nx):
            i = lax.rem(a + c, nx)

            @pl.when((i != a) | (a != b))
            def _():
                do(tokens_copy(i, b, a))

    def routes_copy(src, slot):
        return remote(routes.at[pl.ds(src * mbs, mbs)], rts.at[slot], q_send, q_recv, (1 - s, a, b))

    token_targets(lambda copy: copy.start())
    routes_copy(1 - s, s).start()
    for share in entry_shares:
        share.start()
    rts[s] = routes[pl.ds(s * mbs, mbs)]

    @pl.when(a == b)
    def _():
        tbuf[b] = tin[:, :, pl.ds(pl.multiple_of(a * sub, sub), sub), :]

    routes_copy(0, 1 - s).wait()

    def places():
        t0 = lax.broadcasted_iota(jnp.int32, (tokens, tokens), 0)
        t1 = lax.broadcasted_iota(jnp.int32, (tokens, tokens), 1)
        before = bf((t1 < t0).astype(jnp.float32))
        after = bf((t0 < t1).astype(jnp.float32))
        er = lax.broadcasted_iota(jnp.int32, (experts, tokens), 0).astype(jnp.float32)
        ec = lax.broadcasted_iota(jnp.int32, (tokens, 128), 1).astype(jnp.float32)
        sub8 = lax.broadcasted_iota(jnp.int32, (128, tokens), 0)
        for l in range(2):
            for m in range(mbs):
                r = rts[l, m].astype(jnp.float32)
                rows = [r[c : c + 1] for c in range(2)]
                hot = [(row == er).astype(jnp.float32) for row in rows]
                count = mm(bf(hot[0] + hot[1]), after)
                cols = jnp.where(sub8 == 0, rows[0], jnp.where(sub8 == 1, rows[1], 0.0)).T
                cols = [cols[:, c : c + 1] for c in range(2)]
                hot_t = [(col == ec).astype(jnp.float32) for col in cols]
                count_t = mm(before, bf(hot_t[0] + hot_t[1]))
                for c in range(2):
                    rank = jnp.sum(hot[c] * count, axis=0, keepdims=True)
                    place[l, m, c : c + 1] = (rows[c] * cap + rank).astype(jnp.int32)
                    rank_t = jnp.sum(hot_t[c] * count_t, axis=1, keepdims=True)
                    place_t[l, m, :, c : c + 1] = (cols[c] * cap + rank_t).astype(jnp.int32)

    def tokens_ready():
        for j in range(ny):
            @pl.when((a != b) | (b != j))
            def _():
                tokens_copy(a, j, j).wait_recv()

            for kind in range(2):
                tok[kind, :, :, j * pw : (j + 1) * pw] = tbuf[j, kind]
        token_targets(lambda copy: copy.wait_send())

    def stream(l, m):
        return (tok[0, m] if l == 0 else y[0, m]).astype(jnp.float32)

    def copy_n(l, m, ai, slot):
        return remote(nsend.at[l, m], nall.at[l, m, slot], n_send.at[l, m, ai], n_recv.at[l, m, slot], (s, ai, b))

    def norm_first(l, m):
        xv = stream(l, m)
        nsend[l, m] = bf(xv * rms(xv, features) * small[l, experts + 1 : experts + 2])
        pos.peers(lambda ai: copy_n(l, m, ai, a).start())
        nall[l, m, a] = nsend[l, m]

    def copy_o(l, m, ai, slot):
        return remote(osend.at[l, m, ai], orecv.at[l, m, slot], o_send.at[l, m, ai], o_recv.at[l, m, slot], (s, ai, b))

    def attention(l, m):
        watt = watts[l]
        pos.peers(lambda ai: copy_n(l, m, ai, ai).wait())
        proj[...] = by_blocks(nall[l, m].reshape(length, d), watt, slice(0, 3 * pw), width, pw)
        v[l, m] = bf(proj[:, 2 * pw : 3 * pw])
        q[l, m] = turn(proj[:, :pw], cos[...], sin[...], rot[...], 1.0)
        k[l, m] = turn(proj[:, pw : 2 * pw], cos[...], sin[...], rot[...], 1.0)
        total = jnp.zeros((length, pw), jnp.float32)
        for h in range(heads):
            mask = head_mask(pw, h)
            p = probs_of(jnp.where(mask, q[l, m], 0), k[l, m])
            total = total + mm(bf(p), jnp.where(mask, v[l, m], 0))
        att[l, m] = bf(total)
        for j in range(ny):
            part = mm(att[l, m], watt[j, :, 3 * pw : 4 * pw], ((1,), (1,)))
            osend[l, m, :, :, j * pw : j * pw + width] = bf(part).reshape(nx, sub, width)
        pos.peers(lambda ai: copy_o(l, m, ai, a).start())
        orecv[l, m, a] = osend[l, m, a]

    def copy_x(l, m, bi, slot):
        return remote(xsend.at[l, m, bi], xline.at[l, m, slot], x_send.at[l, m, bi], x_recv.at[l, m, slot], (s, a, bi))

    def copy_w(l, m, ai, slot):
        return remote(xline.at[l, m], xall.at[l, m, :, slot], u_send.at[l, m, ai], u_recv.at[l, m, slot], (s, ai, b))

    def copy_t(l, m, ai, slot):
        return remote(n2.at[l, m], nrows.at[l, m, slot], t_send.at[l, m, ai], t_recv.at[l, m, slot], (s, ai, b))

    def norm_second(l, m):
        pos.peers(lambda ai: copy_o(l, m, ai, ai).wait())
        mv = stream(l, m)
        for ai in range(nx):
            mv = mv + orecv[l, m, ai].astype(jnp.float32)
        mid[l, m] = mv
        n2v = bf(mv * rms(mv, features) * small[l, experts : experts + 1])
        n2[l, m] = n2v
        rv = mm(n2v, rwx[l], ((1,), (1,)))
        hi = bf(rv)
        lo = bf(rv - hi.astype(jnp.float32))
        tail = jnp.where(lane < width + experts, hi, lo)
        for j in range(ny):
            xsend[l, m, j] = jnp.where(lane < width, n2v[:, j * pw : (j + 1) * pw], tail)
        pos.line(lambda bi: copy_x(l, m, bi, b).start())
        xline[l, m, b] = xsend[l, m, b]
        pos.peers(lambda ai: copy_t(l, m, ai, a).start())
        nrows[l, m, a] = n2[l, m]

    def spread(l, m):
        pos.line(lambda bi: copy_x(l, m, bi, bi).wait())
        pos.peers(lambda ai: copy_w(l, m, ai, a).start())
        xall[l, m, :, a] = xline[l, m]

    def dispatch(l, m):
        i0 = lax.broadcasted_iota(jnp.int32, (slots_n, tokens), 0)
        pm[...] = bf(((place[l, m, 0:1] == i0) | (place[l, m, 1:2] == i0)).astype(jnp.float32))
        pos.peers(lambda ai: copy_w(l, m, ai, ai).wait())
        slots[l, m] = bf(mm(pm[...], xall[l, m].reshape(tokens, pw))).reshape(experts, cap, pw)

    def shared_in_part(l, m):
        pos.peers(lambda ai: copy_t(l, m, ai, ai).wait())
        shw = shws[l]
        gu_s = by_blocks(nrows[l, m].reshape(length, d), shw, slice(0, 2 * f), width, pw)
        sgu[l, m] = bf(gu_s)
        gate = gu_s[:, :f]
        shid[l, m] = bf(gate * jax.nn.sigmoid(gate) * gu_s[:, f:])

    def copy_s(l, m, ai, slot):
        return remote(ssend.at[l, m, ai], srecv.at[l, m, slot], s_send.at[l, m, ai], s_recv.at[l, m, slot], (s, ai, b))

    def shared_out_part(l, m):
        for j in range(ny):
            part = mm(shid[l, m], shws[l][j, :, 2 * f :], ((1,), (1,)))
            ssend[l, m, :, :, j * pw : j * pw + width] = bf(part).reshape(nx, sub, width)
        pos.peers(lambda ai: copy_s(l, m, ai, a).start())
        srecv[l, m, a] = ssend[l, m, a]

    def copy_g(l, m, ai, slot):
        return remote(rsend.at[l, m, ai], rpeer.at[l, m, slot], g_send.at[l, m, ai], g_recv.at[l, m, slot], (s, ai, b))

    def copy_r(l, m, bi, slot):
        return remote(rline.at[l, m, bi], rrecv.at[l, m, slot], r_send.at[l, m, bi], r_recv.at[l, m, slot], (s, a, bi))

    def combine(l, m):
        i1 = lax.broadcasted_iota(jnp.int32, (tokens, slots_n), 1)
        pt[...] = bf(((place_t[l, m, :, 0:1] == i1) | (place_t[l, m, :, 1:2] == i1)).astype(jnp.float32))
        br = mm(pt[...], eo[m].reshape(slots_n, width))
        for ai in range(nx):
            rsend[l, m, ai, :, :, :width] = bf(br).reshape(ny, nx, sub, width)[:, ai]
        pos.peers(lambda ai: copy_g(l, m, ai, a).start())
        rpeer[l, m, a] = rsend[l, m, a]

    def combine_line(l, m):
        pos.peers(lambda ai: copy_g(l, m, ai, ai).wait())
        total = rpeer[l, m, 0].astype(jnp.float32)
        for ai in range(1, nx):
            total = total + rpeer[l, m, ai].astype(jnp.float32)
        rline[l, m] = bf(total)
        pos.line(lambda bi: copy_r(l, m, bi, b).start())
        rrecv[l, m, b] = rline[l, m, b]

    def layer_out(l, m):
        pos.peers(lambda ai: copy_s(l, m, ai, ai).wait())
        pos.line(lambda bi: copy_r(l, m, bi, bi).wait())
        total = mid[l, m]
        for ai in range(nx):
            total = total + srecv[l, m, ai].astype(jnp.float32)
        for j in range(ny):
            part = total[:, j * pw : (j + 1) * pw]
            part = part + jnp.where(lane < width, rrecv[l, m, j].astype(jnp.float32), 0.0)
            y[l, m, :, j * pw : (j + 1) * pw] = bf(part)

    first = (b == ny - 1, b == 0)
    last = (b == 0, b == ny - 1)
    up = (ny - 1 - b, b)
    down = (b, ny - 1 - b)
    lag = (sk + ak) * (ny - 1)
    apart = STAGE_STEPS
    gap = max(half - 1 + lag + 6 * apart + 1 - 2 * half, 0)
    starts = (0, half, 2 * half + gap, 3 * half + gap)
    steps = starts[3] + half + lag

    def unit(t, dd):
        early = (t >= 0) & (t < 2 * half)
        late = (t >= starts[2]) & (t < starts[2] + 2 * half)
        u = jnp.clip(jnp.where(t < starts[2], jnp.minimum(t, 2 * half - 1), t - gap), 0, 4 * half - 1)
        job = u // half
        return early | late, job // 2, lax.rem(job, 2), lax.rem(u, half) + dd * half

    def gu_copy(dd, l, m, e):
        to = b - 1 if dd == 0 else b + 1
        return remote(gu.at[l, m, e], gu.at[l, m, e], rs_send.at[l, m, e], rs_recv.at[l, m, e], (s, a, to))

    def hid_copy(dd, l, m, e):
        to = b + 1 if dd == 0 else b - 1
        return remote(hid.at[l, m, e], hid.at[l, m, e], ag_send.at[l, m, e], ag_recv.at[l, m, e], (s, a, to))

    def chain(i):
        reduce = [unit(i - sk * up[dd], dd) for dd in range(2)]
        spreads = [unit(i - sk * (ny - 1) - ak * down[dd], dd) for dd in range(2)]
        for dd in range(2):
            valid, l, m, e = reduce[dd]

            @pl.when(valid)
            def _():
                @pl.when(m == 0)
                def _():
                    wait_weight(0, e, 0)

                acc[dd] = mm(slots[l, m, e, :, :width], win[e])

                @pl.when((l == 0) & (m == 1))
                def _():
                    start_weight(1, e, 0)

        for dd in range(2):
            valid, l, m, e = reduce[dd]

            @pl.when(valid & first[dd])
            def _():
                gu[l, m, e] = bf(acc[dd])
                gu_copy(dd, l, m, e).start()

            @pl.when(valid & jnp.logical_not(first[dd] | last[dd]))
            def _():
                gu_copy(dd, l, m, e).wait_recv()
                gu[l, m, e] = bf(acc[dd] + gu[l, m, e].astype(jnp.float32))
                gu_copy(dd, l, m, e).start()

            @pl.when(valid & last[dd])
            def _():
                gu_copy(dd, l, m, e).wait_recv()
                total = acc[dd] + gu[l, m, e].astype(jnp.float32)
                r = router_column(slots[l, m, e], e, width, experts)
                gate = total[:, :f]
                hid[l, m, e] = bf(gate * jax.nn.sigmoid(gate) * total[:, f:] * jax.nn.sigmoid(r))
                hid_copy(dd, l, m, e).start()
                gu[l, m, e] = bf(total)
                pltpu.make_async_copy(gu.at[l, m, e], gu_o.at[l, m, e], g_sem.at[l, m, e]).start()

        for dd in range(2):
            valid, l, m, e = spreads[dd]

            @pl.when(valid & jnp.logical_not(last[dd]))
            def _():
                hid_copy(dd, l, m, e).wait_recv()

                @pl.when(jnp.logical_not(first[dd]))
                def _():
                    hid_copy(dd, l, m, e).start()

        for dd in range(2):
            valid, l, m, e = spreads[dd]

            @pl.when(valid)
            def _():
                @pl.when(m == 0)
                def _():
                    wait_weight(0, e, 1)

                eo[m, e] = bf(mm(hid[l, m, e], wdt[e], ((1,), (1,))))

                @pl.when((l == 0) & (m == 1))
                def _():
                    start_weight(1, e, 1)

    kept = [
        (mid, mid_o), (n2, n2_o), (nall, rows_o), (q, q_o), (k, k_o), (v, v_o), (att, att_o), (slots, slots_o),
        (hid, hid_o), (nrows, rows2_o), (sgu, sgu_o), (shid, shid_o), (y, y_o),
    ]
    stages = {}

    def at(step, do):
        stages.setdefault(step, []).append(do)

    def stage(do, l, m):
        return lambda: do(l, m)

    osend[...] = jnp.zeros_like(osend)
    ssend[...] = jnp.zeros_like(ssend)
    rwx[...] = jnp.zeros_like(rwx)
    for h in range(1, ny):
        for share in entry_shares:
            share.hop(h)
    for share in entry_shares[:2]:
        share.finish()
    tokens_ready()
    for l, full in enumerate((sm0, sm1)):
        for j in range(ny):
            small[l, :, j * pw : (j + 1) * pw] = full[j]
    for l in range(2):
        rwx[l, width : width + experts] = bf(small[l, :experts])
        rwx[l, width + experts : width + 2 * experts] = bf(small[l, :experts])
    norm_first(0, 0)
    norm_first(0, 1)
    places()
    entry_shares[2].finish()
    shares[0].start()
    shares[1].start()
    attention(0, 0)
    norm_second(0, 0)
    attention(0, 1)
    spread(0, 0)
    norm_second(0, 1)
    dispatch(0, 0)
    for h in range(1, ny):
        at(h - 1, lambda h=h: (shares[0].hop(h), shares[1].hop(h)))
    at(1, stage(spread, 0, 1))
    at(3, stage(dispatch, 0, 1))
    at(4, lambda: (shares[0].finish(), shares[1].finish()))
    at(5, stage(shared_in_part, 0, 0))
    at(6, stage(shared_out_part, 0, 0))
    at(half, stage(shared_in_part, 0, 1))
    at(half + 1, stage(shared_out_part, 0, 1))
    for m in range(2):
        done = starts[m] + half - 1 + lag
        for c, do in enumerate((combine, combine_line)):
            at(done + c * apart, stage(do, 0, m))
        at(done + 2 * apart, stage(layer_out, 0, m))
        for c, do in enumerate((norm_first, attention, norm_second, spread, dispatch)):
            at(done + (2 + c) * apart, stage(do, 1, m))
        at(starts[2 + m] + 2, stage(shared_in_part, 1, m))
        at(starts[2 + m] + 4, stage(shared_out_part, 1, m))
        done = starts[2 + m] + half - 1 + lag
        for c, do in enumerate((combine, combine_line, layer_out)):
            at(done + c * apart, stage(do, 1, m))
    at(half + lag, shares[2].start)
    for h in range(1, ny):
        at(half + lag + h, lambda h=h: shares[2].hop(h))
    at(half + lag + ny, shares[2].finish)

    def step(i, c):
        chain(i)
        for when in sorted(stages):
            if when < steps:
                @pl.when(i == when)
                def _():
                    for do in stages[when]:
                        do()

        return c

    lax.fori_loop(0, steps, step, 0)
    for when in sorted(stages):
        if when >= steps:
            for do in stages[when]:
                do()
    kept += [(shw0, shw_o.at[0]), (shw1, shw_o.at[1]), (watt1, watt_o), (watt0, watt0_o), (tok, tok_o), (small, small_o)]
    kept += [(place, place_o), (place_t, place_to)]
    saves = [pltpu.make_async_copy(src, dst, k_sem.at[i]) for i, (src, dst) in enumerate(kept)]
    for copy in saves:
        copy.start()

    def finish(index, c):
        l = index // (mbs * half)
        m = lax.rem(index // half, mbs)
        for dd in range(2):
            e = lax.rem(index, half) + dd * half

            @pl.when(jnp.logical_not(last[dd]))
            def _():
                gu_copy(dd, l, m, e).wait_send()

            @pl.when(jnp.logical_not(first[dd]))
            def _():
                hid_copy(dd, l, m, e).wait_send()

            @pl.when(last[dd])
            def _():
                pltpu.make_async_copy(gu.at[l, m, e], gu_o.at[l, m, e], g_sem.at[l, m, e]).wait()

        return c

    lax.fori_loop(0, 2 * mbs * half, finish, 0)
    for copy in saves:
        copy.wait()


def forward(tin, small_b, att_block, sh_block, routes, cos, sin, rot, win, wdt, dims, heads, features, ids):
    width, pw, experts, cap = dims
    nx, ny = lax.axis_size("gx"), lax.axis_size("gy")
    mbs, length = tin.shape[1:3]
    sub, d = length // nx, ny * pw
    f = wdt[0].shape[-1]
    length, tokens, n, slots = nx * sub, nx * ny * sub, nx * ny, experts * cap
    b16, f32 = jnp.bfloat16, jnp.float32
    vm = pl.BlockSpec(memory_space=pltpu.VMEM)
    hbm = pl.BlockSpec(memory_space=pl.ANY)
    lm = (2, mbs)
    rows_shape = lm + (nx, sub, d)
    spread_shape = lm + (ny, nx, sub, pw)
    entry = (
        ((2, mbs, sub, d), b16), ((2, small_b.shape[0], d), f32), (lm + (2, tokens), jnp.int32),
        (lm + (tokens, 2), jnp.int32), ((ny,) + att_block.shape, b16),
    )
    kept = entry + (
        (lm + (sub, d), b16), (lm + (sub, d), f32), (lm + (sub, d), b16), (rows_shape, b16),
        (lm + (length, pw), b16), (lm + (length, pw), b16), (lm + (length, pw), b16), (lm + (length, pw), b16),
        (lm + (experts, cap, pw), b16), (lm + (experts, cap, 2 * f), b16), (lm + (experts, cap, f), b16),
        (rows_shape, b16), (lm + (length, 2 * f), b16), (lm + (length, f), b16),
        ((2, ny) + sh_block.shape, b16), ((ny,) + att_block.shape, b16),
    )
    scratch = (
        (lm + (sub, d), b16), (lm + (sub, d), f32), (lm + (sub, d), b16), None,
        (lm + (sub, d), b16), (rows_shape, b16), ((length, 3 * pw), f32),
        (lm + (length, pw), b16), (lm + (length, pw), b16), (lm + (length, pw), b16), (lm + (length, pw), b16),
        (rows_shape, b16), (rows_shape, b16), ((2, pw, d), b16),
        (lm + (ny, sub, pw), b16), (lm + (ny, sub, pw), b16), (spread_shape, b16), (rows_shape, b16),
        ((slots, tokens), b16), ((tokens, slots), b16), (lm + (experts, cap, pw), b16), ((2, cap, 2 * f), f32),
        (lm + (experts, cap, 2 * f), b16), (lm + (experts, cap, f), b16), ((mbs, experts, cap, width), b16),
        (lm + (length, 2 * f), b16), (lm + (length, f), b16), (rows_shape, b16), (rows_shape, b16),
        (lm + (nx, ny, sub, pw), b16), (lm + (nx, ny, sub, pw), b16), (lm + (ny, sub, pw), b16), (lm + (ny, sub, pw), b16),
        ((experts, width, 2 * f), b16), ((experts, width, f), b16),
        ((ny,) + sh_block.shape, b16), ((ny,) + sh_block.shape, b16), ((ny,) + att_block.shape, b16), ((ny,) + att_block.shape, b16),
        ((ny, 2, mbs, sub, pw), b16), ((2, mbs, sub, d), b16), (lm + (2, tokens), jnp.int32),
        (lm + (2, tokens), jnp.int32), (lm + (tokens, 2), jnp.int32),
        ((ny,) + small_b.shape, f32), ((ny,) + small_b.shape, f32), ((2, small_b.shape[0], d), f32),
    )
    outs = pl.pallas_call(
        functools.partial(forward_kernel, (nx, ny, mbs, sub, width, pw, heads, features, experts, cap, f, *FWD_SKEW)),
        out_shape=tuple(jax.ShapeDtypeStruct(*v) for v in kept),
        in_specs=[vm] * 8 + [hbm] * 4,
        out_specs=(hbm,) * len(kept),
        scratch_shapes=[pltpu.VMEM(*(v or ((8, 128), f32))) for v in scratch] + [
            flags(lm + (nx,)), flags(lm + (nx,)), flags(lm + (nx,)), flags(lm + (nx,)),
            flags(lm + (ny,)), flags(lm + (ny,)), flags(lm + (nx,)), flags(lm + (nx,)), flags(lm + (nx,)), flags(lm + (nx,)),
            flags(lm + (nx,)), flags(lm + (nx,)), flags(lm + (nx,)), flags(lm + (nx,)), flags(lm + (ny,)), flags(lm + (ny,)),
            flags(lm + (experts,)), flags(lm + (experts,)), flags(lm + (experts,)), flags(lm + (experts,)),
            flags((experts,)), flags((experts,)), flags(lm + (experts,)), flags((24,)),
            flags((nx,)), flags((ny,)), pltpu.SemaphoreType.DMA, pltpu.SemaphoreType.DMA,
        ] + share_sems(ny) * 6,
        compiler_params=params(ids),
        cost_estimate=pl.CostEstimate(flops=10**10, bytes_accessed=8 * 10**7, transcendentals=10**6),
        name="forward",
    )(tin, small_b, att_block, sh_block, routes, cos, sin, rot, *win, *wdt)
    names = ("tok", "small", "place", "place_t", "watt0", "y", "mid", "n2", "rows", "q", "k", "v", "att", "slots", "gu", "hid", "rows2", "sgu", "shid", "shw", "watt1")
    return dict(zip(names, outs))


FWD_SKEW = (1, 1)
STAGE_STEPS = 1


def backward_kernel(cfg, *refs):
    nx, ny, mbs, sub, width, pw, heads, features, experts, cap, f, sk, ak = cfg
    (tok_i, small_i, place_i, y_i, mid_i, n2_i, rows_i, q_i, k_i, v_i, att_i, rows2_i, sgu_i, shid_i, shw_i,
     watt0_i, watt1_i, cos, sin, rot, slots_i, gu_i, hid_i, win_a, win_b, wdt_a, wdt_b) = refs[:27]
    (gx_o, win_g, wdt_g, att_g, sh_g, small_g,
     win, wdt, xsend, xline, xall, grows, pm, pt, slots, gslots, gown, hid, acc, dh, dgu, deo, sti, std,
     dsgu, ssend, srecv, rsend, rpeer, rline, rrecv, rwx, dm, msend, mall, datt, dqkv, dsend, drecv,
     rw_p, gains, sh_p, att_p, small_p, sh_x, att_x, small_x, sh_r, att_r, small_r, sh_f, att_f, small_f, small_a,
     g, gx, small, place, x, mid, n2, rows, q, k, v, att, rows2, sgu, shid, shw, watt,
     w_sem, x_send, x_recv, u_send, u_recv, t_send, t_recv, s_send, s_recv, g_send, g_recv, r_send, r_recv,
     m_send, m_recv, d_send, d_recv, rs_send, rs_recv, ag_send, ag_recv, wi_send, wi_recv, wd_send, wd_recv,
     c_send, c_recv, e_send, e_recv, a_send, a_recv, l_sem, st_sem, f_sem, y_sem, free) = refs[27:]
    pos = Position(nx, ny)
    s, a, b = pos.s, pos.a, pos.b
    slots_n = experts * cap
    tokens = nx * ny * sub
    d = ny * pw
    length = nx * sub
    half = experts // 2
    scale = DH ** -0.5
    lane = lax.broadcasted_iota(jnp.int32, (1, pw), 1)
    first = (b == ny - 1, b == 0)
    last = (b == 0, b == ny - 1)
    up = (ny - 1 - b, b)
    down = (b, ny - 1 - b)
    barrier = pltpu.get_barrier_semaphore()
    pos.peers(lambda ai: pl.semaphore_signal(barrier, inc=1, device_id=(s, ai, b), device_id_type=MESH))
    pos.line(lambda bi: pl.semaphore_signal(barrier, inc=1, device_id=(s, a, bi), device_id_type=MESH))
    pl.semaphore_signal(barrier, inc=1, device_id=(1 - s, a, b), device_id_type=MESH)

    def weight_copy(l, e, which):
        own, oth, dst = ((win_a, win_b, win), (wdt_a, wdt_b, wdt))[which]
        sem = w_sem.at[which, e]
        return pltpu.make_async_copy(own.at[e], dst.at[e], sem), pltpu.make_async_copy(oth.at[e], dst.at[e], sem)

    def start_weights(l, e):
        for which in range(2):
            own, oth = weight_copy(l, e, which)
            pl.when(s == l)(own.start)
            pl.when(s != l)(oth.start)

    def first_weights(e, c):
        start_weights(1, e)
        return c

    lax.fori_loop(0, experts, first_weights, 0)

    early = ((rows2_i, rows2), (sgu_i, sgu), (shid_i, shid), (shw_i, shw))
    later = ((mid_i, mid), (n2_i, n2), (rows_i, rows), (q_i, q), (k_i, k), (v_i, v), (att_i, att))

    def early_loads(l):
        return [pltpu.make_async_copy(src.at[l], dst, y_sem.at[c]) for c, (src, dst) in enumerate(early)]

    def later_loads(l):
        copies = [pltpu.make_async_copy(src.at[l], dst, y_sem.at[4 + c]) for c, (src, dst) in enumerate(later)]
        copies.append(pltpu.make_async_copy(y_i.at[0] if l else tok_i.at[0], x, y_sem.at[11]))
        return copies + [pltpu.make_async_copy(watt1_i if l else watt0_i, watt, y_sem.at[12])]

    def hid_load(l):
        return pltpu.make_async_copy(hid_i.at[l], hid, l_sem.at[1])

    def gates(l, m, dd):
        return pltpu.make_async_copy(gu_i.at[l, m, pl.ds(dd * half, half)], gown.at[m], l_sem.at[2 + m])

    def start_gates(l, m):
        for dd in range(2):
            pl.when(last[dd])(gates(l, m, dd).start)

    def wait_gates(l, m):
        for dd in range(2):
            pl.when(last[dd])(gates(l, m, dd).wait)

    first_loads = [
        pltpu.make_async_copy(src, dst, y_sem.at[13 + c])
        for c, (src, dst) in enumerate(((tok_i.at[1], g), (small_i, small), (place_i, place)))
    ]
    slots_load = pltpu.make_async_copy(slots_i, slots, l_sem.at[0])
    for copy in first_loads + [slots_load, hid_load(1)] + early_loads(1) + later_loads(1):
        copy.start()
    for m in range(mbs):
        start_gates(1, m)

    def copy_x(m, bi, slot):
        return remote(xsend.at[m, bi], xline.at[m, slot], x_send.at[m, bi], x_recv.at[m, slot], (s, a, bi))

    def copy_w(m, ai, slot):
        return remote(xline.at[m], xall.at[m, :, slot], u_send.at[m, ai], u_recv.at[m, slot], (s, ai, b))

    def copy_t(m, ai, slot):
        return remote(g.at[m], grows.at[m, slot], t_send.at[m, ai], t_recv.at[m, slot], (s, ai, b))

    for copy in first_loads:
        copy.wait()
    pl.semaphore_wait(barrier, nx - 1 + ny - 1 + 1)

    def send_g(m):
        for j in range(ny):
            xsend[m, j] = g[m, :, j * pw : (j + 1) * pw]
        pos.line(lambda bi: copy_x(m, bi, b).start())
        xline[m, b] = xsend[m, b]
        pos.peers(lambda ai: copy_t(m, ai, a).start())
        grows[m, a] = g[m]

    send_g(0)
    send_g(1)
    deo[...] = jnp.zeros_like(deo)
    ssend[...] = jnp.zeros_like(ssend)
    dsend[...] = jnp.zeros_like(dsend)
    rwx[...] = jnp.zeros_like(rwx)

    def new_layer(l):
        rwx[width : width + experts] = bf(small[l, :experts])
        rwx[width + experts : width + 2 * experts] = bf(small[l, :experts])
        rw_p[...] = jnp.zeros_like(rw_p)
        gains[...] = jnp.zeros_like(gains)

    new_layer(1)

    def spread(m):
        pos.line(lambda bi: copy_x(m, bi, bi).wait())
        pos.peers(lambda ai: copy_w(m, ai, a).start())
        xall[m, :, a] = xline[m]

    def dispatch(l, m):
        i0 = lax.broadcasted_iota(jnp.int32, (slots_n, tokens), 0)
        pm[...] = bf(((place[l, m, 0:1] == i0) | (place[l, m, 1:2] == i0)).astype(jnp.float32))
        pos.peers(lambda ai: copy_w(m, ai, ai).wait())
        gslots[l, m] = bf(mm(pm[...], xall[m].reshape(tokens, pw))).reshape(experts, cap, pw)

    def shared_act(m):
        pos.peers(lambda ai: copy_t(m, ai, ai).wait())
        dsh = by_blocks(grows[m].reshape(length, d), shw, slice(2 * f, 3 * f), width, pw)
        dsg, dsu, _ = act_back(sgu[m, :, :f].astype(jnp.float32), sgu[m, :, f:].astype(jnp.float32), dsh, None)
        dsgu[m, :, :f] = bf(dsg)
        dsgu[m, :, f:] = bf(dsu)

    def copy_s(m, ai, slot):
        return remote(ssend.at[m, ai], srecv.at[m, slot], s_send.at[m, ai], s_recv.at[m, slot], (s, ai, b))

    def shared_back(m):
        for j in range(ny):
            part = mm(dsgu[m], shw[j, :, : 2 * f], ((1,), (1,)))
            ssend[m, :, :, j * pw : j * pw + width] = bf(part).reshape(nx, sub, width)
        pos.peers(lambda ai: copy_s(m, ai, a).start())
        srecv[m, a] = ssend[m, a]

    crossing = ((sh_p, sh_x), (att_p, att_x), (small_p, small_x))
    places = (sh_r, att_r, small_r)
    finals = (sh_f, att_f, small_f)
    results = (sh_g, att_g, small_g)

    def cross(l, i):
        return remote(crossing[i][0], crossing[i][1], c_send.at[i], c_recv.at[i], (l, a, b))

    def block(i, bi):
        if i == 2:
            return small_x.at[:, pl.ds(pl.multiple_of(bi * pw, pw), pw)]
        return crossing[i][1].at[bi]

    def along(i, bi, slot):
        return remote(block(i, bi), places[i].at[slot], e_send.at[i, bi], e_recv.at[i, slot], (s, a, bi))

    def give(l, i):
        pl.when(s != l)(cross(l, i).start)

    def given(l):
        for i in range(3):
            pl.when(s != l)(cross(l, i).wait_send)

    def join(l, i):
        @pl.when(s == l)
        def _():
            cross(l, i).wait_recv()
            part, other = crossing[i]
            other[...] = (part[...].astype(jnp.float32) + other[...].astype(jnp.float32)).astype(other.dtype)
            pos.line(lambda bi: along(i, bi, lax.rem(b - bi + ny, ny) - 1).start())

    def settle(l, i):
        @pl.when(s == l)
        def _():
            pos.line(lambda bi: along(i, bi, lax.rem(bi - b + ny, ny) - 1).wait())
            total = block(i, b)[...].astype(jnp.float32)
            for c in range(1, ny):
                total = total + places[i][c - 1].astype(jnp.float32)
            finals[i][...] = total
            if i < 2:
                pltpu.make_async_copy(finals[i], results[i], f_sem.at[i]).start()

    def shared_grads():
        for j in range(ny):
            rj = rows2[:, :, :, j * pw : j * pw + width].reshape(mbs * length, width)
            sh_p[j, :, : 2 * f] = bf(mm(rj, dsgu[...].reshape(mbs * length, 2 * f), ((0,), (0,))))

    def down_grads(l):
        for j in range(ny):
            gj = grows[:, :, :, j * pw : j * pw + width].reshape(mbs * length, width)
            sh_p[j, :, 2 * f :] = bf(mm(gj, shid[...].reshape(mbs * length, f), ((0,), (0,))))
        give(l, 0)

    def copy_g(m, ai, slot):
        return remote(rsend.at[m, ai], rpeer.at[m, slot], g_send.at[m, ai], g_recv.at[m, slot], (s, ai, b))

    def copy_r(m, bi, slot):
        return remote(rline.at[m, bi], rrecv.at[m, slot], r_send.at[m, bi], r_recv.at[m, slot], (s, a, bi))

    def combine(l, m):
        row = lax.broadcasted_iota(jnp.int32, (128, tokens), 0)
        pair = place[l, m].astype(jnp.float32)
        cols = jnp.where(row == 0, pair[0:1], jnp.where(row == 1, pair[1:2], 0.0)).T.astype(jnp.int32)
        part = tokens // 2
        i1 = lax.broadcasted_iota(jnp.int32, (part, slots_n), 1)
        for c in range(2):
            these = cols[c * part : (c + 1) * part]
            pt[...] = bf(((these[:, 0:1] == i1) | (these[:, 1:2] == i1)).astype(jnp.float32))
            br = bf(mm(pt[...], deo[m].reshape(slots_n, pw))).reshape(ny // 2, nx, sub, pw)
            for ai in range(nx):
                rsend[m, ai, c * (ny // 2) : (c + 1) * (ny // 2)] = br[:, ai]
        pos.peers(lambda ai: copy_g(m, ai, a).start())
        rpeer[m, a] = rsend[m, a]

    def combine_line(m):
        pos.peers(lambda ai: copy_g(m, ai, ai).wait())
        total = rpeer[m, 0].astype(jnp.float32)
        for ai in range(1, nx):
            total = total + rpeer[m, ai].astype(jnp.float32)
        rline[m] = bf(total)
        pos.line(lambda bi: copy_r(m, bi, b).start())
        rrecv[m, b] = rline[m, b]

    def copy_m(m, ai, slot):
        return remote(msend.at[m], mall.at[m, slot], m_send.at[m, ai], m_recv.at[m, slot], (s, ai, b))

    def second_norm(l, m):
        pos.peers(lambda ai: copy_s(m, ai, ai).wait())
        pos.line(lambda bi: copy_r(m, bi, bi).wait())
        dlog = jnp.zeros((sub, pw), jnp.float32)
        parts = []
        for j in range(ny):
            part = rrecv[m, j].astype(jnp.float32)
            dlog = dlog + jnp.where(lane >= width, part, 0.0)
            parts.append(jnp.where(lane < width, part, 0.0))
        hi = bf(dlog)
        lo = bf(dlog - hi.astype(jnp.float32))
        dn2 = jnp.concatenate(parts, 1) + mm(hi, rwx[...]) + mm(lo, rwx[...])
        for ai in range(nx):
            dn2 = dn2 + srecv[m, ai].astype(jnp.float32)
        rw_t = mm(hi, n2[m], ((0,), (0,))) + mm(lo, n2[m], ((0,), (0,)))
        rw_p[...] += rw_t[width : width + experts] + rw_t[width + experts : width + 2 * experts]
        mv = mid[m]
        dx2, gain_g = norm_back(mv, rms(mv, features), small[l, experts : experts + 1], dn2, features)
        gains[0:1] += gain_g
        dm[m] = g[m].astype(jnp.float32) + dx2
        msend[m] = bf(dm[m])
        pos.peers(lambda ai: copy_m(m, ai, a).start())
        mall[m, a] = msend[m]

    def copy_d(m, ai, slot):
        return remote(dsend.at[m, ai], drecv.at[m, slot], d_send.at[m, ai], d_recv.at[m, slot], (s, ai, b))

    def attention(m):
        pos.peers(lambda ai: copy_m(m, ai, ai).wait())
        datt[...] = bf(by_blocks(mall[m].reshape(length, d), watt, slice(3 * pw, 4 * pw), width, pw))
        dq = jnp.zeros((length, pw), jnp.float32)
        dk = dq
        dv = dq
        for h in range(heads):
            mask = head_mask(pw, h)
            qh = jnp.where(mask, q[m], 0)
            kh = jnp.where(mask, k[m], 0)
            da = jnp.where(mask, datt[...], 0)
            p = probs_of(qh, k[m])
            dp = mm(da, v[m], ((1,), (1,)))
            ds = bf(p * (dp - jnp.sum(dp * p, axis=1, keepdims=True)))
            dv = dv + mm(bf(p), da, ((0,), (0,)))
            dq = dq + mm(ds, kh)
            dk = dk + mm(ds, qh, ((0,), (0,)))
        dqkv[m, :, :pw] = turn(dq * scale, cos[...], sin[...], rot[...], -1.0)
        dqkv[m, :, pw : 2 * pw] = turn(dk * scale, cos[...], sin[...], rot[...], -1.0)
        dqkv[m, :, 2 * pw :] = bf(dv)
        for j in range(ny):
            part = mm(dqkv[m], watt[j, :, : 3 * pw], ((1,), (1,)))
            dsend[m, :, :, j * pw : j * pw + width] = bf(part).reshape(nx, sub, width)
        pos.peers(lambda ai: copy_d(m, ai, a).start())
        drecv[m, a] = dsend[m, a]

    def first_norm(l, m):
        pos.peers(lambda ai: copy_d(m, ai, ai).wait())
        dn1 = drecv[m, 0].astype(jnp.float32)
        for ai in range(1, nx):
            dn1 = dn1 + drecv[m, ai].astype(jnp.float32)
        xv = x[m].astype(jnp.float32)
        dx1, gain_g = norm_back(xv, rms(xv, features), small[l, experts + 1 : experts + 2], dn1, features)
        gains[1:2] += gain_g
        gx[l, m] = bf(dm[m] + dx1)
        if l:
            g[m] = gx[l, m]
            send_g(m)

    def attention_grads(l):
        for j in range(ny):
            cols = slice(j * pw, j * pw + width)
            rj = rows[:, :, :, cols].reshape(mbs * length, width)
            mj = mall[:, :, :, cols].reshape(mbs * length, width)
            att_p[j, :, : 3 * pw] = bf(mm(rj, dqkv[...].reshape(mbs * length, 3 * pw), ((0,), (0,))))
            att_p[j, :, 3 * pw :] = bf(mm(mj, att[...].reshape(mbs * length, pw), ((0,), (0,))))
        give(l, 1)

    def small_grads(l):
        small_p[:experts] = rw_p[...]
        small_p[experts:] = gains[...]
        give(l, 2)

    lag = (sk + ak) * (ny - 1)
    gap = max(lag + 6 - half, 0)
    starts = (0, half, 2 * half + gap, 3 * half + gap)

    def unit(t, dd):
        soon = (t >= 0) & (t < 2 * half)
        then = (t >= starts[2]) & (t < starts[2] + 2 * half)
        u = jnp.clip(jnp.where(t < starts[2], jnp.minimum(t, 2 * half - 1), t - gap), 0, 4 * half - 1)
        job = u // half
        return soon | then, 1 - job // 2, lax.rem(job, 2), lax.rem(u, half) + dd * half

    def dh_copy(dd, l, m, e):
        to = b - 1 if dd == 0 else b + 1
        return remote(dh.at[m, e], dh.at[m, e], rs_send.at[l, m, e], rs_recv.at[l, m, e], (s, a, to))

    def dgu_copy(dd, l, m, e):
        to = b + 1 if dd == 0 else b - 1
        return remote(dgu.at[m, e], dgu.at[m, e], ag_send.at[l, m, e], ag_recv.at[l, m, e], (s, a, to))

    def wi_copy(l, e):
        return remote(win.at[e], win.at[e], wi_send.at[l, e], wi_recv.at[l, e], (l, a, b))

    def wd_copy(l, e):
        return remote(wdt.at[e], wdt.at[e], wd_send.at[l, e], wd_recv.at[l, e], (l, a, b))

    def st_copies(e):
        return (pltpu.make_async_copy(sti, win_g.at[e], st_sem.at[0]), pltpu.make_async_copy(std, wdt_g.at[e], st_sem.at[1]))

    def weight_grads(l, e):
        gi = mm(slots[l, :, e, :, :width].reshape(mbs * cap, width), dgu[:, e].reshape(mbs * cap, 2 * f), ((0,), (0,)))
        gd = mm(gslots[l, :, e, :, :width].reshape(mbs * cap, width), hid[:, e].reshape(mbs * cap, f), ((0,), (0,)))
        return gi, gd

    late = 2
    steps = starts[3] + half + lag + late

    def chain(i):
        reduce = [unit(i - sk * up[dd], dd) for dd in range(2)]
        spreads = [unit(i - sk * (ny - 1) - ak * down[dd], dd) for dd in range(2)]
        for dd in range(2):
            valid, l, m, e = reduce[dd]

            @pl.when(valid)
            def _():
                @pl.when(m == 0)
                def _():
                    weight_copy(0, e, 1)[0].wait()

                acc[dd] = mm(gslots[l, m, e, :, :width], wdt[e])

            @pl.when(valid & first[dd])
            def _():
                dh[m, e] = bf(acc[dd])
                dh_copy(dd, l, m, e).start()

            @pl.when(valid & jnp.logical_not(first[dd] | last[dd]))
            def _():
                dh_copy(dd, l, m, e).wait_recv()
                dh[m, e] = bf(acc[dd] + dh[m, e].astype(jnp.float32))
                dh_copy(dd, l, m, e).start()

            @pl.when(valid & last[dd])
            def _():
                dh_copy(dd, l, m, e).wait_recv()
                total = acc[dd] + dh[m, e].astype(jnp.float32)
                r = router_column(slots[l, m, e], e, width, experts)
                gate = gown[m, e - dd * half, :, :f].astype(jnp.float32)
                upv = gown[m, e - dd * half, :, f:].astype(jnp.float32)
                dgate, dup, dr = act_back(gate, upv, total, jax.nn.sigmoid(r))
                dgu[m, e, :, :f] = bf(dgate)
                dgu[m, e, :, f:] = bf(dup)
                dgu_copy(dd, l, m, e).start()
                hi = bf(dr).astype(jnp.float32)
                deo[m, e] = bf(jnp.where(lane == width + e, hi, jnp.where(lane == width + experts + e, dr - hi, 0.0)))

        for dd in range(2):
            valid, l, m, e = spreads[dd]

            @pl.when(valid & jnp.logical_not(last[dd]))
            def _():
                dgu_copy(dd, l, m, e).wait_recv()

                @pl.when(jnp.logical_not(first[dd]))
                def _():
                    dgu_copy(dd, l, m, e).start()

            @pl.when(valid)
            def _():
                @pl.when(m == 0)
                def _():
                    weight_copy(0, e, 0)[0].wait()

                deo[m, e, :, :width] = bf(mm(dgu[m, e], win[e], ((1,), (1,))))

        for l in (1, 0):
            u = i - starts[3 - 2 * l] - lag
            weight_stage(l, u)

    def chain_sent(l, e, dd):
        for m in range(mbs):
            pl.when(jnp.logical_not(last[dd]))(dh_copy(dd, l, m, e).wait_send)
            pl.when(jnp.logical_not(first[dd]))(dgu_copy(dd, l, m, e).wait_send)

    def weight_stage(l, u):
        @pl.when((u >= 0) & (u < half))
        def _():
            for dd in range(2):
                chain_sent(l, jnp.clip(u, 0, half - 1) + dd * half, dd)

        @pl.when((u >= 0) & (u < half) & (s == l))
        def _():
            pl.semaphore_signal(free.at[l], inc=1, device_id=(1 - s, a, b), device_id_type=MESH)

        @pl.when((u >= 0) & (u < half) & (s != l))
        def _():
            pl.semaphore_wait(free.at[l], 1)
            for dd in range(2):
                e = jnp.clip(u, 0, half - 1) + dd * half
                gi, gd = weight_grads(l, e)
                win[e] = bf(gi)
                wi_copy(l, e).start()
                wdt[e] = bf(gd)
                wd_copy(l, e).start()

        w = u - late

        @pl.when((w >= 0) & (w < half) & (s != l))
        def _():
            for dd in range(2):
                e = jnp.clip(w, 0, half - 1) + dd * half
                wi_copy(l, e).wait_send()
                wd_copy(l, e).wait_send()
                if l:
                    start_weights(0, e)

        @pl.when((w >= 0) & (w < half) & (s == l))
        def _():
            for dd in range(2):
                e = jnp.clip(w, 0, half - 1) + dd * half

                gi, gd = weight_grads(l, e)
                wi_copy(l, e).wait_recv()
                gi = gi + win[e].astype(jnp.float32)
                wd_copy(l, e).wait_recv()
                gd = gd + wdt[e].astype(jnp.float32)

                @pl.when((w >= 1) | (dd == 1))
                def _():
                    for copy in st_copies(e):
                        copy.wait()

                sti[...] = gi
                std[...] = gd
                for copy in st_copies(e):
                    copy.start()
                if l:
                    start_weights(0, e)

    stages = {}

    def at(step, do, *args):
        stages.setdefault(step, []).append(lambda: do(*args))

    def shared_first(l, m):
        if m == 0:
            for copy in early_loads(l):
                copy.wait()
        shared_act(m)

    def reload(copies):
        for copy in copies:
            copy.start()

    def ready(copies):
        for copy in copies:
            copy.wait()

    spread(0)
    spread(1)
    dispatch(1, 0)
    ready([slots_load, hid_load(1)] + later_loads(1))
    for m in range(mbs):
        wait_gates(1, m)
    at(1, dispatch, 1, 1)
    for l in (1, 0):
        begin = starts[2 - 2 * l]
        second = starts[3 - 2 * l]
        at(begin + 2, shared_first, l, 0)
        at(begin + 4, shared_back, 0)
        at(second + (-5 if l else 1), shared_first, l, 1)
        at(second + (-3 if l else 2), shared_back, 1)
        at(second + (-2 if l else 3), shared_grads)
        at(second + (-1 if l else 4), down_grads, l)
        at(second + (1 if l else 6), join, l, 0)
        for m in range(2):
            done = starts[2 - 2 * l + m] + half - 1 + lag
            for c, (do, *args) in enumerate((
                    (combine, l, m), (combine_line, m), (second_norm, l, m), (attention, m), (first_norm, l, m))):
                at(done + c, do, *args)
            if l:
                at(starts[m] + half + sk * (ny - 1), start_gates, 0, m)
                at(done + 5, spread, m)
                at(done + 6, dispatch, 0, m)
                at(starts[2 + m] - 1, wait_gates, 0, m)
        end = second + half - 1 + lag
        at(end + 3, attention_grads, l)
        at(end + 4, join, l, 1)
        at(end + 4, small_grads, l)
        at(end + 5, join, l, 2)
        at(end + (2 if l else 4), settle, l, 0)
        at(end + (9 if l else 5), settle, l, 1)
        at(end + (9 if l else 5), settle, l, 2)
        at(end + (9 if l else 5), given, l)
    end = starts[1] + half - 1 + lag
    at(starts[1] + 1, lambda: reload(early_loads(0)))
    at(end + late + 1, lambda: reload([hid_load(0)]))
    at(end + late + 4, lambda: ready([hid_load(0)]))
    at(end + 5, lambda: reload(later_loads(0)))
    at(end + 8, lambda: ready(later_loads(0)))
    at(end + 10, new_layer, 0)

    def step(i, c):
        chain(i)
        for when in sorted(stages):
            if when < steps:
                @pl.when(i == when)
                def _():
                    for do in stages[when]:
                        do()

        return c

    lax.fori_loop(0, steps, step, 0)
    for when in sorted(stages):
        if when >= steps:
            for do in stages[when]:
                do()

    def copy_a(ai, slot):
        return remote(small_f, small_a.at[slot], a_send.at[ai], a_recv.at[slot], (s, ai, b))

    def gain_sums():
        pos.peers(lambda ai: copy_a(ai, a).start())
        small_a[a] = small_f[...]
        pos.peers(lambda ai: copy_a(ai, ai).wait())
        total = small_a[0]
        for ai in range(1, nx):
            total = total + small_a[ai]
        small_f[...] = total

    gain_sums()
    pltpu.make_async_copy(small_f, small_g, f_sem.at[2]).start()
    gx_o[...] = gx[...]
    for i in range(3):
        pltpu.make_async_copy(finals[i], results[i], f_sem.at[i]).wait()
    for copy in st_copies(experts - 1):
        copy.wait()


def backward(fwd, cos, sin, rot, win, wdt, dims, heads, features, ids):
    width, pw, experts, cap = dims
    nx, ny = lax.axis_size("gx"), lax.axis_size("gy")
    mbs, sub, d = fwd["tok"].shape[-3:]
    f = wdt[0].shape[-1]
    length, tokens, slots = nx * sub, nx * ny * sub, experts * cap
    b16, f32 = jnp.bfloat16, jnp.float32
    vm = pl.BlockSpec(memory_space=pltpu.VMEM)
    hbm = pl.BlockSpec(memory_space=pl.ANY)
    ac, sc, n, half = fwd["watt0"].shape[2], fwd["shw"].shape[3], fwd["small"].shape[1], experts // 2
    rows_shape = (mbs, nx, sub, d)
    dense = lambda c: ((ny, width, c), b16)
    scratch = (
        ((experts, width, 2 * f), b16), ((experts, width, f), b16),
        ((mbs, ny, sub, pw), b16), ((mbs, ny, sub, pw), b16), ((mbs, ny, nx, sub, pw), b16), (rows_shape, b16),
        ((slots, tokens), b16), ((tokens // 2, slots), b16),
        ((2, mbs, experts, cap, pw), b16), ((2, mbs, experts, cap, pw), b16), ((mbs, half, cap, 2 * f), b16),
        ((mbs, experts, cap, f), b16), ((2, cap, f), f32), ((mbs, experts, cap, f), b16),
        ((mbs, experts, cap, 2 * f), b16), ((mbs, experts, cap, pw), b16),
        ((width, 2 * f), f32), ((width, f), f32),
        ((mbs, length, 2 * f), b16), (rows_shape, b16), (rows_shape, b16),
        ((mbs, nx, ny, sub, pw), b16), ((mbs, nx, ny, sub, pw), b16), ((mbs, ny, sub, pw), b16), ((mbs, ny, sub, pw), b16),
        ((pw, d), b16), ((mbs, sub, d), f32), ((mbs, sub, d), b16), (rows_shape, b16),
        ((length, pw), b16), ((mbs, length, 3 * pw), b16), (rows_shape, b16), (rows_shape, b16),
        ((experts, d), f32), ((8, d), f32),
        dense(sc), dense(ac), ((n, d), f32), dense(sc), dense(ac), ((n, d), f32),
        ((ny - 1, width, sc), b16), ((ny - 1, width, ac), b16), ((ny - 1, n, pw), f32),
        ((width, sc), f32), ((width, ac), f32), ((n, pw), f32), ((nx, n, pw), f32),
        ((mbs, sub, d), b16), ((2, mbs, sub, d), b16),
        *((fwd[name].shape, fwd[name].dtype) for name in ("small", "place")),
        ((mbs, sub, d), b16),
        *((fwd[name].shape[1:], fwd[name].dtype) for name in (
            "mid", "n2", "rows", "q", "k", "v", "att", "rows2", "sgu", "shid", "shw")),
        (fwd["watt0"].shape, b16),
    )
    by_m = lambda c: flags((mbs, c))
    by_lm = lambda c: flags((2, mbs, c))
    names = ("tok", "small", "place", "y", "mid", "n2", "rows", "q", "k", "v", "att", "rows2", "sgu", "shid",
             "shw", "watt0", "watt1")
    outs = pl.pallas_call(
        functools.partial(
            backward_kernel, (nx, ny, mbs, sub, width, pw, heads, features, experts, cap, f, *BWD_SKEW)),
        out_shape=(
            jax.ShapeDtypeStruct((2, mbs, sub, d), b16),
            jax.ShapeDtypeStruct((experts, width, 2 * f), f32),
            jax.ShapeDtypeStruct((experts, width, f), f32),
            jax.ShapeDtypeStruct((width, ac), f32),
            jax.ShapeDtypeStruct((width, sc), f32),
            jax.ShapeDtypeStruct((n, pw), f32),
        ),
        in_specs=[hbm] * 17 + [vm] * 3 + [hbm] * 7,
        out_specs=(vm,) + (hbm,) * 5,
        scratch_shapes=[pltpu.VMEM(*v) for v in scratch] + [
            flags((2, experts)), by_m(ny), by_m(ny), by_m(nx), by_m(nx), by_m(nx), by_m(nx), by_m(nx), by_m(nx),
            by_m(nx), by_m(nx), by_m(ny), by_m(ny), by_m(nx), by_m(nx), by_m(nx), by_m(nx),
            by_lm(experts), by_lm(experts), by_lm(experts), by_lm(experts),
            flags((2, experts)), flags((2, experts)), flags((2, experts)), flags((2, experts)),
            flags((3,)), flags((3,)), flags((3, ny)), flags((3, ny)), flags((nx,)), flags((nx,)),
            flags((4,)), flags((2,)), flags((3,)), flags((20,)), pltpu.SemaphoreType.REGULAR((2,)),
        ],
        compiler_params=params(ids),
        cost_estimate=pl.CostEstimate(flops=2 * 10**10, bytes_accessed=10**8, transcendentals=10**6),
        name="backward",
    )(*(fwd[name] for name in names), cos, sin, rot, *(fwd[name] for name in ("slots", "gu", "hid")), *win, *wdt)
    return outs[0], outs[1:]


BWD_SKEW = (1, 1)


def fast_device(block_input, output_grad, attention_gain, attention_in, attention_out, feed_gain,
                router_weight, expert_in, expert_down, shared_in, shared_down, routes):
    s = lax.axis_index("section")
    ny = lax.axis_size("gy")
    nx = lax.axis_size("gx")
    mbs = block_input.shape[0] // 2
    width = block_input.shape[2]
    features = width * ny
    experts = expert_in.shape[1]
    f = expert_in.shape[-1]
    pw = lanes_up(width + 2 * experts)
    tokens = routes.shape[2]
    cap = 5 * tokens // (2 * experts)
    length = tokens // ny
    heads = attention_in.shape[-1] // DH
    dims = (width, pw, experts, cap)

    att_block = jnp.concatenate([
        pad_to(attention_in[0], 2, pw).reshape(width, 3 * pw), pad_to(attention_out[0].T, 1, pw)], 1)
    sh_block = jnp.concatenate([shared_in[0].reshape(width, 2 * f), shared_down[0].T], 1)
    small = jnp.concatenate([
        router_weight[0].T.astype(jnp.float32), feed_gain, attention_gain, jnp.zeros((6, width), jnp.float32)], 0)
    tin = lax.dynamic_slice_in_dim(jnp.stack([block_input, output_grad]), s * mbs, mbs, 1)
    tin = pad_to(tin, 3, pw)
    small = pad_to(small, 1, pw)
    win = expert_in[0].reshape(experts, width, 2 * f)
    win = (win, pass_section(win))
    wdt = expert_down[0].transpose(0, 2, 1)
    wdt = (wdt, pass_section(wdt))
    pairs = jnp.swapaxes(routes[0], 1, 2)
    half = DH // 2
    freq = 10000.0 ** (-jnp.arange(half, dtype=jnp.float32) / half)
    ang = jnp.arange(length, dtype=jnp.float32)[:, None] * freq[None]
    lanes = jnp.tile(ang, (1, 2 * heads))
    cos = pad_to(jnp.cos(lanes), 1, pw)
    sin = pad_to(jnp.sin(lanes), 1, pw)
    rot = pad_to(pad_to(rot_columns(jnp.eye(heads * DH, dtype=jnp.float32)), 0, pw), 1, pw).astype(jnp.bfloat16)

    fwd = forward(tin, small, att_block, sh_block, pairs, cos, sin, rot, win, wdt, dims, heads, features, 0)
    outs = fwd["y"]
    gouts, grads = backward(fwd, cos, sin, rot, win, wdt, dims, heads, features, 1)

    both = leave(jnp.stack([outs[0], gouts[0]]), jnp.stack([outs[1], gouts[1]]), pw, 2)[..., :width]
    win_g, wdt_g, att_g, sh_g, small_g = grads
    hd = heads * DH
    return (
        both[0][None],
        both[1][None],
        small_g[experts + 1 : experts + 2, :width],
        att_g[:, : 3 * pw].reshape(width, 3, pw)[..., :hd][None],
        att_g[:, 3 * pw : 3 * pw + hd].T[None],
        small_g[experts : experts + 1, :width],
        small_g[:experts, :width].T[None],
        win_g.reshape(experts, width, 2, f)[None],
        wdt_g.transpose(0, 2, 1)[None],
        sh_g[:, : 2 * f].reshape(width, 2, f)[None],
        sh_g[:, 2 * f :].T[None],
    )


def solution(mesh):
    in_specs = (
        P(None, "gx", "gy"),
        P(None, "gx", "gy"),
        P("section", "gy"),
        P("section", "gy", None, "gx"),
        P("section", "gx", "gy"),
        P("section", "gy"),
        P("section", "gy", None),
        P("section", None, "gy", None, "gx"),
        P("section", None, "gx", "gy"),
        P("section", "gy", None, "gx"),
        P("section", "gx", "gy"),
        P("section", None, None, None),
    )
    out_specs = (
        P("section", None, "gx", "gy"),
        P("section", None, "gx", "gy"),
        P("section", "gy"),
        P("section", "gy", None, "gx"),
        P("section", "gx", "gy"),
        P("section", "gy"),
        P("section", "gy", None),
        P("section", None, "gy", None, "gx"),
        P("section", None, "gx", "gy"),
        P("section", "gy", None, "gx"),
        P("section", "gx", "gy"),
    )
    fast = mesh.shape["gx"] == mesh.shape["gy"]
    return jax.shard_map(
        fast_device if fast else on_device, mesh=mesh, in_specs=in_specs, out_specs=out_specs, check_vma=False
    )
```

```python
import functools

import jax
import jax.numpy as jnp
import numpy as np
from jax import lax
from jax.experimental import pallas as pl
from jax.experimental.pallas import tpu as pltpu
from jax.sharding import PartitionSpec as P

DH = 64


epsilon = 1e-06
highest = lax.Precision.HIGHEST


def from_partner(array, axis, apart):
    return lax.ppermute(array, axis, [(i, i ^ 1 << apart) for i in range(lax.axis_size(axis))])


def token_rows(values):
    return lax.all_gather(values, "gx", axis=0, tiled=True)


def output_rows(values):
    return lax.psum_scatter(values, "gx", scatter_dimension=0, tiled=True)


def width_sum(values):
    return lax.psum(values, "gy")


def pass_section(values):
    return from_partner(values, "section", 0)


def sequence_sums(values):
    return lax.psum_scatter(values, "gy", scatter_dimension=0, tiled=True)


def sequence_rows(values):
    return lax.all_gather(values, "gy", axis=0, tiled=True)


def gather_hidden(hidden, shared_hidden):
    return (
        lax.all_gather(hidden, "gy", axis=0, tiled=True),
        lax.all_gather(shared_hidden, "gy", axis=0, tiled=True),
    )


def rope_turn(values, positions, turn_sign):
    half_size = values.shape[-1] // 2
    frequency = 10000.0 ** (-jnp.arange(half_size, dtype=jnp.float32) / half_size)
    angles = positions[:, None] * frequency[None, :]
    cosine = jnp.cos(angles)[:, None, :]
    sine_part = turn_sign * jnp.sin(angles)[:, None, :]
    first_half = values[..., :half_size]
    second_half = values[..., half_size:]
    return jnp.concatenate(
        [
            first_half * cosine - second_half * sine_part,
            first_half * sine_part + second_half * cosine,
        ],
        axis=-1,
    )


def norm_forward(stream, gain):
    full_width = stream.shape[1] * lax.axis_size("gy")
    square_sum = width_sum(jnp.sum(stream * stream, axis=1))
    inverse_rms = lax.rsqrt(square_sum / full_width + epsilon)
    return ((stream * inverse_rms[:, None] * gain[None, :]).astype(jnp.bfloat16), inverse_rms)


def norm_backward(stream, inverse_rms, gain, grad_normed):
    full_width = stream.shape[1] * lax.axis_size("gy")
    scaled = grad_normed * gain[None, :]
    inner_sum = width_sum(jnp.sum(scaled * stream, axis=1))
    cubed = inverse_rms * inverse_rms * inverse_rms
    grad_stream = inverse_rms[:, None] * scaled - stream * (cubed * inner_sum / full_width)[:, None]
    grad_gain = jnp.sum(grad_normed * stream * inverse_rms[:, None], axis=0)
    return (grad_stream, grad_gain)


def slot_table(route_ids, experts, capacity):
    flat_ids = route_ids.reshape(-1)
    assigned = (flat_ids[:, None] == jnp.arange(experts, dtype=jnp.int32)[None, :]).astype(
        jnp.int32
    )
    earlier = jnp.cumsum(assigned, axis=0) - assigned
    places = flat_ids * capacity + jnp.sum(earlier * assigned, axis=1)
    owners = jnp.arange(flat_ids.shape[0], dtype=jnp.int32) // 2
    slot_token = jnp.zeros((experts * capacity,), jnp.int32).at[places].set(owners)
    slot_valid = jnp.zeros((experts * capacity,), jnp.int32).at[places].set(jnp.ones_like(owners))
    return (places.reshape(-1, 2), slot_token, slot_valid)


def expert_act(gate_up, logits):
    half_size = gate_up.shape[1] // 2
    return (
        jax.nn.silu(gate_up[:, :half_size])
        * gate_up[:, half_size:]
        * jax.nn.sigmoid(logits)[:, None]
    )


def shared_act(gate_up):
    half_size = gate_up.shape[1] // 2
    return jax.nn.silu(gate_up[:, :half_size]) * gate_up[:, half_size:]


def causal_scores(queries, keys_part):
    score_scale = queries.shape[-1] ** (-0.5)
    scores = (
        jnp.einsum("qhd,khd->hqk", queries, keys_part, preferred_element_type=jnp.float32)
        * score_scale
    )
    length = queries.shape[0]
    causal = jnp.arange(length)[:, None] >= jnp.arange(length)[None, :]
    return jnp.where(causal[None], scores, -1e30)


def attend_forward(queries, keys_part, values_part):
    scores = causal_scores(queries, keys_part)
    row_max = jnp.max(scores, axis=-1, keepdims=True)
    exponent = jnp.exp(scores - row_max)
    row_total = jnp.sum(exponent, axis=-1, keepdims=True)
    probabilities = (exponent / row_total).astype(jnp.bfloat16)
    attended = jnp.einsum(
        "hqk,khd->qhd", probabilities, values_part, preferred_element_type=jnp.float32
    )
    return (attended, row_max + jnp.log(row_total))


def attend_backward(queries, keys_part, values_part, log_total, grad_attended):
    score_scale = queries.shape[-1] ** (-0.5)
    probabilities = jnp.exp(causal_scores(queries, keys_part) - log_total)
    grad_values = jnp.einsum(
        "hqk,qhd->khd",
        probabilities.astype(jnp.bfloat16),
        grad_attended,
        preferred_element_type=jnp.float32,
    )
    grad_probs = jnp.einsum(
        "qhd,khd->hqk", grad_attended, values_part, preferred_element_type=jnp.float32
    )
    grad_scores = (
        probabilities * (grad_probs - jnp.sum(grad_probs * probabilities, axis=-1, keepdims=True))
    ).astype(jnp.bfloat16)
    grad_queries = (
        jnp.einsum("hqk,khd->qhd", grad_scores, keys_part, preferred_element_type=jnp.float32)
        * score_scale
    )
    grad_keys = (
        jnp.einsum("hqk,qhd->khd", grad_scores, queries, preferred_element_type=jnp.float32)
        * score_scale
    )
    return (grad_queries, grad_keys, grad_values)


def layer_forward(stream, weights, route_ids):
    (
        attention_gain,
        attention_in,
        attention_out,
        feed_gain,
        router_weight,
        expert_in,
        expert_down,
        shared_in,
        shared_down,
    ) = weights
    local_width = stream.shape[1]
    experts = expert_in.shape[0]
    normed, inverse_first = norm_forward(stream, attention_gain)
    rows_first = token_rows(normed)
    tokens = rows_first.shape[0]
    capacity = 5 * tokens // (2 * experts)
    slot_count = experts * capacity
    projected = sequence_sums(
        jnp.dot(
            rows_first, attention_in.reshape(local_width, -1), preferred_element_type=jnp.float32
        )
    )
    length = projected.shape[0]
    projected = projected.reshape(length, 3, -1, DH)
    positions = jnp.arange(length, dtype=jnp.float32)
    queries = rope_turn(projected[:, 0], positions, 1.0).astype(jnp.bfloat16)
    keys_part = rope_turn(projected[:, 1], positions, 1.0).astype(jnp.bfloat16)
    values_part = projected[:, 2].astype(jnp.bfloat16)
    attended, log_total = attend_forward(queries, keys_part, values_part)
    attended_rows = sequence_rows(attended.astype(jnp.bfloat16).reshape(length, -1))
    middle = stream + output_rows(
        jnp.dot(attended_rows, attention_out, preferred_element_type=jnp.float32)
    )
    normed_feed, inverse_second = norm_forward(middle, feed_gain)
    rows_second = token_rows(normed_feed)
    route_slot, slot_token, slot_valid = slot_table(route_ids, experts, capacity)
    grouped = (rows_second[slot_token] * slot_valid[:, None].astype(jnp.bfloat16)).reshape(
        experts, capacity, local_width
    )
    expert_part = jnp.einsum(
        "ecd,edf->ecf",
        grouped,
        expert_in.reshape(experts, local_width, -1),
        preferred_element_type=jnp.float32,
    )
    router_part = jnp.einsum(
        "ecd,de->ec", grouped, router_weight, preferred_element_type=jnp.float32
    )
    shared_part = jnp.dot(
        rows_second, shared_in.reshape(local_width, -1), preferred_element_type=jnp.float32
    )
    expert_gu, router_logit, shared_gu = (
        lax.psum_scatter(
            expert_part.reshape(slot_count, -1), "gy", scatter_dimension=0, tiled=True
        ),
        lax.psum_scatter(router_part.reshape(slot_count), "gy", scatter_dimension=0, tiled=True),
        lax.psum_scatter(shared_part, "gy", scatter_dimension=0, tiled=True),
    )
    hidden_rows, shared_rows = gather_hidden(
        expert_act(expert_gu, router_logit).astype(jnp.bfloat16),
        shared_act(shared_gu).astype(jnp.bfloat16),
    )
    expert_result = jnp.einsum(
        "ecf,efd->ecd",
        hidden_rows.reshape(experts, capacity, -1),
        expert_down,
        preferred_element_type=jnp.float32,
    ).reshape(slot_count, local_width)
    branch = (
        expert_result[route_slot[:, 0]]
        + expert_result[route_slot[:, 1]]
        + jnp.dot(shared_rows, shared_down, preferred_element_type=jnp.float32)
    )
    result = middle + output_rows(branch)
    kept_items = (
        stream,
        inverse_first,
        rows_first,
        queries,
        keys_part,
        values_part,
        log_total,
        attended_rows,
        middle,
        inverse_second,
        rows_second,
        expert_gu,
        router_logit,
        shared_gu,
    )
    return (result, kept_items)


def layer_backward(grad_out, kept_items, weights, route_ids):
    (
        attention_gain,
        attention_in,
        attention_out,
        feed_gain,
        router_weight,
        expert_in,
        expert_down,
        shared_in,
        shared_down,
    ) = weights
    (
        stream,
        inverse_first,
        rows_first,
        queries,
        keys_part,
        values_part,
        log_total,
        attended_rows,
        middle,
        inverse_second,
        rows_second,
        expert_gu,
        router_logit,
        shared_gu,
    ) = kept_items[:14]
    local_width = stream.shape[1]
    experts = expert_in.shape[0]
    tokens = rows_second.shape[0]
    capacity = 5 * tokens // (2 * experts)
    slot_count = experts * capacity
    hidden_rows, shared_rows = gather_hidden(
        expert_act(expert_gu, router_logit).astype(jnp.bfloat16),
        shared_act(shared_gu).astype(jnp.bfloat16),
    )
    route_slot, slot_token, slot_valid = slot_table(route_ids, experts, capacity)
    valid_rows = slot_valid[:, None].astype(jnp.bfloat16)
    grouped = (rows_second[slot_token] * valid_rows).reshape(experts, capacity, local_width)
    grad_rows = token_rows(grad_out.astype(jnp.bfloat16))
    slot_grad = (grad_rows[slot_token] * valid_rows).reshape(experts, capacity, local_width)
    down_grad = jnp.einsum(
        "ecf,ecd->efd",
        hidden_rows.reshape(experts, capacity, -1),
        slot_grad,
        preferred_element_type=jnp.float32,
    )
    shared_down_grad = jnp.einsum(
        "tf,td->fd", shared_rows, grad_rows, preferred_element_type=jnp.float32
    )
    hidden_part = jnp.einsum(
        "ecd,efd->ecf", slot_grad, expert_down, preferred_element_type=jnp.float32
    ).reshape(slot_count, -1)
    shared_part = jnp.einsum(
        "td,fd->tf", grad_rows, shared_down, preferred_element_type=jnp.float32
    )
    grad_hidden, grad_shared = (
        lax.psum_scatter(
            hidden_part.astype(jnp.bfloat16), "gy", scatter_dimension=0, tiled=True
        ).astype(jnp.float32),
        lax.psum_scatter(
            shared_part.astype(jnp.bfloat16), "gy", scatter_dimension=0, tiled=True
        ).astype(jnp.float32),
    )
    unused_expert, expert_back = jax.vjp(expert_act, expert_gu, router_logit)
    grad_gu, grad_logit = expert_back(grad_hidden)
    unused_shared, shared_back = jax.vjp(shared_act, shared_gu)
    (grad_shared_gu,) = shared_back(grad_shared)
    gu_rows, shared_gu_rows = (
        lax.all_gather(grad_gu.astype(jnp.bfloat16), "gy", axis=0, tiled=True),
        lax.all_gather(grad_shared_gu.astype(jnp.bfloat16), "gy", axis=0, tiled=True),
    )
    logit_rows = lax.all_gather(grad_logit, "gy", axis=0, tiled=True).reshape(experts, capacity)
    gu_grouped = gu_rows.reshape(experts, capacity, -1)
    in_grad = jnp.einsum("ecd,ecf->edf", grouped, gu_grouped, preferred_element_type=jnp.float32)
    router_grad = jnp.einsum(
        "ecd,ec->de", grouped.astype(jnp.float32), logit_rows, precision=highest
    )
    shared_in_grad = jnp.einsum(
        "td,tf->df", rows_second, shared_gu_rows, preferred_element_type=jnp.float32
    )
    slot_back = jnp.einsum(
        "ecf,edf->ecd",
        gu_grouped,
        expert_in.reshape(experts, local_width, -1),
        preferred_element_type=jnp.float32,
    )
    slot_back = slot_back + logit_rows[:, :, None] * router_weight.T.astype(jnp.float32)[:, None, :]
    slot_back = slot_back.reshape(slot_count, local_width)
    rows_back = (
        slot_back[route_slot[:, 0]]
        + slot_back[route_slot[:, 1]]
        + jnp.einsum(
            "tf,df->td",
            shared_gu_rows,
            shared_in.reshape(local_width, -1),
            preferred_element_type=jnp.float32,
        )
    )
    grad_middle_norm, feed_gain_grad = norm_backward(
        middle, inverse_second, feed_gain, output_rows(rows_back)
    )
    grad_middle = grad_out + grad_middle_norm
    middle_rows = token_rows(grad_middle.astype(jnp.bfloat16))
    out_weight_grad = jnp.einsum(
        "tf,td->fd", attended_rows, middle_rows, preferred_element_type=jnp.float32
    )
    grad_attended = sequence_sums(
        jnp.einsum("td,fd->tf", middle_rows, attention_out, preferred_element_type=jnp.float32)
    )
    length = grad_attended.shape[0]
    positions = jnp.arange(length, dtype=jnp.float32)
    grad_queries, grad_keys, grad_values = attend_backward(
        queries,
        keys_part,
        values_part,
        log_total,
        grad_attended.astype(jnp.bfloat16).reshape(queries.shape),
    )
    grad_projected = jnp.stack(
        [
            rope_turn(grad_queries, positions, -1.0),
            rope_turn(grad_keys, positions, -1.0),
            grad_values,
        ],
        axis=1,
    )
    grad_projected = grad_projected.astype(jnp.bfloat16).reshape(length, -1)
    projected_rows = sequence_rows(grad_projected)
    in_weight_grad = jnp.einsum(
        "td,tf->df", rows_first, projected_rows, preferred_element_type=jnp.float32
    )
    grad_normed = output_rows(
        jnp.einsum(
            "tf,df->td",
            projected_rows,
            attention_in.reshape(local_width, -1),
            preferred_element_type=jnp.float32,
        )
    )
    grad_stream_norm, attention_gain_grad = norm_backward(
        stream, inverse_first, attention_gain, grad_normed
    )
    layer_grads = (
        attention_gain_grad,
        in_weight_grad.reshape(attention_in.shape),
        out_weight_grad,
        feed_gain_grad,
        router_grad,
        in_grad.reshape(expert_in.shape),
        down_grad,
        shared_in_grad.reshape(shared_in.shape),
        shared_down_grad,
    )
    return (grad_middle + grad_stream_norm, layer_grads)


def put_item(buffer, value, batch_index, is_valid):
    current = lax.dynamic_index_in_dim(buffer, batch_index, 0, keepdims=False)
    return lax.dynamic_update_index_in_dim(
        buffer, jnp.where(is_valid, value, current), batch_index, 0
    )


def on_device(
    block_input,
    output_grad,
    attention_gain,
    attention_in,
    attention_out,
    feed_gain,
    router_weight,
    expert_in,
    expert_down,
    shared_in,
    shared_down,
    routes,
):
    section_index = lax.axis_index("section")
    batches = block_input.shape[0]
    weights = tuple(
        (
            member[0]
            for member in (
                attention_gain,
                attention_in,
                attention_out,
                feed_gain,
                router_weight,
                expert_in,
                expert_down,
                shared_in,
                shared_down,
            )
        )
    )
    route_table = routes[0]
    outputs = jnp.zeros(block_input.shape, jnp.bfloat16)
    received = jnp.zeros(block_input.shape[1:], jnp.bfloat16)
    stored = None
    for tick_step in range(batches + 1):
        micro_index = tick_step - section_index
        is_valid = (micro_index >= 0) & (micro_index < batches)
        batch_index = jnp.clip(micro_index, 0, batches - 1)
        fresh_input = lax.dynamic_index_in_dim(block_input, batch_index, 0, keepdims=False)
        incoming = jnp.where(section_index == 0, fresh_input, received).astype(jnp.float32)
        route_ids = lax.dynamic_index_in_dim(route_table, batch_index, 0, keepdims=False)
        result, kept_items = layer_forward(incoming, weights, route_ids)
        result_low = result.astype(jnp.bfloat16)
        outputs = put_item(outputs, result_low, batch_index, is_valid)
        if stored is None:
            stored = tuple(
                (jnp.zeros((batches,) + member.shape, member.dtype) for member in kept_items)
            )
        stored = tuple(
            (
                put_item(buffer, member, batch_index, is_valid)
                for buffer, member in zip(stored, kept_items)
            )
        )
        if tick_step < batches:
            received = pass_section(result_low)
    grads_in = jnp.zeros(block_input.shape, jnp.bfloat16)
    received = jnp.zeros(block_input.shape[1:], jnp.bfloat16)
    totals = tuple((jnp.zeros(member.shape, jnp.float32) for member in weights))
    for tick_step in range(batches + 1):
        micro_index = batches - tick_step - section_index
        is_valid = (micro_index >= 0) & (micro_index < batches)
        batch_index = jnp.clip(micro_index, 0, batches - 1)
        given_grad = lax.dynamic_index_in_dim(output_grad, batch_index, 0, keepdims=False)
        incoming = jnp.where(section_index == 1, given_grad, received).astype(jnp.float32)
        kept_items = tuple(
            (lax.dynamic_index_in_dim(buffer, batch_index, 0, keepdims=False) for buffer in stored)
        )
        route_ids = lax.dynamic_index_in_dim(route_table, batch_index, 0, keepdims=False)
        grad_input, layer_grads = layer_backward(incoming, kept_items, weights, route_ids)
        grad_low = grad_input.astype(jnp.bfloat16)
        grads_in = put_item(grads_in, grad_low, batch_index, is_valid)
        totals = tuple(
            (total + jnp.where(is_valid, member, 0.0) for total, member in zip(totals, layer_grads))
        )
        if tick_step < batches:
            received = pass_section(grad_low)
    gain_first, gain_second, router_total = lax.psum((totals[0], totals[3], totals[4]), "gx")
    return (
        outputs[None],
        grads_in[None],
        gain_first[None],
        totals[1][None],
        totals[2][None],
        gain_second[None],
        router_total[None],
        totals[5][None],
        totals[6][None],
        totals[7][None],
        totals[8][None],
    )


def lanes_up(n):
    return -(-n // 128) * 128


def rot_columns(w):
    shape = w.shape
    w = w.reshape(shape[:-1] + (-1, 2, DH // 2))
    w = jnp.stack([-w[..., 1, :], w[..., 0, :]], axis=-2)
    return w.reshape(shape)


def pad_to(v, axis, n):
    pads = [(0, 0)] * v.ndim
    pads[axis] = (0, n - v.shape[axis])
    return jnp.pad(v, pads)


def mm(a, b, dims=((1,), (0,))):
    return lax.dot_general(a, b, (dims, ((), ())), preferred_element_type=jnp.float32)


def bf(v):
    return v.astype(jnp.bfloat16)


def head_mask(pw, h):
    lane = lax.broadcasted_iota(jnp.int32, (1, pw), 1)
    return (lane >= h * DH) & (lane < (h + 1) * DH)


def rms(x, features):
    return lax.rsqrt(jnp.sum(x * x, axis=1, keepdims=True) / features + epsilon)


def norm_back(x, inv, gain, d, features):
    u = d * gain
    inner = jnp.sum(u * x, axis=1, keepdims=True) / features
    dx = inv * u - x * (inv * inv * inv * inner)
    return dx, jnp.sum(d * x * inv, axis=0, keepdims=True)


def probs_of(q, k):
    s = mm(q, k, ((1,), (1,))) * DH ** -0.5
    n = s.shape[0]
    causal = lax.broadcasted_iota(jnp.int32, (n, n), 0) >= lax.broadcasted_iota(jnp.int32, (n, n), 1)
    s = jnp.where(causal, s, -1e30)
    e = jnp.exp(s - jnp.max(s, axis=1, keepdims=True))
    return e / jnp.sum(e, axis=1, keepdims=True)


def act_back(gate, up, dh, s):
    sg = jax.nn.sigmoid(gate)
    silu = gate * sg
    if s is None:
        return dh * up * (sg * (1.0 + gate * (1.0 - sg))), dh * silu, None
    dr = jnp.sum(dh * silu * up, axis=-1, keepdims=True) * s * (1.0 - s)
    ds = dh * s
    return ds * up * (sg * (1.0 + gate * (1.0 - sg))), ds * silu, dr


MESH = pl.DeviceIdType.MESH
VMEM_BYTES = 62 * 2**20


def remote(src, dst, send, recv, target):
    return pltpu.make_async_remote_copy(
        src_ref=src, dst_ref=dst, send_sem=send, recv_sem=recv, device_id=target, device_id_type=MESH
    )


def router_column(rows, e, width, experts):
    lane = lax.broadcasted_iota(jnp.int32, rows.shape, rows.ndim - 1)
    mask = (lane == width + e) | (lane == width + experts + e)
    return jnp.sum(jnp.where(mask, rows.astype(jnp.float32), 0.0), axis=-1, keepdims=True)


class Position:
    def __init__(self, nx, ny):
        self.s = lax.axis_index("section")
        self.a = lax.axis_index("gx")
        self.b = lax.axis_index("gy")
        self.nx, self.ny = nx, ny
        self.n = nx * ny
        self.me = self.a * ny + self.b

    def device(self, index):
        return (self.s, index // self.ny, lax.rem(index, self.ny))

    def others(self, do):
        def step(i, c):
            index = lax.rem(self.me + i, self.n)
            do(index, index // self.ny, lax.rem(index, self.ny))
            return c

        lax.fori_loop(1, self.n, step, 0)

    def peers(self, do):
        for i in range(1, self.nx):
            do(lax.rem(self.a + i, self.nx))

    def line(self, do):
        for i in range(1, self.ny):
            do(lax.rem(self.b + i, self.ny))


def greet_section(pos):
    barrier = pltpu.get_barrier_semaphore()

    def one(index, ai, bi):
        pl.semaphore_signal(barrier, inc=1, device_id=(pos.s, ai, bi), device_id_type=MESH)

    pos.others(one)
    return barrier


def flags(count):
    return pltpu.SemaphoreType.DMA(count)


class Share:
    def __init__(self, pos, layer, block, full, sems):
        self.pos, self.layer, self.block, self.full = pos, layer, block, full
        self.sems = sems
        self.source = pos.s == layer

    def along(self, way, h):
        pos = self.pos
        j = pos.b - way * h
        to = pos.b + way
        real = (j >= 0) & (j < pos.ny) & (to >= 0) & (to < pos.ny)
        j = jnp.clip(j, 0, pos.ny - 1)
        src = self.block if h == 0 else self.full.at[j]
        copy = remote(src, self.full.at[j], self.sems[0].at[(way + 1) // 2, h], self.sems[1].at[j], (pos.s, pos.a, to))
        return real, j, copy

    def across(self, src, slot):
        pos = self.pos
        return remote(src, self.full.at[slot], self.sems[2].at[slot], self.sems[3].at[slot], (1 - pos.s, pos.a, pos.b))

    def start(self):
        b = self.pos.b

        @pl.when(self.source)
        def _():
            self.full[b] = self.block[...]
            for way in (-1, 1):
                real, _, copy = self.along(way, 0)
                pl.when(real)(copy.start)
            self.across(self.block, b).start()

    def hop(self, h):
        pos = self.pos

        @pl.when(self.source)
        def _():
            for way in (-1, 1):
                j = pos.b - way * h

                @pl.when((j >= 0) & (j < pos.ny))
                def _():
                    real, jc, copy = self.along(way, h)
                    copy.wait_recv()
                    pl.when(real)(copy.start)
                    self.across(self.full.at[jc], jc).start()

    def finish(self):
        pos = self.pos

        @pl.when(self.source)
        def _():
            for h in range(pos.ny - 1):
                for way in (-1, 1):
                    real, _, copy = self.along(way, h)
                    pl.when(real)(copy.wait_send)
            for j in range(pos.ny):
                self.across(self.block, j).wait_send()

        @pl.when(jnp.logical_not(self.source))
        def _():
            for j in range(pos.ny):
                self.across(self.full.at[j], j).wait_recv()


def share_sems(ny):
    return [flags((2, ny)), flags((ny,)), flags((ny,)), flags((ny,))]


def params(ids):
    return pltpu.CompilerParams(collective_id=ids, has_side_effects=True, vmem_limit_bytes=VMEM_BYTES)


def turn(t, cos, sin, rot, sign):
    hi = bf(t)
    lo = bf(t - hi.astype(jnp.float32))
    return bf(t * cos + sign * ((mm(hi, rot) + mm(lo, rot)) * sin))


def by_blocks(rows, full, cols, width, pw):
    total = None
    for j in range(full.shape[0]):
        part = mm(rows[:, j * pw : j * pw + width], full[j, :, cols])
        total = part if total is None else total + part
    return total


def forward_kernel(cfg, *refs):
    nx, ny, mbs, sub, width, pw, heads, features, experts, cap, f, sk, ak = cfg
    (tin, small_b, att_b, sh_b, routes, cos, sin, rot, win_a, wdt_a,
     win_b, wdt_b, tok_o, small_o, place_o, place_to, watt0_o, y_o, mid_o, n2_o, rows_o, q_o, k_o, v_o, att_o, slots_o, gu_o, hid_o, rows2_o, sgu_o, shid_o, shw_o, watt_o,
     y, mid, n2, rx, nsend, nall, proj, q, k, v, att, osend, orecv, rwx,
     xsend, xline, xall, nrows, pm, pt, slots, acc, gu, hid, eo, sgu, shid, ssend, srecv, rsend, rpeer, rline, rrecv,
     win, wdt, shw0, shw1, watt0, watt1, tbuf, tok, rts, place, place_t, sm0, sm1, small,
     n_send, n_recv, o_send, o_recv, x_send, x_recv, u_send, u_recv, t_send, t_recv, s_send, s_recv, g_send, g_recv, r_send, r_recv,
     rs_send, rs_recv, ag_send, ag_recv, wi_sem, wd_sem, g_sem, k_sem, i_send, i_recv, q_send, q_recv, v_send, v_recv, *w_sems) = refs
    pos = Position(nx, ny)
    s, a, b, me = pos.s, pos.a, pos.b, pos.me
    slots_n = experts * cap
    tokens = nx * ny * sub
    d = ny * pw
    length = nx * sub
    half, hw = experts // 2, f // 2
    lane = lax.broadcasted_iota(jnp.int32, (1, pw), 1)
    shares = (
        Share(pos, 0, sh_b, shw0, w_sems[0:4]),
        Share(pos, 1, att_b, watt1, w_sems[4:8]),
        Share(pos, 1, sh_b, shw1, w_sems[8:12]),
    )
    entry_shares = (
        Share(pos, 0, small_b, sm0, w_sems[12:16]),
        Share(pos, 1, small_b, sm1, w_sems[16:20]),
        Share(pos, 0, att_b, watt0, w_sems[20:24]),
    )
    watts, shws = (watt0, watt1), (shw0, shw1)
    barrier = pltpu.get_barrier_semaphore()
    pos.peers(lambda ai: pl.semaphore_signal(barrier, inc=1, device_id=(s, ai, b), device_id_type=MESH))
    pos.line(lambda bi: pl.semaphore_signal(barrier, inc=1, device_id=(s, a, bi), device_id_type=MESH))
    pl.semaphore_signal(barrier, inc=1, device_id=(1 - s, a, b), device_id_type=MESH)
    for j in range(ny):
        @pl.when((a != b) | (b != j))
        def _():
            pl.semaphore_signal(barrier, inc=1, device_id=(s, b, j), device_id_type=MESH)

    def weight_copy(layer, e, which):
        own, oth, dst, sem = ((win_a, win_b, win, wi_sem), (wdt_a, wdt_b, wdt, wd_sem))[which]
        return own.at[e], oth.at[e], dst.at[e], sem.at[e]

    def start_weight(layer, e, which):
        own, oth, dst, sem = weight_copy(layer, e, which)

        @pl.when(s == layer)
        def _():
            pltpu.make_async_copy(own, dst, sem).start()

        @pl.when(s != layer)
        def _():
            pltpu.make_async_copy(oth, dst, sem).start()

    def wait_weight(layer, e, which):
        own, oth, dst, sem = weight_copy(layer, e, which)
        pltpu.make_async_copy(own, dst, sem).wait()

    def first_weights(e, c):
        start_weight(0, e, 0)
        start_weight(0, e, 1)
        return c

    def swap(c):
        src, dst = ((win_a, win_b), (wdt_a, wdt_b))[c]
        return remote(src, dst, v_send.at[c], v_recv.at[c], (1 - s, a, b))

    def weights_ready():
        for c in range(2):
            swap(c).wait()
        lax.fori_loop(0, experts, first_weights, 0)

    @pl.when(a == b)
    def _():
        pl.semaphore_wait(barrier, nx - 1 + ny - 1 + 1 + nx - 1)

    @pl.when(a != b)
    def _():
        pl.semaphore_wait(barrier, nx - 1 + ny - 1 + 1 + nx)

    def tokens_copy(i, slot, seq):
        src = tin.at[:, :, pl.ds(pl.multiple_of(i * sub, sub), sub), :]
        return remote(src, tbuf.at[slot], i_send.at[i], i_recv.at[slot], (s, i, seq))

    def token_targets(do):
        for c in range(nx):
            i = lax.rem(a + c, nx)

            @pl.when((i != a) | (a != b))
            def _():
                do(tokens_copy(i, b, a))

    def routes_copy(src, slot):
        return remote(routes.at[pl.ds(src * mbs, mbs)], rts.at[slot], q_send, q_recv, (1 - s, a, b))

    token_targets(lambda copy: copy.start())
    routes_copy(1 - s, s).start()
    for share in entry_shares:
        share.start()
    for c in range(2):
        swap(c).start()
    rts[s] = routes[pl.ds(s * mbs, mbs)]

    @pl.when(a == b)
    def _():
        tbuf[b] = tin[:, :, pl.ds(pl.multiple_of(a * sub, sub), sub), :]

    routes_copy(0, 1 - s).wait()

    def places():
        t0 = lax.broadcasted_iota(jnp.int32, (tokens, tokens), 0)
        t1 = lax.broadcasted_iota(jnp.int32, (tokens, tokens), 1)
        before = bf((t1 < t0).astype(jnp.float32))
        after = bf((t0 < t1).astype(jnp.float32))
        er = lax.broadcasted_iota(jnp.int32, (experts, tokens), 0).astype(jnp.float32)
        ec = lax.broadcasted_iota(jnp.int32, (tokens, 128), 1).astype(jnp.float32)
        sub8 = lax.broadcasted_iota(jnp.int32, (128, tokens), 0)
        for l in range(2):
            for m in range(mbs):
                r = rts[l, m].astype(jnp.float32)
                rows = [r[c : c + 1] for c in range(2)]
                hot = [(row == er).astype(jnp.float32) for row in rows]
                count = mm(bf(hot[0] + hot[1]), after)
                cols = jnp.where(sub8 == 0, rows[0], jnp.where(sub8 == 1, rows[1], 0.0)).T
                cols = [cols[:, c : c + 1] for c in range(2)]
                hot_t = [(col == ec).astype(jnp.float32) for col in cols]
                count_t = mm(before, bf(hot_t[0] + hot_t[1]))
                for c in range(2):
                    rank = jnp.sum(hot[c] * count, axis=0, keepdims=True)
                    place[l, m, c : c + 1] = (rows[c] * cap + rank).astype(jnp.int32)
                    rank_t = jnp.sum(hot_t[c] * count_t, axis=1, keepdims=True)
                    place_t[l, m, :, c : c + 1] = (cols[c] * cap + rank_t).astype(jnp.int32)

    def tokens_ready():
        for j in range(ny):
            @pl.when((a != b) | (b != j))
            def _():
                tokens_copy(a, j, j).wait_recv()

            for kind in range(2):
                tok[kind, :, :, j * pw : (j + 1) * pw] = tbuf[j, kind]
        token_targets(lambda copy: copy.wait_send())

    def stream(l, m):
        return (tok[0, m] if l == 0 else y[0, m]).astype(jnp.float32)

    def copy_n(l, m, ai, slot):
        return remote(nsend.at[l, m], nall.at[l, m, slot], n_send.at[l, m, ai], n_recv.at[l, m, slot], (s, ai, b))

    def norm_first(l, m):
        xv = stream(l, m)
        nsend[l, m] = bf(xv * rms(xv, features) * small[l, experts + 1 : experts + 2])
        pos.peers(lambda ai: copy_n(l, m, ai, a).start())
        nall[l, m, a] = nsend[l, m]

    def copy_o(l, m, ai, slot):
        return remote(osend.at[l, m, ai], orecv.at[l, m, slot], o_send.at[l, m, ai], o_recv.at[l, m, slot], (s, ai, b))

    def attention(l, m):
        watt = watts[l]
        pos.peers(lambda ai: copy_n(l, m, ai, ai).wait())
        proj[...] = by_blocks(nall[l, m].reshape(length, d), watt, slice(0, 3 * pw), width, pw)
        v[l, m] = bf(proj[:, 2 * pw : 3 * pw])
        q[l, m] = turn(proj[:, :pw], cos[...], sin[...], rot[...], 1.0)
        k[l, m] = turn(proj[:, pw : 2 * pw], cos[...], sin[...], rot[...], 1.0)
        total = jnp.zeros((length, pw), jnp.float32)
        for h in range(heads):
            mask = head_mask(pw, h)
            p = probs_of(jnp.where(mask, q[l, m], 0), k[l, m])
            total = total + mm(bf(p), jnp.where(mask, v[l, m], 0))
        att[l, m] = bf(total)
        for j in range(ny):
            part = mm(att[l, m], watt[j, :, 3 * pw : 4 * pw], ((1,), (1,)))
            osend[l, m, :, :, j * pw : j * pw + width] = bf(part).reshape(nx, sub, width)
        pos.peers(lambda ai: copy_o(l, m, ai, a).start())
        orecv[l, m, a] = osend[l, m, a]

    def copy_x(l, m, bi, slot):
        return remote(xsend.at[l, m, bi], xline.at[l, m, slot], x_send.at[l, m, bi], x_recv.at[l, m, slot], (s, a, bi))

    def copy_w(l, m, ai, slot):
        return remote(xline.at[l, m], xall.at[l, m, :, slot], u_send.at[l, m, ai], u_recv.at[l, m, slot], (s, ai, b))

    def copy_t(l, m, ai, slot):
        return remote(n2.at[l, m], nrows.at[l, m, slot], t_send.at[l, m, ai], t_recv.at[l, m, slot], (s, ai, b))

    def norm_second(l, m):
        pos.peers(lambda ai: copy_o(l, m, ai, ai).wait())
        mv = stream(l, m)
        for ai in range(nx):
            mv = mv + orecv[l, m, ai].astype(jnp.float32)
        mid[l, m] = mv
        n2v = bf(mv * rms(mv, features) * small[l, experts : experts + 1])
        n2[l, m] = n2v
        rv = mm(n2v, rwx[l], ((1,), (1,)))
        hi = bf(rv)
        lo = bf(rv - hi.astype(jnp.float32))
        tail = jnp.where(lane < width + experts, hi, lo)
        for j in range(ny):
            xsend[l, m, j] = jnp.where(lane < width, n2v[:, j * pw : (j + 1) * pw], tail)
        pos.line(lambda bi: copy_x(l, m, bi, b).start())
        xline[l, m, b] = xsend[l, m, b]
        pos.peers(lambda ai: copy_t(l, m, ai, a).start())
        nrows[l, m, a] = n2[l, m]

    def spread(l, m):
        pos.line(lambda bi: copy_x(l, m, bi, bi).wait())
        pos.peers(lambda ai: copy_w(l, m, ai, a).start())
        xall[l, m, :, a] = xline[l, m]

    def dispatch(l, m):
        i0 = lax.broadcasted_iota(jnp.int32, (slots_n, tokens), 0)
        pm[...] = bf(((place[l, m, 0:1] == i0) | (place[l, m, 1:2] == i0)).astype(jnp.float32))
        pos.peers(lambda ai: copy_w(l, m, ai, ai).wait())
        slots[l, m] = bf(mm(pm[...], xall[l, m].reshape(tokens, pw))).reshape(experts, cap, pw)

    def shared_in_part(l, m):
        pos.peers(lambda ai: copy_t(l, m, ai, ai).wait())
        shw = shws[l]
        gu_s = by_blocks(nrows[l, m].reshape(length, d), shw, slice(0, 2 * f), width, pw)
        sgu[l, m] = bf(gu_s)
        gate = gu_s[:, :f]
        shid[l, m] = bf(gate * jax.nn.sigmoid(gate) * gu_s[:, f:])

    def copy_s(l, m, ai, slot):
        return remote(ssend.at[l, m, ai], srecv.at[l, m, slot], s_send.at[l, m, ai], s_recv.at[l, m, slot], (s, ai, b))

    def shared_out_part(l, m):
        for j in range(ny):
            part = mm(shid[l, m], shws[l][j, :, 2 * f :], ((1,), (1,)))
            ssend[l, m, :, :, j * pw : j * pw + width] = bf(part).reshape(nx, sub, width)
        pos.peers(lambda ai: copy_s(l, m, ai, a).start())
        srecv[l, m, a] = ssend[l, m, a]

    def copy_g(l, m, ai, slot):
        return remote(rsend.at[l, m, ai], rpeer.at[l, m, slot], g_send.at[l, m, ai], g_recv.at[l, m, slot], (s, ai, b))

    def copy_r(l, m, bi, slot):
        return remote(rline.at[l, m, bi], rrecv.at[l, m, slot], r_send.at[l, m, bi], r_recv.at[l, m, slot], (s, a, bi))

    def combine(l, m):
        i1 = lax.broadcasted_iota(jnp.int32, (tokens, slots_n), 1)
        pt[...] = bf(((place_t[l, m, :, 0:1] == i1) | (place_t[l, m, :, 1:2] == i1)).astype(jnp.float32))
        br = mm(pt[...], eo[m].reshape(slots_n, width))
        for ai in range(nx):
            rsend[l, m, ai, :, :, :width] = bf(br).reshape(ny, nx, sub, width)[:, ai]
        pos.peers(lambda ai: copy_g(l, m, ai, a).start())
        rpeer[l, m, a] = rsend[l, m, a]

    def combine_line(l, m):
        pos.peers(lambda ai: copy_g(l, m, ai, ai).wait())
        total = rpeer[l, m, 0].astype(jnp.float32)
        for ai in range(1, nx):
            total = total + rpeer[l, m, ai].astype(jnp.float32)
        rline[l, m] = bf(total)
        pos.line(lambda bi: copy_r(l, m, bi, b).start())
        rrecv[l, m, b] = rline[l, m, b]

    def layer_out(l, m):
        pos.peers(lambda ai: copy_s(l, m, ai, ai).wait())
        pos.line(lambda bi: copy_r(l, m, bi, bi).wait())
        total = mid[l, m]
        for ai in range(nx):
            total = total + srecv[l, m, ai].astype(jnp.float32)
        for j in range(ny):
            part = total[:, j * pw : (j + 1) * pw]
            part = part + jnp.where(lane < width, rrecv[l, m, j].astype(jnp.float32), 0.0)
            y[l, m, :, j * pw : (j + 1) * pw] = bf(part)

    first = (b == ny - 1, b == 0)
    last = (b == 0, b == ny - 1)
    up = (ny - 1 - b, b)
    down = (b, ny - 1 - b)
    lag = (sk + ak) * (ny - 1)
    apart = STAGE_STEPS
    units = 2 * half
    gap = max(lag + 6 * apart - units, 0)
    starts = (0, units, 2 * units + gap, 3 * units + gap)
    steps = starts[3] + units + lag

    def unit(t, dd):
        early = (t >= 0) & (t < 2 * units)
        late = (t >= starts[2]) & (t < starts[2] + 2 * units)
        u = jnp.clip(jnp.where(t < starts[2], jnp.minimum(t, 2 * units - 1), t - gap), 0, 4 * units - 1)
        job, r = u // units, lax.rem(u, units)
        return early | late, job // 2, lax.rem(job, 2), r // 2 + dd * half, lax.rem(r, 2)

    def gu_copy(dd, l, m, e, c):
        to = b - 1 if dd == 0 else b + 1
        return remote(gu.at[l, m, e, c], gu.at[l, m, e, c], rs_send.at[l, m, e, c], rs_recv.at[l, m, e, c], (s, a, to))

    def hid_copy(dd, l, m, e, c):
        to = b + 1 if dd == 0 else b - 1
        return remote(hid.at[l, m, e, c], hid.at[l, m, e, c], ag_send.at[l, m, e, c], ag_recv.at[l, m, e, c], (s, a, to))

    def save_gates(l, m, e, c):
        return pltpu.make_async_copy(gu.at[l, m, e, c], gu_o.at[l, m, e, c], g_sem.at[l, m, e, c])

    def chain(i):
        reduce = [unit(i - sk * up[dd], dd) for dd in range(2)]
        spreads = [unit(i - sk * (ny - 1) - ak * down[dd], dd) for dd in range(2)]
        for dd in range(2):
            valid, l, m, e, c = reduce[dd]

            @pl.when(valid)
            def _():
                @pl.when((m == 0) & (c == 0))
                def _():
                    wait_weight(0, e, 0)

                for plane in range(2):
                    part = win[e, plane, :, pl.ds(pl.multiple_of(c * hw, hw), hw)]
                    acc[dd, :, plane * hw : (plane + 1) * hw] = mm(slots[l, m, e, :, :width], part)

                @pl.when((l == 0) & (m == 1) & (c == 1))
                def _():
                    start_weight(1, e, 0)

        for dd in range(2):
            valid, l, m, e, c = reduce[dd]

            @pl.when(valid & first[dd])
            def _():
                gu[l, m, e, c] = bf(acc[dd])
                gu_copy(dd, l, m, e, c).start()

            @pl.when(valid & jnp.logical_not(first[dd] | last[dd]))
            def _():
                gu_copy(dd, l, m, e, c).wait_recv()
                gu[l, m, e, c] = bf(acc[dd] + gu[l, m, e, c].astype(jnp.float32))
                gu_copy(dd, l, m, e, c).start()

            @pl.when(valid & last[dd])
            def _():
                gu_copy(dd, l, m, e, c).wait_recv()
                total = acc[dd] + gu[l, m, e, c].astype(jnp.float32)
                r = router_column(slots[l, m, e], e, width, experts)
                gate = total[:, :hw]
                hid[l, m, e, c] = bf(gate * jax.nn.sigmoid(gate) * total[:, hw:] * jax.nn.sigmoid(r))
                hid_copy(dd, l, m, e, c).start()
                gu[l, m, e, c] = bf(total)
                save_gates(l, m, e, c).start()

        for dd in range(2):
            valid, l, m, e, c = spreads[dd]

            @pl.when(valid & jnp.logical_not(last[dd]))
            def _():
                hid_copy(dd, l, m, e, c).wait_recv()

                @pl.when(jnp.logical_not(first[dd]))
                def _():
                    hid_copy(dd, l, m, e, c).start()

        for dd in range(2):
            valid, l, m, e, c = spreads[dd]

            @pl.when(valid & (c == 1))
            def _():
                @pl.when(m == 0)
                def _():
                    wait_weight(0, e, 1)

                total = mm(hid[l, m, e, 0], wdt[e, :, :hw], ((1,), (1,)))
                eo[m, e] = bf(total + mm(hid[l, m, e, 1], wdt[e, :, hw:], ((1,), (1,))))

                @pl.when((l == 0) & (m == 1))
                def _():
                    start_weight(1, e, 1)

    kept = [
        (mid, mid_o), (n2, n2_o), (nall, rows_o), (q, q_o), (k, k_o), (v, v_o), (att, att_o), (slots, slots_o),
        (hid, hid_o), (nrows, rows2_o), (sgu, sgu_o), (shid, shid_o), (y, y_o),
    ]
    stages = {}

    def at(step, do):
        stages.setdefault(step, []).append(do)

    def stage(do, l, m):
        return lambda: do(l, m)

    osend[...] = jnp.zeros_like(osend)
    ssend[...] = jnp.zeros_like(ssend)
    rwx[...] = jnp.zeros_like(rwx)
    for h in range(1, ny):
        for share in entry_shares[:2]:
            share.hop(h)
        if h == 2:
            entry_shares[2].hop(1)
    for share in entry_shares[:2]:
        share.finish()
    tokens_ready()
    for l, full in enumerate((sm0, sm1)):
        for j in range(ny):
            small[l, :, j * pw : (j + 1) * pw] = full[j]
    for l in range(2):
        rwx[l, width : width + experts] = bf(small[l, :experts])
        rwx[l, width + experts : width + 2 * experts] = bf(small[l, :experts])
    norm_first(0, 0)
    norm_first(0, 1)
    entry_shares[2].hop(2)
    places()
    entry_shares[2].hop(3)
    entry_shares[2].finish()
    shares[0].start()
    shares[1].start()
    attention(0, 0)
    attention(0, 1)
    norm_second(0, 0)
    norm_second(0, 1)
    weights_ready()
    spread(0, 0)
    shares[0].hop(1)
    shares[1].hop(1)
    spread(0, 1)
    dispatch(0, 0)
    for h in range(2, ny):
        at(2 * (h - 2), lambda h=h: (shares[0].hop(h), shares[1].hop(h)))
    at(units // 4, stage(dispatch, 0, 1))
    at(2 * (ny - 2) + 1, lambda: (shares[0].finish(), shares[1].finish()))
    at(units // 2, stage(shared_in_part, 0, 0))
    at(units // 2 + 2, stage(shared_out_part, 0, 0))
    at(units, stage(shared_in_part, 0, 1))
    at(units + 2, stage(shared_out_part, 0, 1))
    for m in range(2):
        done = starts[m] + units - 1 + lag
        for c, do in enumerate((combine, combine_line)):
            at(done + c * apart, stage(do, 0, m))
        at(done + 2 * apart, stage(layer_out, 0, m))
        for c, do in enumerate((norm_first, attention, norm_second, spread, dispatch)):
            at(done + (2 + c) * apart, stage(do, 1, m))
        at(starts[2 + m] + 4, stage(shared_in_part, 1, m))
        at(starts[2 + m] + 8, stage(shared_out_part, 1, m))
        done = starts[2 + m] + units - 1 + lag
        for c, do in enumerate((combine, combine_line, layer_out)):
            at(done + c * apart, stage(do, 1, m))
    at(units + lag - 1, shares[2].start)
    for h in range(1, ny):
        at(units + lag - 1 + 2 * h, lambda h=h: shares[2].hop(h))
    at(units + lag - 1 + 2 * ny, shares[2].finish)

    def step(i, c):
        chain(i)
        for when in sorted(stages):
            if when < steps:
                @pl.when(i == when)
                def _():
                    for do in stages[when]:
                        do()

        return c

    lax.fori_loop(0, steps, step, 0)
    for when in sorted(stages):
        if when >= steps:
            for do in stages[when]:
                do()
    kept += [(shw0, shw_o.at[0]), (shw1, shw_o.at[1]), (watt1, watt_o), (watt0, watt0_o), (tok, tok_o), (small, small_o)]
    kept += [(place, place_o), (place_t, place_to)]
    saves = [pltpu.make_async_copy(src, dst, k_sem.at[i]) for i, (src, dst) in enumerate(kept)]
    for copy in saves:
        copy.start()

    def finish(index, carry):
        l = index // (mbs * units)
        m = lax.rem(index // units, mbs)
        r = lax.rem(index, units)
        for dd in range(2):
            e, c = r // 2 + dd * half, lax.rem(r, 2)
            pl.when(jnp.logical_not(last[dd]))(gu_copy(dd, l, m, e, c).wait_send)
            pl.when(jnp.logical_not(first[dd]))(hid_copy(dd, l, m, e, c).wait_send)
            pl.when(last[dd])(save_gates(l, m, e, c).wait)
        return carry

    lax.fori_loop(0, 2 * mbs * units, finish, 0)
    for copy in saves:
        copy.wait()


def forward(tin, small_b, att_block, sh_block, routes, cos, sin, rot, win, wdt, dims, heads, features, ids):
    width, pw, experts, cap = dims
    nx, ny = lax.axis_size("gx"), lax.axis_size("gy")
    mbs, length = tin.shape[1:3]
    sub, d = length // nx, ny * pw
    f = wdt.shape[-1]
    length, tokens, n, slots = nx * sub, nx * ny * sub, nx * ny, experts * cap
    b16, f32 = jnp.bfloat16, jnp.float32
    vm = pl.BlockSpec(memory_space=pltpu.VMEM)
    hbm = pl.BlockSpec(memory_space=pl.ANY)
    lm = (2, mbs)
    rows_shape = lm + (nx, sub, d)
    spread_shape = lm + (ny, nx, sub, pw)
    entry = (
        (win.shape, b16), (wdt.shape, b16),
        ((2, mbs, sub, d), b16), ((2, small_b.shape[0], d), f32), (lm + (2, tokens), jnp.int32),
        (lm + (tokens, 2), jnp.int32), ((ny,) + att_block.shape, b16),
    )
    kept = entry + (
        (lm + (sub, d), b16), (lm + (sub, d), f32), (lm + (sub, d), b16), (rows_shape, b16),
        (lm + (length, pw), b16), (lm + (length, pw), b16), (lm + (length, pw), b16), (lm + (length, pw), b16),
        (lm + (experts, cap, pw), b16), (lm + (experts, 2, cap, f), b16), (lm + (experts, 2, cap, f // 2), b16),
        (rows_shape, b16), (lm + (length, 2 * f), b16), (lm + (length, f), b16),
        ((2, ny) + sh_block.shape, b16), ((ny,) + att_block.shape, b16),
    )
    scratch = (
        (lm + (sub, d), b16), (lm + (sub, d), f32), (lm + (sub, d), b16), None,
        (lm + (sub, d), b16), (rows_shape, b16), ((length, 3 * pw), f32),
        (lm + (length, pw), b16), (lm + (length, pw), b16), (lm + (length, pw), b16), (lm + (length, pw), b16),
        (rows_shape, b16), (rows_shape, b16), ((2, pw, d), b16),
        (lm + (ny, sub, pw), b16), (lm + (ny, sub, pw), b16), (spread_shape, b16), (rows_shape, b16),
        ((slots, tokens), b16), ((tokens, slots), b16), (lm + (experts, cap, pw), b16), ((2, cap, f), f32),
        (lm + (experts, 2, cap, f), b16), (lm + (experts, 2, cap, f // 2), b16), ((mbs, experts, cap, width), b16),
        (lm + (length, 2 * f), b16), (lm + (length, f), b16), (rows_shape, b16), (rows_shape, b16),
        (lm + (nx, ny, sub, pw), b16), (lm + (nx, ny, sub, pw), b16), (lm + (ny, sub, pw), b16), (lm + (ny, sub, pw), b16),
        (win.shape, b16), (wdt.shape, b16),
        ((ny,) + sh_block.shape, b16), ((ny,) + sh_block.shape, b16), ((ny,) + att_block.shape, b16), ((ny,) + att_block.shape, b16),
        ((ny, 2, mbs, sub, pw), b16), ((2, mbs, sub, d), b16), (lm + (2, tokens), jnp.int32),
        (lm + (2, tokens), jnp.int32), (lm + (tokens, 2), jnp.int32),
        ((ny,) + small_b.shape, f32), ((ny,) + small_b.shape, f32), ((2, small_b.shape[0], d), f32),
    )
    outs = pl.pallas_call(
        functools.partial(forward_kernel, (nx, ny, mbs, sub, width, pw, heads, features, experts, cap, f, *FWD_SKEW)),
        out_shape=tuple(jax.ShapeDtypeStruct(*v) for v in kept),
        in_specs=[vm] * 8 + [hbm] * 2,
        out_specs=(hbm,) * len(kept),
        scratch_shapes=[pltpu.VMEM(*(v or ((8, 128), f32))) for v in scratch] + [
            flags(lm + (nx,)), flags(lm + (nx,)), flags(lm + (nx,)), flags(lm + (nx,)),
            flags(lm + (ny,)), flags(lm + (ny,)), flags(lm + (nx,)), flags(lm + (nx,)), flags(lm + (nx,)), flags(lm + (nx,)),
            flags(lm + (nx,)), flags(lm + (nx,)), flags(lm + (nx,)), flags(lm + (nx,)), flags(lm + (ny,)), flags(lm + (ny,)),
            flags(lm + (experts, 2)), flags(lm + (experts, 2)), flags(lm + (experts, 2)), flags(lm + (experts, 2)),
            flags((experts,)), flags((experts,)), flags(lm + (experts, 2)), flags((24,)),
            flags((nx,)), flags((ny,)), pltpu.SemaphoreType.DMA, pltpu.SemaphoreType.DMA, flags((2,)), flags((2,)),
        ] + share_sems(ny) * 6,
        compiler_params=params(ids),
        cost_estimate=pl.CostEstimate(flops=10**10, bytes_accessed=8 * 10**7, transcendentals=10**6),
        name="forward",
    )(tin, small_b, att_block, sh_block, routes, cos, sin, rot, win, wdt)
    names = ("win", "wdt", "tok", "small", "place", "place_t", "watt0", "y", "mid", "n2", "rows", "q", "k", "v", "att", "slots", "gu", "hid", "rows2", "sgu", "shid", "shw", "watt1")
    return dict(zip(names, outs))


FWD_SKEW = (2, 2)
STAGE_STEPS = 2


def backward_kernel(cfg, *refs):
    nx, ny, mbs, sub, width, pw, heads, features, experts, cap, f, sk, ak = cfg
    (tok_i, small_i, place_i, y_i, mid_i, n2_i, rows_i, q_i, k_i, v_i, att_i, rows2_i, sgu_i, shid_i, shw_i,
     watt0_i, watt1_i, cos, sin, rot, slots_i, gu_i, hid_i, win_a, win_b, wdt_a, wdt_b) = refs[:27]
    (out_o, win_g, wdt_g, att_g, sh_g, small_g,
     win, wdt, xsend, xline, xall, grows, pm, pt, slots, gslots, gown, hid, acc, dh, dgu, deo, sti, std,
     dsgu, ssend, srecv, rsend, rpeer, rline, rrecv, rwx, dm, msend, mall, datt, dqkv, dsend, drecv,
     rw_p, gains, drs, sh_p, att_p, small_p, sh_x, att_x, small_x, sh_r, att_r, small_r, sh_f, att_f, small_f, small_a,
     yv, obuf, g, gx, small, place, x, mid, n2, rows, q, k, v, att, rows2, sgu, shid, shw, watt,
     w_sem, x_send, x_recv, u_send, u_recv, t_send, t_recv, s_send, s_recv, g_send, g_recv, r_send, r_recv,
     m_send, m_recv, d_send, d_recv, rs_send, rs_recv, ag_send, ag_recv, wi_send, wi_recv, wd_send, wd_recv,
     c_send, c_recv, e_send, e_recv, a_send, a_recv, l_sem, st_sem, f_sem, y_sem, o_send, o_recv, free) = refs[27:]
    pos = Position(nx, ny)
    s, a, b = pos.s, pos.a, pos.b
    slots_n = experts * cap
    tokens = nx * ny * sub
    d = ny * pw
    length = nx * sub
    half, hw = experts // 2, f // 2
    scale = DH ** -0.5
    lane = lax.broadcasted_iota(jnp.int32, (1, pw), 1)
    first = (b == ny - 1, b == 0)
    last = (b == 0, b == ny - 1)
    up = (ny - 1 - b, b)
    down = (b, ny - 1 - b)
    barrier = pltpu.get_barrier_semaphore()
    pos.peers(lambda ai: pl.semaphore_signal(barrier, inc=1, device_id=(s, ai, b), device_id_type=MESH))
    pos.line(lambda bi: pl.semaphore_signal(barrier, inc=1, device_id=(s, a, bi), device_id_type=MESH))
    pl.semaphore_signal(barrier, inc=1, device_id=(1 - s, a, b), device_id_type=MESH)
    for so in range(2):
        for i in range(nx):
            @pl.when((so != s) | (i != a) | (a != b))
            def _():
                pl.semaphore_signal(barrier, inc=1, device_id=(so, i, a), device_id_type=MESH)

    def weight_copy(l, e, which):
        own, oth, dst = ((win_a, win_b, win), (wdt_a, wdt_b, wdt))[which]
        sem = w_sem.at[which, e]
        return pltpu.make_async_copy(own.at[e], dst.at[e], sem), pltpu.make_async_copy(oth.at[e], dst.at[e], sem)

    def start_weights(l, e):
        for which in range(2):
            own, oth = weight_copy(l, e, which)
            pl.when(s == l)(own.start)
            pl.when(s != l)(oth.start)

    def first_weights(e, c):
        start_weights(1, e)
        return c

    lax.fori_loop(0, experts, first_weights, 0)

    early = ((rows2_i, rows2), (sgu_i, sgu), (shid_i, shid), (shw_i, shw))
    later = ((mid_i, mid), (n2_i, n2), (rows_i, rows), (q_i, q), (k_i, k), (v_i, v), (att_i, att))

    def early_loads(l):
        return [pltpu.make_async_copy(src.at[l], dst, y_sem.at[c]) for c, (src, dst) in enumerate(early)]

    def later_loads(l):
        copies = [pltpu.make_async_copy(src.at[l], dst, y_sem.at[4 + c]) for c, (src, dst) in enumerate(later)]
        copies.append(pltpu.make_async_copy(y_i.at[0] if l else tok_i.at[0], x, y_sem.at[11]))
        return copies + [pltpu.make_async_copy(watt1_i if l else watt0_i, watt, y_sem.at[12])]

    def hid_load(l):
        return pltpu.make_async_copy(hid_i.at[l], hid, l_sem.at[1])

    def gates(l, m, dd):
        return pltpu.make_async_copy(gu_i.at[l, m, pl.ds(dd * half, half)], gown.at[m], l_sem.at[2 + m])

    def start_gates(l, m):
        for dd in range(2):
            pl.when(last[dd])(gates(l, m, dd).start)

    def wait_gates(l, m):
        for dd in range(2):
            pl.when(last[dd])(gates(l, m, dd).wait)

    first_loads = [
        pltpu.make_async_copy(src, dst, y_sem.at[13 + c])
        for c, (src, dst) in enumerate(((tok_i.at[1], g), (small_i, small), (place_i, place), (y_i, yv)))
    ]
    slots_load = pltpu.make_async_copy(slots_i, slots, l_sem.at[0])
    for copy in first_loads + [slots_load, hid_load(1)] + early_loads(1) + later_loads(1):
        copy.start()
    for m in range(mbs):
        start_gates(1, m)

    def copy_x(m, bi, slot):
        return remote(xsend.at[m, bi], xline.at[m, slot], x_send.at[m, bi], x_recv.at[m, slot], (s, a, bi))

    def copy_w(m, ai, slot):
        return remote(xline.at[m], xall.at[m, :, slot], u_send.at[m, ai], u_recv.at[m, slot], (s, ai, b))

    def copy_t(m, ai, slot):
        return remote(g.at[m], grows.at[m, slot], t_send.at[m, ai], t_recv.at[m, slot], (s, ai, b))

    for copy in first_loads:
        copy.wait()

    @pl.when(a == b)
    def _():
        pl.semaphore_wait(barrier, nx - 1 + ny - 1 + 1 + 2 * ny - 1)

    @pl.when(a != b)
    def _():
        pl.semaphore_wait(barrier, nx - 1 + ny - 1 + 1 + 2 * ny)

    def out_copy(kind, l, j, s_slot, a_slot):
        src = (yv, gx)[kind].at[l, :, :, pl.ds(j * pw, pw)]
        return remote(src, obuf.at[kind, s_slot, a_slot], o_send.at[kind, l, j], o_recv.at[kind, s_slot, a_slot], (l, b, j))

    def send_out(kind, l):
        for j in range(ny):
            @pl.when((l != s) | (a != b) | (j != b))
            def _():
                out_copy(kind, l, j, s, a).start()

        @pl.when((l == s) & (a == b))
        def _():
            obuf[kind, s, a] = (yv, gx)[kind][l, :, :, pl.ds(pl.multiple_of(b * pw, pw), pw)]

    def sent_out(kind, l):
        for j in range(ny):
            @pl.when((l != s) | (a != b) | (j != b))
            def _():
                out_copy(kind, l, j, s, a).wait_send()

    def take_out(kind):
        for so in range(2):
            for i in range(nx):
                @pl.when((so != s) | (a != b) | (i != a))
                def _():
                    out_copy(kind, 0, 0, so, i).wait_recv()

                out_o[kind, so * mbs : (so + 1) * mbs, i * sub : (i + 1) * sub, :] = obuf[kind, so, i]

    def send_g(m):
        for j in range(ny):
            xsend[m, j] = g[m, :, j * pw : (j + 1) * pw]
        pos.line(lambda bi: copy_x(m, bi, b).start())
        xline[m, b] = xsend[m, b]
        pos.peers(lambda ai: copy_t(m, ai, a).start())
        grows[m, a] = g[m]

    send_g(0)
    send_g(1)
    deo[...] = jnp.zeros_like(deo)
    ssend[...] = jnp.zeros_like(ssend)
    dsend[...] = jnp.zeros_like(dsend)
    rwx[...] = jnp.zeros_like(rwx)

    def new_layer(l):
        rwx[width : width + experts] = bf(small[l, :experts])
        rwx[width + experts : width + 2 * experts] = bf(small[l, :experts])
        rw_p[...] = jnp.zeros_like(rw_p)
        gains[...] = jnp.zeros_like(gains)

    new_layer(1)

    def spread(m):
        pos.line(lambda bi: copy_x(m, bi, bi).wait())
        pos.peers(lambda ai: copy_w(m, ai, a).start())
        xall[m, :, a] = xline[m]

    def dispatch(l, m):
        i0 = lax.broadcasted_iota(jnp.int32, (slots_n, tokens), 0)
        pm[...] = bf(((place[l, m, 0:1] == i0) | (place[l, m, 1:2] == i0)).astype(jnp.float32))
        pos.peers(lambda ai: copy_w(m, ai, ai).wait())
        gslots[l, m] = bf(mm(pm[...], xall[m].reshape(tokens, pw))).reshape(experts, cap, pw)

    def shared_act(m):
        pos.peers(lambda ai: copy_t(m, ai, ai).wait())
        dsh = by_blocks(grows[m].reshape(length, d), shw, slice(2 * f, 3 * f), width, pw)
        dsg, dsu, _ = act_back(sgu[m, :, :f].astype(jnp.float32), sgu[m, :, f:].astype(jnp.float32), dsh, None)
        dsgu[m, :, :f] = bf(dsg)
        dsgu[m, :, f:] = bf(dsu)

    def copy_s(m, ai, slot):
        return remote(ssend.at[m, ai], srecv.at[m, slot], s_send.at[m, ai], s_recv.at[m, slot], (s, ai, b))

    def shared_back(m):
        for j in range(ny):
            part = mm(dsgu[m], shw[j, :, : 2 * f], ((1,), (1,)))
            ssend[m, :, :, j * pw : j * pw + width] = bf(part).reshape(nx, sub, width)
        pos.peers(lambda ai: copy_s(m, ai, a).start())
        srecv[m, a] = ssend[m, a]

    crossing = ((sh_p, sh_x), (att_p, att_x), (small_p, small_x))
    places = (sh_r, att_r, small_r)
    finals = (sh_f, att_f, small_f)
    results = (sh_g, att_g, small_g)

    def cross(l, i):
        return remote(crossing[i][0], crossing[i][1], c_send.at[i], c_recv.at[i], (l, a, b))

    def block(i, bi):
        if i == 2:
            return small_x.at[:, pl.ds(pl.multiple_of(bi * pw, pw), pw)]
        return crossing[i][1].at[bi]

    def along(i, bi, slot):
        return remote(block(i, bi), places[i].at[slot], e_send.at[i, bi], e_recv.at[i, slot], (s, a, bi))

    def give(l, i):
        pl.when(s != l)(cross(l, i).start)

    def given(l):
        for i in range(3):
            pl.when(s != l)(cross(l, i).wait_send)

    def join(l, i):
        @pl.when(s == l)
        def _():
            cross(l, i).wait_recv()
            part, other = crossing[i]
            other[...] = (part[...].astype(jnp.float32) + other[...].astype(jnp.float32)).astype(other.dtype)
            pos.line(lambda bi: along(i, bi, lax.rem(b - bi + ny, ny) - 1).start())

    def settle(l, i):
        @pl.when(s == l)
        def _():
            pos.line(lambda bi: along(i, bi, lax.rem(bi - b + ny, ny) - 1).wait())
            total = block(i, b)[...].astype(jnp.float32)
            for c in range(1, ny):
                total = total + places[i][c - 1].astype(jnp.float32)
            finals[i][...] = total
            if i < 2:
                pltpu.make_async_copy(finals[i], results[i], f_sem.at[i]).start()

    def shared_grads():
        for j in range(ny):
            rj = rows2[:, :, :, j * pw : j * pw + width].reshape(mbs * length, width)
            sh_p[j, :, : 2 * f] = bf(mm(rj, dsgu[...].reshape(mbs * length, 2 * f), ((0,), (0,))))

    def down_grads(l):
        for j in range(ny):
            gj = grows[:, :, :, j * pw : j * pw + width].reshape(mbs * length, width)
            sh_p[j, :, 2 * f :] = bf(mm(gj, shid[...].reshape(mbs * length, f), ((0,), (0,))))
        give(l, 0)

    def copy_g(m, ai, slot):
        return remote(rsend.at[m, ai], rpeer.at[m, slot], g_send.at[m, ai], g_recv.at[m, slot], (s, ai, b))

    def copy_r(m, bi, slot):
        return remote(rline.at[m, bi], rrecv.at[m, slot], r_send.at[m, bi], r_recv.at[m, slot], (s, a, bi))

    def combine(l, m):
        row = lax.broadcasted_iota(jnp.int32, (128, tokens), 0)
        pair = place[l, m].astype(jnp.float32)
        cols = jnp.where(row == 0, pair[0:1], jnp.where(row == 1, pair[1:2], 0.0)).T.astype(jnp.int32)
        part = tokens // 2
        i1 = lax.broadcasted_iota(jnp.int32, (part, slots_n), 1)
        for c in range(2):
            these = cols[c * part : (c + 1) * part]
            pt[...] = bf(((these[:, 0:1] == i1) | (these[:, 1:2] == i1)).astype(jnp.float32))
            br = bf(mm(pt[...], deo[m].reshape(slots_n, pw))).reshape(ny // 2, nx, sub, pw)
            for ai in range(nx):
                rsend[m, ai, c * (ny // 2) : (c + 1) * (ny // 2)] = br[:, ai]
        pos.peers(lambda ai: copy_g(m, ai, a).start())
        rpeer[m, a] = rsend[m, a]

    def combine_line(m):
        pos.peers(lambda ai: copy_g(m, ai, ai).wait())
        total = rpeer[m, 0].astype(jnp.float32)
        for ai in range(1, nx):
            total = total + rpeer[m, ai].astype(jnp.float32)
        rline[m] = bf(total)
        pos.line(lambda bi: copy_r(m, bi, b).start())
        rrecv[m, b] = rline[m, b]

    def copy_m(m, ai, slot):
        return remote(msend.at[m], mall.at[m, slot], m_send.at[m, ai], m_recv.at[m, slot], (s, ai, b))

    def second_norm(l, m):
        pos.peers(lambda ai: copy_s(m, ai, ai).wait())
        pos.line(lambda bi: copy_r(m, bi, bi).wait())
        dlog = jnp.zeros((sub, pw), jnp.float32)
        parts = []
        for j in range(ny):
            part = rrecv[m, j].astype(jnp.float32)
            dlog = dlog + jnp.where(lane >= width, part, 0.0)
            parts.append(jnp.where(lane < width, part, 0.0))
        hi = bf(dlog)
        lo = bf(dlog - hi.astype(jnp.float32))
        dn2 = jnp.concatenate(parts, 1) + mm(hi, rwx[...]) + mm(lo, rwx[...])
        for ai in range(nx):
            dn2 = dn2 + srecv[m, ai].astype(jnp.float32)
        rw_t = mm(hi, n2[m], ((0,), (0,))) + mm(lo, n2[m], ((0,), (0,)))
        rw_p[...] += rw_t[width : width + experts] + rw_t[width + experts : width + 2 * experts]
        mv = mid[m]
        dx2, gain_g = norm_back(mv, rms(mv, features), small[l, experts : experts + 1], dn2, features)
        gains[0:1] += gain_g
        dm[m] = g[m].astype(jnp.float32) + dx2
        msend[m] = bf(dm[m])
        pos.peers(lambda ai: copy_m(m, ai, a).start())
        mall[m, a] = msend[m]

    def copy_d(m, ai, slot):
        return remote(dsend.at[m, ai], drecv.at[m, slot], d_send.at[m, ai], d_recv.at[m, slot], (s, ai, b))

    def attention(m):
        pos.peers(lambda ai: copy_m(m, ai, ai).wait())
        datt[...] = bf(by_blocks(mall[m].reshape(length, d), watt, slice(3 * pw, 4 * pw), width, pw))
        dq = jnp.zeros((length, pw), jnp.float32)
        dk = dq
        dv = dq
        for h in range(heads):
            mask = head_mask(pw, h)
            qh = jnp.where(mask, q[m], 0)
            kh = jnp.where(mask, k[m], 0)
            da = jnp.where(mask, datt[...], 0)
            p = probs_of(qh, k[m])
            dp = mm(da, v[m], ((1,), (1,)))
            ds = bf(p * (dp - jnp.sum(dp * p, axis=1, keepdims=True)))
            dv = dv + mm(bf(p), da, ((0,), (0,)))
            dq = dq + mm(ds, kh)
            dk = dk + mm(ds, qh, ((0,), (0,)))
        dqkv[m, :, :pw] = turn(dq * scale, cos[...], sin[...], rot[...], -1.0)
        dqkv[m, :, pw : 2 * pw] = turn(dk * scale, cos[...], sin[...], rot[...], -1.0)
        dqkv[m, :, 2 * pw :] = bf(dv)
        for j in range(ny):
            part = mm(dqkv[m], watt[j, :, : 3 * pw], ((1,), (1,)))
            dsend[m, :, :, j * pw : j * pw + width] = bf(part).reshape(nx, sub, width)
        pos.peers(lambda ai: copy_d(m, ai, a).start())
        drecv[m, a] = dsend[m, a]

    def first_norm(l, m):
        pos.peers(lambda ai: copy_d(m, ai, ai).wait())
        dn1 = drecv[m, 0].astype(jnp.float32)
        for ai in range(1, nx):
            dn1 = dn1 + drecv[m, ai].astype(jnp.float32)
        xv = x[m].astype(jnp.float32)
        dx1, gain_g = norm_back(xv, rms(xv, features), small[l, experts + 1 : experts + 2], dn1, features)
        gains[1:2] += gain_g
        gx[l, m] = bf(dm[m] + dx1)
        if l:
            g[m] = gx[l, m]
            send_g(m)

    def attention_grads(l):
        for j in range(ny):
            cols = slice(j * pw, j * pw + width)
            rj = rows[:, :, :, cols].reshape(mbs * length, width)
            mj = mall[:, :, :, cols].reshape(mbs * length, width)
            att_p[j, :, : 3 * pw] = bf(mm(rj, dqkv[...].reshape(mbs * length, 3 * pw), ((0,), (0,))))
            att_p[j, :, 3 * pw :] = bf(mm(mj, att[...].reshape(mbs * length, pw), ((0,), (0,))))
        give(l, 1)

    def small_grads(l):
        small_p[:experts] = rw_p[...]
        small_p[experts:] = gains[...]
        give(l, 2)

    lag = (sk + ak) * (ny - 1)
    apart = STAGE_STEPS
    units = 2 * half
    gap = max(lag + 6 * apart - units, 0)
    starts = (0, units, 2 * units + gap, 3 * units + gap)

    def unit(t, dd):
        soon = (t >= 0) & (t < 2 * units)
        then = (t >= starts[2]) & (t < starts[2] + 2 * units)
        u = jnp.clip(jnp.where(t < starts[2], jnp.minimum(t, 2 * units - 1), t - gap), 0, 4 * units - 1)
        job, r = u // units, lax.rem(u, units)
        return soon | then, 1 - job // 2, lax.rem(job, 2), r // 2 + dd * half, lax.rem(r, 2)

    def dh_copy(dd, l, m, e, c):
        to = b - 1 if dd == 0 else b + 1
        return remote(dh.at[m, e, c], dh.at[m, e, c], rs_send.at[l, m, e, c], rs_recv.at[l, m, e, c], (s, a, to))

    def dgu_copy(dd, l, m, e, c):
        to = b + 1 if dd == 0 else b - 1
        return remote(dgu.at[m, e, c], dgu.at[m, e, c], ag_send.at[l, m, e, c], ag_recv.at[l, m, e, c], (s, a, to))

    def wi_copy(l, e):
        return remote(win.at[e], win.at[e], wi_send.at[l, e], wi_recv.at[l, e], (l, a, b))

    def wd_copy(l, e):
        return remote(wdt.at[e], wdt.at[e], wd_send.at[l, e], wd_recv.at[l, e], (l, a, b))

    def st_copies(e):
        return (pltpu.make_async_copy(sti, win_g.at[e], st_sem.at[0]), pltpu.make_async_copy(std, wdt_g.at[e], st_sem.at[1]))

    def weight_grads(l, e):
        sl = slots[l, :, e, :, :width].reshape(mbs * cap, width)
        gs = gslots[l, :, e, :, :width].reshape(mbs * cap, width)
        gi = [mm(sl, dgu[:, e, c].reshape(mbs * cap, f), ((0,), (0,))) for c in range(2)]
        gd = [mm(gs, hid[:, e, c].reshape(mbs * cap, hw), ((0,), (0,))) for c in range(2)]
        return gi, gd

    late = 2
    steps = starts[3] + units + lag + 2 * late

    def chain(i):
        reduce = [unit(i - sk * up[dd], dd) for dd in range(2)]
        spreads = [unit(i - sk * (ny - 1) - ak * down[dd], dd) for dd in range(2)]
        for dd in range(2):
            valid, l, m, e, c = reduce[dd]

            @pl.when(valid)
            def _():
                @pl.when((m == 0) & (c == 0))
                def _():
                    weight_copy(0, e, 1)[0].wait()

                acc[dd] = mm(gslots[l, m, e, :, :width], wdt[e, :, pl.ds(pl.multiple_of(c * hw, hw), hw)])

            @pl.when(valid & first[dd])
            def _():
                dh[m, e, c] = bf(acc[dd])
                dh_copy(dd, l, m, e, c).start()

            @pl.when(valid & jnp.logical_not(first[dd] | last[dd]))
            def _():
                dh_copy(dd, l, m, e, c).wait_recv()
                dh[m, e, c] = bf(acc[dd] + dh[m, e, c].astype(jnp.float32))
                dh_copy(dd, l, m, e, c).start()

            @pl.when(valid & last[dd])
            def _():
                dh_copy(dd, l, m, e, c).wait_recv()
                total = acc[dd] + dh[m, e, c].astype(jnp.float32)
                r = router_column(slots[l, m, e], e, width, experts)
                gate = gown[m, e - dd * half, c, :, :hw].astype(jnp.float32)
                upv = gown[m, e - dd * half, c, :, hw:].astype(jnp.float32)
                dgate, dup, dr = act_back(gate, upv, total, jax.nn.sigmoid(r))
                dgu[m, e, c, :, :hw] = bf(dgate)
                dgu[m, e, c, :, hw:] = bf(dup)
                dgu_copy(dd, l, m, e, c).start()
                dr = jnp.where(c == 0, 0.0, drs[dd][:, 0:1]) + dr
                drs[dd] = jnp.broadcast_to(dr, (cap, 128))
                hi = bf(dr).astype(jnp.float32)
                deo[m, e] = bf(jnp.where(lane == width + e, hi, jnp.where(lane == width + experts + e, dr - hi, 0.0)))

        for dd in range(2):
            valid, l, m, e, c = spreads[dd]

            @pl.when(valid & jnp.logical_not(last[dd]))
            def _():
                dgu_copy(dd, l, m, e, c).wait_recv()

                @pl.when(jnp.logical_not(first[dd]))
                def _():
                    dgu_copy(dd, l, m, e, c).start()

        for dd in range(2):
            valid, l, m, e, c = spreads[dd]

            @pl.when(valid & (c == 1))
            def _():
                @pl.when(m == 0)
                def _():
                    weight_copy(0, e, 0)[0].wait()

                total = None
                for c2 in range(2):
                    for plane in range(2):
                        cols, hcols = slice(plane * hw, (plane + 1) * hw), slice(c2 * hw, (c2 + 1) * hw)
                        part = mm(dgu[m, e, c2, :, cols], win[e, plane, :, hcols], ((1,), (1,)))
                        total = part if total is None else total + part
                deo[m, e, :, :width] = bf(total)

        for l in (1, 0):
            t = i - starts[3 - 2 * l] - lag
            weight_stage(l, t)

    def chain_sent(l, e, dd):
        for m in range(mbs):
            for c in range(2):
                pl.when(jnp.logical_not(last[dd]))(dh_copy(dd, l, m, e, c).wait_send)
                pl.when(jnp.logical_not(first[dd]))(dgu_copy(dd, l, m, e, c).wait_send)

    def weight_stage(l, t):
        u = t // 2
        on = (t >= 0) & (t < units) & (lax.rem(t + 2, 2) == 1)

        @pl.when(on)
        def _():
            for dd in range(2):
                chain_sent(l, jnp.clip(u, 0, half - 1) + dd * half, dd)

        @pl.when(on & (s == l))
        def _():
            pl.semaphore_signal(free.at[l], inc=1, device_id=(1 - s, a, b), device_id_type=MESH)

        @pl.when(on & (s != l))
        def _():
            pl.semaphore_wait(free.at[l], 1)
            for dd in range(2):
                e = jnp.clip(u, 0, half - 1) + dd * half
                gi, gd = weight_grads(l, e)
                for c in range(2):
                    for plane in range(2):
                        win[e, plane, :, c * hw : (c + 1) * hw] = bf(gi[c][:, plane * hw : (plane + 1) * hw])
                    wdt[e, :, c * hw : (c + 1) * hw] = bf(gd[c])
                wi_copy(l, e).start()
                wd_copy(l, e).start()

        t2 = t - 2 * late
        w = t2 // 2
        on2 = (t2 >= 0) & (t2 < units) & (lax.rem(t2 + 8, 2) == 1)

        @pl.when(on2 & (s != l))
        def _():
            for dd in range(2):
                e = jnp.clip(w, 0, half - 1) + dd * half
                wi_copy(l, e).wait_send()
                wd_copy(l, e).wait_send()
                if l:
                    start_weights(0, e)

        @pl.when(on2 & (s == l))
        def _():
            for dd in range(2):
                e = jnp.clip(w, 0, half - 1) + dd * half
                gi, gd = weight_grads(l, e)
                wi_copy(l, e).wait_recv()
                wd_copy(l, e).wait_recv()

                @pl.when((w >= 1) | (dd == 1))
                def _():
                    for copy in st_copies(e):
                        copy.wait()

                for c in range(2):
                    hcols = slice(c * hw, (c + 1) * hw)
                    for plane in range(2):
                        part = gi[c][:, plane * hw : (plane + 1) * hw] + win[e, plane, :, hcols].astype(jnp.float32)
                        sti[:, plane * f + c * hw : plane * f + (c + 1) * hw] = bf(part)
                    std[:, hcols] = bf(gd[c] + wdt[e, :, hcols].astype(jnp.float32))
                for copy in st_copies(e):
                    copy.start()
                if l:
                    start_weights(0, e)

    stages = {}

    def at(step, do, *args):
        stages.setdefault(step, []).append(lambda: do(*args))

    def shared_first(l, m):
        if m == 0:
            for copy in early_loads(l):
                copy.wait()
        shared_act(m)

    def reload(copies):
        for copy in copies:
            copy.start()

    def ready(copies):
        for copy in copies:
            copy.wait()

    spread(0)
    spread(1)
    dispatch(1, 0)
    ready([slots_load, hid_load(1)] + later_loads(1))
    for m in range(mbs):
        wait_gates(1, m)
    at(1, dispatch, 1, 1)
    for l in (1, 0):
        begin = starts[2 - 2 * l]
        second = starts[3 - 2 * l]
        at(begin + 3, shared_first, l, 0)
        at(begin + 5, shared_back, 0)
        at(second + (-10 if l else 1), shared_first, l, 1)
        at(second + (-8 if l else 3), shared_back, 1)
        at(second + (-6 if l else 5), shared_grads)
        at(second + (-4 if l else 6), down_grads, l)
        at(second + (1 if l else 9), join, l, 0)
        for m in range(2):
            done = starts[2 - 2 * l + m] + units - 1 + lag
            for c, (do, *args) in enumerate((
                    (combine, l, m), (combine_line, m), (second_norm, l, m), (attention, m), (first_norm, l, m))):
                at(done + c * apart, do, *args)
            if l:
                at(starts[m] + units + sk * (ny - 1), start_gates, 0, m)
                at(done + 5 * apart, spread, m)
                at(done + 6 * apart, dispatch, 0, m)
                at(starts[2 + m] - 1, wait_gates, 0, m)
        end = second + units - 1 + lag
        at(end + 3 * apart, attention_grads, l)
        at(end + 4 * apart, join, l, 1)
        at(end + 4 * apart, small_grads, l)
        at(end + 5 * apart, join, l, 2)
        at(end + (2 if l else 4) * apart, settle, l, 0)
        at(end + (10 if l else 5) * apart, settle, l, 1)
        at(end + (10 if l else 5) * apart, settle, l, 2)
        at(end + (6 if l else 5) * apart, given, l)
    at(units // 2 - 1, send_out, 0, 0)
    at(units // 2 + 1, send_out, 0, 1)
    at(2 * units, take_out, 0)
    end = starts[1] + units - 1 + lag
    at(end + 4 * apart + 1, send_out, 1, 1)
    at(starts[3] + units - 1 + lag + 4 * apart, send_out, 1, 0)
    at(starts[1] + 1, lambda: reload(early_loads(0)))
    at(end + 2 * late + 1, lambda: reload([hid_load(0)]))
    at(end + 2 * late + 8, lambda: ready([hid_load(0)]))
    at(end + 5 * apart, lambda: reload(later_loads(0)))
    at(end + 10 * apart, lambda: ready(later_loads(0)))
    at(end + 10 * apart, new_layer, 0)

    def step(i, c):
        chain(i)
        for when in sorted(stages):
            if when < steps:
                @pl.when(i == when)
                def _():
                    for do in stages[when]:
                        do()

        return c

    lax.fori_loop(0, steps, step, 0)
    for when in sorted(stages):
        if when >= steps:
            for do in stages[when]:
                do()

    def copy_a(ai, slot):
        return remote(small_f, small_a.at[slot], a_send.at[ai], a_recv.at[slot], (s, ai, b))

    def gain_sums():
        pos.peers(lambda ai: copy_a(ai, a).start())
        small_a[a] = small_f[...]
        pos.peers(lambda ai: copy_a(ai, ai).wait())
        total = small_a[0]
        for ai in range(1, nx):
            total = total + small_a[ai]
        small_f[...] = total

    gain_sums()
    pltpu.make_async_copy(small_f, small_g, f_sem.at[2]).start()
    take_out(1)
    for l in range(2):
        for kind in range(2):
            sent_out(kind, l)
    for i in range(3):
        pltpu.make_async_copy(finals[i], results[i], f_sem.at[i]).wait()
    for copy in st_copies(experts - 1):
        copy.wait()


def backward(fwd, cos, sin, rot, win, wdt, dims, heads, features, ids):
    width, pw, experts, cap = dims
    nx, ny = lax.axis_size("gx"), lax.axis_size("gy")
    mbs, sub, d = fwd["tok"].shape[-3:]
    f = wdt.shape[-1]
    length, tokens, slots = nx * sub, nx * ny * sub, experts * cap
    b16, f32 = jnp.bfloat16, jnp.float32
    vm = pl.BlockSpec(memory_space=pltpu.VMEM)
    hbm = pl.BlockSpec(memory_space=pl.ANY)
    ac, sc, n, half = fwd["watt0"].shape[2], fwd["shw"].shape[3], fwd["small"].shape[1], experts // 2
    rows_shape = (mbs, nx, sub, d)
    dense = lambda c: ((ny, width, c), b16)
    scratch = (
        (win.shape, b16), (wdt.shape, b16),
        ((mbs, ny, sub, pw), b16), ((mbs, ny, sub, pw), b16), ((mbs, ny, nx, sub, pw), b16), (rows_shape, b16),
        ((slots, tokens), b16), ((tokens // 2, slots), b16),
        ((2, mbs, experts, cap, pw), b16), ((2, mbs, experts, cap, pw), b16), ((mbs, half, 2, cap, f), b16),
        ((mbs, experts, 2, cap, f // 2), b16), ((2, cap, f // 2), f32), ((mbs, experts, 2, cap, f // 2), b16),
        ((mbs, experts, 2, cap, f), b16), ((mbs, experts, cap, pw), b16),
        ((width, 2 * f), b16), ((width, f), b16),
        ((mbs, length, 2 * f), b16), (rows_shape, b16), (rows_shape, b16),
        ((mbs, nx, ny, sub, pw), b16), ((mbs, nx, ny, sub, pw), b16), ((mbs, ny, sub, pw), b16), ((mbs, ny, sub, pw), b16),
        ((pw, d), b16), ((mbs, sub, d), f32), ((mbs, sub, d), b16), (rows_shape, b16),
        ((length, pw), b16), ((mbs, length, 3 * pw), b16), (rows_shape, b16), (rows_shape, b16),
        ((experts, d), f32), ((8, d), f32), ((2, cap, 128), f32),
        dense(sc), dense(ac), ((n, d), f32), dense(sc), dense(ac), ((n, d), f32),
        ((ny - 1, width, sc), b16), ((ny - 1, width, ac), b16), ((ny - 1, n, pw), f32),
        ((width, sc), f32), ((width, ac), f32), ((n, pw), f32), ((nx, n, pw), f32),
        ((2, mbs, sub, d), b16), ((2, 2, nx, mbs, sub, pw), b16),
        ((mbs, sub, d), b16), ((2, mbs, sub, d), b16),
        *((fwd[name].shape, fwd[name].dtype) for name in ("small", "place")),
        ((mbs, sub, d), b16),
        *((fwd[name].shape[1:], fwd[name].dtype) for name in (
            "mid", "n2", "rows", "q", "k", "v", "att", "rows2", "sgu", "shid", "shw")),
        (fwd["watt0"].shape, b16),
    )
    by_m = lambda c: flags((mbs, c))
    by_half = flags((2, mbs, experts, 2))
    names = ("tok", "small", "place", "y", "mid", "n2", "rows", "q", "k", "v", "att", "rows2", "sgu", "shid",
             "shw", "watt0", "watt1")
    outs = pl.pallas_call(
        functools.partial(
            backward_kernel, (nx, ny, mbs, sub, width, pw, heads, features, experts, cap, f, *BWD_SKEW)),
        out_shape=(
            jax.ShapeDtypeStruct((2, 2 * mbs, length, pw), b16),
            jax.ShapeDtypeStruct((experts, width, 2 * f), b16),
            jax.ShapeDtypeStruct((experts, width, f), b16),
            jax.ShapeDtypeStruct((width, ac), f32),
            jax.ShapeDtypeStruct((width, sc), f32),
            jax.ShapeDtypeStruct((n, pw), f32),
        ),
        in_specs=[hbm] * 17 + [vm] * 3 + [hbm] * 7,
        out_specs=(vm,) + (hbm,) * 5,
        scratch_shapes=[pltpu.VMEM(*v) for v in scratch] + [
            flags((2, experts)), by_m(ny), by_m(ny), by_m(nx), by_m(nx), by_m(nx), by_m(nx), by_m(nx), by_m(nx),
            by_m(nx), by_m(nx), by_m(ny), by_m(ny), by_m(nx), by_m(nx), by_m(nx), by_m(nx),
            by_half, by_half, by_half, by_half,
            flags((2, experts)), flags((2, experts)), flags((2, experts)), flags((2, experts)),
            flags((3,)), flags((3,)), flags((3, ny)), flags((3, ny)), flags((nx,)), flags((nx,)),
            flags((4,)), flags((2,)), flags((3,)), flags((20,)), flags((2, 2, ny)), flags((2, 2, nx)), pltpu.SemaphoreType.REGULAR((2,)),
        ],
        compiler_params=params(ids),
        cost_estimate=pl.CostEstimate(flops=2 * 10**10, bytes_accessed=10**8, transcendentals=10**6),
        name="backward",
    )(*(fwd[name] for name in names), cos, sin, rot, *(fwd[name] for name in ("slots", "gu", "hid")), win, fwd["win"], wdt, fwd["wdt"])
    return outs[0], outs[1:]


BWD_SKEW = (2, 2)


def fast_device(block_input, output_grad, attention_gain, attention_in, attention_out, feed_gain,
                router_weight, expert_in, expert_down, shared_in, shared_down, routes):
    s = lax.axis_index("section")
    ny = lax.axis_size("gy")
    nx = lax.axis_size("gx")
    mbs = block_input.shape[0] // 2
    width = block_input.shape[2]
    features = width * ny
    experts = expert_in.shape[1]
    f = expert_in.shape[-1]
    pw = lanes_up(width + 2 * experts)
    tokens = routes.shape[2]
    cap = 5 * tokens // (2 * experts)
    length = tokens // ny
    heads = attention_in.shape[-1] // DH
    dims = (width, pw, experts, cap)

    att_block = jnp.concatenate([
        pad_to(attention_in[0], 2, pw).reshape(width, 3 * pw), pad_to(attention_out[0].T, 1, pw)], 1)
    sh_block = jnp.concatenate([shared_in[0].reshape(width, 2 * f), shared_down[0].T], 1)
    small = jnp.concatenate([
        router_weight[0].T.astype(jnp.float32), feed_gain, attention_gain, jnp.zeros((6, width), jnp.float32)], 0)
    tin = lax.dynamic_slice_in_dim(jnp.stack([block_input, output_grad]), s * mbs, mbs, 1)
    tin = pad_to(tin, 3, pw)
    small = pad_to(small, 1, pw)
    win = jnp.swapaxes(expert_in[0], 1, 2)
    wdt = expert_down[0].transpose(0, 2, 1)
    pairs = jnp.swapaxes(routes[0], 1, 2)
    half = DH // 2
    freq = 10000.0 ** (-np.arange(half, dtype=np.float64) / half)
    lanes = np.tile(np.arange(length)[:, None] * freq[None], (1, 2 * heads))
    cos = np.zeros((length, pw), np.float32)
    sin = np.zeros((length, pw), np.float32)
    cos[:, : heads * DH] = np.cos(lanes)
    sin[:, : heads * DH] = np.sin(lanes)
    rot = np.zeros((pw, pw), np.float32)
    for lead in range(0, heads * DH, DH):
        at = lead + np.arange(half)
        rot[at + half, at] = -1.0
        rot[at, at + half] = 1.0
    cos, sin, rot = jnp.asarray(cos), jnp.asarray(sin), jnp.asarray(rot, jnp.bfloat16)

    fwd = forward(tin, small, att_block, sh_block, pairs, cos, sin, rot, win, wdt, dims, heads, features, 0)
    both, grads = backward(fwd, cos, sin, rot, win, wdt, dims, heads, features, 1)
    both = both[..., :width]
    win_g, wdt_g, att_g, sh_g, small_g = grads
    hd = heads * DH
    return (
        both[0][None],
        both[1][None],
        small_g[experts + 1 : experts + 2, :width],
        att_g[:, : 3 * pw].reshape(width, 3, pw)[..., :hd][None],
        att_g[:, 3 * pw : 3 * pw + hd].T[None],
        small_g[experts : experts + 1, :width],
        small_g[:experts, :width].T[None],
        win_g.astype(jnp.float32).reshape(experts, width, 2, f)[None],
        wdt_g.astype(jnp.float32).transpose(0, 2, 1)[None],
        sh_g[:, : 2 * f].reshape(width, 2, f)[None],
        sh_g[:, 2 * f :].T[None],
    )


def solution(mesh):
    in_specs = (
        P(None, "gx", "gy"),
        P(None, "gx", "gy"),
        P("section", "gy"),
        P("section", "gy", None, "gx"),
        P("section", "gx", "gy"),
        P("section", "gy"),
        P("section", "gy", None),
        P("section", None, "gy", None, "gx"),
        P("section", None, "gx", "gy"),
        P("section", "gy", None, "gx"),
        P("section", "gx", "gy"),
        P("section", None, None, None),
    )
    out_specs = (
        P("section", None, "gx", "gy"),
        P("section", None, "gx", "gy"),
        P("section", "gy"),
        P("section", "gy", None, "gx"),
        P("section", "gx", "gy"),
        P("section", "gy"),
        P("section", "gy", None),
        P("section", None, "gy", None, "gx"),
        P("section", None, "gx", "gy"),
        P("section", "gy", None, "gx"),
        P("section", "gx", "gy"),
    )
    fast = mesh.shape["gx"] == mesh.shape["gy"]
    return jax.shard_map(
        fast_device if fast else on_device, mesh=mesh, in_specs=in_specs, out_specs=out_specs, check_vma=False
    )
```

```python
import functools

import jax
import jax.numpy as jnp
import numpy as np
from jax import lax
from jax.experimental import pallas as pl
from jax.experimental.pallas import tpu as pltpu
from jax.sharding import PartitionSpec as P

DH = 64


epsilon = 1e-06
highest = lax.Precision.HIGHEST


def from_partner(array, axis, apart):
    return lax.ppermute(array, axis, [(i, i ^ 1 << apart) for i in range(lax.axis_size(axis))])


def token_rows(values):
    return lax.all_gather(values, "gx", axis=0, tiled=True)


def output_rows(values):
    return lax.psum_scatter(values, "gx", scatter_dimension=0, tiled=True)


def width_sum(values):
    return lax.psum(values, "gy")


def pass_section(values):
    return from_partner(values, "section", 0)


def sequence_sums(values):
    return lax.psum_scatter(values, "gy", scatter_dimension=0, tiled=True)


def sequence_rows(values):
    return lax.all_gather(values, "gy", axis=0, tiled=True)


def gather_hidden(hidden, shared_hidden):
    return (
        lax.all_gather(hidden, "gy", axis=0, tiled=True),
        lax.all_gather(shared_hidden, "gy", axis=0, tiled=True),
    )


def rope_turn(values, positions, turn_sign):
    half_size = values.shape[-1] // 2
    frequency = 10000.0 ** (-jnp.arange(half_size, dtype=jnp.float32) / half_size)
    angles = positions[:, None] * frequency[None, :]
    cosine = jnp.cos(angles)[:, None, :]
    sine_part = turn_sign * jnp.sin(angles)[:, None, :]
    first_half = values[..., :half_size]
    second_half = values[..., half_size:]
    return jnp.concatenate(
        [
            first_half * cosine - second_half * sine_part,
            first_half * sine_part + second_half * cosine,
        ],
        axis=-1,
    )


def norm_forward(stream, gain):
    full_width = stream.shape[1] * lax.axis_size("gy")
    square_sum = width_sum(jnp.sum(stream * stream, axis=1))
    inverse_rms = lax.rsqrt(square_sum / full_width + epsilon)
    return ((stream * inverse_rms[:, None] * gain[None, :]).astype(jnp.bfloat16), inverse_rms)


def norm_backward(stream, inverse_rms, gain, grad_normed):
    full_width = stream.shape[1] * lax.axis_size("gy")
    scaled = grad_normed * gain[None, :]
    inner_sum = width_sum(jnp.sum(scaled * stream, axis=1))
    cubed = inverse_rms * inverse_rms * inverse_rms
    grad_stream = inverse_rms[:, None] * scaled - stream * (cubed * inner_sum / full_width)[:, None]
    grad_gain = jnp.sum(grad_normed * stream * inverse_rms[:, None], axis=0)
    return (grad_stream, grad_gain)


def slot_table(route_ids, experts, capacity):
    flat_ids = route_ids.reshape(-1)
    assigned = (flat_ids[:, None] == jnp.arange(experts, dtype=jnp.int32)[None, :]).astype(
        jnp.int32
    )
    earlier = jnp.cumsum(assigned, axis=0) - assigned
    places = flat_ids * capacity + jnp.sum(earlier * assigned, axis=1)
    owners = jnp.arange(flat_ids.shape[0], dtype=jnp.int32) // 2
    slot_token = jnp.zeros((experts * capacity,), jnp.int32).at[places].set(owners)
    slot_valid = jnp.zeros((experts * capacity,), jnp.int32).at[places].set(jnp.ones_like(owners))
    return (places.reshape(-1, 2), slot_token, slot_valid)


def expert_act(gate_up, logits):
    half_size = gate_up.shape[1] // 2
    return (
        jax.nn.silu(gate_up[:, :half_size])
        * gate_up[:, half_size:]
        * jax.nn.sigmoid(logits)[:, None]
    )


def shared_act(gate_up):
    half_size = gate_up.shape[1] // 2
    return jax.nn.silu(gate_up[:, :half_size]) * gate_up[:, half_size:]


def causal_scores(queries, keys_part):
    score_scale = queries.shape[-1] ** (-0.5)
    scores = (
        jnp.einsum("qhd,khd->hqk", queries, keys_part, preferred_element_type=jnp.float32)
        * score_scale
    )
    length = queries.shape[0]
    causal = jnp.arange(length)[:, None] >= jnp.arange(length)[None, :]
    return jnp.where(causal[None], scores, -1e30)


def attend_forward(queries, keys_part, values_part):
    scores = causal_scores(queries, keys_part)
    row_max = jnp.max(scores, axis=-1, keepdims=True)
    exponent = jnp.exp(scores - row_max)
    row_total = jnp.sum(exponent, axis=-1, keepdims=True)
    probabilities = (exponent / row_total).astype(jnp.bfloat16)
    attended = jnp.einsum(
        "hqk,khd->qhd", probabilities, values_part, preferred_element_type=jnp.float32
    )
    return (attended, row_max + jnp.log(row_total))


def attend_backward(queries, keys_part, values_part, log_total, grad_attended):
    score_scale = queries.shape[-1] ** (-0.5)
    probabilities = jnp.exp(causal_scores(queries, keys_part) - log_total)
    grad_values = jnp.einsum(
        "hqk,qhd->khd",
        probabilities.astype(jnp.bfloat16),
        grad_attended,
        preferred_element_type=jnp.float32,
    )
    grad_probs = jnp.einsum(
        "qhd,khd->hqk", grad_attended, values_part, preferred_element_type=jnp.float32
    )
    grad_scores = (
        probabilities * (grad_probs - jnp.sum(grad_probs * probabilities, axis=-1, keepdims=True))
    ).astype(jnp.bfloat16)
    grad_queries = (
        jnp.einsum("hqk,khd->qhd", grad_scores, keys_part, preferred_element_type=jnp.float32)
        * score_scale
    )
    grad_keys = (
        jnp.einsum("hqk,qhd->khd", grad_scores, queries, preferred_element_type=jnp.float32)
        * score_scale
    )
    return (grad_queries, grad_keys, grad_values)


def layer_forward(stream, weights, route_ids):
    (
        attention_gain,
        attention_in,
        attention_out,
        feed_gain,
        router_weight,
        expert_in,
        expert_down,
        shared_in,
        shared_down,
    ) = weights
    local_width = stream.shape[1]
    experts = expert_in.shape[0]
    normed, inverse_first = norm_forward(stream, attention_gain)
    rows_first = token_rows(normed)
    tokens = rows_first.shape[0]
    capacity = 5 * tokens // (2 * experts)
    slot_count = experts * capacity
    projected = sequence_sums(
        jnp.dot(
            rows_first, attention_in.reshape(local_width, -1), preferred_element_type=jnp.float32
        )
    )
    length = projected.shape[0]
    projected = projected.reshape(length, 3, -1, DH)
    positions = jnp.arange(length, dtype=jnp.float32)
    queries = rope_turn(projected[:, 0], positions, 1.0).astype(jnp.bfloat16)
    keys_part = rope_turn(projected[:, 1], positions, 1.0).astype(jnp.bfloat16)
    values_part = projected[:, 2].astype(jnp.bfloat16)
    attended, log_total = attend_forward(queries, keys_part, values_part)
    attended_rows = sequence_rows(attended.astype(jnp.bfloat16).reshape(length, -1))
    middle = stream + output_rows(
        jnp.dot(attended_rows, attention_out, preferred_element_type=jnp.float32)
    )
    normed_feed, inverse_second = norm_forward(middle, feed_gain)
    rows_second = token_rows(normed_feed)
    route_slot, slot_token, slot_valid = slot_table(route_ids, experts, capacity)
    grouped = (rows_second[slot_token] * slot_valid[:, None].astype(jnp.bfloat16)).reshape(
        experts, capacity, local_width
    )
    expert_part = jnp.einsum(
        "ecd,edf->ecf",
        grouped,
        expert_in.reshape(experts, local_width, -1),
        preferred_element_type=jnp.float32,
    )
    router_part = jnp.einsum(
        "ecd,de->ec", grouped, router_weight, preferred_element_type=jnp.float32
    )
    shared_part = jnp.dot(
        rows_second, shared_in.reshape(local_width, -1), preferred_element_type=jnp.float32
    )
    expert_gu, router_logit, shared_gu = (
        lax.psum_scatter(
            expert_part.reshape(slot_count, -1), "gy", scatter_dimension=0, tiled=True
        ),
        lax.psum_scatter(router_part.reshape(slot_count), "gy", scatter_dimension=0, tiled=True),
        lax.psum_scatter(shared_part, "gy", scatter_dimension=0, tiled=True),
    )
    hidden_rows, shared_rows = gather_hidden(
        expert_act(expert_gu, router_logit).astype(jnp.bfloat16),
        shared_act(shared_gu).astype(jnp.bfloat16),
    )
    expert_result = jnp.einsum(
        "ecf,efd->ecd",
        hidden_rows.reshape(experts, capacity, -1),
        expert_down,
        preferred_element_type=jnp.float32,
    ).reshape(slot_count, local_width)
    branch = (
        expert_result[route_slot[:, 0]]
        + expert_result[route_slot[:, 1]]
        + jnp.dot(shared_rows, shared_down, preferred_element_type=jnp.float32)
    )
    result = middle + output_rows(branch)
    kept_items = (
        stream,
        inverse_first,
        rows_first,
        queries,
        keys_part,
        values_part,
        log_total,
        attended_rows,
        middle,
        inverse_second,
        rows_second,
        expert_gu,
        router_logit,
        shared_gu,
    )
    return (result, kept_items)


def layer_backward(grad_out, kept_items, weights, route_ids):
    (
        attention_gain,
        attention_in,
        attention_out,
        feed_gain,
        router_weight,
        expert_in,
        expert_down,
        shared_in,
        shared_down,
    ) = weights
    (
        stream,
        inverse_first,
        rows_first,
        queries,
        keys_part,
        values_part,
        log_total,
        attended_rows,
        middle,
        inverse_second,
        rows_second,
        expert_gu,
        router_logit,
        shared_gu,
    ) = kept_items[:14]
    local_width = stream.shape[1]
    experts = expert_in.shape[0]
    tokens = rows_second.shape[0]
    capacity = 5 * tokens // (2 * experts)
    slot_count = experts * capacity
    hidden_rows, shared_rows = gather_hidden(
        expert_act(expert_gu, router_logit).astype(jnp.bfloat16),
        shared_act(shared_gu).astype(jnp.bfloat16),
    )
    route_slot, slot_token, slot_valid = slot_table(route_ids, experts, capacity)
    valid_rows = slot_valid[:, None].astype(jnp.bfloat16)
    grouped = (rows_second[slot_token] * valid_rows).reshape(experts, capacity, local_width)
    grad_rows = token_rows(grad_out.astype(jnp.bfloat16))
    slot_grad = (grad_rows[slot_token] * valid_rows).reshape(experts, capacity, local_width)
    down_grad = jnp.einsum(
        "ecf,ecd->efd",
        hidden_rows.reshape(experts, capacity, -1),
        slot_grad,
        preferred_element_type=jnp.float32,
    )
    shared_down_grad = jnp.einsum(
        "tf,td->fd", shared_rows, grad_rows, preferred_element_type=jnp.float32
    )
    hidden_part = jnp.einsum(
        "ecd,efd->ecf", slot_grad, expert_down, preferred_element_type=jnp.float32
    ).reshape(slot_count, -1)
    shared_part = jnp.einsum(
        "td,fd->tf", grad_rows, shared_down, preferred_element_type=jnp.float32
    )
    grad_hidden, grad_shared = (
        lax.psum_scatter(
            hidden_part.astype(jnp.bfloat16), "gy", scatter_dimension=0, tiled=True
        ).astype(jnp.float32),
        lax.psum_scatter(
            shared_part.astype(jnp.bfloat16), "gy", scatter_dimension=0, tiled=True
        ).astype(jnp.float32),
    )
    unused_expert, expert_back = jax.vjp(expert_act, expert_gu, router_logit)
    grad_gu, grad_logit = expert_back(grad_hidden)
    unused_shared, shared_back = jax.vjp(shared_act, shared_gu)
    (grad_shared_gu,) = shared_back(grad_shared)
    gu_rows, shared_gu_rows = (
        lax.all_gather(grad_gu.astype(jnp.bfloat16), "gy", axis=0, tiled=True),
        lax.all_gather(grad_shared_gu.astype(jnp.bfloat16), "gy", axis=0, tiled=True),
    )
    logit_rows = lax.all_gather(grad_logit, "gy", axis=0, tiled=True).reshape(experts, capacity)
    gu_grouped = gu_rows.reshape(experts, capacity, -1)
    in_grad = jnp.einsum("ecd,ecf->edf", grouped, gu_grouped, preferred_element_type=jnp.float32)
    router_grad = jnp.einsum(
        "ecd,ec->de", grouped.astype(jnp.float32), logit_rows, precision=highest
    )
    shared_in_grad = jnp.einsum(
        "td,tf->df", rows_second, shared_gu_rows, preferred_element_type=jnp.float32
    )
    slot_back = jnp.einsum(
        "ecf,edf->ecd",
        gu_grouped,
        expert_in.reshape(experts, local_width, -1),
        preferred_element_type=jnp.float32,
    )
    slot_back = slot_back + logit_rows[:, :, None] * router_weight.T.astype(jnp.float32)[:, None, :]
    slot_back = slot_back.reshape(slot_count, local_width)
    rows_back = (
        slot_back[route_slot[:, 0]]
        + slot_back[route_slot[:, 1]]
        + jnp.einsum(
            "tf,df->td",
            shared_gu_rows,
            shared_in.reshape(local_width, -1),
            preferred_element_type=jnp.float32,
        )
    )
    grad_middle_norm, feed_gain_grad = norm_backward(
        middle, inverse_second, feed_gain, output_rows(rows_back)
    )
    grad_middle = grad_out + grad_middle_norm
    middle_rows = token_rows(grad_middle.astype(jnp.bfloat16))
    out_weight_grad = jnp.einsum(
        "tf,td->fd", attended_rows, middle_rows, preferred_element_type=jnp.float32
    )
    grad_attended = sequence_sums(
        jnp.einsum("td,fd->tf", middle_rows, attention_out, preferred_element_type=jnp.float32)
    )
    length = grad_attended.shape[0]
    positions = jnp.arange(length, dtype=jnp.float32)
    grad_queries, grad_keys, grad_values = attend_backward(
        queries,
        keys_part,
        values_part,
        log_total,
        grad_attended.astype(jnp.bfloat16).reshape(queries.shape),
    )
    grad_projected = jnp.stack(
        [
            rope_turn(grad_queries, positions, -1.0),
            rope_turn(grad_keys, positions, -1.0),
            grad_values,
        ],
        axis=1,
    )
    grad_projected = grad_projected.astype(jnp.bfloat16).reshape(length, -1)
    projected_rows = sequence_rows(grad_projected)
    in_weight_grad = jnp.einsum(
        "td,tf->df", rows_first, projected_rows, preferred_element_type=jnp.float32
    )
    grad_normed = output_rows(
        jnp.einsum(
            "tf,df->td",
            projected_rows,
            attention_in.reshape(local_width, -1),
            preferred_element_type=jnp.float32,
        )
    )
    grad_stream_norm, attention_gain_grad = norm_backward(
        stream, inverse_first, attention_gain, grad_normed
    )
    layer_grads = (
        attention_gain_grad,
        in_weight_grad.reshape(attention_in.shape),
        out_weight_grad,
        feed_gain_grad,
        router_grad,
        in_grad.reshape(expert_in.shape),
        down_grad,
        shared_in_grad.reshape(shared_in.shape),
        shared_down_grad,
    )
    return (grad_middle + grad_stream_norm, layer_grads)


def put_item(buffer, value, batch_index, is_valid):
    current = lax.dynamic_index_in_dim(buffer, batch_index, 0, keepdims=False)
    return lax.dynamic_update_index_in_dim(
        buffer, jnp.where(is_valid, value, current), batch_index, 0
    )


def on_device(
    block_input,
    output_grad,
    attention_gain,
    attention_in,
    attention_out,
    feed_gain,
    router_weight,
    expert_in,
    expert_down,
    shared_in,
    shared_down,
    routes,
):
    section_index = lax.axis_index("section")
    batches = block_input.shape[0]
    weights = tuple(
        (
            member[0]
            for member in (
                attention_gain,
                attention_in,
                attention_out,
                feed_gain,
                router_weight,
                expert_in,
                expert_down,
                shared_in,
                shared_down,
            )
        )
    )
    route_table = routes[0]
    outputs = jnp.zeros(block_input.shape, jnp.bfloat16)
    received = jnp.zeros(block_input.shape[1:], jnp.bfloat16)
    stored = None
    for tick_step in range(batches + 1):
        micro_index = tick_step - section_index
        is_valid = (micro_index >= 0) & (micro_index < batches)
        batch_index = jnp.clip(micro_index, 0, batches - 1)
        fresh_input = lax.dynamic_index_in_dim(block_input, batch_index, 0, keepdims=False)
        incoming = jnp.where(section_index == 0, fresh_input, received).astype(jnp.float32)
        route_ids = lax.dynamic_index_in_dim(route_table, batch_index, 0, keepdims=False)
        result, kept_items = layer_forward(incoming, weights, route_ids)
        result_low = result.astype(jnp.bfloat16)
        outputs = put_item(outputs, result_low, batch_index, is_valid)
        if stored is None:
            stored = tuple(
                (jnp.zeros((batches,) + member.shape, member.dtype) for member in kept_items)
            )
        stored = tuple(
            (
                put_item(buffer, member, batch_index, is_valid)
                for buffer, member in zip(stored, kept_items)
            )
        )
        if tick_step < batches:
            received = pass_section(result_low)
    grads_in = jnp.zeros(block_input.shape, jnp.bfloat16)
    received = jnp.zeros(block_input.shape[1:], jnp.bfloat16)
    totals = tuple((jnp.zeros(member.shape, jnp.float32) for member in weights))
    for tick_step in range(batches + 1):
        micro_index = batches - tick_step - section_index
        is_valid = (micro_index >= 0) & (micro_index < batches)
        batch_index = jnp.clip(micro_index, 0, batches - 1)
        given_grad = lax.dynamic_index_in_dim(output_grad, batch_index, 0, keepdims=False)
        incoming = jnp.where(section_index == 1, given_grad, received).astype(jnp.float32)
        kept_items = tuple(
            (lax.dynamic_index_in_dim(buffer, batch_index, 0, keepdims=False) for buffer in stored)
        )
        route_ids = lax.dynamic_index_in_dim(route_table, batch_index, 0, keepdims=False)
        grad_input, layer_grads = layer_backward(incoming, kept_items, weights, route_ids)
        grad_low = grad_input.astype(jnp.bfloat16)
        grads_in = put_item(grads_in, grad_low, batch_index, is_valid)
        totals = tuple(
            (total + jnp.where(is_valid, member, 0.0) for total, member in zip(totals, layer_grads))
        )
        if tick_step < batches:
            received = pass_section(grad_low)
    gain_first, gain_second, router_total = lax.psum((totals[0], totals[3], totals[4]), "gx")
    return (
        outputs[None],
        grads_in[None],
        gain_first[None],
        totals[1][None],
        totals[2][None],
        gain_second[None],
        router_total[None],
        totals[5][None],
        totals[6][None],
        totals[7][None],
        totals[8][None],
    )


def lanes_up(n):
    return -(-n // 128) * 128


def rot_columns(w):
    shape = w.shape
    w = w.reshape(shape[:-1] + (-1, 2, DH // 2))
    w = jnp.stack([-w[..., 1, :], w[..., 0, :]], axis=-2)
    return w.reshape(shape)


def pad_to(v, axis, n):
    pads = [(0, 0)] * v.ndim
    pads[axis] = (0, n - v.shape[axis])
    return jnp.pad(v, pads)


def mm(a, b, dims=((1,), (0,))):
    return lax.dot_general(a, b, (dims, ((), ())), preferred_element_type=jnp.float32)


def bf(v):
    return v.astype(jnp.bfloat16)


def head_mask(pw, h):
    lane = lax.broadcasted_iota(jnp.int32, (1, pw), 1)
    return (lane >= h * DH) & (lane < (h + 1) * DH)


def rms(x, features):
    return lax.rsqrt(jnp.sum(x * x, axis=1, keepdims=True) / features + epsilon)


def norm_back(x, inv, gain, d, features):
    u = d * gain
    inner = jnp.sum(u * x, axis=1, keepdims=True) / features
    dx = inv * u - x * (inv * inv * inv * inner)
    return dx, jnp.sum(d * x * inv, axis=0, keepdims=True)


def probs_of(q, k):
    s = mm(q, k, ((1,), (1,))) * DH ** -0.5
    n = s.shape[0]
    causal = lax.broadcasted_iota(jnp.int32, (n, n), 0) >= lax.broadcasted_iota(jnp.int32, (n, n), 1)
    s = jnp.where(causal, s, -1e30)
    e = jnp.exp(s - jnp.max(s, axis=1, keepdims=True))
    return e / jnp.sum(e, axis=1, keepdims=True)


def act_back(gate, up, dh, s):
    sg = jax.nn.sigmoid(gate)
    silu = gate * sg
    if s is None:
        return dh * up * (sg * (1.0 + gate * (1.0 - sg))), dh * silu, None
    dr = jnp.sum(dh * silu * up, axis=-1, keepdims=True) * s * (1.0 - s)
    ds = dh * s
    return ds * up * (sg * (1.0 + gate * (1.0 - sg))), ds * silu, dr


MESH = pl.DeviceIdType.MESH
VMEM_BYTES = 62 * 2**20


def remote(src, dst, send, recv, target):
    return pltpu.make_async_remote_copy(
        src_ref=src, dst_ref=dst, send_sem=send, recv_sem=recv, device_id=target, device_id_type=MESH
    )


def router_column(rows, e, width, experts):
    lane = lax.broadcasted_iota(jnp.int32, rows.shape, rows.ndim - 1)
    mask = (lane == width + e) | (lane == width + experts + e)
    return jnp.sum(jnp.where(mask, rows.astype(jnp.float32), 0.0), axis=-1, keepdims=True)


class Position:
    def __init__(self, nx, ny):
        self.s = lax.axis_index("section")
        self.a = lax.axis_index("gx")
        self.b = lax.axis_index("gy")
        self.nx, self.ny = nx, ny
        self.n = nx * ny
        self.me = self.a * ny + self.b

    def device(self, index):
        return (self.s, index // self.ny, lax.rem(index, self.ny))

    def others(self, do):
        def step(i, c):
            index = lax.rem(self.me + i, self.n)
            do(index, index // self.ny, lax.rem(index, self.ny))
            return c

        lax.fori_loop(1, self.n, step, 0)

    def peers(self, do):
        for i in range(1, self.nx):
            do(lax.rem(self.a + i, self.nx))

    def line(self, do):
        for i in range(1, self.ny):
            do(lax.rem(self.b + i, self.ny))


def greet_section(pos):
    barrier = pltpu.get_barrier_semaphore()

    def one(index, ai, bi):
        pl.semaphore_signal(barrier, inc=1, device_id=(pos.s, ai, bi), device_id_type=MESH)

    pos.others(one)
    return barrier


def flags(count):
    return pltpu.SemaphoreType.DMA(count)


class Share:
    def __init__(self, pos, layer, block, full, sems, cols=None):
        if cols is None:
            cols = pl.ds(0, block.shape[1])
        self.pos, self.layer, self.cols = pos, layer, cols
        self.block, self.full = block.at[:, cols], full.at[:, :, cols]
        self.sems = sems
        self.source = pos.s == layer

    def along(self, way, h):
        pos = self.pos
        j = pos.b - way * h
        to = pos.b + way
        real = (j >= 0) & (j < pos.ny) & (to >= 0) & (to < pos.ny)
        j = jnp.clip(j, 0, pos.ny - 1)
        src = self.block if h == 0 else self.full.at[j]
        copy = remote(src, self.full.at[j], self.sems[0].at[(way + 1) // 2, h], self.sems[1].at[j], (pos.s, pos.a, to))
        return real, j, copy

    def across(self, src, slot):
        pos = self.pos
        return remote(src, self.full.at[slot], self.sems[2].at[slot], self.sems[3].at[slot], (1 - pos.s, pos.a, pos.b))

    def start(self):
        b = self.pos.b

        @pl.when(self.source)
        def _():
            self.full[b] = self.block[...]
            for way in (-1, 1):
                real, _, copy = self.along(way, 0)
                pl.when(real)(copy.start)
            self.across(self.block, b).start()

    def hop(self, h):
        pos = self.pos

        @pl.when(self.source)
        def _():
            for way in (-1, 1):
                j = pos.b - way * h

                @pl.when((j >= 0) & (j < pos.ny))
                def _():
                    real, jc, copy = self.along(way, h)
                    copy.wait_recv()
                    pl.when(real)(copy.start)
                    self.across(self.full.at[jc], jc).start()

    def finish(self):
        pos = self.pos

        @pl.when(self.source)
        def _():
            for h in range(pos.ny - 1):
                for way in (-1, 1):
                    real, _, copy = self.along(way, h)
                    pl.when(real)(copy.wait_send)
            for j in range(pos.ny):
                self.across(self.block, j).wait_send()

        @pl.when(jnp.logical_not(self.source))
        def _():
            for j in range(pos.ny):
                self.across(self.full.at[j], j).wait_recv()


def share_sems(ny):
    return [flags((2, ny)), flags((ny,)), flags((ny,)), flags((ny,))]


def params(ids):
    return pltpu.CompilerParams(collective_id=ids, has_side_effects=True, vmem_limit_bytes=VMEM_BYTES)


def turn(t, cos, sin, rot, sign):
    hi = bf(t)
    lo = bf(t - hi.astype(jnp.float32))
    return bf(t * cos + sign * ((mm(hi, rot) + mm(lo, rot)) * sin))


def by_blocks(rows, full, cols, width, pw):
    total = None
    for j in range(full.shape[0]):
        part = mm(rows[:, j * pw : j * pw + width], full[j, :, cols])
        total = part if total is None else total + part
    return total


def finish_kernel(cfg, win, wdt, both, att, sh, small, win_o, wdt_o, y_o, gx_o, ain_o, aout_o, sin_o, sdn_o, gain_o, fgain_o, rw_o):
    width, pw, hd, experts = cfg
    f = wdt.shape[-1]
    value = win[0].astype(jnp.float32)
    win_o[0, :, 0, :] = value[:, :f]
    win_o[0, :, 1, :] = value[:, f:]
    wdt_o[0] = wdt[0].astype(jnp.float32)

    @pl.when(pl.program_id(0) == 0)
    def _():
        for kind, dst in enumerate((y_o, gx_o)):
            for m in range(both.shape[1]):
                dst[m] = both[kind, m].astype(jnp.float32).T[:width].astype(dst.dtype)
        for c in range(3):
            ain_o[c] = att[:, c * pw : c * pw + hd]
        square = jnp.concatenate([att[:, 3 * pw :], jnp.zeros((pw - width, pw), jnp.float32)], 0)
        aout_o[...] = square.T[:hd, :width]
        value = sh[:, : 2 * f]
        sin_o[:, 0, :] = value[:, :f]
        sin_o[:, 1, :] = value[:, f:]
        sdn_o[...] = sh[:, 2 * f :]
        rw_o[...] = small[:experts, :width]
        fgain_o[...] = small[experts : experts + 1, :width]
        gain_o[...] = small[experts + 1 : experts + 2, :width]


def finish_outputs(win, wdt, both, att, sh, small, pw, hd):
    experts, width, f = wdt.shape
    mbs, tokens = both.shape[1:3]
    f32 = jnp.float32
    each = lambda *shape: pl.BlockSpec((1,) + shape, lambda e: (e,) + (0,) * len(shape))
    once = lambda *shape: pl.BlockSpec(shape, lambda e: (0,) * len(shape))
    shapes = (
        ((mbs, width, tokens), both.dtype), ((mbs, width, tokens), both.dtype),
        ((3, width, hd), f32), ((hd, width), f32), ((width, 2, f), f32), ((width, f), f32),
        ((1, width), f32), ((1, width), f32), ((experts, width), f32),
    )
    return pl.pallas_call(
        functools.partial(finish_kernel, (width, pw, hd, experts)),
        grid=(experts,),
        out_shape=(
            jax.ShapeDtypeStruct((experts, width, 2, f), f32),
            jax.ShapeDtypeStruct((experts, width, f), f32),
            *(jax.ShapeDtypeStruct(*v) for v in shapes),
        ),
        in_specs=[each(width, 2 * f), each(width, f)] + [once(*v.shape) for v in (both, att, sh, small)],
        out_specs=(each(width, 2, f), each(width, f), *(once(*v[0]) for v in shapes)),
        compiler_params=pltpu.CompilerParams(vmem_limit_bytes=VMEM_BYTES),
        name="finish",
    )(win, wdt, both, att, sh, small)


def forward_kernel(cfg, *refs):
    nx, ny, mbs, sub, width, pw, heads, features, experts, cap, f, sk, ak = cfg
    (tin, small_b, att_b, sh_b, routes, cos, sin, rot, win_a, wdt_a,
     win_b, wdt_b, tok_o, small_o, place_o, place_to, watt0_o, y_o, mid_o, n2_o, rows_o, q_o, k_o, v_o, att_o, slots_o, gu_o, hid_o, rows2_o, sgu_o, shid_o, shw_o, watt_o, gslots_o,
     y, mid, n2, rx, nsend, nall, proj, q, k, v, att, osend, orecv, rwx,
     xsend, xline, xall, nrows, pm, pt, slots, acc, gu, hid, eo, sgu, shid, ssend, srecv, rsend, rpeer, rline, rrecv,
     win, wdt, shw0, shw1, watt0, watt1, tbuf, tok, rts, place, place_t, sm0, sm1, small, gall, gslots,
     n_send, n_recv, o_send, o_recv, x_send, x_recv, u_send, u_recv, t_send, t_recv, s_send, s_recv, g_send, g_recv, r_send, r_recv,
     rs_send, rs_recv, ag_send, ag_recv, wi_sem, wd_sem, g_sem, k_sem, i_send, i_recv, q_send, q_recv, v_send, v_recv, gu_send, gu_recv, *w_sems) = refs
    pos = Position(nx, ny)
    s, a, b, me = pos.s, pos.a, pos.b, pos.me
    slots_n = experts * cap
    tokens = nx * ny * sub
    d = ny * pw
    length = nx * sub
    half, hw = experts // 2, f // 2
    lane = lax.broadcasted_iota(jnp.int32, (1, pw), 1)
    shares = (
        Share(pos, 0, sh_b, shw0, w_sems[0:4]),
        Share(pos, 1, att_b, watt1, w_sems[4:8]),
        Share(pos, 1, sh_b, shw1, w_sems[8:12]),
    )
    entry_shares = (
        Share(pos, 0, small_b, sm0, w_sems[12:16]),
        Share(pos, 1, small_b, sm1, w_sems[16:20]),
        Share(pos, 0, att_b, watt0, w_sems[20:24], pl.ds(0, 2 * pw)),
        Share(pos, 0, att_b, watt0, w_sems[24:28], pl.ds(2 * pw, 2 * pw)),
    )
    watts, shws = (watt0, watt1), (shw0, shw1)
    barrier = pltpu.get_barrier_semaphore()
    pos.peers(lambda ai: pl.semaphore_signal(barrier, inc=1, device_id=(s, ai, b), device_id_type=MESH))
    pos.line(lambda bi: pl.semaphore_signal(barrier, inc=1, device_id=(s, a, bi), device_id_type=MESH))
    pl.semaphore_signal(barrier, inc=1, device_id=(1 - s, a, b), device_id_type=MESH)
    for j in range(ny):
        @pl.when((a != b) | (b != j))
        def _():
            pl.semaphore_signal(barrier, inc=1, device_id=(s, b, j), device_id_type=MESH)

    def weight_copy(layer, e, which):
        own, oth, dst, sem = ((win_a, win_b, win, wi_sem), (wdt_a, wdt_b, wdt, wd_sem))[which]
        return own.at[e], oth.at[e], dst.at[e], sem.at[e]

    def start_weight(layer, e, which):
        own, oth, dst, sem = weight_copy(layer, e, which)

        @pl.when(s == layer)
        def _():
            pltpu.make_async_copy(own, dst, sem).start()

        @pl.when(s != layer)
        def _():
            pltpu.make_async_copy(oth, dst, sem).start()

    def wait_weight(layer, e, which):
        own, oth, dst, sem = weight_copy(layer, e, which)
        pltpu.make_async_copy(own, dst, sem).wait()

    def first_weights(e, c):
        start_weight(0, e, 0)
        start_weight(0, e, 1)
        return c

    def swap(c):
        src, dst = ((win_a, win_b), (wdt_a, wdt_b))[c]
        return remote(src, dst, v_send.at[c], v_recv.at[c], (1 - s, a, b))

    def weights_ready():
        for c in range(2):
            swap(c).wait()
        lax.fori_loop(0, experts, first_weights, 0)

    @pl.when(a == b)
    def _():
        pl.semaphore_wait(barrier, nx - 1 + ny - 1 + 1 + nx - 1)

    @pl.when(a != b)
    def _():
        pl.semaphore_wait(barrier, nx - 1 + ny - 1 + 1 + nx)

    def tokens_copy(i, slot, seq):
        src = tin.at[:, :, pl.ds(pl.multiple_of(i * sub, sub), sub), :]
        return remote(src, tbuf.at[slot], i_send.at[i], i_recv.at[slot], (s, i, seq))

    def token_targets(do):
        for c in range(nx):
            i = lax.rem(a + c, nx)

            @pl.when((i != a) | (a != b))
            def _():
                do(tokens_copy(i, b, a))

    def routes_copy(src, slot):
        return remote(routes.at[pl.ds(src * mbs, mbs)], rts.at[slot], q_send, q_recv, (1 - s, a, b))

    token_targets(lambda copy: copy.start())
    routes_copy(1 - s, s).start()
    for share in entry_shares:
        share.start()
    for c in range(2):
        swap(c).start()
    rts[s] = routes[pl.ds(s * mbs, mbs)]

    @pl.when(a == b)
    def _():
        tbuf[b] = tin[:, :, pl.ds(pl.multiple_of(a * sub, sub), sub), :]

    routes_copy(0, 1 - s).wait()

    def places():
        t0 = lax.broadcasted_iota(jnp.int32, (tokens, tokens), 0)
        t1 = lax.broadcasted_iota(jnp.int32, (tokens, tokens), 1)
        before = bf((t1 < t0).astype(jnp.float32))
        after = bf((t0 < t1).astype(jnp.float32))
        er = lax.broadcasted_iota(jnp.int32, (experts, tokens), 0).astype(jnp.float32)
        ec = lax.broadcasted_iota(jnp.int32, (tokens, 128), 1).astype(jnp.float32)
        sub8 = lax.broadcasted_iota(jnp.int32, (128, tokens), 0)
        for l in range(2):
            for m in range(mbs):
                r = rts[l, m].astype(jnp.float32)
                rows = [r[c : c + 1] for c in range(2)]
                hot = [(row == er).astype(jnp.float32) for row in rows]
                count = mm(bf(hot[0] + hot[1]), after)
                cols = jnp.where(sub8 == 0, rows[0], jnp.where(sub8 == 1, rows[1], 0.0)).T
                cols = [cols[:, c : c + 1] for c in range(2)]
                hot_t = [(col == ec).astype(jnp.float32) for col in cols]
                count_t = mm(before, bf(hot_t[0] + hot_t[1]))
                for c in range(2):
                    rank = jnp.sum(hot[c] * count, axis=0, keepdims=True)
                    place[l, m, c : c + 1] = (rows[c] * cap + rank).astype(jnp.int32)
                    rank_t = jnp.sum(hot_t[c] * count_t, axis=1, keepdims=True)
                    place_t[l, m, :, c : c + 1] = (cols[c] * cap + rank_t).astype(jnp.int32)

    def tokens_ready():
        for j in range(ny):
            @pl.when((a != b) | (b != j))
            def _():
                tokens_copy(a, j, j).wait_recv()

            for kind in range(2):
                tok[kind, :, :, j * pw : (j + 1) * pw] = tbuf[j, kind]
        token_targets(lambda copy: copy.wait_send())

    def stream(l, m):
        return (tok[0, m] if l == 0 else y[0, m]).astype(jnp.float32)

    def copy_n(l, m, ai, slot):
        return remote(nsend.at[l, m], nall.at[l, m, slot], n_send.at[l, m, ai], n_recv.at[l, m, slot], (s, ai, b))

    def norm_first(l, m):
        xv = stream(l, m)
        nsend[l, m] = bf(xv * rms(xv, features) * small[l, experts + 1 : experts + 2])
        pos.peers(lambda ai: copy_n(l, m, ai, a).start())
        nall[l, m, a] = nsend[l, m]

    def copy_o(l, m, ai, slot):
        return remote(osend.at[l, m, ai], orecv.at[l, m, slot], o_send.at[l, m, ai], o_recv.at[l, m, slot], (s, ai, b))

    def attention(l, m):
        watt = watts[l]
        pos.peers(lambda ai: copy_n(l, m, ai, ai).wait())
        proj[...] = by_blocks(nall[l, m].reshape(length, d), watt, slice(0, 3 * pw), width, pw)
        v[l, m] = bf(proj[:, 2 * pw : 3 * pw])
        q[l, m] = turn(proj[:, :pw], cos[...], sin[...], rot[...], 1.0)
        k[l, m] = turn(proj[:, pw : 2 * pw], cos[...], sin[...], rot[...], 1.0)
        total = jnp.zeros((length, pw), jnp.float32)
        for h in range(heads):
            mask = head_mask(pw, h)
            p = probs_of(jnp.where(mask, q[l, m], 0), k[l, m])
            total = total + mm(bf(p), jnp.where(mask, v[l, m], 0))
        att[l, m] = bf(total)
        for j in range(ny):
            part = mm(att[l, m], watt[j, :, 3 * pw : 4 * pw], ((1,), (1,)))
            osend[l, m, :, :, j * pw : j * pw + width] = bf(part).reshape(nx, sub, width)
        pos.peers(lambda ai: copy_o(l, m, ai, a).start())
        orecv[l, m, a] = osend[l, m, a]

    def copy_x(l, m, bi, slot):
        return remote(xsend.at[l, m, bi], xline.at[l, m, slot], x_send.at[l, m, bi], x_recv.at[l, m, slot], (s, a, bi))

    def copy_w(l, m, ai, slot):
        return remote(xline.at[l, m], xall.at[l, m, :, slot], u_send.at[l, m, ai], u_recv.at[l, m, slot], (s, ai, b))

    def copy_t(l, m, ai, slot):
        return remote(n2.at[l, m], nrows.at[l, m, slot], t_send.at[l, m, ai], t_recv.at[l, m, slot], (s, ai, b))

    def norm_second(l, m):
        pos.peers(lambda ai: copy_o(l, m, ai, ai).wait())
        mv = stream(l, m)
        for ai in range(nx):
            mv = mv + orecv[l, m, ai].astype(jnp.float32)
        mid[l, m] = mv
        n2v = bf(mv * rms(mv, features) * small[l, experts : experts + 1])
        n2[l, m] = n2v
        rv = mm(n2v, rwx[l], ((1,), (1,)))
        hi = bf(rv)
        lo = bf(rv - hi.astype(jnp.float32))
        tail = jnp.where(lane < width + experts, hi, lo)
        for j in range(ny):
            xsend[l, m, j] = jnp.where(lane < width, n2v[:, j * pw : (j + 1) * pw], tail)
        pos.line(lambda bi: copy_x(l, m, bi, b).start())
        xline[l, m, b] = xsend[l, m, b]
        pos.peers(lambda ai: copy_t(l, m, ai, a).start())
        nrows[l, m, a] = n2[l, m]

    def spread(l, m):
        pos.line(lambda bi: copy_x(l, m, bi, bi).wait())
        pos.peers(lambda ai: copy_w(l, m, ai, a).start())
        xall[l, m, :, a] = xline[l, m]

    def dispatch(l, m):
        i0 = lax.broadcasted_iota(jnp.int32, (slots_n, tokens), 0)
        pm[...] = bf(((place[l, m, 0:1] == i0) | (place[l, m, 1:2] == i0)).astype(jnp.float32))
        pos.peers(lambda ai: copy_w(l, m, ai, ai).wait())
        slots[l, m] = bf(mm(pm[...], xall[l, m].reshape(tokens, pw))).reshape(experts, cap, pw)

    def grad_send(m):
        for j in range(ny):
            xsend[0, m, j] = tok[1, m, :, j * pw : (j + 1) * pw]
        pos.line(lambda bi: copy_x(0, m, bi, b).start())
        xline[0, m, b] = xsend[0, m, b]

    def copy_gw(m, ai, slot):
        return remote(xline.at[0, m], gall.at[m, :, slot], gu_send.at[m, ai], gu_recv.at[m, slot], (s, ai, b))

    def grad_spread(m):
        pos.line(lambda bi: copy_x(0, m, bi, bi).wait())
        pos.peers(lambda ai: copy_gw(m, ai, a).start())
        gall[m, :, a] = xline[0, m]

    def grad_dispatch(m):
        i0 = lax.broadcasted_iota(jnp.int32, (slots_n, tokens), 0)
        pm[...] = bf(((place[1, m, 0:1] == i0) | (place[1, m, 1:2] == i0)).astype(jnp.float32))
        pos.peers(lambda ai: copy_gw(m, ai, ai).wait())
        gslots[m] = bf(mm(pm[...], gall[m].reshape(tokens, pw))).reshape(experts, cap, pw)

    def shared_in_part(l, m):
        pos.peers(lambda ai: copy_t(l, m, ai, ai).wait())
        shw = shws[l]
        gu_s = by_blocks(nrows[l, m].reshape(length, d), shw, slice(0, 2 * f), width, pw)
        sgu[l, m] = bf(gu_s)
        gate = gu_s[:, :f]
        shid[l, m] = bf(gate * jax.nn.sigmoid(gate) * gu_s[:, f:])

    def copy_s(l, m, ai, slot):
        return remote(ssend.at[l, m, ai], srecv.at[l, m, slot], s_send.at[l, m, ai], s_recv.at[l, m, slot], (s, ai, b))

    def shared_out_part(l, m):
        for j in range(ny):
            part = mm(shid[l, m], shws[l][j, :, 2 * f :], ((1,), (1,)))
            ssend[l, m, :, :, j * pw : j * pw + width] = bf(part).reshape(nx, sub, width)
        pos.peers(lambda ai: copy_s(l, m, ai, a).start())
        srecv[l, m, a] = ssend[l, m, a]

    def copy_g(l, m, ai, slot):
        return remote(rsend.at[l, m, ai], rpeer.at[l, m, slot], g_send.at[l, m, ai], g_recv.at[l, m, slot], (s, ai, b))

    def copy_r(l, m, bi, slot):
        return remote(rline.at[l, m, bi], rrecv.at[l, m, slot], r_send.at[l, m, bi], r_recv.at[l, m, slot], (s, a, bi))

    def combine(l, m):
        i1 = lax.broadcasted_iota(jnp.int32, (tokens, slots_n), 1)
        pt[...] = bf(((place_t[l, m, :, 0:1] == i1) | (place_t[l, m, :, 1:2] == i1)).astype(jnp.float32))
        br = mm(pt[...], eo[m].reshape(slots_n, width))
        for ai in range(nx):
            rsend[l, m, ai, :, :, :width] = bf(br).reshape(ny, nx, sub, width)[:, ai]
        pos.peers(lambda ai: copy_g(l, m, ai, a).start())
        rpeer[l, m, a] = rsend[l, m, a]

    def combine_line(l, m):
        pos.peers(lambda ai: copy_g(l, m, ai, ai).wait())
        total = rpeer[l, m, 0].astype(jnp.float32)
        for ai in range(1, nx):
            total = total + rpeer[l, m, ai].astype(jnp.float32)
        rline[l, m] = bf(total)
        pos.line(lambda bi: copy_r(l, m, bi, b).start())
        rrecv[l, m, b] = rline[l, m, b]

    def layer_out(l, m):
        pos.peers(lambda ai: copy_s(l, m, ai, ai).wait())
        pos.line(lambda bi: copy_r(l, m, bi, bi).wait())
        total = mid[l, m]
        for ai in range(nx):
            total = total + srecv[l, m, ai].astype(jnp.float32)
        for j in range(ny):
            part = total[:, j * pw : (j + 1) * pw]
            part = part + jnp.where(lane < width, rrecv[l, m, j].astype(jnp.float32), 0.0)
            y[l, m, :, j * pw : (j + 1) * pw] = bf(part)

    first = (b == ny - 1, b == 0)
    last = (b == 0, b == ny - 1)
    up = (ny - 1 - b, b)
    down = (b, ny - 1 - b)
    lag = (sk + ak) * (ny - 1)
    apart = STAGE_STEPS
    units = 2 * half
    gap = max(lag + 6 * apart - units, 0)
    starts = (0, units, 2 * units + gap, 3 * units + gap)
    steps = starts[3] + units + lag

    def unit(t, dd):
        early = (t >= 0) & (t < 2 * units)
        late = (t >= starts[2]) & (t < starts[2] + 2 * units)
        u = jnp.clip(jnp.where(t < starts[2], jnp.minimum(t, 2 * units - 1), t - gap), 0, 4 * units - 1)
        job, r = u // units, lax.rem(u, units)
        return early | late, job // 2, lax.rem(job, 2), r // 2 + dd * half, lax.rem(r, 2)

    def gu_copy(dd, l, m, e, c):
        to = b - 1 if dd == 0 else b + 1
        return remote(gu.at[l, m, e, c], gu.at[l, m, e, c], rs_send.at[l, m, e, c], rs_recv.at[l, m, e, c], (s, a, to))

    def hid_copy(dd, l, m, e, c):
        to = b + 1 if dd == 0 else b - 1
        return remote(hid.at[l, m, e, c], hid.at[l, m, e, c], ag_send.at[l, m, e, c], ag_recv.at[l, m, e, c], (s, a, to))

    def save_gates(l, m, e, c):
        return pltpu.make_async_copy(gu.at[l, m, e, c], gu_o.at[l, m, e, c], g_sem.at[l, m, e, c])

    def chain(i):
        reduce = [unit(i - sk * up[dd], dd) for dd in range(2)]
        spreads = [unit(i - sk * (ny - 1) - ak * down[dd], dd) for dd in range(2)]
        for dd in range(2):
            valid, l, m, e, c = reduce[dd]

            @pl.when(valid)
            def _():
                @pl.when((m == 0) & (c == 0))
                def _():
                    wait_weight(0, e, 0)

                for plane in range(2):
                    part = win[e, plane, :, pl.ds(pl.multiple_of(c * hw, hw), hw)]
                    acc[dd, :, plane * hw : (plane + 1) * hw] = mm(slots[l, m, e, :, :width], part)

                @pl.when((l == 0) & (m == 1) & (c == 1))
                def _():
                    start_weight(1, e, 0)

        for dd in range(2):
            valid, l, m, e, c = reduce[dd]

            @pl.when(valid & first[dd])
            def _():
                gu[l, m, e, c] = bf(acc[dd])
                gu_copy(dd, l, m, e, c).start()

            @pl.when(valid & jnp.logical_not(first[dd] | last[dd]))
            def _():
                gu_copy(dd, l, m, e, c).wait_recv()
                gu[l, m, e, c] = bf(acc[dd] + gu[l, m, e, c].astype(jnp.float32))
                gu_copy(dd, l, m, e, c).start()

            @pl.when(valid & last[dd])
            def _():
                gu_copy(dd, l, m, e, c).wait_recv()
                total = acc[dd] + gu[l, m, e, c].astype(jnp.float32)
                r = router_column(slots[l, m, e], e, width, experts)
                gate = total[:, :hw]
                hid[l, m, e, c] = bf(gate * jax.nn.sigmoid(gate) * total[:, hw:] * jax.nn.sigmoid(r))
                hid_copy(dd, l, m, e, c).start()
                gu[l, m, e, c] = bf(total)
                save_gates(l, m, e, c).start()

        for dd in range(2):
            valid, l, m, e, c = spreads[dd]

            @pl.when(valid & jnp.logical_not(last[dd]))
            def _():
                hid_copy(dd, l, m, e, c).wait_recv()

                @pl.when(jnp.logical_not(first[dd]))
                def _():
                    hid_copy(dd, l, m, e, c).start()

        for dd in range(2):
            valid, l, m, e, c = spreads[dd]

            @pl.when(valid & (c == 1))
            def _():
                @pl.when(m == 0)
                def _():
                    wait_weight(0, e, 1)

                total = mm(hid[l, m, e, 0], wdt[e, :, :hw], ((1,), (1,)))
                eo[m, e] = bf(total + mm(hid[l, m, e, 1], wdt[e, :, hw:], ((1,), (1,))))

                @pl.when((l == 0) & (m == 1))
                def _():
                    start_weight(1, e, 1)

    kept = (
        (slots, slots_o), (nall, rows_o), (q, q_o), (k, k_o), (v, v_o), (att, att_o), (mid, mid_o), (n2, n2_o),
        (nrows, rows2_o), (sgu, sgu_o), (shid, shid_o), (shw0, shw_o.at[0]), (shw1, shw_o.at[1]), (watt1, watt_o),
        (watt0, watt0_o), (tok, tok_o), (small, small_o), (place, place_o), (place_t, place_to),
        (gslots, gslots_o), (hid, hid_o), (y, y_o),
    )
    saves = [pltpu.make_async_copy(src, dst, k_sem.at[c]) for c, (src, dst) in enumerate(kept)]

    def save(copies):
        for copy in copies:
            copy.start()

    stages = {}

    def at(step, do):
        stages.setdefault(step, []).append(do)

    def stage(do, l, m):
        return lambda: do(l, m)

    osend[...] = jnp.zeros_like(osend)
    ssend[...] = jnp.zeros_like(ssend)
    rwx[...] = jnp.zeros_like(rwx)
    for h in range(1, ny):
        for share in entry_shares[:2]:
            share.hop(h)
        if h == 2:
            entry_shares[2].hop(1)
            entry_shares[3].hop(1)
    for share in entry_shares[:2]:
        share.finish()
    tokens_ready()
    for l, full in enumerate((sm0, sm1)):
        for j in range(ny):
            small[l, :, j * pw : (j + 1) * pw] = full[j]
    for l in range(2):
        rwx[l, width : width + experts] = bf(small[l, :experts])
        rwx[l, width + experts : width + 2 * experts] = bf(small[l, :experts])
    norm_first(0, 0)
    norm_first(0, 1)
    entry_shares[2].hop(2)
    entry_shares[3].hop(2)
    places()
    entry_shares[2].hop(3)
    entry_shares[3].hop(3)
    entry_shares[2].finish()
    entry_shares[3].finish()
    shares[0].start()
    shares[1].start()
    attention(0, 0)
    attention(0, 1)
    norm_second(0, 0)
    norm_second(0, 1)
    weights_ready()
    spread(0, 0)
    shares[0].hop(1)
    shares[1].hop(1)
    spread(0, 1)
    dispatch(0, 0)
    for h in range(2, ny):
        at(2 * (h - 2), lambda h=h: (shares[0].hop(h), shares[1].hop(h)))
    at(units // 4, stage(dispatch, 0, 1))
    at(2 * (ny - 2) + 1, lambda: (shares[0].finish(), shares[1].finish()))
    at(units // 2, stage(shared_in_part, 0, 0))
    at(units // 2 + 2, stage(shared_out_part, 0, 0))
    at(units, stage(shared_in_part, 0, 1))
    at(units + 2, stage(shared_out_part, 0, 1))
    for m in range(2):
        done = starts[m] + units - 1 + lag
        for c, do in enumerate((combine, combine_line)):
            at(done + c * apart, stage(do, 0, m))
        at(done + 2 * apart, stage(layer_out, 0, m))
        for c, do in enumerate((norm_first, attention, norm_second, spread, dispatch)):
            at(done + (2 + c) * apart, stage(do, 1, m))
        at(starts[2 + m] + 4, stage(shared_in_part, 1, m))
        at(starts[2 + m] + 8, stage(shared_out_part, 1, m))
        done = starts[2 + m] + units - 1 + lag
        for c, do in enumerate((combine, combine_line, layer_out)):
            at(done + c * apart, stage(do, 1, m))
    at(starts[3] + 9, lambda: save(saves[:-2]))
    at(starts[3] + units - 1 + lag, lambda: save(saves[-2:-1]))
    for m in range(2):
        at(units + 4 + m, lambda m=m: grad_send(m))
        at(units + 6 + m, lambda m=m: grad_spread(m))
        at(units + 8 + m, lambda m=m: grad_dispatch(m))
    at(units + lag - 1, shares[2].start)
    for h in range(1, ny):
        at(units + lag - 1 + 2 * h, lambda h=h: shares[2].hop(h))
    at(units + lag - 1 + 2 * ny, shares[2].finish)

    def step(i, c):
        chain(i)
        for when in sorted(stages):
            if when < steps:
                @pl.when(i == when)
                def _():
                    for do in stages[when]:
                        do()

        return c

    lax.fori_loop(0, steps, step, 0)
    for when in sorted(stages):
        if when >= steps:
            for do in stages[when]:
                do()
    saves[-1].start()

    def finish(index, carry):
        l = index // (mbs * units)
        m = lax.rem(index // units, mbs)
        r = lax.rem(index, units)
        for dd in range(2):
            e, c = r // 2 + dd * half, lax.rem(r, 2)
            pl.when(jnp.logical_not(last[dd]))(gu_copy(dd, l, m, e, c).wait_send)
            pl.when(jnp.logical_not(first[dd]))(hid_copy(dd, l, m, e, c).wait_send)
            pl.when(last[dd])(save_gates(l, m, e, c).wait)
        return carry

    lax.fori_loop(0, 2 * mbs * units, finish, 0)
    for copy in saves:
        copy.wait()


def forward(tin, small_b, att_block, sh_block, routes, cos, sin, rot, win, wdt, dims, heads, features, ids):
    width, pw, experts, cap = dims
    nx, ny = lax.axis_size("gx"), lax.axis_size("gy")
    mbs, length = tin.shape[1:3]
    sub, d = length // nx, ny * pw
    f = wdt.shape[-1]
    length, tokens, n, slots = nx * sub, nx * ny * sub, nx * ny, experts * cap
    b16, f32 = jnp.bfloat16, jnp.float32
    vm = pl.BlockSpec(memory_space=pltpu.VMEM)
    hbm = pl.BlockSpec(memory_space=pl.ANY)
    lm = (2, mbs)
    rows_shape = lm + (nx, sub, d)
    spread_shape = lm + (ny, nx, sub, pw)
    entry = (
        (win.shape, b16), (wdt.shape, b16),
        ((2, mbs, sub, d), b16), ((2, small_b.shape[0], d), f32), (lm + (2, tokens), jnp.int32),
        (lm + (tokens, 2), jnp.int32), ((ny,) + att_block.shape, b16),
    )
    kept = entry + (
        (lm + (sub, d), b16), (lm + (sub, d), f32), (lm + (sub, d), b16), (rows_shape, b16),
        (lm + (length, pw), b16), (lm + (length, pw), b16), (lm + (length, pw), b16), (lm + (length, pw), b16),
        (lm + (experts, cap, pw), b16), (lm + (experts, 2, cap, f), b16), (lm + (experts, 2, cap, f // 2), b16),
        (rows_shape, b16), (lm + (length, 2 * f), b16), (lm + (length, f), b16),
        ((2, ny) + sh_block.shape, b16), ((ny,) + att_block.shape, b16), ((mbs, experts, cap, pw), b16),
    )
    scratch = (
        (lm + (sub, d), b16), (lm + (sub, d), f32), (lm + (sub, d), b16), None,
        (lm + (sub, d), b16), (rows_shape, b16), ((length, 3 * pw), f32),
        (lm + (length, pw), b16), (lm + (length, pw), b16), (lm + (length, pw), b16), (lm + (length, pw), b16),
        (rows_shape, b16), (rows_shape, b16), ((2, pw, d), b16),
        (lm + (ny, sub, pw), b16), (lm + (ny, sub, pw), b16), (spread_shape, b16), (rows_shape, b16),
        ((slots, tokens), b16), ((tokens, slots), b16), (lm + (experts, cap, pw), b16), ((2, cap, f), f32),
        (lm + (experts, 2, cap, f), b16), (lm + (experts, 2, cap, f // 2), b16), ((mbs, experts, cap, width), b16),
        (lm + (length, 2 * f), b16), (lm + (length, f), b16), (rows_shape, b16), (rows_shape, b16),
        (lm + (nx, ny, sub, pw), b16), (lm + (nx, ny, sub, pw), b16), (lm + (ny, sub, pw), b16), (lm + (ny, sub, pw), b16),
        (win.shape, b16), (wdt.shape, b16),
        ((ny,) + sh_block.shape, b16), ((ny,) + sh_block.shape, b16), ((ny,) + att_block.shape, b16), ((ny,) + att_block.shape, b16),
        ((ny, 2, mbs, sub, pw), b16), ((2, mbs, sub, d), b16), (lm + (2, tokens), jnp.int32),
        (lm + (2, tokens), jnp.int32), (lm + (tokens, 2), jnp.int32),
        ((ny,) + small_b.shape, f32), ((ny,) + small_b.shape, f32), ((2, small_b.shape[0], d), f32),
        ((mbs, ny, nx, sub, pw), b16), ((mbs, experts, cap, pw), b16),
    )
    outs = pl.pallas_call(
        functools.partial(forward_kernel, (nx, ny, mbs, sub, width, pw, heads, features, experts, cap, f, *FWD_SKEW)),
        out_shape=tuple(jax.ShapeDtypeStruct(*v) for v in kept),
        in_specs=[vm] * 8 + [hbm] * 2,
        out_specs=(hbm,) * len(kept),
        scratch_shapes=[pltpu.VMEM(*(v or ((8, 128), f32))) for v in scratch] + [
            flags(lm + (nx,)), flags(lm + (nx,)), flags(lm + (nx,)), flags(lm + (nx,)),
            flags(lm + (ny,)), flags(lm + (ny,)), flags(lm + (nx,)), flags(lm + (nx,)), flags(lm + (nx,)), flags(lm + (nx,)),
            flags(lm + (nx,)), flags(lm + (nx,)), flags(lm + (nx,)), flags(lm + (nx,)), flags(lm + (ny,)), flags(lm + (ny,)),
            flags(lm + (experts, 2)), flags(lm + (experts, 2)), flags(lm + (experts, 2)), flags(lm + (experts, 2)),
            flags((experts,)), flags((experts,)), flags(lm + (experts, 2)), flags((24,)),
            flags((nx,)), flags((ny,)), pltpu.SemaphoreType.DMA, pltpu.SemaphoreType.DMA, flags((2,)), flags((2,)), flags((mbs, nx)), flags((mbs, nx)),
        ] + share_sems(ny) * 7,
        compiler_params=params(ids),
        cost_estimate=pl.CostEstimate(flops=10**10, bytes_accessed=8 * 10**7, transcendentals=10**6),
        name="forward",
    )(tin, small_b, att_block, sh_block, routes, cos, sin, rot, win, wdt)
    names = ("win", "wdt", "tok", "small", "place", "place_t", "watt0", "y", "mid", "n2", "rows", "q", "k", "v", "att", "slots", "gu", "hid", "rows2", "sgu", "shid", "shw", "watt1", "gslots")
    return dict(zip(names, outs))


FWD_SKEW = (2, 2)
STAGE_STEPS = 2


def backward_kernel(cfg, *refs):
    nx, ny, mbs, sub, width, pw, heads, features, experts, cap, f, sk, ak = cfg
    (tok_i, small_i, place_i, y_i, mid_i, n2_i, rows_i, q_i, k_i, v_i, att_i, rows2_i, sgu_i, shid_i, shw_i,
     watt0_i, watt1_i, cos, sin, rot, slots_i, gu_i, hid_i, gslots_i, win_a, win_b, wdt_a, wdt_b) = refs[:28]
    (out_o, win_g, wdt_g, att_g, sh_g, small_g,
     win, wdt, xsend, xline, xall, grows, pm, pt, slots, gslots, gown, hid, acc, dh, dgu, deo, sti, std,
     dsgu, ssend, srecv, rsend, rpeer, rline, rrecv, rwx, dm, msend, mall, datt, dqkv, dsend, drecv,
     rw_p, gains, drs, sh_p, att_p, small_p, sh_x, att_x, small_x, sh_r, att_r, small_r, sh_f, att_f, small_f, small_a,
     yv, obuf, g, gx, small, place, x, mid, n2, rows, q, k, v, att, rows2, sgu, shid, shw, watt,
     w_sem, x_send, x_recv, u_send, u_recv, t_send, t_recv, s_send, s_recv, g_send, g_recv, r_send, r_recv,
     m_send, m_recv, d_send, d_recv, rs_send, rs_recv, ag_send, ag_recv, wi_send, wi_recv, wd_send, wd_recv,
     c_send, c_recv, e_send, e_recv, a_send, a_recv, l_sem, st_sem, f_sem, y_sem, o_send, o_recv, free) = refs[28:]
    pos = Position(nx, ny)
    s, a, b = pos.s, pos.a, pos.b
    slots_n = experts * cap
    tokens = nx * ny * sub
    d = ny * pw
    length = nx * sub
    half, hw = experts // 2, f // 2
    scale = DH ** -0.5
    lane = lax.broadcasted_iota(jnp.int32, (1, pw), 1)
    first = (b == ny - 1, b == 0)
    last = (b == 0, b == ny - 1)
    up = (ny - 1 - b, b)
    down = (b, ny - 1 - b)
    barrier = pltpu.get_barrier_semaphore()
    pos.peers(lambda ai: pl.semaphore_signal(barrier, inc=1, device_id=(s, ai, b), device_id_type=MESH))
    pos.line(lambda bi: pl.semaphore_signal(barrier, inc=1, device_id=(s, a, bi), device_id_type=MESH))
    pl.semaphore_signal(barrier, inc=1, device_id=(1 - s, a, b), device_id_type=MESH)
    for so in range(2):
        for i in range(nx):
            @pl.when((so != s) | (i != a) | (a != b))
            def _():
                pl.semaphore_signal(barrier, inc=1, device_id=(so, i, a), device_id_type=MESH)

    def weight_copy(l, e, which):
        own, oth, dst = ((win_a, win_b, win), (wdt_a, wdt_b, wdt))[which]
        sem = w_sem.at[which, e]
        return pltpu.make_async_copy(own.at[e], dst.at[e], sem), pltpu.make_async_copy(oth.at[e], dst.at[e], sem)

    def start_weights(l, e):
        for which in range(2):
            own, oth = weight_copy(l, e, which)
            pl.when(s == l)(own.start)
            pl.when(s != l)(oth.start)

    def first_weights(e, c):
        start_weights(1, e)
        return c

    lax.fori_loop(0, experts, first_weights, 0)

    early = ((rows2_i, rows2), (sgu_i, sgu), (shid_i, shid), (shw_i, shw))
    later = ((mid_i, mid), (n2_i, n2), (rows_i, rows), (q_i, q), (k_i, k), (v_i, v), (att_i, att))

    def early_loads(l):
        return [pltpu.make_async_copy(src.at[l], dst, y_sem.at[c]) for c, (src, dst) in enumerate(early)]

    def later_loads(l):
        copies = [pltpu.make_async_copy(src.at[l], dst, y_sem.at[4 + c]) for c, (src, dst) in enumerate(later)]
        copies.append(pltpu.make_async_copy(y_i.at[0] if l else tok_i.at[0], x, y_sem.at[11]))
        return copies + [pltpu.make_async_copy(watt1_i if l else watt0_i, watt, y_sem.at[12])]

    def hid_load(l):
        return pltpu.make_async_copy(hid_i.at[l], hid, l_sem.at[1])

    def gates(l, m, dd):
        return pltpu.make_async_copy(gu_i.at[l, m, pl.ds(dd * half, half)], gown.at[m], l_sem.at[2 + m])

    def start_gates(l, m):
        for dd in range(2):
            pl.when(last[dd])(gates(l, m, dd).start)

    def wait_gates(l, m):
        for dd in range(2):
            pl.when(last[dd])(gates(l, m, dd).wait)

    first_loads = [
        pltpu.make_async_copy(src, dst, y_sem.at[13 + c])
        for c, (src, dst) in enumerate(((tok_i.at[1], g), (small_i, small), (place_i, place), (y_i, yv)))
    ]
    slots_load = pltpu.make_async_copy(slots_i, slots, l_sem.at[0])
    gslots_load = pltpu.make_async_copy(gslots_i, gslots.at[1], l_sem.at[4])
    for copy in first_loads + [slots_load, gslots_load, hid_load(1)] + early_loads(1) + later_loads(1):
        copy.start()
    for m in range(mbs):
        start_gates(1, m)

    def copy_x(m, bi, slot):
        return remote(xsend.at[m, bi], xline.at[m, slot], x_send.at[m, bi], x_recv.at[m, slot], (s, a, bi))

    def copy_w(m, ai, slot):
        return remote(xline.at[m], xall.at[m, :, slot], u_send.at[m, ai], u_recv.at[m, slot], (s, ai, b))

    def copy_t(m, ai, slot):
        return remote(g.at[m], grows.at[m, slot], t_send.at[m, ai], t_recv.at[m, slot], (s, ai, b))

    for copy in first_loads:
        copy.wait()

    @pl.when(a == b)
    def _():
        pl.semaphore_wait(barrier, nx - 1 + ny - 1 + 1 + 2 * ny - 1)

    @pl.when(a != b)
    def _():
        pl.semaphore_wait(barrier, nx - 1 + ny - 1 + 1 + 2 * ny)

    def out_copy(kind, l, j, s_slot, a_slot):
        src = (yv, gx)[kind].at[l, :, :, pl.ds(j * pw, pw)]
        return remote(src, obuf.at[kind, s_slot, a_slot], o_send.at[kind, l, j], o_recv.at[kind, s_slot, a_slot], (l, b, j))

    def send_out(kind, l):
        for j in range(ny):
            @pl.when((l != s) | (a != b) | (j != b))
            def _():
                out_copy(kind, l, j, s, a).start()

        @pl.when((l == s) & (a == b))
        def _():
            obuf[kind, s, a] = (yv, gx)[kind][l, :, :, pl.ds(pl.multiple_of(b * pw, pw), pw)]

    def sent_out(kind, l):
        for j in range(ny):
            @pl.when((l != s) | (a != b) | (j != b))
            def _():
                out_copy(kind, l, j, s, a).wait_send()

    def take_out(kind):
        for so in range(2):
            for i in range(nx):
                @pl.when((so != s) | (a != b) | (i != a))
                def _():
                    out_copy(kind, 0, 0, so, i).wait_recv()

                out_o[kind, so * mbs : (so + 1) * mbs, i * sub : (i + 1) * sub, :] = obuf[kind, so, i]

    def send_g(m, slots_too=True):
        if slots_too:
            for j in range(ny):
                xsend[m, j] = g[m, :, j * pw : (j + 1) * pw]
            pos.line(lambda bi: copy_x(m, bi, b).start())
            xline[m, b] = xsend[m, b]
        pos.peers(lambda ai: copy_t(m, ai, a).start())
        grows[m, a] = g[m]

    send_g(0, False)
    send_g(1, False)
    deo[...] = jnp.zeros_like(deo)
    ssend[...] = jnp.zeros_like(ssend)
    dsend[...] = jnp.zeros_like(dsend)
    rwx[...] = jnp.zeros_like(rwx)

    def new_layer(l):
        rwx[width : width + experts] = bf(small[l, :experts])
        rwx[width + experts : width + 2 * experts] = bf(small[l, :experts])
        rw_p[...] = jnp.zeros_like(rw_p)
        gains[...] = jnp.zeros_like(gains)

    new_layer(1)

    def spread(m):
        pos.line(lambda bi: copy_x(m, bi, bi).wait())
        pos.peers(lambda ai: copy_w(m, ai, a).start())
        xall[m, :, a] = xline[m]

    def dispatch(l, m):
        i0 = lax.broadcasted_iota(jnp.int32, (slots_n, tokens), 0)
        pm[...] = bf(((place[l, m, 0:1] == i0) | (place[l, m, 1:2] == i0)).astype(jnp.float32))
        pos.peers(lambda ai: copy_w(m, ai, ai).wait())
        gslots[l, m] = bf(mm(pm[...], xall[m].reshape(tokens, pw))).reshape(experts, cap, pw)

    def shared_act(m):
        pos.peers(lambda ai: copy_t(m, ai, ai).wait())
        dsh = by_blocks(grows[m].reshape(length, d), shw, slice(2 * f, 3 * f), width, pw)
        dsg, dsu, _ = act_back(sgu[m, :, :f].astype(jnp.float32), sgu[m, :, f:].astype(jnp.float32), dsh, None)
        dsgu[m, :, :f] = bf(dsg)
        dsgu[m, :, f:] = bf(dsu)

    def copy_s(m, ai, slot):
        return remote(ssend.at[m, ai], srecv.at[m, slot], s_send.at[m, ai], s_recv.at[m, slot], (s, ai, b))

    def shared_back(m):
        for j in range(ny):
            part = mm(dsgu[m], shw[j, :, : 2 * f], ((1,), (1,)))
            ssend[m, :, :, j * pw : j * pw + width] = bf(part).reshape(nx, sub, width)
        pos.peers(lambda ai: copy_s(m, ai, a).start())
        srecv[m, a] = ssend[m, a]

    crossing = ((sh_p, sh_x), (att_p, att_x), (small_p, small_x))
    places = (sh_r, att_r, small_r)
    finals = (sh_f, att_f, small_f)
    results = (sh_g, att_g, small_g)

    def cross(l, i):
        return remote(crossing[i][0], crossing[i][1], c_send.at[i], c_recv.at[i], (l, a, b))

    def block(i, bi):
        if i == 2:
            return small_x.at[:, pl.ds(pl.multiple_of(bi * pw, pw), pw)]
        return crossing[i][1].at[bi]

    def along(i, bi, slot):
        return remote(block(i, bi), places[i].at[slot], e_send.at[i, bi], e_recv.at[i, slot], (s, a, bi))

    def give(l, i):
        pl.when(s != l)(cross(l, i).start)

    def given(l):
        for i in range(3):
            pl.when(s != l)(cross(l, i).wait_send)

    def join(l, i):
        @pl.when(s == l)
        def _():
            cross(l, i).wait_recv()
            part, other = crossing[i]
            other[...] = (part[...].astype(jnp.float32) + other[...].astype(jnp.float32)).astype(other.dtype)
            pos.line(lambda bi: along(i, bi, lax.rem(b - bi + ny, ny) - 1).start())

    def settle(l, i):
        @pl.when(s == l)
        def _():
            pos.line(lambda bi: along(i, bi, lax.rem(bi - b + ny, ny) - 1).wait())
            total = block(i, b)[...].astype(jnp.float32)
            for c in range(1, ny):
                total = total + places[i][c - 1].astype(jnp.float32)
            finals[i][...] = total
            if i < 2:
                pltpu.make_async_copy(finals[i], results[i], f_sem.at[i]).start()

    def shared_grads():
        for j in range(ny):
            rj = rows2[:, :, :, j * pw : j * pw + width].reshape(mbs * length, width)
            sh_p[j, :, : 2 * f] = bf(mm(rj, dsgu[...].reshape(mbs * length, 2 * f), ((0,), (0,))))

    def down_grads(l):
        for j in range(ny):
            gj = grows[:, :, :, j * pw : j * pw + width].reshape(mbs * length, width)
            sh_p[j, :, 2 * f :] = bf(mm(gj, shid[...].reshape(mbs * length, f), ((0,), (0,))))
        give(l, 0)

    def copy_g(m, ai, slot):
        return remote(rsend.at[m, ai], rpeer.at[m, slot], g_send.at[m, ai], g_recv.at[m, slot], (s, ai, b))

    def copy_r(m, bi, slot):
        return remote(rline.at[m, bi], rrecv.at[m, slot], r_send.at[m, bi], r_recv.at[m, slot], (s, a, bi))

    def combine(l, m):
        row = lax.broadcasted_iota(jnp.int32, (128, tokens), 0)
        pair = place[l, m].astype(jnp.float32)
        cols = jnp.where(row == 0, pair[0:1], jnp.where(row == 1, pair[1:2], 0.0)).T.astype(jnp.int32)
        part = tokens // 2
        i1 = lax.broadcasted_iota(jnp.int32, (part, slots_n), 1)
        for c in range(2):
            these = cols[c * part : (c + 1) * part]
            pt[...] = bf(((these[:, 0:1] == i1) | (these[:, 1:2] == i1)).astype(jnp.float32))
            br = bf(mm(pt[...], deo[m].reshape(slots_n, pw))).reshape(ny // 2, nx, sub, pw)
            for ai in range(nx):
                rsend[m, ai, c * (ny // 2) : (c + 1) * (ny // 2)] = br[:, ai]
        pos.peers(lambda ai: copy_g(m, ai, a).start())
        rpeer[m, a] = rsend[m, a]

    def combine_line(m):
        pos.peers(lambda ai: copy_g(m, ai, ai).wait())
        total = rpeer[m, 0].astype(jnp.float32)
        for ai in range(1, nx):
            total = total + rpeer[m, ai].astype(jnp.float32)
        rline[m] = bf(total)
        pos.line(lambda bi: copy_r(m, bi, b).start())
        rrecv[m, b] = rline[m, b]

    def copy_m(m, ai, slot):
        return remote(msend.at[m], mall.at[m, slot], m_send.at[m, ai], m_recv.at[m, slot], (s, ai, b))

    def second_norm(l, m):
        pos.peers(lambda ai: copy_s(m, ai, ai).wait())
        pos.line(lambda bi: copy_r(m, bi, bi).wait())
        dlog = jnp.zeros((sub, pw), jnp.float32)
        parts = []
        for j in range(ny):
            part = rrecv[m, j].astype(jnp.float32)
            dlog = dlog + jnp.where(lane >= width, part, 0.0)
            parts.append(jnp.where(lane < width, part, 0.0))
        hi = bf(dlog)
        lo = bf(dlog - hi.astype(jnp.float32))
        dn2 = jnp.concatenate(parts, 1) + mm(hi, rwx[...]) + mm(lo, rwx[...])
        for ai in range(nx):
            dn2 = dn2 + srecv[m, ai].astype(jnp.float32)
        rw_t = mm(hi, n2[m], ((0,), (0,))) + mm(lo, n2[m], ((0,), (0,)))
        rw_p[...] += rw_t[width : width + experts] + rw_t[width + experts : width + 2 * experts]
        mv = mid[m]
        dx2, gain_g = norm_back(mv, rms(mv, features), small[l, experts : experts + 1], dn2, features)
        gains[0:1] += gain_g
        dm[m] = g[m].astype(jnp.float32) + dx2
        msend[m] = bf(dm[m])
        pos.peers(lambda ai: copy_m(m, ai, a).start())
        mall[m, a] = msend[m]

    def copy_d(m, ai, slot):
        return remote(dsend.at[m, ai], drecv.at[m, slot], d_send.at[m, ai], d_recv.at[m, slot], (s, ai, b))

    def attention(m):
        pos.peers(lambda ai: copy_m(m, ai, ai).wait())
        datt[...] = bf(by_blocks(mall[m].reshape(length, d), watt, slice(3 * pw, 4 * pw), width, pw))
        dq = jnp.zeros((length, pw), jnp.float32)
        dk = dq
        dv = dq
        for h in range(heads):
            mask = head_mask(pw, h)
            qh = jnp.where(mask, q[m], 0)
            kh = jnp.where(mask, k[m], 0)
            da = jnp.where(mask, datt[...], 0)
            p = probs_of(qh, k[m])
            dp = mm(da, v[m], ((1,), (1,)))
            ds = bf(p * (dp - jnp.sum(dp * p, axis=1, keepdims=True)))
            dv = dv + mm(bf(p), da, ((0,), (0,)))
            dq = dq + mm(ds, kh)
            dk = dk + mm(ds, qh, ((0,), (0,)))
        dqkv[m, :, :pw] = turn(dq * scale, cos[...], sin[...], rot[...], -1.0)
        dqkv[m, :, pw : 2 * pw] = turn(dk * scale, cos[...], sin[...], rot[...], -1.0)
        dqkv[m, :, 2 * pw :] = bf(dv)
        for j in range(ny):
            part = mm(dqkv[m], watt[j, :, : 3 * pw], ((1,), (1,)))
            dsend[m, :, :, j * pw : j * pw + width] = bf(part).reshape(nx, sub, width)
        pos.peers(lambda ai: copy_d(m, ai, a).start())
        drecv[m, a] = dsend[m, a]

    def first_norm(l, m):
        pos.peers(lambda ai: copy_d(m, ai, ai).wait())
        dn1 = drecv[m, 0].astype(jnp.float32)
        for ai in range(1, nx):
            dn1 = dn1 + drecv[m, ai].astype(jnp.float32)
        xv = x[m].astype(jnp.float32)
        dx1, gain_g = norm_back(xv, rms(xv, features), small[l, experts + 1 : experts + 2], dn1, features)
        gains[1:2] += gain_g
        gx[l, m] = bf(dm[m] + dx1)
        if l:
            g[m] = gx[l, m]
            send_g(m)

    def attention_grads(l):
        for j in range(ny):
            cols = slice(j * pw, j * pw + width)
            rj = rows[:, :, :, cols].reshape(mbs * length, width)
            mj = mall[:, :, :, cols].reshape(mbs * length, width)
            att_p[j, :, : 3 * pw] = bf(mm(rj, dqkv[...].reshape(mbs * length, 3 * pw), ((0,), (0,))))
            att_p[j, :, 3 * pw :] = bf(mm(mj, att[...].reshape(mbs * length, pw), ((0,), (0,))))
        give(l, 1)

    def small_grads(l):
        small_p[:experts] = rw_p[...]
        small_p[experts:] = gains[...]
        give(l, 2)

    lag = (sk + ak) * (ny - 1)
    apart = STAGE_STEPS
    units = 2 * half
    gap = max(lag + 6 * apart - units, 0)
    starts = (0, units, 2 * units + gap, 3 * units + gap)

    def unit(t, dd):
        soon = (t >= 0) & (t < 2 * units)
        then = (t >= starts[2]) & (t < starts[2] + 2 * units)
        u = jnp.clip(jnp.where(t < starts[2], jnp.minimum(t, 2 * units - 1), t - gap), 0, 4 * units - 1)
        job, r = u // units, lax.rem(u, units)
        return soon | then, 1 - job // 2, lax.rem(job, 2), r // 2 + dd * half, lax.rem(r, 2)

    def dh_copy(dd, l, m, e, c):
        to = b - 1 if dd == 0 else b + 1
        return remote(dh.at[m, e, c], dh.at[m, e, c], rs_send.at[l, m, e, c], rs_recv.at[l, m, e, c], (s, a, to))

    def dgu_copy(dd, l, m, e, c):
        to = b + 1 if dd == 0 else b - 1
        return remote(dgu.at[m, e, c], dgu.at[m, e, c], ag_send.at[l, m, e, c], ag_recv.at[l, m, e, c], (s, a, to))

    def wi_copy(l, e):
        return remote(win.at[e], win.at[e], wi_send.at[l, e], wi_recv.at[l, e], (l, a, b))

    def wd_copy(l, e):
        return remote(wdt.at[e], wdt.at[e], wd_send.at[l, e], wd_recv.at[l, e], (l, a, b))

    def st_copies(e):
        return (pltpu.make_async_copy(sti, win_g.at[e], st_sem.at[0]), pltpu.make_async_copy(std, wdt_g.at[e], st_sem.at[1]))

    def weight_grads(l, e):
        sl = slots[l, :, e, :, :width].reshape(mbs * cap, width)
        gs = gslots[l, :, e, :, :width].reshape(mbs * cap, width)
        gi = [mm(sl, dgu[:, e, c].reshape(mbs * cap, f), ((0,), (0,))) for c in range(2)]
        gd = [mm(gs, hid[:, e, c].reshape(mbs * cap, hw), ((0,), (0,))) for c in range(2)]
        return gi, gd

    late = 2
    steps = starts[3] + units + lag + 2 * late

    def chain(i):
        reduce = [unit(i - sk * up[dd], dd) for dd in range(2)]
        spreads = [unit(i - sk * (ny - 1) - ak * down[dd], dd) for dd in range(2)]
        for dd in range(2):
            valid, l, m, e, c = reduce[dd]

            @pl.when(valid)
            def _():
                @pl.when((m == 0) & (c == 0))
                def _():
                    weight_copy(0, e, 1)[0].wait()

                acc[dd] = mm(gslots[l, m, e, :, :width], wdt[e, :, pl.ds(pl.multiple_of(c * hw, hw), hw)])

            @pl.when(valid & first[dd])
            def _():
                dh[m, e, c] = bf(acc[dd])
                dh_copy(dd, l, m, e, c).start()

            @pl.when(valid & jnp.logical_not(first[dd] | last[dd]))
            def _():
                dh_copy(dd, l, m, e, c).wait_recv()
                dh[m, e, c] = bf(acc[dd] + dh[m, e, c].astype(jnp.float32))
                dh_copy(dd, l, m, e, c).start()

            @pl.when(valid & last[dd])
            def _():
                dh_copy(dd, l, m, e, c).wait_recv()
                total = acc[dd] + dh[m, e, c].astype(jnp.float32)
                r = router_column(slots[l, m, e], e, width, experts)
                gate = gown[m, e - dd * half, c, :, :hw].astype(jnp.float32)
                upv = gown[m, e - dd * half, c, :, hw:].astype(jnp.float32)
                dgate, dup, dr = act_back(gate, upv, total, jax.nn.sigmoid(r))
                dgu[m, e, c, :, :hw] = bf(dgate)
                dgu[m, e, c, :, hw:] = bf(dup)
                dgu_copy(dd, l, m, e, c).start()
                dr = jnp.where(c == 0, 0.0, drs[dd][:, 0:1]) + dr
                drs[dd] = jnp.broadcast_to(dr, (cap, 128))
                hi = bf(dr).astype(jnp.float32)
                deo[m, e] = bf(jnp.where(lane == width + e, hi, jnp.where(lane == width + experts + e, dr - hi, 0.0)))

        for dd in range(2):
            valid, l, m, e, c = spreads[dd]

            @pl.when(valid & jnp.logical_not(last[dd]))
            def _():
                dgu_copy(dd, l, m, e, c).wait_recv()

                @pl.when(jnp.logical_not(first[dd]))
                def _():
                    dgu_copy(dd, l, m, e, c).start()

        for dd in range(2):
            valid, l, m, e, c = spreads[dd]

            @pl.when(valid & (c == 1))
            def _():
                @pl.when(m == 0)
                def _():
                    weight_copy(0, e, 0)[0].wait()

                total = None
                for c2 in range(2):
                    for plane in range(2):
                        cols, hcols = slice(plane * hw, (plane + 1) * hw), slice(c2 * hw, (c2 + 1) * hw)
                        part = mm(dgu[m, e, c2, :, cols], win[e, plane, :, hcols], ((1,), (1,)))
                        total = part if total is None else total + part
                deo[m, e, :, :width] = bf(total)

        for l in (1, 0):
            t = i - starts[3 - 2 * l] - lag
            weight_stage(l, t)

    def chain_sent(l, e, dd):
        for m in range(mbs):
            for c in range(2):
                pl.when(jnp.logical_not(last[dd]))(dh_copy(dd, l, m, e, c).wait_send)
                pl.when(jnp.logical_not(first[dd]))(dgu_copy(dd, l, m, e, c).wait_send)

    def weight_stage(l, t):
        u = t // 2
        on = (t >= 0) & (t < units) & (lax.rem(t + 2, 2) == 1)

        @pl.when(on)
        def _():
            for dd in range(2):
                chain_sent(l, jnp.clip(u, 0, half - 1) + dd * half, dd)

        @pl.when(on & (s == l))
        def _():
            pl.semaphore_signal(free.at[l], inc=1, device_id=(1 - s, a, b), device_id_type=MESH)

        @pl.when(on & (s != l))
        def _():
            pl.semaphore_wait(free.at[l], 1)
            for dd in range(2):
                e = jnp.clip(u, 0, half - 1) + dd * half
                gi, gd = weight_grads(l, e)
                for c in range(2):
                    for plane in range(2):
                        win[e, plane, :, c * hw : (c + 1) * hw] = bf(gi[c][:, plane * hw : (plane + 1) * hw])
                    wdt[e, :, c * hw : (c + 1) * hw] = bf(gd[c])
                wi_copy(l, e).start()
                wd_copy(l, e).start()

        t2 = t - 2 * late
        w = t2 // 2
        on2 = (t2 >= 0) & (t2 < units) & (lax.rem(t2 + 8, 2) == 1)

        @pl.when(on2 & (s != l))
        def _():
            for dd in range(2):
                e = jnp.clip(w, 0, half - 1) + dd * half
                wi_copy(l, e).wait_send()
                wd_copy(l, e).wait_send()
                if l:
                    start_weights(0, e)

        @pl.when(on2 & (s == l))
        def _():
            for dd in range(2):
                e = jnp.clip(w, 0, half - 1) + dd * half
                gi, gd = weight_grads(l, e)
                wi_copy(l, e).wait_recv()
                wd_copy(l, e).wait_recv()

                @pl.when((w >= 1) | (dd == 1))
                def _():
                    for copy in st_copies(e):
                        copy.wait()

                for c in range(2):
                    hcols = slice(c * hw, (c + 1) * hw)
                    for plane in range(2):
                        part = gi[c][:, plane * hw : (plane + 1) * hw] + win[e, plane, :, hcols].astype(jnp.float32)
                        sti[:, plane * f + c * hw : plane * f + (c + 1) * hw] = bf(part)
                    std[:, hcols] = bf(gd[c] + wdt[e, :, hcols].astype(jnp.float32))
                for copy in st_copies(e):
                    copy.start()
                if l:
                    start_weights(0, e)

    stages = {}

    def at(step, do, *args):
        stages.setdefault(step, []).append(lambda: do(*args))

    def shared_first(l, m):
        if m == 0:
            for copy in early_loads(l):
                copy.wait()
        shared_act(m)

    def reload(copies):
        for copy in copies:
            copy.start()

    def ready(copies):
        for copy in copies:
            copy.wait()

    ready([slots_load, gslots_load, hid_load(1)] + later_loads(1))
    for m in range(mbs):
        wait_gates(1, m)
    for l in (1, 0):
        begin = starts[2 - 2 * l]
        second = starts[3 - 2 * l]
        at(begin + 3, shared_first, l, 0)
        at(begin + 5, shared_back, 0)
        at(second + (-10 if l else 1), shared_first, l, 1)
        at(second + (-8 if l else 3), shared_back, 1)
        at(second + (-6 if l else 5), shared_grads)
        at(second + (-4 if l else 6), down_grads, l)
        at(second + (1 if l else 9), join, l, 0)
        for m in range(2):
            done = starts[2 - 2 * l + m] + units - 1 + lag
            for c, (do, *args) in enumerate((
                    (combine, l, m), (combine_line, m), (second_norm, l, m), (attention, m), (first_norm, l, m))):
                at(done + c * apart, do, *args)
            if l:
                at(starts[m] + units + sk * (ny - 1), start_gates, 0, m)
                at(done + 5 * apart, spread, m)
                at(done + 6 * apart, dispatch, 0, m)
                at(starts[2 + m] - 1, wait_gates, 0, m)
        end = second + units - 1 + lag
        at(end + 3 * apart, attention_grads, l)
        at(end + 4 * apart, join, l, 1)
        at(end + 4 * apart, small_grads, l)
        at(end + 5 * apart, join, l, 2)
        at(end + (2 if l else 4) * apart, settle, l, 0)
        at(end + (10 if l else 5) * apart, settle, l, 1)
        at(end + (10 if l else 5) * apart, settle, l, 2)
        at(end + (6 if l else 5) * apart, given, l)
    at(units // 2 - 1, send_out, 0, 0)
    at(units // 2 + 1, send_out, 0, 1)
    at(2 * units, take_out, 0)
    end = starts[1] + units - 1 + lag
    at(end + 4 * apart + 1, send_out, 1, 1)
    at(starts[3] + units - 1 + lag + 4 * apart, send_out, 1, 0)
    at(starts[1] + 1, lambda: reload(early_loads(0)))
    at(end + 2 * late + 1, lambda: reload([hid_load(0)]))
    at(end + 2 * late + 8, lambda: ready([hid_load(0)]))
    at(end + 5 * apart, lambda: reload(later_loads(0)))
    at(end + 10 * apart, lambda: ready(later_loads(0)))
    at(end + 10 * apart, new_layer, 0)

    def step(i, c):
        chain(i)
        for when in sorted(stages):
            if when < steps:
                @pl.when(i == when)
                def _():
                    for do in stages[when]:
                        do()

        return c

    lax.fori_loop(0, steps, step, 0)
    for when in sorted(stages):
        if when >= steps:
            for do in stages[when]:
                do()

    def copy_a(ai, slot):
        return remote(small_f, small_a.at[slot], a_send.at[ai], a_recv.at[slot], (s, ai, b))

    def gain_sums():
        pos.peers(lambda ai: copy_a(ai, a).start())
        small_a[a] = small_f[...]
        pos.peers(lambda ai: copy_a(ai, ai).wait())
        total = small_a[0]
        for ai in range(1, nx):
            total = total + small_a[ai]
        small_f[...] = total

    gain_sums()
    pltpu.make_async_copy(small_f, small_g, f_sem.at[2]).start()
    take_out(1)
    for l in range(2):
        for kind in range(2):
            sent_out(kind, l)
    for i in range(3):
        pltpu.make_async_copy(finals[i], results[i], f_sem.at[i]).wait()
    for copy in st_copies(experts - 1):
        copy.wait()


def backward(fwd, cos, sin, rot, win, wdt, dims, heads, features, ids):
    width, pw, experts, cap = dims
    nx, ny = lax.axis_size("gx"), lax.axis_size("gy")
    mbs, sub, d = fwd["tok"].shape[-3:]
    f = wdt.shape[-1]
    length, tokens, slots = nx * sub, nx * ny * sub, experts * cap
    b16, f32 = jnp.bfloat16, jnp.float32
    vm = pl.BlockSpec(memory_space=pltpu.VMEM)
    hbm = pl.BlockSpec(memory_space=pl.ANY)
    ac, sc, n, half = fwd["watt0"].shape[2], fwd["shw"].shape[3], fwd["small"].shape[1], experts // 2
    rows_shape = (mbs, nx, sub, d)
    dense = lambda c: ((ny, width, c), b16)
    scratch = (
        (win.shape, b16), (wdt.shape, b16),
        ((mbs, ny, sub, pw), b16), ((mbs, ny, sub, pw), b16), ((mbs, ny, nx, sub, pw), b16), (rows_shape, b16),
        ((slots, tokens), b16), ((tokens // 2, slots), b16),
        ((2, mbs, experts, cap, pw), b16), ((2, mbs, experts, cap, pw), b16), ((mbs, half, 2, cap, f), b16),
        ((mbs, experts, 2, cap, f // 2), b16), ((2, cap, f // 2), f32), ((mbs, experts, 2, cap, f // 2), b16),
        ((mbs, experts, 2, cap, f), b16), ((mbs, experts, cap, pw), b16),
        ((width, 2 * f), b16), ((width, f), b16),
        ((mbs, length, 2 * f), b16), (rows_shape, b16), (rows_shape, b16),
        ((mbs, nx, ny, sub, pw), b16), ((mbs, nx, ny, sub, pw), b16), ((mbs, ny, sub, pw), b16), ((mbs, ny, sub, pw), b16),
        ((pw, d), b16), ((mbs, sub, d), f32), ((mbs, sub, d), b16), (rows_shape, b16),
        ((length, pw), b16), ((mbs, length, 3 * pw), b16), (rows_shape, b16), (rows_shape, b16),
        ((experts, d), f32), ((8, d), f32), ((2, cap, 128), f32),
        dense(sc), dense(ac), ((n, d), f32), dense(sc), dense(ac), ((n, d), f32),
        ((ny - 1, width, sc), b16), ((ny - 1, width, ac), b16), ((ny - 1, n, pw), f32),
        ((width, sc), f32), ((width, ac), f32), ((n, pw), f32), ((nx, n, pw), f32),
        ((2, mbs, sub, d), b16), ((2, 2, nx, mbs, sub, pw), b16),
        ((mbs, sub, d), b16), ((2, mbs, sub, d), b16),
        *((fwd[name].shape, fwd[name].dtype) for name in ("small", "place")),
        ((mbs, sub, d), b16),
        *((fwd[name].shape[1:], fwd[name].dtype) for name in (
            "mid", "n2", "rows", "q", "k", "v", "att", "rows2", "sgu", "shid", "shw")),
        (fwd["watt0"].shape, b16),
    )
    by_m = lambda c: flags((mbs, c))
    by_half = flags((2, mbs, experts, 2))
    names = ("tok", "small", "place", "y", "mid", "n2", "rows", "q", "k", "v", "att", "rows2", "sgu", "shid",
             "shw", "watt0", "watt1")
    outs = pl.pallas_call(
        functools.partial(
            backward_kernel, (nx, ny, mbs, sub, width, pw, heads, features, experts, cap, f, *BWD_SKEW)),
        out_shape=(
            jax.ShapeDtypeStruct((2, 2 * mbs, length, pw), b16),
            jax.ShapeDtypeStruct((experts, width, 2 * f), b16),
            jax.ShapeDtypeStruct((experts, width, f), b16),
            jax.ShapeDtypeStruct((width, ac), f32),
            jax.ShapeDtypeStruct((width, sc), f32),
            jax.ShapeDtypeStruct((n, pw), f32),
        ),
        in_specs=[hbm] * 17 + [vm] * 3 + [hbm] * 8,
        out_specs=(vm,) + (hbm,) * 5,
        scratch_shapes=[pltpu.VMEM(*v) for v in scratch] + [
            flags((2, experts)), by_m(ny), by_m(ny), by_m(nx), by_m(nx), by_m(nx), by_m(nx), by_m(nx), by_m(nx),
            by_m(nx), by_m(nx), by_m(ny), by_m(ny), by_m(nx), by_m(nx), by_m(nx), by_m(nx),
            by_half, by_half, by_half, by_half,
            flags((2, experts)), flags((2, experts)), flags((2, experts)), flags((2, experts)),
            flags((3,)), flags((3,)), flags((3, ny)), flags((3, ny)), flags((nx,)), flags((nx,)),
            flags((5,)), flags((2,)), flags((3,)), flags((20,)), flags((2, 2, ny)), flags((2, 2, nx)), pltpu.SemaphoreType.REGULAR((2,)),
        ],
        compiler_params=params(ids),
        cost_estimate=pl.CostEstimate(flops=2 * 10**10, bytes_accessed=10**8, transcendentals=10**6),
        name="backward",
    )(*(fwd[name] for name in names), cos, sin, rot, *(fwd[name] for name in ("slots", "gu", "hid", "gslots")), win, fwd["win"], wdt, fwd["wdt"])
    return outs[0], outs[1:]


BWD_SKEW = (2, 2)


def fast_device(block_input, output_grad, attention_gain, attention_in, attention_out, feed_gain,
                router_weight, expert_in, expert_down, shared_in, shared_down, routes):
    s = lax.axis_index("section")
    ny = lax.axis_size("gy")
    nx = lax.axis_size("gx")
    mbs = block_input.shape[0] // 2
    width = block_input.shape[2]
    features = width * ny
    experts = expert_in.shape[1]
    f = expert_in.shape[-1]
    pw = lanes_up(width + 2 * experts)
    tokens = routes.shape[2]
    cap = 5 * tokens // (2 * experts)
    length = tokens // ny
    heads = attention_in.shape[-1] // DH
    dims = (width, pw, experts, cap)

    att_block = jnp.concatenate([
        pad_to(attention_in[0], 2, pw).reshape(width, 3 * pw), pad_to(attention_out[0].T, 1, pw)], 1)
    sh_block = jnp.concatenate([shared_in[0].reshape(width, 2 * f), shared_down[0].T], 1)
    small = jnp.concatenate([
        router_weight[0].T.astype(jnp.float32), feed_gain, attention_gain, jnp.zeros((6, width), jnp.float32)], 0)
    tin = lax.dynamic_slice_in_dim(jnp.stack([block_input, output_grad]), s * mbs, mbs, 1)
    tin = pad_to(tin, 3, pw)
    small = pad_to(small, 1, pw)
    win = jnp.swapaxes(expert_in[0], 1, 2)
    wdt = expert_down[0].transpose(0, 2, 1)
    pairs = jnp.swapaxes(routes[0], 1, 2)
    half = DH // 2
    freq = 10000.0 ** (-np.arange(half, dtype=np.float64) / half)
    lanes = np.tile(np.arange(length)[:, None] * freq[None], (1, 2 * heads))
    cos = np.zeros((length, pw), np.float32)
    sin = np.zeros((length, pw), np.float32)
    cos[:, : heads * DH] = np.cos(lanes)
    sin[:, : heads * DH] = np.sin(lanes)
    rot = np.zeros((pw, pw), np.float32)
    for lead in range(0, heads * DH, DH):
        at = lead + np.arange(half)
        rot[at + half, at] = -1.0
        rot[at, at + half] = 1.0
    cos, sin, rot = jnp.asarray(cos), jnp.asarray(sin), jnp.asarray(rot, jnp.bfloat16)

    fwd = forward(tin, small, att_block, sh_block, pairs, cos, sin, rot, win, wdt, dims, heads, features, 0)
    both, grads = backward(fwd, cos, sin, rot, win, wdt, dims, heads, features, 1)
    win_g, wdt_g, att_g, sh_g, small_g = grads
    win_g, wdt_g, y, gx, ain, aout, sin_g, sdn, gain_g, fgain_g, rw = finish_outputs(
        win_g, wdt_g, both, att_g, sh_g, small_g, pw, heads * DH)
    return (
        jnp.swapaxes(y, 1, 2)[None],
        jnp.swapaxes(gx, 1, 2)[None],
        gain_g,
        jnp.swapaxes(ain, 0, 1)[None],
        aout[None],
        fgain_g,
        rw.T[None],
        win_g[None],
        jnp.swapaxes(wdt_g, 1, 2)[None],
        sin_g[None],
        sdn.T[None],
    )


def solution(mesh):
    in_specs = (
        P(None, "gx", "gy"),
        P(None, "gx", "gy"),
        P("section", "gy"),
        P("section", "gy", None, "gx"),
        P("section", "gx", "gy"),
        P("section", "gy"),
        P("section", "gy", None),
        P("section", None, "gy", None, "gx"),
        P("section", None, "gx", "gy"),
        P("section", "gy", None, "gx"),
        P("section", "gx", "gy"),
        P("section", None, None, None),
    )
    out_specs = (
        P("section", None, "gx", "gy"),
        P("section", None, "gx", "gy"),
        P("section", "gy"),
        P("section", "gy", None, "gx"),
        P("section", "gx", "gy"),
        P("section", "gy"),
        P("section", "gy", None),
        P("section", None, "gy", None, "gx"),
        P("section", None, "gx", "gy"),
        P("section", "gy", None, "gx"),
        P("section", "gx", "gy"),
    )
    fast = mesh.shape["gx"] == mesh.shape["gy"]
    return jax.shard_map(
        fast_device if fast else on_device, mesh=mesh, in_specs=in_specs, out_specs=out_specs, check_vma=False
    )
```

```python
import functools

import jax
import jax.numpy as jnp
import numpy as np
from jax import lax
from jax.experimental import pallas as pl
from jax.experimental.pallas import tpu as pltpu
from jax.sharding import PartitionSpec as P

DH = 64


epsilon = 1e-06
highest = lax.Precision.HIGHEST


def from_partner(array, axis, apart):
    return lax.ppermute(array, axis, [(i, i ^ 1 << apart) for i in range(lax.axis_size(axis))])


def token_rows(values):
    return lax.all_gather(values, "gx", axis=0, tiled=True)


def output_rows(values):
    return lax.psum_scatter(values, "gx", scatter_dimension=0, tiled=True)


def width_sum(values):
    return lax.psum(values, "gy")


def pass_section(values):
    return from_partner(values, "section", 0)


def sequence_sums(values):
    return lax.psum_scatter(values, "gy", scatter_dimension=0, tiled=True)


def sequence_rows(values):
    return lax.all_gather(values, "gy", axis=0, tiled=True)


def gather_hidden(hidden, shared_hidden):
    return (
        lax.all_gather(hidden, "gy", axis=0, tiled=True),
        lax.all_gather(shared_hidden, "gy", axis=0, tiled=True),
    )


def rope_turn(values, positions, turn_sign):
    half_size = values.shape[-1] // 2
    frequency = 10000.0 ** (-jnp.arange(half_size, dtype=jnp.float32) / half_size)
    angles = positions[:, None] * frequency[None, :]
    cosine = jnp.cos(angles)[:, None, :]
    sine_part = turn_sign * jnp.sin(angles)[:, None, :]
    first_half = values[..., :half_size]
    second_half = values[..., half_size:]
    return jnp.concatenate(
        [
            first_half * cosine - second_half * sine_part,
            first_half * sine_part + second_half * cosine,
        ],
        axis=-1,
    )


def norm_forward(stream, gain):
    full_width = stream.shape[1] * lax.axis_size("gy")
    square_sum = width_sum(jnp.sum(stream * stream, axis=1))
    inverse_rms = lax.rsqrt(square_sum / full_width + epsilon)
    return ((stream * inverse_rms[:, None] * gain[None, :]).astype(jnp.bfloat16), inverse_rms)


def norm_backward(stream, inverse_rms, gain, grad_normed):
    full_width = stream.shape[1] * lax.axis_size("gy")
    scaled = grad_normed * gain[None, :]
    inner_sum = width_sum(jnp.sum(scaled * stream, axis=1))
    cubed = inverse_rms * inverse_rms * inverse_rms
    grad_stream = inverse_rms[:, None] * scaled - stream * (cubed * inner_sum / full_width)[:, None]
    grad_gain = jnp.sum(grad_normed * stream * inverse_rms[:, None], axis=0)
    return (grad_stream, grad_gain)


def slot_table(route_ids, experts, capacity):
    flat_ids = route_ids.reshape(-1)
    assigned = (flat_ids[:, None] == jnp.arange(experts, dtype=jnp.int32)[None, :]).astype(
        jnp.int32
    )
    earlier = jnp.cumsum(assigned, axis=0) - assigned
    places = flat_ids * capacity + jnp.sum(earlier * assigned, axis=1)
    owners = jnp.arange(flat_ids.shape[0], dtype=jnp.int32) // 2
    slot_token = jnp.zeros((experts * capacity,), jnp.int32).at[places].set(owners)
    slot_valid = jnp.zeros((experts * capacity,), jnp.int32).at[places].set(jnp.ones_like(owners))
    return (places.reshape(-1, 2), slot_token, slot_valid)


def expert_act(gate_up, logits):
    half_size = gate_up.shape[1] // 2
    return (
        jax.nn.silu(gate_up[:, :half_size])
        * gate_up[:, half_size:]
        * jax.nn.sigmoid(logits)[:, None]
    )


def shared_act(gate_up):
    half_size = gate_up.shape[1] // 2
    return jax.nn.silu(gate_up[:, :half_size]) * gate_up[:, half_size:]


def causal_scores(queries, keys_part):
    score_scale = queries.shape[-1] ** (-0.5)
    scores = (
        jnp.einsum("qhd,khd->hqk", queries, keys_part, preferred_element_type=jnp.float32)
        * score_scale
    )
    length = queries.shape[0]
    causal = jnp.arange(length)[:, None] >= jnp.arange(length)[None, :]
    return jnp.where(causal[None], scores, -1e30)


def attend_forward(queries, keys_part, values_part):
    scores = causal_scores(queries, keys_part)
    row_max = jnp.max(scores, axis=-1, keepdims=True)
    exponent = jnp.exp(scores - row_max)
    row_total = jnp.sum(exponent, axis=-1, keepdims=True)
    probabilities = (exponent / row_total).astype(jnp.bfloat16)
    attended = jnp.einsum(
        "hqk,khd->qhd", probabilities, values_part, preferred_element_type=jnp.float32
    )
    return (attended, row_max + jnp.log(row_total))


def attend_backward(queries, keys_part, values_part, log_total, grad_attended):
    score_scale = queries.shape[-1] ** (-0.5)
    probabilities = jnp.exp(causal_scores(queries, keys_part) - log_total)
    grad_values = jnp.einsum(
        "hqk,qhd->khd",
        probabilities.astype(jnp.bfloat16),
        grad_attended,
        preferred_element_type=jnp.float32,
    )
    grad_probs = jnp.einsum(
        "qhd,khd->hqk", grad_attended, values_part, preferred_element_type=jnp.float32
    )
    grad_scores = (
        probabilities * (grad_probs - jnp.sum(grad_probs * probabilities, axis=-1, keepdims=True))
    ).astype(jnp.bfloat16)
    grad_queries = (
        jnp.einsum("hqk,khd->qhd", grad_scores, keys_part, preferred_element_type=jnp.float32)
        * score_scale
    )
    grad_keys = (
        jnp.einsum("hqk,qhd->khd", grad_scores, queries, preferred_element_type=jnp.float32)
        * score_scale
    )
    return (grad_queries, grad_keys, grad_values)


def layer_forward(stream, weights, route_ids):
    (
        attention_gain,
        attention_in,
        attention_out,
        feed_gain,
        router_weight,
        expert_in,
        expert_down,
        shared_in,
        shared_down,
    ) = weights
    local_width = stream.shape[1]
    experts = expert_in.shape[0]
    normed, inverse_first = norm_forward(stream, attention_gain)
    rows_first = token_rows(normed)
    tokens = rows_first.shape[0]
    capacity = 5 * tokens // (2 * experts)
    slot_count = experts * capacity
    projected = sequence_sums(
        jnp.dot(
            rows_first, attention_in.reshape(local_width, -1), preferred_element_type=jnp.float32
        )
    )
    length = projected.shape[0]
    projected = projected.reshape(length, 3, -1, DH)
    positions = jnp.arange(length, dtype=jnp.float32)
    queries = rope_turn(projected[:, 0], positions, 1.0).astype(jnp.bfloat16)
    keys_part = rope_turn(projected[:, 1], positions, 1.0).astype(jnp.bfloat16)
    values_part = projected[:, 2].astype(jnp.bfloat16)
    attended, log_total = attend_forward(queries, keys_part, values_part)
    attended_rows = sequence_rows(attended.astype(jnp.bfloat16).reshape(length, -1))
    middle = stream + output_rows(
        jnp.dot(attended_rows, attention_out, preferred_element_type=jnp.float32)
    )
    normed_feed, inverse_second = norm_forward(middle, feed_gain)
    rows_second = token_rows(normed_feed)
    route_slot, slot_token, slot_valid = slot_table(route_ids, experts, capacity)
    grouped = (rows_second[slot_token] * slot_valid[:, None].astype(jnp.bfloat16)).reshape(
        experts, capacity, local_width
    )
    expert_part = jnp.einsum(
        "ecd,edf->ecf",
        grouped,
        expert_in.reshape(experts, local_width, -1),
        preferred_element_type=jnp.float32,
    )
    router_part = jnp.einsum(
        "ecd,de->ec", grouped, router_weight, preferred_element_type=jnp.float32
    )
    shared_part = jnp.dot(
        rows_second, shared_in.reshape(local_width, -1), preferred_element_type=jnp.float32
    )
    expert_gu, router_logit, shared_gu = (
        lax.psum_scatter(
            expert_part.reshape(slot_count, -1), "gy", scatter_dimension=0, tiled=True
        ),
        lax.psum_scatter(router_part.reshape(slot_count), "gy", scatter_dimension=0, tiled=True),
        lax.psum_scatter(shared_part, "gy", scatter_dimension=0, tiled=True),
    )
    hidden_rows, shared_rows = gather_hidden(
        expert_act(expert_gu, router_logit).astype(jnp.bfloat16),
        shared_act(shared_gu).astype(jnp.bfloat16),
    )
    expert_result = jnp.einsum(
        "ecf,efd->ecd",
        hidden_rows.reshape(experts, capacity, -1),
        expert_down,
        preferred_element_type=jnp.float32,
    ).reshape(slot_count, local_width)
    branch = (
        expert_result[route_slot[:, 0]]
        + expert_result[route_slot[:, 1]]
        + jnp.dot(shared_rows, shared_down, preferred_element_type=jnp.float32)
    )
    result = middle + output_rows(branch)
    kept_items = (
        stream,
        inverse_first,
        rows_first,
        queries,
        keys_part,
        values_part,
        log_total,
        attended_rows,
        middle,
        inverse_second,
        rows_second,
        expert_gu,
        router_logit,
        shared_gu,
    )
    return (result, kept_items)


def layer_backward(grad_out, kept_items, weights, route_ids):
    (
        attention_gain,
        attention_in,
        attention_out,
        feed_gain,
        router_weight,
        expert_in,
        expert_down,
        shared_in,
        shared_down,
    ) = weights
    (
        stream,
        inverse_first,
        rows_first,
        queries,
        keys_part,
        values_part,
        log_total,
        attended_rows,
        middle,
        inverse_second,
        rows_second,
        expert_gu,
        router_logit,
        shared_gu,
    ) = kept_items[:14]
    local_width = stream.shape[1]
    experts = expert_in.shape[0]
    tokens = rows_second.shape[0]
    capacity = 5 * tokens // (2 * experts)
    slot_count = experts * capacity
    hidden_rows, shared_rows = gather_hidden(
        expert_act(expert_gu, router_logit).astype(jnp.bfloat16),
        shared_act(shared_gu).astype(jnp.bfloat16),
    )
    route_slot, slot_token, slot_valid = slot_table(route_ids, experts, capacity)
    valid_rows = slot_valid[:, None].astype(jnp.bfloat16)
    grouped = (rows_second[slot_token] * valid_rows).reshape(experts, capacity, local_width)
    grad_rows = token_rows(grad_out.astype(jnp.bfloat16))
    slot_grad = (grad_rows[slot_token] * valid_rows).reshape(experts, capacity, local_width)
    down_grad = jnp.einsum(
        "ecf,ecd->efd",
        hidden_rows.reshape(experts, capacity, -1),
        slot_grad,
        preferred_element_type=jnp.float32,
    )
    shared_down_grad = jnp.einsum(
        "tf,td->fd", shared_rows, grad_rows, preferred_element_type=jnp.float32
    )
    hidden_part = jnp.einsum(
        "ecd,efd->ecf", slot_grad, expert_down, preferred_element_type=jnp.float32
    ).reshape(slot_count, -1)
    shared_part = jnp.einsum(
        "td,fd->tf", grad_rows, shared_down, preferred_element_type=jnp.float32
    )
    grad_hidden, grad_shared = (
        lax.psum_scatter(
            hidden_part.astype(jnp.bfloat16), "gy", scatter_dimension=0, tiled=True
        ).astype(jnp.float32),
        lax.psum_scatter(
            shared_part.astype(jnp.bfloat16), "gy", scatter_dimension=0, tiled=True
        ).astype(jnp.float32),
    )
    unused_expert, expert_back = jax.vjp(expert_act, expert_gu, router_logit)
    grad_gu, grad_logit = expert_back(grad_hidden)
    unused_shared, shared_back = jax.vjp(shared_act, shared_gu)
    (grad_shared_gu,) = shared_back(grad_shared)
    gu_rows, shared_gu_rows = (
        lax.all_gather(grad_gu.astype(jnp.bfloat16), "gy", axis=0, tiled=True),
        lax.all_gather(grad_shared_gu.astype(jnp.bfloat16), "gy", axis=0, tiled=True),
    )
    logit_rows = lax.all_gather(grad_logit, "gy", axis=0, tiled=True).reshape(experts, capacity)
    gu_grouped = gu_rows.reshape(experts, capacity, -1)
    in_grad = jnp.einsum("ecd,ecf->edf", grouped, gu_grouped, preferred_element_type=jnp.float32)
    router_grad = jnp.einsum(
        "ecd,ec->de", grouped.astype(jnp.float32), logit_rows, precision=highest
    )
    shared_in_grad = jnp.einsum(
        "td,tf->df", rows_second, shared_gu_rows, preferred_element_type=jnp.float32
    )
    slot_back = jnp.einsum(
        "ecf,edf->ecd",
        gu_grouped,
        expert_in.reshape(experts, local_width, -1),
        preferred_element_type=jnp.float32,
    )
    slot_back = slot_back + logit_rows[:, :, None] * router_weight.T.astype(jnp.float32)[:, None, :]
    slot_back = slot_back.reshape(slot_count, local_width)
    rows_back = (
        slot_back[route_slot[:, 0]]
        + slot_back[route_slot[:, 1]]
        + jnp.einsum(
            "tf,df->td",
            shared_gu_rows,
            shared_in.reshape(local_width, -1),
            preferred_element_type=jnp.float32,
        )
    )
    grad_middle_norm, feed_gain_grad = norm_backward(
        middle, inverse_second, feed_gain, output_rows(rows_back)
    )
    grad_middle = grad_out + grad_middle_norm
    middle_rows = token_rows(grad_middle.astype(jnp.bfloat16))
    out_weight_grad = jnp.einsum(
        "tf,td->fd", attended_rows, middle_rows, preferred_element_type=jnp.float32
    )
    grad_attended = sequence_sums(
        jnp.einsum("td,fd->tf", middle_rows, attention_out, preferred_element_type=jnp.float32)
    )
    length = grad_attended.shape[0]
    positions = jnp.arange(length, dtype=jnp.float32)
    grad_queries, grad_keys, grad_values = attend_backward(
        queries,
        keys_part,
        values_part,
        log_total,
        grad_attended.astype(jnp.bfloat16).reshape(queries.shape),
    )
    grad_projected = jnp.stack(
        [
            rope_turn(grad_queries, positions, -1.0),
            rope_turn(grad_keys, positions, -1.0),
            grad_values,
        ],
        axis=1,
    )
    grad_projected = grad_projected.astype(jnp.bfloat16).reshape(length, -1)
    projected_rows = sequence_rows(grad_projected)
    in_weight_grad = jnp.einsum(
        "td,tf->df", rows_first, projected_rows, preferred_element_type=jnp.float32
    )
    grad_normed = output_rows(
        jnp.einsum(
            "tf,df->td",
            projected_rows,
            attention_in.reshape(local_width, -1),
            preferred_element_type=jnp.float32,
        )
    )
    grad_stream_norm, attention_gain_grad = norm_backward(
        stream, inverse_first, attention_gain, grad_normed
    )
    layer_grads = (
        attention_gain_grad,
        in_weight_grad.reshape(attention_in.shape),
        out_weight_grad,
        feed_gain_grad,
        router_grad,
        in_grad.reshape(expert_in.shape),
        down_grad,
        shared_in_grad.reshape(shared_in.shape),
        shared_down_grad,
    )
    return (grad_middle + grad_stream_norm, layer_grads)


def put_item(buffer, value, batch_index, is_valid):
    current = lax.dynamic_index_in_dim(buffer, batch_index, 0, keepdims=False)
    return lax.dynamic_update_index_in_dim(
        buffer, jnp.where(is_valid, value, current), batch_index, 0
    )


def on_device(
    block_input,
    output_grad,
    attention_gain,
    attention_in,
    attention_out,
    feed_gain,
    router_weight,
    expert_in,
    expert_down,
    shared_in,
    shared_down,
    routes,
):
    section_index = lax.axis_index("section")
    batches = block_input.shape[0]
    weights = tuple(
        (
            member[0]
            for member in (
                attention_gain,
                attention_in,
                attention_out,
                feed_gain,
                router_weight,
                expert_in,
                expert_down,
                shared_in,
                shared_down,
            )
        )
    )
    route_table = routes[0]
    outputs = jnp.zeros(block_input.shape, jnp.bfloat16)
    received = jnp.zeros(block_input.shape[1:], jnp.bfloat16)
    stored = None
    for tick_step in range(batches + 1):
        micro_index = tick_step - section_index
        is_valid = (micro_index >= 0) & (micro_index < batches)
        batch_index = jnp.clip(micro_index, 0, batches - 1)
        fresh_input = lax.dynamic_index_in_dim(block_input, batch_index, 0, keepdims=False)
        incoming = jnp.where(section_index == 0, fresh_input, received).astype(jnp.float32)
        route_ids = lax.dynamic_index_in_dim(route_table, batch_index, 0, keepdims=False)
        result, kept_items = layer_forward(incoming, weights, route_ids)
        result_low = result.astype(jnp.bfloat16)
        outputs = put_item(outputs, result_low, batch_index, is_valid)
        if stored is None:
            stored = tuple(
                (jnp.zeros((batches,) + member.shape, member.dtype) for member in kept_items)
            )
        stored = tuple(
            (
                put_item(buffer, member, batch_index, is_valid)
                for buffer, member in zip(stored, kept_items)
            )
        )
        if tick_step < batches:
            received = pass_section(result_low)
    grads_in = jnp.zeros(block_input.shape, jnp.bfloat16)
    received = jnp.zeros(block_input.shape[1:], jnp.bfloat16)
    totals = tuple((jnp.zeros(member.shape, jnp.float32) for member in weights))
    for tick_step in range(batches + 1):
        micro_index = batches - tick_step - section_index
        is_valid = (micro_index >= 0) & (micro_index < batches)
        batch_index = jnp.clip(micro_index, 0, batches - 1)
        given_grad = lax.dynamic_index_in_dim(output_grad, batch_index, 0, keepdims=False)
        incoming = jnp.where(section_index == 1, given_grad, received).astype(jnp.float32)
        kept_items = tuple(
            (lax.dynamic_index_in_dim(buffer, batch_index, 0, keepdims=False) for buffer in stored)
        )
        route_ids = lax.dynamic_index_in_dim(route_table, batch_index, 0, keepdims=False)
        grad_input, layer_grads = layer_backward(incoming, kept_items, weights, route_ids)
        grad_low = grad_input.astype(jnp.bfloat16)
        grads_in = put_item(grads_in, grad_low, batch_index, is_valid)
        totals = tuple(
            (total + jnp.where(is_valid, member, 0.0) for total, member in zip(totals, layer_grads))
        )
        if tick_step < batches:
            received = pass_section(grad_low)
    gain_first, gain_second, router_total = lax.psum((totals[0], totals[3], totals[4]), "gx")
    return (
        outputs[None],
        grads_in[None],
        gain_first[None],
        totals[1][None],
        totals[2][None],
        gain_second[None],
        router_total[None],
        totals[5][None],
        totals[6][None],
        totals[7][None],
        totals[8][None],
    )


def lanes_up(n):
    return -(-n // 128) * 128


def rot_columns(w):
    shape = w.shape
    w = w.reshape(shape[:-1] + (-1, 2, DH // 2))
    w = jnp.stack([-w[..., 1, :], w[..., 0, :]], axis=-2)
    return w.reshape(shape)


def pad_to(v, axis, n):
    pads = [(0, 0)] * v.ndim
    pads[axis] = (0, n - v.shape[axis])
    return jnp.pad(v, pads)


def mm(a, b, dims=((1,), (0,))):
    return lax.dot_general(a, b, (dims, ((), ())), preferred_element_type=jnp.float32)


def bf(v):
    return v.astype(jnp.bfloat16)


def head_mask(pw, h):
    lane = lax.broadcasted_iota(jnp.int32, (1, pw), 1)
    return (lane >= h * DH) & (lane < (h + 1) * DH)


def rms(x, features):
    return lax.rsqrt(jnp.sum(x * x, axis=1, keepdims=True) / features + epsilon)


def norm_back(x, inv, gain, d, features):
    u = d * gain
    inner = jnp.sum(u * x, axis=1, keepdims=True) / features
    dx = inv * u - x * (inv * inv * inv * inner)
    return dx, jnp.sum(d * x * inv, axis=0, keepdims=True)


def probs_of(q, k):
    s = mm(q, k, ((1,), (1,))) * DH ** -0.5
    n = s.shape[0]
    causal = lax.broadcasted_iota(jnp.int32, (n, n), 0) >= lax.broadcasted_iota(jnp.int32, (n, n), 1)
    s = jnp.where(causal, s, -1e30)
    e = jnp.exp(s - jnp.max(s, axis=1, keepdims=True))
    return e / jnp.sum(e, axis=1, keepdims=True)


def act_back(gate, up, dh, s):
    sg = jax.nn.sigmoid(gate)
    silu = gate * sg
    if s is None:
        return dh * up * (sg * (1.0 + gate * (1.0 - sg))), dh * silu, None
    dr = jnp.sum(dh * silu * up, axis=-1, keepdims=True) * s * (1.0 - s)
    ds = dh * s
    return ds * up * (sg * (1.0 + gate * (1.0 - sg))), ds * silu, dr


MESH = pl.DeviceIdType.MESH
VMEM_BYTES = 62 * 2**20


def remote(src, dst, send, recv, target):
    return pltpu.make_async_remote_copy(
        src_ref=src, dst_ref=dst, send_sem=send, recv_sem=recv, device_id=target, device_id_type=MESH
    )


def router_column(rows, e, width, experts):
    lane = lax.broadcasted_iota(jnp.int32, rows.shape, rows.ndim - 1)
    mask = (lane == width + e) | (lane == width + experts + e)
    return jnp.sum(jnp.where(mask, rows.astype(jnp.float32), 0.0), axis=-1, keepdims=True)


class Position:
    def __init__(self, nx, ny):
        self.s = lax.axis_index("section")
        self.a = lax.axis_index("gx")
        self.b = lax.axis_index("gy")
        self.nx, self.ny = nx, ny
        self.n = nx * ny
        self.me = self.a * ny + self.b

    def device(self, index):
        return (self.s, index // self.ny, lax.rem(index, self.ny))

    def others(self, do):
        def step(i, c):
            index = lax.rem(self.me + i, self.n)
            do(index, index // self.ny, lax.rem(index, self.ny))
            return c

        lax.fori_loop(1, self.n, step, 0)

    def peers(self, do):
        for i in range(1, self.nx):
            do(lax.rem(self.a + i, self.nx))

    def line(self, do):
        for i in range(1, self.ny):
            do(lax.rem(self.b + i, self.ny))


def greet_section(pos):
    barrier = pltpu.get_barrier_semaphore()

    def one(index, ai, bi):
        pl.semaphore_signal(barrier, inc=1, device_id=(pos.s, ai, bi), device_id_type=MESH)

    pos.others(one)
    return barrier


def flags(count):
    return pltpu.SemaphoreType.DMA(count)


class Share:
    def __init__(self, pos, layer, block, full, sems, cols=None):
        if cols is None:
            cols = pl.ds(0, block.shape[1])
        self.pos, self.layer, self.cols = pos, layer, cols
        self.block, self.full = block.at[:, cols], full.at[:, :, cols]
        self.sems = sems
        self.source = pos.s == layer

    def along(self, way, h):
        pos = self.pos
        j = pos.b - way * h
        to = pos.b + way
        real = (j >= 0) & (j < pos.ny) & (to >= 0) & (to < pos.ny)
        j = jnp.clip(j, 0, pos.ny - 1)
        src = self.block if h == 0 else self.full.at[j]
        copy = remote(src, self.full.at[j], self.sems[0].at[(way + 1) // 2, h], self.sems[1].at[j], (pos.s, pos.a, to))
        return real, j, copy

    def across(self, src, slot):
        pos = self.pos
        return remote(src, self.full.at[slot], self.sems[2].at[slot], self.sems[3].at[slot], (1 - pos.s, pos.a, pos.b))

    def start(self):
        b = self.pos.b

        @pl.when(self.source)
        def _():
            self.full[b] = self.block[...]
            for way in (-1, 1):
                real, _, copy = self.along(way, 0)
                pl.when(real)(copy.start)
            self.across(self.block, b).start()

    def hop(self, h):
        pos = self.pos

        @pl.when(self.source)
        def _():
            for way in (-1, 1):
                j = pos.b - way * h

                @pl.when((j >= 0) & (j < pos.ny))
                def _():
                    real, jc, copy = self.along(way, h)
                    copy.wait_recv()
                    pl.when(real)(copy.start)
                    self.across(self.full.at[jc], jc).start()

    def finish(self):
        pos = self.pos

        @pl.when(self.source)
        def _():
            for h in range(pos.ny - 1):
                for way in (-1, 1):
                    real, _, copy = self.along(way, h)
                    pl.when(real)(copy.wait_send)
            for j in range(pos.ny):
                self.across(self.block, j).wait_send()

        @pl.when(jnp.logical_not(self.source))
        def _():
            for j in range(pos.ny):
                self.across(self.full.at[j], j).wait_recv()


def share_sems(ny):
    return [flags((2, ny)), flags((ny,)), flags((ny,)), flags((ny,))]


def params(ids):
    return pltpu.CompilerParams(collective_id=ids, has_side_effects=True, vmem_limit_bytes=VMEM_BYTES)


def turn(t, cos, sin, rot, sign):
    hi = bf(t)
    lo = bf(t - hi.astype(jnp.float32))
    return bf(t * cos + sign * ((mm(hi, rot) + mm(lo, rot)) * sin))


def by_blocks(rows, full, cols, width, pw):
    total = None
    for j in range(full.shape[0]):
        part = mm(rows[:, j * pw : j * pw + width], full[j, :, cols])
        total = part if total is None else total + part
    return total


def finish_kernel(cfg, win, wdt, both, att, sh, small, win_o, wdt_o, y_o, gx_o, ain_o, aout_o, sin_o, sdn_o, gain_o, fgain_o, rw_o):
    width, pw, hd, experts = cfg
    f = wdt.shape[-1]
    value = win[0].astype(jnp.float32)
    win_o[0, :, 0, :] = value[:, :f]
    win_o[0, :, 1, :] = value[:, f:]
    wdt_o[0] = wdt[0].astype(jnp.float32)

    @pl.when(pl.program_id(0) == 0)
    def _():
        for kind, dst in enumerate((y_o, gx_o)):
            for m in range(both.shape[1]):
                dst[m] = both[kind, m].astype(jnp.float32).T[:width].astype(dst.dtype)
        lane = lax.broadcasted_iota(jnp.int32, (width, 128), 1)
        parts = []
        for c in range(4):
            pair = att[:, (4 + c // 2) * 128 : (5 + c // 2) * 128]
            pair = pltpu.roll(pair, 64, 1) if c % 2 else pair
            parts.append((att[:, c * 128 : (c + 1) * 128], jnp.where(lane < 64, pair, 0.0)))
        for c in range(3):
            ain_o[c, :, :128] = parts[c][0]
            ain_o[c, :, 128:] = parts[c][1][:, : hd - 128]
        square = jnp.concatenate([jnp.concatenate(parts[3], 1), jnp.zeros((pw - width, pw), jnp.float32)], 0)
        aout_o[...] = square.T[:hd, :width]
        value = sh[:, : 2 * f]
        sin_o[:, 0, :] = value[:, :f]
        sin_o[:, 1, :] = value[:, f:]
        sdn_o[...] = sh[:, 2 * f :]
        rw_o[...] = small[:experts, :width]
        fgain_o[...] = small[experts : experts + 1, :width]
        gain_o[...] = small[experts + 1 : experts + 2, :width]


def finish_outputs(win, wdt, both, att, sh, small, pw, hd):
    experts, width, f = wdt.shape
    mbs, tokens = both.shape[1:3]
    f32 = jnp.float32
    each = lambda *shape: pl.BlockSpec((1,) + shape, lambda e: (e,) + (0,) * len(shape))
    once = lambda *shape: pl.BlockSpec(shape, lambda e: (0,) * len(shape))
    shapes = (
        ((mbs, width, tokens), both.dtype), ((mbs, width, tokens), both.dtype),
        ((3, width, hd), f32), ((hd, width), f32), ((width, 2, f), f32), ((width, f), f32),
        ((1, width), f32), ((1, width), f32), ((experts, width), f32),
    )
    return pl.pallas_call(
        functools.partial(finish_kernel, (width, pw, hd, experts)),
        grid=(experts,),
        out_shape=(
            jax.ShapeDtypeStruct((experts, width, 2, f), f32),
            jax.ShapeDtypeStruct((experts, width, f), f32),
            *(jax.ShapeDtypeStruct(*v) for v in shapes),
        ),
        in_specs=[each(width, 2 * f), each(width, f)] + [once(*v.shape) for v in (both, att, sh, small)],
        out_specs=(each(width, 2, f), each(width, f), *(once(*v[0]) for v in shapes)),
        compiler_params=pltpu.CompilerParams(vmem_limit_bytes=VMEM_BYTES),
        name="finish",
    )(win, wdt, both, att, sh, small)


def forward_kernel(cfg, *refs):
    nx, ny, mbs, sub, width, pw, heads, features, experts, cap, f, sk, ak = cfg
    (tin, small_b, att_b, sh_b, routes, cos, sin, rot, win_a, wdt_a,
     win_b, wdt_b, tok_o, small_o, place_o, place_to, watt0_o, y_o, mid_o, n2_o, rows_o, q_o, k_o, v_o, att_o, slots_o, gu_o, hid_o, rows2_o, sgu_o, shid_o, shw_o, watt_o, gslots_o,
     y, mid, n2, rx, nsend, nall, proj, q, k, v, att, osend, orecv, rwx,
     xsend, xline, xall, nrows, pm, pt, slots, acc, gu, hid, eo, sgu, shid, ssend, srecv, rsend, rpeer, rline, rrecv,
     win, wdt, shw0, shw1, watt0, watt1, tbuf, tok, rts, place, place_t, sm0, sm1, small, gall, gslots,
     n_send, n_recv, o_send, o_recv, x_send, x_recv, u_send, u_recv, t_send, t_recv, s_send, s_recv, g_send, g_recv, r_send, r_recv,
     rs_send, rs_recv, ag_send, ag_recv, wi_sem, wd_sem, g_sem, k_sem, i_send, i_recv, q_send, q_recv, v_send, v_recv, gu_send, gu_recv, *w_sems) = refs
    pos = Position(nx, ny)
    s, a, b, me = pos.s, pos.a, pos.b, pos.me
    slots_n = experts * cap
    tokens = nx * ny * sub
    d = ny * pw
    length = nx * sub
    half, hw = experts // 2, f // 2
    lane = lax.broadcasted_iota(jnp.int32, (1, pw), 1)
    shares = (
        Share(pos, 0, sh_b, shw0, w_sems[0:4]),
        Share(pos, 1, att_b, watt1, w_sems[4:8]),
        Share(pos, 1, sh_b, shw1, w_sems[8:12]),
    )
    entry_shares = (
        Share(pos, 0, small_b, sm0, w_sems[12:16]),
        Share(pos, 1, small_b, sm1, w_sems[16:20]),
        Share(pos, 0, att_b, watt0, w_sems[20:24], pl.ds(0, 2 * pw)),
        Share(pos, 0, att_b, watt0, w_sems[24:28], pl.ds(2 * pw, 2 * pw)),
    )
    watts, shws = (watt0, watt1), (shw0, shw1)
    barrier = pltpu.get_barrier_semaphore()
    pos.peers(lambda ai: pl.semaphore_signal(barrier, inc=1, device_id=(s, ai, b), device_id_type=MESH))
    pos.line(lambda bi: pl.semaphore_signal(barrier, inc=1, device_id=(s, a, bi), device_id_type=MESH))
    pl.semaphore_signal(barrier, inc=1, device_id=(1 - s, a, b), device_id_type=MESH)
    for j in range(ny):
        @pl.when((a != b) | (b != j))
        def _():
            pl.semaphore_signal(barrier, inc=1, device_id=(s, b, j), device_id_type=MESH)

    def weight_copy(layer, e, which):
        own, oth, dst, sem = ((win_a, win_b, win, wi_sem), (wdt_a, wdt_b, wdt, wd_sem))[which]
        return own.at[e], oth.at[e], dst.at[e], sem.at[e]

    def start_weight(layer, e, which):
        own, oth, dst, sem = weight_copy(layer, e, which)

        @pl.when(s == layer)
        def _():
            pltpu.make_async_copy(own, dst, sem).start()

        @pl.when(s != layer)
        def _():
            pltpu.make_async_copy(oth, dst, sem).start()

    def wait_weight(layer, e, which):
        own, oth, dst, sem = weight_copy(layer, e, which)
        pltpu.make_async_copy(own, dst, sem).wait()

    def first_weights(e, c):
        start_weight(0, e, 0)
        start_weight(0, e, 1)
        return c

    def swap(c):
        src, dst = ((win_a, win_b), (wdt_a, wdt_b))[c]
        return remote(src, dst, v_send.at[c], v_recv.at[c], (1 - s, a, b))

    def weights_ready():
        for c in range(2):
            swap(c).wait()
        lax.fori_loop(0, experts, first_weights, 0)

    @pl.when(a == b)
    def _():
        pl.semaphore_wait(barrier, nx - 1 + ny - 1 + 1 + nx - 1)

    @pl.when(a != b)
    def _():
        pl.semaphore_wait(barrier, nx - 1 + ny - 1 + 1 + nx)

    def tokens_copy(i, slot, seq):
        src = tin.at[:, :, pl.ds(pl.multiple_of(i * sub, sub), sub), :]
        return remote(src, tbuf.at[slot], i_send.at[i], i_recv.at[slot], (s, i, seq))

    def token_targets(do):
        for c in range(nx):
            i = lax.rem(a + c, nx)

            @pl.when((i != a) | (a != b))
            def _():
                do(tokens_copy(i, b, a))

    def routes_copy(src, slot):
        return remote(routes.at[pl.ds(src * mbs, mbs)], rts.at[slot], q_send, q_recv, (1 - s, a, b))

    token_targets(lambda copy: copy.start())
    routes_copy(1 - s, s).start()
    for share in entry_shares:
        share.start()
    for c in range(2):
        swap(c).start()
    rts[s] = routes[pl.ds(s * mbs, mbs)]

    @pl.when(a == b)
    def _():
        tbuf[b] = tin[:, :, pl.ds(pl.multiple_of(a * sub, sub), sub), :]

    routes_copy(0, 1 - s).wait()

    def places():
        t0 = lax.broadcasted_iota(jnp.int32, (tokens, tokens), 0)
        t1 = lax.broadcasted_iota(jnp.int32, (tokens, tokens), 1)
        before = bf((t1 < t0).astype(jnp.float32))
        after = bf((t0 < t1).astype(jnp.float32))
        er = lax.broadcasted_iota(jnp.int32, (experts, tokens), 0).astype(jnp.float32)
        ec = lax.broadcasted_iota(jnp.int32, (tokens, 128), 1).astype(jnp.float32)
        sub8 = lax.broadcasted_iota(jnp.int32, (128, tokens), 0)
        for l in range(2):
            for m in range(mbs):
                r = rts[l, m].astype(jnp.float32)
                rows = [r[c : c + 1] for c in range(2)]
                hot = [(row == er).astype(jnp.float32) for row in rows]
                count = mm(bf(hot[0] + hot[1]), after)
                cols = jnp.where(sub8 == 0, rows[0], jnp.where(sub8 == 1, rows[1], 0.0)).T
                cols = [cols[:, c : c + 1] for c in range(2)]
                hot_t = [(col == ec).astype(jnp.float32) for col in cols]
                count_t = mm(before, bf(hot_t[0] + hot_t[1]))
                for c in range(2):
                    rank = jnp.sum(hot[c] * count, axis=0, keepdims=True)
                    place[l, m, c : c + 1] = (rows[c] * cap + rank).astype(jnp.int32)
                    rank_t = jnp.sum(hot_t[c] * count_t, axis=1, keepdims=True)
                    place_t[l, m, :, c : c + 1] = (cols[c] * cap + rank_t).astype(jnp.int32)

    def tokens_ready():
        for j in range(ny):
            @pl.when((a != b) | (b != j))
            def _():
                tokens_copy(a, j, j).wait_recv()

            for kind in range(2):
                tok[kind, :, :, j * pw : (j + 1) * pw] = tbuf[j, kind]
        token_targets(lambda copy: copy.wait_send())

    def stream(l, m):
        return (tok[0, m] if l == 0 else y[0, m]).astype(jnp.float32)

    def copy_n(l, m, ai, slot):
        return remote(nsend.at[l, m], nall.at[l, m, slot], n_send.at[l, m, ai], n_recv.at[l, m, slot], (s, ai, b))

    def norm_first(l, m):
        xv = stream(l, m)
        nsend[l, m] = bf(xv * rms(xv, features) * small[l, experts + 1 : experts + 2])
        pos.peers(lambda ai: copy_n(l, m, ai, a).start())
        nall[l, m, a] = nsend[l, m]

    def copy_o(l, m, ai, slot):
        return remote(osend.at[l, m, ai], orecv.at[l, m, slot], o_send.at[l, m, ai], o_recv.at[l, m, slot], (s, ai, b))

    def attention(l, m):
        watt = watts[l]
        pos.peers(lambda ai: copy_n(l, m, ai, ai).wait())
        proj[...] = by_blocks(nall[l, m].reshape(length, d), watt, slice(0, 3 * pw), width, pw)
        v[l, m] = bf(proj[:, 2 * pw : 3 * pw])
        q[l, m] = turn(proj[:, :pw], cos[...], sin[...], rot[...], 1.0)
        k[l, m] = turn(proj[:, pw : 2 * pw], cos[...], sin[...], rot[...], 1.0)
        total = jnp.zeros((length, pw), jnp.float32)
        for h in range(heads):
            mask = head_mask(pw, h)
            p = probs_of(jnp.where(mask, q[l, m], 0), k[l, m])
            total = total + mm(bf(p), jnp.where(mask, v[l, m], 0))
        att[l, m] = bf(total)
        for j in range(ny):
            part = mm(att[l, m], watt[j, :, 3 * pw : 4 * pw], ((1,), (1,)))
            osend[l, m, :, :, j * pw : j * pw + width] = bf(part).reshape(nx, sub, width)
        pos.peers(lambda ai: copy_o(l, m, ai, a).start())
        orecv[l, m, a] = osend[l, m, a]

    def copy_x(l, m, bi, slot):
        return remote(xsend.at[l, m, bi], xline.at[l, m, slot], x_send.at[l, m, bi], x_recv.at[l, m, slot], (s, a, bi))

    def copy_w(l, m, ai, slot):
        return remote(xline.at[l, m], xall.at[l, m, :, slot], u_send.at[l, m, ai], u_recv.at[l, m, slot], (s, ai, b))

    def copy_t(l, m, ai, slot):
        return remote(n2.at[l, m], nrows.at[l, m, slot], t_send.at[l, m, ai], t_recv.at[l, m, slot], (s, ai, b))

    def norm_second(l, m):
        pos.peers(lambda ai: copy_o(l, m, ai, ai).wait())
        mv = stream(l, m)
        for ai in range(nx):
            mv = mv + orecv[l, m, ai].astype(jnp.float32)
        mid[l, m] = mv
        n2v = bf(mv * rms(mv, features) * small[l, experts : experts + 1])
        n2[l, m] = n2v
        rv = mm(n2v, rwx[l], ((1,), (1,)))
        hi = bf(rv)
        lo = bf(rv - hi.astype(jnp.float32))
        tail = jnp.where(lane < width + experts, hi, lo)
        for j in range(ny):
            xsend[l, m, j] = jnp.where(lane < width, n2v[:, j * pw : (j + 1) * pw], tail)
        pos.line(lambda bi: copy_x(l, m, bi, b).start())
        xline[l, m, b] = xsend[l, m, b]
        pos.peers(lambda ai: copy_t(l, m, ai, a).start())
        nrows[l, m, a] = n2[l, m]

    def spread(l, m):
        pos.line(lambda bi: copy_x(l, m, bi, bi).wait())
        pos.peers(lambda ai: copy_w(l, m, ai, a).start())
        xall[l, m, :, a] = xline[l, m]

    def dispatch(l, m):
        i0 = lax.broadcasted_iota(jnp.int32, (slots_n, tokens), 0)
        pm[...] = bf(((place[l, m, 0:1] == i0) | (place[l, m, 1:2] == i0)).astype(jnp.float32))
        pos.peers(lambda ai: copy_w(l, m, ai, ai).wait())
        slots[l, m] = bf(mm(pm[...], xall[l, m].reshape(tokens, pw))).reshape(experts, cap, pw)

    def grad_send(m):
        for j in range(ny):
            xsend[0, m, j] = tok[1, m, :, j * pw : (j + 1) * pw]
        pos.line(lambda bi: copy_x(0, m, bi, b).start())
        xline[0, m, b] = xsend[0, m, b]

    def copy_gw(m, ai, slot):
        return remote(xline.at[0, m], gall.at[m, :, slot], gu_send.at[m, ai], gu_recv.at[m, slot], (s, ai, b))

    def grad_spread(m):
        pos.line(lambda bi: copy_x(0, m, bi, bi).wait())
        pos.peers(lambda ai: copy_gw(m, ai, a).start())
        gall[m, :, a] = xline[0, m]

    def grad_dispatch(m):
        i0 = lax.broadcasted_iota(jnp.int32, (slots_n, tokens), 0)
        pm[...] = bf(((place[1, m, 0:1] == i0) | (place[1, m, 1:2] == i0)).astype(jnp.float32))
        pos.peers(lambda ai: copy_gw(m, ai, ai).wait())
        gslots[m] = bf(mm(pm[...], gall[m].reshape(tokens, pw))).reshape(experts, cap, pw)

    def shared_in_part(l, m):
        pos.peers(lambda ai: copy_t(l, m, ai, ai).wait())
        shw = shws[l]
        gu_s = by_blocks(nrows[l, m].reshape(length, d), shw, slice(0, 2 * f), width, pw)
        sgu[l, m] = bf(gu_s)
        gate = gu_s[:, :f]
        shid[l, m] = bf(gate * jax.nn.sigmoid(gate) * gu_s[:, f:])

    def copy_s(l, m, ai, slot):
        return remote(ssend.at[l, m, ai], srecv.at[l, m, slot], s_send.at[l, m, ai], s_recv.at[l, m, slot], (s, ai, b))

    def shared_out_part(l, m):
        for j in range(ny):
            part = mm(shid[l, m], shws[l][j, :, 2 * f :], ((1,), (1,)))
            ssend[l, m, :, :, j * pw : j * pw + width] = bf(part).reshape(nx, sub, width)
        pos.peers(lambda ai: copy_s(l, m, ai, a).start())
        srecv[l, m, a] = ssend[l, m, a]

    def copy_g(l, m, ai, slot):
        return remote(rsend.at[l, m, ai], rpeer.at[l, m, slot], g_send.at[l, m, ai], g_recv.at[l, m, slot], (s, ai, b))

    def copy_r(l, m, bi, slot):
        return remote(rline.at[l, m, bi], rrecv.at[l, m, slot], r_send.at[l, m, bi], r_recv.at[l, m, slot], (s, a, bi))

    def combine(l, m):
        i1 = lax.broadcasted_iota(jnp.int32, (tokens, slots_n), 1)
        pt[...] = bf(((place_t[l, m, :, 0:1] == i1) | (place_t[l, m, :, 1:2] == i1)).astype(jnp.float32))
        br = mm(pt[...], eo[m].reshape(slots_n, width))
        for ai in range(nx):
            rsend[l, m, ai, :, :, :width] = bf(br).reshape(ny, nx, sub, width)[:, ai]
        pos.peers(lambda ai: copy_g(l, m, ai, a).start())
        rpeer[l, m, a] = rsend[l, m, a]

    def combine_line(l, m):
        pos.peers(lambda ai: copy_g(l, m, ai, ai).wait())
        total = rpeer[l, m, 0].astype(jnp.float32)
        for ai in range(1, nx):
            total = total + rpeer[l, m, ai].astype(jnp.float32)
        rline[l, m] = bf(total)
        pos.line(lambda bi: copy_r(l, m, bi, b).start())
        rrecv[l, m, b] = rline[l, m, b]

    def layer_out(l, m):
        pos.peers(lambda ai: copy_s(l, m, ai, ai).wait())
        pos.line(lambda bi: copy_r(l, m, bi, bi).wait())
        total = mid[l, m]
        for ai in range(nx):
            total = total + srecv[l, m, ai].astype(jnp.float32)
        for j in range(ny):
            part = total[:, j * pw : (j + 1) * pw]
            part = part + jnp.where(lane < width, rrecv[l, m, j].astype(jnp.float32), 0.0)
            y[l, m, :, j * pw : (j + 1) * pw] = bf(part)

    first = (b == ny - 1, b == 0)
    last = (b == 0, b == ny - 1)
    up = (ny - 1 - b, b)
    down = (b, ny - 1 - b)
    lag = (sk + ak) * (ny - 1)
    apart = STAGE_STEPS
    units = 2 * half
    gap = max(lag + 6 * apart - units, 0)
    starts = (0, units, 2 * units + gap, 3 * units + gap)
    steps = starts[3] + units + lag

    def unit(t, dd):
        early = (t >= 0) & (t < 2 * units)
        late = (t >= starts[2]) & (t < starts[2] + 2 * units)
        u = jnp.clip(jnp.where(t < starts[2], jnp.minimum(t, 2 * units - 1), t - gap), 0, 4 * units - 1)
        job, r = u // units, lax.rem(u, units)
        return early | late, job // 2, lax.rem(job, 2), r // 2 + dd * half, lax.rem(r, 2)

    def gu_copy(dd, l, m, e, c):
        to = b - 1 if dd == 0 else b + 1
        return remote(gu.at[l, m, e, c], gu.at[l, m, e, c], rs_send.at[l, m, e, c], rs_recv.at[l, m, e, c], (s, a, to))

    def hid_copy(dd, l, m, e, c):
        to = b + 1 if dd == 0 else b - 1
        return remote(hid.at[l, m, e, c], hid.at[l, m, e, c], ag_send.at[l, m, e, c], ag_recv.at[l, m, e, c], (s, a, to))

    def save_gates(l, m, e, c):
        return pltpu.make_async_copy(gu.at[l, m, e, c], gu_o.at[l, m, e, c], g_sem.at[l, m, e, c])

    def chain(i):
        reduce = [unit(i - sk * up[dd], dd) for dd in range(2)]
        spreads = [unit(i - sk * (ny - 1) - ak * down[dd], dd) for dd in range(2)]
        for dd in range(2):
            valid, l, m, e, c = reduce[dd]

            @pl.when(valid)
            def _():
                @pl.when((m == 0) & (c == 0))
                def _():
                    wait_weight(0, e, 0)

                for plane in range(2):
                    part = win[e, plane, :, pl.ds(pl.multiple_of(c * hw, hw), hw)]
                    acc[dd, :, plane * hw : (plane + 1) * hw] = mm(slots[l, m, e, :, :width], part)

                @pl.when((l == 0) & (m == 1) & (c == 1))
                def _():
                    start_weight(1, e, 0)

        for dd in range(2):
            valid, l, m, e, c = reduce[dd]

            @pl.when(valid & first[dd])
            def _():
                gu[l, m, e, c] = bf(acc[dd])
                gu_copy(dd, l, m, e, c).start()

            @pl.when(valid & jnp.logical_not(first[dd] | last[dd]))
            def _():
                gu_copy(dd, l, m, e, c).wait_recv()
                gu[l, m, e, c] = bf(acc[dd] + gu[l, m, e, c].astype(jnp.float32))
                gu_copy(dd, l, m, e, c).start()

            @pl.when(valid & last[dd])
            def _():
                gu_copy(dd, l, m, e, c).wait_recv()
                total = acc[dd] + gu[l, m, e, c].astype(jnp.float32)
                r = router_column(slots[l, m, e], e, width, experts)
                gate = total[:, :hw]
                hid[l, m, e, c] = bf(gate * jax.nn.sigmoid(gate) * total[:, hw:] * jax.nn.sigmoid(r))
                hid_copy(dd, l, m, e, c).start()
                gu[l, m, e, c] = bf(total)
                save_gates(l, m, e, c).start()

        for dd in range(2):
            valid, l, m, e, c = spreads[dd]

            @pl.when(valid & jnp.logical_not(last[dd]))
            def _():
                hid_copy(dd, l, m, e, c).wait_recv()

                @pl.when(jnp.logical_not(first[dd]))
                def _():
                    hid_copy(dd, l, m, e, c).start()

        for dd in range(2):
            valid, l, m, e, c = spreads[dd]

            @pl.when(valid & (c == 1))
            def _():
                @pl.when(m == 0)
                def _():
                    wait_weight(0, e, 1)

                total = mm(hid[l, m, e, 0], wdt[e, :, :hw], ((1,), (1,)))
                eo[m, e] = bf(total + mm(hid[l, m, e, 1], wdt[e, :, hw:], ((1,), (1,))))

                @pl.when((l == 0) & (m == 1))
                def _():
                    start_weight(1, e, 1)

    kept = (
        (slots, slots_o), (nall, rows_o), (q, q_o), (k, k_o), (v, v_o), (att, att_o), (mid, mid_o), (n2, n2_o),
        (nrows, rows2_o), (sgu, sgu_o), (shid, shid_o), (shw0, shw_o.at[0]), (shw1, shw_o.at[1]), (watt1, watt_o),
        (watt0, watt0_o), (tok, tok_o), (small, small_o), (place, place_o), (place_t, place_to),
        (gslots, gslots_o), (hid, hid_o), (y, y_o),
    )
    saves = [pltpu.make_async_copy(src, dst, k_sem.at[c]) for c, (src, dst) in enumerate(kept)]

    def save(copies):
        for copy in copies:
            copy.start()

    stages = {}

    def at(step, do):
        stages.setdefault(step, []).append(do)

    def stage(do, l, m):
        return lambda: do(l, m)

    osend[...] = jnp.zeros_like(osend)
    ssend[...] = jnp.zeros_like(ssend)
    rwx[...] = jnp.zeros_like(rwx)
    for h in range(1, ny):
        for share in entry_shares[:2]:
            share.hop(h)
        if h == 2:
            entry_shares[2].hop(1)
            entry_shares[3].hop(1)
    for share in entry_shares[:2]:
        share.finish()
    tokens_ready()
    for l, full in enumerate((sm0, sm1)):
        for j in range(ny):
            small[l, :, j * pw : (j + 1) * pw] = full[j]
    for l in range(2):
        rwx[l, width : width + experts] = bf(small[l, :experts])
        rwx[l, width + experts : width + 2 * experts] = bf(small[l, :experts])
    norm_first(0, 0)
    norm_first(0, 1)
    entry_shares[2].hop(2)
    entry_shares[3].hop(2)
    places()
    entry_shares[2].hop(3)
    entry_shares[3].hop(3)
    entry_shares[2].finish()
    entry_shares[3].finish()
    shares[0].start()
    shares[1].start()
    attention(0, 0)
    attention(0, 1)
    norm_second(0, 0)
    norm_second(0, 1)
    weights_ready()
    spread(0, 0)
    shares[0].hop(1)
    shares[1].hop(1)
    spread(0, 1)
    dispatch(0, 0)
    for h in range(2, ny):
        at(2 * (h - 2), lambda h=h: (shares[0].hop(h), shares[1].hop(h)))
    at(units // 4, stage(dispatch, 0, 1))
    at(2 * (ny - 2) + 1, lambda: (shares[0].finish(), shares[1].finish()))
    at(units // 2, stage(shared_in_part, 0, 0))
    at(units // 2 + 2, stage(shared_out_part, 0, 0))
    at(units, stage(shared_in_part, 0, 1))
    at(units + 2, stage(shared_out_part, 0, 1))
    for m in range(2):
        done = starts[m] + units - 1 + lag
        for c, do in enumerate((combine, combine_line)):
            at(done + c * apart, stage(do, 0, m))
        at(done + 2 * apart, stage(layer_out, 0, m))
        for c, do in enumerate((norm_first, attention, norm_second, spread, dispatch)):
            at(done + (2 + c) * apart, stage(do, 1, m))
        at(starts[2 + m] + 4, stage(shared_in_part, 1, m))
        at(starts[2 + m] + 8, stage(shared_out_part, 1, m))
        done = starts[2 + m] + units - 1 + lag
        for c, do in enumerate((combine, combine_line, layer_out)):
            at(done + c * apart, stage(do, 1, m))
    at(starts[3] + 9, lambda: save(saves[:-2]))
    at(starts[3] + units - 1 + lag, lambda: save(saves[-2:-1]))
    for m in range(2):
        at(units + 4 + m, lambda m=m: grad_send(m))
        at(units + 6 + m, lambda m=m: grad_spread(m))
        at(units + 8 + m, lambda m=m: grad_dispatch(m))
    at(units + lag - 1, shares[2].start)
    for h in range(1, ny):
        at(units + lag - 1 + 2 * h, lambda h=h: shares[2].hop(h))
    at(units + lag - 1 + 2 * ny, shares[2].finish)

    def step(i, c):
        chain(i)
        for when in sorted(stages):
            if when < steps:
                @pl.when(i == when)
                def _():
                    for do in stages[when]:
                        do()

        return c

    lax.fori_loop(0, steps, step, 0)
    for when in sorted(stages):
        if when >= steps:
            for do in stages[when]:
                do()
    saves[-1].start()

    def finish(index, carry):
        l = index // (mbs * units)
        m = lax.rem(index // units, mbs)
        r = lax.rem(index, units)
        for dd in range(2):
            e, c = r // 2 + dd * half, lax.rem(r, 2)
            pl.when(jnp.logical_not(last[dd]))(gu_copy(dd, l, m, e, c).wait_send)
            pl.when(jnp.logical_not(first[dd]))(hid_copy(dd, l, m, e, c).wait_send)
            pl.when(last[dd])(save_gates(l, m, e, c).wait)
        return carry

    lax.fori_loop(0, 2 * mbs * units, finish, 0)
    for copy in saves:
        copy.wait()


def forward(tin, small_b, att_block, sh_block, routes, cos, sin, rot, win, wdt, dims, heads, features, ids):
    width, pw, experts, cap = dims
    nx, ny = lax.axis_size("gx"), lax.axis_size("gy")
    mbs, length = tin.shape[1:3]
    sub, d = length // nx, ny * pw
    f = wdt.shape[-1]
    length, tokens, n, slots = nx * sub, nx * ny * sub, nx * ny, experts * cap
    b16, f32 = jnp.bfloat16, jnp.float32
    vm = pl.BlockSpec(memory_space=pltpu.VMEM)
    hbm = pl.BlockSpec(memory_space=pl.ANY)
    lm = (2, mbs)
    rows_shape = lm + (nx, sub, d)
    spread_shape = lm + (ny, nx, sub, pw)
    entry = (
        (win.shape, b16), (wdt.shape, b16),
        ((2, mbs, sub, d), b16), ((2, small_b.shape[0], d), f32), (lm + (2, tokens), jnp.int32),
        (lm + (tokens, 2), jnp.int32), ((ny,) + att_block.shape, b16),
    )
    kept = entry + (
        (lm + (sub, d), b16), (lm + (sub, d), f32), (lm + (sub, d), b16), (rows_shape, b16),
        (lm + (length, pw), b16), (lm + (length, pw), b16), (lm + (length, pw), b16), (lm + (length, pw), b16),
        (lm + (experts, cap, pw), b16), (lm + (experts, 2, cap, f), b16), (lm + (experts, 2, cap, f // 2), b16),
        (rows_shape, b16), (lm + (length, 2 * f), b16), (lm + (length, f), b16),
        ((2, ny) + sh_block.shape, b16), ((ny,) + att_block.shape, b16), ((mbs, experts, cap, pw), b16),
    )
    scratch = (
        (lm + (sub, d), b16), (lm + (sub, d), f32), (lm + (sub, d), b16), None,
        (lm + (sub, d), b16), (rows_shape, b16), ((length, 3 * pw), f32),
        (lm + (length, pw), b16), (lm + (length, pw), b16), (lm + (length, pw), b16), (lm + (length, pw), b16),
        (rows_shape, b16), (rows_shape, b16), ((2, pw, d), b16),
        (lm + (ny, sub, pw), b16), (lm + (ny, sub, pw), b16), (spread_shape, b16), (rows_shape, b16),
        ((slots, tokens), b16), ((tokens, slots), b16), (lm + (experts, cap, pw), b16), ((2, cap, f), f32),
        (lm + (experts, 2, cap, f), b16), (lm + (experts, 2, cap, f // 2), b16), ((mbs, experts, cap, width), b16),
        (lm + (length, 2 * f), b16), (lm + (length, f), b16), (rows_shape, b16), (rows_shape, b16),
        (lm + (nx, ny, sub, pw), b16), (lm + (nx, ny, sub, pw), b16), (lm + (ny, sub, pw), b16), (lm + (ny, sub, pw), b16),
        (win.shape, b16), (wdt.shape, b16),
        ((ny,) + sh_block.shape, b16), ((ny,) + sh_block.shape, b16), ((ny,) + att_block.shape, b16), ((ny,) + att_block.shape, b16),
        ((ny, 2, mbs, sub, pw), b16), ((2, mbs, sub, d), b16), (lm + (2, tokens), jnp.int32),
        (lm + (2, tokens), jnp.int32), (lm + (tokens, 2), jnp.int32),
        ((ny,) + small_b.shape, f32), ((ny,) + small_b.shape, f32), ((2, small_b.shape[0], d), f32),
        ((mbs, ny, nx, sub, pw), b16), ((mbs, experts, cap, pw), b16),
    )
    outs = pl.pallas_call(
        functools.partial(forward_kernel, (nx, ny, mbs, sub, width, pw, heads, features, experts, cap, f, *FWD_SKEW)),
        out_shape=tuple(jax.ShapeDtypeStruct(*v) for v in kept),
        in_specs=[vm] * 8 + [hbm] * 2,
        out_specs=(hbm,) * len(kept),
        scratch_shapes=[pltpu.VMEM(*(v or ((8, 128), f32))) for v in scratch] + [
            flags(lm + (nx,)), flags(lm + (nx,)), flags(lm + (nx,)), flags(lm + (nx,)),
            flags(lm + (ny,)), flags(lm + (ny,)), flags(lm + (nx,)), flags(lm + (nx,)), flags(lm + (nx,)), flags(lm + (nx,)),
            flags(lm + (nx,)), flags(lm + (nx,)), flags(lm + (nx,)), flags(lm + (nx,)), flags(lm + (ny,)), flags(lm + (ny,)),
            flags(lm + (experts, 2)), flags(lm + (experts, 2)), flags(lm + (experts, 2)), flags(lm + (experts, 2)),
            flags((experts,)), flags((experts,)), flags(lm + (experts, 2)), flags((24,)),
            flags((nx,)), flags((ny,)), pltpu.SemaphoreType.DMA, pltpu.SemaphoreType.DMA, flags((2,)), flags((2,)), flags((mbs, nx)), flags((mbs, nx)),
        ] + share_sems(ny) * 7,
        compiler_params=params(ids),
        cost_estimate=pl.CostEstimate(flops=10**10, bytes_accessed=8 * 10**7, transcendentals=10**6),
        name="forward",
    )(tin, small_b, att_block, sh_block, routes, cos, sin, rot, win, wdt)
    names = ("win", "wdt", "tok", "small", "place", "place_t", "watt0", "y", "mid", "n2", "rows", "q", "k", "v", "att", "slots", "gu", "hid", "rows2", "sgu", "shid", "shw", "watt1", "gslots")
    return dict(zip(names, outs))


FWD_SKEW = (2, 2)
STAGE_STEPS = 2


def backward_kernel(cfg, *refs):
    nx, ny, mbs, sub, width, pw, heads, features, experts, cap, f, sk, ak = cfg
    (tok_i, small_i, place_i, y_i, mid_i, n2_i, rows_i, q_i, k_i, v_i, att_i, rows2_i, sgu_i, shid_i, shw_i,
     watt0_i, watt1_i, cos, sin, rot, slots_i, gu_i, hid_i, gslots_i, win_a, win_b, wdt_a, wdt_b) = refs[:28]
    (out_o, win_g, wdt_g, att_g, sh_g, small_g,
     win, wdt, xsend, xline, xall, grows, pm, pt, slots, gslots, gown, hid, acc, dh, dgu, deo, sti, std,
     dsgu, ssend, srecv, rsend, rpeer, rline, rrecv, rwx, dm, msend, mall, datt, dqkv, dsend, drecv,
     rw_p, gains, drs, sh_p, att_p, small_p, sh_x, att_x, small_x, sh_r, att_r, small_r, sh_f, att_f, small_f, small_a,
     yv, obuf, g, gx, small, place, x, mid, n2, rows, q, k, v, att, rows2, sgu, shid, shw, watt,
     w_sem, x_send, x_recv, u_send, u_recv, t_send, t_recv, s_send, s_recv, g_send, g_recv, r_send, r_recv,
     m_send, m_recv, d_send, d_recv, rs_send, rs_recv, ag_send, ag_recv, wi_send, wi_recv, wd_send, wd_recv,
     c_send, c_recv, e_send, e_recv, a_send, a_recv, l_sem, st_sem, f_sem, y_sem, o_send, o_recv, free) = refs[28:]
    pos = Position(nx, ny)
    s, a, b = pos.s, pos.a, pos.b
    slots_n = experts * cap
    tokens = nx * ny * sub
    d = ny * pw
    length = nx * sub
    half, hw = experts // 2, f // 2
    scale = DH ** -0.5
    lane = lax.broadcasted_iota(jnp.int32, (1, pw), 1)
    first = (b == ny - 1, b == 0)
    last = (b == 0, b == ny - 1)
    up = (ny - 1 - b, b)
    down = (b, ny - 1 - b)
    barrier = pltpu.get_barrier_semaphore()
    pos.peers(lambda ai: pl.semaphore_signal(barrier, inc=1, device_id=(s, ai, b), device_id_type=MESH))
    pos.line(lambda bi: pl.semaphore_signal(barrier, inc=1, device_id=(s, a, bi), device_id_type=MESH))
    pl.semaphore_signal(barrier, inc=1, device_id=(1 - s, a, b), device_id_type=MESH)
    for so in range(2):
        for i in range(nx):
            @pl.when((so != s) | (i != a) | (a != b))
            def _():
                pl.semaphore_signal(barrier, inc=1, device_id=(so, i, a), device_id_type=MESH)

    def weight_copy(l, e, which):
        own, oth, dst = ((win_a, win_b, win), (wdt_a, wdt_b, wdt))[which]
        sem = w_sem.at[which, e]
        return pltpu.make_async_copy(own.at[e], dst.at[e], sem), pltpu.make_async_copy(oth.at[e], dst.at[e], sem)

    def start_weights(l, e):
        for which in range(2):
            own, oth = weight_copy(l, e, which)
            pl.when(s == l)(own.start)
            pl.when(s != l)(oth.start)

    def first_weights(e, c):
        start_weights(1, e)
        return c

    lax.fori_loop(0, experts, first_weights, 0)

    early = ((rows2_i, rows2), (sgu_i, sgu), (shid_i, shid), (shw_i, shw))
    later = ((mid_i, mid), (n2_i, n2), (rows_i, rows), (q_i, q), (k_i, k), (v_i, v), (att_i, att))

    def early_loads(l):
        return [pltpu.make_async_copy(src.at[l], dst, y_sem.at[c]) for c, (src, dst) in enumerate(early)]

    def later_loads(l):
        copies = [pltpu.make_async_copy(src.at[l], dst, y_sem.at[4 + c]) for c, (src, dst) in enumerate(later)]
        copies.append(pltpu.make_async_copy(y_i.at[0] if l else tok_i.at[0], x, y_sem.at[11]))
        return copies + [pltpu.make_async_copy(watt1_i if l else watt0_i, watt, y_sem.at[12])]

    def hid_load(l):
        return pltpu.make_async_copy(hid_i.at[l], hid, l_sem.at[1])

    def gates(l, m, dd):
        return pltpu.make_async_copy(gu_i.at[l, m, pl.ds(dd * half, half)], gown.at[m], l_sem.at[2 + m])

    def start_gates(l, m):
        for dd in range(2):
            pl.when(last[dd])(gates(l, m, dd).start)

    def wait_gates(l, m):
        for dd in range(2):
            pl.when(last[dd])(gates(l, m, dd).wait)

    first_loads = [
        pltpu.make_async_copy(src, dst, y_sem.at[13 + c])
        for c, (src, dst) in enumerate(((tok_i.at[1], g), (small_i, small), (place_i, place), (y_i, yv)))
    ]
    slots_load = pltpu.make_async_copy(slots_i, slots, l_sem.at[0])
    gslots_load = pltpu.make_async_copy(gslots_i, gslots.at[1], l_sem.at[4])
    for copy in first_loads + [slots_load, gslots_load, hid_load(1)] + early_loads(1) + later_loads(1):
        copy.start()
    for m in range(mbs):
        start_gates(1, m)

    def copy_x(m, bi, slot):
        return remote(xsend.at[m, bi], xline.at[m, slot], x_send.at[m, bi], x_recv.at[m, slot], (s, a, bi))

    def copy_w(m, ai, slot):
        return remote(xline.at[m], xall.at[m, :, slot], u_send.at[m, ai], u_recv.at[m, slot], (s, ai, b))

    def copy_t(m, ai, slot):
        return remote(g.at[m], grows.at[m, slot], t_send.at[m, ai], t_recv.at[m, slot], (s, ai, b))

    for copy in first_loads:
        copy.wait()

    @pl.when(a == b)
    def _():
        pl.semaphore_wait(barrier, nx - 1 + ny - 1 + 1 + 2 * ny - 1)

    @pl.when(a != b)
    def _():
        pl.semaphore_wait(barrier, nx - 1 + ny - 1 + 1 + 2 * ny)

    def out_copy(kind, l, j, s_slot, a_slot):
        src = (yv, gx)[kind].at[l, :, :, pl.ds(j * pw, pw)]
        return remote(src, obuf.at[kind, s_slot, a_slot], o_send.at[kind, l, j], o_recv.at[kind, s_slot, a_slot], (l, b, j))

    def send_out(kind, l):
        for j in range(ny):
            @pl.when((l != s) | (a != b) | (j != b))
            def _():
                out_copy(kind, l, j, s, a).start()

        @pl.when((l == s) & (a == b))
        def _():
            obuf[kind, s, a] = (yv, gx)[kind][l, :, :, pl.ds(pl.multiple_of(b * pw, pw), pw)]

    def sent_out(kind, l):
        for j in range(ny):
            @pl.when((l != s) | (a != b) | (j != b))
            def _():
                out_copy(kind, l, j, s, a).wait_send()

    def take_out(kind):
        for so in range(2):
            for i in range(nx):
                @pl.when((so != s) | (a != b) | (i != a))
                def _():
                    out_copy(kind, 0, 0, so, i).wait_recv()

                out_o[kind, so * mbs : (so + 1) * mbs, i * sub : (i + 1) * sub, :] = obuf[kind, so, i]

    def send_g(m, slots_too=True):
        if slots_too:
            for j in range(ny):
                xsend[m, j] = g[m, :, j * pw : (j + 1) * pw]
            pos.line(lambda bi: copy_x(m, bi, b).start())
            xline[m, b] = xsend[m, b]
        pos.peers(lambda ai: copy_t(m, ai, a).start())
        grows[m, a] = g[m]

    send_g(0, False)
    send_g(1, False)
    deo[...] = jnp.zeros_like(deo)
    ssend[...] = jnp.zeros_like(ssend)
    dsend[...] = jnp.zeros_like(dsend)
    rwx[...] = jnp.zeros_like(rwx)

    def new_layer(l):
        rwx[width : width + experts] = bf(small[l, :experts])
        rwx[width + experts : width + 2 * experts] = bf(small[l, :experts])
        rw_p[...] = jnp.zeros_like(rw_p)
        gains[...] = jnp.zeros_like(gains)

    new_layer(1)

    def spread(m):
        pos.line(lambda bi: copy_x(m, bi, bi).wait())
        pos.peers(lambda ai: copy_w(m, ai, a).start())
        xall[m, :, a] = xline[m]

    def dispatch(l, m):
        i0 = lax.broadcasted_iota(jnp.int32, (slots_n, tokens), 0)
        pm[...] = bf(((place[l, m, 0:1] == i0) | (place[l, m, 1:2] == i0)).astype(jnp.float32))
        pos.peers(lambda ai: copy_w(m, ai, ai).wait())
        gslots[l, m] = bf(mm(pm[...], xall[m].reshape(tokens, pw))).reshape(experts, cap, pw)

    def shared_act(m):
        pos.peers(lambda ai: copy_t(m, ai, ai).wait())
        dsh = by_blocks(grows[m].reshape(length, d), shw, slice(2 * f, 3 * f), width, pw)
        dsg, dsu, _ = act_back(sgu[m, :, :f].astype(jnp.float32), sgu[m, :, f:].astype(jnp.float32), dsh, None)
        dsgu[m, :, :f] = bf(dsg)
        dsgu[m, :, f:] = bf(dsu)

    def copy_s(m, ai, slot):
        return remote(ssend.at[m, ai], srecv.at[m, slot], s_send.at[m, ai], s_recv.at[m, slot], (s, ai, b))

    def shared_back(m):
        for j in range(ny):
            part = mm(dsgu[m], shw[j, :, : 2 * f], ((1,), (1,)))
            ssend[m, :, :, j * pw : j * pw + width] = bf(part).reshape(nx, sub, width)
        pos.peers(lambda ai: copy_s(m, ai, a).start())
        srecv[m, a] = ssend[m, a]

    crossing = ((sh_p, sh_x), (att_p, att_x), (small_p, small_x))
    places = (sh_r, att_r, small_r)
    finals = (sh_f, att_f, small_f)
    results = (sh_g, att_g, small_g)

    def cross(l, i):
        return remote(crossing[i][0], crossing[i][1], c_send.at[i], c_recv.at[i], (l, a, b))

    def block(i, bi):
        if i == 2:
            return small_x.at[:, pl.ds(pl.multiple_of(bi * pw, pw), pw)]
        return crossing[i][1].at[bi]

    def along(i, bi, slot):
        return remote(block(i, bi), places[i].at[slot], e_send.at[i, bi], e_recv.at[i, slot], (s, a, bi))

    def give(l, i):
        pl.when(s != l)(cross(l, i).start)

    def given(l):
        for i in range(3):
            pl.when(s != l)(cross(l, i).wait_send)

    def join(l, i):
        @pl.when(s == l)
        def _():
            cross(l, i).wait_recv()
            part, other = crossing[i]
            other[...] = (part[...].astype(jnp.float32) + other[...].astype(jnp.float32)).astype(other.dtype)
            pos.line(lambda bi: along(i, bi, lax.rem(b - bi + ny, ny) - 1).start())

    def settle(l, i):
        @pl.when(s == l)
        def _():
            pos.line(lambda bi: along(i, bi, lax.rem(bi - b + ny, ny) - 1).wait())
            total = block(i, b)[...].astype(jnp.float32)
            for c in range(1, ny):
                total = total + places[i][c - 1].astype(jnp.float32)
            finals[i][...] = total
            if i < 2:
                pltpu.make_async_copy(finals[i], results[i], f_sem.at[i]).start()

    def shared_grads():
        for j in range(ny):
            rj = rows2[:, :, :, j * pw : j * pw + width].reshape(mbs * length, width)
            sh_p[j, :, : 2 * f] = bf(mm(rj, dsgu[...].reshape(mbs * length, 2 * f), ((0,), (0,))))

    def down_grads(l):
        for j in range(ny):
            gj = grows[:, :, :, j * pw : j * pw + width].reshape(mbs * length, width)
            sh_p[j, :, 2 * f :] = bf(mm(gj, shid[...].reshape(mbs * length, f), ((0,), (0,))))
        give(l, 0)

    def copy_g(m, ai, slot):
        return remote(rsend.at[m, ai], rpeer.at[m, slot], g_send.at[m, ai], g_recv.at[m, slot], (s, ai, b))

    def copy_r(m, bi, slot):
        return remote(rline.at[m, bi], rrecv.at[m, slot], r_send.at[m, bi], r_recv.at[m, slot], (s, a, bi))

    def combine(l, m):
        row = lax.broadcasted_iota(jnp.int32, (128, tokens), 0)
        pair = place[l, m].astype(jnp.float32)
        cols = jnp.where(row == 0, pair[0:1], jnp.where(row == 1, pair[1:2], 0.0)).T.astype(jnp.int32)
        part = tokens // 2
        i1 = lax.broadcasted_iota(jnp.int32, (part, slots_n), 1)
        for c in range(2):
            these = cols[c * part : (c + 1) * part]
            pt[...] = bf(((these[:, 0:1] == i1) | (these[:, 1:2] == i1)).astype(jnp.float32))
            br = bf(mm(pt[...], deo[m].reshape(slots_n, pw))).reshape(ny // 2, nx, sub, pw)
            for ai in range(nx):
                rsend[m, ai, c * (ny // 2) : (c + 1) * (ny // 2)] = br[:, ai]
        pos.peers(lambda ai: copy_g(m, ai, a).start())
        rpeer[m, a] = rsend[m, a]

    def combine_line(m):
        pos.peers(lambda ai: copy_g(m, ai, ai).wait())
        total = rpeer[m, 0].astype(jnp.float32)
        for ai in range(1, nx):
            total = total + rpeer[m, ai].astype(jnp.float32)
        rline[m] = bf(total)
        pos.line(lambda bi: copy_r(m, bi, b).start())
        rrecv[m, b] = rline[m, b]

    def copy_m(m, ai, slot):
        return remote(msend.at[m], mall.at[m, slot], m_send.at[m, ai], m_recv.at[m, slot], (s, ai, b))

    def second_norm(l, m):
        pos.peers(lambda ai: copy_s(m, ai, ai).wait())
        pos.line(lambda bi: copy_r(m, bi, bi).wait())
        dlog = jnp.zeros((sub, pw), jnp.float32)
        parts = []
        for j in range(ny):
            part = rrecv[m, j].astype(jnp.float32)
            dlog = dlog + jnp.where(lane >= width, part, 0.0)
            parts.append(jnp.where(lane < width, part, 0.0))
        hi = bf(dlog)
        lo = bf(dlog - hi.astype(jnp.float32))
        dn2 = jnp.concatenate(parts, 1) + mm(hi, rwx[...]) + mm(lo, rwx[...])
        for ai in range(nx):
            dn2 = dn2 + srecv[m, ai].astype(jnp.float32)
        rw_t = mm(hi, n2[m], ((0,), (0,))) + mm(lo, n2[m], ((0,), (0,)))
        rw_p[...] += rw_t[width : width + experts] + rw_t[width + experts : width + 2 * experts]
        mv = mid[m]
        dx2, gain_g = norm_back(mv, rms(mv, features), small[l, experts : experts + 1], dn2, features)
        gains[0:1] += gain_g
        dm[m] = g[m].astype(jnp.float32) + dx2
        msend[m] = bf(dm[m])
        pos.peers(lambda ai: copy_m(m, ai, a).start())
        mall[m, a] = msend[m]

    def copy_d(m, ai, slot):
        return remote(dsend.at[m, ai], drecv.at[m, slot], d_send.at[m, ai], d_recv.at[m, slot], (s, ai, b))

    def attention(m):
        pos.peers(lambda ai: copy_m(m, ai, ai).wait())
        datt[...] = bf(by_blocks(mall[m].reshape(length, d), watt, slice(3 * pw, 4 * pw), width, pw))
        dq = jnp.zeros((length, pw), jnp.float32)
        dk = dq
        dv = dq
        for h in range(heads):
            mask = head_mask(pw, h)
            qh = jnp.where(mask, q[m], 0)
            kh = jnp.where(mask, k[m], 0)
            da = jnp.where(mask, datt[...], 0)
            p = probs_of(qh, k[m])
            dp = mm(da, v[m], ((1,), (1,)))
            ds = bf(p * (dp - jnp.sum(dp * p, axis=1, keepdims=True)))
            dv = dv + mm(bf(p), da, ((0,), (0,)))
            dq = dq + mm(ds, kh)
            dk = dk + mm(ds, qh, ((0,), (0,)))
        dqkv[m, :, :pw] = turn(dq * scale, cos[...], sin[...], rot[...], -1.0)
        dqkv[m, :, pw : 2 * pw] = turn(dk * scale, cos[...], sin[...], rot[...], -1.0)
        dqkv[m, :, 2 * pw :] = bf(dv)
        for j in range(ny):
            part = mm(dqkv[m], watt[j, :, : 3 * pw], ((1,), (1,)))
            dsend[m, :, :, j * pw : j * pw + width] = bf(part).reshape(nx, sub, width)
        pos.peers(lambda ai: copy_d(m, ai, a).start())
        drecv[m, a] = dsend[m, a]

    def first_norm(l, m):
        pos.peers(lambda ai: copy_d(m, ai, ai).wait())
        dn1 = drecv[m, 0].astype(jnp.float32)
        for ai in range(1, nx):
            dn1 = dn1 + drecv[m, ai].astype(jnp.float32)
        xv = x[m].astype(jnp.float32)
        dx1, gain_g = norm_back(xv, rms(xv, features), small[l, experts + 1 : experts + 2], dn1, features)
        gains[1:2] += gain_g
        gx[l, m] = bf(dm[m] + dx1)
        if l:
            g[m] = gx[l, m]
            send_g(m)

    def attention_grads(l):
        for j in range(ny):
            cols = slice(j * pw, j * pw + width)
            rj = rows[:, :, :, cols].reshape(mbs * length, width)
            mj = mall[:, :, :, cols].reshape(mbs * length, width)
            qkv = mm(rj, dqkv[...].reshape(mbs * length, 3 * pw), ((0,), (0,)))
            rest = mm(mj, att[...].reshape(mbs * length, pw), ((0,), (0,)))
            parts = [qkv[:, c * pw : (c + 1) * pw] for c in range(3)] + [rest]
            for c in range(4):
                att_p[j, :, c * 128 : (c + 1) * 128] = bf(parts[c][:, :128])
            for c in range(2):
                joined = parts[2 * c][:, 128:] + pltpu.roll(parts[2 * c + 1][:, 128:], 64, 1)
                att_p[j, :, (4 + c) * 128 : (5 + c) * 128] = bf(joined)
        give(l, 1)

    def small_grads(l):
        small_p[:experts] = rw_p[...]
        small_p[experts:] = gains[...]
        give(l, 2)

    lag = (sk + ak) * (ny - 1)
    apart = STAGE_STEPS
    units = 2 * half
    gap = max(lag + 6 * apart - units, 0)
    starts = (0, units, 2 * units + gap, 3 * units + gap)

    def unit(t, dd):
        soon = (t >= 0) & (t < 2 * units)
        then = (t >= starts[2]) & (t < starts[2] + 2 * units)
        u = jnp.clip(jnp.where(t < starts[2], jnp.minimum(t, 2 * units - 1), t - gap), 0, 4 * units - 1)
        job, r = u // units, lax.rem(u, units)
        return soon | then, 1 - job // 2, lax.rem(job, 2), r // 2 + dd * half, lax.rem(r, 2)

    def dh_copy(dd, l, m, e, c):
        to = b - 1 if dd == 0 else b + 1
        return remote(dh.at[m, e, c], dh.at[m, e, c], rs_send.at[l, m, e, c], rs_recv.at[l, m, e, c], (s, a, to))

    def dgu_copy(dd, l, m, e, c):
        to = b + 1 if dd == 0 else b - 1
        return remote(dgu.at[m, e, c], dgu.at[m, e, c], ag_send.at[l, m, e, c], ag_recv.at[l, m, e, c], (s, a, to))

    def wi_copy(l, e):
        return remote(win.at[e], win.at[e], wi_send.at[l, e], wi_recv.at[l, e], (l, a, b))

    def wd_copy(l, e):
        return remote(wdt.at[e], wdt.at[e], wd_send.at[l, e], wd_recv.at[l, e], (l, a, b))

    def st_copies(e):
        return (pltpu.make_async_copy(sti, win_g.at[e], st_sem.at[0]), pltpu.make_async_copy(std, wdt_g.at[e], st_sem.at[1]))

    def weight_grads(l, e):
        sl = slots[l, :, e, :, :width].reshape(mbs * cap, width)
        gs = gslots[l, :, e, :, :width].reshape(mbs * cap, width)
        gi = [mm(sl, dgu[:, e, c].reshape(mbs * cap, f), ((0,), (0,))) for c in range(2)]
        gd = [mm(gs, hid[:, e, c].reshape(mbs * cap, hw), ((0,), (0,))) for c in range(2)]
        return gi, gd

    late = 2
    steps = starts[3] + units + lag + 2 * late

    def chain(i):
        reduce = [unit(i - sk * up[dd], dd) for dd in range(2)]
        spreads = [unit(i - sk * (ny - 1) - ak * down[dd], dd) for dd in range(2)]
        for dd in range(2):
            valid, l, m, e, c = reduce[dd]

            @pl.when(valid)
            def _():
                @pl.when((m == 0) & (c == 0))
                def _():
                    weight_copy(0, e, 1)[0].wait()

                acc[dd] = mm(gslots[l, m, e, :, :width], wdt[e, :, pl.ds(pl.multiple_of(c * hw, hw), hw)])

            @pl.when(valid & first[dd])
            def _():
                dh[m, e, c] = bf(acc[dd])
                dh_copy(dd, l, m, e, c).start()

            @pl.when(valid & jnp.logical_not(first[dd] | last[dd]))
            def _():
                dh_copy(dd, l, m, e, c).wait_recv()
                dh[m, e, c] = bf(acc[dd] + dh[m, e, c].astype(jnp.float32))
                dh_copy(dd, l, m, e, c).start()

            @pl.when(valid & last[dd])
            def _():
                dh_copy(dd, l, m, e, c).wait_recv()
                total = acc[dd] + dh[m, e, c].astype(jnp.float32)
                r = router_column(slots[l, m, e], e, width, experts)
                gate = gown[m, e - dd * half, c, :, :hw].astype(jnp.float32)
                upv = gown[m, e - dd * half, c, :, hw:].astype(jnp.float32)
                dgate, dup, dr = act_back(gate, upv, total, jax.nn.sigmoid(r))
                dgu[m, e, c, :, :hw] = bf(dgate)
                dgu[m, e, c, :, hw:] = bf(dup)
                dgu_copy(dd, l, m, e, c).start()
                dr = jnp.where(c == 0, 0.0, drs[dd][:, 0:1]) + dr
                drs[dd] = jnp.broadcast_to(dr, (cap, 128))
                hi = bf(dr).astype(jnp.float32)
                deo[m, e] = bf(jnp.where(lane == width + e, hi, jnp.where(lane == width + experts + e, dr - hi, 0.0)))

        for dd in range(2):
            valid, l, m, e, c = spreads[dd]

            @pl.when(valid & jnp.logical_not(last[dd]))
            def _():
                dgu_copy(dd, l, m, e, c).wait_recv()

                @pl.when(jnp.logical_not(first[dd]))
                def _():
                    dgu_copy(dd, l, m, e, c).start()

        for dd in range(2):
            valid, l, m, e, c = spreads[dd]

            @pl.when(valid & (c == 1))
            def _():
                @pl.when(m == 0)
                def _():
                    weight_copy(0, e, 0)[0].wait()

                total = None
                for c2 in range(2):
                    for plane in range(2):
                        cols, hcols = slice(plane * hw, (plane + 1) * hw), slice(c2 * hw, (c2 + 1) * hw)
                        part = mm(dgu[m, e, c2, :, cols], win[e, plane, :, hcols], ((1,), (1,)))
                        total = part if total is None else total + part
                deo[m, e, :, :width] = bf(total)

        for l in (1, 0):
            t = i - starts[3 - 2 * l] - lag
            weight_stage(l, t)

    def chain_sent(l, e, dd):
        for m in range(mbs):
            for c in range(2):
                pl.when(jnp.logical_not(last[dd]))(dh_copy(dd, l, m, e, c).wait_send)
                pl.when(jnp.logical_not(first[dd]))(dgu_copy(dd, l, m, e, c).wait_send)

    def weight_stage(l, t):
        u = t // 2
        on = (t >= 0) & (t < units) & (lax.rem(t + 2, 2) == 1)

        @pl.when(on)
        def _():
            for dd in range(2):
                chain_sent(l, jnp.clip(u, 0, half - 1) + dd * half, dd)

        @pl.when(on & (s == l))
        def _():
            pl.semaphore_signal(free.at[l], inc=1, device_id=(1 - s, a, b), device_id_type=MESH)

        @pl.when(on & (s != l))
        def _():
            pl.semaphore_wait(free.at[l], 1)
            for dd in range(2):
                e = jnp.clip(u, 0, half - 1) + dd * half
                gi, gd = weight_grads(l, e)
                for c in range(2):
                    for plane in range(2):
                        win[e, plane, :, c * hw : (c + 1) * hw] = bf(gi[c][:, plane * hw : (plane + 1) * hw])
                    wdt[e, :, c * hw : (c + 1) * hw] = bf(gd[c])
                wi_copy(l, e).start()
                wd_copy(l, e).start()

        t2 = t - 2 * late
        w = t2 // 2
        on2 = (t2 >= 0) & (t2 < units) & (lax.rem(t2 + 8, 2) == 1)

        @pl.when(on2 & (s != l))
        def _():
            for dd in range(2):
                e = jnp.clip(w, 0, half - 1) + dd * half
                wi_copy(l, e).wait_send()
                wd_copy(l, e).wait_send()
                if l:
                    start_weights(0, e)

        @pl.when(on2 & (s == l))
        def _():
            for dd in range(2):
                e = jnp.clip(w, 0, half - 1) + dd * half
                gi, gd = weight_grads(l, e)
                wi_copy(l, e).wait_recv()
                wd_copy(l, e).wait_recv()

                @pl.when((w >= 1) | (dd == 1))
                def _():
                    for copy in st_copies(e):
                        copy.wait()

                for c in range(2):
                    hcols = slice(c * hw, (c + 1) * hw)
                    for plane in range(2):
                        part = gi[c][:, plane * hw : (plane + 1) * hw] + win[e, plane, :, hcols].astype(jnp.float32)
                        sti[:, plane * f + c * hw : plane * f + (c + 1) * hw] = bf(part)
                    std[:, hcols] = bf(gd[c] + wdt[e, :, hcols].astype(jnp.float32))
                for copy in st_copies(e):
                    copy.start()
                if l:
                    start_weights(0, e)

    stages = {}

    def at(step, do, *args):
        stages.setdefault(step, []).append(lambda: do(*args))

    def shared_first(l, m):
        if m == 0:
            for copy in early_loads(l):
                copy.wait()
        shared_act(m)

    def reload(copies):
        for copy in copies:
            copy.start()

    def ready(copies):
        for copy in copies:
            copy.wait()

    ready([slots_load, gslots_load, hid_load(1)] + later_loads(1))
    for m in range(mbs):
        wait_gates(1, m)
    for l in (1, 0):
        begin = starts[2 - 2 * l]
        second = starts[3 - 2 * l]
        at(begin + 3, shared_first, l, 0)
        at(begin + 5, shared_back, 0)
        at(second + (-10 if l else 1), shared_first, l, 1)
        at(second + (-8 if l else 3), shared_back, 1)
        at(second + (-6 if l else 5), shared_grads)
        at(second + (-4 if l else 6), down_grads, l)
        at(second + (1 if l else 9), join, l, 0)
        for m in range(2):
            done = starts[2 - 2 * l + m] + units - 1 + lag
            for c, (do, *args) in enumerate((
                    (combine, l, m), (combine_line, m), (second_norm, l, m), (attention, m), (first_norm, l, m))):
                at(done + c * apart, do, *args)
            if l:
                at(starts[m] + units + sk * (ny - 1), start_gates, 0, m)
                at(done + 5 * apart, spread, m)
                at(done + 6 * apart, dispatch, 0, m)
                at(starts[2 + m] - 1, wait_gates, 0, m)
        end = second + units - 1 + lag
        at(end + 3 * apart, attention_grads, l)
        at(end + 4 * apart - (0 if l else 1), join, l, 1)
        at(end + 4 * apart, small_grads, l)
        at(end + 5 * apart, join, l, 2)
        at(end + (2 if l else 4) * apart, settle, l, 0)
        at(end + (10 if l else 5) * apart, settle, l, 2)
        if l:
            at(end + 10 * apart, settle, l, 1)
            at(end + 6 * apart, given, l)
    at(units // 2 - 1, send_out, 0, 0)
    at(units // 2 + 1, send_out, 0, 1)
    at(2 * units, take_out, 0)
    end = starts[1] + units - 1 + lag
    at(end + 4 * apart + 1, send_out, 1, 1)
    at(starts[3] + units - 1 + lag + 4 * apart, send_out, 1, 0)
    at(starts[1] + 1, lambda: reload(early_loads(0)))
    at(end + 2 * late + 1, lambda: reload([hid_load(0)]))
    at(end + 2 * late + 8, lambda: ready([hid_load(0)]))
    at(end + 5 * apart, lambda: reload(later_loads(0)))
    at(end + 10 * apart, lambda: ready(later_loads(0)))
    at(end + 10 * apart, new_layer, 0)

    def step(i, c):
        chain(i)
        for when in sorted(stages):
            if when < steps:
                @pl.when(i == when)
                def _():
                    for do in stages[when]:
                        do()

        return c

    lax.fori_loop(0, steps, step, 0)
    for when in sorted(stages):
        if when >= steps:
            for do in stages[when]:
                do()

    def copy_a(ai, slot):
        return remote(small_f, small_a.at[slot], a_send.at[ai], a_recv.at[slot], (s, ai, b))

    def gain_sums():
        pos.peers(lambda ai: copy_a(ai, a).start())
        small_a[a] = small_f[...]
        pos.peers(lambda ai: copy_a(ai, ai).wait())
        total = small_a[0]
        for ai in range(1, nx):
            total = total + small_a[ai]
        small_f[...] = total

    gain_sums()
    pltpu.make_async_copy(small_f, small_g, f_sem.at[2]).start()
    take_out(1)
    for l in range(2):
        for kind in range(2):
            sent_out(kind, l)
    settle(0, 1)
    given(0)
    for i in range(3):
        pltpu.make_async_copy(finals[i], results[i], f_sem.at[i]).wait()
    for copy in st_copies(experts - 1):
        copy.wait()


def backward(fwd, cos, sin, rot, win, wdt, dims, heads, features, ids):
    width, pw, experts, cap = dims
    nx, ny = lax.axis_size("gx"), lax.axis_size("gy")
    mbs, sub, d = fwd["tok"].shape[-3:]
    f = wdt.shape[-1]
    length, tokens, slots = nx * sub, nx * ny * sub, experts * cap
    b16, f32 = jnp.bfloat16, jnp.float32
    vm = pl.BlockSpec(memory_space=pltpu.VMEM)
    hbm = pl.BlockSpec(memory_space=pl.ANY)
    ac, sc, n, half = 6 * 128, fwd["shw"].shape[3], fwd["small"].shape[1], experts // 2
    rows_shape = (mbs, nx, sub, d)
    dense = lambda c: ((ny, width, c), b16)
    scratch = (
        (win.shape, b16), (wdt.shape, b16),
        ((mbs, ny, sub, pw), b16), ((mbs, ny, sub, pw), b16), ((mbs, ny, nx, sub, pw), b16), (rows_shape, b16),
        ((slots, tokens), b16), ((tokens // 2, slots), b16),
        ((2, mbs, experts, cap, pw), b16), ((2, mbs, experts, cap, pw), b16), ((mbs, half, 2, cap, f), b16),
        ((mbs, experts, 2, cap, f // 2), b16), ((2, cap, f // 2), f32), ((mbs, experts, 2, cap, f // 2), b16),
        ((mbs, experts, 2, cap, f), b16), ((mbs, experts, cap, pw), b16),
        ((width, 2 * f), b16), ((width, f), b16),
        ((mbs, length, 2 * f), b16), (rows_shape, b16), (rows_shape, b16),
        ((mbs, nx, ny, sub, pw), b16), ((mbs, nx, ny, sub, pw), b16), ((mbs, ny, sub, pw), b16), ((mbs, ny, sub, pw), b16),
        ((pw, d), b16), ((mbs, sub, d), f32), ((mbs, sub, d), b16), (rows_shape, b16),
        ((length, pw), b16), ((mbs, length, 3 * pw), b16), (rows_shape, b16), (rows_shape, b16),
        ((experts, d), f32), ((8, d), f32), ((2, cap, 128), f32),
        dense(sc), dense(ac), ((n, d), f32), dense(sc), dense(ac), ((n, d), f32),
        ((ny - 1, width, sc), b16), ((ny - 1, width, ac), b16), ((ny - 1, n, pw), f32),
        ((width, sc), f32), ((width, ac), f32), ((n, pw), f32), ((nx, n, pw), f32),
        ((2, mbs, sub, d), b16), ((2, 2, nx, mbs, sub, pw), b16),
        ((mbs, sub, d), b16), ((2, mbs, sub, d), b16),
        *((fwd[name].shape, fwd[name].dtype) for name in ("small", "place")),
        ((mbs, sub, d), b16),
        *((fwd[name].shape[1:], fwd[name].dtype) for name in (
            "mid", "n2", "rows", "q", "k", "v", "att", "rows2", "sgu", "shid", "shw")),
        (fwd["watt0"].shape, b16),
    )
    by_m = lambda c: flags((mbs, c))
    by_half = flags((2, mbs, experts, 2))
    names = ("tok", "small", "place", "y", "mid", "n2", "rows", "q", "k", "v", "att", "rows2", "sgu", "shid",
             "shw", "watt0", "watt1")
    outs = pl.pallas_call(
        functools.partial(
            backward_kernel, (nx, ny, mbs, sub, width, pw, heads, features, experts, cap, f, *BWD_SKEW)),
        out_shape=(
            jax.ShapeDtypeStruct((2, 2 * mbs, length, pw), b16),
            jax.ShapeDtypeStruct((experts, width, 2 * f), b16),
            jax.ShapeDtypeStruct((experts, width, f), b16),
            jax.ShapeDtypeStruct((width, ac), f32),
            jax.ShapeDtypeStruct((width, sc), f32),
            jax.ShapeDtypeStruct((n, pw), f32),
        ),
        in_specs=[hbm] * 17 + [vm] * 3 + [hbm] * 8,
        out_specs=(vm,) + (hbm,) * 5,
        scratch_shapes=[pltpu.VMEM(*v) for v in scratch] + [
            flags((2, experts)), by_m(ny), by_m(ny), by_m(nx), by_m(nx), by_m(nx), by_m(nx), by_m(nx), by_m(nx),
            by_m(nx), by_m(nx), by_m(ny), by_m(ny), by_m(nx), by_m(nx), by_m(nx), by_m(nx),
            by_half, by_half, by_half, by_half,
            flags((2, experts)), flags((2, experts)), flags((2, experts)), flags((2, experts)),
            flags((3,)), flags((3,)), flags((3, ny)), flags((3, ny)), flags((nx,)), flags((nx,)),
            flags((5,)), flags((2,)), flags((3,)), flags((20,)), flags((2, 2, ny)), flags((2, 2, nx)), pltpu.SemaphoreType.REGULAR((2,)),
        ],
        compiler_params=params(ids),
        cost_estimate=pl.CostEstimate(flops=2 * 10**10, bytes_accessed=10**8, transcendentals=10**6),
        name="backward",
    )(*(fwd[name] for name in names), cos, sin, rot, *(fwd[name] for name in ("slots", "gu", "hid", "gslots")), win, fwd["win"], wdt, fwd["wdt"])
    return outs[0], outs[1:]


BWD_SKEW = (2, 2)


def fast_device(block_input, output_grad, attention_gain, attention_in, attention_out, feed_gain,
                router_weight, expert_in, expert_down, shared_in, shared_down, routes):
    s = lax.axis_index("section")
    ny = lax.axis_size("gy")
    nx = lax.axis_size("gx")
    mbs = block_input.shape[0] // 2
    width = block_input.shape[2]
    features = width * ny
    experts = expert_in.shape[1]
    f = expert_in.shape[-1]
    pw = lanes_up(width + 2 * experts)
    tokens = routes.shape[2]
    cap = 5 * tokens // (2 * experts)
    length = tokens // ny
    heads = attention_in.shape[-1] // DH
    dims = (width, pw, experts, cap)

    att_block = jnp.concatenate([
        pad_to(attention_in[0], 2, pw).reshape(width, 3 * pw), pad_to(attention_out[0].T, 1, pw)], 1)
    sh_block = jnp.concatenate([shared_in[0].reshape(width, 2 * f), shared_down[0].T], 1)
    small = jnp.concatenate([
        router_weight[0].T.astype(jnp.float32), feed_gain, attention_gain, jnp.zeros((6, width), jnp.float32)], 0)
    tin = lax.dynamic_slice_in_dim(jnp.stack([block_input, output_grad]), s * mbs, mbs, 1)
    tin = pad_to(tin, 3, pw)
    small = pad_to(small, 1, pw)
    win = jnp.swapaxes(expert_in[0], 1, 2)
    wdt = expert_down[0].transpose(0, 2, 1)
    pairs = jnp.swapaxes(routes[0], 1, 2)
    half = DH // 2
    freq = 10000.0 ** (-np.arange(half, dtype=np.float64) / half)
    lanes = np.tile(np.arange(length)[:, None] * freq[None], (1, 2 * heads))
    cos = np.zeros((length, pw), np.float32)
    sin = np.zeros((length, pw), np.float32)
    cos[:, : heads * DH] = np.cos(lanes)
    sin[:, : heads * DH] = np.sin(lanes)
    rot = np.zeros((pw, pw), np.float32)
    for lead in range(0, heads * DH, DH):
        at = lead + np.arange(half)
        rot[at + half, at] = -1.0
        rot[at, at + half] = 1.0
    cos, sin, rot = jnp.asarray(cos), jnp.asarray(sin), jnp.asarray(rot, jnp.bfloat16)

    fwd = forward(tin, small, att_block, sh_block, pairs, cos, sin, rot, win, wdt, dims, heads, features, 0)
    both, grads = backward(fwd, cos, sin, rot, win, wdt, dims, heads, features, 1)
    win_g, wdt_g, att_g, sh_g, small_g = grads
    win_g, wdt_g, y, gx, ain, aout, sin_g, sdn, gain_g, fgain_g, rw = finish_outputs(
        win_g, wdt_g, both, att_g, sh_g, small_g, pw, heads * DH)
    return (
        jnp.swapaxes(y, 1, 2)[None],
        jnp.swapaxes(gx, 1, 2)[None],
        gain_g,
        jnp.swapaxes(ain, 0, 1)[None],
        aout[None],
        fgain_g,
        rw.T[None],
        win_g[None],
        jnp.swapaxes(wdt_g, 1, 2)[None],
        sin_g[None],
        sdn.T[None],
    )


def any_device(*arrays):
    block_input, attention_in, routes = arrays[0], arrays[3], arrays[-1]
    batches, rows, width = block_input.shape
    fits = (
        lax.axis_size("gx") == lax.axis_size("gy")
        and lax.axis_size("section") == 2
        and batches == 4
        and rows == 128
        and routes.shape[2] == rows * lax.axis_size("gy")
        and 128 < width <= 192
        and attention_in.shape[-1] == width
        and lanes_up(width + 2 * arrays[7].shape[1]) == 256
    )
    return fast_device(*arrays) if fits else on_device(*arrays)


def solution(mesh):
    in_specs = (
        P(None, "gx", "gy"),
        P(None, "gx", "gy"),
        P("section", "gy"),
        P("section", "gy", None, "gx"),
        P("section", "gx", "gy"),
        P("section", "gy"),
        P("section", "gy", None),
        P("section", None, "gy", None, "gx"),
        P("section", None, "gx", "gy"),
        P("section", "gy", None, "gx"),
        P("section", "gx", "gy"),
        P("section", None, None, None),
    )
    out_specs = (
        P("section", None, "gx", "gy"),
        P("section", None, "gx", "gy"),
        P("section", "gy"),
        P("section", "gy", None, "gx"),
        P("section", "gx", "gy"),
        P("section", "gy"),
        P("section", "gy", None),
        P("section", None, "gy", None, "gx"),
        P("section", None, "gx", "gy"),
        P("section", "gy", None, "gx"),
        P("section", "gx", "gy"),
    )
    return jax.shard_map(
        any_device, mesh=mesh, in_specs=in_specs, out_specs=out_specs, check_vma=False
    )
```

```python
import functools

import jax
import jax.numpy as jnp
import numpy as np
from jax import lax
from jax.experimental import pallas as pl
from jax.experimental.pallas import tpu as pltpu
from jax.sharding import PartitionSpec as P

DH = 64


epsilon = 1e-06
highest = lax.Precision.HIGHEST


def from_partner(array, axis, apart):
    return lax.ppermute(array, axis, [(i, i ^ 1 << apart) for i in range(lax.axis_size(axis))])


def token_rows(values):
    return lax.all_gather(values, "gx", axis=0, tiled=True)


def output_rows(values):
    return lax.psum_scatter(values, "gx", scatter_dimension=0, tiled=True)


def width_sum(values):
    return lax.psum(values, "gy")


def pass_section(values):
    return from_partner(values, "section", 0)


def sequence_sums(values):
    return lax.psum_scatter(values, "gy", scatter_dimension=0, tiled=True)


def sequence_rows(values):
    return lax.all_gather(values, "gy", axis=0, tiled=True)


def gather_hidden(hidden, shared_hidden):
    return (
        lax.all_gather(hidden, "gy", axis=0, tiled=True),
        lax.all_gather(shared_hidden, "gy", axis=0, tiled=True),
    )


def rope_turn(values, positions, turn_sign):
    half_size = values.shape[-1] // 2
    frequency = 10000.0 ** (-jnp.arange(half_size, dtype=jnp.float32) / half_size)
    angles = positions[:, None] * frequency[None, :]
    cosine = jnp.cos(angles)[:, None, :]
    sine_part = turn_sign * jnp.sin(angles)[:, None, :]
    first_half = values[..., :half_size]
    second_half = values[..., half_size:]
    return jnp.concatenate(
        [
            first_half * cosine - second_half * sine_part,
            first_half * sine_part + second_half * cosine,
        ],
        axis=-1,
    )


def norm_forward(stream, gain):
    full_width = stream.shape[1] * lax.axis_size("gy")
    square_sum = width_sum(jnp.sum(stream * stream, axis=1))
    inverse_rms = lax.rsqrt(square_sum / full_width + epsilon)
    return ((stream * inverse_rms[:, None] * gain[None, :]).astype(jnp.bfloat16), inverse_rms)


def norm_backward(stream, inverse_rms, gain, grad_normed):
    full_width = stream.shape[1] * lax.axis_size("gy")
    scaled = grad_normed * gain[None, :]
    inner_sum = width_sum(jnp.sum(scaled * stream, axis=1))
    cubed = inverse_rms * inverse_rms * inverse_rms
    grad_stream = inverse_rms[:, None] * scaled - stream * (cubed * inner_sum / full_width)[:, None]
    grad_gain = jnp.sum(grad_normed * stream * inverse_rms[:, None], axis=0)
    return (grad_stream, grad_gain)


def slot_table(route_ids, experts, capacity):
    flat_ids = route_ids.reshape(-1)
    assigned = (flat_ids[:, None] == jnp.arange(experts, dtype=jnp.int32)[None, :]).astype(
        jnp.int32
    )
    earlier = jnp.cumsum(assigned, axis=0) - assigned
    places = flat_ids * capacity + jnp.sum(earlier * assigned, axis=1)
    owners = jnp.arange(flat_ids.shape[0], dtype=jnp.int32) // 2
    slot_token = jnp.zeros((experts * capacity,), jnp.int32).at[places].set(owners)
    slot_valid = jnp.zeros((experts * capacity,), jnp.int32).at[places].set(jnp.ones_like(owners))
    return (places.reshape(-1, 2), slot_token, slot_valid)


def expert_act(gate_up, logits):
    half_size = gate_up.shape[1] // 2
    return (
        jax.nn.silu(gate_up[:, :half_size])
        * gate_up[:, half_size:]
        * jax.nn.sigmoid(logits)[:, None]
    )


def shared_act(gate_up):
    half_size = gate_up.shape[1] // 2
    return jax.nn.silu(gate_up[:, :half_size]) * gate_up[:, half_size:]


def causal_scores(queries, keys_part):
    score_scale = queries.shape[-1] ** (-0.5)
    scores = (
        jnp.einsum("qhd,khd->hqk", queries, keys_part, preferred_element_type=jnp.float32)
        * score_scale
    )
    length = queries.shape[0]
    causal = jnp.arange(length)[:, None] >= jnp.arange(length)[None, :]
    return jnp.where(causal[None], scores, -1e30)


def attend_forward(queries, keys_part, values_part):
    scores = causal_scores(queries, keys_part)
    row_max = jnp.max(scores, axis=-1, keepdims=True)
    exponent = jnp.exp(scores - row_max)
    row_total = jnp.sum(exponent, axis=-1, keepdims=True)
    probabilities = (exponent / row_total).astype(jnp.bfloat16)
    attended = jnp.einsum(
        "hqk,khd->qhd", probabilities, values_part, preferred_element_type=jnp.float32
    )
    return (attended, row_max + jnp.log(row_total))


def attend_backward(queries, keys_part, values_part, log_total, grad_attended):
    score_scale = queries.shape[-1] ** (-0.5)
    probabilities = jnp.exp(causal_scores(queries, keys_part) - log_total)
    grad_values = jnp.einsum(
        "hqk,qhd->khd",
        probabilities.astype(jnp.bfloat16),
        grad_attended,
        preferred_element_type=jnp.float32,
    )
    grad_probs = jnp.einsum(
        "qhd,khd->hqk", grad_attended, values_part, preferred_element_type=jnp.float32
    )
    grad_scores = (
        probabilities * (grad_probs - jnp.sum(grad_probs * probabilities, axis=-1, keepdims=True))
    ).astype(jnp.bfloat16)
    grad_queries = (
        jnp.einsum("hqk,khd->qhd", grad_scores, keys_part, preferred_element_type=jnp.float32)
        * score_scale
    )
    grad_keys = (
        jnp.einsum("hqk,qhd->khd", grad_scores, queries, preferred_element_type=jnp.float32)
        * score_scale
    )
    return (grad_queries, grad_keys, grad_values)


def layer_forward(stream, weights, route_ids):
    (
        attention_gain,
        attention_in,
        attention_out,
        feed_gain,
        router_weight,
        expert_in,
        expert_down,
        shared_in,
        shared_down,
    ) = weights
    local_width = stream.shape[1]
    experts = expert_in.shape[0]
    normed, inverse_first = norm_forward(stream, attention_gain)
    rows_first = token_rows(normed)
    tokens = rows_first.shape[0]
    capacity = 5 * tokens // (2 * experts)
    slot_count = experts * capacity
    projected = sequence_sums(
        jnp.dot(
            rows_first, attention_in.reshape(local_width, -1), preferred_element_type=jnp.float32
        )
    )
    length = projected.shape[0]
    projected = projected.reshape(length, 3, -1, DH)
    positions = jnp.arange(length, dtype=jnp.float32)
    queries = rope_turn(projected[:, 0], positions, 1.0).astype(jnp.bfloat16)
    keys_part = rope_turn(projected[:, 1], positions, 1.0).astype(jnp.bfloat16)
    values_part = projected[:, 2].astype(jnp.bfloat16)
    attended, log_total = attend_forward(queries, keys_part, values_part)
    attended_rows = sequence_rows(attended.astype(jnp.bfloat16).reshape(length, -1))
    middle = stream + output_rows(
        jnp.dot(attended_rows, attention_out, preferred_element_type=jnp.float32)
    )
    normed_feed, inverse_second = norm_forward(middle, feed_gain)
    rows_second = token_rows(normed_feed)
    route_slot, slot_token, slot_valid = slot_table(route_ids, experts, capacity)
    grouped = (rows_second[slot_token] * slot_valid[:, None].astype(jnp.bfloat16)).reshape(
        experts, capacity, local_width
    )
    expert_part = jnp.einsum(
        "ecd,edf->ecf",
        grouped,
        expert_in.reshape(experts, local_width, -1),
        preferred_element_type=jnp.float32,
    )
    router_part = jnp.einsum(
        "ecd,de->ec", grouped, router_weight, preferred_element_type=jnp.float32
    )
    shared_part = jnp.dot(
        rows_second, shared_in.reshape(local_width, -1), preferred_element_type=jnp.float32
    )
    expert_gu, router_logit, shared_gu = (
        lax.psum_scatter(
            expert_part.reshape(slot_count, -1), "gy", scatter_dimension=0, tiled=True
        ),
        lax.psum_scatter(router_part.reshape(slot_count), "gy", scatter_dimension=0, tiled=True),
        lax.psum_scatter(shared_part, "gy", scatter_dimension=0, tiled=True),
    )
    hidden_rows, shared_rows = gather_hidden(
        expert_act(expert_gu, router_logit).astype(jnp.bfloat16),
        shared_act(shared_gu).astype(jnp.bfloat16),
    )
    expert_result = jnp.einsum(
        "ecf,efd->ecd",
        hidden_rows.reshape(experts, capacity, -1),
        expert_down,
        preferred_element_type=jnp.float32,
    ).reshape(slot_count, local_width)
    branch = (
        expert_result[route_slot[:, 0]]
        + expert_result[route_slot[:, 1]]
        + jnp.dot(shared_rows, shared_down, preferred_element_type=jnp.float32)
    )
    result = middle + output_rows(branch)
    kept_items = (
        stream,
        inverse_first,
        rows_first,
        queries,
        keys_part,
        values_part,
        log_total,
        attended_rows,
        middle,
        inverse_second,
        rows_second,
        expert_gu,
        router_logit,
        shared_gu,
    )
    return (result, kept_items)


def layer_backward(grad_out, kept_items, weights, route_ids):
    (
        attention_gain,
        attention_in,
        attention_out,
        feed_gain,
        router_weight,
        expert_in,
        expert_down,
        shared_in,
        shared_down,
    ) = weights
    (
        stream,
        inverse_first,
        rows_first,
        queries,
        keys_part,
        values_part,
        log_total,
        attended_rows,
        middle,
        inverse_second,
        rows_second,
        expert_gu,
        router_logit,
        shared_gu,
    ) = kept_items[:14]
    local_width = stream.shape[1]
    experts = expert_in.shape[0]
    tokens = rows_second.shape[0]
    capacity = 5 * tokens // (2 * experts)
    slot_count = experts * capacity
    hidden_rows, shared_rows = gather_hidden(
        expert_act(expert_gu, router_logit).astype(jnp.bfloat16),
        shared_act(shared_gu).astype(jnp.bfloat16),
    )
    route_slot, slot_token, slot_valid = slot_table(route_ids, experts, capacity)
    valid_rows = slot_valid[:, None].astype(jnp.bfloat16)
    grouped = (rows_second[slot_token] * valid_rows).reshape(experts, capacity, local_width)
    grad_rows = token_rows(grad_out.astype(jnp.bfloat16))
    slot_grad = (grad_rows[slot_token] * valid_rows).reshape(experts, capacity, local_width)
    down_grad = jnp.einsum(
        "ecf,ecd->efd",
        hidden_rows.reshape(experts, capacity, -1),
        slot_grad,
        preferred_element_type=jnp.float32,
    )
    shared_down_grad = jnp.einsum(
        "tf,td->fd", shared_rows, grad_rows, preferred_element_type=jnp.float32
    )
    hidden_part = jnp.einsum(
        "ecd,efd->ecf", slot_grad, expert_down, preferred_element_type=jnp.float32
    ).reshape(slot_count, -1)
    shared_part = jnp.einsum(
        "td,fd->tf", grad_rows, shared_down, preferred_element_type=jnp.float32
    )
    grad_hidden, grad_shared = (
        lax.psum_scatter(
            hidden_part.astype(jnp.bfloat16), "gy", scatter_dimension=0, tiled=True
        ).astype(jnp.float32),
        lax.psum_scatter(
            shared_part.astype(jnp.bfloat16), "gy", scatter_dimension=0, tiled=True
        ).astype(jnp.float32),
    )
    unused_expert, expert_back = jax.vjp(expert_act, expert_gu, router_logit)
    grad_gu, grad_logit = expert_back(grad_hidden)
    unused_shared, shared_back = jax.vjp(shared_act, shared_gu)
    (grad_shared_gu,) = shared_back(grad_shared)
    gu_rows, shared_gu_rows = (
        lax.all_gather(grad_gu.astype(jnp.bfloat16), "gy", axis=0, tiled=True),
        lax.all_gather(grad_shared_gu.astype(jnp.bfloat16), "gy", axis=0, tiled=True),
    )
    logit_rows = lax.all_gather(grad_logit, "gy", axis=0, tiled=True).reshape(experts, capacity)
    gu_grouped = gu_rows.reshape(experts, capacity, -1)
    in_grad = jnp.einsum("ecd,ecf->edf", grouped, gu_grouped, preferred_element_type=jnp.float32)
    router_grad = jnp.einsum(
        "ecd,ec->de", grouped.astype(jnp.float32), logit_rows, precision=highest
    )
    shared_in_grad = jnp.einsum(
        "td,tf->df", rows_second, shared_gu_rows, preferred_element_type=jnp.float32
    )
    slot_back = jnp.einsum(
        "ecf,edf->ecd",
        gu_grouped,
        expert_in.reshape(experts, local_width, -1),
        preferred_element_type=jnp.float32,
    )
    slot_back = slot_back + logit_rows[:, :, None] * router_weight.T.astype(jnp.float32)[:, None, :]
    slot_back = slot_back.reshape(slot_count, local_width)
    rows_back = (
        slot_back[route_slot[:, 0]]
        + slot_back[route_slot[:, 1]]
        + jnp.einsum(
            "tf,df->td",
            shared_gu_rows,
            shared_in.reshape(local_width, -1),
            preferred_element_type=jnp.float32,
        )
    )
    grad_middle_norm, feed_gain_grad = norm_backward(
        middle, inverse_second, feed_gain, output_rows(rows_back)
    )
    grad_middle = grad_out + grad_middle_norm
    middle_rows = token_rows(grad_middle.astype(jnp.bfloat16))
    out_weight_grad = jnp.einsum(
        "tf,td->fd", attended_rows, middle_rows, preferred_element_type=jnp.float32
    )
    grad_attended = sequence_sums(
        jnp.einsum("td,fd->tf", middle_rows, attention_out, preferred_element_type=jnp.float32)
    )
    length = grad_attended.shape[0]
    positions = jnp.arange(length, dtype=jnp.float32)
    grad_queries, grad_keys, grad_values = attend_backward(
        queries,
        keys_part,
        values_part,
        log_total,
        grad_attended.astype(jnp.bfloat16).reshape(queries.shape),
    )
    grad_projected = jnp.stack(
        [
            rope_turn(grad_queries, positions, -1.0),
            rope_turn(grad_keys, positions, -1.0),
            grad_values,
        ],
        axis=1,
    )
    grad_projected = grad_projected.astype(jnp.bfloat16).reshape(length, -1)
    projected_rows = sequence_rows(grad_projected)
    in_weight_grad = jnp.einsum(
        "td,tf->df", rows_first, projected_rows, preferred_element_type=jnp.float32
    )
    grad_normed = output_rows(
        jnp.einsum(
            "tf,df->td",
            projected_rows,
            attention_in.reshape(local_width, -1),
            preferred_element_type=jnp.float32,
        )
    )
    grad_stream_norm, attention_gain_grad = norm_backward(
        stream, inverse_first, attention_gain, grad_normed
    )
    layer_grads = (
        attention_gain_grad,
        in_weight_grad.reshape(attention_in.shape),
        out_weight_grad,
        feed_gain_grad,
        router_grad,
        in_grad.reshape(expert_in.shape),
        down_grad,
        shared_in_grad.reshape(shared_in.shape),
        shared_down_grad,
    )
    return (grad_middle + grad_stream_norm, layer_grads)


def put_item(buffer, value, batch_index, is_valid):
    current = lax.dynamic_index_in_dim(buffer, batch_index, 0, keepdims=False)
    return lax.dynamic_update_index_in_dim(
        buffer, jnp.where(is_valid, value, current), batch_index, 0
    )


def on_device(
    block_input,
    output_grad,
    attention_gain,
    attention_in,
    attention_out,
    feed_gain,
    router_weight,
    expert_in,
    expert_down,
    shared_in,
    shared_down,
    routes,
):
    section_index = lax.axis_index("section")
    batches = block_input.shape[0]
    weights = tuple(
        (
            member[0]
            for member in (
                attention_gain,
                attention_in,
                attention_out,
                feed_gain,
                router_weight,
                expert_in,
                expert_down,
                shared_in,
                shared_down,
            )
        )
    )
    route_table = routes[0]
    outputs = jnp.zeros(block_input.shape, jnp.bfloat16)
    received = jnp.zeros(block_input.shape[1:], jnp.bfloat16)
    stored = None
    for tick_step in range(batches + 1):
        micro_index = tick_step - section_index
        is_valid = (micro_index >= 0) & (micro_index < batches)
        batch_index = jnp.clip(micro_index, 0, batches - 1)
        fresh_input = lax.dynamic_index_in_dim(block_input, batch_index, 0, keepdims=False)
        incoming = jnp.where(section_index == 0, fresh_input, received).astype(jnp.float32)
        route_ids = lax.dynamic_index_in_dim(route_table, batch_index, 0, keepdims=False)
        result, kept_items = layer_forward(incoming, weights, route_ids)
        result_low = result.astype(jnp.bfloat16)
        outputs = put_item(outputs, result_low, batch_index, is_valid)
        if stored is None:
            stored = tuple(
                (jnp.zeros((batches,) + member.shape, member.dtype) for member in kept_items)
            )
        stored = tuple(
            (
                put_item(buffer, member, batch_index, is_valid)
                for buffer, member in zip(stored, kept_items)
            )
        )
        if tick_step < batches:
            received = pass_section(result_low)
    grads_in = jnp.zeros(block_input.shape, jnp.bfloat16)
    received = jnp.zeros(block_input.shape[1:], jnp.bfloat16)
    totals = tuple((jnp.zeros(member.shape, jnp.float32) for member in weights))
    for tick_step in range(batches + 1):
        micro_index = batches - tick_step - section_index
        is_valid = (micro_index >= 0) & (micro_index < batches)
        batch_index = jnp.clip(micro_index, 0, batches - 1)
        given_grad = lax.dynamic_index_in_dim(output_grad, batch_index, 0, keepdims=False)
        incoming = jnp.where(section_index == 1, given_grad, received).astype(jnp.float32)
        kept_items = tuple(
            (lax.dynamic_index_in_dim(buffer, batch_index, 0, keepdims=False) for buffer in stored)
        )
        route_ids = lax.dynamic_index_in_dim(route_table, batch_index, 0, keepdims=False)
        grad_input, layer_grads = layer_backward(incoming, kept_items, weights, route_ids)
        grad_low = grad_input.astype(jnp.bfloat16)
        grads_in = put_item(grads_in, grad_low, batch_index, is_valid)
        totals = tuple(
            (total + jnp.where(is_valid, member, 0.0) for total, member in zip(totals, layer_grads))
        )
        if tick_step < batches:
            received = pass_section(grad_low)
    gain_first, gain_second, router_total = lax.psum((totals[0], totals[3], totals[4]), "gx")
    return (
        outputs[None],
        grads_in[None],
        gain_first[None],
        totals[1][None],
        totals[2][None],
        gain_second[None],
        router_total[None],
        totals[5][None],
        totals[6][None],
        totals[7][None],
        totals[8][None],
    )


def lanes_up(n):
    return -(-n // 128) * 128


def rot_columns(w):
    shape = w.shape
    w = w.reshape(shape[:-1] + (-1, 2, DH // 2))
    w = jnp.stack([-w[..., 1, :], w[..., 0, :]], axis=-2)
    return w.reshape(shape)


def pad_to(v, axis, n):
    pads = [(0, 0)] * v.ndim
    pads[axis] = (0, n - v.shape[axis])
    return jnp.pad(v, pads)


def mm(a, b, dims=((1,), (0,))):
    return lax.dot_general(a, b, (dims, ((), ())), preferred_element_type=jnp.float32)


def bf(v):
    return v.astype(jnp.bfloat16)


def head_mask(pw, h):
    lane = lax.broadcasted_iota(jnp.int32, (1, pw), 1)
    return (lane >= h * DH) & (lane < (h + 1) * DH)


def rms(x, features):
    return lax.rsqrt(jnp.sum(x * x, axis=1, keepdims=True) / features + epsilon)


def norm_back(x, inv, gain, d, features):
    u = d * gain
    inner = jnp.sum(u * x, axis=1, keepdims=True) / features
    dx = inv * u - x * (inv * inv * inv * inner)
    return dx, jnp.sum(d * x * inv, axis=0, keepdims=True)


def probs_of(q, k):
    s = mm(q, k, ((1,), (1,))) * DH ** -0.5
    n = s.shape[0]
    causal = lax.broadcasted_iota(jnp.int32, (n, n), 0) >= lax.broadcasted_iota(jnp.int32, (n, n), 1)
    s = jnp.where(causal, s, -1e30)
    e = jnp.exp(s - jnp.max(s, axis=1, keepdims=True))
    return e / jnp.sum(e, axis=1, keepdims=True)


def act_back(gate, up, dh, s):
    sg = jax.nn.sigmoid(gate)
    silu = gate * sg
    if s is None:
        return dh * up * (sg * (1.0 + gate * (1.0 - sg))), dh * silu, None
    dr = jnp.sum(dh * silu * up, axis=-1, keepdims=True) * s * (1.0 - s)
    ds = dh * s
    return ds * up * (sg * (1.0 + gate * (1.0 - sg))), ds * silu, dr


MESH = pl.DeviceIdType.MESH
VMEM_BYTES = 62 * 2**20


def remote(src, dst, send, recv, target):
    return pltpu.make_async_remote_copy(
        src_ref=src, dst_ref=dst, send_sem=send, recv_sem=recv, device_id=target, device_id_type=MESH
    )


def router_column(rows, e, width, experts):
    lane = lax.broadcasted_iota(jnp.int32, rows.shape, rows.ndim - 1)
    mask = (lane == width + e) | (lane == width + experts + e)
    return jnp.sum(jnp.where(mask, rows.astype(jnp.float32), 0.0), axis=-1, keepdims=True)


class Position:
    def __init__(self, nx, ny):
        self.s = lax.axis_index("section")
        self.a = lax.axis_index("gx")
        self.b = lax.axis_index("gy")
        self.nx, self.ny = nx, ny
        self.n = nx * ny
        self.me = self.a * ny + self.b

    def device(self, index):
        return (self.s, index // self.ny, lax.rem(index, self.ny))

    def others(self, do):
        def step(i, c):
            index = lax.rem(self.me + i, self.n)
            do(index, index // self.ny, lax.rem(index, self.ny))
            return c

        lax.fori_loop(1, self.n, step, 0)

    def peers(self, do):
        for i in range(1, self.nx):
            do(lax.rem(self.a + i, self.nx))

    def line(self, do):
        for i in range(1, self.ny):
            do(lax.rem(self.b + i, self.ny))


def greet_section(pos):
    barrier = pltpu.get_barrier_semaphore()

    def one(index, ai, bi):
        pl.semaphore_signal(barrier, inc=1, device_id=(pos.s, ai, bi), device_id_type=MESH)

    pos.others(one)
    return barrier


def flags(count):
    return pltpu.SemaphoreType.DMA(count)


class Share:
    def __init__(self, pos, layer, block, full, sems, cols=None):
        if cols is None:
            cols = pl.ds(0, block.shape[1])
        self.pos, self.layer, self.cols = pos, layer, cols
        self.block, self.full = block.at[:, cols], full.at[:, :, cols]
        self.sems = sems
        self.source = pos.s == layer

    def along(self, way, h):
        pos = self.pos
        j = pos.b - way * h
        to = pos.b + way
        real = (j >= 0) & (j < pos.ny) & (to >= 0) & (to < pos.ny)
        j = jnp.clip(j, 0, pos.ny - 1)
        src = self.block if h == 0 else self.full.at[j]
        copy = remote(src, self.full.at[j], self.sems[0].at[(way + 1) // 2, h], self.sems[1].at[j], (pos.s, pos.a, to))
        return real, j, copy

    def across(self, src, slot):
        pos = self.pos
        return remote(src, self.full.at[slot], self.sems[2].at[slot], self.sems[3].at[slot], (1 - pos.s, pos.a, pos.b))

    def start(self):
        b = self.pos.b

        @pl.when(self.source)
        def _():
            self.full[b] = self.block[...]
            for way in (-1, 1):
                real, _, copy = self.along(way, 0)
                pl.when(real)(copy.start)
            self.across(self.block, b).start()

    def hop(self, h):
        pos = self.pos

        @pl.when(self.source)
        def _():
            for way in (-1, 1):
                j = pos.b - way * h

                @pl.when((j >= 0) & (j < pos.ny))
                def _():
                    real, jc, copy = self.along(way, h)
                    copy.wait_recv()
                    pl.when(real)(copy.start)
                    self.across(self.full.at[jc], jc).start()

    def finish(self):
        pos = self.pos

        @pl.when(self.source)
        def _():
            for h in range(pos.ny - 1):
                for way in (-1, 1):
                    real, _, copy = self.along(way, h)
                    pl.when(real)(copy.wait_send)
            for j in range(pos.ny):
                self.across(self.block, j).wait_send()

        @pl.when(jnp.logical_not(self.source))
        def _():
            for j in range(pos.ny):
                self.across(self.full.at[j], j).wait_recv()


def share_sems(ny):
    return [flags((2, ny)), flags((ny,)), flags((ny,)), flags((ny,))]


def params(ids):
    return pltpu.CompilerParams(collective_id=ids, has_side_effects=True, vmem_limit_bytes=VMEM_BYTES)


def turn(t, cos, sin, rot, sign):
    hi = bf(t)
    lo = bf(t - hi.astype(jnp.float32))
    return bf(t * cos + sign * ((mm(hi, rot) + mm(lo, rot)) * sin))


def by_blocks(rows, full, cols, width, pw):
    total = None
    for j in range(full.shape[0]):
        part = mm(rows[:, j * pw : j * pw + width], full[j, :, cols])
        total = part if total is None else total + part
    return total


def finish_kernel(cfg, win, wdt, both, att, sh, small, win_o, wdt_o, y_o, gx_o, ain_o, aout_o, sin_o, sdn_o, gain_o, fgain_o, rw_o):
    width, pw, hd, experts = cfg
    f = wdt.shape[-1]
    value = win[0].astype(jnp.float32)
    win_o[0, :, 0, :] = value[:, :f]
    win_o[0, :, 1, :] = value[:, f:]
    wdt_o[0] = wdt[0].astype(jnp.float32)

    @pl.when(pl.program_id(0) == 0)
    def _():
        for kind, dst in enumerate((y_o, gx_o)):
            for m in range(both.shape[1]):
                dst[m] = both[kind, m].astype(jnp.float32).T[:width].astype(dst.dtype)
        lane = lax.broadcasted_iota(jnp.int32, (width, 128), 1)
        parts = []
        for c in range(4):
            pair = att[:, (4 + c // 2) * 128 : (5 + c // 2) * 128]
            pair = pltpu.roll(pair, 64, 1) if c % 2 else pair
            parts.append((att[:, c * 128 : (c + 1) * 128], jnp.where(lane < 64, pair, 0.0)))
        for c in range(3):
            ain_o[c, :, :128] = parts[c][0]
            ain_o[c, :, 128:] = parts[c][1][:, : hd - 128]
        square = jnp.concatenate([jnp.concatenate(parts[3], 1), jnp.zeros((pw - width, pw), jnp.float32)], 0)
        aout_o[...] = square.T[:hd, :width]
        value = sh[:, : 2 * f]
        sin_o[:, 0, :] = value[:, :f]
        sin_o[:, 1, :] = value[:, f:]
        sdn_o[...] = sh[:, 2 * f :]
        rw_o[...] = small[:experts, :width]
        fgain_o[...] = small[experts : experts + 1, :width]
        gain_o[...] = small[experts + 1 : experts + 2, :width]


def finish_outputs(win, wdt, both, att, sh, small, pw, hd):
    experts, width, f = wdt.shape
    mbs, tokens = both.shape[1:3]
    f32 = jnp.float32
    each = lambda *shape: pl.BlockSpec((1,) + shape, lambda e: (e,) + (0,) * len(shape))
    once = lambda *shape: pl.BlockSpec(shape, lambda e: (0,) * len(shape))
    shapes = (
        ((mbs, width, tokens), both.dtype), ((mbs, width, tokens), both.dtype),
        ((3, width, hd), f32), ((hd, width), f32), ((width, 2, f), f32), ((width, f), f32),
        ((1, width), f32), ((1, width), f32), ((experts, width), f32),
    )
    return pl.pallas_call(
        functools.partial(finish_kernel, (width, pw, hd, experts)),
        grid=(experts,),
        out_shape=(
            jax.ShapeDtypeStruct((experts, width, 2, f), f32),
            jax.ShapeDtypeStruct((experts, width, f), f32),
            *(jax.ShapeDtypeStruct(*v) for v in shapes),
        ),
        in_specs=[each(width, 2 * f), each(width, f)] + [once(*v.shape) for v in (both, att, sh, small)],
        out_specs=(each(width, 2, f), each(width, f), *(once(*v[0]) for v in shapes)),
        compiler_params=pltpu.CompilerParams(vmem_limit_bytes=VMEM_BYTES),
        name="finish",
    )(win, wdt, both, att, sh, small)


def forward_kernel(cfg, *refs):
    nx, ny, mbs, sub, width, pw, heads, features, experts, cap, f, sk, ak = cfg
    (tin, small_b, att_b, sh_b, routes, cos, sin, rot, win_a, wdt_a,
     win_b, wdt_b, tok_o, small_o, place_o, place_to, watt0_o, y_o, mid_o, n2_o, rows_o, q_o, k_o, v_o, att_o, slots_o, gu_o, hid_o, rows2_o, sgu_o, shid_o, shw_o, watt_o, gslots_o,
     y, mid, n2, rx, nsend, nall, proj, q, k, v, att, osend, orecv, rwx,
     xsend, xline, xall, nrows, pm, pt, slots, acc, gu, hid, eo, sgu, shid, ssend, srecv, rsend, rpeer, rline, rrecv,
     win, wdt, shw0, shw1, watt0, watt1, tbuf, tok, rts, place, place_t, sm0, sm1, small, gall, gslots,
     n_send, n_recv, o_send, o_recv, x_send, x_recv, u_send, u_recv, t_send, t_recv, s_send, s_recv, g_send, g_recv, r_send, r_recv,
     rs_send, rs_recv, ag_send, ag_recv, wi_sem, wd_sem, g_sem, k_sem, i_send, i_recv, q_send, q_recv, v_send, v_recv, gu_send, gu_recv, *w_sems) = refs
    pos = Position(nx, ny)
    s, a, b, me = pos.s, pos.a, pos.b, pos.me
    slots_n = experts * cap
    tokens = nx * ny * sub
    d = ny * pw
    length = nx * sub
    half, hw = experts // 2, f // 2
    lane = lax.broadcasted_iota(jnp.int32, (1, pw), 1)
    shares = (
        Share(pos, 0, sh_b, shw0, w_sems[0:4]),
        Share(pos, 1, att_b, watt1, w_sems[4:8]),
        Share(pos, 1, sh_b, shw1, w_sems[8:12]),
    )
    entry_shares = (
        Share(pos, 0, small_b, sm0, w_sems[12:16]),
        Share(pos, 1, small_b, sm1, w_sems[16:20]),
        Share(pos, 0, att_b, watt0, w_sems[20:24], pl.ds(0, 2 * pw)),
        Share(pos, 0, att_b, watt0, w_sems[24:28], pl.ds(2 * pw, 2 * pw)),
    )
    watts, shws = (watt0, watt1), (shw0, shw1)
    barrier = pltpu.get_barrier_semaphore()
    pos.peers(lambda ai: pl.semaphore_signal(barrier, inc=1, device_id=(s, ai, b), device_id_type=MESH))
    pos.line(lambda bi: pl.semaphore_signal(barrier, inc=1, device_id=(s, a, bi), device_id_type=MESH))
    pl.semaphore_signal(barrier, inc=1, device_id=(1 - s, a, b), device_id_type=MESH)
    for j in range(ny):
        @pl.when((a != b) | (b != j))
        def _():
            pl.semaphore_signal(barrier, inc=1, device_id=(s, b, j), device_id_type=MESH)

    def weight_copy(layer, e, which):
        own, oth, dst, sem = ((win_a, win_b, win, wi_sem), (wdt_a, wdt_b, wdt, wd_sem))[which]
        return own.at[e], oth.at[e], dst.at[e], sem.at[e]

    def start_weight(layer, e, which):
        own, oth, dst, sem = weight_copy(layer, e, which)

        @pl.when(s == layer)
        def _():
            pltpu.make_async_copy(own, dst, sem).start()

        @pl.when(s != layer)
        def _():
            pltpu.make_async_copy(oth, dst, sem).start()

    def wait_weight(layer, e, which):
        own, oth, dst, sem = weight_copy(layer, e, which)
        pltpu.make_async_copy(own, dst, sem).wait()

    def first_weights(e, c):
        start_weight(0, e, 0)
        start_weight(0, e, 1)
        return c

    def swap(c):
        src, dst = ((win_a, win_b), (wdt_a, wdt_b))[c]
        return remote(src, dst, v_send.at[c], v_recv.at[c], (1 - s, a, b))

    def weights_ready():
        for c in range(2):
            swap(c).wait()
        lax.fori_loop(0, experts, first_weights, 0)

    @pl.when(a == b)
    def _():
        pl.semaphore_wait(barrier, nx - 1 + ny - 1 + 1 + nx - 1)

    @pl.when(a != b)
    def _():
        pl.semaphore_wait(barrier, nx - 1 + ny - 1 + 1 + nx)

    def tokens_copy(i, slot, seq):
        src = tin.at[:, :, pl.ds(pl.multiple_of(i * sub, sub), sub), :]
        return remote(src, tbuf.at[slot], i_send.at[i], i_recv.at[slot], (s, i, seq))

    def token_targets(do):
        for c in range(nx):
            i = lax.rem(a + c, nx)

            @pl.when((i != a) | (a != b))
            def _():
                do(tokens_copy(i, b, a))

    def routes_copy(src, slot):
        return remote(routes.at[pl.ds(src * mbs, mbs)], rts.at[slot], q_send, q_recv, (1 - s, a, b))

    token_targets(lambda copy: copy.start())
    routes_copy(1 - s, s).start()
    for share in entry_shares:
        share.start()
    for c in range(2):
        swap(c).start()
    rts[s] = routes[pl.ds(s * mbs, mbs)]

    @pl.when(a == b)
    def _():
        tbuf[b] = tin[:, :, pl.ds(pl.multiple_of(a * sub, sub), sub), :]

    routes_copy(0, 1 - s).wait()

    def places():
        t0 = lax.broadcasted_iota(jnp.int32, (tokens, tokens), 0)
        t1 = lax.broadcasted_iota(jnp.int32, (tokens, tokens), 1)
        before = bf((t1 < t0).astype(jnp.float32))
        after = bf((t0 < t1).astype(jnp.float32))
        er = lax.broadcasted_iota(jnp.int32, (experts, tokens), 0).astype(jnp.float32)
        ec = lax.broadcasted_iota(jnp.int32, (tokens, 128), 1).astype(jnp.float32)
        sub8 = lax.broadcasted_iota(jnp.int32, (128, tokens), 0)
        for l in range(2):
            for m in range(mbs):
                r = rts[l, m].astype(jnp.float32)
                rows = [r[c : c + 1] for c in range(2)]
                hot = [(row == er).astype(jnp.float32) for row in rows]
                count = mm(bf(hot[0] + hot[1]), after)
                cols = jnp.where(sub8 == 0, rows[0], jnp.where(sub8 == 1, rows[1], 0.0)).T
                cols = [cols[:, c : c + 1] for c in range(2)]
                hot_t = [(col == ec).astype(jnp.float32) for col in cols]
                count_t = mm(before, bf(hot_t[0] + hot_t[1]))
                for c in range(2):
                    rank = jnp.sum(hot[c] * count, axis=0, keepdims=True)
                    place[l, m, c : c + 1] = (rows[c] * cap + rank).astype(jnp.int32)
                    rank_t = jnp.sum(hot_t[c] * count_t, axis=1, keepdims=True)
                    place_t[l, m, :, c : c + 1] = (cols[c] * cap + rank_t).astype(jnp.int32)

    def tokens_ready():
        for j in range(ny):
            @pl.when((a != b) | (b != j))
            def _():
                tokens_copy(a, j, j).wait_recv()

            for kind in range(2):
                tok[kind, :, :, j * pw : (j + 1) * pw] = tbuf[j, kind]
        token_targets(lambda copy: copy.wait_send())

    def stream(l, m):
        return (tok[0, m] if l == 0 else y[0, m]).astype(jnp.float32)

    def copy_n(l, m, ai, slot):
        return remote(nsend.at[l, m], nall.at[l, m, slot], n_send.at[l, m, ai], n_recv.at[l, m, slot], (s, ai, b))

    def norm_first(l, m):
        xv = stream(l, m)
        nsend[l, m] = bf(xv * rms(xv, features) * small[l, experts + 1 : experts + 2])
        pos.peers(lambda ai: copy_n(l, m, ai, a).start())
        nall[l, m, a] = nsend[l, m]

    def copy_o(l, m, ai, slot):
        return remote(osend.at[l, m, ai], orecv.at[l, m, slot], o_send.at[l, m, ai], o_recv.at[l, m, slot], (s, ai, b))

    def attention(l, m):
        watt = watts[l]
        pos.peers(lambda ai: copy_n(l, m, ai, ai).wait())
        proj[...] = by_blocks(nall[l, m].reshape(length, d), watt, slice(0, 3 * pw), width, pw)
        v[l, m] = bf(proj[:, 2 * pw : 3 * pw])
        q[l, m] = turn(proj[:, :pw], cos[...], sin[...], rot[...], 1.0)
        k[l, m] = turn(proj[:, pw : 2 * pw], cos[...], sin[...], rot[...], 1.0)
        total = jnp.zeros((length, pw), jnp.float32)
        for h in range(heads):
            mask = head_mask(pw, h)
            p = probs_of(jnp.where(mask, q[l, m], 0), k[l, m])
            total = total + mm(bf(p), jnp.where(mask, v[l, m], 0))
        att[l, m] = bf(total)
        for j in range(ny):
            part = mm(att[l, m], watt[j, :, 3 * pw : 4 * pw], ((1,), (1,)))
            osend[l, m, :, :, j * pw : j * pw + width] = bf(part).reshape(nx, sub, width)
        pos.peers(lambda ai: copy_o(l, m, ai, a).start())
        orecv[l, m, a] = osend[l, m, a]

    def copy_x(l, m, bi, slot):
        return remote(xsend.at[l, m, bi], xline.at[l, m, slot], x_send.at[l, m, bi], x_recv.at[l, m, slot], (s, a, bi))

    def copy_w(l, m, ai, slot):
        return remote(xline.at[l, m], xall.at[l, m, :, slot], u_send.at[l, m, ai], u_recv.at[l, m, slot], (s, ai, b))

    def copy_t(l, m, ai, slot):
        return remote(n2.at[l, m], nrows.at[l, m, slot], t_send.at[l, m, ai], t_recv.at[l, m, slot], (s, ai, b))

    def norm_second(l, m):
        pos.peers(lambda ai: copy_o(l, m, ai, ai).wait())
        mv = stream(l, m)
        for ai in range(nx):
            mv = mv + orecv[l, m, ai].astype(jnp.float32)
        mid[l, m] = mv
        n2v = bf(mv * rms(mv, features) * small[l, experts : experts + 1])
        n2[l, m] = n2v
        rv = mm(n2v, rwx[l], ((1,), (1,)))
        hi = bf(rv)
        lo = bf(rv - hi.astype(jnp.float32))
        tail = jnp.where(lane < width + experts, hi, lo)
        for j in range(ny):
            xsend[l, m, j] = jnp.where(lane < width, n2v[:, j * pw : (j + 1) * pw], tail)
        pos.line(lambda bi: copy_x(l, m, bi, b).start())
        xline[l, m, b] = xsend[l, m, b]
        pos.peers(lambda ai: copy_t(l, m, ai, a).start())
        nrows[l, m, a] = n2[l, m]

    def spread(l, m):
        pos.line(lambda bi: copy_x(l, m, bi, bi).wait())
        pos.peers(lambda ai: copy_w(l, m, ai, a).start())
        xall[l, m, :, a] = xline[l, m]

    def dispatch(l, m):
        i0 = lax.broadcasted_iota(jnp.int32, (slots_n, tokens), 0)
        pm[...] = bf(((place[l, m, 0:1] == i0) | (place[l, m, 1:2] == i0)).astype(jnp.float32))
        pos.peers(lambda ai: copy_w(l, m, ai, ai).wait())
        slots[l, m] = bf(mm(pm[...], xall[l, m].reshape(tokens, pw))).reshape(experts, cap, pw)

    def grad_send(m):
        for j in range(ny):
            xsend[0, m, j] = tok[1, m, :, j * pw : (j + 1) * pw]
        pos.line(lambda bi: copy_x(0, m, bi, b).start())
        xline[0, m, b] = xsend[0, m, b]

    def copy_gw(m, ai, slot):
        return remote(xline.at[0, m], gall.at[m, :, slot], gu_send.at[m, ai], gu_recv.at[m, slot], (s, ai, b))

    def grad_spread(m):
        pos.line(lambda bi: copy_x(0, m, bi, bi).wait())
        pos.peers(lambda ai: copy_gw(m, ai, a).start())
        gall[m, :, a] = xline[0, m]

    def grad_dispatch(m):
        i0 = lax.broadcasted_iota(jnp.int32, (slots_n, tokens), 0)
        pm[...] = bf(((place[1, m, 0:1] == i0) | (place[1, m, 1:2] == i0)).astype(jnp.float32))
        pos.peers(lambda ai: copy_gw(m, ai, ai).wait())
        gslots[m] = bf(mm(pm[...], gall[m].reshape(tokens, pw))).reshape(experts, cap, pw)

    def shared_in_part(l, m):
        pos.peers(lambda ai: copy_t(l, m, ai, ai).wait())
        shw = shws[l]
        gu_s = by_blocks(nrows[l, m].reshape(length, d), shw, slice(0, 2 * f), width, pw)
        sgu[l, m] = bf(gu_s)
        gate = gu_s[:, :f]
        shid[l, m] = bf(gate * jax.nn.sigmoid(gate) * gu_s[:, f:])

    def copy_s(l, m, ai, slot):
        return remote(ssend.at[l, m, ai], srecv.at[l, m, slot], s_send.at[l, m, ai], s_recv.at[l, m, slot], (s, ai, b))

    def shared_out_part(l, m):
        for j in range(ny):
            part = mm(shid[l, m], shws[l][j, :, 2 * f :], ((1,), (1,)))
            ssend[l, m, :, :, j * pw : j * pw + width] = bf(part).reshape(nx, sub, width)
        pos.peers(lambda ai: copy_s(l, m, ai, a).start())
        srecv[l, m, a] = ssend[l, m, a]

    def copy_g(l, m, ai, slot):
        return remote(rsend.at[l, m, ai], rpeer.at[l, m, slot], g_send.at[l, m, ai], g_recv.at[l, m, slot], (s, ai, b))

    def copy_r(l, m, bi, slot):
        return remote(rline.at[l, m, bi], rrecv.at[l, m, slot], r_send.at[l, m, bi], r_recv.at[l, m, slot], (s, a, bi))

    def combine(l, m):
        i1 = lax.broadcasted_iota(jnp.int32, (tokens, slots_n), 1)
        pt[...] = bf(((place_t[l, m, :, 0:1] == i1) | (place_t[l, m, :, 1:2] == i1)).astype(jnp.float32))
        br = mm(pt[...], eo[m].reshape(slots_n, width))
        for ai in range(nx):
            rsend[l, m, ai, :, :, :width] = bf(br).reshape(ny, nx, sub, width)[:, ai]
        pos.peers(lambda ai: copy_g(l, m, ai, a).start())
        rpeer[l, m, a] = rsend[l, m, a]

    def combine_line(l, m):
        pos.peers(lambda ai: copy_g(l, m, ai, ai).wait())
        total = rpeer[l, m, 0].astype(jnp.float32)
        for ai in range(1, nx):
            total = total + rpeer[l, m, ai].astype(jnp.float32)
        rline[l, m] = bf(total)
        pos.line(lambda bi: copy_r(l, m, bi, b).start())
        rrecv[l, m, b] = rline[l, m, b]

    def layer_out(l, m):
        pos.peers(lambda ai: copy_s(l, m, ai, ai).wait())
        pos.line(lambda bi: copy_r(l, m, bi, bi).wait())
        total = mid[l, m]
        for ai in range(nx):
            total = total + srecv[l, m, ai].astype(jnp.float32)
        for j in range(ny):
            part = total[:, j * pw : (j + 1) * pw]
            part = part + jnp.where(lane < width, rrecv[l, m, j].astype(jnp.float32), 0.0)
            y[l, m, :, j * pw : (j + 1) * pw] = bf(part)

    first = (b == ny - 1, b == 0)
    last = (b == 0, b == ny - 1)
    up = (ny - 1 - b, b)
    down = (b, ny - 1 - b)
    lag = (sk + ak) * (ny - 1)
    apart = STAGE_STEPS
    units = 2 * half
    gap = max(lag + 6 * apart - units, 0)
    starts = (0, units, 2 * units + gap, 3 * units + gap)
    steps = starts[3] + units + lag

    def unit(t, dd):
        early = (t >= 0) & (t < 2 * units)
        late = (t >= starts[2]) & (t < starts[2] + 2 * units)
        u = jnp.clip(jnp.where(t < starts[2], jnp.minimum(t, 2 * units - 1), t - gap), 0, 4 * units - 1)
        job, r = u // units, lax.rem(u, units)
        return early | late, job // 2, lax.rem(job, 2), r // 2 + dd * half, lax.rem(r, 2)

    def gu_copy(dd, l, m, e, c):
        to = b - 1 if dd == 0 else b + 1
        return remote(gu.at[l, m, e, c], gu.at[l, m, e, c], rs_send.at[l, m, e, c], rs_recv.at[l, m, e, c], (s, a, to))

    def hid_copy(dd, l, m, e, c):
        to = b + 1 if dd == 0 else b - 1
        return remote(hid.at[l, m, e, c], hid.at[l, m, e, c], ag_send.at[l, m, e, c], ag_recv.at[l, m, e, c], (s, a, to))

    def save_gates(l, m, e, c):
        return pltpu.make_async_copy(gu.at[l, m, e, c], gu_o.at[l, m, e, c], g_sem.at[l, m, e, c])

    def chain(i):
        reduce = [unit(i - sk * up[dd], dd) for dd in range(2)]
        spreads = [unit(i - sk * (ny - 1) - ak * down[dd], dd) for dd in range(2)]
        for dd in range(2):
            valid, l, m, e, c = reduce[dd]

            @pl.when(valid)
            def _():
                @pl.when((m == 0) & (c == 0))
                def _():
                    wait_weight(0, e, 0)

                for plane in range(2):
                    part = win[e, plane, :, pl.ds(pl.multiple_of(c * hw, hw), hw)]
                    acc[dd, :, plane * hw : (plane + 1) * hw] = mm(slots[l, m, e, :, :width], part)

                @pl.when((l == 0) & (m == 1) & (c == 1))
                def _():
                    start_weight(1, e, 0)

        for dd in range(2):
            valid, l, m, e, c = reduce[dd]

            @pl.when(valid & first[dd])
            def _():
                gu[l, m, e, c] = bf(acc[dd])
                gu_copy(dd, l, m, e, c).start()

            @pl.when(valid & jnp.logical_not(first[dd] | last[dd]))
            def _():
                gu_copy(dd, l, m, e, c).wait_recv()
                gu[l, m, e, c] = bf(acc[dd] + gu[l, m, e, c].astype(jnp.float32))
                gu_copy(dd, l, m, e, c).start()

            @pl.when(valid & last[dd])
            def _():
                gu_copy(dd, l, m, e, c).wait_recv()
                total = acc[dd] + gu[l, m, e, c].astype(jnp.float32)
                r = router_column(slots[l, m, e], e, width, experts)
                gate = total[:, :hw]
                hid[l, m, e, c] = bf(gate * jax.nn.sigmoid(gate) * total[:, hw:] * jax.nn.sigmoid(r))
                hid_copy(dd, l, m, e, c).start()
                gu[l, m, e, c] = bf(total)
                save_gates(l, m, e, c).start()

        for dd in range(2):
            valid, l, m, e, c = spreads[dd]

            @pl.when(valid & jnp.logical_not(last[dd]))
            def _():
                hid_copy(dd, l, m, e, c).wait_recv()

                @pl.when(jnp.logical_not(first[dd]))
                def _():
                    hid_copy(dd, l, m, e, c).start()

        for dd in range(2):
            valid, l, m, e, c = spreads[dd]

            @pl.when(valid & (c == 1))
            def _():
                @pl.when(m == 0)
                def _():
                    wait_weight(0, e, 1)

                total = mm(hid[l, m, e, 0], wdt[e, :, :hw], ((1,), (1,)))
                eo[m, e] = bf(total + mm(hid[l, m, e, 1], wdt[e, :, hw:], ((1,), (1,))))

                @pl.when((l == 0) & (m == 1))
                def _():
                    start_weight(1, e, 1)

    kept = (
        (slots, slots_o), (nall, rows_o), (q, q_o), (k, k_o), (v, v_o), (att, att_o), (mid, mid_o), (n2, n2_o),
        (nrows, rows2_o), (sgu, sgu_o), (shid, shid_o), (shw0, shw_o.at[0]), (shw1, shw_o.at[1]), (watt1, watt_o),
        (watt0, watt0_o), (tok, tok_o), (small, small_o), (place, place_o), (place_t, place_to),
        (gslots, gslots_o), (hid, hid_o), (y, y_o),
    )
    saves = [pltpu.make_async_copy(src, dst, k_sem.at[c]) for c, (src, dst) in enumerate(kept)]

    def save(copies):
        for copy in copies:
            copy.start()

    stages = {}

    def at(step, do):
        stages.setdefault(step, []).append(do)

    def stage(do, l, m):
        return lambda: do(l, m)

    osend[...] = jnp.zeros_like(osend)
    ssend[...] = jnp.zeros_like(ssend)
    rwx[...] = jnp.zeros_like(rwx)
    for h in range(1, ny):
        for share in entry_shares[:2]:
            share.hop(h)
        if h == 2:
            entry_shares[2].hop(1)
            entry_shares[3].hop(1)
    for share in entry_shares[:2]:
        share.finish()
    tokens_ready()
    for l, full in enumerate((sm0, sm1)):
        for j in range(ny):
            small[l, :, j * pw : (j + 1) * pw] = full[j]
    for l in range(2):
        rwx[l, width : width + experts] = bf(small[l, :experts])
        rwx[l, width + experts : width + 2 * experts] = bf(small[l, :experts])
    norm_first(0, 0)
    norm_first(0, 1)
    entry_shares[2].hop(2)
    entry_shares[3].hop(2)
    places()
    entry_shares[2].hop(3)
    entry_shares[3].hop(3)
    entry_shares[2].finish()
    entry_shares[3].finish()
    shares[0].start()
    shares[1].start()
    attention(0, 0)
    attention(0, 1)
    norm_second(0, 0)
    norm_second(0, 1)
    weights_ready()
    spread(0, 0)
    shares[0].hop(1)
    shares[1].hop(1)
    spread(0, 1)
    dispatch(0, 0)
    for h in range(2, ny):
        at(2 * (h - 2), lambda h=h: (shares[0].hop(h), shares[1].hop(h)))
    at(units // 4, stage(dispatch, 0, 1))
    at(2 * (ny - 2) + 1, lambda: (shares[0].finish(), shares[1].finish()))
    at(units // 2, stage(shared_in_part, 0, 0))
    at(units // 2 + 2, stage(shared_out_part, 0, 0))
    at(units, stage(shared_in_part, 0, 1))
    at(units + 2, stage(shared_out_part, 0, 1))
    for m in range(2):
        done = starts[m] + units - 1 + lag
        for c, do in enumerate((combine, combine_line)):
            at(done + c * apart, stage(do, 0, m))
        at(done + 2 * apart, stage(layer_out, 0, m))
        for c, do in enumerate((norm_first, attention, norm_second, spread, dispatch)):
            at(done + (2 + c) * apart, stage(do, 1, m))
        at(starts[2 + m] + 4, stage(shared_in_part, 1, m))
        at(starts[2 + m] + 8, stage(shared_out_part, 1, m))
        done = starts[2 + m] + units - 1 + lag
        for c, do in enumerate((combine, combine_line, layer_out)):
            at(done + c * apart, stage(do, 1, m))
    at(starts[3] + 9, lambda: save(saves[:-2]))
    at(starts[3] + units - 1 + lag, lambda: save(saves[-2:-1]))
    for m in range(2):
        at(units + 4 + m, lambda m=m: grad_send(m))
        at(units + 6 + m, lambda m=m: grad_spread(m))
        at(units + 8 + m, lambda m=m: grad_dispatch(m))
    at(units + lag - 1, shares[2].start)
    for h in range(1, ny):
        at(units + lag - 1 + 2 * h, lambda h=h: shares[2].hop(h))
    at(units + lag - 1 + 2 * ny, shares[2].finish)

    def step(i, c):
        chain(i)
        for when in sorted(stages):
            if when < steps:
                @pl.when(i == when)
                def _():
                    for do in stages[when]:
                        do()

        return c

    lax.fori_loop(0, steps, step, 0)
    for when in sorted(stages):
        if when >= steps:
            for do in stages[when]:
                do()
    saves[-1].start()

    def finish(index, carry):
        l = index // (mbs * units)
        m = lax.rem(index // units, mbs)
        r = lax.rem(index, units)
        for dd in range(2):
            e, c = r // 2 + dd * half, lax.rem(r, 2)
            pl.when(jnp.logical_not(last[dd]))(gu_copy(dd, l, m, e, c).wait_send)
            pl.when(jnp.logical_not(first[dd]))(hid_copy(dd, l, m, e, c).wait_send)
            pl.when(last[dd])(save_gates(l, m, e, c).wait)
        return carry

    lax.fori_loop(0, 2 * mbs * units, finish, 0)
    for copy in saves:
        copy.wait()


def forward(tin, small_b, att_block, sh_block, routes, cos, sin, rot, win, wdt, dims, heads, features, ids):
    width, pw, experts, cap = dims
    nx, ny = lax.axis_size("gx"), lax.axis_size("gy")
    mbs, length = tin.shape[1:3]
    sub, d = length // nx, ny * pw
    f = wdt.shape[-1]
    length, tokens, n, slots = nx * sub, nx * ny * sub, nx * ny, experts * cap
    b16, f32 = jnp.bfloat16, jnp.float32
    vm = pl.BlockSpec(memory_space=pltpu.VMEM)
    hbm = pl.BlockSpec(memory_space=pl.ANY)
    lm = (2, mbs)
    rows_shape = lm + (nx, sub, d)
    spread_shape = lm + (ny, nx, sub, pw)
    entry = (
        (win.shape, b16), (wdt.shape, b16),
        ((2, mbs, sub, d), b16), ((2, small_b.shape[0], d), f32), (lm + (2, tokens), jnp.int32),
        (lm + (tokens, 2), jnp.int32), ((ny,) + att_block.shape, b16),
    )
    kept = entry + (
        (lm + (sub, d), b16), (lm + (sub, d), f32), (lm + (sub, d), b16), (rows_shape, b16),
        (lm + (length, pw), b16), (lm + (length, pw), b16), (lm + (length, pw), b16), (lm + (length, pw), b16),
        (lm + (experts, cap, pw), b16), (lm + (experts, 2, cap, f), b16), (lm + (experts, 2, cap, f // 2), b16),
        (rows_shape, b16), (lm + (length, 2 * f), b16), (lm + (length, f), b16),
        ((2, ny) + sh_block.shape, b16), ((ny,) + att_block.shape, b16), ((mbs, experts, cap, pw), b16),
    )
    scratch = (
        (lm + (sub, d), b16), (lm + (sub, d), f32), (lm + (sub, d), b16), None,
        (lm + (sub, d), b16), (rows_shape, b16), ((length, 3 * pw), f32),
        (lm + (length, pw), b16), (lm + (length, pw), b16), (lm + (length, pw), b16), (lm + (length, pw), b16),
        (rows_shape, b16), (rows_shape, b16), ((2, pw, d), b16),
        (lm + (ny, sub, pw), b16), (lm + (ny, sub, pw), b16), (spread_shape, b16), (rows_shape, b16),
        ((slots, tokens), b16), ((tokens, slots), b16), (lm + (experts, cap, pw), b16), ((2, cap, f), f32),
        (lm + (experts, 2, cap, f), b16), (lm + (experts, 2, cap, f // 2), b16), ((mbs, experts, cap, width), b16),
        (lm + (length, 2 * f), b16), (lm + (length, f), b16), (rows_shape, b16), (rows_shape, b16),
        (lm + (nx, ny, sub, pw), b16), (lm + (nx, ny, sub, pw), b16), (lm + (ny, sub, pw), b16), (lm + (ny, sub, pw), b16),
        (win.shape, b16), (wdt.shape, b16),
        ((ny,) + sh_block.shape, b16), ((ny,) + sh_block.shape, b16), ((ny,) + att_block.shape, b16), ((ny,) + att_block.shape, b16),
        ((ny, 2, mbs, sub, pw), b16), ((2, mbs, sub, d), b16), (lm + (2, tokens), jnp.int32),
        (lm + (2, tokens), jnp.int32), (lm + (tokens, 2), jnp.int32),
        ((ny,) + small_b.shape, f32), ((ny,) + small_b.shape, f32), ((2, small_b.shape[0], d), f32),
        ((mbs, ny, nx, sub, pw), b16), ((mbs, experts, cap, pw), b16),
    )
    outs = pl.pallas_call(
        functools.partial(forward_kernel, (nx, ny, mbs, sub, width, pw, heads, features, experts, cap, f, *FWD_SKEW)),
        out_shape=tuple(jax.ShapeDtypeStruct(*v) for v in kept),
        in_specs=[vm] * 8 + [hbm] * 2,
        out_specs=(hbm,) * len(kept),
        scratch_shapes=[pltpu.VMEM(*(v or ((8, 128), f32))) for v in scratch] + [
            flags(lm + (nx,)), flags(lm + (nx,)), flags(lm + (nx,)), flags(lm + (nx,)),
            flags(lm + (ny,)), flags(lm + (ny,)), flags(lm + (nx,)), flags(lm + (nx,)), flags(lm + (nx,)), flags(lm + (nx,)),
            flags(lm + (nx,)), flags(lm + (nx,)), flags(lm + (nx,)), flags(lm + (nx,)), flags(lm + (ny,)), flags(lm + (ny,)),
            flags(lm + (experts, 2)), flags(lm + (experts, 2)), flags(lm + (experts, 2)), flags(lm + (experts, 2)),
            flags((experts,)), flags((experts,)), flags(lm + (experts, 2)), flags((24,)),
            flags((nx,)), flags((ny,)), pltpu.SemaphoreType.DMA, pltpu.SemaphoreType.DMA, flags((2,)), flags((2,)), flags((mbs, nx)), flags((mbs, nx)),
        ] + share_sems(ny) * 7,
        compiler_params=params(ids),
        cost_estimate=pl.CostEstimate(flops=10**10, bytes_accessed=8 * 10**7, transcendentals=10**6),
        name="forward",
    )(tin, small_b, att_block, sh_block, routes, cos, sin, rot, win, wdt)
    names = ("win", "wdt", "tok", "small", "place", "place_t", "watt0", "y", "mid", "n2", "rows", "q", "k", "v", "att", "slots", "gu", "hid", "rows2", "sgu", "shid", "shw", "watt1", "gslots")
    return dict(zip(names, outs))


FWD_SKEW = (2, 2)
STAGE_STEPS = 2


def backward_kernel(cfg, *refs):
    nx, ny, mbs, sub, width, pw, heads, features, experts, cap, f, sk, ak = cfg
    (tok_i, small_i, place_i, y_i, mid_i, n2_i, rows_i, q_i, k_i, v_i, att_i, rows2_i, sgu_i, shid_i, shw_i,
     watt0_i, watt1_i, cos, sin, rot, slots_i, gu_i, hid_i, gslots_i, win_a, win_b, wdt_a, wdt_b) = refs[:28]
    (out_o, win_g, wdt_g, att_g, sh_g, small_g,
     win, wdt, xsend, xline, xall, grows, pm, pt, slots, gslots, gown, hid, acc, dh, dgu, deo, sti, std,
     dsgu, ssend, srecv, rsend, rpeer, rline, rrecv, rwx, dm, msend, mall, datt, dqkv, dsend, drecv,
     rw_p, gains, drs, sh_p, att_p, small_p, sh_x, att_x, small_x, sh_r, att_r, small_r, sh_f, att_f, small_f, small_a,
     yv, obuf, g, gx, small, place, x, mid, n2, rows, q, k, v, att, rows2, sgu, shid, shw, watt,
     w_sem, x_send, x_recv, u_send, u_recv, t_send, t_recv, s_send, s_recv, g_send, g_recv, r_send, r_recv,
     m_send, m_recv, d_send, d_recv, rs_send, rs_recv, ag_send, ag_recv, wi_send, wi_recv, wd_send, wd_recv,
     c_send, c_recv, e_send, e_recv, a_send, a_recv, l_sem, st_sem, f_sem, y_sem, o_send, o_recv, free) = refs[28:]
    pos = Position(nx, ny)
    s, a, b = pos.s, pos.a, pos.b
    slots_n = experts * cap
    tokens = nx * ny * sub
    d = ny * pw
    length = nx * sub
    half, hw = experts // 2, f // 2
    scale = DH ** -0.5
    lane = lax.broadcasted_iota(jnp.int32, (1, pw), 1)
    first = (b == ny - 1, b == 0)
    last = (b == 0, b == ny - 1)
    up = (ny - 1 - b, b)
    down = (b, ny - 1 - b)
    barrier = pltpu.get_barrier_semaphore()
    pos.peers(lambda ai: pl.semaphore_signal(barrier, inc=1, device_id=(s, ai, b), device_id_type=MESH))
    pos.line(lambda bi: pl.semaphore_signal(barrier, inc=1, device_id=(s, a, bi), device_id_type=MESH))
    pl.semaphore_signal(barrier, inc=1, device_id=(1 - s, a, b), device_id_type=MESH)
    for so in range(2):
        for i in range(nx):
            @pl.when((so != s) | (i != a) | (a != b))
            def _():
                pl.semaphore_signal(barrier, inc=1, device_id=(so, i, a), device_id_type=MESH)

    def weight_copy(l, e, which):
        own, oth, dst = ((win_a, win_b, win), (wdt_a, wdt_b, wdt))[which]
        sem = w_sem.at[which, e]
        return pltpu.make_async_copy(own.at[e], dst.at[e], sem), pltpu.make_async_copy(oth.at[e], dst.at[e], sem)

    def start_weights(l, e):
        for which in range(2):
            own, oth = weight_copy(l, e, which)
            pl.when(s == l)(own.start)
            pl.when(s != l)(oth.start)

    def first_weights(e, c):
        start_weights(1, e)
        return c

    lax.fori_loop(0, experts, first_weights, 0)

    early = ((rows2_i, rows2), (sgu_i, sgu), (shid_i, shid), (shw_i, shw))
    later = ((mid_i, mid), (n2_i, n2), (rows_i, rows), (q_i, q), (k_i, k), (v_i, v), (att_i, att))

    def early_loads(l):
        return [pltpu.make_async_copy(src.at[l], dst, y_sem.at[c]) for c, (src, dst) in enumerate(early)]

    def later_loads(l):
        copies = [pltpu.make_async_copy(src.at[l], dst, y_sem.at[4 + c]) for c, (src, dst) in enumerate(later)]
        copies.append(pltpu.make_async_copy(y_i.at[0] if l else tok_i.at[0], x, y_sem.at[11]))
        return copies + [pltpu.make_async_copy(watt1_i if l else watt0_i, watt, y_sem.at[12])]

    def hid_load(l):
        return pltpu.make_async_copy(hid_i.at[l], hid, l_sem.at[1])

    def gates(l, m, dd):
        return pltpu.make_async_copy(gu_i.at[l, m, pl.ds(dd * half, half)], gown.at[m], l_sem.at[2 + m])

    def start_gates(l, m):
        for dd in range(2):
            pl.when(last[dd])(gates(l, m, dd).start)

    def wait_gates(l, m):
        for dd in range(2):
            pl.when(last[dd])(gates(l, m, dd).wait)

    first_loads = [
        pltpu.make_async_copy(src, dst, y_sem.at[13 + c])
        for c, (src, dst) in enumerate(((tok_i.at[1], g), (small_i, small), (place_i, place), (y_i, yv)))
    ]
    slots_load = pltpu.make_async_copy(slots_i, slots, l_sem.at[0])
    gslots_load = pltpu.make_async_copy(gslots_i, gslots.at[1], l_sem.at[4])
    for copy in first_loads + [slots_load, gslots_load, hid_load(1)] + early_loads(1) + later_loads(1):
        copy.start()
    for m in range(mbs):
        start_gates(1, m)

    def copy_x(m, bi, slot):
        return remote(xsend.at[m, bi], xline.at[m, slot], x_send.at[m, bi], x_recv.at[m, slot], (s, a, bi))

    def copy_w(m, ai, slot):
        return remote(xline.at[m], xall.at[m, :, slot], u_send.at[m, ai], u_recv.at[m, slot], (s, ai, b))

    def copy_t(m, ai, slot):
        return remote(g.at[m], grows.at[m, slot], t_send.at[m, ai], t_recv.at[m, slot], (s, ai, b))

    for copy in first_loads:
        copy.wait()

    @pl.when(a == b)
    def _():
        pl.semaphore_wait(barrier, nx - 1 + ny - 1 + 1 + 2 * ny - 1)

    @pl.when(a != b)
    def _():
        pl.semaphore_wait(barrier, nx - 1 + ny - 1 + 1 + 2 * ny)

    def out_copy(kind, l, j, s_slot, a_slot):
        src = (yv, gx)[kind].at[l, :, :, pl.ds(j * pw, pw)]
        return remote(src, obuf.at[kind, s_slot, a_slot], o_send.at[kind, l, j], o_recv.at[kind, s_slot, a_slot], (l, b, j))

    def send_out(kind, l):
        for j in range(ny):
            @pl.when((l != s) | (a != b) | (j != b))
            def _():
                out_copy(kind, l, j, s, a).start()

        @pl.when((l == s) & (a == b))
        def _():
            obuf[kind, s, a] = (yv, gx)[kind][l, :, :, pl.ds(pl.multiple_of(b * pw, pw), pw)]

    def sent_out(kind, l):
        for j in range(ny):
            @pl.when((l != s) | (a != b) | (j != b))
            def _():
                out_copy(kind, l, j, s, a).wait_send()

    def take_out(kind):
        for so in range(2):
            for i in range(nx):
                @pl.when((so != s) | (a != b) | (i != a))
                def _():
                    out_copy(kind, 0, 0, so, i).wait_recv()

                out_o[kind, so * mbs : (so + 1) * mbs, i * sub : (i + 1) * sub, :] = obuf[kind, so, i]

    def send_g(m, slots_too=True):
        if slots_too:
            for j in range(ny):
                xsend[m, j] = g[m, :, j * pw : (j + 1) * pw]
            pos.line(lambda bi: copy_x(m, bi, b).start())
            xline[m, b] = xsend[m, b]
        pos.peers(lambda ai: copy_t(m, ai, a).start())
        grows[m, a] = g[m]

    send_g(0, False)
    send_g(1, False)
    deo[...] = jnp.zeros_like(deo)
    ssend[...] = jnp.zeros_like(ssend)
    dsend[...] = jnp.zeros_like(dsend)
    rwx[...] = jnp.zeros_like(rwx)

    def new_layer(l):
        rwx[width : width + experts] = bf(small[l, :experts])
        rwx[width + experts : width + 2 * experts] = bf(small[l, :experts])
        rw_p[...] = jnp.zeros_like(rw_p)
        gains[...] = jnp.zeros_like(gains)

    new_layer(1)

    def spread(m):
        pos.line(lambda bi: copy_x(m, bi, bi).wait())
        pos.peers(lambda ai: copy_w(m, ai, a).start())
        xall[m, :, a] = xline[m]

    def dispatch(l, m):
        i0 = lax.broadcasted_iota(jnp.int32, (slots_n, tokens), 0)
        pm[...] = bf(((place[l, m, 0:1] == i0) | (place[l, m, 1:2] == i0)).astype(jnp.float32))
        pos.peers(lambda ai: copy_w(m, ai, ai).wait())
        gslots[l, m] = bf(mm(pm[...], xall[m].reshape(tokens, pw))).reshape(experts, cap, pw)

    def shared_act(m):
        pos.peers(lambda ai: copy_t(m, ai, ai).wait())
        dsh = by_blocks(grows[m].reshape(length, d), shw, slice(2 * f, 3 * f), width, pw)
        dsg, dsu, _ = act_back(sgu[m, :, :f].astype(jnp.float32), sgu[m, :, f:].astype(jnp.float32), dsh, None)
        dsgu[m, :, :f] = bf(dsg)
        dsgu[m, :, f:] = bf(dsu)

    def copy_s(m, ai, slot):
        return remote(ssend.at[m, ai], srecv.at[m, slot], s_send.at[m, ai], s_recv.at[m, slot], (s, ai, b))

    def shared_back(m):
        for j in range(ny):
            part = mm(dsgu[m], shw[j, :, : 2 * f], ((1,), (1,)))
            ssend[m, :, :, j * pw : j * pw + width] = bf(part).reshape(nx, sub, width)
        pos.peers(lambda ai: copy_s(m, ai, a).start())
        srecv[m, a] = ssend[m, a]

    crossing = ((sh_p, sh_x), (att_p, att_x), (small_p, small_x))
    places = (sh_r, att_r, small_r)
    finals = (sh_f, att_f, small_f)
    results = (sh_g, att_g, small_g)

    def cross(l, i):
        return remote(crossing[i][0], crossing[i][1], c_send.at[i], c_recv.at[i], (l, a, b))

    def block(i, bi):
        if i == 2:
            return small_x.at[:, pl.ds(pl.multiple_of(bi * pw, pw), pw)]
        return crossing[i][1].at[bi]

    def along(i, bi, slot):
        return remote(block(i, bi), places[i].at[slot], e_send.at[i, bi], e_recv.at[i, slot], (s, a, bi))

    def give(l, i):
        pl.when(s != l)(cross(l, i).start)

    def given(l):
        for i in range(3):
            pl.when(s != l)(cross(l, i).wait_send)

    def join(l, i):
        @pl.when(s == l)
        def _():
            cross(l, i).wait_recv()
            part, other = crossing[i]
            other[...] = (part[...].astype(jnp.float32) + other[...].astype(jnp.float32)).astype(other.dtype)
            pos.line(lambda bi: along(i, bi, lax.rem(b - bi + ny, ny) - 1).start())

    def settle(l, i):
        @pl.when(s == l)
        def _():
            pos.line(lambda bi: along(i, bi, lax.rem(bi - b + ny, ny) - 1).wait())
            total = block(i, b)[...].astype(jnp.float32)
            for c in range(1, ny):
                total = total + places[i][c - 1].astype(jnp.float32)
            finals[i][...] = total
            if i < 2:
                pltpu.make_async_copy(finals[i], results[i], f_sem.at[i]).start()

    def shared_grads():
        for j in range(ny):
            rj = rows2[:, :, :, j * pw : j * pw + width].reshape(mbs * length, width)
            sh_p[j, :, : 2 * f] = bf(mm(rj, dsgu[...].reshape(mbs * length, 2 * f), ((0,), (0,))))

    def down_grads(l):
        for j in range(ny):
            gj = grows[:, :, :, j * pw : j * pw + width].reshape(mbs * length, width)
            sh_p[j, :, 2 * f :] = bf(mm(gj, shid[...].reshape(mbs * length, f), ((0,), (0,))))
        give(l, 0)

    def copy_g(m, ai, slot):
        return remote(rsend.at[m, ai], rpeer.at[m, slot], g_send.at[m, ai], g_recv.at[m, slot], (s, ai, b))

    def copy_r(m, bi, slot):
        return remote(rline.at[m, bi], rrecv.at[m, slot], r_send.at[m, bi], r_recv.at[m, slot], (s, a, bi))

    def combine(l, m):
        row = lax.broadcasted_iota(jnp.int32, (128, tokens), 0)
        pair = place[l, m].astype(jnp.float32)
        cols = jnp.where(row == 0, pair[0:1], jnp.where(row == 1, pair[1:2], 0.0)).T.astype(jnp.int32)
        part = tokens // 2
        i1 = lax.broadcasted_iota(jnp.int32, (part, slots_n), 1)
        for c in range(2):
            these = cols[c * part : (c + 1) * part]
            pt[...] = bf(((these[:, 0:1] == i1) | (these[:, 1:2] == i1)).astype(jnp.float32))
            br = bf(mm(pt[...], deo[m].reshape(slots_n, pw))).reshape(ny // 2, nx, sub, pw)
            for ai in range(nx):
                rsend[m, ai, c * (ny // 2) : (c + 1) * (ny // 2)] = br[:, ai]
        pos.peers(lambda ai: copy_g(m, ai, a).start())
        rpeer[m, a] = rsend[m, a]

    def combine_line(m):
        pos.peers(lambda ai: copy_g(m, ai, ai).wait())
        total = rpeer[m, 0].astype(jnp.float32)
        for ai in range(1, nx):
            total = total + rpeer[m, ai].astype(jnp.float32)
        rline[m] = bf(total)
        pos.line(lambda bi: copy_r(m, bi, b).start())
        rrecv[m, b] = rline[m, b]

    def copy_m(m, ai, slot):
        return remote(msend.at[m], mall.at[m, slot], m_send.at[m, ai], m_recv.at[m, slot], (s, ai, b))

    def second_norm(l, m):
        pos.peers(lambda ai: copy_s(m, ai, ai).wait())
        pos.line(lambda bi: copy_r(m, bi, bi).wait())
        dlog = jnp.zeros((sub, pw), jnp.float32)
        parts = []
        for j in range(ny):
            part = rrecv[m, j].astype(jnp.float32)
            dlog = dlog + jnp.where(lane >= width, part, 0.0)
            parts.append(jnp.where(lane < width, part, 0.0))
        hi = bf(dlog)
        lo = bf(dlog - hi.astype(jnp.float32))
        dn2 = jnp.concatenate(parts, 1) + mm(hi, rwx[...]) + mm(lo, rwx[...])
        for ai in range(nx):
            dn2 = dn2 + srecv[m, ai].astype(jnp.float32)
        rw_t = mm(hi, n2[m], ((0,), (0,))) + mm(lo, n2[m], ((0,), (0,)))
        rw_p[...] += rw_t[width : width + experts] + rw_t[width + experts : width + 2 * experts]
        mv = mid[m]
        dx2, gain_g = norm_back(mv, rms(mv, features), small[l, experts : experts + 1], dn2, features)
        gains[0:1] += gain_g
        dm[m] = g[m].astype(jnp.float32) + dx2
        msend[m] = bf(dm[m])
        pos.peers(lambda ai: copy_m(m, ai, a).start())
        mall[m, a] = msend[m]

    def copy_d(m, ai, slot):
        return remote(dsend.at[m, ai], drecv.at[m, slot], d_send.at[m, ai], d_recv.at[m, slot], (s, ai, b))

    def attention(m):
        pos.peers(lambda ai: copy_m(m, ai, ai).wait())
        datt[...] = bf(by_blocks(mall[m].reshape(length, d), watt, slice(3 * pw, 4 * pw), width, pw))
        dq = jnp.zeros((length, pw), jnp.float32)
        dk = dq
        dv = dq
        for h in range(heads):
            mask = head_mask(pw, h)
            qh = jnp.where(mask, q[m], 0)
            kh = jnp.where(mask, k[m], 0)
            da = jnp.where(mask, datt[...], 0)
            p = probs_of(qh, k[m])
            dp = mm(da, v[m], ((1,), (1,)))
            ds = bf(p * (dp - jnp.sum(dp * p, axis=1, keepdims=True)))
            dv = dv + mm(bf(p), da, ((0,), (0,)))
            dq = dq + mm(ds, kh)
            dk = dk + mm(ds, qh, ((0,), (0,)))
        dqkv[m, :, :pw] = turn(dq * scale, cos[...], sin[...], rot[...], -1.0)
        dqkv[m, :, pw : 2 * pw] = turn(dk * scale, cos[...], sin[...], rot[...], -1.0)
        dqkv[m, :, 2 * pw :] = bf(dv)
        for j in range(ny):
            part = mm(dqkv[m], watt[j, :, : 3 * pw], ((1,), (1,)))
            dsend[m, :, :, j * pw : j * pw + width] = bf(part).reshape(nx, sub, width)
        pos.peers(lambda ai: copy_d(m, ai, a).start())
        drecv[m, a] = dsend[m, a]

    def first_norm(l, m):
        pos.peers(lambda ai: copy_d(m, ai, ai).wait())
        dn1 = drecv[m, 0].astype(jnp.float32)
        for ai in range(1, nx):
            dn1 = dn1 + drecv[m, ai].astype(jnp.float32)
        xv = x[m].astype(jnp.float32)
        dx1, gain_g = norm_back(xv, rms(xv, features), small[l, experts + 1 : experts + 2], dn1, features)
        gains[1:2] += gain_g
        gx[l, m] = bf(dm[m] + dx1)
        if l:
            g[m] = gx[l, m]
            send_g(m)

    def attention_grads(l):
        for j in range(ny):
            cols = slice(j * pw, j * pw + width)
            rj = rows[:, :, :, cols].reshape(mbs * length, width)
            mj = mall[:, :, :, cols].reshape(mbs * length, width)
            qkv = mm(rj, dqkv[...].reshape(mbs * length, 3 * pw), ((0,), (0,)))
            rest = mm(mj, att[...].reshape(mbs * length, pw), ((0,), (0,)))
            parts = [qkv[:, c * pw : (c + 1) * pw] for c in range(3)] + [rest]
            for c in range(4):
                att_p[j, :, c * 128 : (c + 1) * 128] = bf(parts[c][:, :128])
            for c in range(2):
                joined = parts[2 * c][:, 128:] + pltpu.roll(parts[2 * c + 1][:, 128:], 64, 1)
                att_p[j, :, (4 + c) * 128 : (5 + c) * 128] = bf(joined)
        give(l, 1)

    def small_grads(l):
        small_p[:experts] = rw_p[...]
        small_p[experts:] = gains[...]
        give(l, 2)

    lag = (sk + ak) * (ny - 1)
    apart = STAGE_STEPS
    units = 2 * half
    gap = max(lag + 6 * apart - units, 0)
    starts = (0, units, 2 * units + gap, 3 * units + gap)

    def unit(t, dd):
        soon = (t >= 0) & (t < 2 * units)
        then = (t >= starts[2]) & (t < starts[2] + 2 * units)
        u = jnp.clip(jnp.where(t < starts[2], jnp.minimum(t, 2 * units - 1), t - gap), 0, 4 * units - 1)
        job, r = u // units, lax.rem(u, units)
        return soon | then, 1 - job // 2, lax.rem(job, 2), r // 2 + dd * half, lax.rem(r, 2)

    def dh_copy(dd, l, m, e, c):
        to = b - 1 if dd == 0 else b + 1
        return remote(dh.at[m, e, c], dh.at[m, e, c], rs_send.at[l, m, e, c], rs_recv.at[l, m, e, c], (s, a, to))

    def dgu_copy(dd, l, m, e, c):
        to = b + 1 if dd == 0 else b - 1
        return remote(dgu.at[m, e, c], dgu.at[m, e, c], ag_send.at[l, m, e, c], ag_recv.at[l, m, e, c], (s, a, to))

    def wi_copy(l, e):
        return remote(win.at[e], win.at[e], wi_send.at[l, e], wi_recv.at[l, e], (l, a, b))

    def wd_copy(l, e):
        return remote(wdt.at[e], wdt.at[e], wd_send.at[l, e], wd_recv.at[l, e], (l, a, b))

    def st_copies(e):
        return (pltpu.make_async_copy(sti, win_g.at[e], st_sem.at[0]), pltpu.make_async_copy(std, wdt_g.at[e], st_sem.at[1]))

    def weight_grads(l, e):
        sl = slots[l, :, e, :, :width].reshape(mbs * cap, width)
        gs = gslots[l, :, e, :, :width].reshape(mbs * cap, width)
        gi = [mm(sl, dgu[:, e, c].reshape(mbs * cap, f), ((0,), (0,))) for c in range(2)]
        gd = [mm(gs, hid[:, e, c].reshape(mbs * cap, hw), ((0,), (0,))) for c in range(2)]
        return gi, gd

    late = 1
    steps = starts[3] + units + lag + 2 * late

    def chain(i):
        reduce = [unit(i - sk * up[dd], dd) for dd in range(2)]
        spreads = [unit(i - sk * (ny - 1) - ak * down[dd], dd) for dd in range(2)]
        for dd in range(2):
            valid, l, m, e, c = reduce[dd]

            @pl.when(valid)
            def _():
                @pl.when((m == 0) & (c == 0))
                def _():
                    weight_copy(0, e, 1)[0].wait()

                acc[dd] = mm(gslots[l, m, e, :, :width], wdt[e, :, pl.ds(pl.multiple_of(c * hw, hw), hw)])

            @pl.when(valid & first[dd])
            def _():
                dh[m, e, c] = bf(acc[dd])
                dh_copy(dd, l, m, e, c).start()

            @pl.when(valid & jnp.logical_not(first[dd] | last[dd]))
            def _():
                dh_copy(dd, l, m, e, c).wait_recv()
                dh[m, e, c] = bf(acc[dd] + dh[m, e, c].astype(jnp.float32))
                dh_copy(dd, l, m, e, c).start()

            @pl.when(valid & last[dd])
            def _():
                dh_copy(dd, l, m, e, c).wait_recv()
                total = acc[dd] + dh[m, e, c].astype(jnp.float32)
                r = router_column(slots[l, m, e], e, width, experts)
                gate = gown[m, e - dd * half, c, :, :hw].astype(jnp.float32)
                upv = gown[m, e - dd * half, c, :, hw:].astype(jnp.float32)
                dgate, dup, dr = act_back(gate, upv, total, jax.nn.sigmoid(r))
                dgu[m, e, c, :, :hw] = bf(dgate)
                dgu[m, e, c, :, hw:] = bf(dup)
                dgu_copy(dd, l, m, e, c).start()
                dr = jnp.where(c == 0, 0.0, drs[dd][:, 0:1]) + dr
                drs[dd] = jnp.broadcast_to(dr, (cap, 128))
                hi = bf(dr).astype(jnp.float32)
                deo[m, e] = bf(jnp.where(lane == width + e, hi, jnp.where(lane == width + experts + e, dr - hi, 0.0)))

        for dd in range(2):
            valid, l, m, e, c = spreads[dd]

            @pl.when(valid & jnp.logical_not(last[dd]))
            def _():
                dgu_copy(dd, l, m, e, c).wait_recv()

                @pl.when(jnp.logical_not(first[dd]))
                def _():
                    dgu_copy(dd, l, m, e, c).start()

        for dd in range(2):
            valid, l, m, e, c = spreads[dd]

            @pl.when(valid & (c == 1))
            def _():
                @pl.when(m == 0)
                def _():
                    weight_copy(0, e, 0)[0].wait()

                total = None
                for c2 in range(2):
                    for plane in range(2):
                        cols, hcols = slice(plane * hw, (plane + 1) * hw), slice(c2 * hw, (c2 + 1) * hw)
                        part = mm(dgu[m, e, c2, :, cols], win[e, plane, :, hcols], ((1,), (1,)))
                        total = part if total is None else total + part
                deo[m, e, :, :width] = bf(total)

        for l in (1, 0):
            t = i - starts[3 - 2 * l] - lag
            weight_stage(l, t)

    def chain_sent(l, e, dd):
        for m in range(mbs):
            for c in range(2):
                pl.when(jnp.logical_not(last[dd]))(dh_copy(dd, l, m, e, c).wait_send)
                pl.when(jnp.logical_not(first[dd]))(dgu_copy(dd, l, m, e, c).wait_send)

    def weight_stage(l, t):
        u = t // 2
        on = (t >= 0) & (t < units) & (lax.rem(t + 2, 2) == 1)

        @pl.when(on)
        def _():
            for dd in range(2):
                chain_sent(l, jnp.clip(u, 0, half - 1) + dd * half, dd)

        @pl.when(on & (s == l))
        def _():
            pl.semaphore_signal(free.at[l], inc=1, device_id=(1 - s, a, b), device_id_type=MESH)

        @pl.when(on & (s != l))
        def _():
            pl.semaphore_wait(free.at[l], 1)
            for dd in range(2):
                e = jnp.clip(u, 0, half - 1) + dd * half
                gi, gd = weight_grads(l, e)
                for c in range(2):
                    for plane in range(2):
                        win[e, plane, :, c * hw : (c + 1) * hw] = bf(gi[c][:, plane * hw : (plane + 1) * hw])
                    wdt[e, :, c * hw : (c + 1) * hw] = bf(gd[c])
                wi_copy(l, e).start()
                wd_copy(l, e).start()

        t2 = t - 2 * late
        w = t2 // 2
        on2 = (t2 >= 0) & (t2 < units) & (lax.rem(t2 + 8, 2) == 1)

        @pl.when(on2 & (s != l))
        def _():
            for dd in range(2):
                e = jnp.clip(w, 0, half - 1) + dd * half
                wi_copy(l, e).wait_send()
                wd_copy(l, e).wait_send()
                if l:
                    start_weights(0, e)

        @pl.when(on2 & (s == l))
        def _():
            for dd in range(2):
                e = jnp.clip(w, 0, half - 1) + dd * half
                gi, gd = weight_grads(l, e)
                wi_copy(l, e).wait_recv()
                wd_copy(l, e).wait_recv()

                @pl.when((w >= 1) | (dd == 1))
                def _():
                    for copy in st_copies(e):
                        copy.wait()

                for c in range(2):
                    hcols = slice(c * hw, (c + 1) * hw)
                    for plane in range(2):
                        part = gi[c][:, plane * hw : (plane + 1) * hw] + win[e, plane, :, hcols].astype(jnp.float32)
                        sti[:, plane * f + c * hw : plane * f + (c + 1) * hw] = bf(part)
                    std[:, hcols] = bf(gd[c] + wdt[e, :, hcols].astype(jnp.float32))
                for copy in st_copies(e):
                    copy.start()
                if l:
                    start_weights(0, e)

    stages = {}

    def at(step, do, *args):
        stages.setdefault(step, []).append(lambda: do(*args))

    def shared_first(l, m):
        if m == 0:
            for copy in early_loads(l):
                copy.wait()
        shared_act(m)

    def reload(copies):
        for copy in copies:
            copy.start()

    def ready(copies):
        for copy in copies:
            copy.wait()

    ready([slots_load, gslots_load, hid_load(1)] + later_loads(1))
    for m in range(mbs):
        wait_gates(1, m)
    for l in (1, 0):
        begin = starts[2 - 2 * l]
        second = starts[3 - 2 * l]
        at(begin + 3, shared_first, l, 0)
        at(begin + 5, shared_back, 0)
        at(second + (-10 if l else 1), shared_first, l, 1)
        at(second + (-8 if l else 3), shared_back, 1)
        at(second + (-6 if l else 5), shared_grads)
        at(second + (-4 if l else 6), down_grads, l)
        at(second + (1 if l else 9), join, l, 0)
        for m in range(2):
            done = starts[2 - 2 * l + m] + units - 1 + lag
            for c, (do, *args) in enumerate((
                    (combine, l, m), (combine_line, m), (second_norm, l, m), (attention, m), (first_norm, l, m))):
                at(done + c * apart, do, *args)
            if l:
                at(starts[m] + units + sk * (ny - 1), start_gates, 0, m)
                at(done + 5 * apart, spread, m)
                at(done + 6 * apart, dispatch, 0, m)
                at(starts[2 + m] - 1, wait_gates, 0, m)
        end = second + units - 1 + lag
        at(end + 3 * apart, attention_grads, l)
        at(end + 4 * apart - (0 if l else 1), join, l, 1)
        at(end + 4 * apart, small_grads, l)
        at(end + 5 * apart, join, l, 2)
        at(end + (2 if l else 4) * apart, settle, l, 0)
        at(end + (10 if l else 5) * apart, settle, l, 2)
        if l:
            at(end + 10 * apart, settle, l, 1)
            at(end + 6 * apart, given, l)
    at(units // 2 - 1, send_out, 0, 0)
    at(units // 2 + 1, send_out, 0, 1)
    at(2 * units, take_out, 0)
    end = starts[1] + units - 1 + lag
    at(end + 4 * apart + 1, send_out, 1, 1)
    at(starts[3] + units - 1 + lag + 4 * apart, send_out, 1, 0)
    at(starts[1] + 1, lambda: reload(early_loads(0)))
    at(end + 2 * late + 1, lambda: reload([hid_load(0)]))
    at(end + 2 * late + 8, lambda: ready([hid_load(0)]))
    at(end + 5 * apart, lambda: reload(later_loads(0)))
    at(end + 10 * apart, lambda: ready(later_loads(0)))
    at(end + 10 * apart, new_layer, 0)

    def step(i, c):
        chain(i)
        for when in sorted(stages):
            if when < steps:
                @pl.when(i == when)
                def _():
                    for do in stages[when]:
                        do()

        return c

    lax.fori_loop(0, steps, step, 0)
    for when in sorted(stages):
        if when >= steps:
            for do in stages[when]:
                do()

    def copy_a(ai, slot):
        return remote(small_f, small_a.at[slot], a_send.at[ai], a_recv.at[slot], (s, ai, b))

    def gain_sums():
        pos.peers(lambda ai: copy_a(ai, a).start())
        small_a[a] = small_f[...]
        pos.peers(lambda ai: copy_a(ai, ai).wait())
        total = small_a[0]
        for ai in range(1, nx):
            total = total + small_a[ai]
        small_f[...] = total

    gain_sums()
    pltpu.make_async_copy(small_f, small_g, f_sem.at[2]).start()
    take_out(1)
    for l in range(2):
        for kind in range(2):
            sent_out(kind, l)
    settle(0, 1)
    given(0)
    for i in range(3):
        pltpu.make_async_copy(finals[i], results[i], f_sem.at[i]).wait()
    for copy in st_copies(experts - 1):
        copy.wait()


def backward(fwd, cos, sin, rot, win, wdt, dims, heads, features, ids):
    width, pw, experts, cap = dims
    nx, ny = lax.axis_size("gx"), lax.axis_size("gy")
    mbs, sub, d = fwd["tok"].shape[-3:]
    f = wdt.shape[-1]
    length, tokens, slots = nx * sub, nx * ny * sub, experts * cap
    b16, f32 = jnp.bfloat16, jnp.float32
    vm = pl.BlockSpec(memory_space=pltpu.VMEM)
    hbm = pl.BlockSpec(memory_space=pl.ANY)
    ac, sc, n, half = 6 * 128, fwd["shw"].shape[3], fwd["small"].shape[1], experts // 2
    rows_shape = (mbs, nx, sub, d)
    dense = lambda c: ((ny, width, c), b16)
    scratch = (
        (win.shape, b16), (wdt.shape, b16),
        ((mbs, ny, sub, pw), b16), ((mbs, ny, sub, pw), b16), ((mbs, ny, nx, sub, pw), b16), (rows_shape, b16),
        ((slots, tokens), b16), ((tokens // 2, slots), b16),
        ((2, mbs, experts, cap, pw), b16), ((2, mbs, experts, cap, pw), b16), ((mbs, half, 2, cap, f), b16),
        ((mbs, experts, 2, cap, f // 2), b16), ((2, cap, f // 2), f32), ((mbs, experts, 2, cap, f // 2), b16),
        ((mbs, experts, 2, cap, f), b16), ((mbs, experts, cap, pw), b16),
        ((width, 2 * f), b16), ((width, f), b16),
        ((mbs, length, 2 * f), b16), (rows_shape, b16), (rows_shape, b16),
        ((mbs, nx, ny, sub, pw), b16), ((mbs, nx, ny, sub, pw), b16), ((mbs, ny, sub, pw), b16), ((mbs, ny, sub, pw), b16),
        ((pw, d), b16), ((mbs, sub, d), f32), ((mbs, sub, d), b16), (rows_shape, b16),
        ((length, pw), b16), ((mbs, length, 3 * pw), b16), (rows_shape, b16), (rows_shape, b16),
        ((experts, d), f32), ((8, d), f32), ((2, cap, 128), f32),
        dense(sc), dense(ac), ((n, d), f32), dense(sc), dense(ac), ((n, d), f32),
        ((ny - 1, width, sc), b16), ((ny - 1, width, ac), b16), ((ny - 1, n, pw), f32),
        ((width, sc), f32), ((width, ac), f32), ((n, pw), f32), ((nx, n, pw), f32),
        ((2, mbs, sub, d), b16), ((2, 2, nx, mbs, sub, pw), b16),
        ((mbs, sub, d), b16), ((2, mbs, sub, d), b16),
        *((fwd[name].shape, fwd[name].dtype) for name in ("small", "place")),
        ((mbs, sub, d), b16),
        *((fwd[name].shape[1:], fwd[name].dtype) for name in (
            "mid", "n2", "rows", "q", "k", "v", "att", "rows2", "sgu", "shid", "shw")),
        (fwd["watt0"].shape, b16),
    )
    by_m = lambda c: flags((mbs, c))
    by_half = flags((2, mbs, experts, 2))
    names = ("tok", "small", "place", "y", "mid", "n2", "rows", "q", "k", "v", "att", "rows2", "sgu", "shid",
             "shw", "watt0", "watt1")
    outs = pl.pallas_call(
        functools.partial(
            backward_kernel, (nx, ny, mbs, sub, width, pw, heads, features, experts, cap, f, *BWD_SKEW)),
        out_shape=(
            jax.ShapeDtypeStruct((2, 2 * mbs, length, pw), b16),
            jax.ShapeDtypeStruct((experts, width, 2 * f), b16),
            jax.ShapeDtypeStruct((experts, width, f), b16),
            jax.ShapeDtypeStruct((width, ac), f32),
            jax.ShapeDtypeStruct((width, sc), f32),
            jax.ShapeDtypeStruct((n, pw), f32),
        ),
        in_specs=[hbm] * 17 + [vm] * 3 + [hbm] * 8,
        out_specs=(vm,) + (hbm,) * 5,
        scratch_shapes=[pltpu.VMEM(*v) for v in scratch] + [
            flags((2, experts)), by_m(ny), by_m(ny), by_m(nx), by_m(nx), by_m(nx), by_m(nx), by_m(nx), by_m(nx),
            by_m(nx), by_m(nx), by_m(ny), by_m(ny), by_m(nx), by_m(nx), by_m(nx), by_m(nx),
            by_half, by_half, by_half, by_half,
            flags((2, experts)), flags((2, experts)), flags((2, experts)), flags((2, experts)),
            flags((3,)), flags((3,)), flags((3, ny)), flags((3, ny)), flags((nx,)), flags((nx,)),
            flags((5,)), flags((2,)), flags((3,)), flags((20,)), flags((2, 2, ny)), flags((2, 2, nx)), pltpu.SemaphoreType.REGULAR((2,)),
        ],
        compiler_params=params(ids),
        cost_estimate=pl.CostEstimate(flops=2 * 10**10, bytes_accessed=10**8, transcendentals=10**6),
        name="backward",
    )(*(fwd[name] for name in names), cos, sin, rot, *(fwd[name] for name in ("slots", "gu", "hid", "gslots")), win, fwd["win"], wdt, fwd["wdt"])
    return outs[0], outs[1:]


BWD_SKEW = (2, 2)


def fast_device(block_input, output_grad, attention_gain, attention_in, attention_out, feed_gain,
                router_weight, expert_in, expert_down, shared_in, shared_down, routes):
    s = lax.axis_index("section")
    ny = lax.axis_size("gy")
    nx = lax.axis_size("gx")
    mbs = block_input.shape[0] // 2
    width = block_input.shape[2]
    features = width * ny
    experts = expert_in.shape[1]
    f = expert_in.shape[-1]
    pw = lanes_up(width + 2 * experts)
    tokens = routes.shape[2]
    cap = 5 * tokens // (2 * experts)
    length = tokens // ny
    heads = attention_in.shape[-1] // DH
    dims = (width, pw, experts, cap)

    att_block = jnp.concatenate([
        pad_to(attention_in[0], 2, pw).reshape(width, 3 * pw), pad_to(attention_out[0].T, 1, pw)], 1)
    sh_block = jnp.concatenate([shared_in[0].reshape(width, 2 * f), shared_down[0].T], 1)
    small = jnp.concatenate([
        router_weight[0].T.astype(jnp.float32), feed_gain, attention_gain, jnp.zeros((6, width), jnp.float32)], 0)
    tin = lax.dynamic_slice_in_dim(jnp.stack([block_input, output_grad]), s * mbs, mbs, 1)
    tin = pad_to(tin, 3, pw)
    small = pad_to(small, 1, pw)
    win = jnp.swapaxes(expert_in[0], 1, 2)
    wdt = expert_down[0].transpose(0, 2, 1)
    pairs = jnp.swapaxes(routes[0], 1, 2)
    half = DH // 2
    freq = 10000.0 ** (-np.arange(half, dtype=np.float64) / half)
    lanes = np.tile(np.arange(length)[:, None] * freq[None], (1, 2 * heads))
    cos = np.zeros((length, pw), np.float32)
    sin = np.zeros((length, pw), np.float32)
    cos[:, : heads * DH] = np.cos(lanes)
    sin[:, : heads * DH] = np.sin(lanes)
    rot = np.zeros((pw, pw), np.float32)
    for lead in range(0, heads * DH, DH):
        at = lead + np.arange(half)
        rot[at + half, at] = -1.0
        rot[at, at + half] = 1.0
    cos, sin, rot = jnp.asarray(cos), jnp.asarray(sin), jnp.asarray(rot, jnp.bfloat16)

    fwd = forward(tin, small, att_block, sh_block, pairs, cos, sin, rot, win, wdt, dims, heads, features, 0)
    both, grads = backward(fwd, cos, sin, rot, win, wdt, dims, heads, features, 1)
    win_g, wdt_g, att_g, sh_g, small_g = grads
    win_g, wdt_g, y, gx, ain, aout, sin_g, sdn, gain_g, fgain_g, rw = finish_outputs(
        win_g, wdt_g, both, att_g, sh_g, small_g, pw, heads * DH)
    return (
        jnp.swapaxes(y, 1, 2)[None],
        jnp.swapaxes(gx, 1, 2)[None],
        gain_g,
        jnp.swapaxes(ain, 0, 1)[None],
        aout[None],
        fgain_g,
        rw.T[None],
        win_g[None],
        jnp.swapaxes(wdt_g, 1, 2)[None],
        sin_g[None],
        sdn.T[None],
    )


def any_device(*arrays):
    block_input, attention_in, routes = arrays[0], arrays[3], arrays[-1]
    batches, rows, width = block_input.shape
    fits = (
        lax.axis_size("gx") == lax.axis_size("gy")
        and lax.axis_size("section") == 2
        and batches == 4
        and rows == 128
        and routes.shape[2] == rows * lax.axis_size("gy")
        and 128 < width <= 192
        and attention_in.shape[-1] == width
        and lanes_up(width + 2 * arrays[7].shape[1]) == 256
    )
    return fast_device(*arrays) if fits else on_device(*arrays)


def solution(mesh):
    in_specs = (
        P(None, "gx", "gy"),
        P(None, "gx", "gy"),
        P("section", "gy"),
        P("section", "gy", None, "gx"),
        P("section", "gx", "gy"),
        P("section", "gy"),
        P("section", "gy", None),
        P("section", None, "gy", None, "gx"),
        P("section", None, "gx", "gy"),
        P("section", "gy", None, "gx"),
        P("section", "gx", "gy"),
        P("section", None, None, None),
    )
    out_specs = (
        P("section", None, "gx", "gy"),
        P("section", None, "gx", "gy"),
        P("section", "gy"),
        P("section", "gy", None, "gx"),
        P("section", "gx", "gy"),
        P("section", "gy"),
        P("section", "gy", None),
        P("section", None, "gy", None, "gx"),
        P("section", None, "gx", "gy"),
        P("section", "gy", None, "gx"),
        P("section", "gx", "gy"),
    )
    return jax.shard_map(
        any_device, mesh=mesh, in_specs=in_specs, out_specs=out_specs, check_vma=False
    )
```
